128 devices in a mesh: grp: 32 (over z, x, core), nar: 4 (over y).
Axes of the slice: x: 4, y: 4, z: 4, core: 2. Of those that a mesh axis runs over, the one named last changes fastest.
Arguments:
- features: bfloat16 [1048576, 128], P(('grp', 'nar')), may hold values from -6 to 6
- requests: int32 [16384, 64], P(('grp', 'nar')), may hold values from 0 to 8191
- index_one: int32 [262144, 16], P(('grp', 'nar')), may hold values from 0 to 8191
- mask_one: int32 [262144, 15], P(('grp', 'nar')), may hold values from 0 to 1, as said below
- index_two: int32 [65536, 11], P(('grp', 'nar')), may hold values from 0 to 8191
- mask_two: int32 [65536, 10], P(('grp', 'nar')), may hold values from 0 to 1, as said below
- labels: int32 [65536], P(('grp', 'nar')), may hold values from 0 to 171
- seed_live: int32 [65536], P(('grp', 'nar')), may hold values from 0 to 1
- w_first: float32 [256, 256], P('nar'), may hold values from -0.5 to 0.5
- w_second: float32 [512, 172], P('nar'), may hold values from -0.375 to 0.375
- mom_first: float32 [256, 256], P('nar')
- mom_second: float32 [512, 172], P('nar')
- biases: float32 [428], replicated, may hold values from -4 to 4
- bias_m: float32 [428], replicated, may hold values from -0.0004272461 to 0.0004272461
- bias_v: float32 [428], replicated, may hold values from 8.871389e-11 to 3.5485556e-10
Outputs:
- loss: float32 [], replicated
- first_new: float32 [256, 256], P('nar')
- second_new: float32 [512, 172], P('nar')
- mom_first_new: float32 [256, 256], P('nar')
- mom_second_new: float32 [512, 172], P('nar')
- first_low: bfloat16 [256, 256], P('nar')
- second_low: bfloat16 [512, 172], P('nar')
- biases_new: float32 [428], replicated
- bias_m_new: float32 [428], replicated
- bias_v_new: float32 [428], replicated
The draws below stay inside these ranges and needn't reach their ends.
Inputs may be any that keep to these rules, and one draw needn't show every extreme that they name: `index_one`: column 0 names the node's own row, the others its sampled neighbours. `index_two`: column 0 names the seed's own first-layer row in its group. `mask_one`: some rows have no live slot. `mask_two`: some rows have no live slot.
All inputs are finite; a program needn't handle non-finite values.
Results may differ from the reference program's by a relative error of at most 0.0031.
Values may be sent and summed in bfloat16 or wider, within the bound.
A program may use at most 128 MiB of HBM per device.

```python
import math
import jax
import jax.numpy as jnp
from jax import lax

D_IN = 128
HID = 256
CLS = 172
F1 = 15
F2 = 10
NS_ITERS = 5
STEP = 10
SEED_DEV = 512
OWN_DEV = 8192
FRONT_DEV = 2048
SRC_DEV = 8192
CAP = 64
GROUP_ROWS = 8192
SEEDS = 65536
FRONT = 262144
NODES = 1048576
N_NAR = 4
DEVICES = 128


def alive_slots(key, row_count, slot_count, ones_of_four, rarity):
    alive = jax.random.randint(key, (row_count, slot_count), 0, 4) < ones_of_four
    empty_rows = jax.random.randint(jax.random.fold_in(key, 1), (row_count, 1), 0, rarity) == 0
    return jnp.where(empty_rows, 0, alive.astype(jnp.int32)).astype(jnp.int32)


def dominant_matrix(key, row_count, col_count, scale):
    noise = jax.random.normal(key, (row_count, col_count), jnp.float32)
    sizes = jnp.exp(jax.random.uniform(jax.random.fold_in(key, 1), (row_count, col_count), jnp.float32, 0.0, 0.6931))
    signs = jnp.where(jax.random.bernoulli(jax.random.fold_in(key, 2), 0.5, (row_count, col_count)), 1.0, -1.0)
    diag = jnp.eye(row_count, col_count, dtype=jnp.float32) * (3.0 * max(row_count, col_count) ** 0.5)
    return (scale * (noise + diag * sizes * signs)).astype(jnp.float32)


def draw_mask_one(key, part):
    key = jax.random.fold_in(key, 11)
    return alive_slots(key, FRONT, F1, 3, 32)


def draw_mask_two(key, part):
    key = jax.random.fold_in(key, 12)
    return alive_slots(key, SEEDS, F2, 2, 32)


def draw_seed_live(key, part):
    key = jax.random.fold_in(key, 13)
    trainer = jnp.arange(SEEDS, dtype=jnp.int32) // SEED_DEV
    picks = jax.random.randint(key, (SEEDS,), 0, 3 * (DEVICES - 1))
    return (picks < DEVICES - 1 + 2 * trainer).astype(jnp.int32)


def draw_mom_first(key, part):
    key = jax.random.fold_in(key, 21)
    return dominant_matrix(key, 2 * D_IN, HID, 0.1 * (SEED_DEV * DEVICES) ** (-0.5))


def draw_mom_second(key, part):
    key = jax.random.fold_in(key, 22)
    return dominant_matrix(key, 2 * HID, CLS, 0.5 * (CLS * SEED_DEV * DEVICES) ** (-0.5))


def with_ends(values, rng, least, top_value):
    longest = values.shape.index(max(values.shape))
    spots = []
    for shift in (0, 1):
        where = [jax.random.randint(jax.random.fold_in(rng, axis), (), 0, length) for axis, length in enumerate(values.shape)]
        where[longest] = (where[longest] + shift) % values.shape[longest]
        spots.append(tuple(where))
    return values.at[spots[0]].set(least).at[spots[1]].set(top_value)


def levels(stream_key, shape, shards, low, high):
    def one(axis_at, shards_of):
        draws = jax.random.uniform(jax.random.fold_in(jax.random.fold_in(stream_key, 6), axis_at), (shards_of,), jnp.float32, low / len(shards), high / len(shards))
        return jnp.repeat(jnp.exp(draws), shape[axis_at] // shards_of).reshape((-1,) + (1,) * (len(shape) - axis_at - 1))

    loudness = one(*shards[0])
    for cut in shards[1:]:
        loudness = loudness * one(*cut)
    return loudness


def gaussian(key, dims, scale, bound, pieces=(), kind=jnp.bfloat16):
    gain = levels(key, dims, pieces, -0.22, 0.18) if pieces else 1.0
    entries = jax.random.normal(key, dims, jnp.float32) * scale * gain
    return jnp.minimum(jnp.maximum(entries, -bound), bound).astype(kind)


def setup_inputs(seed: int = 0) -> dict:
    key_list = jax.random.split(jax.random.key(seed), 16)
    features = gaussian(key_list[0], (NODES, D_IN), 1.0, 6.0, ((0, 128),))
    requests = with_ends(jax.random.randint(key_list[1], (DEVICES * DEVICES, CAP), 0, OWN_DEV), jax.random.fold_in(key_list[1], 1), 0, OWN_DEV - 1).astype(jnp.int32)
    index_one = with_ends(jax.random.randint(key_list[2], (FRONT, 1 + F1), 0, SRC_DEV), jax.random.fold_in(key_list[2], 1), 0, SRC_DEV - 1).astype(jnp.int32)
    mask_one = draw_mask_one(jax.random.fold_in(key_list[15], 71), 0)
    index_two = with_ends(jax.random.randint(key_list[4], (SEEDS, 1 + F2), 0, GROUP_ROWS), jax.random.fold_in(key_list[4], 1), 0, GROUP_ROWS - 1).astype(jnp.int32)
    mask_two = draw_mask_two(jax.random.fold_in(key_list[15], 71), 0)
    labels = with_ends(jax.random.randint(key_list[6], (SEEDS,), 0, CLS), jax.random.fold_in(key_list[6], 1), 0, CLS - 1).astype(jnp.int32)
    seed_live = draw_seed_live(jax.random.fold_in(key_list[15], 71), 0)
    w_first = gaussian(key_list[8], (2 * D_IN, HID), D_IN ** -0.5, 0.5, ((0, 4),), jnp.float32)
    w_second = gaussian(key_list[9], (2 * HID, CLS), HID ** -0.5, 0.375, ((0, 4),), jnp.float32)
    mom_first = draw_mom_first(jax.random.fold_in(key_list[15], 71), 0)
    mom_second = draw_mom_second(jax.random.fold_in(key_list[15], 71), 0)
    biases = gaussian(key_list[12], (HID + CLS,), 0.3, 4.0, (), jnp.float32)
    bias_m = gaussian(key_list[13], (HID + CLS,), (0.1 * (CLS * SEED_DEV * DEVICES) ** -0.5), 0.0004272461, (), jnp.float32)
    bias_v = jnp.clip(jnp.exp(jax.random.uniform(key_list[14], (HID + CLS,), jnp.float32, math.log(8.871389040043809e-11), math.log(3.5485556160175236e-10))), 8.871389040043809e-11, 3.5485556160175236e-10)
    return {"features": features, "requests": requests, "index_one": index_one, "mask_one": mask_one, "index_two": index_two, "mask_two": mask_two, "labels": labels, "seed_live": seed_live, "w_first": w_first, "w_second": w_second, "mom_first": mom_first, "mom_second": mom_second, "biases": biases, "bias_m": bias_m, "bias_v": bias_v}


LAM = 0.5
MU = 0.95
WDECAY = 0.01
LR_BIAS = 0.05
BETA_ONE = 0.9
BETA_TWO = 0.999
EPSILON = 1e-08
NS_A = 3.4445
NS_B = -4.775
NS_C = 2.0315
HIGH = lax.Precision.HIGHEST

@jax.custom_vjp
def low(v):
    return lax.optimization_barrier(v.astype(jnp.bfloat16)).astype(jnp.float32)

@jax.custom_vjp
def low_back(v):
    return v

def low_keep(v):
    return (low(v), None)

def low_pass(kept, grad):
    return (grad,)

def back_keep(v):
    return (v, None)

def back_low(kept, grad):
    return (low(grad),)
low.defvjp(low_keep, low_pass)
low_back.defvjp(back_keep, back_low)

def first_inputs(features, requests, index_one, mask_one):
    feats = features.astype(jnp.float32)
    req = requests.reshape(DEVICES, DEVICES, CAP).astype(jnp.int32)
    idx = index_one.reshape(DEVICES, FRONT_DEV, 1 + F1).astype(jnp.int32)
    msk = mask_one.reshape(DEVICES, FRONT_DEV, F1).astype(jnp.float32)
    base = (jnp.arange(DEVICES, dtype=jnp.int32) * OWN_DEV)[:, None]

    def one_trainer(items):
        rq, ix, mk = items
        table = (rq + base).reshape(-1)
        rows = feats[table[ix]]
        total = lax.optimization_barrier(jnp.sum(rows[:, 1:, :] * mk[:, :, None], axis=1))
        count = jnp.maximum(lax.optimization_barrier(jnp.sum(mk, axis=1)), 1.0)
        return jnp.concatenate([rows[:, 0, :], low(total / count[:, None])], axis=1)
    return lax.map(one_trainer, (req, idx, msk)).reshape(FRONT, 2 * D_IN)

def forward(params, act_one, index_two, mask_two, labels, live):
    w_one, w_two, bias = params
    z_one = jnp.dot(act_one, low(w_one), precision=HIGH) + bias[:HID]
    z_one = low_back(z_one)
    hidden = low(jax.nn.silu(z_one))
    self_two = hidden[index_two[:, 0]]
    mk = mask_two.astype(jnp.float32)
    total = jnp.zeros((SEEDS, HID), jnp.float32)
    for slot in range(F2):
        total = total + mk[:, slot:slot + 1] * hidden[index_two[:, 1 + slot]]
    count = jnp.maximum(lax.optimization_barrier(jnp.sum(mk, axis=1)), 1.0)
    near_two = low(total / count[:, None])
    act_two = jnp.concatenate([self_two, near_two], axis=1)
    logits = low_back(jnp.dot(act_two, low(w_two), precision=HIGH) + bias[HID:])
    lse = jax.nn.logsumexp(logits, axis=1)
    picked = jnp.take_along_axis(logits, labels[:, None], axis=1)[:, 0]
    diff = self_two - near_two
    terms = lse - picked + LAM / HID * lax.optimization_barrier(jnp.sum(diff * diff, axis=1))
    return jnp.sum(live * terms)

def orthogonal(mom):
    x = mom / (jnp.sqrt(jnp.sum(mom * mom)) + 1e-07)
    for _ in range(NS_ITERS):
        gram = jnp.dot(x.T, x, precision=HIGH)
        mix = NS_B * gram + NS_C * jnp.dot(gram, gram, precision=HIGH)
        x = NS_A * x + jnp.dot(x, mix, precision=HIGH)
    return x

def muon(weight, grad, mom):
    mom_new = MU * mom + grad
    scale = max(1.0, weight.shape[0] / weight.shape[1]) ** 0.5
    new = weight * (1.0 - WDECAY) - scale * orthogonal(mom_new)
    return (new, mom_new)

def reference(features, requests, index_one, mask_one, index_two, mask_two, labels, seed_live, w_first, w_second, mom_first, mom_second, biases, bias_m, bias_v):
    act_one = first_inputs(features, requests, index_one, mask_one)
    group_base = jnp.arange(DEVICES, dtype=jnp.int32) // N_NAR * (N_NAR * FRONT_DEV)
    idx_two = (index_two.reshape(DEVICES, SEED_DEV, 1 + F2).astype(jnp.int32) + group_base[:, None, None]).reshape(SEEDS, 1 + F2)
    live = seed_live.astype(jnp.float32)

    def loss_of(params):
        return forward(params, act_one, idx_two, mask_two, labels.astype(jnp.int32), live)
    loss, pullback = jax.vjp(loss_of, (w_first, w_second, biases))
    grad_one, grad_two, grad_bias = pullback(jnp.float32(1.0 / SEEDS))[0]
    first_new, mom_first_new = muon(w_first, grad_one, mom_first)
    second_new, mom_second_new = muon(w_second, grad_two, mom_second)
    m_new = BETA_ONE * bias_m + (1.0 - BETA_ONE) * grad_bias
    v_new = BETA_TWO * bias_v + (1.0 - BETA_TWO) * grad_bias * grad_bias
    m_hat = m_new / (1.0 - BETA_ONE ** STEP)
    v_hat = v_new / (1.0 - BETA_TWO ** STEP)
    bias_new = biases * (1.0 - LR_BIAS * WDECAY) - LR_BIAS * m_hat / (jnp.sqrt(v_hat) + EPSILON)
    return (loss, first_new, second_new, mom_first_new, mom_second_new, first_new.astype(jnp.bfloat16), second_new.astype(jnp.bfloat16), bias_new, m_new, v_new)
```

```python
import functools

import jax
import jax.numpy as jnp
from jax import lax
from jax.experimental import pallas as pl
from jax.experimental.pallas import tpu as pltpu
from jax.sharding import PartitionSpec as P

HID = 256
CLS = 172
CLS_PAD = 176
D_IN = 128
F1 = 15
F2 = 10
NS_ITERS = 5
STEP = 10
LAM = 0.5
MU = 0.95
WDECAY = 0.01
LR_BIAS = 0.05
BETA_ONE = 0.9
BETA_TWO = 0.999
EPSILON = 1e-08
NS_A = 3.4445
NS_B = -4.775
NS_C = 2.0315
HIGH = lax.Precision.HIGHEST
MESH = pl.DeviceIdType.MESH
BF = jnp.bfloat16
F32 = jnp.float32

DEV = 128
NAR = 4
OWN = 8192
CAP = 64
SRC = 8192
FRONT = 2048
SEED = 512


def all_to(t):
    return (t // NAR, t % NAR)


def pull_kernel(
    req, feat, w1, w2t, m1, m2t, idx2,
    pulled, gw1, gw2t, gm1, gm2t, gidx2,
    featb, featf, reqin, reqs, stage, sendbuf,
    feat_sem, req_send, req_recv, loc_sem, row_send, row_recv, nar_send, nar_recv,
):
    g = lax.axis_index("grp")
    y = lax.axis_index("nar")
    me = g * NAR + y

    load = pltpu.make_async_copy(feat, featb, feat_sem)
    load.start()

    barrier = pltpu.get_barrier_semaphore()

    def greet(i, c):
        pl.semaphore_signal(barrier, inc=1, device_id=all_to((me + i) % DEV), device_id_type=MESH)
        return c

    lax.fori_loop(1, DEV, greet, 0)
    pl.semaphore_wait(barrier, DEV - 1)

    def ask(i, c):
        t = (me + i * 37) % DEV
        pltpu.make_async_remote_copy(
            src_ref=req.at[t], dst_ref=reqin.at[me], send_sem=req_send, recv_sem=req_recv,
            device_id=all_to(t), device_id_type=MESH,
        ).start()
        return c

    lax.fori_loop(1, DEV, ask, 0)

    own = []
    for n, (a, b) in enumerate(((w1, gw1), (w2t, gw2t), (m1, gm1), (m2t, gm2t), (idx2, gidx2))):
        own.append(pltpu.make_async_copy(a, b.at[y], loc_sem.at[n]))
        own[-1].start()
        for d in range(1, NAR):
            pltpu.make_async_remote_copy(
                src_ref=a, dst_ref=b.at[y], send_sem=nar_send.at[n, d - 1], recv_sem=nar_recv.at[n, d - 1],
                device_id=(g, (y + d) % NAR), device_id_type=MESH,
            ).start()

    load.wait()

    def widen(i, c):
        rows = pl.ds(pl.multiple_of(i * 256, 256), 256)
        featf[rows, :] = featb[rows, :].astype(F32)
        return c

    lax.fori_loop(0, OWN // 256, widen, 0)

    mine = pltpu.make_async_copy(req.at[me], reqin.at[me], loc_sem.at[5])
    mine.start()
    mine.wait()
    got = reqin.at[pl.ds(0, DEV - 1)]
    pltpu.make_async_copy(got, got, req_recv).wait()
    fetch = pltpu.make_async_copy(reqin, reqs, loc_sem.at[6])
    fetch.start()
    fetch.wait()

    def serve(i, c):
        t = (me + i * 37) % DEV
        for r in range(CAP):
            stage[r:r + 1, :] = featf[pl.ds(reqs[t, 0, r], 1), :]
        slot = pl.ds(pl.multiple_of(i * CAP, CAP), CAP)
        sendbuf[slot, :] = stage[...].astype(BF)
        return t, slot

    def serve_far(i, c):
        t, slot = serve(i, c)
        pltpu.make_async_remote_copy(
            src_ref=sendbuf.at[slot], dst_ref=pulled.at[pl.ds(pl.multiple_of(me * CAP, CAP), CAP)],
            send_sem=row_send, recv_sem=row_recv, device_id=all_to(t), device_id_type=MESH,
        ).start()
        return c

    lax.fori_loop(1, DEV, serve_far, 0)
    serve(0, 0)
    pulled[pl.ds(pl.multiple_of(me * CAP, CAP), CAP), :] = sendbuf[0:CAP, :]

    for n, (a, b) in enumerate(((w1, gw1), (w2t, gw2t), (m1, gm1), (m2t, gm2t), (idx2, gidx2))):
        own[n].wait()
        for d in range(1, NAR):
            pltpu.make_async_remote_copy(
                src_ref=a, dst_ref=b.at[y], send_sem=nar_send.at[n, d - 1], recv_sem=nar_recv.at[n, d - 1],
                device_id=(g, (y + d) % NAR), device_id_type=MESH,
            ).wait()
    sent = req.at[pl.ds(0, DEV - 1)]
    pltpu.make_async_copy(sent, sent, req_send).wait()
    gone = sendbuf.at[pl.ds(0, (DEV - 1) * CAP)]
    pltpu.make_async_copy(gone, gone, row_send).wait()
    come = pulled.at[pl.ds(0, (DEV - 1) * CAP)]
    pltpu.make_async_copy(come, come, row_recv).wait()


def pull(req, feat, w1, w2t, m1, m2t, idx2):
    vm = pl.BlockSpec(memory_space=pltpu.VMEM)
    small = (w1, w2t, m1, m2t, idx2)
    return pl.pallas_call(
        pull_kernel,
        out_shape=[jax.ShapeDtypeStruct((SRC, D_IN), BF)]
        + [jax.ShapeDtypeStruct((NAR,) + a.shape, a.dtype) for a in small],
        in_specs=[vm, pl.BlockSpec(memory_space=pl.ANY)] + [vm] * 5,
        out_specs=[vm] * 6,
        scratch_shapes=[
            pltpu.VMEM((OWN, D_IN), BF),
            pltpu.VMEM((OWN, D_IN), F32),
            pltpu.VMEM((DEV, 1, 128), jnp.int32),
            pltpu.SMEM((DEV, 1, 128), jnp.int32),
            pltpu.VMEM((CAP, D_IN), F32),
            pltpu.VMEM((DEV * CAP, D_IN), BF),
            pltpu.SemaphoreType.DMA,
            pltpu.SemaphoreType.DMA,
            pltpu.SemaphoreType.DMA,
            pltpu.SemaphoreType.DMA((7,)),
            pltpu.SemaphoreType.DMA,
            pltpu.SemaphoreType.DMA,
            pltpu.SemaphoreType.DMA((5, 3)),
            pltpu.SemaphoreType.DMA((5, 3)),
        ],
        compiler_params=pltpu.CompilerParams(
            collective_id=0, has_side_effects=True, vmem_limit_bytes=56 * 2**20
        ),
    )(req, feat, *small)


def first_kernel(idx, inv, pulled, w1t, b1, a1, z1t, h1t, table, near, own):
    def widen(i, c):
        rows = pl.ds(pl.multiple_of(i * 256, 256), 256)
        table[rows, :] = pulled[rows, :].astype(F32)
        return c

    lax.fori_loop(0, SRC // 256, widen, 0)
    table[SRC:SRC + 8, :] = jnp.zeros((8, D_IN), F32)

    def some(i, c):
        base = pl.multiple_of(i * 8, 8)
        for j in range(8):
            m = base + j
            own[pl.ds(m, 1), :] = table[pl.ds(idx[0, m], 1), :]
            rows = [table[pl.ds(idx[1 + k, m], 1), :] for k in range(F1)]
            while len(rows) > 1:
                rows = [a + b for a, b in zip(rows[::2], rows[1::2])] + ([rows[-1]] if len(rows) % 2 else [])
            near[pl.ds(m, 1), :] = rows[0] * inv[0, m]
        return c

    lax.fori_loop(0, FRONT // 8, some, 0)

    def block(i, c):
        rows = pl.ds(pl.multiple_of(i * 256, 256), 256)
        act = jnp.concatenate([own[rows, :].astype(BF), near[rows, :].astype(BF)], axis=1)
        a1[rows, :] = act
        z = lax.dot_general(
            w1t[...], act, (((1,), (1,)), ((), ())), preferred_element_type=F32
        ) + b1[...]
        z1t[:, rows] = z
        h1t[:, rows] = (z * jax.nn.sigmoid(z)).astype(BF)
        return c

    lax.fori_loop(0, FRONT // 256, block, 0)


def first(idx, inv, pulled, w1t, b1):
    vm = pl.BlockSpec(memory_space=pltpu.VMEM)
    sm = pl.BlockSpec(memory_space=pltpu.SMEM)
    return pl.pallas_call(
        first_kernel,
        out_shape=[
            jax.ShapeDtypeStruct((FRONT, 2 * D_IN), BF),
            jax.ShapeDtypeStruct((HID, FRONT), F32),
            jax.ShapeDtypeStruct((HID, FRONT), BF),
        ],
        in_specs=[sm, sm, vm, vm, vm],
        out_specs=[vm] * 3,
        scratch_shapes=[
            pltpu.VMEM((SRC + 8, D_IN), F32),
            pltpu.VMEM((FRONT, D_IN), F32),
            pltpu.VMEM((FRONT, D_IN), F32),
        ],
        compiler_params=pltpu.CompilerParams(vmem_limit_bytes=56 * 2**20),
    )(idx, inv, pulled, w1t, b1)


def dot(a, b, dims=((1,), (0,)), precision=None):
    return lax.dot_general(a, b, (dims, ((), ())), preferred_element_type=F32, precision=precision)


def newton_schulz(x):
    x = x / (jnp.sqrt(jnp.sum(x * x)) + 1e-07)
    for _ in range(NS_ITERS):
        gram = dot(x, x, ((1,), (1,)), HIGH)
        mix = NS_B * gram + NS_C * dot(gram, gram, precision=HIGH)
        x = NS_A * x + dot(mix, x, precision=HIGH)
    return x


def per_device(
    features, requests, index_one, mask_one, index_two, mask_two, labels, seed_live,
    w_first, w_second, mom_first, mom_second, biases, bias_m, bias_v,
):
    y = lax.axis_index("nar")
    seeds_all = SEED * DEV
    live = seed_live.astype(F32)[None, :]
    idx_one, msk_one = index_one.T, mask_one.T
    idx_two, msk_two = index_two.T, mask_two.T
    idx_one = jnp.concatenate([idx_one[:1], jnp.where(msk_one > 0, idx_one[1:], SRC)], axis=0)
    inv_one = 1.0 / jnp.maximum(jnp.sum(msk_one.astype(F32), axis=0, keepdims=True), 1.0)
    idx_two = jnp.concatenate(
        [idx_two[:1], jnp.where(msk_two > 0, idx_two[1:], -1), jnp.zeros((5, SEED), jnp.int32)], axis=0
    )
    inv_two = 1.0 / jnp.maximum(jnp.sum(msk_two.astype(F32), axis=0, keepdims=True), 1.0)
    w2t = jnp.pad(w_second.astype(BF).T, ((0, CLS_PAD - CLS), (0, 0)))
    m2t = jnp.pad(mom_second.T, ((0, CLS_PAD - CLS), (0, 0)))
    req = jnp.pad(requests, ((0, 0), (0, 64))).reshape(DEV, 1, 128)
    pulled, gw1, gw2t, gm1, gm2t, gidx2 = pull(
        req, features, w_first.astype(BF), w2t, mom_first, m2t, idx_two
    )
    w1t = gw1.reshape(HID, 2 * D_IN).T
    w2t = jnp.transpose(gw2t, (1, 0, 2)).reshape(CLS_PAD, 2 * HID)[:CLS]
    b1 = biases[:HID][:, None]
    b2 = biases[HID:][:, None]
    a1, z1t, h1t = first(idx_one, inv_one, pulled, w1t, b1)

    group = lax.all_gather(h1t, "nar", axis=1, tiled=True)
    iota = jnp.arange(NAR * FRONT, dtype=jnp.int32)[:, None]
    pick_near = sum((iota == idx_two[1 + k][None, :]).astype(F32) for k in range(F2)).astype(BF)
    pick_self = (iota == idx_two[:1]).astype(BF)
    near = (dot(group, pick_near) * inv_two).astype(BF)
    self2 = dot(group, pick_self).astype(BF)
    act2 = jnp.concatenate([self2, near], axis=0)
    logits = dot(w2t, act2) + b2
    top = jnp.max(logits, axis=0, keepdims=True)
    e = jnp.exp(logits - top)
    tot = jnp.sum(e, axis=0, keepdims=True)
    lse = top + jnp.log(tot)
    hot = (jnp.arange(CLS, dtype=jnp.int32)[:, None] == labels[None, :]).astype(F32)
    picked = jnp.sum(hot * logits, axis=0, keepdims=True)
    diff = self2.astype(F32) - near.astype(F32)
    terms = lse - picked + LAM / HID * jnp.sum(diff * diff, axis=0, keepdims=True)
    loss = jnp.sum(live * terms)
    dlog = (live * (e / tot - hot) / seeds_all).astype(BF)
    g2t = dot(dlog, act2, ((1,), (1,)))
    db2 = jnp.sum(dlog.astype(F32), axis=1)
    da = dot(w2t, dlog, ((0,), (0,)))
    reg = 2.0 * LAM / HID / seeds_all * live * diff
    dself = (da[:HID] + reg).astype(BF)
    dnear = ((da[HID:] - reg) * inv_two).astype(BF)
    back = lax.all_gather(jnp.concatenate([dself, dnear], axis=0), "nar", axis=1, tiled=True)
    rows = jnp.arange(FRONT, dtype=jnp.int32)[:, None] + y * FRONT
    alls = jnp.transpose(gidx2, (1, 0, 2)).reshape(16, NAR * SEED)
    put_near = sum((rows == alls[1 + k][None, :]).astype(F32) for k in range(F2)).astype(BF)
    put_self = (rows == alls[:1]).astype(BF)
    dh1 = dot(back[:HID], put_self, ((1,), (1,))) + dot(back[HID:], put_near, ((1,), (1,)))
    sig = jax.nn.sigmoid(z1t)
    dz1 = (dh1 * sig * (1.0 + z1t * (1.0 - sig))).astype(BF)
    g1t = dot(dz1, a1)
    db1 = jnp.sum(dz1.astype(F32), axis=1)
    flat = jnp.concatenate([g1t.reshape(-1), g2t.reshape(-1), db1, db2, loss[None]])
    flat = lax.psum(flat, ("grp", "nar"))
    n1, n2 = HID * 2 * D_IN, CLS * 2 * HID
    g1 = flat[:n1].reshape(HID, 2 * D_IN).T
    g2t = flat[n1:n1 + n2].reshape(CLS, 2 * HID)
    grad_bias = flat[n1 + n2:-1]
    loss = flat[-1]
    mom1 = MU * gm1.reshape(2 * D_IN, HID) + g1
    mom2t = MU * jnp.transpose(gm2t, (1, 0, 2)).reshape(CLS_PAD, 2 * HID)[:CLS] + g2t
    x1 = newton_schulz(mom1.T).T
    x2t = newton_schulz(mom2t)
    x1 = lax.dynamic_slice_in_dim(x1, y * 64, 64, 0)
    x2 = lax.dynamic_slice_in_dim(x2t, y * 128, 128, 1).T
    mom_one_new = lax.dynamic_slice_in_dim(mom1, y * 64, 64, 0)
    mom_two_new = lax.dynamic_slice_in_dim(mom2t, y * 128, 128, 1).T
    first_new = w_first * (1.0 - WDECAY) - x1
    second_new = w_second * (1.0 - WDECAY) - (2 * HID / CLS) ** 0.5 * x2
    m_new = BETA_ONE * bias_m + (1.0 - BETA_ONE) * grad_bias
    v_new = BETA_TWO * bias_v + (1.0 - BETA_TWO) * grad_bias * grad_bias
    m_hat = m_new / (1.0 - BETA_ONE**STEP)
    v_hat = v_new / (1.0 - BETA_TWO**STEP)
    bias_new = biases * (1.0 - LR_BIAS * WDECAY) - LR_BIAS * m_hat / (jnp.sqrt(v_hat) + EPSILON)
    return (
        loss, first_new, second_new, mom_one_new, mom_two_new,
        first_new.astype(BF), second_new.astype(BF), bias_new, m_new, v_new,
    )


def solution(mesh):
    both = ("grp", "nar")
    placed = (
        P(both, None), P(both, None), P(both, None), P(both, None), P(both, None), P(both, None),
        P(both), P(both), P("nar", None), P("nar", None), P("nar", None), P("nar", None), P(), P(), P(),
    )
    nar = P("nar", None)
    return jax.shard_map(
        per_device, mesh=mesh, in_specs=placed,
        out_specs=(P(), nar, nar, nar, nar, nar, nar, P(), P(), P()), check_vma=False,
    )
```

```python
import functools

import jax
import jax.numpy as jnp
from jax import lax
from jax.experimental import pallas as pl
from jax.experimental.pallas import tpu as pltpu
from jax.sharding import PartitionSpec as P

HID = 256
CLS = 172
CLS_PAD = 176
D_IN = 128
F1 = 15
F2 = 10
NS_ITERS = 5
STEP = 10
LAM = 0.5
MU = 0.95
WDECAY = 0.01
LR_BIAS = 0.05
BETA_ONE = 0.9
BETA_TWO = 0.999
EPSILON = 1e-08
NS_A = 3.4445
NS_B = -4.775
NS_C = 2.0315
HIGH = lax.Precision.HIGHEST
MESH = pl.DeviceIdType.MESH
BF = jnp.bfloat16
F32 = jnp.float32

DEV = 128
NAR = 4
OWN = 8192
CAP = 64
SRC = 8192
FRONT = 2048
SEED = 512


def all_to(t):
    return (t // NAR, t % NAR)


def pull_kernel(
    req, feat, w1, w2t, m1, m2t, idx2,
    pulled, gw1, gw2t, gm1, gm2t, gidx2,
    featb, featf, reqin, reqs, stage, sendbuf,
    feat_sem, req_send, req_recv, loc_sem, row_send, row_recv, nar_send, nar_recv,
):
    g = lax.axis_index("grp")
    y = lax.axis_index("nar")
    me = g * NAR + y

    load = pltpu.make_async_copy(feat, featb, feat_sem)
    load.start()

    barrier = pltpu.get_barrier_semaphore()

    def greet(i, c):
        pl.semaphore_signal(barrier, inc=1, device_id=all_to((me + i) % DEV), device_id_type=MESH)
        return c

    lax.fori_loop(1, DEV, greet, 0)
    pl.semaphore_wait(barrier, DEV - 1)

    def ask(i, c):
        t = (me + i * 37) % DEV
        pltpu.make_async_remote_copy(
            src_ref=req.at[t], dst_ref=reqin.at[me], send_sem=req_send, recv_sem=req_recv,
            device_id=all_to(t), device_id_type=MESH,
        ).start()
        return c

    lax.fori_loop(1, DEV, ask, 0)

    own = []
    for n, (a, b) in enumerate(((w1, gw1), (w2t, gw2t), (m1, gm1), (m2t, gm2t), (idx2, gidx2))):
        own.append(pltpu.make_async_copy(a, b.at[y], loc_sem.at[n]))
        own[-1].start()
        for d in range(1, NAR):
            pltpu.make_async_remote_copy(
                src_ref=a, dst_ref=b.at[y], send_sem=nar_send.at[n, d - 1], recv_sem=nar_recv.at[n, d - 1],
                device_id=(g, (y + d) % NAR), device_id_type=MESH,
            ).start()

    load.wait()

    def widen(i, c):
        rows = pl.ds(pl.multiple_of(i * 256, 256), 256)
        featf[rows, :] = featb[rows, :].astype(F32)
        return c

    lax.fori_loop(0, OWN // 256, widen, 0)

    mine = pltpu.make_async_copy(req.at[me], reqin.at[me], loc_sem.at[5])
    mine.start()
    mine.wait()
    got = reqin.at[pl.ds(0, DEV - 1)]
    pltpu.make_async_copy(got, got, req_recv).wait()
    fetch = pltpu.make_async_copy(reqin, reqs, loc_sem.at[6])
    fetch.start()
    fetch.wait()

    def serve(i, c):
        t = (me + i * 37) % DEV
        for r in range(CAP):
            stage[r:r + 1, :] = featf[pl.ds(reqs[t, 0, r], 1), :]
        slot = pl.ds(pl.multiple_of(i * CAP, CAP), CAP)
        sendbuf[slot, :] = stage[...].astype(BF)
        return t, slot

    def serve_far(i, c):
        t, slot = serve(i, c)
        pltpu.make_async_remote_copy(
            src_ref=sendbuf.at[slot], dst_ref=pulled.at[pl.ds(pl.multiple_of(me * CAP, CAP), CAP)],
            send_sem=row_send, recv_sem=row_recv, device_id=all_to(t), device_id_type=MESH,
        ).start()
        return c

    lax.fori_loop(1, DEV, serve_far, 0)
    serve(0, 0)
    pulled[pl.ds(pl.multiple_of(me * CAP, CAP), CAP), :] = sendbuf[0:CAP, :]

    for n, (a, b) in enumerate(((w1, gw1), (w2t, gw2t), (m1, gm1), (m2t, gm2t), (idx2, gidx2))):
        own[n].wait()
        for d in range(1, NAR):
            pltpu.make_async_remote_copy(
                src_ref=a, dst_ref=b.at[y], send_sem=nar_send.at[n, d - 1], recv_sem=nar_recv.at[n, d - 1],
                device_id=(g, (y + d) % NAR), device_id_type=MESH,
            ).wait()
    sent = req.at[pl.ds(0, DEV - 1)]
    pltpu.make_async_copy(sent, sent, req_send).wait()
    gone = sendbuf.at[pl.ds(0, (DEV - 1) * CAP)]
    pltpu.make_async_copy(gone, gone, row_send).wait()
    come = pulled.at[pl.ds(0, (DEV - 1) * CAP)]
    pltpu.make_async_copy(come, come, row_recv).wait()


def pull(req, feat, w1, w2t, m1, m2t, idx2):
    vm = pl.BlockSpec(memory_space=pltpu.VMEM)
    small = (w1, w2t, m1, m2t, idx2)
    return pl.pallas_call(
        pull_kernel,
        out_shape=[jax.ShapeDtypeStruct((SRC, D_IN), BF)]
        + [jax.ShapeDtypeStruct((NAR,) + a.shape, a.dtype) for a in small],
        in_specs=[vm, pl.BlockSpec(memory_space=pl.ANY)] + [vm] * 5,
        out_specs=[vm] * 6,
        scratch_shapes=[
            pltpu.VMEM((OWN, D_IN), BF),
            pltpu.VMEM((OWN, D_IN), F32),
            pltpu.VMEM((DEV, 1, 128), jnp.int32),
            pltpu.SMEM((DEV, 1, 128), jnp.int32),
            pltpu.VMEM((CAP, D_IN), F32),
            pltpu.VMEM((DEV * CAP, D_IN), BF),
            pltpu.SemaphoreType.DMA,
            pltpu.SemaphoreType.DMA,
            pltpu.SemaphoreType.DMA,
            pltpu.SemaphoreType.DMA((7,)),
            pltpu.SemaphoreType.DMA,
            pltpu.SemaphoreType.DMA,
            pltpu.SemaphoreType.DMA((5, 3)),
            pltpu.SemaphoreType.DMA((5, 3)),
        ],
        compiler_params=pltpu.CompilerParams(
            collective_id=0, has_side_effects=True, vmem_limit_bytes=56 * 2**20
        ),
    )(req, feat, *small)


P1 = 33
P2 = 44
PIECES = P1 + P2
SEEDS_ALL = SEED * DEV


def dot(a, b, dims=((1,), (0,))):
    return lax.dot_general(a, b, (dims, ((), ())), preferred_element_type=F32)


NN = ((1,), (0,))
NT = ((1,), (1,))


def split(a):
    hi = a.astype(BF)
    return hi, (a - hi.astype(F32)).astype(BF)


def dot3(a, b, dims):
    (ah, al), (bh, bl) = a, b
    return dot(ah, bh, dims) + (dot(ah, bl, dims) + dot(al, bh, dims))


def ns_step(x):
    xs = split(x)
    gram = dot3(xs, xs, NT)
    gs = split(gram)
    mix = NS_B * gram + NS_C * dot3(gs, gs, NN)
    return NS_A * x + dot3(split(mix), xs, NN)


def spread(row):
    return jnp.broadcast_to(row, (128, 128)).T


def step_kernel(
    idx, inv, pulled, gw1, gw2t, gm1, gm2t, idx2, gidx2, labels, live, bias, biasm, biasv, w1own, w2own,
    o_loss, o_first, o_second, o_mom1, o_mom2, o_flow, o_slow, o_bias, o_bm, o_bv,
    table, near, own, a1, z1t, gbuf, fsel, bsel, rbuf, dbuf, dh1, w1t, w2, b1c, b2c, pay1, pay2, misc,
    inbox, res1, res2, mine, x1s, x2s,
    h_send, h_recv, r_send, r_recv, d_send, d_recv, rs_send, rs_recv, ag_send, ag_recv,
):
    g = lax.axis_index("grp")
    y = lax.axis_index("nar")
    me = g * NAR + y
    left, right, opp = (y + 3) % NAR, (y + 1) % NAR, (y + 2) % NAR

    barrier = pltpu.get_barrier_semaphore()

    def greet(i, c):
        pl.semaphore_signal(barrier, inc=1, device_id=all_to((me + i) % DEV), device_id_type=MESH)
        return c

    lax.fori_loop(1, DEV, greet, 0)

    def link(src, dst, ssem, rsem, to):
        return pltpu.make_async_remote_copy(
            src_ref=src, dst_ref=dst, send_sem=ssem, recv_sem=rsem, device_id=(g, to), device_id_type=MESH
        )

    def widen(i, c):
        rows = pl.ds(pl.multiple_of(i * 256, 256), 256)
        table[rows, :] = pulled[rows, :].astype(F32)
        return c

    lax.fori_loop(0, SRC // 256, widen, 0)
    table[SRC:SRC + 8, :] = jnp.zeros((8, D_IN), F32)
    w1t[...] = gw1[...].reshape(2 * D_IN, HID).T
    w2t = jnp.concatenate([gw2t[q] for q in range(NAR)], axis=1)
    w2[...] = w2t.T
    b1c[...] = jnp.concatenate([spread(bias[0:1, :]), spread(bias[1:2, :])], axis=0)
    b2c[...] = jnp.concatenate([spread(bias[2:3, :]), spread(bias[3:4, :])], axis=0)

    iota16 = lax.broadcasted_iota(jnp.int32, (16, 128), 0).astype(jnp.int16)
    one, zero = jnp.ones((16, 128), BF), jnp.zeros((16, 128), BF)

    def select(ids, base, groups, put):
        ids = ids - base
        rows = [
            [jnp.broadcast_to(ids[k:k + 1, c * 128:(c + 1) * 128], (16, 128)).astype(jnp.int16) for c in range(4)]
            for k in range(1 + F2)
        ]

        def body(i, carry):
            here = iota16 + jnp.full((16, 128), i * 16, jnp.int32).astype(jnp.int16)
            out = pl.ds(pl.multiple_of(i * 16, 16), 16)
            for c in range(4):
                acc = jnp.where(here == rows[1][c], one, zero)
                for k in range(2, 1 + F2):
                    acc = acc + jnp.where(here == rows[k][c], one, zero)
                put(out, c * 128, acc)
                put(out, SEED + c * 128, jnp.where(here == rows[0][c], one, zero))
            return carry

        lax.fori_loop(0, groups, body, 0)

    def put_f(rows, col, v):
        fsel[rows, col:col + 128] = v

    select(idx2[...], 0, SRC // 16, put_f)
    for q in range(NAR):
        def put_b(rows, col, v, q=q):
            bsel[q, rows, col:col + 128] = v

        select(gidx2[q], y * FRONT, FRONT // 16, put_b)

    pl.semaphore_wait(barrier, DEV - 1)

    view = table.reshape(SRC + 8, 1, D_IN)

    def cols(b):
        return pl.ds(pl.multiple_of(b * 256, 256), 256)

    def forward(b):
        @pl.when(b % 2 == 0)
        def _():
            blk = gbuf.at[left, :, cols(b)]
            link(blk, blk, h_send.at[0, b], h_recv.at[0, b], right).wait_recv()
            link(blk, blk, h_send.at[2, b], h_recv.at[2, b], right).start()

        @pl.when(b % 2 == 1)
        def _():
            blk = gbuf.at[right, :, cols(b)]
            link(blk, blk, h_send.at[1, b], h_recv.at[1, b], left).wait_recv()
            link(blk, blk, h_send.at[2, b], h_recv.at[2, b], left).start()

    def block(b, c):
        def some(i, c2):
            base = pl.multiple_of(b * 256 + i * 8, 8)
            for j in range(8):
                m = base + j
                own[pl.ds(m, 1), :] = view[idx[0, m]]
                rows = [view[idx[1 + k, m]] for k in range(F1)]
                while len(rows) > 1:
                    rows = [p + q for p, q in zip(rows[::2], rows[1::2])] + ([rows[-1]] if len(rows) % 2 else [])
                near[pl.ds(m, 1), :] = rows[0] * inv[0, m]
            return c2

        lax.fori_loop(0, 32, some, 0)
        rows = cols(b)
        act = jnp.concatenate([own[rows, :].astype(BF), near[rows, :].astype(BF)], axis=1)
        a1[rows, :] = act
        z = dot(w1t[...], act, NT) + jnp.concatenate([b1c[...], b1c[...]], axis=1)
        z1t[:, rows] = z
        gbuf[y, :, rows] = (z / (1.0 + jnp.exp(-z))).astype(BF)
        blk = gbuf.at[y, :, rows]
        link(blk, blk, h_send.at[0, b], h_recv.at[0, b], right).start()
        link(blk, blk, h_send.at[1, b], h_recv.at[1, b], left).start()

        @pl.when(b > 0)
        def _():
            forward(b - 1)

        return c

    lax.fori_loop(0, 8, block, 0)
    forward(7)

    def from_source(q):
        return dot(gbuf[q], fsel[pl.ds(pl.multiple_of(q * FRONT, FRONT), FRONT), :])

    total = from_source(y)
    for b in range(1, 8, 2):
        blk = gbuf.at[left, :, b * 256:(b + 1) * 256]
        link(blk, blk, h_send.at[0, b], h_recv.at[0, b], right).wait_recv()
    total = total + from_source(left)
    for b in range(0, 8, 2):
        blk = gbuf.at[right, :, b * 256:(b + 1) * 256]
        link(blk, blk, h_send.at[1, b], h_recv.at[1, b], left).wait_recv()
    total = total + from_source(right)
    for b in range(8):
        blk = gbuf.at[opp, :, b * 256:(b + 1) * 256]
        link(blk, blk, h_send.at[2, b], h_recv.at[2, b], right).wait_recv()
    total = total + from_source(opp)

    def inverse_count(ids):
        n = jnp.sum((ids[1:1 + F2, :] >= 0).astype(F32), axis=0, keepdims=True)
        return 1.0 / jnp.maximum(n, 1.0)

    near2 = (total[:, :SEED] * inverse_count(idx2[...])).astype(BF)
    self2 = total[:, SEED:].astype(BF)
    alive = live[...].astype(F32)
    diff = self2.astype(F32) - near2.astype(F32)

    def swap_start(buf, ssem, rsem):
        blk = buf.at[y]
        link(blk, blk, ssem.at[0], rsem.at[0], right).start()
        link(blk, blk, ssem.at[1], rsem.at[1], left).start()

    def swap_forward(buf, ssem, rsem, cut):
        blk = buf.at[left]
        link(blk, blk, ssem.at[0], rsem.at[0], right).wait_recv()
        half = buf.at[left, 0:cut, :]
        link(half, half, ssem.at[2], rsem.at[2], right).start()
        blk = buf.at[right]
        link(blk, blk, ssem.at[1], rsem.at[1], left).wait_recv()
        half = buf.at[right, cut:, :]
        link(half, half, ssem.at[3], rsem.at[3], left).start()

    def swap_end(buf, ssem, rsem, cut):
        half = buf.at[opp, 0:cut, :]
        link(half, half, ssem.at[2], rsem.at[2], right).wait_recv()
        half = buf.at[opp, cut:, :]
        link(half, half, ssem.at[3], rsem.at[3], left).wait_recv()

    def swap_sent(buf, ssem, rsem, cut):
        blk = buf.at[y]
        link(blk, blk, ssem.at[0], rsem.at[0], right).wait_send()
        link(blk, blk, ssem.at[1], rsem.at[1], left).wait_send()
        half = buf.at[left, 0:cut, :]
        link(half, half, ssem.at[2], rsem.at[2], right).wait_send()
        half = buf.at[right, cut:, :]
        link(half, half, ssem.at[3], rsem.at[3], left).wait_send()

    rbuf[y] = (2.0 * LAM / HID / SEEDS_ALL * alive * diff).astype(BF)
    swap_start(rbuf, r_send, r_recv)

    act2 = jnp.concatenate([self2, near2], axis=0)
    w2t = jnp.concatenate([gw2t[q] for q in range(NAR)], axis=1)
    cls = lax.broadcasted_iota(jnp.int32, (CLS_PAD, SEED), 0)
    b2 = b2c[0:CLS_PAD, :]
    logits = dot(w2t, act2) + jnp.concatenate([b2] * 4, axis=1)
    logits = jnp.where(cls < CLS, logits, -1e30)
    top = jnp.max(logits, axis=0, keepdims=True)
    e = jnp.exp(logits - top)
    tot = jnp.sum(e, axis=0, keepdims=True)
    hot = cls == labels[...]
    picked = jnp.sum(jnp.where(hot, logits, 0.0), axis=0, keepdims=True)
    dlog = (alive * (e * (1.0 / tot) - jnp.where(hot, 1.0, 0.0)) * (1.0 / SEEDS_ALL)).astype(BF)
    dbuf[y] = dlog
    swap_start(dbuf, d_send, d_recv)

    terms = top + jnp.log(tot) - picked + LAM / HID * jnp.sum(diff * diff, axis=0, keepdims=True)
    loss = jnp.sum(alive * terms, axis=1, keepdims=True)
    g2t = dot(dlog, act2, NT).astype(BF)
    for q in range(NAR):
        pay2[q * CLS_PAD:(q + 1) * CLS_PAD, :] = g2t[:, q * 128:(q + 1) * 128]

    my_piece = (me * 77) % DEV

    def to_owner(pay, first, count):
        def body(i, c):
            t = (me + i) % DEV
            p = (t * 77) % DEV - first

            @pl.when((p >= 0) & (p < count))
            def _():
                pltpu.make_async_remote_copy(
                    src_ref=pay.at[pl.ds(pl.multiple_of(p * 16, 16), 16)], dst_ref=inbox.at[me],
                    send_sem=rs_send, recv_sem=rs_recv, device_id=all_to(t), device_id_type=MESH,
                ).start()

            return c

        lax.fori_loop(1, DEV, body, 0)

    def add_up(pay, res, first, count, ssem, rsem):
        q = my_piece - first

        @pl.when((q >= 0) & (q < count))
        def _():
            rows16 = pl.ds(pl.multiple_of(q * 16, 16), 16)
            got = inbox.at[pl.ds(0, DEV - 1)]
            pltpu.make_async_copy(got, got, rs_recv).wait()
            inbox[me] = pay[rows16, :]

            def body(i, acc):
                part = inbox[pl.ds(pl.multiple_of(i * 8, 8), 8)].astype(F32)
                return acc + jnp.sum(part, axis=0)

            res[rows16, :] = lax.fori_loop(0, DEV // 8, body, jnp.zeros((16, 128), F32))

            def tell(i, c):
                pltpu.make_async_remote_copy(
                    src_ref=res.at[rows16], dst_ref=res.at[rows16],
                    send_sem=ssem, recv_sem=rsem, device_id=all_to((me + i) % DEV), device_id_type=MESH,
                ).start()
                return c

            lax.fori_loop(1, DEV, tell, 0)

    def take(res, first, count, rsem):
        q = my_piece - first
        holds = (q >= 0) & (q < count)

        @pl.when(holds)
        def _():
            got = res.at[pl.ds(0, (count - 1) * 16)]
            pltpu.make_async_copy(got, got, rsem).wait()

        @pl.when(jnp.logical_not(holds))
        def _():
            got = res.at[pl.ds(0, count * 16)]
            pltpu.make_async_copy(got, got, rsem).wait()

    to_owner(pay2, P1, P2)

    def grads(q):
        da = dot(w2[...], dbuf[q])
        r = rbuf[q].astype(F32)
        ds = (da[:HID] + r).astype(BF)
        dn = ((da[HID:] - r) * inverse_count(gidx2[q])).astype(BF)
        return dot(jnp.concatenate([dn, ds], axis=1), bsel[q], NT)

    swap_forward(rbuf, r_send, r_recv, 128)
    dh1[...] = grads(y)
    swap_forward(dbuf, d_send, d_recv, 96)
    dh1[...] += grads(left)
    dh1[...] += grads(right)
    swap_end(rbuf, r_send, r_recv, 128)
    swap_end(dbuf, d_send, d_recv, 96)
    dh1[...] += grads(opp)
    add_up(pay2, res2, P1, P2, ag_send.at[0], ag_recv.at[0])

    z = z1t[...]
    sig = 1.0 / (1.0 + jnp.exp(-z))
    dz = (dh1[...] * sig * (1.0 + z * (1.0 - sig))).astype(BF)
    g1 = dot(dz, a1[...]).T.astype(BF)
    pay1[0:256, :] = g1[:, :128]
    pay1[256:512, :] = g1[:, 128:]
    ones_f = jnp.ones((8, FRONT), BF)
    ones_s = jnp.ones((8, SEED), BF)
    db1 = dot(ones_f, dz, NT)[0:1, :]
    db2 = dot(ones_s, dlog, NT)[0:1, :]
    misc[...] = jnp.zeros((16, 128), F32)

    def two(rows, v):
        hi = v.astype(BF).astype(F32)
        misc[rows:rows + 1, 0:v.shape[1]] = hi
        misc[rows + 4:rows + 5, 0:v.shape[1]] = v - hi

    two(0, db1[:, :128])
    two(1, db1[:, 128:])
    two(2, db2[:, :128])
    two(3, db2[:, 128:])
    hi = loss.astype(BF).astype(F32)
    misc[8:9, 0:1] = hi
    misc[9:10, 0:1] = loss - hi
    pay1[512:528, :] = misc[...].astype(BF)
    to_owner(pay1, 0, P1)

    take(res2, P1, P2, ag_recv.at[0])
    mom2 = jnp.concatenate(
        [MU * gm2t[q] + res2[q * CLS_PAD:(q + 1) * CLS_PAD, :] for q in range(NAR)], axis=1
    )
    for q in range(NAR):
        x2s[q] = mom2[:, q * 128:(q + 1) * 128]
    o_mom2[...] = x2s[y][0:CLS, :]
    x2 = mom2 * (1.0 / (jnp.sqrt(jnp.sum(mom2 * mom2, keepdims=True)) + 1e-07))
    for _ in range(3):
        x2 = ns_step(x2)
    add_up(pay1, res1, 0, P1, ag_send.at[1], ag_recv.at[1])
    for _ in range(NS_ITERS - 3):
        x2 = ns_step(x2)
    for q in range(NAR):
        x2s[q] = x2[:, q * 128:(q + 1) * 128]
    second = w2own[...] * (1.0 - WDECAY) - (2 * HID / CLS) ** 0.5 * x2s[y][0:CLS, :]
    o_second[...] = second
    o_slow[...] = second.astype(BF)

    take(res1, 0, P1, ag_recv.at[1])
    grad1 = jnp.concatenate([res1[0:256, :], res1[256:512, :]], axis=1)
    mom1 = MU * gm1[...].reshape(2 * D_IN, HID) + grad1
    x1s[...] = mom1
    block64 = pl.ds(pl.multiple_of(y * 64, 64), 64)
    o_mom1[...] = x1s[block64, :]
    x1 = mom1 * (1.0 / (jnp.sqrt(jnp.sum(mom1 * mom1, keepdims=True)) + 1e-07))
    for _ in range(NS_ITERS):
        x1 = ns_step(x1)
    x1s[...] = x1
    first_new = w1own[...] * (1.0 - WDECAY) - x1s[block64, :]
    o_first[...] = first_new
    o_flow[...] = first_new.astype(BF)

    gb = res1[512:516, :] + res1[516:520, :]
    m_new = BETA_ONE * biasm[...] + (1.0 - BETA_ONE) * gb
    v_new = BETA_TWO * biasv[...] + (1.0 - BETA_TWO) * gb * gb
    m_hat = m_new / (1.0 - BETA_ONE**STEP)
    v_hat = v_new / (1.0 - BETA_TWO**STEP)
    o_bias[...] = bias[...] * (1.0 - LR_BIAS * WDECAY) - LR_BIAS * m_hat / (jnp.sqrt(v_hat) + EPSILON)
    o_bm[...] = m_new
    o_bv[...] = v_new
    o_loss[...] = res1[520:521, :] + res1[521:522, :]

    for b in range(8):
        blk = gbuf.at[y, :, b * 256:(b + 1) * 256]
        link(blk, blk, h_send.at[0, b], h_recv.at[0, b], right).wait_send()
        link(blk, blk, h_send.at[1, b], h_recv.at[1, b], left).wait_send()
        blk = gbuf.at[opp, :, b * 256:(b + 1) * 256]
        link(blk, blk, h_send.at[2, b], h_recv.at[2, b], right).wait_send()
    swap_sent(rbuf, r_send, r_recv, 128)
    swap_sent(dbuf, d_send, d_recv, 96)

    owner = my_piece < PIECES

    @pl.when(owner)
    def _():
        gone = inbox.at[pl.ds(0, PIECES - 1)]
        pltpu.make_async_copy(gone, gone, rs_send).wait()

    @pl.when(jnp.logical_not(owner))
    def _():
        gone = inbox.at[pl.ds(0, PIECES)]
        pltpu.make_async_copy(gone, gone, rs_send).wait()

    for n, (lo, hi) in enumerate(((P1, PIECES), (0, P1))):
        @pl.when((my_piece >= lo) & (my_piece < hi))
        def _():
            gone = mine.at[pl.ds(0, DEV - 1)]
            pltpu.make_async_copy(gone, gone, ag_send.at[n]).wait()


def step(idx, inv, pulled, gw1, gw2t, gm1, gm2t, idx2, gidx2, labels, live, bias, biasm, biasv, w1own, w2own):
    vm = pl.BlockSpec(memory_space=pltpu.VMEM)
    sm = pl.BlockSpec(memory_space=pltpu.SMEM)
    dma = pltpu.SemaphoreType.DMA
    sds = jax.ShapeDtypeStruct
    return pl.pallas_call(
        step_kernel,
        out_shape=[
            sds((1, 128), F32), sds((64, HID), F32), sds((CLS, 128), F32), sds((64, HID), F32), sds((CLS, 128), F32),
            sds((64, HID), BF), sds((CLS, 128), BF), sds((4, 128), F32), sds((4, 128), F32), sds((4, 128), F32),
        ],
        in_specs=[sm, sm] + [vm] * 14,
        out_specs=[vm] * 10,
        scratch_shapes=[
            pltpu.VMEM((SRC + 8, D_IN), F32),
            pltpu.VMEM((FRONT, D_IN), F32),
            pltpu.VMEM((FRONT, D_IN), F32),
            pltpu.VMEM((FRONT, 2 * D_IN), BF),
            pltpu.VMEM((HID, FRONT), F32),
            pltpu.VMEM((NAR, HID, FRONT), BF),
            pltpu.VMEM((SRC, 2 * SEED), BF),
            pltpu.VMEM((NAR, FRONT, 2 * SEED), BF),
            pltpu.VMEM((NAR, HID, SEED), BF),
            pltpu.VMEM((NAR, CLS_PAD, SEED), BF),
            pltpu.VMEM((HID, FRONT), F32),
            pltpu.VMEM((HID, 2 * D_IN), BF),
            pltpu.VMEM((2 * HID, CLS_PAD), BF),
            pltpu.VMEM((HID, 128), F32),
            pltpu.VMEM((HID, 128), F32),
            pltpu.VMEM((P1 * 16, 128), BF),
            pltpu.VMEM((P2 * 16, 128), BF),
            pltpu.VMEM((16, 128), F32),
            pltpu.VMEM((DEV, 16, 128), BF),
            pltpu.VMEM((P1 * 16, 128), F32),
            pltpu.VMEM((P2 * 16, 128), F32),
            pltpu.VMEM((DEV, 16, 128), F32),
            pltpu.VMEM((2 * D_IN, HID), F32),
            pltpu.VMEM((NAR, CLS_PAD, 128), F32),
            dma((3, 8)), dma((3, 8)), dma((4,)), dma((4,)), dma((4,)), dma((4,)), dma, dma, dma((2,)), dma((2,)),
        ],
        compiler_params=pltpu.CompilerParams(
            collective_id=1, has_side_effects=True, vmem_limit_bytes=62 * 2**20
        ),
    )(idx, inv, pulled, gw1, gw2t, gm1, gm2t, idx2, gidx2, labels, live, bias, biasm, biasv, w1own, w2own)


def as_rows(v):
    return jnp.pad(v, (0, 512 - v.shape[0])).reshape(4, 128)


def per_device(
    features, requests, index_one, mask_one, index_two, mask_two, labels, seed_live,
    w_first, w_second, mom_first, mom_second, biases, bias_m, bias_v,
):
    idx_one, msk_one = index_one.T, mask_one.T
    idx_two, msk_two = index_two.T, mask_two.T
    idx_one = jnp.concatenate([idx_one[:1], jnp.where(msk_one > 0, idx_one[1:], SRC)], axis=0)
    inv_one = 1.0 / jnp.maximum(jnp.sum(msk_one.astype(F32), axis=0, keepdims=True), 1.0)
    idx_two = jnp.concatenate(
        [idx_two[:1], jnp.where(msk_two > 0, idx_two[1:], -1), jnp.zeros((5, SEED), jnp.int32)], axis=0
    )
    w2t = jnp.pad(w_second.astype(BF).T, ((0, CLS_PAD - CLS), (0, 0)))
    m2t = jnp.pad(mom_second.T, ((0, CLS_PAD - CLS), (0, 0)))
    req = jnp.pad(requests, ((0, 0), (0, 64))).reshape(DEV, 1, 128)
    pulled, gw1, gw2t, gm1, gm2t, gidx2 = pull(
        req, features, w_first.astype(BF), w2t, mom_first, m2t, idx_two
    )
    loss, first_new, second_new, mom_one, mom_two, first_low, second_low, bias_new, m_new, v_new = step(
        idx_one, inv_one, pulled, gw1, gw2t, gm1, gm2t, idx_two, gidx2, labels[None, :], seed_live[None, :],
        as_rows(biases), as_rows(bias_m), as_rows(bias_v), w_first, w_second.T,
    )
    n = HID + CLS
    return (
        loss[0, 0], first_new, second_new.T, mom_one, mom_two.T, first_low, second_low.T,
        bias_new.reshape(512)[:n], m_new.reshape(512)[:n], v_new.reshape(512)[:n],
    )


def solution(mesh):
    both = ("grp", "nar")
    placed = (
        P(both, None), P(both, None), P(both, None), P(both, None), P(both, None), P(both, None),
        P(both), P(both), P("nar", None), P("nar", None), P("nar", None), P("nar", None), P(), P(), P(),
    )
    nar = P("nar", None)
    return jax.shard_map(
        per_device, mesh=mesh, in_specs=placed,
        out_specs=(P(), nar, nar, nar, nar, nar, nar, P(), P(), P()), check_vma=False,
    )
```

```python
import functools

import jax
import jax.numpy as jnp
from jax import lax
from jax.experimental import pallas as pl
from jax.experimental.pallas import tpu as pltpu
from jax.sharding import PartitionSpec as P

HID = 256
CLS = 172
CLS_PAD = 176
D_IN = 128
F1 = 15
F2 = 10
NS_ITERS = 5
STEP = 10
LAM = 0.5
MU = 0.95
WDECAY = 0.01
LR_BIAS = 0.05
BETA_ONE = 0.9
BETA_TWO = 0.999
EPSILON = 1e-08
NS_A = 3.4445
NS_B = -4.775
NS_C = 2.0315
HIGH = lax.Precision.HIGHEST
MESH = pl.DeviceIdType.MESH
BF = jnp.bfloat16
F32 = jnp.float32

DEV = 128
NAR = 4
OWN = 8192
CAP = 64
SRC = 8192
FRONT = 2048
SEED = 512


def all_to(t):
    return (t // NAR, t % NAR)


P1 = 33
P2 = 44
PIECES = P1 + P2
SEEDS_ALL = SEED * DEV


def dot(a, b, dims=((1,), (0,))):
    return lax.dot_general(a, b, (dims, ((), ())), preferred_element_type=F32)


NN = ((1,), (0,))
NT = ((1,), (1,))


def split(a):
    hi = a.astype(BF)
    return hi, (a - hi.astype(F32)).astype(BF)


def dot3(a, b, dims):
    (ah, al), (bh, bl) = a, b
    return dot(ah, bh, dims) + (dot(ah, bl, dims) + dot(al, bh, dims))


def ns_step(x):
    xs = split(x)
    gram = dot3(xs, xs, NT)
    gs = split(gram)
    mix = NS_B * gram + NS_C * dot3(gs, gs, NN)
    return NS_A * x + dot3(split(mix), xs, NN)


def spread(row):
    return jnp.broadcast_to(row, (128, 128)).T


def main_kernel(
    reqt, feat, idx1t, msk1t, idx2t, msk2t, labels, live, w1, w2own, m1, m2own, bias,
    o_res1, o_gm1, o_mom2, o_x2,
    table, featb, pulled, stage, reqv, reqin, idxv, invv, near, own, a1, z1t, gbuf, fsel, bsel, rbuf, dbuf, dh1,
    gw1, gw2t, gm2t, gidx2, w1t, w2, b1c, b2c, pay1, pay2, misc, inbox, res2, x2s,
    reqs, idx, inv,
    feat_sem, loc_sem, req_send, req_recv, row_send, row_recv, nar_send, nar_recv,
    h_send, h_recv, r_send, r_recv, d_send, d_recv, rs_send, rs_recv, ag_send, ag_recv,
):
    g = lax.axis_index("grp")
    y = lax.axis_index("nar")
    me = g * NAR + y
    left, right, opp = (y + 3) % NAR, (y + 1) % NAR, (y + 2) % NAR

    load = pltpu.make_async_copy(feat, featb, feat_sem)
    load.start()

    barrier = pltpu.get_barrier_semaphore()

    def greet(i, c):
        pl.semaphore_signal(barrier, inc=1, device_id=all_to((me + i) % DEV), device_id_type=MESH)
        return c

    lax.fori_loop(1, DEV, greet, 0)

    def link(src, dst, ssem, rsem, to):
        return pltpu.make_async_remote_copy(
            src_ref=src, dst_ref=dst, send_sem=ssem, recv_sem=rsem, device_id=(g, to), device_id_type=MESH
        )

    reqv[...] = jnp.concatenate([reqt[...], jnp.zeros((DEV - CAP, DEV), jnp.int32)], axis=0).T
    ask_rows = reqv.reshape(DEV, 1, 128)
    got_rows = reqin.reshape(DEV, 1, 128)

    gw1[y] = w1[...].astype(BF)
    pad = CLS_PAD - CLS
    gw2t[y] = jnp.concatenate([w2own[...], jnp.zeros((pad, 128), F32)], axis=0).astype(BF)
    o_gm1[y] = m1[...]
    gm2t[y] = jnp.concatenate([m2own[...], jnp.zeros((pad, 128), F32)], axis=0)
    gidx2[y] = jnp.concatenate(
        [idx2t[0:1, :], jnp.where(msk2t[...] > 0, idx2t[1:, :], -1), jnp.zeros((5, SEED), jnp.int32)], axis=0
    )
    shared = (gidx2, gw1, gw2t, o_gm1, gm2t)

    pl.semaphore_wait(barrier, DEV - 1)

    def ask(i, c):
        t = (me + i * 37) % DEV
        pltpu.make_async_remote_copy(
            src_ref=ask_rows.at[t], dst_ref=got_rows.at[me], send_sem=req_send, recv_sem=req_recv,
            device_id=all_to(t), device_id_type=MESH,
        ).start()
        return c

    lax.fori_loop(1, DEV, ask, 0)
    for n, a in enumerate(shared):
        for d in range(1, NAR):
            link(a.at[y], a.at[y], nar_send.at[n, d - 1], nar_recv.at[n, d - 1], (y + d) % NAR).start()

    reqin[pl.ds(me, 1), :] = reqv[pl.ds(me, 1), :]
    msk = msk1t[...]
    idxv[0:1, :] = idx1t[0:1, :]
    idxv[1:16, :] = jnp.where(msk > 0, idx1t[1:16, :], SRC)
    invv[...] = 1.0 / jnp.maximum(jnp.sum(msk.astype(F32), axis=0, keepdims=True), 1.0)
    to_smem = [pltpu.make_async_copy(idxv, idx, loc_sem.at[0]), pltpu.make_async_copy(invv, inv, loc_sem.at[1])]
    for c in to_smem:
        c.start()

    load.wait()

    def widen_features(i, c):
        rows = pl.ds(pl.multiple_of(i * 256, 256), 256)
        table[rows, :] = featb[rows, :].astype(F32)
        return c

    lax.fori_loop(0, OWN // 256, widen_features, 0)

    got = got_rows.at[pl.ds(0, DEV - 1)]
    pltpu.make_async_copy(got, got, req_recv).wait()
    fetch = pltpu.make_async_copy(reqin, reqs, loc_sem.at[2])
    fetch.start()
    fetch.wait()

    view = table.reshape(SRC + 8, 1, D_IN)
    my_rows = pl.ds(pl.multiple_of(me * CAP, CAP), CAP)

    def serve(i, c):
        t = (me + i * 37) % DEV
        for r in range(CAP):
            stage[r:r + 1, :] = view[reqs[t, r]]
        slot = pl.ds(pl.multiple_of(i * CAP, CAP), CAP)
        featb[slot, :] = stage[...].astype(BF)

        @pl.when(i > 0)
        def _():
            pltpu.make_async_remote_copy(
                src_ref=featb.at[slot], dst_ref=pulled.at[my_rows],
                send_sem=row_send, recv_sem=row_recv, device_id=all_to(t), device_id_type=MESH,
            ).start()

        return c

    lax.fori_loop(1, DEV, serve, 0)
    serve(0, 0)
    pulled[my_rows, :] = featb[0:CAP, :]

    for n, a in enumerate(shared):
        for d in range(1, NAR):
            link(a.at[y], a.at[y], nar_send.at[n, d - 1], nar_recv.at[n, d - 1], (y + d) % NAR).wait()
    w1t[...] = gw1[...].reshape(2 * D_IN, HID).T
    w2t = jnp.concatenate([gw2t[q] for q in range(NAR)], axis=1)
    w2[...] = w2t.T
    b1c[...] = jnp.concatenate([spread(bias[0:1, 0:128]), spread(bias[0:1, 128:256])], axis=0)
    last = jnp.concatenate([bias[0:1, 384:428], jnp.zeros((1, 84), F32)], axis=1)
    b2c[...] = jnp.concatenate([spread(bias[0:1, 256:384]), spread(last)], axis=0)

    iota16 = lax.broadcasted_iota(jnp.int32, (16, 128), 0).astype(jnp.int16)
    one, zero = jnp.ones((16, 128), BF), jnp.zeros((16, 128), BF)

    def select(ids, base, groups, put):
        ids = ids - base
        rows = [
            [jnp.broadcast_to(ids[k:k + 1, c * 128:(c + 1) * 128], (16, 128)).astype(jnp.int16) for c in range(4)]
            for k in range(1 + F2)
        ]

        def body(i, carry):
            here = iota16 + jnp.full((16, 128), i * 16, jnp.int32).astype(jnp.int16)
            out = pl.ds(pl.multiple_of(i * 16, 16), 16)
            for c in range(4):
                acc = jnp.where(here == rows[1][c], one, zero)
                for k in range(2, 1 + F2):
                    acc = acc + jnp.where(here == rows[k][c], one, zero)
                put(out, c * 128, acc)
                put(out, SEED + c * 128, jnp.where(here == rows[0][c], one, zero))
            return carry

        lax.fori_loop(0, groups, body, 0)

    def put_f(rows, col, v):
        fsel[rows, col:col + 128] = v

    select(gidx2[y], 0, SRC // 16, put_f)
    for q in range(NAR):
        def put_b(rows, col, v, q=q):
            bsel[q, rows, col:col + 128] = v

        select(gidx2[q], y * FRONT, FRONT // 16, put_b)

    come = pulled.at[pl.ds(0, (DEV - 1) * CAP)]
    pltpu.make_async_copy(come, come, row_recv).wait()
    gone = featb.at[pl.ds(0, (DEV - 1) * CAP)]
    pltpu.make_async_copy(gone, gone, row_send).wait()
    sent = ask_rows.at[pl.ds(0, DEV - 1)]
    pltpu.make_async_copy(sent, sent, req_send).wait()

    def widen(i, c):
        rows = pl.ds(pl.multiple_of(i * 256, 256), 256)
        table[rows, :] = pulled[rows, :].astype(F32)
        return c

    lax.fori_loop(0, SRC // 256, widen, 0)
    table[SRC:SRC + 8, :] = jnp.zeros((8, D_IN), F32)
    for c in to_smem:
        c.wait()

    def cols(b):
        return pl.ds(pl.multiple_of(b * 256, 256), 256)

    def forward(b):
        @pl.when(b % 2 == 0)
        def _():
            blk = gbuf.at[left, :, cols(b)]
            link(blk, blk, h_send.at[0, b], h_recv.at[0, b], right).wait_recv()
            link(blk, blk, h_send.at[2, b], h_recv.at[2, b], right).start()

        @pl.when(b % 2 == 1)
        def _():
            blk = gbuf.at[right, :, cols(b)]
            link(blk, blk, h_send.at[1, b], h_recv.at[1, b], left).wait_recv()
            link(blk, blk, h_send.at[2, b], h_recv.at[2, b], left).start()

    def block(b, c):
        def some(i, c2):
            base = pl.multiple_of(b * 256 + i * 8, 8)
            for j in range(8):
                m = base + j
                here = pl.ds(pl.multiple_of(i * 8, 8) + j, 1)
                own[here, :] = view[idx[0, m]]
                rows = [view[idx[1 + k, m]] for k in range(F1)]
                while len(rows) > 1:
                    rows = [p + q for p, q in zip(rows[::2], rows[1::2])] + ([rows[-1]] if len(rows) % 2 else [])
                near[here, :] = rows[0] * inv[0, m]
            return c2

        lax.fori_loop(0, 32, some, 0)
        rows = cols(b)
        act = jnp.concatenate([own[...].astype(BF), near[...].astype(BF)], axis=1)
        a1[rows, :] = act
        z = dot(w1t[...], act, NT) + jnp.concatenate([b1c[...], b1c[...]], axis=1)
        z1t[:, rows] = z
        gbuf[y, :, rows] = (z / (1.0 + jnp.exp(-z))).astype(BF)
        blk = gbuf.at[y, :, rows]
        link(blk, blk, h_send.at[0, b], h_recv.at[0, b], right).start()
        link(blk, blk, h_send.at[1, b], h_recv.at[1, b], left).start()

        @pl.when(b > 0)
        def _():
            forward(b - 1)

        return c

    lax.fori_loop(0, 8, block, 0)
    forward(7)

    def from_source(q):
        return dot(gbuf[q], fsel[pl.ds(pl.multiple_of(q * FRONT, FRONT), FRONT), :])

    total = from_source(y)
    for b in range(1, 8, 2):
        blk = gbuf.at[left, :, b * 256:(b + 1) * 256]
        link(blk, blk, h_send.at[0, b], h_recv.at[0, b], right).wait_recv()
    total = total + from_source(left)
    for b in range(0, 8, 2):
        blk = gbuf.at[right, :, b * 256:(b + 1) * 256]
        link(blk, blk, h_send.at[1, b], h_recv.at[1, b], left).wait_recv()
    total = total + from_source(right)
    for b in range(8):
        blk = gbuf.at[opp, :, b * 256:(b + 1) * 256]
        link(blk, blk, h_send.at[2, b], h_recv.at[2, b], right).wait_recv()
    total = total + from_source(opp)

    def inverse_count(ids):
        n = jnp.sum((ids[1:1 + F2, :] >= 0).astype(F32), axis=0, keepdims=True)
        return 1.0 / jnp.maximum(n, 1.0)

    near2 = (total[:, :SEED] * inverse_count(gidx2[y])).astype(BF)
    self2 = total[:, SEED:].astype(BF)
    alive = live[...].astype(F32)
    diff = self2.astype(F32) - near2.astype(F32)

    def swap_start(buf, ssem, rsem):
        blk = buf.at[y]
        link(blk, blk, ssem.at[0], rsem.at[0], right).start()
        link(blk, blk, ssem.at[1], rsem.at[1], left).start()

    def swap_forward(buf, ssem, rsem, cut):
        blk = buf.at[left]
        link(blk, blk, ssem.at[0], rsem.at[0], right).wait_recv()
        half = buf.at[left, 0:cut, :]
        link(half, half, ssem.at[2], rsem.at[2], right).start()
        blk = buf.at[right]
        link(blk, blk, ssem.at[1], rsem.at[1], left).wait_recv()
        half = buf.at[right, cut:, :]
        link(half, half, ssem.at[3], rsem.at[3], left).start()

    def swap_end(buf, ssem, rsem, cut):
        half = buf.at[opp, 0:cut, :]
        link(half, half, ssem.at[2], rsem.at[2], right).wait_recv()
        half = buf.at[opp, cut:, :]
        link(half, half, ssem.at[3], rsem.at[3], left).wait_recv()

    def swap_sent(buf, ssem, rsem, cut):
        blk = buf.at[y]
        link(blk, blk, ssem.at[0], rsem.at[0], right).wait_send()
        link(blk, blk, ssem.at[1], rsem.at[1], left).wait_send()
        half = buf.at[left, 0:cut, :]
        link(half, half, ssem.at[2], rsem.at[2], right).wait_send()
        half = buf.at[right, cut:, :]
        link(half, half, ssem.at[3], rsem.at[3], left).wait_send()

    rbuf[y] = (2.0 * LAM / HID / SEEDS_ALL * alive * diff).astype(BF)
    swap_start(rbuf, r_send, r_recv)

    act2 = jnp.concatenate([self2, near2], axis=0)
    w2t = jnp.concatenate([gw2t[q] for q in range(NAR)], axis=1)
    cls = lax.broadcasted_iota(jnp.int32, (CLS_PAD, SEED), 0)
    b2 = b2c[0:CLS_PAD, :]
    logits = dot(w2t, act2) + jnp.concatenate([b2] * 4, axis=1)
    logits = jnp.where(cls < CLS, logits, -1e30)
    top = jnp.max(logits, axis=0, keepdims=True)
    e = jnp.exp(logits - top)
    tot = jnp.sum(e, axis=0, keepdims=True)
    hot = cls == labels[...]
    picked = jnp.sum(jnp.where(hot, logits, 0.0), axis=0, keepdims=True)
    dlog = (alive * (e * (1.0 / tot) - jnp.where(hot, 1.0, 0.0)) * (1.0 / SEEDS_ALL)).astype(BF)
    dbuf[y] = dlog
    swap_start(dbuf, d_send, d_recv)

    terms = top + jnp.log(tot) - picked + LAM / HID * jnp.sum(diff * diff, axis=0, keepdims=True)
    loss = jnp.sum(alive * terms, axis=1, keepdims=True)
    g2t = dot(dlog, act2, NT).astype(BF)
    for q in range(NAR):
        pay2[q * CLS_PAD:(q + 1) * CLS_PAD, :] = g2t[:, q * 128:(q + 1) * 128]

    my_piece = (me * 77) % DEV

    def to_owner(pay, first, count):
        def body(i, c):
            t = (me + i) % DEV
            p = (t * 77) % DEV - first

            @pl.when((p >= 0) & (p < count))
            def _():
                pltpu.make_async_remote_copy(
                    src_ref=pay.at[pl.ds(pl.multiple_of(p * 16, 16), 16)], dst_ref=inbox.at[me],
                    send_sem=rs_send, recv_sem=rs_recv, device_id=all_to(t), device_id_type=MESH,
                ).start()

            return c

        lax.fori_loop(1, DEV, body, 0)

    def add_up(pay, res, first, count, ssem, rsem):
        q = my_piece - first

        @pl.when((q >= 0) & (q < count))
        def _():
            rows16 = pl.ds(pl.multiple_of(q * 16, 16), 16)
            got = inbox.at[pl.ds(0, DEV - 1)]
            pltpu.make_async_copy(got, got, rs_recv).wait()
            inbox[me] = pay[rows16, :]

            def body(i, acc):
                part = inbox[pl.ds(pl.multiple_of(i * 8, 8), 8)].astype(F32)
                return acc + jnp.sum(part, axis=0)

            res[rows16, :] = lax.fori_loop(0, DEV // 8, body, jnp.zeros((16, 128), F32))

            def tell(i, c):
                pltpu.make_async_remote_copy(
                    src_ref=res.at[rows16], dst_ref=res.at[rows16],
                    send_sem=ssem, recv_sem=rsem, device_id=all_to((me + i) % DEV), device_id_type=MESH,
                ).start()
                return c

            lax.fori_loop(1, DEV, tell, 0)

    def take(res, first, count, rsem):
        q = my_piece - first
        holds = (q >= 0) & (q < count)

        @pl.when(holds)
        def _():
            got = res.at[pl.ds(0, (count - 1) * 16)]
            pltpu.make_async_copy(got, got, rsem).wait()

        @pl.when(jnp.logical_not(holds))
        def _():
            got = res.at[pl.ds(0, count * 16)]
            pltpu.make_async_copy(got, got, rsem).wait()

    to_owner(pay2, P1, P2)

    def grads(q):
        da = dot(w2[...], dbuf[q])
        r = rbuf[q].astype(F32)
        ds = (da[:HID] + r).astype(BF)
        dn = ((da[HID:] - r) * inverse_count(gidx2[q])).astype(BF)
        return dot(jnp.concatenate([dn, ds], axis=1), bsel[q], NT)

    swap_forward(rbuf, r_send, r_recv, 128)
    dh1[...] = grads(y)
    swap_forward(dbuf, d_send, d_recv, 96)
    dh1[...] += grads(left)
    dh1[...] += grads(right)
    swap_end(rbuf, r_send, r_recv, 128)
    swap_end(dbuf, d_send, d_recv, 96)
    dh1[...] += grads(opp)
    add_up(pay2, res2, P1, P2, ag_send.at[0], ag_recv.at[0])

    z = z1t[...]
    sig = 1.0 / (1.0 + jnp.exp(-z))
    dz = (dh1[...] * sig * (1.0 + z * (1.0 - sig))).astype(BF)
    g1 = dot(dz, a1[...]).T.astype(BF)
    pay1[0:256, :] = g1[:, :128]
    pay1[256:512, :] = g1[:, 128:]
    ones_f = jnp.ones((8, FRONT), BF)
    ones_s = jnp.ones((8, SEED), BF)
    db1 = dot(ones_f, dz, NT)[0:1, :]
    db2 = dot(ones_s, dlog, NT)[0:1, :]
    misc[...] = jnp.zeros((16, 128), F32)

    def two(rows, v):
        hi = v.astype(BF).astype(F32)
        misc[rows:rows + 1, 0:v.shape[1]] = hi
        misc[rows + 4:rows + 5, 0:v.shape[1]] = v - hi

    two(0, db1[:, :128])
    two(1, db1[:, 128:])
    two(2, db2[:, :128])
    two(3, db2[:, 128:])
    hi = loss.astype(BF).astype(F32)
    misc[8:9, 0:1] = hi
    misc[9:10, 0:1] = loss - hi
    pay1[512:528, :] = misc[...].astype(BF)
    to_owner(pay1, 0, P1)

    take(res2, P1, P2, ag_recv.at[0])
    mom2 = jnp.concatenate(
        [MU * gm2t[q] + res2[q * CLS_PAD:(q + 1) * CLS_PAD, :] for q in range(NAR)], axis=1
    )
    for q in range(NAR):
        x2s[q] = mom2[:, q * 128:(q + 1) * 128]
    o_mom2[...] = x2s[y]
    x2 = mom2 * (1.0 / (jnp.sqrt(jnp.sum(mom2 * mom2, keepdims=True)) + 1e-07))
    for _ in range(3):
        x2 = ns_step(x2)
    add_up(pay1, o_res1, 0, P1, ag_send.at[1], ag_recv.at[1])
    for _ in range(NS_ITERS - 3):
        x2 = ns_step(x2)
    for q in range(NAR):
        x2s[q] = x2[:, q * 128:(q + 1) * 128]
    o_x2[...] = x2s[y]
    take(o_res1, 0, P1, ag_recv.at[1])

    for b in range(8):
        blk = gbuf.at[y, :, b * 256:(b + 1) * 256]
        link(blk, blk, h_send.at[0, b], h_recv.at[0, b], right).wait_send()
        link(blk, blk, h_send.at[1, b], h_recv.at[1, b], left).wait_send()
        blk = gbuf.at[opp, :, b * 256:(b + 1) * 256]
        link(blk, blk, h_send.at[2, b], h_recv.at[2, b], right).wait_send()
    swap_sent(rbuf, r_send, r_recv, 128)
    swap_sent(dbuf, d_send, d_recv, 96)

    owner = my_piece < PIECES

    @pl.when(owner)
    def _():
        gone = inbox.at[pl.ds(0, PIECES - 1)]
        pltpu.make_async_copy(gone, gone, rs_send).wait()

    @pl.when(jnp.logical_not(owner))
    def _():
        gone = inbox.at[pl.ds(0, PIECES)]
        pltpu.make_async_copy(gone, gone, rs_send).wait()

    for n, (lo, hi) in enumerate(((P1, PIECES), (0, P1))):
        @pl.when((my_piece >= lo) & (my_piece < hi))
        def _():
            gone = table.at[pl.ds(0, (DEV - 1) * 16)]
            pltpu.make_async_copy(gone, gone, ag_send.at[n]).wait()


def main(reqt, feat, idx1t, msk1t, idx2t, msk2t, labels, live, w1, w2own, m1, m2own, bias):
    vm = pl.BlockSpec(memory_space=pltpu.VMEM)
    dma = pltpu.SemaphoreType.DMA
    sds = jax.ShapeDtypeStruct
    V = pltpu.VMEM
    return pl.pallas_call(
        main_kernel,
        out_shape=[
            sds((P1 * 16, 128), F32), sds((NAR, 64, HID), F32), sds((CLS_PAD, 128), F32), sds((CLS_PAD, 128), F32),
        ],
        in_specs=[vm, pl.BlockSpec(memory_space=pl.ANY)] + [vm] * 11,
        out_specs=[vm] * 4,
        scratch_shapes=[
            V((SRC + 8, D_IN), F32),
            V((OWN, D_IN), BF),
            V((SRC, D_IN), BF),
            V((CAP, D_IN), F32),
            V((DEV, 128), jnp.int32),
            V((DEV, 128), jnp.int32),
            V((16, FRONT), jnp.int32),
            V((1, FRONT), F32),
            V((256, D_IN), F32),
            V((256, D_IN), F32),
            V((FRONT, 2 * D_IN), BF),
            V((HID, FRONT), F32),
            V((NAR, HID, FRONT), BF),
            V((SRC, 2 * SEED), BF),
            V((NAR, FRONT, 2 * SEED), BF),
            V((NAR, HID, SEED), BF),
            V((NAR, CLS_PAD, SEED), BF),
            V((HID, FRONT), F32),
            V((NAR, 64, HID), BF),
            V((NAR, CLS_PAD, 128), BF),
            V((NAR, CLS_PAD, 128), F32),
            V((NAR, 16, SEED), jnp.int32),
            V((HID, 2 * D_IN), BF),
            V((2 * HID, CLS_PAD), BF),
            V((HID, 128), F32),
            V((HID, 128), F32),
            V((P1 * 16, 128), BF),
            V((P2 * 16, 128), BF),
            V((16, 128), F32),
            V((DEV, 16, 128), BF),
            V((P2 * 16, 128), F32),
            V((NAR, CLS_PAD, 128), F32),
            pltpu.SMEM((DEV, 128), jnp.int32),
            pltpu.SMEM((16, FRONT), jnp.int32),
            pltpu.SMEM((1, FRONT), F32),
            dma, dma((3,)), dma, dma, dma, dma, dma((5, 3)), dma((5, 3)),
            dma((3, 8)), dma((3, 8)), dma((4,)), dma((4,)), dma((4,)), dma((4,)), dma, dma, dma((2,)), dma((2,)),
        ],
        compiler_params=pltpu.CompilerParams(
            collective_id=0, has_side_effects=True, vmem_limit_bytes=62 * 2**20
        ),
    )(reqt, feat, idx1t, msk1t, idx2t, msk2t, labels, live, w1, w2own, m1, m2own, bias)


def update_kernel(
    res1, gm1, mom2, x2, w1own, w2own, bias, biasm, biasv,
    o_loss, o_first, o_second, o_mom1, o_mom2, o_flow, o_slow, o_bias, o_bm, o_bv,
    x1s,
):
    y = lax.axis_index("nar")
    grad1 = jnp.concatenate([res1[0:256, :], res1[256:512, :]], axis=1)
    mom1 = MU * gm1[...].reshape(2 * D_IN, HID) + grad1
    x1s[...] = mom1
    block64 = pl.ds(pl.multiple_of(y * 64, 64), 64)
    o_mom1[...] = x1s[block64, :]
    x1 = mom1 * (1.0 / (jnp.sqrt(jnp.sum(mom1 * mom1, keepdims=True)) + 1e-07))
    for _ in range(NS_ITERS):
        x1 = ns_step(x1)
    x1s[...] = x1
    first_new = w1own[...] * (1.0 - WDECAY) - x1s[block64, :]
    o_first[...] = first_new
    o_flow[...] = first_new.astype(BF)
    second = w2own[...] * (1.0 - WDECAY) - (2 * HID / CLS) ** 0.5 * x2[0:CLS, :]
    o_second[...] = second
    o_slow[...] = second.astype(BF)
    o_mom2[...] = mom2[0:CLS, :]

    gb = res1[512:516, :] + res1[516:520, :]
    gb = jnp.concatenate([gb[0:1, :], gb[1:2, :], gb[2:3, :], gb[3:4, 0:44]], axis=1)
    m_new = BETA_ONE * biasm[...] + (1.0 - BETA_ONE) * gb
    v_new = BETA_TWO * biasv[...] + (1.0 - BETA_TWO) * gb * gb
    m_hat = m_new / (1.0 - BETA_ONE**STEP)
    v_hat = v_new / (1.0 - BETA_TWO**STEP)
    o_bias[...] = bias[...] * (1.0 - LR_BIAS * WDECAY) - LR_BIAS * m_hat / (jnp.sqrt(v_hat) + EPSILON)
    o_bm[...] = m_new
    o_bv[...] = v_new
    o_loss[...] = res1[520:521, 0:1] + res1[521:522, 0:1]


def update(*args):
    vm = pl.BlockSpec(memory_space=pltpu.VMEM)
    sds = jax.ShapeDtypeStruct
    return pl.pallas_call(
        update_kernel,
        out_shape=[
            sds((1, 1), F32), sds((64, HID), F32), sds((CLS, 128), F32), sds((64, HID), F32), sds((CLS, 128), F32),
            sds((64, HID), BF), sds((CLS, 128), BF), sds((1, 428), F32), sds((1, 428), F32), sds((1, 428), F32),
        ],
        in_specs=[vm] * 9,
        out_specs=[vm] * 10,
        scratch_shapes=[pltpu.VMEM((2 * D_IN, HID), F32)],
        compiler_params=pltpu.CompilerParams(vmem_limit_bytes=32 * 2**20),
    )(*args)


def per_device(
    features, requests, index_one, mask_one, index_two, mask_two, labels, seed_live,
    w_first, w_second, mom_first, mom_second, biases, bias_m, bias_v,
):
    w2own, bias = w_second.T, biases[None, :]
    res1, gm1, mom2, x2 = main(
        requests.T, features, index_one.T, mask_one.T, index_two.T, mask_two.T, labels[None, :], seed_live[None, :],
        w_first, w2own, mom_first, mom_second.T, bias,
    )
    loss, first_new, second_new, mom_one, mom_two, first_low, second_low, bias_new, m_new, v_new = update(
        res1, gm1, mom2, x2, w_first, w2own, bias, bias_m[None, :], bias_v[None, :]
    )
    return (
        loss.reshape(()), first_new, second_new.T, mom_one, mom_two.T, first_low, second_low.T,
        bias_new.reshape(-1), m_new.reshape(-1), v_new.reshape(-1),
    )


def solution(mesh):
    both = ("grp", "nar")
    placed = (
        P(both, None), P(both, None), P(both, None), P(both, None), P(both, None), P(both, None),
        P(both), P(both), P("nar", None), P("nar", None), P("nar", None), P("nar", None), P(), P(), P(),
    )
    nar = P("nar", None)
    return jax.shard_map(
        per_device, mesh=mesh, in_specs=placed,
        out_specs=(P(), nar, nar, nar, nar, nar, nar, P(), P(), P()), check_vma=False,
    )
```

```python
import functools

import jax
import jax.numpy as jnp
from jax import lax
from jax.experimental import pallas as pl
from jax.experimental.pallas import tpu as pltpu
from jax.sharding import PartitionSpec as P

HID = 256
CLS = 172
CLS_PAD = 176
D_IN = 128
F1 = 15
F2 = 10
NS_ITERS = 5
STEP = 10
LAM = 0.5
MU = 0.95
WDECAY = 0.01
LR_BIAS = 0.05
BETA_ONE = 0.9
BETA_TWO = 0.999
EPSILON = 1e-08
NS_A = 3.4445
NS_B = -4.775
NS_C = 2.0315
HIGH = lax.Precision.HIGHEST
MESH = pl.DeviceIdType.MESH
BF = jnp.bfloat16
F32 = jnp.float32

DEV = 128
NAR = 4
OWN = 8192
CAP = 64
SRC = 8192
FRONT = 2048
SEED = 512


def all_to(t):
    return (t // NAR, t % NAR)


P1 = 33
P2 = 44
GRP = 32
ROW_G1 = P1 * 16
ROW_M2 = ROW_G1 + 512
ROW_X2 = ROW_M2 + CLS_PAD
ROWS = ROW_X2 + CLS_PAD
SEEDS_ALL = SEED * DEV


def dot(a, b, dims=((1,), (0,))):
    return lax.dot_general(a, b, (dims, ((), ())), preferred_element_type=F32)


NN = ((1,), (0,))
NT = ((1,), (1,))


def split(a):
    hi = a.astype(BF)
    return hi, (a - hi.astype(F32)).astype(BF)


def dot3(a, b, dims):
    (ah, al), (bh, bl) = a, b
    return dot(ah, bh, dims) + (dot(ah, bl, dims) + dot(al, bh, dims))


def ns_step(x):
    xs = split(x)
    gram = dot3(xs, xs, NT)
    gs = split(gram)
    mix = NS_B * gram + NS_C * dot3(gs, gs, NN)
    return NS_A * x + dot3(split(mix), xs, NN)


def spread(row):
    return jnp.broadcast_to(row, (128, 128)).T


def main_kernel(
    reqt, feat, idx1t, msk1t, idx2t, msk2t, labels, live, w1, w2own, m1, m2own, bias,
    o_all,
    table, featb, pulled, stage, reqv, reqin, idxv, invv, near, own, z1t, gbuf, fsel, bsel, idc, rbuf, dbuf,
    gw1, gw2t, gm1, gm2t, gidx2, w1t, w2, b1c, b2c, pay1, pay2, misc, inbox1, inbox2, ybox1, ybox2, res2, x2s,
    reqs, idx, inv,
    feat_sem, loc_sem, req_send, req_recv, row_send, row_recv, nar_send, nar_recv,
    h_send, h_recv, r_send, r_recv, d_send, d_recv, rs_send, rs_recv, y_send, y_recv, ag_send, ag_recv,
):
    a1, dh1 = pulled, table
    g = lax.axis_index("grp")
    y = lax.axis_index("nar")
    me = g * NAR + y
    left, right, opp = (y + 3) % NAR, (y + 1) % NAR, (y + 2) % NAR

    load = pltpu.make_async_copy(feat, featb, feat_sem)
    load.start()

    barrier = pltpu.get_barrier_semaphore()

    def greet(i, c):
        pl.semaphore_signal(barrier, inc=1, device_id=all_to((me + i) % DEV), device_id_type=MESH)
        return c

    lax.fori_loop(1, DEV, greet, 0)

    def link(src, dst, ssem, rsem, to):
        return pltpu.make_async_remote_copy(
            src_ref=src, dst_ref=dst, send_sem=ssem, recv_sem=rsem, device_id=(g, to), device_id_type=MESH
        )

    reqv[...] = jnp.concatenate([reqt[...], jnp.zeros((DEV - CAP, DEV), jnp.int32)], axis=0).T
    ask_rows = reqv.reshape(DEV, 1, 128)
    got_rows = reqin.reshape(DEV, 1, 128)

    gw1[y] = w1[...].astype(BF)
    pad = CLS_PAD - CLS
    gw2t[y] = jnp.concatenate([w2own[...], jnp.zeros((pad, 128), F32)], axis=0).astype(BF)
    gm1[y] = m1[...]
    gm2t[y] = jnp.concatenate([m2own[...], jnp.zeros((pad, 128), F32)], axis=0)
    gidx2[y] = jnp.concatenate(
        [idx2t[0:1, :], jnp.where(msk2t[...] > 0, idx2t[1:, :], -1), jnp.zeros((5, SEED), jnp.int32)], axis=0
    )
    shared = (gidx2, gw1, gw2t, gm1, gm2t)

    pl.semaphore_wait(barrier, DEV - 1)

    def ask(i, c):
        t = (me + i * 37) % DEV
        pltpu.make_async_remote_copy(
            src_ref=ask_rows.at[t], dst_ref=got_rows.at[me], send_sem=req_send, recv_sem=req_recv,
            device_id=all_to(t), device_id_type=MESH,
        ).start()
        return c

    lax.fori_loop(1, DEV, ask, 0)
    for n, a in enumerate(shared):
        for d in range(1, NAR):
            link(a.at[y], a.at[y], nar_send.at[n, d - 1], nar_recv.at[n, d - 1], (y + d) % NAR).start()

    reqin[pl.ds(me, 1), :] = reqv[pl.ds(me, 1), :]
    msk = msk1t[...]
    idxv[0:1, :] = idx1t[0:1, :]
    idxv[1:16, :] = jnp.where(msk > 0, idx1t[1:16, :], SRC)
    invv[...] = 1.0 / jnp.maximum(jnp.sum(msk.astype(F32), axis=0, keepdims=True), 1.0)
    to_smem = [pltpu.make_async_copy(idxv, idx, loc_sem.at[0]), pltpu.make_async_copy(invv, inv, loc_sem.at[1])]
    for c in to_smem:
        c.start()

    load.wait()

    def widen_features(i, c):
        rows = pl.ds(pl.multiple_of(i * 256, 256), 256)
        table[rows, :] = featb[rows, :].astype(F32)
        return c

    lax.fori_loop(0, OWN // 256, widen_features, 0)

    got = got_rows.at[pl.ds(0, DEV - 1)]
    pltpu.make_async_copy(got, got, req_recv).wait()
    fetch = pltpu.make_async_copy(reqin, reqs, loc_sem.at[2])
    fetch.start()
    fetch.wait()

    view = table.reshape(SRC + 8, 1, D_IN)
    my_rows = pl.ds(pl.multiple_of(me * CAP, CAP), CAP)

    def serve(i, c):
        t = (me + i * 37) % DEV
        for r in range(CAP):
            stage[r:r + 1, :] = view[reqs[t, r]]
        slot = pl.ds(pl.multiple_of(i * CAP, CAP), CAP)
        featb[slot, :] = stage[...].astype(BF)

        @pl.when(i > 0)
        def _():
            pltpu.make_async_remote_copy(
                src_ref=featb.at[slot], dst_ref=pulled.at[my_rows],
                send_sem=row_send, recv_sem=row_recv, device_id=all_to(t), device_id_type=MESH,
            ).start()

        return c

    lax.fori_loop(1, DEV, serve, 0)
    serve(0, 0)
    pulled[my_rows, :] = featb[0:CAP, :]

    for n, a in enumerate(shared):
        for d in range(1, NAR):
            link(a.at[y], a.at[y], nar_send.at[n, d - 1], nar_recv.at[n, d - 1], (y + d) % NAR).wait()
    w1t[...] = gw1[...].reshape(2 * D_IN, HID).T
    for q in range(NAR):
        o_all[ROW_G1 + q * 64:ROW_G1 + q * 64 + 64, :] = MU * gm1[q, :, 0:128]
        o_all[ROW_G1 + 256 + q * 64:ROW_G1 + 256 + q * 64 + 64, :] = MU * gm1[q, :, 128:256]
    w2t = jnp.concatenate([gw2t[q] for q in range(NAR)], axis=1)
    w2[...] = w2t.T
    b1c[...] = jnp.concatenate([spread(bias[0:1, 0:128]), spread(bias[0:1, 128:256])], axis=0)
    last = jnp.concatenate([bias[0:1, 384:428], jnp.zeros((1, 84), F32)], axis=1)
    b2c[...] = jnp.concatenate([spread(bias[0:1, 256:384]), spread(last)], axis=0)

    iota16 = lax.broadcasted_iota(jnp.int32, (16, 128), 0).astype(jnp.int16)
    one, zero = jnp.ones((16, 128), BF), jnp.zeros((16, 128), BF)

    def select(ids, base, groups, put):
        ids = ids - base
        rows = [
            [jnp.broadcast_to(ids[k:k + 1, c * 128:(c + 1) * 128], (16, 128)).astype(jnp.int16) for c in range(4)]
            for k in range(1 + F2)
        ]

        def body(i, carry):
            here = iota16 + jnp.full((16, 128), i * 16, jnp.int32).astype(jnp.int16)
            out = pl.ds(pl.multiple_of(i * 16, 16), 16)
            for c in range(4):
                acc = jnp.where(here == rows[1][c], one, zero)
                for k in range(2, 1 + F2):
                    acc = acc + jnp.where(here == rows[k][c], one, zero)
                put(out, c * 128, acc)
                put(out, SEED + c * 128, jnp.where(here == rows[0][c], one, zero))
            return carry

        lax.fori_loop(0, groups, body, 0)

    def put_f(rows, col, v):
        fsel[rows, col:col + 128] = v

    select(gidx2[y], 0, SRC // 16, put_f)
    lane16 = lax.broadcasted_iota(jnp.int32, (16, 128), 1).astype(jnp.int16)

    idc[...] = (jnp.concatenate([gidx2[q] for q in range(NAR)], axis=0) - y * FRONT).T

    def select_rows(q, group):
        at = pl.multiple_of(group * 16, 16)
        blk = idc[pl.ds(at, 16), :]
        want = [jnp.broadcast_to(blk[:, q * 16 + k:q * 16 + k + 1], (16, 128)).astype(jnp.int16) for k in range(1 + F2)]
        for c in range(FRONT // 128):
            here = lane16 + jnp.full((16, 128), c * 128, jnp.int32).astype(jnp.int16)
            acc = jnp.where(here == want[1], one, zero)
            for k in range(2, 1 + F2):
                acc = acc + jnp.where(here == want[k], one, zero)
            bsel[q, pl.ds(at, 16), c * 128:(c + 1) * 128] = acc
            bsel[q, pl.ds(SEED + at, 16), c * 128:(c + 1) * 128] = jnp.where(here == want[0], one, zero)

    for q in range(NAR):
        def all_rows(i, carry, q=q):
            select_rows(q, i)
            return carry

        lax.fori_loop(0, SEED // 16, all_rows, 0)

    come = pulled.at[pl.ds(0, (DEV - 1) * CAP)]
    pltpu.make_async_copy(come, come, row_recv).wait()
    gone = featb.at[pl.ds(0, (DEV - 1) * CAP)]
    pltpu.make_async_copy(gone, gone, row_send).wait()
    sent = ask_rows.at[pl.ds(0, DEV - 1)]
    pltpu.make_async_copy(sent, sent, req_send).wait()

    def widen(i, c):
        rows = pl.ds(pl.multiple_of(i * 256, 256), 256)
        table[rows, :] = pulled[rows, :].astype(F32)
        return c

    lax.fori_loop(0, SRC // 256, widen, 0)
    table[SRC:SRC + 8, :] = jnp.zeros((8, D_IN), F32)
    for c in to_smem:
        c.wait()

    def cols(b):
        return pl.ds(pl.multiple_of(b * 256, 256), 256)

    def forward(b):
        @pl.when(b % 2 == 0)
        def _():
            blk = gbuf.at[left, :, cols(b)]
            link(blk, blk, h_send.at[0, b], h_recv.at[0, b], right).wait_recv()
            link(blk, blk, h_send.at[2, b], h_recv.at[2, b], right).start()

        @pl.when(b % 2 == 1)
        def _():
            blk = gbuf.at[right, :, cols(b)]
            link(blk, blk, h_send.at[1, b], h_recv.at[1, b], left).wait_recv()
            link(blk, blk, h_send.at[2, b], h_recv.at[2, b], left).start()

    def block(b, c):
        def some(i, c2):
            base = pl.multiple_of(b * 256 + i * 16, 16)
            for j in range(16):
                m = base + j
                here = pl.ds(pl.multiple_of(i * 16, 16) + j, 1)
                own[here, :] = view[idx[0, m]]
                rows = [view[idx[1 + k, m]] for k in range(F1)]
                while len(rows) > 1:
                    rows = [p + q for p, q in zip(rows[::2], rows[1::2])] + ([rows[-1]] if len(rows) % 2 else [])
                near[here, :] = rows[0] * inv[0, m]
            return c2

        lax.fori_loop(0, 16, some, 0)
        rows = cols(b)
        act = jnp.concatenate([own[...].astype(BF), near[...].astype(BF)], axis=1)
        a1[rows, :] = act[:, :128]
        a1[pl.ds(pl.multiple_of(FRONT + b * 256, 256), 256), :] = act[:, 128:]
        z = dot(w1t[...], act, NT) + jnp.concatenate([b1c[...], b1c[...]], axis=1)
        z1t[:, rows] = z
        gbuf[y, :, rows] = (z / (1.0 + jnp.exp(-z))).astype(BF)
        blk = gbuf.at[y, :, rows]
        link(blk, blk, h_send.at[0, b], h_recv.at[0, b], right).start()
        link(blk, blk, h_send.at[1, b], h_recv.at[1, b], left).start()

        @pl.when(b > 0)
        def _():
            forward(b - 1)

        return c

    lax.fori_loop(0, 8, block, 0)
    forward(7)

    def from_source(q):
        return dot(gbuf[q], fsel[pl.ds(pl.multiple_of(q * FRONT, FRONT), FRONT), :])

    total = from_source(y)
    for b in range(1, 8, 2):
        blk = gbuf.at[left, :, b * 256:(b + 1) * 256]
        link(blk, blk, h_send.at[0, b], h_recv.at[0, b], right).wait_recv()
    total = total + from_source(left)
    for b in range(0, 8, 2):
        blk = gbuf.at[right, :, b * 256:(b + 1) * 256]
        link(blk, blk, h_send.at[1, b], h_recv.at[1, b], left).wait_recv()
    total = total + from_source(right)
    for b in range(8):
        blk = gbuf.at[opp, :, b * 256:(b + 1) * 256]
        link(blk, blk, h_send.at[2, b], h_recv.at[2, b], right).wait_recv()
    total = total + from_source(opp)

    def inverse_count(ids):
        n = jnp.sum((ids[1:1 + F2, :] >= 0).astype(F32), axis=0, keepdims=True)
        return 1.0 / jnp.maximum(n, 1.0)

    near2 = (total[:, :SEED] * inverse_count(gidx2[y])).astype(BF)
    self2 = total[:, SEED:].astype(BF)
    alive = live[...].astype(F32)
    diff = self2.astype(F32) - near2.astype(F32)

    def swap_start(buf, ssem, rsem):
        blk = buf.at[y]
        link(blk, blk, ssem.at[0], rsem.at[0], right).start()
        link(blk, blk, ssem.at[1], rsem.at[1], left).start()

    def swap_forward(buf, ssem, rsem, cut):
        blk = buf.at[left]
        link(blk, blk, ssem.at[0], rsem.at[0], right).wait_recv()
        half = buf.at[left, 0:cut, :]
        link(half, half, ssem.at[2], rsem.at[2], right).start()
        blk = buf.at[right]
        link(blk, blk, ssem.at[1], rsem.at[1], left).wait_recv()
        half = buf.at[right, cut:, :]
        link(half, half, ssem.at[3], rsem.at[3], left).start()

    def swap_end(buf, ssem, rsem, cut):
        half = buf.at[opp, 0:cut, :]
        link(half, half, ssem.at[2], rsem.at[2], right).wait_recv()
        half = buf.at[opp, cut:, :]
        link(half, half, ssem.at[3], rsem.at[3], left).wait_recv()

    def swap_sent(buf, ssem, rsem, cut):
        blk = buf.at[y]
        link(blk, blk, ssem.at[0], rsem.at[0], right).wait_send()
        link(blk, blk, ssem.at[1], rsem.at[1], left).wait_send()
        half = buf.at[left, 0:cut, :]
        link(half, half, ssem.at[2], rsem.at[2], right).wait_send()
        half = buf.at[right, cut:, :]
        link(half, half, ssem.at[3], rsem.at[3], left).wait_send()

    rbuf[y] = (2.0 * LAM / HID / SEEDS_ALL * alive * diff).astype(BF)
    swap_start(rbuf, r_send, r_recv)

    act2 = jnp.concatenate([self2, near2], axis=0)
    w2t = jnp.concatenate([gw2t[q] for q in range(NAR)], axis=1)
    cls = lax.broadcasted_iota(jnp.int32, (CLS_PAD, SEED), 0)
    b2 = b2c[0:CLS_PAD, :]
    logits = dot(w2t, act2) + jnp.concatenate([b2] * 4, axis=1)
    logits = jnp.where(cls < CLS, logits, -1e30)
    top = jnp.max(logits, axis=0, keepdims=True)
    e = jnp.exp(logits - top)
    tot = jnp.sum(e, axis=0, keepdims=True)
    hot = cls == labels[...]
    picked = jnp.sum(jnp.where(hot, logits, 0.0), axis=0, keepdims=True)
    dlog = (alive * (e * (1.0 / tot) - jnp.where(hot, 1.0, 0.0)) * (1.0 / SEEDS_ALL)).astype(BF)
    dbuf[y] = dlog
    swap_start(dbuf, d_send, d_recv)

    terms = top + jnp.log(tot) - picked + LAM / HID * jnp.sum(diff * diff, axis=0, keepdims=True)
    loss = jnp.sum(alive * terms, axis=1, keepdims=True)
    g2t = dot(dlog, act2, NT).astype(BF)
    for q in range(NAR):
        pay2[q * CLS_PAD:(q + 1) * CLS_PAD, :] = g2t[:, q * 128:(q + 1) * 128]

    def plane(i):
        return ((g + i) % GRP, y)

    def to_owner(pay, inbox, count, n):
        def body(i, c):
            t = (g + i) % GRP
            for slot in range(2):
                p = t + slot * GRP

                @pl.when(p < count)
                def _():
                    pltpu.make_async_remote_copy(
                        src_ref=pay.at[pl.ds(pl.multiple_of(p * 16, 16), 16)], dst_ref=inbox.at[slot, g],
                        send_sem=rs_send.at[n], recv_sem=rs_recv.at[n, slot], device_id=(t, y), device_id_type=MESH,
                    ).start()

            return c

        lax.fori_loop(1, GRP, body, 0)

    def add_plane(pay, inbox, ybox, count, n):
        for slot in range(2):
            p = g + slot * GRP

            @pl.when(p < count)
            def _():
                got = inbox.at[slot, pl.ds(0, GRP - 1)]
                pltpu.make_async_copy(got, got, rs_recv.at[n, slot]).wait()
                inbox[slot, g] = pay[pl.ds(pl.multiple_of(p * 16, 16), 16), :]
                ybox[slot, y] = jnp.sum(inbox[slot].astype(F32), axis=0)
                blk = ybox.at[slot, y]
                for d in range(1, NAR):
                    link(blk, blk, y_send.at[n, slot, d - 1], y_recv.at[n, slot, d - 1], (y + d) % NAR).start()

    def add_group(ybox, res, count, n):
        for slot in range(2):
            p = g + slot * GRP

            @pl.when(p < count)
            def _():
                blk = ybox.at[slot, y]
                for d in range(1, NAR):
                    link(blk, blk, y_send.at[n, slot, d - 1], y_recv.at[n, slot, d - 1], (y + d) % NAR).wait()
                rows16 = pl.ds(pl.multiple_of(p * 16, 16), 16)
                res[rows16, :] = (ybox[slot, 0] + ybox[slot, 1]) + (ybox[slot, 2] + ybox[slot, 3])

                def tell(i, c):
                    pltpu.make_async_remote_copy(
                        src_ref=res.at[rows16], dst_ref=res.at[rows16], send_sem=ag_send.at[n], recv_sem=ag_recv.at[n],
                        device_id=plane(i), device_id_type=MESH,
                    ).start()
                    return c

                lax.fori_loop(1, GRP, tell, 0)

    def take(res, count, n):
        two_here = g + GRP < count
        for own, here in ((2, two_here), (1, jnp.logical_not(two_here))):
            @pl.when(here)
            def _(own=own):
                got = res.at[pl.ds(0, (count - own) * 16)]
                pltpu.make_async_copy(got, got, ag_recv.at[n]).wait()

    def sums_sent(pay, count, n):
        two_here = g + GRP < count
        for own, here in ((2, two_here), (1, jnp.logical_not(two_here))):
            @pl.when(here)
            def _(own=own):
                gone = pay.at[pl.ds(0, (count - own) * 16)]
                pltpu.make_async_copy(gone, gone, rs_send.at[n]).wait()
                gone = table.at[pl.ds(0, own * (GRP - 1) * 16)]
                pltpu.make_async_copy(gone, gone, ag_send.at[n]).wait()

    to_owner(pay2, inbox2, P2, 1)

    def grads(q):
        da = dot(w2[...], dbuf[q])
        r = rbuf[q].astype(F32)
        ds = (da[:HID] + r).astype(BF)
        dn = ((da[HID:] - r) * inverse_count(gidx2[q])).astype(BF)
        return dot(jnp.concatenate([dn, ds], axis=1), bsel[q])

    swap_forward(rbuf, r_send, r_recv, 128)
    def add_grads(q, fresh=False):
        part = grads(q)
        for c in range(FRONT // 128):
            now = part[:, c * 128:(c + 1) * 128]
            dh1[c * 256:(c + 1) * 256, :] = now if fresh else dh1[c * 256:(c + 1) * 256, :] + now

    add_grads(y, True)
    swap_forward(dbuf, d_send, d_recv, 96)
    add_grads(left)
    add_grads(right)
    swap_end(rbuf, r_send, r_recv, 128)
    swap_end(dbuf, d_send, d_recv, 96)
    add_grads(opp)
    add_plane(pay2, inbox2, ybox2, P2, 1)

    z = z1t[...]
    sig = 1.0 / (1.0 + jnp.exp(-z))
    dh = jnp.concatenate([dh1[c * 256:(c + 1) * 256, :] for c in range(FRONT // 128)], axis=1)
    dz = (dh * sig * (1.0 + z * (1.0 - sig))).astype(BF)
    g1 = jnp.concatenate([dot(dz, a1[0:FRONT, :]), dot(dz, a1[FRONT:2 * FRONT, :])], axis=1).T.astype(BF)
    pay1[0:256, :] = g1[:, :128]
    pay1[256:512, :] = g1[:, 128:]
    ones_f = jnp.ones((8, FRONT), BF)
    ones_s = jnp.ones((8, SEED), BF)
    db1 = dot(ones_f, dz, NT)[0:1, :]
    db2 = dot(ones_s, dlog, NT)[0:1, :]
    misc[...] = jnp.zeros((16, 128), F32)

    def two(rows, v):
        hi = v.astype(BF).astype(F32)
        misc[rows:rows + 1, 0:v.shape[1]] = hi
        misc[rows + 4:rows + 5, 0:v.shape[1]] = v - hi

    two(0, db1[:, :128])
    two(1, db1[:, 128:])
    two(2, db2[:, :128])
    two(3, db2[:, 128:])
    hi = loss.astype(BF).astype(F32)
    misc[8:9, 0:1] = hi
    misc[9:10, 0:1] = loss - hi
    pay1[512:528, :] = misc[...].astype(BF)
    to_owner(pay1, inbox1, P1, 0)
    add_group(ybox2, res2, P2, 1)

    add_plane(pay1, inbox1, ybox1, P1, 0)
    take(res2, P2, 1)
    mom2 = jnp.concatenate(
        [MU * gm2t[q] + res2[q * CLS_PAD:(q + 1) * CLS_PAD, :] for q in range(NAR)], axis=1
    )
    for q in range(NAR):
        x2s[q] = mom2[:, q * 128:(q + 1) * 128]
    o_all[ROW_M2:ROW_M2 + CLS_PAD, :] = x2s[y]
    x2 = mom2 * (1.0 / (jnp.sqrt(jnp.sum(mom2 * mom2, keepdims=True)) + 1e-07))
    x2 = ns_step(x2)
    add_group(ybox1, o_all, P1, 0)
    for _ in range(NS_ITERS - 1):
        x2 = ns_step(x2)
    for q in range(NAR):
        x2s[q] = x2[:, q * 128:(q + 1) * 128]
    o_all[ROW_X2:ROW_X2 + CLS_PAD, :] = x2s[y]
    take(o_all, P1, 0)

    for b in range(8):
        blk = gbuf.at[y, :, b * 256:(b + 1) * 256]
        link(blk, blk, h_send.at[0, b], h_recv.at[0, b], right).wait_send()
        link(blk, blk, h_send.at[1, b], h_recv.at[1, b], left).wait_send()
        blk = gbuf.at[opp, :, b * 256:(b + 1) * 256]
        link(blk, blk, h_send.at[2, b], h_recv.at[2, b], right).wait_send()
    swap_sent(rbuf, r_send, r_recv, 128)
    swap_sent(dbuf, d_send, d_recv, 96)

    sums_sent(pay2, P2, 1)
    sums_sent(pay1, P1, 0)


def main(reqt, feat, idx1t, msk1t, idx2t, msk2t, labels, live, w1, w2own, m1, m2own, bias):
    vm = pl.BlockSpec(memory_space=pltpu.VMEM)
    dma = pltpu.SemaphoreType.DMA
    sds = jax.ShapeDtypeStruct
    V = pltpu.VMEM
    return pl.pallas_call(
        main_kernel,
        out_shape=sds((ROWS, 128), F32),
        in_specs=[vm, pl.BlockSpec(memory_space=pl.ANY)] + [vm] * 11,
        out_specs=vm,
        scratch_shapes=[
            V((SRC + 8, D_IN), F32),
            V((OWN, D_IN), BF),
            V((SRC, D_IN), BF),
            V((CAP, D_IN), F32),
            V((DEV, 128), jnp.int32),
            V((DEV, 128), jnp.int32),
            V((16, FRONT), jnp.int32),
            V((1, FRONT), F32),
            V((256, D_IN), F32),
            V((256, D_IN), F32),
            V((HID, FRONT), F32),
            V((NAR, HID, FRONT), BF),
            V((SRC, 2 * SEED), BF),
            V((NAR, 2 * SEED, FRONT), BF),
            V((SEED, 16 * NAR), jnp.int32),
            V((NAR, HID, SEED), BF),
            V((NAR, CLS_PAD, SEED), BF),
            V((NAR, 64, HID), BF),
            V((NAR, CLS_PAD, 128), BF),
            V((NAR, 64, HID), F32),
            V((NAR, CLS_PAD, 128), F32),
            V((NAR, 16, SEED), jnp.int32),
            V((HID, 2 * D_IN), BF),
            V((2 * HID, CLS_PAD), BF),
            V((HID, 128), F32),
            V((HID, 128), F32),
            V((P1 * 16, 128), BF),
            V((P2 * 16, 128), BF),
            V((16, 128), F32),
            V((2, GRP, 16, 128), BF),
            V((2, GRP, 16, 128), BF),
            V((2, NAR, 16, 128), F32),
            V((2, NAR, 16, 128), F32),
            V((P2 * 16, 128), F32),
            V((NAR, CLS_PAD, 128), F32),
            pltpu.SMEM((DEV, 128), jnp.int32),
            pltpu.SMEM((16, FRONT), jnp.int32),
            pltpu.SMEM((1, FRONT), F32),
            dma, dma((3,)), dma, dma, dma, dma, dma((5, 3)), dma((5, 3)),
            dma((3, 8)), dma((3, 8)), dma((4,)), dma((4,)), dma((4,)), dma((4,)),
            dma((2,)), dma((2, 2)), dma((2, 2, 3)), dma((2, 2, 3)), dma((2,)), dma((2,)),
        ],
        compiler_params=pltpu.CompilerParams(
            collective_id=0, has_side_effects=True, vmem_limit_bytes=62 * 2**20
        ),
    )(reqt, feat, idx1t, msk1t, idx2t, msk2t, labels, live, w1, w2own, m1, m2own, bias)


def update_kernel(
    res, w1own, w2own, bias, biasm, biasv,
    o_loss, o_first, o_second, o_mom1, o_mom2, o_flow, o_slow, o_bias, o_bm, o_bv,
    x1s,
):
    y = lax.axis_index("nar")
    mom1 = jnp.concatenate(
        [res[i * 256:i * 256 + 256, :] + res[ROW_G1 + i * 256:ROW_G1 + i * 256 + 256, :] for i in range(2)], axis=1
    )
    x1s[...] = mom1
    block64 = pl.ds(pl.multiple_of(y * 64, 64), 64)
    o_mom1[...] = x1s[block64, :]
    x1 = mom1 * (1.0 / (jnp.sqrt(jnp.sum(mom1 * mom1, keepdims=True)) + 1e-07))
    for _ in range(NS_ITERS):
        x1 = ns_step(x1)
    x1s[...] = x1
    first_new = w1own[...] * (1.0 - WDECAY) - x1s[block64, :]
    o_first[...] = first_new
    o_flow[...] = first_new.astype(BF)
    second = w2own[...] * (1.0 - WDECAY) - (2 * HID / CLS) ** 0.5 * res[ROW_X2:ROW_X2 + CLS, :]
    o_second[...] = second
    o_slow[...] = second.astype(BF)
    o_mom2[...] = res[ROW_M2:ROW_M2 + CLS, :]

    gb = res[512:516, :] + res[516:520, :]
    gb = jnp.concatenate([gb[0:1, :], gb[1:2, :], gb[2:3, :], gb[3:4, 0:44]], axis=1)
    m_new = BETA_ONE * biasm[...] + (1.0 - BETA_ONE) * gb
    v_new = BETA_TWO * biasv[...] + (1.0 - BETA_TWO) * gb * gb
    m_hat = m_new / (1.0 - BETA_ONE**STEP)
    v_hat = v_new / (1.0 - BETA_TWO**STEP)
    o_bias[...] = bias[...] * (1.0 - LR_BIAS * WDECAY) - LR_BIAS * m_hat / (jnp.sqrt(v_hat) + EPSILON)
    o_bm[...] = m_new
    o_bv[...] = v_new
    o_loss[...] = res[520:521, 0:1] + res[521:522, 0:1]


def update(*args):
    vm = pl.BlockSpec(memory_space=pltpu.VMEM)
    sds = jax.ShapeDtypeStruct
    return pl.pallas_call(
        update_kernel,
        out_shape=[
            sds((1, 1), F32), sds((64, HID), F32), sds((CLS, 128), F32), sds((64, HID), F32), sds((CLS, 128), F32),
            sds((64, HID), BF), sds((CLS, 128), BF), sds((1, 428), F32), sds((1, 428), F32), sds((1, 428), F32),
        ],
        in_specs=[vm] * 6,
        out_specs=[vm] * 10,
        scratch_shapes=[pltpu.VMEM((2 * D_IN, HID), F32)],
        compiler_params=pltpu.CompilerParams(vmem_limit_bytes=32 * 2**20),
    )(*args)


def per_device(
    features, requests, index_one, mask_one, index_two, mask_two, labels, seed_live,
    w_first, w_second, mom_first, mom_second, biases, bias_m, bias_v,
):
    w2own, bias = w_second.T, biases[None, :]
    res = main(
        requests.T, features, index_one.T, mask_one.T, index_two.T, mask_two.T, labels[None, :], seed_live[None, :],
        w_first, w2own, mom_first, mom_second.T, bias,
    )
    loss, first_new, second_new, mom_one, mom_two, first_low, second_low, bias_new, m_new, v_new = update(
        res, w_first, w2own, bias, bias_m[None, :], bias_v[None, :]
    )
    return (
        loss.reshape(()), first_new, second_new.T, mom_one, mom_two.T, first_low, second_low.T,
        bias_new.reshape(-1), m_new.reshape(-1), v_new.reshape(-1),
    )


def solution(mesh):
    both = ("grp", "nar")
    placed = (
        P(both, None), P(both, None), P(both, None), P(both, None), P(both, None), P(both, None),
        P(both), P(both), P("nar", None), P("nar", None), P("nar", None), P("nar", None), P(), P(), P(),
    )
    nar = P("nar", None)
    return jax.shard_map(
        per_device, mesh=mesh, in_specs=placed,
        out_specs=(P(), nar, nar, nar, nar, nar, nar, P(), P(), P()), check_vma=False,
    )
```

```python
import functools

import jax
import jax.numpy as jnp
from jax import lax
from jax.experimental import pallas as pl
from jax.experimental.pallas import tpu as pltpu
from jax.sharding import PartitionSpec as P

HID = 256
CLS = 172
CLS_PAD = 176
D_IN = 128
F1 = 15
F2 = 10
NS_ITERS = 5
STEP = 10
LAM = 0.5
MU = 0.95
WDECAY = 0.01
LR_BIAS = 0.05
BETA_ONE = 0.9
BETA_TWO = 0.999
EPSILON = 1e-08
NS_A = 3.4445
NS_B = -4.775
NS_C = 2.0315
HIGH = lax.Precision.HIGHEST
MESH = pl.DeviceIdType.MESH
BF = jnp.bfloat16
F32 = jnp.float32

DEV = 128
NAR = 4
OWN = 8192
CAP = 64
SRC = 8192
FRONT = 2048
SEED = 512


def all_to(t):
    return (t // NAR, t % NAR)


P1 = 33
P2 = 44
GRP = 32
ROW_G1 = P1 * 16
ROW_M2 = ROW_G1 + 512
ROW_X2 = ROW_M2 + CLS_PAD
ROWS = ROW_X2 + CLS_PAD
SEEDS_ALL = SEED * DEV


def dot(a, b, dims=((1,), (0,))):
    return lax.dot_general(a, b, (dims, ((), ())), preferred_element_type=F32)


NN = ((1,), (0,))
NT = ((1,), (1,))
TN = ((0,), (0,))


def split(a):
    hi = a.astype(BF)
    return hi, (a - hi.astype(F32)).astype(BF)


def dot3(a, b, dims):
    (ah, al), (bh, bl) = a, b
    return dot(ah, bh, dims) + (dot(ah, bl, dims) + dot(al, bh, dims))


def ns_step(x):
    xs = split(x)
    gram = dot3(xs, xs, NT)
    gs = split(gram)
    mix = NS_B * gram + NS_C * dot3(gs, gs, NN)
    return NS_A * x + dot3(split(mix), xs, NN)


def spread(row):
    return jnp.broadcast_to(row, (128, 128)).T


def main_kernel(
    reqt, feat, idx1t, msk1t, idx2t, msk2t, labels, live, w1, w2own, m1, m2own, bias,
    o_all,
    table, featb, pulled, stage, reqv, reqin, idxv, invv, near, own, z1, a1t, gbuf, fsel, bsel, idc, invc, livec, rbuf, dbuf,
    gw1, gw2t, gm1, gm2t, gidx2, w2t, b2c, pay1, pay2, misc, inbox1, inbox2, ybox1, ybox2, res2, x2s,
    reqs, idx, inv,
    feat_sem, loc_sem, req_send, req_recv, row_send, row_recv, nar_send, nar_recv,
    h_send, h_recv, r_send, r_recv, d_send, d_recv, rs_send, rs_recv, y_send, y_recv, ag_send, ag_recv,
):
    a1, dh1 = pulled, table
    g = lax.axis_index("grp")
    y = lax.axis_index("nar")
    me = g * NAR + y
    left, right, opp = (y + 3) % NAR, (y + 1) % NAR, (y + 2) % NAR

    load = pltpu.make_async_copy(feat, featb, feat_sem)
    load.start()

    barrier = pltpu.get_barrier_semaphore()

    def greet(i, c):
        pl.semaphore_signal(barrier, inc=1, device_id=all_to((me + i) % DEV), device_id_type=MESH)
        return c

    lax.fori_loop(1, DEV, greet, 0)

    def link(src, dst, ssem, rsem, to):
        return pltpu.make_async_remote_copy(
            src_ref=src, dst_ref=dst, send_sem=ssem, recv_sem=rsem, device_id=(g, to), device_id_type=MESH
        )

    reqv[...] = jnp.concatenate([reqt[...], jnp.zeros((DEV - CAP, DEV), jnp.int32)], axis=0).T
    ask_rows = reqv.reshape(DEV, 1, 128)
    got_rows = reqin.reshape(DEV, 1, 128)

    gw1[y] = w1[...].astype(BF)
    pad = CLS_PAD - CLS
    gw2t[y] = jnp.concatenate([w2own[...], jnp.zeros((pad, 128), F32)], axis=0).astype(BF)
    gm1[y] = m1[...]
    gm2t[y] = jnp.concatenate([m2own[...], jnp.zeros((pad, 128), F32)], axis=0)
    gidx2[y] = jnp.concatenate(
        [idx2t[0:1, :], jnp.where(msk2t[...] > 0, idx2t[1:, :], -1), jnp.zeros((5, SEED), jnp.int32)], axis=0
    )
    shared = (gidx2, gw1, gw2t, gm1, gm2t)

    pl.semaphore_wait(barrier, DEV - 1)

    def ask(i, c):
        t = (me + i * 37) % DEV
        pltpu.make_async_remote_copy(
            src_ref=ask_rows.at[t], dst_ref=got_rows.at[me], send_sem=req_send, recv_sem=req_recv,
            device_id=all_to(t), device_id_type=MESH,
        ).start()
        return c

    lax.fori_loop(1, DEV, ask, 0)
    for n, a in enumerate(shared):
        for d in range(1, NAR):
            link(a.at[y], a.at[y], nar_send.at[n, d - 1], nar_recv.at[n, d - 1], (y + d) % NAR).start()

    reqin[pl.ds(me, 1), :] = reqv[pl.ds(me, 1), :]
    msk = msk1t[...]
    idxv[0:1, :] = idx1t[0:1, :]
    idxv[1:16, :] = jnp.where(msk > 0, idx1t[1:16, :], SRC)
    invv[...] = 1.0 / jnp.maximum(jnp.sum(msk.astype(F32), axis=0, keepdims=True), 1.0)
    to_smem = [pltpu.make_async_copy(idxv, idx, loc_sem.at[0]), pltpu.make_async_copy(invv, inv, loc_sem.at[1])]
    for c in to_smem:
        c.start()

    load.wait()

    def widen_features(i, c):
        rows = pl.ds(pl.multiple_of(i * 256, 256), 256)
        table[rows, :] = featb[rows, :].astype(F32)
        return c

    lax.fori_loop(0, OWN // 256, widen_features, 0)

    got = got_rows.at[pl.ds(0, DEV - 1)]
    pltpu.make_async_copy(got, got, req_recv).wait()
    fetch = pltpu.make_async_copy(reqin, reqs, loc_sem.at[2])
    fetch.start()
    fetch.wait()

    view = table.reshape(SRC + 8, 1, D_IN)
    my_rows = pl.ds(pl.multiple_of(me * CAP, CAP), CAP)

    def serve(i, c):
        t = (me + i * 37) % DEV
        for r in range(CAP):
            stage[r:r + 1, :] = view[reqs[t, r]]
        slot = pl.ds(pl.multiple_of(i * CAP, CAP), CAP)
        featb[slot, :] = stage[...].astype(BF)

        @pl.when(i > 0)
        def _():
            pltpu.make_async_remote_copy(
                src_ref=featb.at[slot], dst_ref=pulled.at[my_rows],
                send_sem=row_send, recv_sem=row_recv, device_id=all_to(t), device_id_type=MESH,
            ).start()

        return c

    lax.fori_loop(1, DEV, serve, 0)
    serve(0, 0)
    pulled[my_rows, :] = featb[0:CAP, :]

    for n, a in enumerate(shared):
        for d in range(1, NAR):
            link(a.at[y], a.at[y], nar_send.at[n, d - 1], nar_recv.at[n, d - 1], (y + d) % NAR).wait()
    for q in range(NAR):
        o_all[ROW_G1 + q * 64:ROW_G1 + q * 64 + 64, :] = MU * gm1[q, :, 0:128]
        o_all[ROW_G1 + 256 + q * 64:ROW_G1 + 256 + q * 64 + 64, :] = MU * gm1[q, :, 128:256]
    for q in range(NAR):
        w2t[:, q * 128:(q + 1) * 128] = gw2t[q]
    last = jnp.concatenate([bias[0:1, 384:428], jnp.zeros((1, 84), F32)], axis=1)
    b2c[...] = jnp.concatenate([spread(bias[0:1, 256:384]), spread(last)], axis=0)

    def column(row):
        return jnp.concatenate([spread(row[:, c * 128:(c + 1) * 128]) for c in range(SEED // 128)], axis=0)

    for q in range(NAR):
        n = jnp.sum((gidx2[q, 1:1 + F2, :] >= 0).astype(F32), axis=0, keepdims=True)
        invc[q] = column(1.0 / jnp.maximum(n, 1.0))
    livec[...] = column(2.0 * LAM / HID / SEEDS_ALL * live[...].astype(F32))

    lane16 = lax.broadcasted_iota(jnp.int32, (16, 128), 1).astype(jnp.int16)
    iota16 = lax.broadcasted_iota(jnp.int32, (16, 128), 0).astype(jnp.int16)
    one, zero = jnp.ones((16, 128), BF), jnp.zeros((16, 128), BF)

    def marks(here, want):
        acc = jnp.where(here == want[1], one, zero)
        for k in range(2, 1 + F2):
            acc = acc + jnp.where(here == want[k], one, zero)
        return acc, jnp.where(here == want[0], one, zero)

    idc[...] = gidx2[y].T

    def forward_marks(i, carry):
        at = pl.multiple_of(i * 16, 16)
        blk = idc[pl.ds(at, 16), :]
        want = [jnp.broadcast_to(blk[:, k:k + 1], (16, 128)).astype(jnp.int16) for k in range(1 + F2)]
        for q in range(NAR):
            for c in range(FRONT // 128):
                here = lane16 + jnp.full((16, 128), q * FRONT + c * 128, jnp.int32).astype(jnp.int16)
                a, b = marks(here, want)
                fsel[q, pl.ds(at, 16), c * 128:(c + 1) * 128] = a
                fsel[q, pl.ds(SEED + at, 16), c * 128:(c + 1) * 128] = b
        return carry

    lax.fori_loop(0, SEED // 16, forward_marks, 0)

    for q in range(NAR):
        ids = gidx2[q] - y * FRONT
        wants = [
            [jnp.broadcast_to(ids[k:k + 1, c * 128:(c + 1) * 128], (16, 128)).astype(jnp.int16) for k in range(1 + F2)]
            for c in range(SEED // 128)
        ]

        def backward_marks(i, carry, q=q, wants=wants):
            here = iota16 + jnp.full((16, 128), i * 16, jnp.int32).astype(jnp.int16)
            out = pl.ds(pl.multiple_of(i * 16, 16), 16)
            for c in range(SEED // 128):
                a, b = marks(here, wants[c])
                bsel[q, out, c * 128:(c + 1) * 128] = a
                bsel[q, out, SEED + c * 128:SEED + (c + 1) * 128] = b
            return carry

        lax.fori_loop(0, FRONT // 16, backward_marks, 0)

    come = pulled.at[pl.ds(0, (DEV - 1) * CAP)]
    pltpu.make_async_copy(come, come, row_recv).wait()
    gone = featb.at[pl.ds(0, (DEV - 1) * CAP)]
    pltpu.make_async_copy(gone, gone, row_send).wait()
    sent = ask_rows.at[pl.ds(0, DEV - 1)]
    pltpu.make_async_copy(sent, sent, req_send).wait()

    def widen(i, c):
        rows = pl.ds(pl.multiple_of(i * 256, 256), 256)
        table[rows, :] = pulled[rows, :].astype(F32)
        return c

    lax.fori_loop(0, SRC // 256, widen, 0)
    table[SRC:SRC + 8, :] = jnp.zeros((8, D_IN), F32)
    for c in to_smem:
        c.wait()

    def cols(b):
        return pl.ds(pl.multiple_of(b * 256, 256), 256)

    def forward(b):
        @pl.when(b % 2 == 0)
        def _():
            blk = gbuf.at[left, cols(b), :]
            link(blk, blk, h_send.at[0, b], h_recv.at[0, b], right).wait_recv()
            link(blk, blk, h_send.at[2, b], h_recv.at[2, b], right).start()

        @pl.when(b % 2 == 1)
        def _():
            blk = gbuf.at[right, cols(b), :]
            link(blk, blk, h_send.at[1, b], h_recv.at[1, b], left).wait_recv()
            link(blk, blk, h_send.at[2, b], h_recv.at[2, b], left).start()

    def block(b, c):
        def some(i, c2):
            base = pl.multiple_of(b * 256 + i * 16, 16)
            for j in range(16):
                m = base + j
                here = pl.ds(pl.multiple_of(i * 16, 16) + j, 1)
                own[here, :] = view[idx[0, m]]
                rows = [view[idx[1 + k, m]] for k in range(F1)]
                while len(rows) > 1:
                    rows = [p + q for p, q in zip(rows[::2], rows[1::2])] + ([rows[-1]] if len(rows) % 2 else [])
                near[here, :] = rows[0] * inv[0, m]
            return c2

        lax.fori_loop(0, 16, some, 0)
        rows = cols(b)
        act = jnp.concatenate([own[...].astype(BF), near[...].astype(BF)], axis=1)
        a1[rows, :] = act[:, :128]
        a1[pl.ds(pl.multiple_of(FRONT + b * 256, 256), 256), :] = act[:, 128:]
        z = dot(act, gw1[...].reshape(2 * D_IN, HID)) + bias[0:1, 0:HID]
        z1[rows, :] = z
        gbuf[y, rows, :] = (z / (1.0 + jnp.exp(-z))).astype(BF)
        blk = gbuf.at[y, rows, :]
        link(blk, blk, h_send.at[0, b], h_recv.at[0, b], right).start()
        link(blk, blk, h_send.at[1, b], h_recv.at[1, b], left).start()

        @pl.when(b > 0)
        def _():
            forward(b - 1)

        return c

    lax.fori_loop(0, 8, block, 0)
    forward(7)

    def from_source(q):
        return dot(fsel[q], gbuf[q])

    total = from_source(y)
    for b in range(1, 8, 2):
        blk = gbuf.at[left, b * 256:(b + 1) * 256, :]
        link(blk, blk, h_send.at[0, b], h_recv.at[0, b], right).wait_recv()
    total = total + from_source(left)
    for b in range(0, 8, 2):
        blk = gbuf.at[right, b * 256:(b + 1) * 256, :]
        link(blk, blk, h_send.at[1, b], h_recv.at[1, b], left).wait_recv()
    total = total + from_source(right)
    for b in range(8):
        blk = gbuf.at[opp, b * 256:(b + 1) * 256, :]
        link(blk, blk, h_send.at[2, b], h_recv.at[2, b], right).wait_recv()
    total = total + from_source(opp)

    def wide(a):
        return jnp.concatenate([a, a], axis=1)

    near2 = (total[:SEED, :] * wide(invc[y])).astype(BF)
    self2 = total[SEED:, :].astype(BF)
    alive = live[...].astype(F32)
    diff = self2.astype(F32) - near2.astype(F32)
    pull_apart = wide(livec[...]) * diff

    def swap_start(buf, ssem, rsem):
        blk = buf.at[y]
        link(blk, blk, ssem.at[0], rsem.at[0], right).start()
        link(blk, blk, ssem.at[1], rsem.at[1], left).start()

    def swap_forward(buf, ssem, rsem, cut):
        blk = buf.at[left]
        link(blk, blk, ssem.at[0], rsem.at[0], right).wait_recv()
        half = buf.at[left, 0:cut, :]
        link(half, half, ssem.at[2], rsem.at[2], right).start()
        blk = buf.at[right]
        link(blk, blk, ssem.at[1], rsem.at[1], left).wait_recv()
        half = buf.at[right, cut:, :]
        link(half, half, ssem.at[3], rsem.at[3], left).start()

    def swap_end(buf, ssem, rsem, cut):
        half = buf.at[opp, 0:cut, :]
        link(half, half, ssem.at[2], rsem.at[2], right).wait_recv()
        half = buf.at[opp, cut:, :]
        link(half, half, ssem.at[3], rsem.at[3], left).wait_recv()

    def swap_sent(buf, ssem, rsem, cut):
        blk = buf.at[y]
        link(blk, blk, ssem.at[0], rsem.at[0], right).wait_send()
        link(blk, blk, ssem.at[1], rsem.at[1], left).wait_send()
        half = buf.at[left, 0:cut, :]
        link(half, half, ssem.at[2], rsem.at[2], right).wait_send()
        half = buf.at[right, cut:, :]
        link(half, half, ssem.at[3], rsem.at[3], left).wait_send()

    rbuf[y] = pull_apart.astype(BF)
    swap_start(rbuf, r_send, r_recv)

    act2 = jnp.concatenate([self2, near2], axis=1)
    cls = lax.broadcasted_iota(jnp.int32, (CLS_PAD, SEED), 0)
    b2 = b2c[0:CLS_PAD, :]
    logits = dot(w2t[...], act2, NT) + jnp.concatenate([b2] * 4, axis=1)
    logits = jnp.where(cls < CLS, logits, -1e30)
    top = jnp.max(logits, axis=0, keepdims=True)
    e = jnp.exp(logits - top)
    tot = jnp.sum(e, axis=0, keepdims=True)
    hot = cls == labels[...]
    picked = jnp.sum(jnp.where(hot, logits, 0.0), axis=0, keepdims=True)
    dlog = (alive * (e * (1.0 / tot) - jnp.where(hot, 1.0, 0.0)) * (1.0 / SEEDS_ALL)).astype(BF)
    dbuf[y] = dlog
    swap_start(dbuf, d_send, d_recv)

    loss = jnp.sum(alive * (top + jnp.log(tot) - picked), axis=1, keepdims=True)
    loss = loss + SEEDS_ALL / 2 * jnp.sum(pull_apart * diff, keepdims=True)
    g2t = dot(dlog, act2).astype(BF)
    for q in range(NAR):
        pay2[q * CLS_PAD:(q + 1) * CLS_PAD, :] = g2t[:, q * 128:(q + 1) * 128]

    def plane(i):
        return ((g + i) % GRP, y)

    def to_owner(pay, inbox, count, n):
        def body(i, c):
            t = (g + i) % GRP
            for slot in range(2):
                p = t + slot * GRP

                @pl.when(p < count)
                def _():
                    pltpu.make_async_remote_copy(
                        src_ref=pay.at[pl.ds(pl.multiple_of(p * 16, 16), 16)], dst_ref=inbox.at[slot, g],
                        send_sem=rs_send.at[n], recv_sem=rs_recv.at[n, slot], device_id=(t, y), device_id_type=MESH,
                    ).start()

            return c

        lax.fori_loop(1, GRP, body, 0)

    def add_plane(pay, inbox, ybox, count, n):
        for slot in range(2):
            p = g + slot * GRP

            @pl.when(p < count)
            def _():
                got = inbox.at[slot, pl.ds(0, GRP - 1)]
                pltpu.make_async_copy(got, got, rs_recv.at[n, slot]).wait()
                inbox[slot, g] = pay[pl.ds(pl.multiple_of(p * 16, 16), 16), :]
                ybox[slot, y] = jnp.sum(inbox[slot].astype(F32), axis=0)
                blk = ybox.at[slot, y]
                for d in range(1, NAR):
                    link(blk, blk, y_send.at[n, slot, d - 1], y_recv.at[n, slot, d - 1], (y + d) % NAR).start()

    def add_group(ybox, res, count, n):
        for slot in range(2):
            p = g + slot * GRP

            @pl.when(p < count)
            def _():
                blk = ybox.at[slot, y]
                for d in range(1, NAR):
                    link(blk, blk, y_send.at[n, slot, d - 1], y_recv.at[n, slot, d - 1], (y + d) % NAR).wait()
                rows16 = pl.ds(pl.multiple_of(p * 16, 16), 16)
                res[rows16, :] = (ybox[slot, 0] + ybox[slot, 1]) + (ybox[slot, 2] + ybox[slot, 3])

                def tell(i, c):
                    pltpu.make_async_remote_copy(
                        src_ref=res.at[rows16], dst_ref=res.at[rows16], send_sem=ag_send.at[n], recv_sem=ag_recv.at[n],
                        device_id=plane(i), device_id_type=MESH,
                    ).start()
                    return c

                lax.fori_loop(1, GRP, tell, 0)

    def take(res, count, n):
        two_here = g + GRP < count
        for own, here in ((2, two_here), (1, jnp.logical_not(two_here))):
            @pl.when(here)
            def _(own=own):
                got = res.at[pl.ds(0, (count - own) * 16)]
                pltpu.make_async_copy(got, got, ag_recv.at[n]).wait()

    def sums_sent(pay, count, n):
        two_here = g + GRP < count
        for own, here in ((2, two_here), (1, jnp.logical_not(two_here))):
            @pl.when(here)
            def _(own=own):
                gone = pay.at[pl.ds(0, (count - own) * 16)]
                pltpu.make_async_copy(gone, gone, rs_send.at[n]).wait()
                gone = table.at[pl.ds(0, own * (GRP - 1) * 16)]
                pltpu.make_async_copy(gone, gone, ag_send.at[n]).wait()

    to_owner(pay2, inbox2, P2, 1)

    def add_grads(q, fresh=False):
        da = dot(dbuf[q], w2t[...], TN)
        r = rbuf[q].astype(F32)
        ds = (da[:, :HID] + r).astype(BF)
        dn = ((da[:, HID:] - r) * wide(invc[q])).astype(BF)
        part = dot(bsel[q], jnp.concatenate([dn, ds], axis=0))
        for c in range(2):
            rows = slice(c * FRONT, (c + 1) * FRONT)
            now = part[:, c * 128:(c + 1) * 128]
            dh1[rows, :] = now if fresh else dh1[rows, :] + now

    for c in range(2):
        a1t[c * 128:(c + 1) * 128, :] = a1[c * FRONT:(c + 1) * FRONT, :].T
    db2 = jnp.sum(dlog.astype(F32), axis=1, keepdims=True)
    db2 = jnp.broadcast_to(db2, (CLS_PAD, 128)).T[0:1, :]
    swap_forward(rbuf, r_send, r_recv, SEED // 2)
    add_grads(y, True)
    swap_forward(dbuf, d_send, d_recv, 96)
    add_grads(left)
    add_grads(right)
    swap_end(rbuf, r_send, r_recv, SEED // 2)
    swap_end(dbuf, d_send, d_recv, 96)
    add_grads(opp)
    add_plane(pay2, inbox2, ybox2, P2, 1)

    z = z1[...]
    sig = 1.0 / (1.0 + jnp.exp(-z))
    dh = jnp.concatenate([dh1[0:FRONT, :], dh1[FRONT:2 * FRONT, :]], axis=1)
    dz = (dh * sig * (1.0 + z * (1.0 - sig))).astype(BF)
    g1 = dot(a1t[...], dz).astype(BF)
    pay1[0:256, :] = g1[:, :128]
    pay1[256:512, :] = g1[:, 128:]
    db1 = jnp.sum(dz.astype(F32), axis=0, keepdims=True)
    misc[...] = jnp.zeros((16, 128), F32)

    def two(rows, v):
        hi = v.astype(BF).astype(F32)
        misc[rows:rows + 1, 0:v.shape[1]] = hi
        misc[rows + 4:rows + 5, 0:v.shape[1]] = v - hi

    two(0, db1[:, :128])
    two(1, db1[:, 128:])
    two(2, db2[:, :128])
    two(3, db2[:, 128:])
    hi = loss.astype(BF).astype(F32)
    misc[8:9, 0:1] = hi
    misc[9:10, 0:1] = loss - hi
    pay1[512:528, :] = misc[...].astype(BF)
    to_owner(pay1, inbox1, P1, 0)
    add_group(ybox2, res2, P2, 1)

    add_plane(pay1, inbox1, ybox1, P1, 0)
    take(res2, P2, 1)
    mom2 = jnp.concatenate(
        [MU * gm2t[q] + res2[q * CLS_PAD:(q + 1) * CLS_PAD, :] for q in range(NAR)], axis=1
    )
    for q in range(NAR):
        x2s[q] = mom2[:, q * 128:(q + 1) * 128]
    o_all[ROW_M2:ROW_M2 + CLS_PAD, :] = x2s[y]
    x2 = mom2 * (1.0 / (jnp.sqrt(jnp.sum(mom2 * mom2, keepdims=True)) + 1e-07))
    x2 = ns_step(x2)
    add_group(ybox1, o_all, P1, 0)
    for _ in range(NS_ITERS - 1):
        x2 = ns_step(x2)
    for q in range(NAR):
        x2s[q] = x2[:, q * 128:(q + 1) * 128]
    o_all[ROW_X2:ROW_X2 + CLS_PAD, :] = x2s[y]
    take(o_all, P1, 0)

    for b in range(8):
        blk = gbuf.at[y, b * 256:(b + 1) * 256, :]
        link(blk, blk, h_send.at[0, b], h_recv.at[0, b], right).wait_send()
        link(blk, blk, h_send.at[1, b], h_recv.at[1, b], left).wait_send()
        blk = gbuf.at[opp, b * 256:(b + 1) * 256, :]
        link(blk, blk, h_send.at[2, b], h_recv.at[2, b], right).wait_send()
    swap_sent(rbuf, r_send, r_recv, SEED // 2)
    swap_sent(dbuf, d_send, d_recv, 96)

    sums_sent(pay2, P2, 1)
    sums_sent(pay1, P1, 0)


def main(reqt, feat, idx1t, msk1t, idx2t, msk2t, labels, live, w1, w2own, m1, m2own, bias):
    vm = pl.BlockSpec(memory_space=pltpu.VMEM)
    dma = pltpu.SemaphoreType.DMA
    sds = jax.ShapeDtypeStruct
    V = pltpu.VMEM
    return pl.pallas_call(
        main_kernel,
        out_shape=sds((ROWS, 128), F32),
        in_specs=[vm, pl.BlockSpec(memory_space=pl.ANY)] + [vm] * 11,
        out_specs=vm,
        scratch_shapes=[
            V((SRC + 8, D_IN), F32),
            V((OWN, D_IN), BF),
            V((SRC, D_IN), BF),
            V((CAP, D_IN), F32),
            V((DEV, 128), jnp.int32),
            V((DEV, 128), jnp.int32),
            V((16, FRONT), jnp.int32),
            V((1, FRONT), F32),
            V((256, D_IN), F32),
            V((256, D_IN), F32),
            V((FRONT, HID), F32),
            V((2 * D_IN, FRONT), BF),
            V((NAR, FRONT, HID), BF),
            V((NAR, 2 * SEED, FRONT), BF),
            V((NAR, FRONT, 2 * SEED), BF),
            V((SEED, 16), jnp.int32),
            V((NAR, SEED, 128), F32),
            V((SEED, 128), F32),
            V((NAR, SEED, HID), BF),
            V((NAR, CLS_PAD, SEED), BF),
            V((NAR, 64, HID), BF),
            V((NAR, CLS_PAD, 128), BF),
            V((NAR, 64, HID), F32),
            V((NAR, CLS_PAD, 128), F32),
            V((NAR, 16, SEED), jnp.int32),
            V((CLS_PAD, 2 * HID), BF),
            V((HID, 128), F32),
            V((P1 * 16, 128), BF),
            V((P2 * 16, 128), BF),
            V((16, 128), F32),
            V((2, GRP, 16, 128), BF),
            V((2, GRP, 16, 128), BF),
            V((2, NAR, 16, 128), F32),
            V((2, NAR, 16, 128), F32),
            V((P2 * 16, 128), F32),
            V((NAR, CLS_PAD, 128), F32),
            pltpu.SMEM((DEV, 128), jnp.int32),
            pltpu.SMEM((16, FRONT), jnp.int32),
            pltpu.SMEM((1, FRONT), F32),
            dma, dma((3,)), dma, dma, dma, dma, dma((5, 3)), dma((5, 3)),
            dma((3, 8)), dma((3, 8)), dma((4,)), dma((4,)), dma((4,)), dma((4,)),
            dma((2,)), dma((2, 2)), dma((2, 2, 3)), dma((2, 2, 3)), dma((2,)), dma((2,)),
        ],
        compiler_params=pltpu.CompilerParams(
            collective_id=0, has_side_effects=True, vmem_limit_bytes=62 * 2**20
        ),
    )(reqt, feat, idx1t, msk1t, idx2t, msk2t, labels, live, w1, w2own, m1, m2own, bias)


def update_kernel(
    res, w1own, w2own, bias, biasm, biasv,
    o_loss, o_first, o_second, o_mom1, o_mom2, o_flow, o_slow, o_bias, o_bm, o_bv,
    x1s,
):
    y = lax.axis_index("nar")
    mom1 = jnp.concatenate(
        [res[i * 256:i * 256 + 256, :] + res[ROW_G1 + i * 256:ROW_G1 + i * 256 + 256, :] for i in range(2)], axis=1
    )
    x1s[...] = mom1
    block64 = pl.ds(pl.multiple_of(y * 64, 64), 64)
    o_mom1[...] = x1s[block64, :]
    x1 = mom1 * (1.0 / (jnp.sqrt(jnp.sum(mom1 * mom1, keepdims=True)) + 1e-07))
    for _ in range(NS_ITERS):
        x1 = ns_step(x1)
    x1s[...] = x1
    first_new = w1own[...] * (1.0 - WDECAY) - x1s[block64, :]
    o_first[...] = first_new
    o_flow[...] = first_new.astype(BF)
    second = w2own[...] * (1.0 - WDECAY) - (2 * HID / CLS) ** 0.5 * res[ROW_X2:ROW_X2 + CLS, :]
    o_second[...] = second
    o_slow[...] = second.astype(BF)
    o_mom2[...] = res[ROW_M2:ROW_M2 + CLS, :]

    gb = res[512:516, :] + res[516:520, :]
    gb = jnp.concatenate([gb[0:1, :], gb[1:2, :], gb[2:3, :], gb[3:4, 0:44]], axis=1)
    m_new = BETA_ONE * biasm[...] + (1.0 - BETA_ONE) * gb
    v_new = BETA_TWO * biasv[...] + (1.0 - BETA_TWO) * gb * gb
    m_hat = m_new / (1.0 - BETA_ONE**STEP)
    v_hat = v_new / (1.0 - BETA_TWO**STEP)
    o_bias[...] = bias[...] * (1.0 - LR_BIAS * WDECAY) - LR_BIAS * m_hat / (jnp.sqrt(v_hat) + EPSILON)
    o_bm[...] = m_new
    o_bv[...] = v_new
    o_loss[...] = res[520:521, 0:1] + res[521:522, 0:1]


def update(*args):
    vm = pl.BlockSpec(memory_space=pltpu.VMEM)
    sds = jax.ShapeDtypeStruct
    return pl.pallas_call(
        update_kernel,
        out_shape=[
            sds((1, 1), F32), sds((64, HID), F32), sds((CLS, 128), F32), sds((64, HID), F32), sds((CLS, 128), F32),
            sds((64, HID), BF), sds((CLS, 128), BF), sds((1, 428), F32), sds((1, 428), F32), sds((1, 428), F32),
        ],
        in_specs=[vm] * 6,
        out_specs=[vm] * 10,
        scratch_shapes=[pltpu.VMEM((2 * D_IN, HID), F32)],
        compiler_params=pltpu.CompilerParams(vmem_limit_bytes=32 * 2**20),
    )(*args)


def per_device(
    features, requests, index_one, mask_one, index_two, mask_two, labels, seed_live,
    w_first, w_second, mom_first, mom_second, biases, bias_m, bias_v,
):
    w2own, bias = w_second.T, biases[None, :]
    res = main(
        requests.T, features, index_one.T, mask_one.T, index_two.T, mask_two.T, labels[None, :], seed_live[None, :],
        w_first, w2own, mom_first, mom_second.T, bias,
    )
    loss, first_new, second_new, mom_one, mom_two, first_low, second_low, bias_new, m_new, v_new = update(
        res, w_first, w2own, bias, bias_m[None, :], bias_v[None, :]
    )
    return (
        loss.reshape(()), first_new, second_new.T, mom_one, mom_two.T, first_low, second_low.T,
        bias_new.reshape(-1), m_new.reshape(-1), v_new.reshape(-1),
    )


def solution(mesh):
    both = ("grp", "nar")
    placed = (
        P(both, None), P(both, None), P(both, None), P(both, None), P(both, None), P(both, None),
        P(both), P(both), P("nar", None), P("nar", None), P("nar", None), P("nar", None), P(), P(), P(),
    )
    nar = P("nar", None)
    return jax.shard_map(
        per_device, mesh=mesh, in_specs=placed,
        out_specs=(P(), nar, nar, nar, nar, nar, nar, P(), P(), P()), check_vma=False,
    )
```

```python
import functools

import jax
import jax.numpy as jnp
from jax import lax
from jax.experimental import pallas as pl
from jax.experimental.pallas import tpu as pltpu
from jax.sharding import PartitionSpec as P

HID = 256
CLS = 172
CLS_PAD = 176
D_IN = 128
F1 = 15
F2 = 10
NS_ITERS = 5
STEP = 10
LAM = 0.5
MU = 0.95
WDECAY = 0.01
LR_BIAS = 0.05
BETA_ONE = 0.9
BETA_TWO = 0.999
EPSILON = 1e-08
NS_A = 3.4445
NS_B = -4.775
NS_C = 2.0315
HIGH = lax.Precision.HIGHEST
MESH = pl.DeviceIdType.MESH
BF = jnp.bfloat16
F32 = jnp.float32

DEV = 128
NAR = 4
OWN = 8192
CAP = 64
SRC = 8192
FRONT = 2048
SEED = 512


def all_to(t):
    return (t // NAR, t % NAR)


P1 = 33
P2 = 44
GRP = 32
ROW_G1 = P1 * 16
ROW_M2 = ROW_G1 + 512
ROW_X2 = ROW_M2 + CLS_PAD
ROWS = ROW_X2 + CLS_PAD
SEEDS_ALL = SEED * DEV


def dot(a, b, dims=((1,), (0,))):
    return lax.dot_general(a, b, (dims, ((), ())), preferred_element_type=F32)


NN = ((1,), (0,))
NT = ((1,), (1,))
TN = ((0,), (0,))


def split(a):
    hi = a.astype(BF)
    return hi, (a - hi.astype(F32)).astype(BF)


def dot3(a, b, dims):
    (ah, al), (bh, bl) = a, b
    return dot(ah, bh, dims) + (dot(ah, bl, dims) + dot(al, bh, dims))


def ns_step(x):
    xs = split(x)
    gram = dot3(xs, xs, NT)
    gs = split(gram)
    mix = NS_B * gram + NS_C * dot3(gs, gs, NN)
    return NS_A * x + dot3(split(mix), xs, NN)


def spread(row):
    return jnp.broadcast_to(row, (128, 128)).T


def main_kernel(
    reqt, feat, idx1t, msk1t, idx2t, msk2t, labels, live, w1, w2own, m1, m2own, bias,
    o_all,
    table, featb, pulled, stage, reqv, reqin, idxv, invv, near, own, z1, a1t, gbuf, fsel, bsel, wants, idc, invc, livec, rbuf, dbuf,
    gw1, gw2t, gm1, gm2t, gidx2, w2t, b2c, pay1, pay2, misc, inbox1, inbox2, ybox1, ybox2, res2, x2s,
    reqs, idx, inv,
    feat_sem, loc_sem, req_send, req_recv, row_send, row_recv, nar_send, nar_recv,
    h_send, h_recv, r_send, r_recv, d_send, d_recv, rs_send, rs_recv, y_send, y_recv, ag_send, ag_recv,
):
    a1, dh1 = pulled, table
    g = lax.axis_index("grp")
    y = lax.axis_index("nar")
    me = g * NAR + y
    left, right, opp = (y + 3) % NAR, (y + 1) % NAR, (y + 2) % NAR

    load = pltpu.make_async_copy(feat, featb, feat_sem)
    load.start()

    barrier = pltpu.get_barrier_semaphore()

    def greet(i, c):
        pl.semaphore_signal(barrier, inc=1, device_id=all_to((me + i) % DEV), device_id_type=MESH)
        return c

    lax.fori_loop(1, DEV, greet, 0)

    def link(src, dst, ssem, rsem, to):
        return pltpu.make_async_remote_copy(
            src_ref=src, dst_ref=dst, send_sem=ssem, recv_sem=rsem, device_id=(g, to), device_id_type=MESH
        )

    reqv[...] = jnp.concatenate([reqt[...], jnp.zeros((DEV - CAP, DEV), jnp.int32)], axis=0).T
    ask_rows = reqv.reshape(DEV, 1, 128)
    got_rows = reqin.reshape(DEV, 1, 128)

    gw1[y] = w1[...].astype(BF)
    pad = CLS_PAD - CLS
    gw2t[y] = jnp.concatenate([w2own[...], jnp.zeros((pad, 128), F32)], axis=0).astype(BF)
    gm1[y] = m1[...]
    gm2t[y] = jnp.concatenate([m2own[...], jnp.zeros((pad, 128), F32)], axis=0)
    gidx2[y] = jnp.concatenate(
        [idx2t[0:1, :], jnp.where(msk2t[...] > 0, idx2t[1:, :], -1), jnp.zeros((5, SEED), jnp.int32)], axis=0
    )
    shared = (gidx2, gw1, gw2t, gm1, gm2t)

    pl.semaphore_wait(barrier, DEV - 1)

    def ask(i, c):
        t = (me + i * 37) % DEV
        pltpu.make_async_remote_copy(
            src_ref=ask_rows.at[t], dst_ref=got_rows.at[me], send_sem=req_send, recv_sem=req_recv,
            device_id=all_to(t), device_id_type=MESH,
        ).start()
        return c

    lax.fori_loop(1, DEV, ask, 0)
    for n, a in enumerate(shared):
        for d in range(1, NAR):
            link(a.at[y], a.at[y], nar_send.at[n, d - 1], nar_recv.at[n, d - 1], (y + d) % NAR).start()

    reqin[pl.ds(me, 1), :] = reqv[pl.ds(me, 1), :]
    msk = msk1t[...]
    idxv[0:1, :] = idx1t[0:1, :]
    idxv[1:16, :] = jnp.where(msk > 0, idx1t[1:16, :], SRC)
    invv[...] = 1.0 / jnp.maximum(jnp.sum(msk.astype(F32), axis=0, keepdims=True), 1.0)
    to_smem = [pltpu.make_async_copy(idxv, idx, loc_sem.at[0]), pltpu.make_async_copy(invv, inv, loc_sem.at[1])]
    for c in to_smem:
        c.start()

    load.wait()

    def widen_features(i, c):
        rows = pl.ds(pl.multiple_of(i * 256, 256), 256)
        table[rows, :] = featb[rows, :].astype(F32)
        return c

    lax.fori_loop(0, OWN // 256, widen_features, 0)

    got = got_rows.at[pl.ds(0, DEV - 1)]
    pltpu.make_async_copy(got, got, req_recv).wait()
    fetch = pltpu.make_async_copy(reqin, reqs, loc_sem.at[2])
    fetch.start()
    fetch.wait()

    view = table.reshape(SRC + 8, 1, D_IN)
    my_rows = pl.ds(pl.multiple_of(me * CAP, CAP), CAP)

    def serve(i, c):
        t = (me + i * 37) % DEV
        for r in range(CAP):
            stage[r:r + 1, :] = view[reqs[t, r]]
        slot = pl.ds(pl.multiple_of(i * CAP, CAP), CAP)
        featb[slot, :] = stage[...].astype(BF)

        @pl.when(i > 0)
        def _():
            pltpu.make_async_remote_copy(
                src_ref=featb.at[slot], dst_ref=pulled.at[my_rows],
                send_sem=row_send, recv_sem=row_recv, device_id=all_to(t), device_id_type=MESH,
            ).start()

        return c

    lax.fori_loop(1, DEV, serve, 0)
    serve(0, 0)
    pulled[my_rows, :] = featb[0:CAP, :]

    for n, a in enumerate(shared):
        for d in range(1, NAR):
            link(a.at[y], a.at[y], nar_send.at[n, d - 1], nar_recv.at[n, d - 1], (y + d) % NAR).wait()
    for q in range(NAR):
        o_all[ROW_G1 + q * 64:ROW_G1 + q * 64 + 64, :] = MU * gm1[q, :, 0:128]
        o_all[ROW_G1 + 256 + q * 64:ROW_G1 + 256 + q * 64 + 64, :] = MU * gm1[q, :, 128:256]
    for q in range(NAR):
        w2t[:, q * 128:(q + 1) * 128] = gw2t[q]
    last = jnp.concatenate([bias[0:1, 384:428], jnp.zeros((1, 84), F32)], axis=1)
    b2c[...] = jnp.concatenate([spread(bias[0:1, 256:384]), spread(last)], axis=0)

    def column(row):
        return jnp.concatenate([spread(row[:, c * 128:(c + 1) * 128]) for c in range(SEED // 128)], axis=0)

    for q in range(NAR):
        n = jnp.sum((gidx2[q, 1:1 + F2, :] >= 0).astype(F32), axis=0, keepdims=True)
        invc[q] = column(1.0 / jnp.maximum(n, 1.0))
    livec[...] = column(2.0 * LAM / HID / SEEDS_ALL * live[...].astype(F32))

    lane16 = lax.broadcasted_iota(jnp.int32, (16, 128), 1).astype(jnp.int16)
    iota16 = lax.broadcasted_iota(jnp.int32, (16, 128), 0).astype(jnp.int16)
    one, zero = jnp.ones((16, 128), BF), jnp.zeros((16, 128), BF)

    def marks(here, want):
        acc = jnp.where(here == want[1], one, zero)
        for k in range(2, 1 + F2):
            acc = acc + jnp.where(here == want[k], one, zero)
        return acc, jnp.where(here == want[0], one, zero)

    idc[...] = gidx2[y].T

    def forward_marks(i, carry):
        at = pl.multiple_of(i * 16, 16)
        blk = idc[pl.ds(at, 16), :]
        want = [jnp.broadcast_to(blk[:, k:k + 1], (16, 128)).astype(jnp.int16) for k in range(1 + F2)]
        for q in range(NAR):
            for c in range(FRONT // 128):
                here = lane16 + jnp.full((16, 128), q * FRONT + c * 128, jnp.int32).astype(jnp.int16)
                a, b = marks(here, want)
                fsel[q, pl.ds(at, 16), c * 128:(c + 1) * 128] = a
                fsel[q, pl.ds(SEED + at, 16), c * 128:(c + 1) * 128] = b
        return carry

    lax.fori_loop(0, SEED // 16, forward_marks, 0)

    for q in range(NAR):
        ids = gidx2[q] - y * FRONT
        for c in range(SEED // 128):
            for k in range(1 + F2):
                row = ids[k:k + 1, c * 128:(c + 1) * 128]
                wants[q, c, k] = jnp.broadcast_to(row, (16, 128)).astype(jnp.int16)

    def backward_marks(i):
        here = iota16 + jnp.full((16, 128), i * 16, jnp.int32).astype(jnp.int16)
        out = pl.ds(pl.multiple_of(i * 16, 16), 16)
        for q in range(NAR):
            for c in range(SEED // 128):
                a, b = marks(here, [wants[q, c, k] for k in range(1 + F2)])
                bsel[q, out, c * 128:(c + 1) * 128] = a
                bsel[q, out, SEED + c * 128:SEED + (c + 1) * 128] = b

    come = pulled.at[pl.ds(0, (DEV - 1) * CAP)]
    pltpu.make_async_copy(come, come, row_recv).wait()
    gone = featb.at[pl.ds(0, (DEV - 1) * CAP)]
    pltpu.make_async_copy(gone, gone, row_send).wait()
    sent = ask_rows.at[pl.ds(0, DEV - 1)]
    pltpu.make_async_copy(sent, sent, req_send).wait()

    def widen(i, c):
        rows = pl.ds(pl.multiple_of(i * 256, 256), 256)
        table[rows, :] = pulled[rows, :].astype(F32)
        return c

    lax.fori_loop(0, SRC // 256, widen, 0)
    table[SRC:SRC + 8, :] = jnp.zeros((8, D_IN), F32)
    for c in to_smem:
        c.wait()

    def cols(b):
        return pl.ds(pl.multiple_of(b * 256, 256), 256)

    def forward(b):
        @pl.when(b % 2 == 0)
        def _():
            blk = gbuf.at[left, cols(b), :]
            link(blk, blk, h_send.at[0, b], h_recv.at[0, b], right).wait_recv()
            link(blk, blk, h_send.at[2, b], h_recv.at[2, b], right).start()

        @pl.when(b % 2 == 1)
        def _():
            blk = gbuf.at[right, cols(b), :]
            link(blk, blk, h_send.at[1, b], h_recv.at[1, b], left).wait_recv()
            link(blk, blk, h_send.at[2, b], h_recv.at[2, b], left).start()

    def block(b, c):
        def some(i, c2):
            backward_marks(b * 16 + i)
            base = pl.multiple_of(b * 256 + i * 16, 16)
            for j in range(16):
                m = base + j
                here = pl.ds(pl.multiple_of(i * 16, 16) + j, 1)
                own[here, :] = view[idx[0, m]]
                rows = [view[idx[1 + k, m]] for k in range(F1)]
                while len(rows) > 1:
                    rows = [p + q for p, q in zip(rows[::2], rows[1::2])] + ([rows[-1]] if len(rows) % 2 else [])
                near[here, :] = rows[0] * inv[0, m]
            return c2

        lax.fori_loop(0, 16, some, 0)
        rows = cols(b)
        act = jnp.concatenate([own[...].astype(BF), near[...].astype(BF)], axis=1)
        a1[rows, :] = act[:, :128]
        a1[pl.ds(pl.multiple_of(FRONT + b * 256, 256), 256), :] = act[:, 128:]
        z = dot(act, gw1[...].reshape(2 * D_IN, HID)) + bias[0:1, 0:HID]
        z1[rows, :] = z
        gbuf[y, rows, :] = (z / (1.0 + jnp.exp(-z))).astype(BF)
        blk = gbuf.at[y, rows, :]
        link(blk, blk, h_send.at[0, b], h_recv.at[0, b], right).start()
        link(blk, blk, h_send.at[1, b], h_recv.at[1, b], left).start()

        @pl.when(b > 0)
        def _():
            forward(b - 1)

        return c

    lax.fori_loop(0, 8, block, 0)
    forward(7)

    def from_source(q):
        return dot(fsel[q], gbuf[q])

    total = from_source(y)
    for b in range(1, 8, 2):
        blk = gbuf.at[left, b * 256:(b + 1) * 256, :]
        link(blk, blk, h_send.at[0, b], h_recv.at[0, b], right).wait_recv()
    total = total + from_source(left)
    for b in range(0, 8, 2):
        blk = gbuf.at[right, b * 256:(b + 1) * 256, :]
        link(blk, blk, h_send.at[1, b], h_recv.at[1, b], left).wait_recv()
    total = total + from_source(right)
    for b in range(8):
        blk = gbuf.at[opp, b * 256:(b + 1) * 256, :]
        link(blk, blk, h_send.at[2, b], h_recv.at[2, b], right).wait_recv()
    total = total + from_source(opp)

    def wide(a):
        return jnp.concatenate([a, a], axis=1)

    near2 = (total[:SEED, :] * wide(invc[y])).astype(BF)
    self2 = total[SEED:, :].astype(BF)
    alive = live[...].astype(F32)
    diff = self2.astype(F32) - near2.astype(F32)
    pull_apart = wide(livec[...]) * diff

    def swap_start(buf, ssem, rsem):
        blk = buf.at[y]
        link(blk, blk, ssem.at[0], rsem.at[0], right).start()
        link(blk, blk, ssem.at[1], rsem.at[1], left).start()

    def swap_forward(buf, ssem, rsem, cut):
        blk = buf.at[left]
        link(blk, blk, ssem.at[0], rsem.at[0], right).wait_recv()
        half = buf.at[left, 0:cut, :]
        link(half, half, ssem.at[2], rsem.at[2], right).start()
        blk = buf.at[right]
        link(blk, blk, ssem.at[1], rsem.at[1], left).wait_recv()
        half = buf.at[right, cut:, :]
        link(half, half, ssem.at[3], rsem.at[3], left).start()

    def swap_end(buf, ssem, rsem, cut):
        half = buf.at[opp, 0:cut, :]
        link(half, half, ssem.at[2], rsem.at[2], right).wait_recv()
        half = buf.at[opp, cut:, :]
        link(half, half, ssem.at[3], rsem.at[3], left).wait_recv()

    def swap_sent(buf, ssem, rsem, cut):
        blk = buf.at[y]
        link(blk, blk, ssem.at[0], rsem.at[0], right).wait_send()
        link(blk, blk, ssem.at[1], rsem.at[1], left).wait_send()
        half = buf.at[left, 0:cut, :]
        link(half, half, ssem.at[2], rsem.at[2], right).wait_send()
        half = buf.at[right, cut:, :]
        link(half, half, ssem.at[3], rsem.at[3], left).wait_send()

    rbuf[y] = pull_apart.astype(BF)
    swap_start(rbuf, r_send, r_recv)

    act2 = jnp.concatenate([self2, near2], axis=1)
    cls = lax.broadcasted_iota(jnp.int32, (CLS_PAD, SEED), 0)
    b2 = b2c[0:CLS_PAD, :]
    logits = dot(w2t[...], act2, NT) + jnp.concatenate([b2] * 4, axis=1)
    logits = jnp.where(cls < CLS, logits, -1e30)
    top = jnp.max(logits, axis=0, keepdims=True)
    e = jnp.exp(logits - top)
    tot = jnp.sum(e, axis=0, keepdims=True)
    hot = cls == labels[...]
    picked = jnp.sum(jnp.where(hot, logits, 0.0), axis=0, keepdims=True)
    dlog = (alive * (e * (1.0 / tot) - jnp.where(hot, 1.0, 0.0)) * (1.0 / SEEDS_ALL)).astype(BF)
    dbuf[y] = dlog
    swap_start(dbuf, d_send, d_recv)

    loss = jnp.sum(alive * (top + jnp.log(tot) - picked), axis=1, keepdims=True)
    loss = loss + SEEDS_ALL / 2 * jnp.sum(pull_apart * diff, keepdims=True)
    g2t = dot(dlog, act2).astype(BF)
    for q in range(NAR):
        pay2[q * CLS_PAD:(q + 1) * CLS_PAD, :] = g2t[:, q * 128:(q + 1) * 128]

    def plane(i):
        return ((g + i) % GRP, y)

    def to_owner(pay, inbox, count, n):
        def body(i, c):
            t = (g + i) % GRP
            for slot in range(2):
                p = t + slot * GRP

                @pl.when(p < count)
                def _():
                    pltpu.make_async_remote_copy(
                        src_ref=pay.at[pl.ds(pl.multiple_of(p * 16, 16), 16)], dst_ref=inbox.at[slot, g],
                        send_sem=rs_send.at[n], recv_sem=rs_recv.at[n, slot], device_id=(t, y), device_id_type=MESH,
                    ).start()

            return c

        lax.fori_loop(1, GRP, body, 0)

    def add_plane(pay, inbox, ybox, count, n):
        for slot in range(2):
            p = g + slot * GRP

            @pl.when(p < count)
            def _():
                got = inbox.at[slot, pl.ds(0, GRP - 1)]
                pltpu.make_async_copy(got, got, rs_recv.at[n, slot]).wait()
                inbox[slot, g] = pay[pl.ds(pl.multiple_of(p * 16, 16), 16), :]
                ybox[slot, y] = jnp.sum(inbox[slot].astype(F32), axis=0)
                blk = ybox.at[slot, y]
                for d in range(1, NAR):
                    link(blk, blk, y_send.at[n, slot, d - 1], y_recv.at[n, slot, d - 1], (y + d) % NAR).start()

    def add_group(ybox, res, count, n):
        for slot in range(2):
            p = g + slot * GRP

            @pl.when(p < count)
            def _():
                blk = ybox.at[slot, y]
                for d in range(1, NAR):
                    link(blk, blk, y_send.at[n, slot, d - 1], y_recv.at[n, slot, d - 1], (y + d) % NAR).wait()
                rows16 = pl.ds(pl.multiple_of(p * 16, 16), 16)
                res[rows16, :] = (ybox[slot, 0] + ybox[slot, 1]) + (ybox[slot, 2] + ybox[slot, 3])

                def tell(i, c):
                    pltpu.make_async_remote_copy(
                        src_ref=res.at[rows16], dst_ref=res.at[rows16], send_sem=ag_send.at[n], recv_sem=ag_recv.at[n],
                        device_id=plane(i), device_id_type=MESH,
                    ).start()
                    return c

                lax.fori_loop(1, GRP, tell, 0)

    def take(res, count, n):
        two_here = g + GRP < count
        for own, here in ((2, two_here), (1, jnp.logical_not(two_here))):
            @pl.when(here)
            def _(own=own):
                got = res.at[pl.ds(0, (count - own) * 16)]
                pltpu.make_async_copy(got, got, ag_recv.at[n]).wait()

    def sums_sent(pay, count, n):
        two_here = g + GRP < count
        for own, here in ((2, two_here), (1, jnp.logical_not(two_here))):
            @pl.when(here)
            def _(own=own):
                gone = pay.at[pl.ds(0, (count - own) * 16)]
                pltpu.make_async_copy(gone, gone, rs_send.at[n]).wait()
                gone = table.at[pl.ds(0, own * (GRP - 1) * 16)]
                pltpu.make_async_copy(gone, gone, ag_send.at[n]).wait()

    to_owner(pay2, inbox2, P2, 1)

    def add_grads(q, fresh=False):
        da = dot(dbuf[q], w2t[...], TN)
        r = rbuf[q].astype(F32)
        ds = (da[:, :HID] + r).astype(BF)
        dn = ((da[:, HID:] - r) * wide(invc[q])).astype(BF)
        part = dot(bsel[q], jnp.concatenate([dn, ds], axis=0))
        for c in range(2):
            rows = slice(c * FRONT, (c + 1) * FRONT)
            now = part[:, c * 128:(c + 1) * 128]
            dh1[rows, :] = now if fresh else dh1[rows, :] + now

    for c in range(2):
        a1t[c * 128:(c + 1) * 128, :] = a1[c * FRONT:(c + 1) * FRONT, :].T
    db2 = jnp.sum(dlog.astype(F32), axis=1, keepdims=True)
    db2 = jnp.broadcast_to(db2, (CLS_PAD, 128)).T[0:1, :]
    swap_forward(rbuf, r_send, r_recv, SEED // 2)
    add_grads(y, True)
    swap_forward(dbuf, d_send, d_recv, 96)
    add_grads(left)
    add_grads(right)
    add_plane(pay2, inbox2, ybox2, P2, 1)
    swap_end(rbuf, r_send, r_recv, SEED // 2)
    swap_end(dbuf, d_send, d_recv, 96)
    add_group(ybox2, res2, P2, 1)
    add_grads(opp)

    z = z1[...]
    sig = 1.0 / (1.0 + jnp.exp(-z))
    dh = jnp.concatenate([dh1[0:FRONT, :], dh1[FRONT:2 * FRONT, :]], axis=1)
    dz = (dh * sig * (1.0 + z * (1.0 - sig))).astype(BF)
    g1 = dot(a1t[...], dz).astype(BF)
    pay1[0:256, :] = g1[:, :128]
    pay1[256:512, :] = g1[:, 128:]
    db1 = jnp.sum(dz.astype(F32), axis=0, keepdims=True)
    misc[...] = jnp.zeros((16, 128), F32)

    def two(rows, v):
        hi = v.astype(BF).astype(F32)
        misc[rows:rows + 1, 0:v.shape[1]] = hi
        misc[rows + 4:rows + 5, 0:v.shape[1]] = v - hi

    two(0, db1[:, :128])
    two(1, db1[:, 128:])
    two(2, db2[:, :128])
    two(3, db2[:, 128:])
    hi = loss.astype(BF).astype(F32)
    misc[8:9, 0:1] = hi
    misc[9:10, 0:1] = loss - hi
    pay1[512:528, :] = misc[...].astype(BF)
    to_owner(pay1, inbox1, P1, 0)

    take(res2, P2, 1)
    mom2 = jnp.concatenate(
        [MU * gm2t[q] + res2[q * CLS_PAD:(q + 1) * CLS_PAD, :] for q in range(NAR)], axis=1
    )
    for q in range(NAR):
        x2s[q] = mom2[:, q * 128:(q + 1) * 128]
    o_all[ROW_M2:ROW_M2 + CLS_PAD, :] = x2s[y]
    x2 = mom2 * (1.0 / (jnp.sqrt(jnp.sum(mom2 * mom2, keepdims=True)) + 1e-07))
    x2 = ns_step(x2)
    add_plane(pay1, inbox1, ybox1, P1, 0)
    x2 = ns_step(x2)
    add_group(ybox1, o_all, P1, 0)
    for _ in range(NS_ITERS - 2):
        x2 = ns_step(x2)
    for q in range(NAR):
        x2s[q] = x2[:, q * 128:(q + 1) * 128]
    o_all[ROW_X2:ROW_X2 + CLS_PAD, :] = x2s[y]
    take(o_all, P1, 0)

    for b in range(8):
        blk = gbuf.at[y, b * 256:(b + 1) * 256, :]
        link(blk, blk, h_send.at[0, b], h_recv.at[0, b], right).wait_send()
        link(blk, blk, h_send.at[1, b], h_recv.at[1, b], left).wait_send()
        blk = gbuf.at[opp, b * 256:(b + 1) * 256, :]
        link(blk, blk, h_send.at[2, b], h_recv.at[2, b], right).wait_send()
    swap_sent(rbuf, r_send, r_recv, SEED // 2)
    swap_sent(dbuf, d_send, d_recv, 96)

    sums_sent(pay2, P2, 1)
    sums_sent(pay1, P1, 0)


def main(reqt, feat, idx1t, msk1t, idx2t, msk2t, labels, live, w1, w2own, m1, m2own, bias):
    vm = pl.BlockSpec(memory_space=pltpu.VMEM)
    dma = pltpu.SemaphoreType.DMA
    sds = jax.ShapeDtypeStruct
    V = pltpu.VMEM
    return pl.pallas_call(
        main_kernel,
        out_shape=sds((ROWS, 128), F32),
        in_specs=[vm, pl.BlockSpec(memory_space=pl.ANY)] + [vm] * 11,
        out_specs=vm,
        scratch_shapes=[
            V((SRC + 8, D_IN), F32),
            V((OWN, D_IN), BF),
            V((SRC, D_IN), BF),
            V((CAP, D_IN), F32),
            V((DEV, 128), jnp.int32),
            V((DEV, 128), jnp.int32),
            V((16, FRONT), jnp.int32),
            V((1, FRONT), F32),
            V((256, D_IN), F32),
            V((256, D_IN), F32),
            V((FRONT, HID), F32),
            V((2 * D_IN, FRONT), BF),
            V((NAR, FRONT, HID), BF),
            V((NAR, 2 * SEED, FRONT), BF),
            V((NAR, FRONT, 2 * SEED), BF),
            V((NAR, 4, 1 + F2, 16, 128), jnp.int16),
            V((SEED, 16), jnp.int32),
            V((NAR, SEED, 128), F32),
            V((SEED, 128), F32),
            V((NAR, SEED, HID), BF),
            V((NAR, CLS_PAD, SEED), BF),
            V((NAR, 64, HID), BF),
            V((NAR, CLS_PAD, 128), BF),
            V((NAR, 64, HID), F32),
            V((NAR, CLS_PAD, 128), F32),
            V((NAR, 16, SEED), jnp.int32),
            V((CLS_PAD, 2 * HID), BF),
            V((HID, 128), F32),
            V((P1 * 16, 128), BF),
            V((P2 * 16, 128), BF),
            V((16, 128), F32),
            V((2, GRP, 16, 128), BF),
            V((2, GRP, 16, 128), BF),
            V((2, NAR, 16, 128), F32),
            V((2, NAR, 16, 128), F32),
            V((P2 * 16, 128), F32),
            V((NAR, CLS_PAD, 128), F32),
            pltpu.SMEM((DEV, 128), jnp.int32),
            pltpu.SMEM((16, FRONT), jnp.int32),
            pltpu.SMEM((1, FRONT), F32),
            dma, dma((3,)), dma, dma, dma, dma, dma((5, 3)), dma((5, 3)),
            dma((3, 8)), dma((3, 8)), dma((4,)), dma((4,)), dma((4,)), dma((4,)),
            dma((2,)), dma((2, 2)), dma((2, 2, 3)), dma((2, 2, 3)), dma((2,)), dma((2,)),
        ],
        compiler_params=pltpu.CompilerParams(
            collective_id=0, has_side_effects=True, vmem_limit_bytes=62 * 2**20
        ),
    )(reqt, feat, idx1t, msk1t, idx2t, msk2t, labels, live, w1, w2own, m1, m2own, bias)


def update_kernel(
    res, w1own, w2own, bias, biasm, biasv,
    o_loss, o_first, o_second, o_mom1, o_mom2, o_flow, o_slow, o_bias, o_bm, o_bv,
    x1s,
):
    y = lax.axis_index("nar")
    mom1 = jnp.concatenate(
        [res[i * 256:i * 256 + 256, :] + res[ROW_G1 + i * 256:ROW_G1 + i * 256 + 256, :] for i in range(2)], axis=1
    )
    x1s[...] = mom1
    block64 = pl.ds(pl.multiple_of(y * 64, 64), 64)
    o_mom1[...] = x1s[block64, :]
    x1 = mom1 * (1.0 / (jnp.sqrt(jnp.sum(mom1 * mom1, keepdims=True)) + 1e-07))
    for _ in range(NS_ITERS):
        x1 = ns_step(x1)
    x1s[...] = x1
    first_new = w1own[...] * (1.0 - WDECAY) - x1s[block64, :]
    o_first[...] = first_new
    o_flow[...] = first_new.astype(BF)
    second = w2own[...] * (1.0 - WDECAY) - (2 * HID / CLS) ** 0.5 * res[ROW_X2:ROW_X2 + CLS, :]
    o_second[...] = second
    o_slow[...] = second.astype(BF)
    o_mom2[...] = res[ROW_M2:ROW_M2 + CLS, :]

    gb = res[512:516, :] + res[516:520, :]
    gb = jnp.concatenate([gb[0:1, :], gb[1:2, :], gb[2:3, :], gb[3:4, 0:44]], axis=1)
    m_new = BETA_ONE * biasm[...] + (1.0 - BETA_ONE) * gb
    v_new = BETA_TWO * biasv[...] + (1.0 - BETA_TWO) * gb * gb
    m_hat = m_new / (1.0 - BETA_ONE**STEP)
    v_hat = v_new / (1.0 - BETA_TWO**STEP)
    o_bias[...] = bias[...] * (1.0 - LR_BIAS * WDECAY) - LR_BIAS * m_hat / (jnp.sqrt(v_hat) + EPSILON)
    o_bm[...] = m_new
    o_bv[...] = v_new
    o_loss[...] = res[520:521, 0:1] + res[521:522, 0:1]


def update(*args):
    vm = pl.BlockSpec(memory_space=pltpu.VMEM)
    sds = jax.ShapeDtypeStruct
    return pl.pallas_call(
        update_kernel,
        out_shape=[
            sds((1, 1), F32), sds((64, HID), F32), sds((CLS, 128), F32), sds((64, HID), F32), sds((CLS, 128), F32),
            sds((64, HID), BF), sds((CLS, 128), BF), sds((1, 428), F32), sds((1, 428), F32), sds((1, 428), F32),
        ],
        in_specs=[vm] * 6,
        out_specs=[vm] * 10,
        scratch_shapes=[pltpu.VMEM((2 * D_IN, HID), F32)],
        compiler_params=pltpu.CompilerParams(vmem_limit_bytes=32 * 2**20),
    )(*args)


def per_device(
    features, requests, index_one, mask_one, index_two, mask_two, labels, seed_live,
    w_first, w_second, mom_first, mom_second, biases, bias_m, bias_v,
):
    w2own, bias = w_second.T, biases[None, :]
    res = main(
        requests.T, features, index_one.T, mask_one.T, index_two.T, mask_two.T, labels[None, :], seed_live[None, :],
        w_first, w2own, mom_first, mom_second.T, bias,
    )
    loss, first_new, second_new, mom_one, mom_two, first_low, second_low, bias_new, m_new, v_new = update(
        res, w_first, w2own, bias, bias_m[None, :], bias_v[None, :]
    )
    return (
        loss.reshape(()), first_new, second_new.T, mom_one, mom_two.T, first_low, second_low.T,
        bias_new.reshape(-1), m_new.reshape(-1), v_new.reshape(-1),
    )


def solution(mesh):
    both = ("grp", "nar")
    placed = (
        P(both, None), P(both, None), P(both, None), P(both, None), P(both, None), P(both, None),
        P(both), P(both), P("nar", None), P("nar", None), P("nar", None), P("nar", None), P(), P(), P(),
    )
    nar = P("nar", None)
    return jax.shard_map(
        per_device, mesh=mesh, in_specs=placed,
        out_specs=(P(), nar, nar, nar, nar, nar, nar, P(), P(), P()), check_vma=False,
    )
```

```python
import functools

import jax
import jax.numpy as jnp
from jax import lax
from jax.experimental import pallas as pl
from jax.experimental.pallas import tpu as pltpu
from jax.sharding import PartitionSpec as P

HID = 256
CLS = 172
CLS_PAD = 176
D_IN = 128
F1 = 15
F2 = 10
NS_ITERS = 5
STEP = 10
LAM = 0.5
MU = 0.95
WDECAY = 0.01
LR_BIAS = 0.05
BETA_ONE = 0.9
BETA_TWO = 0.999
EPSILON = 1e-08
NS_A = 3.4445
NS_B = -4.775
NS_C = 2.0315
HIGH = lax.Precision.HIGHEST
MESH = pl.DeviceIdType.MESH
BF = jnp.bfloat16
F32 = jnp.float32

DEV = 128
NAR = 4
OWN = 8192
CAP = 64
SRC = 8192
FRONT = 2048
SEED = 512


def all_to(t):
    return (t // NAR, t % NAR)


P1 = 33
P2 = 44
GRP = 32
ROW_G1 = P1 * 16
ROW_M2 = ROW_G1 + 512
ROW_X2 = ROW_M2 + CLS_PAD
ROWS = ROW_X2 + CLS_PAD
SEEDS_ALL = SEED * DEV


def dot(a, b, dims=((1,), (0,))):
    return lax.dot_general(a, b, (dims, ((), ())), preferred_element_type=F32)


NN = ((1,), (0,))
NT = ((1,), (1,))
TN = ((0,), (0,))


def split(a):
    hi = a.astype(BF)
    return hi, (a - hi.astype(F32)).astype(BF)


def dot3(a, b, dims):
    (ah, al), (bh, bl) = a, b
    return dot(ah, bh, dims) + (dot(ah, bl, dims) + dot(al, bh, dims))


def ns_step(x):
    xs = split(x)
    gram = dot3(xs, xs, NT)
    gs = split(gram)
    mix = NS_B * gram + NS_C * dot3(gs, gs, NN)
    return NS_A * x + dot3(split(mix), xs, NN)


def spread(row):
    return jnp.broadcast_to(row, (128, 128)).T


def main_kernel(
    reqt, feat, idx1t, msk1t, idx2t, msk2t, labels, live, w1, w2own, m1, m2own, bias,
    o_all,
    table, featb, pulled, stage, reqv, reqin, idxv, invv, near, own, z1, a1t, gbuf, fsel, bsel, wants, idc, invc, livec, rbuf, dbuf,
    gw1, gw2t, gm1, gm2t, gidx2, w2t, b2c, pay1, pay2, misc, inbox1, inbox2, ybox1, ybox2, res2, x2s,
    reqs, idx, inv,
    feat_sem, loc_sem, ask_sem, req_send, req_recv, row_send, row_recv, nar_send, nar_recv,
    h_send, h_recv, r_send, r_recv, d_send, d_recv, rs_send, rs_recv, y_send, y_recv, ag_send, ag_recv,
):
    a1, dh1 = pulled, table
    g = lax.axis_index("grp")
    y = lax.axis_index("nar")
    me = g * NAR + y
    left, right, opp = (y + 3) % NAR, (y + 1) % NAR, (y + 2) % NAR

    load = pltpu.make_async_copy(feat, featb, feat_sem)
    load.start()

    barrier = pltpu.get_barrier_semaphore()

    ys = [(y + d) % NAR for d in range(NAR)]

    def greet(i, c):
        t = (g + i) % GRP
        for d in range(NAR):
            pl.semaphore_signal(barrier, inc=1, device_id=(t, ys[d]), device_id_type=MESH)
        return c

    for d in range(1, NAR):
        pl.semaphore_signal(barrier, inc=1, device_id=(g, ys[d]), device_id_type=MESH)
    lax.fori_loop(1, GRP, greet, 0)

    def link(src, dst, ssem, rsem, to):
        return pltpu.make_async_remote_copy(
            src_ref=src, dst_ref=dst, send_sem=ssem, recv_sem=rsem, device_id=(g, to), device_id_type=MESH
        )

    reqv[...] = jnp.concatenate([reqt[...], jnp.zeros((DEV - CAP, DEV), jnp.int32)], axis=0).T
    ask_rows = reqv.reshape(DEV, 1, 128)
    got_rows = reqin.reshape(DEV, 1, 128)

    gw1[y] = w1[...].astype(BF)
    pad = CLS_PAD - CLS
    gw2t[y] = jnp.concatenate([w2own[...], jnp.zeros((pad, 128), F32)], axis=0).astype(BF)
    gm1[y] = m1[...]
    gm2t[y] = jnp.concatenate([m2own[...], jnp.zeros((pad, 128), F32)], axis=0)
    gidx2[y] = jnp.concatenate(
        [idx2t[0:1, :], jnp.where(msk2t[...] > 0, idx2t[1:, :], -1), jnp.zeros((5, SEED), jnp.int32)], axis=0
    )
    shared = (gidx2, gw1, gw2t, gm1, gm2t)

    pl.semaphore_wait(barrier, DEV - 1)

    def ask_one(t, u, n):
        row = t * NAR + u
        pltpu.make_async_remote_copy(
            src_ref=ask_rows.at[row], dst_ref=got_rows.at[me], send_sem=req_send, recv_sem=req_recv.at[n],
            device_id=(t, u), device_id_type=MESH,
        ).start()

    def ask(i, c):
        n = (i * 13) % GRP
        t = (g + n) % GRP
        for d in range(NAR):
            ask_one(t, ys[d], n)
        return c

    for d in range(1, NAR):
        ask_one(g, ys[d], 0)
    lax.fori_loop(1, GRP, ask, 0)
    reqin[pl.ds(me, 1), :] = reqv[pl.ds(me, 1), :]
    for n, a in enumerate(shared):
        for d in range(1, NAR):
            link(a.at[y], a.at[y], nar_send.at[n, d - 1], nar_recv.at[n, d - 1], (y + d) % NAR).start()

    msk = msk1t[...]
    idxv[0:1, :] = idx1t[0:1, :]
    idxv[1:16, :] = jnp.where(msk > 0, idx1t[1:16, :], SRC)
    invv[...] = 1.0 / jnp.maximum(jnp.sum(msk.astype(F32), axis=0, keepdims=True), 1.0)
    to_smem = [pltpu.make_async_copy(idxv, idx, loc_sem.at[0]), pltpu.make_async_copy(invv, inv, loc_sem.at[1])]
    for c in to_smem:
        c.start()

    load.wait()

    def widen_features(i, c):
        rows = pl.ds(pl.multiple_of(i * 256, 256), 256)
        table[rows, :] = featb[rows, :].astype(F32)
        return c

    lax.fori_loop(0, OWN // 256, widen_features, 0)

    view = table.reshape(SRC + 8, 1, D_IN)
    my_rows = pl.ds(pl.multiple_of(me * CAP, CAP), CAP)

    def pick(t, u, slot):
        for r in range(CAP):
            stage[r:r + 1, :] = view[reqs[t * NAR + u, 0, r]]
        featb[slot, :] = stage[...].astype(BF)

    def serve_one(t, u, slot):
        pick(t, u, slot)
        pltpu.make_async_remote_copy(
            src_ref=featb.at[slot], dst_ref=pulled.at[my_rows],
            send_sem=row_send, recv_sem=row_recv, device_id=(t, u), device_id_type=MESH,
        ).start()

    def asked(count, n):
        rows = got_rows.at[pl.ds(0, count)]
        pltpu.make_async_copy(rows, rows, req_recv.at[n]).wait()

    def to_scalars(t, n):
        rows = pl.ds(pl.multiple_of(t * NAR, NAR), NAR)
        return pltpu.make_async_copy(got_rows.at[rows], reqs.at[rows], ask_sem.at[n])

    def whose(i):
        n = (i * 13) % GRP
        return n, (g + GRP - n) % GRP

    def fetch(i):
        n, t = whose(i)
        asked(NAR, n)
        to_scalars(t, n).start()

    def serve(i, c):
        n, t = whose(i)

        @pl.when(i < GRP - 1)
        def _():
            fetch(i + 1)

        to_scalars(t, n).wait()
        for d in range(NAR):
            serve_one(t, ys[d], pl.ds(pl.multiple_of((i * NAR + d) * CAP, CAP), CAP))
        return c

    fetch(1)
    lax.fori_loop(1, GRP, serve, 0)
    asked(NAR - 1, 0)
    to_scalars(g, 0).start()
    to_scalars(g, 0).wait()
    for d in range(1, NAR):
        serve_one(g, ys[d], pl.ds(d * CAP, CAP))
    pick(g, y, pl.ds(0, CAP))
    pulled[my_rows, :] = featb[0:CAP, :]

    for n, a in enumerate(shared):
        for d in range(1, NAR):
            link(a.at[y], a.at[y], nar_send.at[n, d - 1], nar_recv.at[n, d - 1], (y + d) % NAR).wait()
    for q in range(NAR):
        o_all[ROW_G1 + q * 64:ROW_G1 + q * 64 + 64, :] = MU * gm1[q, :, 0:128]
        o_all[ROW_G1 + 256 + q * 64:ROW_G1 + 256 + q * 64 + 64, :] = MU * gm1[q, :, 128:256]
    for q in range(NAR):
        w2t[:, q * 128:(q + 1) * 128] = gw2t[q]
    last = jnp.concatenate([bias[0:1, 384:428], jnp.zeros((1, 84), F32)], axis=1)
    b2c[...] = jnp.concatenate([spread(bias[0:1, 256:384]), spread(last)], axis=0)

    def column(row):
        return jnp.concatenate([spread(row[:, c * 128:(c + 1) * 128]) for c in range(SEED // 128)], axis=0)

    for q in range(NAR):
        n = jnp.sum((gidx2[q, 1:1 + F2, :] >= 0).astype(F32), axis=0, keepdims=True)
        invc[q] = column(1.0 / jnp.maximum(n, 1.0))
    livec[...] = column(2.0 * LAM / HID / SEEDS_ALL * live[...].astype(F32))

    lane16 = lax.broadcasted_iota(jnp.int32, (16, 128), 1).astype(jnp.int16)
    iota16 = lax.broadcasted_iota(jnp.int32, (16, 128), 0).astype(jnp.int16)
    one, zero = jnp.ones((16, 128), BF), jnp.zeros((16, 128), BF)

    def marks(here, want):
        acc = jnp.where(here == want[1], one, zero)
        for k in range(2, 1 + F2):
            acc = acc + jnp.where(here == want[k], one, zero)
        return acc, jnp.where(here == want[0], one, zero)

    idc[...] = gidx2[y].T

    def forward_marks(i, carry):
        at = pl.multiple_of(i * 16, 16)
        blk = idc[pl.ds(at, 16), :]
        want = [jnp.broadcast_to(blk[:, k:k + 1], (16, 128)).astype(jnp.int16) for k in range(1 + F2)]
        for q in range(NAR):
            for c in range(FRONT // 128):
                here = lane16 + jnp.full((16, 128), q * FRONT + c * 128, jnp.int32).astype(jnp.int16)
                a, b = marks(here, want)
                fsel[q, pl.ds(at, 16), c * 128:(c + 1) * 128] = a
                fsel[q, pl.ds(SEED + at, 16), c * 128:(c + 1) * 128] = b
        return carry

    lax.fori_loop(0, SEED // 16, forward_marks, 0)

    for q in range(NAR):
        ids = gidx2[q] - y * FRONT
        for c in range(SEED // 128):
            for k in range(1 + F2):
                row = ids[k:k + 1, c * 128:(c + 1) * 128]
                wants[q, c, k] = jnp.broadcast_to(row, (16, 128)).astype(jnp.int16)

    def backward_marks(i):
        here = iota16 + jnp.full((16, 128), i * 16, jnp.int32).astype(jnp.int16)
        out = pl.ds(pl.multiple_of(i * 16, 16), 16)
        for q in range(NAR):
            for c in range(SEED // 128):
                a, b = marks(here, [wants[q, c, k] for k in range(1 + F2)])
                bsel[q, out, c * 128:(c + 1) * 128] = a
                bsel[q, out, SEED + c * 128:SEED + (c + 1) * 128] = b

    come = pulled.at[pl.ds(0, (DEV - 1) * CAP)]
    pltpu.make_async_copy(come, come, row_recv).wait()
    gone = featb.at[pl.ds(CAP, (DEV - 1) * CAP)]
    pltpu.make_async_copy(gone, gone, row_send).wait()
    sent = ask_rows.at[pl.ds(0, DEV - 1)]
    pltpu.make_async_copy(sent, sent, req_send).wait()

    def widen(i, c):
        rows = pl.ds(pl.multiple_of(i * 256, 256), 256)
        table[rows, :] = pulled[rows, :].astype(F32)
        return c

    lax.fori_loop(0, SRC // 256, widen, 0)
    table[SRC:SRC + 8, :] = jnp.zeros((8, D_IN), F32)
    for c in to_smem:
        c.wait()

    def cols(b):
        return pl.ds(pl.multiple_of(b * 256, 256), 256)

    def forward(b):
        @pl.when(b % 2 == 0)
        def _():
            blk = gbuf.at[left, cols(b), :]
            link(blk, blk, h_send.at[0, b], h_recv.at[0, b], right).wait_recv()
            link(blk, blk, h_send.at[2, b], h_recv.at[2, b], right).start()

        @pl.when(b % 2 == 1)
        def _():
            blk = gbuf.at[right, cols(b), :]
            link(blk, blk, h_send.at[1, b], h_recv.at[1, b], left).wait_recv()
            link(blk, blk, h_send.at[2, b], h_recv.at[2, b], left).start()

    def finish(n):
        rows = pl.ds(pl.multiple_of(n * 16, 16), 16)
        act = jnp.concatenate([own[...].astype(BF), near[...].astype(BF)], axis=1)
        a1[rows, :] = act[:, :128]
        a1[pl.ds(pl.multiple_of(FRONT + n * 16, 16), 16), :] = act[:, 128:]
        z = dot(act, gw1[...].reshape(2 * D_IN, HID)) + bias[0:1, 0:HID]
        z1[rows, :] = z
        gbuf[y, rows, :] = (z / (1.0 + jnp.exp(-z))).astype(BF)

    def send(b):
        blk = gbuf.at[y, cols(b), :]
        link(blk, blk, h_send.at[0, b], h_recv.at[0, b], right).start()
        link(blk, blk, h_send.at[1, b], h_recv.at[1, b], left).start()

    def some(n, c):
        finish(jnp.maximum(n - 1, 0))
        backward_marks(n)
        for j in range(16):
            m = n * 16 + j
            own[j:j + 1, :] = view[idx[0, m]]
            rows = [view[idx[1 + k, m]] for k in range(F1)]
            while len(rows) > 1:
                rows = [p + q for p, q in zip(rows[::2], rows[1::2])] + ([rows[-1]] if len(rows) % 2 else [])
            near[j:j + 1, :] = rows[0] * inv[0, m]

        @pl.when((n > 0) & (n % 16 == 0))
        def _():
            send(n // 16 - 1)

        @pl.when((n > 16) & (n % 16 == 0))
        def _():
            forward(n // 16 - 2)

        return c

    own[...] = jnp.zeros((16, D_IN), F32)
    near[...] = jnp.zeros((16, D_IN), F32)
    lax.fori_loop(0, FRONT // 16, some, 0)
    finish(FRONT // 16 - 1)
    send(7)
    forward(6)
    forward(7)

    def from_source(q):
        return dot(fsel[q], gbuf[q])

    total = from_source(y)
    for b in range(1, 8, 2):
        blk = gbuf.at[left, b * 256:(b + 1) * 256, :]
        link(blk, blk, h_send.at[0, b], h_recv.at[0, b], right).wait_recv()
    total = total + from_source(left)
    for b in range(0, 8, 2):
        blk = gbuf.at[right, b * 256:(b + 1) * 256, :]
        link(blk, blk, h_send.at[1, b], h_recv.at[1, b], left).wait_recv()
    total = total + from_source(right)
    for b in range(8):
        blk = gbuf.at[opp, b * 256:(b + 1) * 256, :]
        link(blk, blk, h_send.at[2, b], h_recv.at[2, b], right).wait_recv()
    total = total + from_source(opp)

    def wide(a):
        return jnp.concatenate([a, a], axis=1)

    near2 = (total[:SEED, :] * wide(invc[y])).astype(BF)
    self2 = total[SEED:, :].astype(BF)
    alive = live[...].astype(F32)
    diff = self2.astype(F32) - near2.astype(F32)
    pull_apart = wide(livec[...]) * diff

    def swap_start(buf, ssem, rsem):
        blk = buf.at[y]
        link(blk, blk, ssem.at[0], rsem.at[0], right).start()
        link(blk, blk, ssem.at[1], rsem.at[1], left).start()

    def swap_forward(buf, ssem, rsem, cut):
        blk = buf.at[left]
        link(blk, blk, ssem.at[0], rsem.at[0], right).wait_recv()
        half = buf.at[left, 0:cut, :]
        link(half, half, ssem.at[2], rsem.at[2], right).start()
        blk = buf.at[right]
        link(blk, blk, ssem.at[1], rsem.at[1], left).wait_recv()
        half = buf.at[right, cut:, :]
        link(half, half, ssem.at[3], rsem.at[3], left).start()

    def swap_end(buf, ssem, rsem, cut):
        half = buf.at[opp, 0:cut, :]
        link(half, half, ssem.at[2], rsem.at[2], right).wait_recv()
        half = buf.at[opp, cut:, :]
        link(half, half, ssem.at[3], rsem.at[3], left).wait_recv()

    def swap_sent(buf, ssem, rsem, cut):
        blk = buf.at[y]
        link(blk, blk, ssem.at[0], rsem.at[0], right).wait_send()
        link(blk, blk, ssem.at[1], rsem.at[1], left).wait_send()
        half = buf.at[left, 0:cut, :]
        link(half, half, ssem.at[2], rsem.at[2], right).wait_send()
        half = buf.at[right, cut:, :]
        link(half, half, ssem.at[3], rsem.at[3], left).wait_send()

    rbuf[y] = pull_apart.astype(BF)
    swap_start(rbuf, r_send, r_recv)

    act2 = jnp.concatenate([self2, near2], axis=1)
    cls = lax.broadcasted_iota(jnp.int32, (CLS_PAD, SEED), 0)
    b2 = b2c[0:CLS_PAD, :]
    logits = dot(w2t[...], act2, NT) + jnp.concatenate([b2] * 4, axis=1)
    logits = jnp.where(cls < CLS, logits, -1e30)
    top = jnp.max(logits, axis=0, keepdims=True)
    e = jnp.exp(logits - top)
    tot = jnp.sum(e, axis=0, keepdims=True)
    hot = cls == labels[...]
    picked = jnp.sum(jnp.where(hot, logits, 0.0), axis=0, keepdims=True)
    dlog = (alive * (e * (1.0 / tot) - jnp.where(hot, 1.0, 0.0)) * (1.0 / SEEDS_ALL)).astype(BF)
    dbuf[y] = dlog
    swap_start(dbuf, d_send, d_recv)

    loss = jnp.sum(alive * (top + jnp.log(tot) - picked), axis=1, keepdims=True)
    loss = loss + SEEDS_ALL / 2 * jnp.sum(pull_apart * diff, keepdims=True)
    g2t = dot(dlog, act2).astype(BF)
    for q in range(NAR):
        pay2[q * CLS_PAD:(q + 1) * CLS_PAD, :] = g2t[:, q * 128:(q + 1) * 128]

    def plane(i):
        return ((g + i) % GRP, y)

    def to_owner(pay, inbox, count, n):
        def body(i, c):
            t = (g + i) % GRP
            for slot in range(2):
                p = t + slot * GRP

                @pl.when(p < count)
                def _():
                    pltpu.make_async_remote_copy(
                        src_ref=pay.at[pl.ds(pl.multiple_of(p * 16, 16), 16)], dst_ref=inbox.at[slot, g],
                        send_sem=rs_send.at[n], recv_sem=rs_recv.at[n, slot], device_id=(t, y), device_id_type=MESH,
                    ).start()

            return c

        lax.fori_loop(1, GRP, body, 0)

    def add_plane(pay, inbox, ybox, count, n):
        for slot in range(2):
            p = g + slot * GRP

            @pl.when(p < count)
            def _():
                got = inbox.at[slot, pl.ds(0, GRP - 1)]
                pltpu.make_async_copy(got, got, rs_recv.at[n, slot]).wait()
                inbox[slot, g] = pay[pl.ds(pl.multiple_of(p * 16, 16), 16), :]
                ybox[slot, y] = jnp.sum(inbox[slot].astype(F32), axis=0)
                blk = ybox.at[slot, y]
                for d in range(1, NAR):
                    link(blk, blk, y_send.at[n, slot, d - 1], y_recv.at[n, slot, d - 1], (y + d) % NAR).start()

    def add_group(ybox, res, count, n):
        for slot in range(2):
            p = g + slot * GRP

            @pl.when(p < count)
            def _():
                blk = ybox.at[slot, y]
                for d in range(1, NAR):
                    link(blk, blk, y_send.at[n, slot, d - 1], y_recv.at[n, slot, d - 1], (y + d) % NAR).wait()
                rows16 = pl.ds(pl.multiple_of(p * 16, 16), 16)
                res[rows16, :] = (ybox[slot, 0] + ybox[slot, 1]) + (ybox[slot, 2] + ybox[slot, 3])

                def tell(i, c):
                    pltpu.make_async_remote_copy(
                        src_ref=res.at[rows16], dst_ref=res.at[rows16], send_sem=ag_send.at[n], recv_sem=ag_recv.at[n],
                        device_id=plane(i), device_id_type=MESH,
                    ).start()
                    return c

                lax.fori_loop(1, GRP, tell, 0)

    def take(res, count, n):
        two_here = g + GRP < count
        for own, here in ((2, two_here), (1, jnp.logical_not(two_here))):
            @pl.when(here)
            def _(own=own):
                got = res.at[pl.ds(0, (count - own) * 16)]
                pltpu.make_async_copy(got, got, ag_recv.at[n]).wait()

    def sums_sent(pay, count, n):
        two_here = g + GRP < count
        for own, here in ((2, two_here), (1, jnp.logical_not(two_here))):
            @pl.when(here)
            def _(own=own):
                gone = pay.at[pl.ds(0, (count - own) * 16)]
                pltpu.make_async_copy(gone, gone, rs_send.at[n]).wait()
                gone = table.at[pl.ds(0, own * (GRP - 1) * 16)]
                pltpu.make_async_copy(gone, gone, ag_send.at[n]).wait()

    to_owner(pay2, inbox2, P2, 1)

    def add_grads(q, fresh=False):
        da = dot(dbuf[q], w2t[...], TN)
        r = rbuf[q].astype(F32)
        ds = (da[:, :HID] + r).astype(BF)
        dn = ((da[:, HID:] - r) * wide(invc[q])).astype(BF)
        both = jnp.concatenate([dn, ds], axis=0)

        def rows512(i, c):
            part = dot(bsel[q, pl.ds(pl.multiple_of(i * 512, 512), 512), :], both)
            for h in range(2):
                rows = pl.ds(pl.multiple_of(h * FRONT + i * 512, 512), 512)
                now = part[:, h * 128:(h + 1) * 128]
                dh1[rows, :] = now if fresh else dh1[rows, :] + now
            return c

        lax.fori_loop(0, FRONT // 512, rows512, 0)

    for c in range(2):
        a1t[c * 128:(c + 1) * 128, :] = a1[c * FRONT:(c + 1) * FRONT, :].T
    db2 = jnp.sum(dlog.astype(F32), axis=1, keepdims=True)
    db2 = jnp.broadcast_to(db2, (CLS_PAD, 128)).T[0:1, :]
    swap_forward(rbuf, r_send, r_recv, SEED // 2)
    add_grads(y, True)
    swap_forward(dbuf, d_send, d_recv, 96)
    add_grads(left)
    add_grads(right)
    add_plane(pay2, inbox2, ybox2, P2, 1)
    swap_end(rbuf, r_send, r_recv, SEED // 2)
    swap_end(dbuf, d_send, d_recv, 96)
    add_group(ybox2, res2, P2, 1)
    add_grads(opp)

    def to_z(i, db):
        z = z1[pl.ds(pl.multiple_of(i * 128, 128), 128), :]
        sig = 1.0 / (1.0 + jnp.exp(-z))
        dh = jnp.concatenate(
            [dh1[pl.ds(pl.multiple_of(h * FRONT + i * 128, 128), 128), :] for h in range(2)], axis=1
        )
        dz = dh * sig * (1.0 + z * (1.0 - sig))
        low = dz.astype(BF)
        for h in range(2):
            a1[pl.ds(pl.multiple_of((2 + h) * FRONT + i * 128, 128), 128), :] = low[:, h * 128:(h + 1) * 128]
        return db + jnp.sum(low.astype(F32), axis=0, keepdims=True)

    db1 = lax.fori_loop(0, FRONT // 128, to_z, jnp.zeros((1, HID), F32))
    dz = jnp.concatenate([a1[2 * FRONT:3 * FRONT, :], a1[3 * FRONT:4 * FRONT, :]], axis=1)
    g1 = dot(a1t[...], dz).astype(BF)
    pay1[0:256, :] = g1[:, :128]
    pay1[256:512, :] = g1[:, 128:]
    misc[...] = jnp.zeros((16, 128), F32)

    def two(rows, v):
        hi = v.astype(BF).astype(F32)
        misc[rows:rows + 1, 0:v.shape[1]] = hi
        misc[rows + 4:rows + 5, 0:v.shape[1]] = v - hi

    two(0, db1[:, :128])
    two(1, db1[:, 128:])
    two(2, db2[:, :128])
    two(3, db2[:, 128:])
    hi = loss.astype(BF).astype(F32)
    misc[8:9, 0:1] = hi
    misc[9:10, 0:1] = loss - hi
    pay1[512:528, :] = misc[...].astype(BF)
    to_owner(pay1, inbox1, P1, 0)

    take(res2, P2, 1)
    mom2 = jnp.concatenate(
        [MU * gm2t[q] + res2[q * CLS_PAD:(q + 1) * CLS_PAD, :] for q in range(NAR)], axis=1
    )
    for q in range(NAR):
        x2s[q] = mom2[:, q * 128:(q + 1) * 128]
    o_all[ROW_M2:ROW_M2 + CLS_PAD, :] = x2s[y]
    x2 = mom2 * (1.0 / (jnp.sqrt(jnp.sum(mom2 * mom2, keepdims=True)) + 1e-07))
    x2 = ns_step(x2)
    add_plane(pay1, inbox1, ybox1, P1, 0)
    x2 = ns_step(x2)
    add_group(ybox1, o_all, P1, 0)
    for _ in range(NS_ITERS - 2):
        x2 = ns_step(x2)
    for q in range(NAR):
        x2s[q] = x2[:, q * 128:(q + 1) * 128]
    o_all[ROW_X2:ROW_X2 + CLS_PAD, :] = x2s[y]
    take(o_all, P1, 0)

    for b in range(8):
        blk = gbuf.at[y, b * 256:(b + 1) * 256, :]
        link(blk, blk, h_send.at[0, b], h_recv.at[0, b], right).wait_send()
        link(blk, blk, h_send.at[1, b], h_recv.at[1, b], left).wait_send()
        blk = gbuf.at[opp, b * 256:(b + 1) * 256, :]
        link(blk, blk, h_send.at[2, b], h_recv.at[2, b], right).wait_send()
    swap_sent(rbuf, r_send, r_recv, SEED // 2)
    swap_sent(dbuf, d_send, d_recv, 96)

    sums_sent(pay2, P2, 1)
    sums_sent(pay1, P1, 0)


def main(reqt, feat, idx1t, msk1t, idx2t, msk2t, labels, live, w1, w2own, m1, m2own, bias):
    vm = pl.BlockSpec(memory_space=pltpu.VMEM)
    dma = pltpu.SemaphoreType.DMA
    sds = jax.ShapeDtypeStruct
    V = pltpu.VMEM
    return pl.pallas_call(
        main_kernel,
        out_shape=sds((ROWS, 128), F32),
        in_specs=[vm, pl.BlockSpec(memory_space=pl.ANY)] + [vm] * 11,
        out_specs=vm,
        scratch_shapes=[
            V((SRC + 8, D_IN), F32),
            V((OWN, D_IN), BF),
            V((SRC, D_IN), BF),
            V((CAP, D_IN), F32),
            V((DEV, 128), jnp.int32),
            V((DEV, 128), jnp.int32),
            V((16, FRONT), jnp.int32),
            V((1, FRONT), F32),
            V((16, D_IN), F32),
            V((16, D_IN), F32),
            V((FRONT, HID), F32),
            V((2 * D_IN, FRONT), BF),
            V((NAR, FRONT, HID), BF),
            V((NAR, 2 * SEED, FRONT), BF),
            V((NAR, FRONT, 2 * SEED), BF),
            V((NAR, 4, 1 + F2, 16, 128), jnp.int16),
            V((SEED, 16), jnp.int32),
            V((NAR, SEED, 128), F32),
            V((SEED, 128), F32),
            V((NAR, SEED, HID), BF),
            V((NAR, CLS_PAD, SEED), BF),
            V((NAR, 64, HID), BF),
            V((NAR, CLS_PAD, 128), BF),
            V((NAR, 64, HID), F32),
            V((NAR, CLS_PAD, 128), F32),
            V((NAR, 16, SEED), jnp.int32),
            V((CLS_PAD, 2 * HID), BF),
            V((HID, 128), F32),
            V((P1 * 16, 128), BF),
            V((P2 * 16, 128), BF),
            V((16, 128), F32),
            V((2, GRP, 16, 128), BF),
            V((2, GRP, 16, 128), BF),
            V((2, NAR, 16, 128), F32),
            V((2, NAR, 16, 128), F32),
            V((P2 * 16, 128), F32),
            V((NAR, CLS_PAD, 128), F32),
            pltpu.SMEM((DEV, 1, 128), jnp.int32),
            pltpu.SMEM((16, FRONT), jnp.int32),
            pltpu.SMEM((1, FRONT), F32),
            dma, dma((2,)), dma((GRP,)), dma, dma((GRP,)), dma, dma, dma((5, 3)), dma((5, 3)),
            dma((3, 8)), dma((3, 8)), dma((4,)), dma((4,)), dma((4,)), dma((4,)),
            dma((2,)), dma((2, 2)), dma((2, 2, 3)), dma((2, 2, 3)), dma((2,)), dma((2,)),
        ],
        compiler_params=pltpu.CompilerParams(
            collective_id=0, has_side_effects=True, vmem_limit_bytes=62 * 2**20
        ),
    )(reqt, feat, idx1t, msk1t, idx2t, msk2t, labels, live, w1, w2own, m1, m2own, bias)


def update_kernel(
    res, w1own, w2own, bias, biasm, biasv,
    o_loss, o_first, o_second, o_mom1, o_mom2, o_flow, o_slow, o_bias, o_bm, o_bv,
    x1s,
):
    y = lax.axis_index("nar")
    mom1 = jnp.concatenate(
        [res[i * 256:i * 256 + 256, :] + res[ROW_G1 + i * 256:ROW_G1 + i * 256 + 256, :] for i in range(2)], axis=1
    )
    x1s[...] = mom1
    block64 = pl.ds(pl.multiple_of(y * 64, 64), 64)
    o_mom1[...] = x1s[block64, :]
    x1 = mom1 * (1.0 / (jnp.sqrt(jnp.sum(mom1 * mom1, keepdims=True)) + 1e-07))
    for _ in range(NS_ITERS):
        x1 = ns_step(x1)
    x1s[...] = x1
    first_new = w1own[...] * (1.0 - WDECAY) - x1s[block64, :]
    o_first[...] = first_new
    o_flow[...] = first_new.astype(BF)
    second = w2own[...] * (1.0 - WDECAY) - (2 * HID / CLS) ** 0.5 * res[ROW_X2:ROW_X2 + CLS, :]
    o_second[...] = second
    o_slow[...] = second.astype(BF)
    o_mom2[...] = res[ROW_M2:ROW_M2 + CLS, :]

    gb = res[512:516, :] + res[516:520, :]
    gb = jnp.concatenate([gb[0:1, :], gb[1:2, :], gb[2:3, :], gb[3:4, 0:44]], axis=1)
    m_new = BETA_ONE * biasm[...] + (1.0 - BETA_ONE) * gb
    v_new = BETA_TWO * biasv[...] + (1.0 - BETA_TWO) * gb * gb
    m_hat = m_new / (1.0 - BETA_ONE**STEP)
    v_hat = v_new / (1.0 - BETA_TWO**STEP)
    o_bias[...] = bias[...] * (1.0 - LR_BIAS * WDECAY) - LR_BIAS * m_hat / (jnp.sqrt(v_hat) + EPSILON)
    o_bm[...] = m_new
    o_bv[...] = v_new
    o_loss[...] = res[520:521, 0:1] + res[521:522, 0:1]


def update(*args):
    vm = pl.BlockSpec(memory_space=pltpu.VMEM)
    sds = jax.ShapeDtypeStruct
    return pl.pallas_call(
        update_kernel,
        out_shape=[
            sds((1, 1), F32), sds((64, HID), F32), sds((CLS, 128), F32), sds((64, HID), F32), sds((CLS, 128), F32),
            sds((64, HID), BF), sds((CLS, 128), BF), sds((1, 428), F32), sds((1, 428), F32), sds((1, 428), F32),
        ],
        in_specs=[vm] * 6,
        out_specs=[vm] * 10,
        scratch_shapes=[pltpu.VMEM((2 * D_IN, HID), F32)],
        compiler_params=pltpu.CompilerParams(vmem_limit_bytes=32 * 2**20),
    )(*args)


def per_device(
    features, requests, index_one, mask_one, index_two, mask_two, labels, seed_live,
    w_first, w_second, mom_first, mom_second, biases, bias_m, bias_v,
):
    w2own, bias = w_second.T, biases[None, :]
    res = main(
        requests.T, features, index_one.T, mask_one.T, index_two.T, mask_two.T, labels[None, :], seed_live[None, :],
        w_first, w2own, mom_first, mom_second.T, bias,
    )
    loss, first_new, second_new, mom_one, mom_two, first_low, second_low, bias_new, m_new, v_new = update(
        res, w_first, w2own, bias, bias_m[None, :], bias_v[None, :]
    )
    return (
        loss.reshape(()), first_new, second_new.T, mom_one, mom_two.T, first_low, second_low.T,
        bias_new.reshape(-1), m_new.reshape(-1), v_new.reshape(-1),
    )


def solution(mesh):
    both = ("grp", "nar")
    placed = (
        P(both, None), P(both, None), P(both, None), P(both, None), P(both, None), P(both, None),
        P(both), P(both), P("nar", None), P("nar", None), P("nar", None), P("nar", None), P(), P(), P(),
    )
    nar = P("nar", None)
    return jax.shard_map(
        per_device, mesh=mesh, in_specs=placed,
        out_specs=(P(), nar, nar, nar, nar, nar, nar, P(), P(), P()), check_vma=False,
    )
```

```python
import functools

import jax
import jax.numpy as jnp
from jax import lax
from jax.experimental import pallas as pl
from jax.experimental.pallas import tpu as pltpu
from jax.sharding import PartitionSpec as P

HID = 256
CLS = 172
CLS_PAD = 176
D_IN = 128
F1 = 15
F2 = 10
NS_ITERS = 5
STEP = 10
LAM = 0.5
MU = 0.95
WDECAY = 0.01
LR_BIAS = 0.05
BETA_ONE = 0.9
BETA_TWO = 0.999
EPSILON = 1e-08
NS_A = 3.4445
NS_B = -4.775
NS_C = 2.0315
HIGH = lax.Precision.HIGHEST
MESH = pl.DeviceIdType.MESH
BF = jnp.bfloat16
F32 = jnp.float32

DEV = 128
NAR = 4
OWN = 8192
CAP = 64
SRC = 8192
FRONT = 2048
SEED = 512


def all_to(t):
    return (t // NAR, t % NAR)


P1 = 33
P2 = 44
GRP = 32
ROW_G1 = P1 * 16
ROW_M2 = ROW_G1 + 512
ROW_X2 = ROW_M2 + CLS_PAD
ROWS = ROW_X2 + CLS_PAD
SEEDS_ALL = SEED * DEV


def dot(a, b, dims=((1,), (0,))):
    return lax.dot_general(a, b, (dims, ((), ())), preferred_element_type=F32)


NN = ((1,), (0,))
NT = ((1,), (1,))
TN = ((0,), (0,))


def split(a):
    hi = a.astype(BF)
    return hi, (a - hi.astype(F32)).astype(BF)


def dot3(a, b, dims):
    (ah, al), (bh, bl) = a, b
    return dot(ah, bh, dims) + (dot(ah, bl, dims) + dot(al, bh, dims))


def ns_step(x):
    xs = split(x)
    gram = dot3(xs, xs, NT)
    gs = split(gram)
    mix = NS_B * gram + NS_C * dot3(gs, gs, NN)
    return NS_A * x + dot3(split(mix), xs, NN)


def spread(row):
    return jnp.broadcast_to(row, (128, 128)).T


def main_kernel(
    reqt, feat, idx1t, msk1t, idx2t, msk2t, labels, live, w1, w2own, m1, m2own, bias,
    o_all,
    table, featb, pulled, stage, reqv, reqin, idxv, invv, near, own, z1, a1t, gbuf, fsel, bsel, wants, idc, invc, livec, rbuf, dbuf,
    gw1, gw2t, gm1, gm2t, gidx2, w2t, b2c, pay1, pay2, misc, inbox1, inbox2, ybox1, ybox2, res2, x2s,
    reqs, idx, inv,
    feat_sem, loc_sem, ask_sem, req_send, req_recv, row_send, row_recv, nar_send, nar_recv,
    h_send, h_recv, r_send, r_recv, d_send, d_recv, rs_send, rs_recv, y_send, y_recv, ag_send, ag_recv,
):
    a1, dh1 = pulled, table
    g = lax.axis_index("grp")
    y = lax.axis_index("nar")
    me = g * NAR + y
    left, right, opp = (y + 3) % NAR, (y + 1) % NAR, (y + 2) % NAR

    load = pltpu.make_async_copy(feat, featb, feat_sem)
    load.start()

    barrier = pltpu.get_barrier_semaphore()

    ys = [(y + d) % NAR for d in range(NAR)]

    def greet(i, c):
        t = (g + i) % GRP
        for d in range(NAR):
            pl.semaphore_signal(barrier, inc=1, device_id=(t, ys[d]), device_id_type=MESH)
        return c

    for d in range(1, NAR):
        pl.semaphore_signal(barrier, inc=1, device_id=(g, ys[d]), device_id_type=MESH)
    lax.fori_loop(1, GRP, greet, 0)

    def link(src, dst, ssem, rsem, to):
        return pltpu.make_async_remote_copy(
            src_ref=src, dst_ref=dst, send_sem=ssem, recv_sem=rsem, device_id=(g, to), device_id_type=MESH
        )

    reqv[...] = jnp.concatenate([reqt[...], jnp.zeros((DEV - CAP, DEV), jnp.int32)], axis=0).T
    ask_rows = reqv.reshape(DEV, 1, 128)
    got_rows = reqin.reshape(DEV, 1, 128)

    gw1[y] = w1[...].astype(BF)
    pad = CLS_PAD - CLS
    gw2t[y] = jnp.concatenate([w2own[...], jnp.zeros((pad, 128), F32)], axis=0).astype(BF)
    gm1[y] = m1[...]
    gm2t[y] = jnp.concatenate([m2own[...], jnp.zeros((pad, 128), F32)], axis=0)
    gidx2[y] = jnp.concatenate(
        [idx2t[0:1, :], jnp.where(msk2t[...] > 0, idx2t[1:, :], -1), jnp.zeros((5, SEED), jnp.int32)], axis=0
    )
    shared = (gidx2, gw1, gw2t, gm1, gm2t)

    pl.semaphore_wait(barrier, DEV - 1)

    def ask_one(t, u, n):
        row = t * NAR + u
        pltpu.make_async_remote_copy(
            src_ref=ask_rows.at[row], dst_ref=got_rows.at[me], send_sem=req_send, recv_sem=req_recv.at[n],
            device_id=(t, u), device_id_type=MESH,
        ).start()

    def ask(i, c):
        n = (i * 13) % GRP
        t = (g + n) % GRP
        for d in range(NAR):
            ask_one(t, ys[d], n)
        return c

    for d in range(1, NAR):
        ask_one(g, ys[d], 0)
    lax.fori_loop(1, GRP, ask, 0)
    reqin[pl.ds(me, 1), :] = reqv[pl.ds(me, 1), :]
    for n, a in enumerate(shared):
        for d in range(1, NAR):
            link(a.at[y], a.at[y], nar_send.at[n, d - 1], nar_recv.at[n, d - 1], (y + d) % NAR).start()

    msk = msk1t[...]
    idxv[0:1, :] = idx1t[0:1, :]
    idxv[1:16, :] = jnp.where(msk > 0, idx1t[1:16, :], SRC)
    invv[...] = 1.0 / jnp.maximum(jnp.sum(msk.astype(F32), axis=0, keepdims=True), 1.0)
    to_smem = [pltpu.make_async_copy(idxv, idx, loc_sem.at[0]), pltpu.make_async_copy(invv, inv, loc_sem.at[1])]
    for c in to_smem:
        c.start()

    load.wait()

    def widen_features(i, c):
        rows = pl.ds(pl.multiple_of(i * 256, 256), 256)
        table[rows, :] = featb[rows, :].astype(F32)
        return c

    lax.fori_loop(0, OWN // 256, widen_features, 0)

    view = table.reshape(SRC + 8, 1, D_IN)
    my_rows = pl.ds(pl.multiple_of(me * CAP, CAP), CAP)

    def pick(t, u, slot):
        for r in range(CAP):
            stage[r:r + 1, :] = view[reqs[t * NAR + u, 0, r]]
        featb[slot, :] = stage[...].astype(BF)

    def serve_one(t, u, slot):
        pick(t, u, slot)
        pltpu.make_async_remote_copy(
            src_ref=featb.at[slot], dst_ref=pulled.at[my_rows],
            send_sem=row_send, recv_sem=row_recv, device_id=(t, u), device_id_type=MESH,
        ).start()

    def asked(count, n):
        rows = got_rows.at[pl.ds(0, count)]
        pltpu.make_async_copy(rows, rows, req_recv.at[n]).wait()

    def to_scalars(t, n):
        rows = pl.ds(pl.multiple_of(t * NAR, NAR), NAR)
        return pltpu.make_async_copy(got_rows.at[rows], reqs.at[rows], ask_sem.at[n])

    def whose(i):
        n = (i * 13) % GRP
        return n, (g + GRP - n) % GRP

    def fetch(i):
        n, t = whose(i)
        asked(NAR, n)
        to_scalars(t, n).start()

    def serve(i, c):
        n, t = whose(i)

        @pl.when(i < GRP - 1)
        def _():
            fetch(i + 1)

        to_scalars(t, n).wait()
        for d in range(NAR):
            serve_one(t, ys[d], pl.ds(pl.multiple_of((i * NAR + d) * CAP, CAP), CAP))
        return c

    fetch(1)
    lax.fori_loop(1, GRP, serve, 0)
    asked(NAR - 1, 0)
    to_scalars(g, 0).start()
    to_scalars(g, 0).wait()
    for d in range(1, NAR):
        serve_one(g, ys[d], pl.ds(d * CAP, CAP))
    pick(g, y, pl.ds(0, CAP))
    pulled[my_rows, :] = featb[0:CAP, :]

    for n, a in enumerate(shared):
        for d in range(1, NAR):
            link(a.at[y], a.at[y], nar_send.at[n, d - 1], nar_recv.at[n, d - 1], (y + d) % NAR).wait()
    for q in range(NAR):
        o_all[ROW_G1 + q * 64:ROW_G1 + q * 64 + 64, :] = MU * gm1[q, :, 0:128]
        o_all[ROW_G1 + 256 + q * 64:ROW_G1 + 256 + q * 64 + 64, :] = MU * gm1[q, :, 128:256]
    for q in range(NAR):
        w2t[:, q * 128:(q + 1) * 128] = gw2t[q]
    last = jnp.concatenate([bias[0:1, 384:428], jnp.zeros((1, 84), F32)], axis=1)
    b2c[...] = jnp.concatenate([spread(bias[0:1, 256:384]), spread(last)], axis=0)

    def column(row):
        return jnp.concatenate([spread(row[:, c * 128:(c + 1) * 128]) for c in range(SEED // 128)], axis=0)

    for q in range(NAR):
        n = jnp.sum((gidx2[q, 1:1 + F2, :] >= 0).astype(F32), axis=0, keepdims=True)
        invc[q] = column(1.0 / jnp.maximum(n, 1.0))
    livec[...] = column(2.0 * LAM / HID / SEEDS_ALL * live[...].astype(F32))

    lane16 = lax.broadcasted_iota(jnp.int32, (16, 128), 1).astype(jnp.int16)
    iota16 = lax.broadcasted_iota(jnp.int32, (16, 128), 0).astype(jnp.int16)
    one, zero = jnp.ones((16, 128), BF), jnp.zeros((16, 128), BF)

    def marks(here, want):
        acc = jnp.where(here == want[1], one, zero)
        for k in range(2, 1 + F2):
            acc = acc + jnp.where(here == want[k], one, zero)
        return acc, jnp.where(here == want[0], one, zero)

    idc[...] = gidx2[y].T

    def forward_marks(i, carry):
        at = pl.multiple_of(i * 16, 16)
        blk = idc[pl.ds(at, 16), :]
        want = [jnp.broadcast_to(blk[:, k:k + 1], (16, 128)).astype(jnp.int16) for k in range(1 + F2)]
        for q in range(NAR):
            for c in range(FRONT // 128):
                here = lane16 + jnp.full((16, 128), q * FRONT + c * 128, jnp.int32).astype(jnp.int16)
                a, b = marks(here, want)
                fsel[q, pl.ds(at, 16), c * 128:(c + 1) * 128] = a
                fsel[q, pl.ds(SEED + at, 16), c * 128:(c + 1) * 128] = b
        return carry

    lax.fori_loop(0, SEED // 16, forward_marks, 0)

    for q in range(NAR):
        ids = gidx2[q] - y * FRONT
        for c in range(SEED // 128):
            for k in range(1 + F2):
                row = ids[k:k + 1, c * 128:(c + 1) * 128]
                wants[q, c, k] = jnp.broadcast_to(row, (16, 128)).astype(jnp.int16)

    def backward_marks(i):
        here = iota16 + jnp.full((16, 128), i * 16, jnp.int32).astype(jnp.int16)
        out = pl.ds(pl.multiple_of(i * 16, 16), 16)
        for q in range(NAR):
            for c in range(SEED // 128):
                a, b = marks(here, [wants[q, c, k] for k in range(1 + F2)])
                bsel[q, out, c * 128:(c + 1) * 128] = a
                bsel[q, out, SEED + c * 128:SEED + (c + 1) * 128] = b

    come = pulled.at[pl.ds(0, (DEV - 1) * CAP)]
    pltpu.make_async_copy(come, come, row_recv).wait()
    gone = featb.at[pl.ds(CAP, (DEV - 1) * CAP)]
    pltpu.make_async_copy(gone, gone, row_send).wait()
    sent = ask_rows.at[pl.ds(0, DEV - 1)]
    pltpu.make_async_copy(sent, sent, req_send).wait()

    def widen(i, c):
        rows = pl.ds(pl.multiple_of(i * 256, 256), 256)
        table[rows, :] = pulled[rows, :].astype(F32)
        return c

    lax.fori_loop(0, SRC // 256, widen, 0)
    table[SRC:SRC + 8, :] = jnp.zeros((8, D_IN), F32)
    for c in to_smem:
        c.wait()

    def cols(b):
        return pl.ds(pl.multiple_of(b * 256, 256), 256)

    def forward(b):
        @pl.when(b % 2 == 0)
        def _():
            blk = gbuf.at[left, cols(b), :]
            link(blk, blk, h_send.at[0, b], h_recv.at[0, b], right).wait_recv()
            link(blk, blk, h_send.at[2, b], h_recv.at[2, b], right).start()

        @pl.when(b % 2 == 1)
        def _():
            blk = gbuf.at[right, cols(b), :]
            link(blk, blk, h_send.at[1, b], h_recv.at[1, b], left).wait_recv()
            link(blk, blk, h_send.at[2, b], h_recv.at[2, b], left).start()

    def block(b, c):
        def some(i, c2):
            backward_marks(b * 16 + i)
            base = pl.multiple_of(b * 256 + i * 16, 16)
            for j in range(16):
                m = base + j
                here = pl.ds(pl.multiple_of(i * 16, 16) + j, 1)
                own[here, :] = view[idx[0, m]]
                rows = [view[idx[1 + k, m]] for k in range(F1)]
                while len(rows) > 1:
                    rows = [p + q for p, q in zip(rows[::2], rows[1::2])] + ([rows[-1]] if len(rows) % 2 else [])
                near[here, :] = rows[0] * inv[0, m]
            return c2

        lax.fori_loop(0, 16, some, 0)
        rows = cols(b)
        act = jnp.concatenate([own[...].astype(BF), near[...].astype(BF)], axis=1)
        a1[rows, :] = act[:, :128]
        a1[pl.ds(pl.multiple_of(FRONT + b * 256, 256), 256), :] = act[:, 128:]
        z = dot(act, gw1[...].reshape(2 * D_IN, HID)) + bias[0:1, 0:HID]
        z1[rows, :] = z
        gbuf[y, rows, :] = (z / (1.0 + jnp.exp(-z))).astype(BF)
        blk = gbuf.at[y, rows, :]
        link(blk, blk, h_send.at[0, b], h_recv.at[0, b], right).start()
        link(blk, blk, h_send.at[1, b], h_recv.at[1, b], left).start()

        @pl.when(b > 0)
        def _():
            forward(b - 1)

        return c

    lax.fori_loop(0, 8, block, 0)
    forward(7)

    def from_source(q):
        return dot(fsel[q], gbuf[q])

    total = from_source(y)
    for b in range(1, 8, 2):
        blk = gbuf.at[left, b * 256:(b + 1) * 256, :]
        link(blk, blk, h_send.at[0, b], h_recv.at[0, b], right).wait_recv()
    total = total + from_source(left)
    for b in range(0, 8, 2):
        blk = gbuf.at[right, b * 256:(b + 1) * 256, :]
        link(blk, blk, h_send.at[1, b], h_recv.at[1, b], left).wait_recv()
    total = total + from_source(right)
    for b in range(8):
        blk = gbuf.at[opp, b * 256:(b + 1) * 256, :]
        link(blk, blk, h_send.at[2, b], h_recv.at[2, b], right).wait_recv()
    total = total + from_source(opp)

    def wide(a):
        return jnp.concatenate([a, a], axis=1)

    near2 = (total[:SEED, :] * wide(invc[y])).astype(BF)
    self2 = total[SEED:, :].astype(BF)
    alive = live[...].astype(F32)
    diff = self2.astype(F32) - near2.astype(F32)
    pull_apart = wide(livec[...]) * diff

    def swap_start(buf, ssem, rsem):
        blk = buf.at[y]
        link(blk, blk, ssem.at[0], rsem.at[0], right).start()
        link(blk, blk, ssem.at[1], rsem.at[1], left).start()

    def swap_forward(buf, ssem, rsem, cut):
        blk = buf.at[left]
        link(blk, blk, ssem.at[0], rsem.at[0], right).wait_recv()
        half = buf.at[left, 0:cut, :]
        link(half, half, ssem.at[2], rsem.at[2], right).start()
        blk = buf.at[right]
        link(blk, blk, ssem.at[1], rsem.at[1], left).wait_recv()
        half = buf.at[right, cut:, :]
        link(half, half, ssem.at[3], rsem.at[3], left).start()

    def swap_end(buf, ssem, rsem, cut):
        half = buf.at[opp, 0:cut, :]
        link(half, half, ssem.at[2], rsem.at[2], right).wait_recv()
        half = buf.at[opp, cut:, :]
        link(half, half, ssem.at[3], rsem.at[3], left).wait_recv()

    def swap_sent(buf, ssem, rsem, cut):
        blk = buf.at[y]
        link(blk, blk, ssem.at[0], rsem.at[0], right).wait_send()
        link(blk, blk, ssem.at[1], rsem.at[1], left).wait_send()
        half = buf.at[left, 0:cut, :]
        link(half, half, ssem.at[2], rsem.at[2], right).wait_send()
        half = buf.at[right, cut:, :]
        link(half, half, ssem.at[3], rsem.at[3], left).wait_send()

    rbuf[y] = pull_apart.astype(BF)
    swap_start(rbuf, r_send, r_recv)

    act2 = jnp.concatenate([self2, near2], axis=1)
    cls = lax.broadcasted_iota(jnp.int32, (CLS_PAD, SEED), 0)
    b2 = b2c[0:CLS_PAD, :]
    logits = dot(w2t[...], act2, NT) + jnp.concatenate([b2] * 4, axis=1)
    logits = jnp.where(cls < CLS, logits, -1e30)
    top = jnp.max(logits, axis=0, keepdims=True)
    e = jnp.exp(logits - top)
    tot = jnp.sum(e, axis=0, keepdims=True)
    hot = cls == labels[...]
    picked = jnp.sum(jnp.where(hot, logits, 0.0), axis=0, keepdims=True)
    dlog = (alive * (e * (1.0 / tot) - jnp.where(hot, 1.0, 0.0)) * (1.0 / SEEDS_ALL)).astype(BF)
    dbuf[y] = dlog
    swap_start(dbuf, d_send, d_recv)

    loss = jnp.sum(alive * (top + jnp.log(tot) - picked), axis=1, keepdims=True)
    loss = loss + SEEDS_ALL / 2 * jnp.sum(pull_apart * diff, keepdims=True)
    g2t = dot(dlog, act2).astype(BF)
    for q in range(NAR):
        pay2[q * CLS_PAD:(q + 1) * CLS_PAD, :] = g2t[:, q * 128:(q + 1) * 128]

    def plane(i):
        return ((g + i) % GRP, y)

    def to_owner(pay, inbox, count, n):
        def body(i, c):
            t = (g + i) % GRP
            for slot in range(2):
                p = t + slot * GRP

                @pl.when(p < count)
                def _():
                    pltpu.make_async_remote_copy(
                        src_ref=pay.at[pl.ds(pl.multiple_of(p * 16, 16), 16)], dst_ref=inbox.at[slot, g],
                        send_sem=rs_send.at[n], recv_sem=rs_recv.at[n, slot], device_id=(t, y), device_id_type=MESH,
                    ).start()

            return c

        lax.fori_loop(1, GRP, body, 0)

    def add_plane(pay, inbox, ybox, count, n):
        for slot in range(2):
            p = g + slot * GRP

            @pl.when(p < count)
            def _():
                got = inbox.at[slot, pl.ds(0, GRP - 1)]
                pltpu.make_async_copy(got, got, rs_recv.at[n, slot]).wait()
                inbox[slot, g] = pay[pl.ds(pl.multiple_of(p * 16, 16), 16), :]
                ybox[slot, y] = jnp.sum(inbox[slot].astype(F32), axis=0)
                blk = ybox.at[slot, y]
                for d in range(1, NAR):
                    link(blk, blk, y_send.at[n, slot, d - 1], y_recv.at[n, slot, d - 1], (y + d) % NAR).start()

    def add_group(ybox, res, count, n):
        for slot in range(2):
            p = g + slot * GRP

            @pl.when(p < count)
            def _():
                blk = ybox.at[slot, y]
                for d in range(1, NAR):
                    link(blk, blk, y_send.at[n, slot, d - 1], y_recv.at[n, slot, d - 1], (y + d) % NAR).wait()
                rows16 = pl.ds(pl.multiple_of(p * 16, 16), 16)
                res[rows16, :] = (ybox[slot, 0] + ybox[slot, 1]) + (ybox[slot, 2] + ybox[slot, 3])

                def tell(i, c):
                    pltpu.make_async_remote_copy(
                        src_ref=res.at[rows16], dst_ref=res.at[rows16], send_sem=ag_send.at[n], recv_sem=ag_recv.at[n],
                        device_id=plane(i), device_id_type=MESH,
                    ).start()
                    return c

                lax.fori_loop(1, GRP, tell, 0)

    def take(res, count, n):
        two_here = g + GRP < count
        for own, here in ((2, two_here), (1, jnp.logical_not(two_here))):
            @pl.when(here)
            def _(own=own):
                got = res.at[pl.ds(0, (count - own) * 16)]
                pltpu.make_async_copy(got, got, ag_recv.at[n]).wait()

    def sums_sent(pay, count, n):
        two_here = g + GRP < count
        for own, here in ((2, two_here), (1, jnp.logical_not(two_here))):
            @pl.when(here)
            def _(own=own):
                gone = pay.at[pl.ds(0, (count - own) * 16)]
                pltpu.make_async_copy(gone, gone, rs_send.at[n]).wait()
                gone = table.at[pl.ds(0, own * (GRP - 1) * 16)]
                pltpu.make_async_copy(gone, gone, ag_send.at[n]).wait()

    to_owner(pay2, inbox2, P2, 1)

    def add_grads(q, fresh=False):
        da = dot(dbuf[q], w2t[...], TN)
        r = rbuf[q].astype(F32)
        ds = (da[:, :HID] + r).astype(BF)
        dn = ((da[:, HID:] - r) * wide(invc[q])).astype(BF)
        both = jnp.concatenate([dn, ds], axis=0)

        def rows512(i, c):
            part = dot(bsel[q, pl.ds(pl.multiple_of(i * 512, 512), 512), :], both)
            for h in range(2):
                rows = pl.ds(pl.multiple_of(h * FRONT + i * 512, 512), 512)
                now = part[:, h * 128:(h + 1) * 128]
                dh1[rows, :] = now if fresh else dh1[rows, :] + now
            return c

        lax.fori_loop(0, FRONT // 512, rows512, 0)

    for c in range(2):
        a1t[c * 128:(c + 1) * 128, :] = a1[c * FRONT:(c + 1) * FRONT, :].T
    db2 = jnp.sum(dlog.astype(F32), axis=1, keepdims=True)
    db2 = jnp.broadcast_to(db2, (CLS_PAD, 128)).T[0:1, :]
    swap_forward(rbuf, r_send, r_recv, SEED // 2)
    add_grads(y, True)
    swap_forward(dbuf, d_send, d_recv, 96)
    add_grads(left)
    add_grads(right)
    add_plane(pay2, inbox2, ybox2, P2, 1)
    swap_end(rbuf, r_send, r_recv, SEED // 2)
    swap_end(dbuf, d_send, d_recv, 96)
    add_group(ybox2, res2, P2, 1)
    add_grads(opp)

    def to_z(i, db):
        z = z1[pl.ds(pl.multiple_of(i * 128, 128), 128), :]
        sig = 1.0 / (1.0 + jnp.exp(-z))
        dh = jnp.concatenate(
            [dh1[pl.ds(pl.multiple_of(h * FRONT + i * 128, 128), 128), :] for h in range(2)], axis=1
        )
        dz = dh * sig * (1.0 + z * (1.0 - sig))
        low = dz.astype(BF)
        for h in range(2):
            a1[pl.ds(pl.multiple_of((2 + h) * FRONT + i * 128, 128), 128), :] = low[:, h * 128:(h + 1) * 128]
        return db + jnp.sum(low.astype(F32), axis=0, keepdims=True)

    db1 = lax.fori_loop(0, FRONT // 128, to_z, jnp.zeros((1, HID), F32))
    dz = jnp.concatenate([a1[2 * FRONT:3 * FRONT, :], a1[3 * FRONT:4 * FRONT, :]], axis=1)
    g1 = dot(a1t[...], dz).astype(BF)
    pay1[0:256, :] = g1[:, :128]
    pay1[256:512, :] = g1[:, 128:]
    misc[...] = jnp.zeros((16, 128), F32)

    def two(rows, v):
        hi = v.astype(BF).astype(F32)
        misc[rows:rows + 1, 0:v.shape[1]] = hi
        misc[rows + 4:rows + 5, 0:v.shape[1]] = v - hi

    two(0, db1[:, :128])
    two(1, db1[:, 128:])
    two(2, db2[:, :128])
    two(3, db2[:, 128:])
    hi = loss.astype(BF).astype(F32)
    misc[8:9, 0:1] = hi
    misc[9:10, 0:1] = loss - hi
    pay1[512:528, :] = misc[...].astype(BF)
    to_owner(pay1, inbox1, P1, 0)

    take(res2, P2, 1)
    mom2 = jnp.concatenate(
        [MU * gm2t[q] + res2[q * CLS_PAD:(q + 1) * CLS_PAD, :] for q in range(NAR)], axis=1
    )
    for q in range(NAR):
        x2s[q] = mom2[:, q * 128:(q + 1) * 128]
    o_all[ROW_M2:ROW_M2 + CLS_PAD, :] = x2s[y]
    x2 = mom2 * (1.0 / (jnp.sqrt(jnp.sum(mom2 * mom2, keepdims=True)) + 1e-07))
    x2 = ns_step(x2)
    add_plane(pay1, inbox1, ybox1, P1, 0)
    x2 = ns_step(x2)
    add_group(ybox1, o_all, P1, 0)
    for _ in range(NS_ITERS - 2):
        x2 = ns_step(x2)
    for q in range(NAR):
        x2s[q] = x2[:, q * 128:(q + 1) * 128]
    o_all[ROW_X2:ROW_X2 + CLS_PAD, :] = x2s[y]
    take(o_all, P1, 0)

    for b in range(8):
        blk = gbuf.at[y, b * 256:(b + 1) * 256, :]
        link(blk, blk, h_send.at[0, b], h_recv.at[0, b], right).wait_send()
        link(blk, blk, h_send.at[1, b], h_recv.at[1, b], left).wait_send()
        blk = gbuf.at[opp, b * 256:(b + 1) * 256, :]
        link(blk, blk, h_send.at[2, b], h_recv.at[2, b], right).wait_send()
    swap_sent(rbuf, r_send, r_recv, SEED // 2)
    swap_sent(dbuf, d_send, d_recv, 96)

    sums_sent(pay2, P2, 1)
    sums_sent(pay1, P1, 0)


def main(reqt, feat, idx1t, msk1t, idx2t, msk2t, labels, live, w1, w2own, m1, m2own, bias):
    vm = pl.BlockSpec(memory_space=pltpu.VMEM)
    dma = pltpu.SemaphoreType.DMA
    sds = jax.ShapeDtypeStruct
    V = pltpu.VMEM
    return pl.pallas_call(
        main_kernel,
        out_shape=sds((ROWS, 128), F32),
        in_specs=[vm, pl.BlockSpec(memory_space=pl.ANY)] + [vm] * 11,
        out_specs=vm,
        scratch_shapes=[
            V((SRC + 8, D_IN), F32),
            V((OWN, D_IN), BF),
            V((SRC, D_IN), BF),
            V((CAP, D_IN), F32),
            V((DEV, 128), jnp.int32),
            V((DEV, 128), jnp.int32),
            V((16, FRONT), jnp.int32),
            V((1, FRONT), F32),
            V((256, D_IN), F32),
            V((256, D_IN), F32),
            V((FRONT, HID), F32),
            V((2 * D_IN, FRONT), BF),
            V((NAR, FRONT, HID), BF),
            V((NAR, 2 * SEED, FRONT), BF),
            V((NAR, FRONT, 2 * SEED), BF),
            V((NAR, 4, 1 + F2, 16, 128), jnp.int16),
            V((SEED, 16), jnp.int32),
            V((NAR, SEED, 128), F32),
            V((SEED, 128), F32),
            V((NAR, SEED, HID), BF),
            V((NAR, CLS_PAD, SEED), BF),
            V((NAR, 64, HID), BF),
            V((NAR, CLS_PAD, 128), BF),
            V((NAR, 64, HID), F32),
            V((NAR, CLS_PAD, 128), F32),
            V((NAR, 16, SEED), jnp.int32),
            V((CLS_PAD, 2 * HID), BF),
            V((HID, 128), F32),
            V((P1 * 16, 128), BF),
            V((P2 * 16, 128), BF),
            V((16, 128), F32),
            V((2, GRP, 16, 128), BF),
            V((2, GRP, 16, 128), BF),
            V((2, NAR, 16, 128), F32),
            V((2, NAR, 16, 128), F32),
            V((P2 * 16, 128), F32),
            V((NAR, CLS_PAD, 128), F32),
            pltpu.SMEM((DEV, 1, 128), jnp.int32),
            pltpu.SMEM((16, FRONT), jnp.int32),
            pltpu.SMEM((1, FRONT), F32),
            dma, dma((2,)), dma((GRP,)), dma, dma((GRP,)), dma, dma, dma((5, 3)), dma((5, 3)),
            dma((3, 8)), dma((3, 8)), dma((4,)), dma((4,)), dma((4,)), dma((4,)),
            dma((2,)), dma((2, 2)), dma((2, 2, 3)), dma((2, 2, 3)), dma((2,)), dma((2,)),
        ],
        compiler_params=pltpu.CompilerParams(
            collective_id=0, has_side_effects=True, vmem_limit_bytes=62 * 2**20
        ),
    )(reqt, feat, idx1t, msk1t, idx2t, msk2t, labels, live, w1, w2own, m1, m2own, bias)


def update_kernel(
    res, w1own, w2own, bias, biasm, biasv,
    o_loss, o_first, o_second, o_mom1, o_mom2, o_flow, o_slow, o_bias, o_bm, o_bv,
    x1s,
):
    y = lax.axis_index("nar")
    mom1 = jnp.concatenate(
        [res[i * 256:i * 256 + 256, :] + res[ROW_G1 + i * 256:ROW_G1 + i * 256 + 256, :] for i in range(2)], axis=1
    )
    x1s[...] = mom1
    block64 = pl.ds(pl.multiple_of(y * 64, 64), 64)
    o_mom1[...] = x1s[block64, :]
    x1 = mom1 * (1.0 / (jnp.sqrt(jnp.sum(mom1 * mom1, keepdims=True)) + 1e-07))
    for _ in range(NS_ITERS):
        x1 = ns_step(x1)
    x1s[...] = x1
    first_new = w1own[...] * (1.0 - WDECAY) - x1s[block64, :]
    o_first[...] = first_new
    o_flow[...] = first_new.astype(BF)
    second = w2own[...] * (1.0 - WDECAY) - (2 * HID / CLS) ** 0.5 * res[ROW_X2:ROW_X2 + CLS, :]
    o_second[...] = second
    o_slow[...] = second.astype(BF)
    o_mom2[...] = res[ROW_M2:ROW_M2 + CLS, :]

    gb = res[512:516, :] + res[516:520, :]
    gb = jnp.concatenate([gb[0:1, :], gb[1:2, :], gb[2:3, :], gb[3:4, 0:44]], axis=1)
    m_new = BETA_ONE * biasm[...] + (1.0 - BETA_ONE) * gb
    v_new = BETA_TWO * biasv[...] + (1.0 - BETA_TWO) * gb * gb
    m_hat = m_new / (1.0 - BETA_ONE**STEP)
    v_hat = v_new / (1.0 - BETA_TWO**STEP)
    o_bias[...] = bias[...] * (1.0 - LR_BIAS * WDECAY) - LR_BIAS * m_hat / (jnp.sqrt(v_hat) + EPSILON)
    o_bm[...] = m_new
    o_bv[...] = v_new
    o_loss[...] = res[520:521, 0:1] + res[521:522, 0:1]


def update(*args):
    vm = pl.BlockSpec(memory_space=pltpu.VMEM)
    sds = jax.ShapeDtypeStruct
    return pl.pallas_call(
        update_kernel,
        out_shape=[
            sds((1, 1), F32), sds((64, HID), F32), sds((CLS, 128), F32), sds((64, HID), F32), sds((CLS, 128), F32),
            sds((64, HID), BF), sds((CLS, 128), BF), sds((1, 428), F32), sds((1, 428), F32), sds((1, 428), F32),
        ],
        in_specs=[vm] * 6,
        out_specs=[vm] * 10,
        scratch_shapes=[pltpu.VMEM((2 * D_IN, HID), F32)],
        compiler_params=pltpu.CompilerParams(vmem_limit_bytes=32 * 2**20),
    )(*args)


def per_device(
    features, requests, index_one, mask_one, index_two, mask_two, labels, seed_live,
    w_first, w_second, mom_first, mom_second, biases, bias_m, bias_v,
):
    w2own, bias = w_second.T, biases[None, :]
    res = main(
        requests.T, features, index_one.T, mask_one.T, index_two.T, mask_two.T, labels[None, :], seed_live[None, :],
        w_first, w2own, mom_first, mom_second.T, bias,
    )
    loss, first_new, second_new, mom_one, mom_two, first_low, second_low, bias_new, m_new, v_new = update(
        res, w_first, w2own, bias, bias_m[None, :], bias_v[None, :]
    )
    return (
        loss.reshape(()), first_new, second_new.T, mom_one, mom_two.T, first_low, second_low.T,
        bias_new.reshape(-1), m_new.reshape(-1), v_new.reshape(-1),
    )


def solution(mesh):
    both = ("grp", "nar")
    placed = (
        P(both, None), P(both, None), P(both, None), P(both, None), P(both, None), P(both, None),
        P(both), P(both), P("nar", None), P("nar", None), P("nar", None), P("nar", None), P(), P(), P(),
    )
    nar = P("nar", None)
    return jax.shard_map(
        per_device, mesh=mesh, in_specs=placed,
        out_specs=(P(), nar, nar, nar, nar, nar, nar, P(), P(), P()), check_vma=False,
    )
```

```python
import functools

import jax
import jax.numpy as jnp
from jax import lax
from jax.experimental import pallas as pl
from jax.experimental.pallas import tpu as pltpu
from jax.sharding import PartitionSpec as P

HID = 256
CLS = 172
CLS_PAD = 176
D_IN = 128
F1 = 15
F2 = 10
NS_ITERS = 5
STEP = 10
LAM = 0.5
MU = 0.95
WDECAY = 0.01
LR_BIAS = 0.05
BETA_ONE = 0.9
BETA_TWO = 0.999
EPSILON = 1e-08
NS_A = 3.4445
NS_B = -4.775
NS_C = 2.0315
HIGH = lax.Precision.HIGHEST
MESH = pl.DeviceIdType.MESH
BF = jnp.bfloat16
F32 = jnp.float32

DEV = 128
NAR = 4
OWN = 8192
CAP = 64
SRC = 8192
FRONT = 2048
SEED = 512


def all_to(t):
    return (t // NAR, t % NAR)


P1 = 33
P2 = 44
GRP = 32
ROW_G1 = P1 * 16
ROW_M2 = ROW_G1 + 512
ROW_X2 = ROW_M2 + CLS_PAD
ROWS = ROW_X2 + CLS_PAD
SEEDS_ALL = SEED * DEV


def dot(a, b, dims=((1,), (0,))):
    return lax.dot_general(a, b, (dims, ((), ())), preferred_element_type=F32)


NN = ((1,), (0,))
NT = ((1,), (1,))
TN = ((0,), (0,))


def split(a):
    hi = a.astype(BF)
    return hi, (a - hi.astype(F32)).astype(BF)


def dot3(a, b, dims):
    (ah, al), (bh, bl) = a, b
    return dot(ah, bh, dims) + (dot(ah, bl, dims) + dot(al, bh, dims))


def ns_step(x):
    xs = split(x)
    gram = dot3(xs, xs, NT)
    gs = split(gram)
    mix = NS_B * gram + NS_C * dot3(gs, gs, NN)
    return NS_A * x + dot3(split(mix), xs, NN)


def spread(row):
    return jnp.broadcast_to(row, (128, 128)).T


def main_kernel(
    reqt, feat, idx1t, msk1t, idx2t, msk2t, labels, live, w1, w2own, m1, m2own, bias,
    o_all,
    table, featb, pulled, stage, reqv, reqin, idxv, invv, near, own, z1, a1t, gbuf, fsel, bsel, wants, idc, invc, livec, rbuf, dbuf,
    gw1, gw2t, gm1, gm2t, gidx2, w2t, b2c, pay1, pay2, misc, inbox1, inbox2, ybox1, ybox2, res2, x2s,
    reqs, idx, inv,
    feat_sem, loc_sem, ask_sem, req_send, req_recv, row_send, row_recv, nar_send, nar_recv,
    h_send, h_recv, r_send, r_recv, d_send, d_recv, rs_send, rs_recv, y_send, y_recv, ag_send, ag_recv,
):
    a1, dh1 = pulled, table
    g = lax.axis_index("grp")
    y = lax.axis_index("nar")
    me = g * NAR + y
    left, right, opp = (y + 3) % NAR, (y + 1) % NAR, (y + 2) % NAR

    load = pltpu.make_async_copy(feat, featb, feat_sem)
    load.start()

    barrier = pltpu.get_barrier_semaphore()

    ys = [(y + d) % NAR for d in range(NAR)]

    def greet(i, c):
        t = (g + i) % GRP
        for d in range(NAR):
            pl.semaphore_signal(barrier, inc=1, device_id=(t, ys[d]), device_id_type=MESH)
        return c

    for d in range(1, NAR):
        pl.semaphore_signal(barrier, inc=1, device_id=(g, ys[d]), device_id_type=MESH)
    lax.fori_loop(1, GRP, greet, 0)

    def link(src, dst, ssem, rsem, to):
        return pltpu.make_async_remote_copy(
            src_ref=src, dst_ref=dst, send_sem=ssem, recv_sem=rsem, device_id=(g, to), device_id_type=MESH
        )

    reqv[...] = jnp.concatenate([reqt[...], jnp.zeros((DEV - CAP, DEV), jnp.int32)], axis=0).T
    ask_rows = reqv.reshape(DEV, 1, 128)
    got_rows = reqin.reshape(DEV, 1, 128)

    gw1[y] = w1[...].astype(BF)
    pad = CLS_PAD - CLS
    gw2t[y] = jnp.concatenate([w2own[...], jnp.zeros((pad, 128), F32)], axis=0).astype(BF)
    gm1[y] = m1[...]
    gm2t[y] = jnp.concatenate([m2own[...], jnp.zeros((pad, 128), F32)], axis=0)
    gidx2[y] = jnp.concatenate(
        [idx2t[0:1, :], jnp.where(msk2t[...] > 0, idx2t[1:, :], -1), jnp.zeros((5, SEED), jnp.int32)], axis=0
    )
    shared = (gidx2, gw1, gw2t, gm1, gm2t)

    pl.semaphore_wait(barrier, DEV - 1)

    def ask_one(t, u, n):
        row = t * NAR + u
        pltpu.make_async_remote_copy(
            src_ref=ask_rows.at[row], dst_ref=got_rows.at[me], send_sem=req_send, recv_sem=req_recv.at[n],
            device_id=(t, u), device_id_type=MESH,
        ).start()

    def ask(i, c):
        n = (i * 13) % GRP
        t = (g + n) % GRP
        for d in range(NAR):
            ask_one(t, ys[d], n)
        return c

    for d in range(1, NAR):
        ask_one(g, ys[d], 0)
    lax.fori_loop(1, GRP, ask, 0)
    reqin[pl.ds(me, 1), :] = reqv[pl.ds(me, 1), :]
    for n, a in enumerate(shared):
        for d in range(1, NAR):
            link(a.at[y], a.at[y], nar_send.at[n, d - 1], nar_recv.at[n, d - 1], (y + d) % NAR).start()

    msk = msk1t[...]
    idxv[0:1, :] = idx1t[0:1, :]
    idxv[1:16, :] = jnp.where(msk > 0, idx1t[1:16, :], SRC)
    invv[...] = 1.0 / jnp.maximum(jnp.sum(msk.astype(F32), axis=0, keepdims=True), 1.0)
    to_smem = [pltpu.make_async_copy(idxv, idx, loc_sem.at[0]), pltpu.make_async_copy(invv, inv, loc_sem.at[1])]
    for c in to_smem:
        c.start()

    load.wait()

    def widen_features(i, c):
        rows = pl.ds(pl.multiple_of(i * 256, 256), 256)
        table[rows, :] = featb[rows, :].astype(F32)
        return c

    lax.fori_loop(0, OWN // 256, widen_features, 0)

    view = table.reshape(SRC + 8, 1, D_IN)
    my_rows = pl.ds(pl.multiple_of(me * CAP, CAP), CAP)

    stage_rows = stage.reshape(CAP, 1, D_IN)

    def pick(t, u, slot):
        for r in range(CAP):
            stage_rows[r] = view[reqs[t * NAR + u, 0, r]]
        featb[slot, :] = stage[...].astype(BF)

    def serve_one(t, u, slot):
        pick(t, u, slot)
        pltpu.make_async_remote_copy(
            src_ref=featb.at[slot], dst_ref=pulled.at[my_rows],
            send_sem=row_send, recv_sem=row_recv, device_id=(t, u), device_id_type=MESH,
        ).start()

    def asked(count, n):
        rows = got_rows.at[pl.ds(0, count)]
        pltpu.make_async_copy(rows, rows, req_recv.at[n]).wait()

    def to_scalars(t, n):
        rows = pl.ds(pl.multiple_of(t * NAR, NAR), NAR)
        return pltpu.make_async_copy(got_rows.at[rows], reqs.at[rows], ask_sem.at[n])

    def whose(i):
        n = (i * 13) % GRP
        return n, (g + GRP - n) % GRP

    def fetch(i):
        n, t = whose(i)
        asked(NAR, n)
        to_scalars(t, n).start()

    def serve(i, c):
        n, t = whose(i)

        @pl.when(i < GRP - 1)
        def _():
            fetch(i + 1)

        to_scalars(t, n).wait()
        for d in range(NAR):
            serve_one(t, ys[d], pl.ds(pl.multiple_of((i * NAR + d) * CAP, CAP), CAP))
        return c

    fetch(1)
    lax.fori_loop(1, GRP, serve, 0)
    asked(NAR - 1, 0)
    to_scalars(g, 0).start()
    to_scalars(g, 0).wait()
    for d in range(1, NAR):
        serve_one(g, ys[d], pl.ds(d * CAP, CAP))
    pick(g, y, pl.ds(0, CAP))
    pulled[my_rows, :] = featb[0:CAP, :]

    for n, a in enumerate(shared):
        for d in range(1, NAR):
            link(a.at[y], a.at[y], nar_send.at[n, d - 1], nar_recv.at[n, d - 1], (y + d) % NAR).wait()
    for q in range(NAR):
        o_all[ROW_G1 + q * 64:ROW_G1 + q * 64 + 64, :] = MU * gm1[q, :, 0:128]
        o_all[ROW_G1 + 256 + q * 64:ROW_G1 + 256 + q * 64 + 64, :] = MU * gm1[q, :, 128:256]
    for q in range(NAR):
        w2t[:, q * 128:(q + 1) * 128] = gw2t[q]
    last = jnp.concatenate([bias[0:1, 384:428], jnp.zeros((1, 84), F32)], axis=1)
    b2c[...] = jnp.concatenate([spread(bias[0:1, 256:384]), spread(last)], axis=0)

    def column(row):
        return jnp.concatenate([spread(row[:, c * 128:(c + 1) * 128]) for c in range(SEED // 128)], axis=0)

    for q in range(NAR):
        n = jnp.sum((gidx2[q, 1:1 + F2, :] >= 0).astype(F32), axis=0, keepdims=True)
        invc[q] = column(1.0 / jnp.maximum(n, 1.0))
    livec[...] = column(2.0 * LAM / HID / SEEDS_ALL * live[...].astype(F32))

    lane16 = lax.broadcasted_iota(jnp.int32, (16, 128), 1).astype(jnp.int16)
    iota16 = lax.broadcasted_iota(jnp.int32, (16, 128), 0).astype(jnp.int16)
    one, zero = jnp.ones((16, 128), BF), jnp.zeros((16, 128), BF)

    def marks(here, want):
        acc = jnp.where(here == want[1], one, zero)
        for k in range(2, 1 + F2):
            acc = acc + jnp.where(here == want[k], one, zero)
        return acc, jnp.where(here == want[0], one, zero)

    idc[...] = gidx2[y].T

    def forward_marks(i, carry):
        at = pl.multiple_of(i * 16, 16)
        blk = idc[pl.ds(at, 16), :]
        want = [jnp.broadcast_to(blk[:, k:k + 1], (16, 128)).astype(jnp.int16) for k in range(1 + F2)]
        for q in range(NAR):
            for c in range(FRONT // 128):
                here = lane16 + jnp.full((16, 128), q * FRONT + c * 128, jnp.int32).astype(jnp.int16)
                a, b = marks(here, want)
                fsel[q, pl.ds(at, 16), c * 128:(c + 1) * 128] = a
                fsel[q, pl.ds(SEED + at, 16), c * 128:(c + 1) * 128] = b
        return carry

    lax.fori_loop(0, SEED // 16, forward_marks, 0)

    for q in range(NAR):
        ids = gidx2[q] - y * FRONT
        for c in range(SEED // 128):
            for k in range(1 + F2):
                row = ids[k:k + 1, c * 128:(c + 1) * 128]
                wants[q, c, k] = jnp.broadcast_to(row, (16, 128)).astype(jnp.int16)

    def backward_marks(i):
        here = iota16 + jnp.full((16, 128), i * 16, jnp.int32).astype(jnp.int16)
        out = pl.ds(pl.multiple_of(i * 16, 16), 16)
        for q in range(NAR):
            for c in range(SEED // 128):
                a, b = marks(here, [wants[q, c, k] for k in range(1 + F2)])
                bsel[q, out, c * 128:(c + 1) * 128] = a
                bsel[q, out, SEED + c * 128:SEED + (c + 1) * 128] = b

    come = pulled.at[pl.ds(0, (DEV - 1) * CAP)]
    pltpu.make_async_copy(come, come, row_recv).wait()
    gone = featb.at[pl.ds(CAP, (DEV - 1) * CAP)]
    pltpu.make_async_copy(gone, gone, row_send).wait()
    sent = ask_rows.at[pl.ds(0, DEV - 1)]
    pltpu.make_async_copy(sent, sent, req_send).wait()

    def widen(i, c):
        rows = pl.ds(pl.multiple_of(i * 256, 256), 256)
        table[rows, :] = pulled[rows, :].astype(F32)
        return c

    lax.fori_loop(0, SRC // 256, widen, 0)
    table[SRC:SRC + 8, :] = jnp.zeros((8, D_IN), F32)
    for c in to_smem:
        c.wait()

    def cols(b):
        return pl.ds(pl.multiple_of(b * 256, 256), 256)

    def forward(b):
        @pl.when(b % 2 == 0)
        def _():
            blk = gbuf.at[left, cols(b), :]
            link(blk, blk, h_send.at[0, b], h_recv.at[0, b], right).wait_recv()
            link(blk, blk, h_send.at[2, b], h_recv.at[2, b], right).start()

        @pl.when(b % 2 == 1)
        def _():
            blk = gbuf.at[right, cols(b), :]
            link(blk, blk, h_send.at[1, b], h_recv.at[1, b], left).wait_recv()
            link(blk, blk, h_send.at[2, b], h_recv.at[2, b], left).start()

    own_rows, near_rows = own.reshape(256, 1, D_IN), near.reshape(256, 1, D_IN)

    def block(b, c):
        def some(i, c2):
            backward_marks(b * 16 + i)
            base = pl.multiple_of(b * 256 + i * 16, 16)
            for j in range(16):
                m = base + j
                here = i * 16 + j
                own_rows[here] = view[idx[0, m]]
                rows = [view[idx[1 + k, m]] for k in range(F1)]
                while len(rows) > 1:
                    rows = [p + q for p, q in zip(rows[::2], rows[1::2])] + ([rows[-1]] if len(rows) % 2 else [])
                near_rows[here] = rows[0] * inv[0, m]
            return c2

        lax.fori_loop(0, 16, some, 0)
        rows = cols(b)
        act = jnp.concatenate([own[...].astype(BF), near[...].astype(BF)], axis=1)
        a1[rows, :] = act[:, :128]
        a1[pl.ds(pl.multiple_of(FRONT + b * 256, 256), 256), :] = act[:, 128:]
        z = dot(act, gw1[...].reshape(2 * D_IN, HID)) + bias[0:1, 0:HID]
        z1[rows, :] = z
        gbuf[y, rows, :] = (z / (1.0 + jnp.exp(-z))).astype(BF)
        blk = gbuf.at[y, rows, :]
        link(blk, blk, h_send.at[0, b], h_recv.at[0, b], right).start()
        link(blk, blk, h_send.at[1, b], h_recv.at[1, b], left).start()

        @pl.when(b > 0)
        def _():
            forward(b - 1)

        return c

    lax.fori_loop(0, 8, block, 0)
    forward(7)

    def from_source(q):
        return dot(fsel[q], gbuf[q])

    total = from_source(y)
    for b in range(1, 8, 2):
        blk = gbuf.at[left, b * 256:(b + 1) * 256, :]
        link(blk, blk, h_send.at[0, b], h_recv.at[0, b], right).wait_recv()
    total = total + from_source(left)
    for b in range(0, 8, 2):
        blk = gbuf.at[right, b * 256:(b + 1) * 256, :]
        link(blk, blk, h_send.at[1, b], h_recv.at[1, b], left).wait_recv()
    total = total + from_source(right)
    for b in range(8):
        blk = gbuf.at[opp, b * 256:(b + 1) * 256, :]
        link(blk, blk, h_send.at[2, b], h_recv.at[2, b], right).wait_recv()
    total = total + from_source(opp)

    def wide(a):
        return jnp.concatenate([a, a], axis=1)

    near2 = (total[:SEED, :] * wide(invc[y])).astype(BF)
    self2 = total[SEED:, :].astype(BF)
    alive = live[...].astype(F32)
    diff = self2.astype(F32) - near2.astype(F32)
    pull_apart = wide(livec[...]) * diff

    def swap_start(buf, ssem, rsem):
        blk = buf.at[y]
        link(blk, blk, ssem.at[0], rsem.at[0], right).start()
        link(blk, blk, ssem.at[1], rsem.at[1], left).start()

    def swap_forward(buf, ssem, rsem, cut):
        blk = buf.at[left]
        link(blk, blk, ssem.at[0], rsem.at[0], right).wait_recv()
        half = buf.at[left, 0:cut, :]
        link(half, half, ssem.at[2], rsem.at[2], right).start()
        blk = buf.at[right]
        link(blk, blk, ssem.at[1], rsem.at[1], left).wait_recv()
        half = buf.at[right, cut:, :]
        link(half, half, ssem.at[3], rsem.at[3], left).start()

    def swap_end(buf, ssem, rsem, cut):
        half = buf.at[opp, 0:cut, :]
        link(half, half, ssem.at[2], rsem.at[2], right).wait_recv()
        half = buf.at[opp, cut:, :]
        link(half, half, ssem.at[3], rsem.at[3], left).wait_recv()

    def swap_sent(buf, ssem, rsem, cut):
        blk = buf.at[y]
        link(blk, blk, ssem.at[0], rsem.at[0], right).wait_send()
        link(blk, blk, ssem.at[1], rsem.at[1], left).wait_send()
        half = buf.at[left, 0:cut, :]
        link(half, half, ssem.at[2], rsem.at[2], right).wait_send()
        half = buf.at[right, cut:, :]
        link(half, half, ssem.at[3], rsem.at[3], left).wait_send()

    rbuf[y] = pull_apart.astype(BF)
    swap_start(rbuf, r_send, r_recv)

    act2 = jnp.concatenate([self2, near2], axis=1)
    cls = lax.broadcasted_iota(jnp.int32, (CLS_PAD, SEED), 0)
    b2 = b2c[0:CLS_PAD, :]
    logits = dot(w2t[...], act2, NT) + jnp.concatenate([b2] * 4, axis=1)
    logits = jnp.where(cls < CLS, logits, -1e30)
    top = jnp.max(logits, axis=0, keepdims=True)
    e = jnp.exp(logits - top)
    tot = jnp.sum(e, axis=0, keepdims=True)
    hot = cls == labels[...]
    picked = jnp.sum(jnp.where(hot, logits, 0.0), axis=0, keepdims=True)
    dlog = (alive * (e * (1.0 / tot) - jnp.where(hot, 1.0, 0.0)) * (1.0 / SEEDS_ALL)).astype(BF)
    dbuf[y] = dlog
    swap_start(dbuf, d_send, d_recv)

    loss = jnp.sum(alive * (top + jnp.log(tot) - picked), axis=1, keepdims=True)
    loss = loss + SEEDS_ALL / 2 * jnp.sum(pull_apart * diff, keepdims=True)
    g2t = dot(dlog, act2).astype(BF)
    for q in range(NAR):
        pay2[q * CLS_PAD:(q + 1) * CLS_PAD, :] = g2t[:, q * 128:(q + 1) * 128]

    def plane(i):
        return ((g + i) % GRP, y)

    def to_owner(pay, inbox, count, n):
        def body(i, c):
            t = (g + i) % GRP
            for slot in range(2):
                p = t + slot * GRP

                @pl.when(p < count)
                def _():
                    pltpu.make_async_remote_copy(
                        src_ref=pay.at[pl.ds(pl.multiple_of(p * 16, 16), 16)], dst_ref=inbox.at[slot, g],
                        send_sem=rs_send.at[n], recv_sem=rs_recv.at[n, slot], device_id=(t, y), device_id_type=MESH,
                    ).start()

            return c

        lax.fori_loop(1, GRP, body, 0)

    def add_plane(pay, inbox, ybox, count, n):
        for slot in range(2):
            p = g + slot * GRP

            @pl.when(p < count)
            def _():
                got = inbox.at[slot, pl.ds(0, GRP - 1)]
                pltpu.make_async_copy(got, got, rs_recv.at[n, slot]).wait()
                inbox[slot, g] = pay[pl.ds(pl.multiple_of(p * 16, 16), 16), :]
                ybox[slot, y] = jnp.sum(inbox[slot].astype(F32), axis=0)
                blk = ybox.at[slot, y]
                for d in range(1, NAR):
                    link(blk, blk, y_send.at[n, slot, d - 1], y_recv.at[n, slot, d - 1], (y + d) % NAR).start()

    def add_group(ybox, res, count, n):
        for slot in range(2):
            p = g + slot * GRP

            @pl.when(p < count)
            def _():
                blk = ybox.at[slot, y]
                for d in range(1, NAR):
                    link(blk, blk, y_send.at[n, slot, d - 1], y_recv.at[n, slot, d - 1], (y + d) % NAR).wait()
                rows16 = pl.ds(pl.multiple_of(p * 16, 16), 16)
                res[rows16, :] = (ybox[slot, 0] + ybox[slot, 1]) + (ybox[slot, 2] + ybox[slot, 3])

                def tell(i, c):
                    pltpu.make_async_remote_copy(
                        src_ref=res.at[rows16], dst_ref=res.at[rows16], send_sem=ag_send.at[n], recv_sem=ag_recv.at[n],
                        device_id=plane(i), device_id_type=MESH,
                    ).start()
                    return c

                lax.fori_loop(1, GRP, tell, 0)

    def take(res, count, n):
        two_here = g + GRP < count
        for own, here in ((2, two_here), (1, jnp.logical_not(two_here))):
            @pl.when(here)
            def _(own=own):
                got = res.at[pl.ds(0, (count - own) * 16)]
                pltpu.make_async_copy(got, got, ag_recv.at[n]).wait()

    def sums_sent(pay, count, n):
        two_here = g + GRP < count
        for own, here in ((2, two_here), (1, jnp.logical_not(two_here))):
            @pl.when(here)
            def _(own=own):
                gone = pay.at[pl.ds(0, (count - own) * 16)]
                pltpu.make_async_copy(gone, gone, rs_send.at[n]).wait()
                gone = table.at[pl.ds(0, own * (GRP - 1) * 16)]
                pltpu.make_async_copy(gone, gone, ag_send.at[n]).wait()

    to_owner(pay2, inbox2, P2, 1)

    def add_grads(q, fresh=False):
        da = dot(dbuf[q], w2t[...], TN)
        r = rbuf[q].astype(F32)
        ds = (da[:, :HID] + r).astype(BF)
        dn = ((da[:, HID:] - r) * wide(invc[q])).astype(BF)
        both = jnp.concatenate([dn, ds], axis=0)

        def rows512(i, c):
            part = dot(bsel[q, pl.ds(pl.multiple_of(i * 512, 512), 512), :], both)
            for h in range(2):
                rows = pl.ds(pl.multiple_of(h * FRONT + i * 512, 512), 512)
                now = part[:, h * 128:(h + 1) * 128]
                dh1[rows, :] = now if fresh else dh1[rows, :] + now
            return c

        lax.fori_loop(0, FRONT // 512, rows512, 0)

    for c in range(2):
        a1t[c * 128:(c + 1) * 128, :] = a1[c * FRONT:(c + 1) * FRONT, :].T
    db2 = jnp.sum(dlog.astype(F32), axis=1, keepdims=True)
    db2 = jnp.broadcast_to(db2, (CLS_PAD, 128)).T[0:1, :]
    swap_forward(rbuf, r_send, r_recv, SEED // 2)
    add_grads(y, True)
    swap_forward(dbuf, d_send, d_recv, 96)
    add_grads(left)
    add_grads(right)
    add_plane(pay2, inbox2, ybox2, P2, 1)
    swap_end(rbuf, r_send, r_recv, SEED // 2)
    swap_end(dbuf, d_send, d_recv, 96)
    add_group(ybox2, res2, P2, 1)
    add_grads(opp)

    def to_z(i, db):
        z = z1[pl.ds(pl.multiple_of(i * 128, 128), 128), :]
        sig = 1.0 / (1.0 + jnp.exp(-z))
        dh = jnp.concatenate(
            [dh1[pl.ds(pl.multiple_of(h * FRONT + i * 128, 128), 128), :] for h in range(2)], axis=1
        )
        dz = dh * sig * (1.0 + z * (1.0 - sig))
        low = dz.astype(BF)
        for h in range(2):
            a1[pl.ds(pl.multiple_of((2 + h) * FRONT + i * 128, 128), 128), :] = low[:, h * 128:(h + 1) * 128]
        return db + jnp.sum(low.astype(F32), axis=0, keepdims=True)

    db1 = lax.fori_loop(0, FRONT // 128, to_z, jnp.zeros((1, HID), F32))
    dz = jnp.concatenate([a1[2 * FRONT:3 * FRONT, :], a1[3 * FRONT:4 * FRONT, :]], axis=1)
    g1 = dot(a1t[...], dz).astype(BF)
    pay1[0:256, :] = g1[:, :128]
    pay1[256:512, :] = g1[:, 128:]
    misc[...] = jnp.zeros((16, 128), F32)

    def two(rows, v):
        hi = v.astype(BF).astype(F32)
        misc[rows:rows + 1, 0:v.shape[1]] = hi
        misc[rows + 4:rows + 5, 0:v.shape[1]] = v - hi

    two(0, db1[:, :128])
    two(1, db1[:, 128:])
    two(2, db2[:, :128])
    two(3, db2[:, 128:])
    hi = loss.astype(BF).astype(F32)
    misc[8:9, 0:1] = hi
    misc[9:10, 0:1] = loss - hi
    pay1[512:528, :] = misc[...].astype(BF)
    to_owner(pay1, inbox1, P1, 0)

    take(res2, P2, 1)
    mom2 = jnp.concatenate(
        [MU * gm2t[q] + res2[q * CLS_PAD:(q + 1) * CLS_PAD, :] for q in range(NAR)], axis=1
    )
    for q in range(NAR):
        x2s[q] = mom2[:, q * 128:(q + 1) * 128]
    o_all[ROW_M2:ROW_M2 + CLS_PAD, :] = x2s[y]
    x2 = mom2 * (1.0 / (jnp.sqrt(jnp.sum(mom2 * mom2, keepdims=True)) + 1e-07))
    x2 = ns_step(x2)
    add_plane(pay1, inbox1, ybox1, P1, 0)
    x2 = ns_step(x2)
    add_group(ybox1, o_all, P1, 0)
    for _ in range(NS_ITERS - 2):
        x2 = ns_step(x2)
    for q in range(NAR):
        x2s[q] = x2[:, q * 128:(q + 1) * 128]
    o_all[ROW_X2:ROW_X2 + CLS_PAD, :] = x2s[y]
    take(o_all, P1, 0)

    for b in range(8):
        blk = gbuf.at[y, b * 256:(b + 1) * 256, :]
        link(blk, blk, h_send.at[0, b], h_recv.at[0, b], right).wait_send()
        link(blk, blk, h_send.at[1, b], h_recv.at[1, b], left).wait_send()
        blk = gbuf.at[opp, b * 256:(b + 1) * 256, :]
        link(blk, blk, h_send.at[2, b], h_recv.at[2, b], right).wait_send()
    swap_sent(rbuf, r_send, r_recv, SEED // 2)
    swap_sent(dbuf, d_send, d_recv, 96)

    sums_sent(pay2, P2, 1)
    sums_sent(pay1, P1, 0)


def main(reqt, feat, idx1t, msk1t, idx2t, msk2t, labels, live, w1, w2own, m1, m2own, bias):
    vm = pl.BlockSpec(memory_space=pltpu.VMEM)
    dma = pltpu.SemaphoreType.DMA
    sds = jax.ShapeDtypeStruct
    V = pltpu.VMEM
    return pl.pallas_call(
        main_kernel,
        out_shape=sds((ROWS, 128), F32),
        in_specs=[vm, pl.BlockSpec(memory_space=pl.ANY)] + [vm] * 11,
        out_specs=vm,
        scratch_shapes=[
            V((SRC + 8, D_IN), F32),
            V((OWN, D_IN), BF),
            V((SRC, D_IN), BF),
            V((CAP, D_IN), F32),
            V((DEV, 128), jnp.int32),
            V((DEV, 128), jnp.int32),
            V((16, FRONT), jnp.int32),
            V((1, FRONT), F32),
            V((256, D_IN), F32),
            V((256, D_IN), F32),
            V((FRONT, HID), F32),
            V((2 * D_IN, FRONT), BF),
            V((NAR, FRONT, HID), BF),
            V((NAR, 2 * SEED, FRONT), BF),
            V((NAR, FRONT, 2 * SEED), BF),
            V((NAR, 4, 1 + F2, 16, 128), jnp.int16),
            V((SEED, 16), jnp.int32),
            V((NAR, SEED, 128), F32),
            V((SEED, 128), F32),
            V((NAR, SEED, HID), BF),
            V((NAR, CLS_PAD, SEED), BF),
            V((NAR, 64, HID), BF),
            V((NAR, CLS_PAD, 128), BF),
            V((NAR, 64, HID), F32),
            V((NAR, CLS_PAD, 128), F32),
            V((NAR, 16, SEED), jnp.int32),
            V((CLS_PAD, 2 * HID), BF),
            V((HID, 128), F32),
            V((P1 * 16, 128), BF),
            V((P2 * 16, 128), BF),
            V((16, 128), F32),
            V((2, GRP, 16, 128), BF),
            V((2, GRP, 16, 128), BF),
            V((2, NAR, 16, 128), F32),
            V((2, NAR, 16, 128), F32),
            V((P2 * 16, 128), F32),
            V((NAR, CLS_PAD, 128), F32),
            pltpu.SMEM((DEV, 1, 128), jnp.int32),
            pltpu.SMEM((16, FRONT), jnp.int32),
            pltpu.SMEM((1, FRONT), F32),
            dma, dma((2,)), dma((GRP,)), dma, dma((GRP,)), dma, dma, dma((5, 3)), dma((5, 3)),
            dma((3, 8)), dma((3, 8)), dma((4,)), dma((4,)), dma((4,)), dma((4,)),
            dma((2,)), dma((2, 2)), dma((2, 2, 3)), dma((2, 2, 3)), dma((2,)), dma((2,)),
        ],
        compiler_params=pltpu.CompilerParams(
            collective_id=0, has_side_effects=True, vmem_limit_bytes=62 * 2**20
        ),
    )(reqt, feat, idx1t, msk1t, idx2t, msk2t, labels, live, w1, w2own, m1, m2own, bias)


def update_kernel(
    res, w1own, w2own, bias, biasm, biasv,
    o_loss, o_first, o_second, o_mom1, o_mom2, o_flow, o_slow, o_bias, o_bm, o_bv,
    x1s,
):
    y = lax.axis_index("nar")
    mom1 = jnp.concatenate(
        [res[i * 256:i * 256 + 256, :] + res[ROW_G1 + i * 256:ROW_G1 + i * 256 + 256, :] for i in range(2)], axis=1
    )
    x1s[...] = mom1
    block64 = pl.ds(pl.multiple_of(y * 64, 64), 64)
    o_mom1[...] = x1s[block64, :]
    x1 = mom1 * (1.0 / (jnp.sqrt(jnp.sum(mom1 * mom1, keepdims=True)) + 1e-07))
    for _ in range(NS_ITERS):
        x1 = ns_step(x1)
    x1s[...] = x1
    first_new = w1own[...] * (1.0 - WDECAY) - x1s[block64, :]
    o_first[...] = first_new
    o_flow[...] = first_new.astype(BF)
    second = w2own[...] * (1.0 - WDECAY) - (2 * HID / CLS) ** 0.5 * res[ROW_X2:ROW_X2 + CLS, :]
    o_second[...] = second
    o_slow[...] = second.astype(BF)
    o_mom2[...] = res[ROW_M2:ROW_M2 + CLS, :]

    gb = res[512:516, :] + res[516:520, :]
    gb = jnp.concatenate([gb[0:1, :], gb[1:2, :], gb[2:3, :], gb[3:4, 0:44]], axis=1)
    m_new = BETA_ONE * biasm[...] + (1.0 - BETA_ONE) * gb
    v_new = BETA_TWO * biasv[...] + (1.0 - BETA_TWO) * gb * gb
    m_hat = m_new / (1.0 - BETA_ONE**STEP)
    v_hat = v_new / (1.0 - BETA_TWO**STEP)
    o_bias[...] = bias[...] * (1.0 - LR_BIAS * WDECAY) - LR_BIAS * m_hat / (jnp.sqrt(v_hat) + EPSILON)
    o_bm[...] = m_new
    o_bv[...] = v_new
    o_loss[...] = res[520:521, 0:1] + res[521:522, 0:1]


def update(*args):
    vm = pl.BlockSpec(memory_space=pltpu.VMEM)
    sds = jax.ShapeDtypeStruct
    return pl.pallas_call(
        update_kernel,
        out_shape=[
            sds((1, 1), F32), sds((64, HID), F32), sds((CLS, 128), F32), sds((64, HID), F32), sds((CLS, 128), F32),
            sds((64, HID), BF), sds((CLS, 128), BF), sds((1, 428), F32), sds((1, 428), F32), sds((1, 428), F32),
        ],
        in_specs=[vm] * 6,
        out_specs=[vm] * 10,
        scratch_shapes=[pltpu.VMEM((2 * D_IN, HID), F32)],
        compiler_params=pltpu.CompilerParams(vmem_limit_bytes=32 * 2**20),
    )(*args)


def per_device(
    features, requests, index_one, mask_one, index_two, mask_two, labels, seed_live,
    w_first, w_second, mom_first, mom_second, biases, bias_m, bias_v,
):
    w2own, bias = w_second.T, biases[None, :]
    res = main(
        requests.T, features, index_one.T, mask_one.T, index_two.T, mask_two.T, labels[None, :], seed_live[None, :],
        w_first, w2own, mom_first, mom_second.T, bias,
    )
    loss, first_new, second_new, mom_one, mom_two, first_low, second_low, bias_new, m_new, v_new = update(
        res, w_first, w2own, bias, bias_m[None, :], bias_v[None, :]
    )
    return (
        loss.reshape(()), first_new, second_new.T, mom_one, mom_two.T, first_low, second_low.T,
        bias_new.reshape(-1), m_new.reshape(-1), v_new.reshape(-1),
    )


def solution(mesh):
    both = ("grp", "nar")
    placed = (
        P(both, None), P(both, None), P(both, None), P(both, None), P(both, None), P(both, None),
        P(both), P(both), P("nar", None), P("nar", None), P("nar", None), P("nar", None), P(), P(), P(),
    )
    nar = P("nar", None)
    return jax.shard_map(
        per_device, mesh=mesh, in_specs=placed,
        out_specs=(P(), nar, nar, nar, nar, nar, nar, P(), P(), P()), check_vma=False,
    )
```

```python
import functools

import jax
import jax.numpy as jnp
from jax import lax
from jax.experimental import pallas as pl
from jax.experimental.pallas import tpu as pltpu
from jax.sharding import PartitionSpec as P

HID = 256
CLS = 172
CLS_PAD = 176
D_IN = 128
F1 = 15
F2 = 10
NS_ITERS = 5
STEP = 10
LAM = 0.5
MU = 0.95
WDECAY = 0.01
LR_BIAS = 0.05
BETA_ONE = 0.9
BETA_TWO = 0.999
EPSILON = 1e-08
NS_A = 3.4445
NS_B = -4.775
NS_C = 2.0315
HIGH = lax.Precision.HIGHEST
MESH = pl.DeviceIdType.MESH
BF = jnp.bfloat16
F32 = jnp.float32

DEV = 128
NAR = 4
OWN = 8192
CAP = 64
SRC = 8192
FRONT = 2048
SEED = 512


def all_to(t):
    return (t // NAR, t % NAR)


P1 = 33
P2 = 44
GRP = 32
ROW_G1 = P1 * 16
ROW_M2 = ROW_G1 + 512
ROW_X2 = ROW_M2 + CLS_PAD
ROWS = ROW_X2 + CLS_PAD
SEEDS_ALL = SEED * DEV


def dot(a, b, dims=((1,), (0,))):
    return lax.dot_general(a, b, (dims, ((), ())), preferred_element_type=F32)


NN = ((1,), (0,))
NT = ((1,), (1,))
TN = ((0,), (0,))


def split(a):
    hi = a.astype(BF)
    return hi, (a - hi.astype(F32)).astype(BF)


def dot3(a, b, dims):
    (ah, al), (bh, bl) = a, b
    return dot(ah, bh, dims) + (dot(ah, bl, dims) + dot(al, bh, dims))


def ns_step(x):
    xs = split(x)
    gram = dot3(xs, xs, NT)
    gs = split(gram)
    mix = NS_B * gram + NS_C * dot3(gs, gs, NN)
    return NS_A * x + dot3(split(mix), xs, NN)


def spread(row):
    return jnp.broadcast_to(row, (128, 128)).T


def main_kernel(
    reqt, feat, idx1t, msk1t, idx2t, msk2t, labels, live, w1, w2own, m1, m2own, bias,
    o_all,
    table, featb, pulled, stage, reqv, reqin, idxv, invv, near, own, z1, a1t, gbuf, fsel, bsel, wants, idc, invc, livec, rbuf, dbuf,
    gw1, gw2t, gm1, gm2t, gidx2, w2t, b2c, pay1, pay2, misc, inbox1, inbox2, ybox1, ybox2, res2, x2s,
    reqs, idx, inv,
    feat_sem, loc_sem, ask_sem, req_send, req_recv, row_send, row_recv, nar_send, nar_recv,
    h_send, h_recv, r_send, r_recv, d_send, d_recv, rs_send, rs_recv, y_send, y_recv, ag_send, ag_recv,
):
    a1, dh1 = pulled, table
    g = lax.axis_index("grp")
    y = lax.axis_index("nar")
    me = g * NAR + y
    left, right, opp = (y + 3) % NAR, (y + 1) % NAR, (y + 2) % NAR

    load = pltpu.make_async_copy(feat, featb, feat_sem)
    load.start()

    ys = [(y + d) % NAR for d in range(NAR)]

    def link(src, dst, ssem, rsem, to):
        return pltpu.make_async_remote_copy(
            src_ref=src, dst_ref=dst, send_sem=ssem, recv_sem=rsem, device_id=(g, to), device_id_type=MESH
        )

    reqv[...] = jnp.concatenate([reqt[...], jnp.zeros((DEV - CAP, DEV), jnp.int32)], axis=0).T
    ask_rows = reqv.reshape(DEV, 1, 128)
    got_rows = reqin.reshape(DEV, 1, 128)

    gw1[y] = w1[...].astype(BF)
    pad = CLS_PAD - CLS
    gw2t[y] = jnp.concatenate([w2own[...], jnp.zeros((pad, 128), F32)], axis=0).astype(BF)
    gm1[y] = m1[...]
    gm2t[y] = jnp.concatenate([m2own[...], jnp.zeros((pad, 128), F32)], axis=0)
    gidx2[y] = jnp.concatenate(
        [idx2t[0:1, :], jnp.where(msk2t[...] > 0, idx2t[1:, :], -1), jnp.zeros((5, SEED), jnp.int32)], axis=0
    )
    shared = (gidx2, gw1, gw2t, gm1, gm2t)

    def ask_one(t, u, n):
        row = t * NAR + u
        pltpu.make_async_remote_copy(
            src_ref=ask_rows.at[row], dst_ref=got_rows.at[me], send_sem=req_send, recv_sem=req_recv.at[n],
            device_id=(t, u), device_id_type=MESH,
        ).start()

    def ask(i, c):
        n = (i * 13) % GRP
        t = (g + n) % GRP
        for d in range(NAR):
            ask_one(t, ys[d], n)
        return c

    for d in range(1, NAR):
        ask_one(g, ys[d], 0)
    lax.fori_loop(1, GRP, ask, 0)
    reqin[pl.ds(me, 1), :] = reqv[pl.ds(me, 1), :]
    for n, a in enumerate(shared):
        for d in range(1, NAR):
            link(a.at[y], a.at[y], nar_send.at[n, d - 1], nar_recv.at[n, d - 1], (y + d) % NAR).start()

    msk = msk1t[...]
    idxv[0:1, :] = idx1t[0:1, :]
    idxv[1:16, :] = jnp.where(msk > 0, idx1t[1:16, :], SRC)
    invv[...] = 1.0 / jnp.maximum(jnp.sum(msk.astype(F32), axis=0, keepdims=True), 1.0)
    to_smem = [pltpu.make_async_copy(idxv, idx, loc_sem.at[0]), pltpu.make_async_copy(invv, inv, loc_sem.at[1])]
    for c in to_smem:
        c.start()

    load.wait()

    def widen_features(i, c):
        rows = pl.ds(pl.multiple_of(i * 256, 256), 256)
        table[rows, :] = featb[rows, :].astype(F32)
        return c

    lax.fori_loop(0, OWN // 256, widen_features, 0)

    view = table.reshape(SRC + 8, 1, D_IN)
    my_rows = pl.ds(pl.multiple_of(me * CAP, CAP), CAP)

    def pick(t, u, slot):
        for r in range(CAP):
            stage[r:r + 1, :] = view[reqs[t * NAR + u, 0, r]]
        featb[slot, :] = stage[...].astype(BF)

    def serve_one(t, u, slot):
        pick(t, u, slot)
        pltpu.make_async_remote_copy(
            src_ref=featb.at[slot], dst_ref=pulled.at[my_rows],
            send_sem=row_send, recv_sem=row_recv, device_id=(t, u), device_id_type=MESH,
        ).start()

    def asked(count, n):
        rows = got_rows.at[pl.ds(0, count)]
        pltpu.make_async_copy(rows, rows, req_recv.at[n]).wait()

    def to_scalars(t, n):
        rows = pl.ds(pl.multiple_of(t * NAR, NAR), NAR)
        return pltpu.make_async_copy(got_rows.at[rows], reqs.at[rows], ask_sem.at[n])

    def whose(i):
        n = (i * 13) % GRP
        return n, (g + GRP - n) % GRP

    def fetch(i):
        n, t = whose(i)
        asked(NAR, n)
        to_scalars(t, n).start()

    def serve(i, c):
        n, t = whose(i)

        @pl.when(i < GRP - 1)
        def _():
            fetch(i + 1)

        to_scalars(t, n).wait()
        for d in range(NAR):
            serve_one(t, ys[d], pl.ds(pl.multiple_of((i * NAR + d) * CAP, CAP), CAP))
        return c

    fetch(1)
    lax.fori_loop(1, GRP, serve, 0)
    asked(NAR - 1, 0)
    to_scalars(g, 0).start()
    to_scalars(g, 0).wait()
    for d in range(1, NAR):
        serve_one(g, ys[d], pl.ds(d * CAP, CAP))
    pick(g, y, pl.ds(0, CAP))
    pulled[my_rows, :] = featb[0:CAP, :]

    for n, a in enumerate(shared):
        for d in range(1, NAR):
            link(a.at[y], a.at[y], nar_send.at[n, d - 1], nar_recv.at[n, d - 1], (y + d) % NAR).wait()
    for q in range(NAR):
        o_all[ROW_G1 + q * 64:ROW_G1 + q * 64 + 64, :] = MU * gm1[q, :, 0:128]
        o_all[ROW_G1 + 256 + q * 64:ROW_G1 + 256 + q * 64 + 64, :] = MU * gm1[q, :, 128:256]
    for q in range(NAR):
        w2t[:, q * 128:(q + 1) * 128] = gw2t[q]
    last = jnp.concatenate([bias[0:1, 384:428], jnp.zeros((1, 84), F32)], axis=1)
    b2c[...] = jnp.concatenate([spread(bias[0:1, 256:384]), spread(last)], axis=0)

    def column(row):
        return jnp.concatenate([spread(row[:, c * 128:(c + 1) * 128]) for c in range(SEED // 128)], axis=0)

    for q in range(NAR):
        n = jnp.sum((gidx2[q, 1:1 + F2, :] >= 0).astype(F32), axis=0, keepdims=True)
        invc[q] = column(1.0 / jnp.maximum(n, 1.0))
    livec[...] = column(2.0 * LAM / HID / SEEDS_ALL * live[...].astype(F32))

    lane16 = lax.broadcasted_iota(jnp.int32, (16, 128), 1).astype(jnp.int16)
    iota16 = lax.broadcasted_iota(jnp.int32, (16, 128), 0).astype(jnp.int16)
    one, zero = jnp.ones((16, 128), BF), jnp.zeros((16, 128), BF)

    def marks(here, want):
        acc = jnp.where(here == want[1], one, zero)
        for k in range(2, 1 + F2):
            acc = acc + jnp.where(here == want[k], one, zero)
        return acc, jnp.where(here == want[0], one, zero)

    idc[...] = gidx2[y].T

    def forward_marks(i, carry):
        at = pl.multiple_of(i * 16, 16)
        blk = idc[pl.ds(at, 16), :]
        want = [jnp.broadcast_to(blk[:, k:k + 1], (16, 128)).astype(jnp.int16) for k in range(1 + F2)]
        for q in range(NAR):
            for c in range(FRONT // 128):
                here = lane16 + jnp.full((16, 128), q * FRONT + c * 128, jnp.int32).astype(jnp.int16)
                a, b = marks(here, want)
                fsel[q, pl.ds(at, 16), c * 128:(c + 1) * 128] = a
                fsel[q, pl.ds(SEED + at, 16), c * 128:(c + 1) * 128] = b
        return carry

    lax.fori_loop(0, SEED // 16, forward_marks, 0)

    for q in range(NAR):
        ids = gidx2[q] - y * FRONT
        for c in range(SEED // 128):
            for k in range(1 + F2):
                row = ids[k:k + 1, c * 128:(c + 1) * 128]
                wants[q, c, k] = jnp.broadcast_to(row, (16, 128)).astype(jnp.int16)

    def backward_marks(i):
        here = iota16 + jnp.full((16, 128), i * 16, jnp.int32).astype(jnp.int16)
        out = pl.ds(pl.multiple_of(i * 16, 16), 16)
        for q in range(NAR):
            for c in range(SEED // 128):
                a, b = marks(here, [wants[q, c, k] for k in range(1 + F2)])
                bsel[q, out, c * 128:(c + 1) * 128] = a
                bsel[q, out, SEED + c * 128:SEED + (c + 1) * 128] = b

    come = pulled.at[pl.ds(0, (DEV - 1) * CAP)]
    pltpu.make_async_copy(come, come, row_recv).wait()
    gone = featb.at[pl.ds(CAP, (DEV - 1) * CAP)]
    pltpu.make_async_copy(gone, gone, row_send).wait()
    sent = ask_rows.at[pl.ds(0, DEV - 1)]
    pltpu.make_async_copy(sent, sent, req_send).wait()

    def widen(i, c):
        rows = pl.ds(pl.multiple_of(i * 256, 256), 256)
        table[rows, :] = pulled[rows, :].astype(F32)
        return c

    lax.fori_loop(0, SRC // 256, widen, 0)
    table[SRC:SRC + 8, :] = jnp.zeros((8, D_IN), F32)
    for c in to_smem:
        c.wait()

    def cols(b):
        return pl.ds(pl.multiple_of(b * 256, 256), 256)

    def forward(b):
        @pl.when(b % 2 == 0)
        def _():
            blk = gbuf.at[left, cols(b), :]
            link(blk, blk, h_send.at[0, b], h_recv.at[0, b], right).wait_recv()
            link(blk, blk, h_send.at[2, b], h_recv.at[2, b], right).start()

        @pl.when(b % 2 == 1)
        def _():
            blk = gbuf.at[right, cols(b), :]
            link(blk, blk, h_send.at[1, b], h_recv.at[1, b], left).wait_recv()
            link(blk, blk, h_send.at[2, b], h_recv.at[2, b], left).start()

    def block(b, c):
        def some(i, c2):
            backward_marks(b * 16 + i)
            base = pl.multiple_of(b * 256 + i * 16, 16)
            for j in range(16):
                m = base + j
                here = pl.ds(pl.multiple_of(i * 16, 16) + j, 1)
                own[here, :] = view[idx[0, m]]
                rows = [view[idx[1 + k, m]] for k in range(F1)]
                while len(rows) > 1:
                    rows = [p + q for p, q in zip(rows[::2], rows[1::2])] + ([rows[-1]] if len(rows) % 2 else [])
                near[here, :] = rows[0] * inv[0, m]
            return c2

        lax.fori_loop(0, 16, some, 0)
        rows = cols(b)
        act = jnp.concatenate([own[...].astype(BF), near[...].astype(BF)], axis=1)
        a1[rows, :] = act[:, :128]
        a1[pl.ds(pl.multiple_of(FRONT + b * 256, 256), 256), :] = act[:, 128:]
        z = dot(act, gw1[...].reshape(2 * D_IN, HID)) + bias[0:1, 0:HID]
        z1[rows, :] = z
        gbuf[y, rows, :] = (z / (1.0 + jnp.exp(-z))).astype(BF)
        blk = gbuf.at[y, rows, :]
        link(blk, blk, h_send.at[0, b], h_recv.at[0, b], right).start()
        link(blk, blk, h_send.at[1, b], h_recv.at[1, b], left).start()

        @pl.when(b > 0)
        def _():
            forward(b - 1)

        return c

    lax.fori_loop(0, 8, block, 0)
    forward(7)

    def from_source(q):
        return dot(fsel[q], gbuf[q])

    total = from_source(y)
    for b in range(1, 8, 2):
        blk = gbuf.at[left, b * 256:(b + 1) * 256, :]
        link(blk, blk, h_send.at[0, b], h_recv.at[0, b], right).wait_recv()
    total = total + from_source(left)
    for b in range(0, 8, 2):
        blk = gbuf.at[right, b * 256:(b + 1) * 256, :]
        link(blk, blk, h_send.at[1, b], h_recv.at[1, b], left).wait_recv()
    total = total + from_source(right)
    for b in range(8):
        blk = gbuf.at[opp, b * 256:(b + 1) * 256, :]
        link(blk, blk, h_send.at[2, b], h_recv.at[2, b], right).wait_recv()
    total = total + from_source(opp)

    def wide(a):
        return jnp.concatenate([a, a], axis=1)

    near2 = (total[:SEED, :] * wide(invc[y])).astype(BF)
    self2 = total[SEED:, :].astype(BF)
    alive = live[...].astype(F32)
    diff = self2.astype(F32) - near2.astype(F32)
    pull_apart = wide(livec[...]) * diff

    def swap_start(buf, ssem, rsem):
        blk = buf.at[y]
        link(blk, blk, ssem.at[0], rsem.at[0], right).start()
        link(blk, blk, ssem.at[1], rsem.at[1], left).start()

    def swap_forward(buf, ssem, rsem, cut):
        blk = buf.at[left]
        link(blk, blk, ssem.at[0], rsem.at[0], right).wait_recv()
        half = buf.at[left, 0:cut, :]
        link(half, half, ssem.at[2], rsem.at[2], right).start()
        blk = buf.at[right]
        link(blk, blk, ssem.at[1], rsem.at[1], left).wait_recv()
        half = buf.at[right, cut:, :]
        link(half, half, ssem.at[3], rsem.at[3], left).start()

    def swap_end(buf, ssem, rsem, cut):
        half = buf.at[opp, 0:cut, :]
        link(half, half, ssem.at[2], rsem.at[2], right).wait_recv()
        half = buf.at[opp, cut:, :]
        link(half, half, ssem.at[3], rsem.at[3], left).wait_recv()

    def swap_sent(buf, ssem, rsem, cut):
        blk = buf.at[y]
        link(blk, blk, ssem.at[0], rsem.at[0], right).wait_send()
        link(blk, blk, ssem.at[1], rsem.at[1], left).wait_send()
        half = buf.at[left, 0:cut, :]
        link(half, half, ssem.at[2], rsem.at[2], right).wait_send()
        half = buf.at[right, cut:, :]
        link(half, half, ssem.at[3], rsem.at[3], left).wait_send()

    rbuf[y] = pull_apart.astype(BF)
    swap_start(rbuf, r_send, r_recv)

    act2 = jnp.concatenate([self2, near2], axis=1)
    cls = lax.broadcasted_iota(jnp.int32, (CLS_PAD, SEED), 0)
    b2 = b2c[0:CLS_PAD, :]
    logits = dot(w2t[...], act2, NT) + jnp.concatenate([b2] * 4, axis=1)
    logits = jnp.where(cls < CLS, logits, -1e30)
    top = jnp.max(logits, axis=0, keepdims=True)
    e = jnp.exp(logits - top)
    tot = jnp.sum(e, axis=0, keepdims=True)
    hot = cls == labels[...]
    picked = jnp.sum(jnp.where(hot, logits, 0.0), axis=0, keepdims=True)
    dlog = (alive * (e * (1.0 / tot) - jnp.where(hot, 1.0, 0.0)) * (1.0 / SEEDS_ALL)).astype(BF)
    dbuf[y] = dlog
    swap_start(dbuf, d_send, d_recv)

    loss = jnp.sum(alive * (top + jnp.log(tot) - picked), axis=1, keepdims=True)
    loss = loss + SEEDS_ALL / 2 * jnp.sum(pull_apart * diff, keepdims=True)
    g2t = dot(dlog, act2).astype(BF)
    for q in range(NAR):
        pay2[q * CLS_PAD:(q + 1) * CLS_PAD, :] = g2t[:, q * 128:(q + 1) * 128]

    def plane(i):
        return ((g + i) % GRP, y)

    def to_owner(pay, inbox, count, n):
        def body(i, c):
            t = (g + i) % GRP
            for slot in range(2):
                p = t + slot * GRP

                @pl.when(p < count)
                def _():
                    pltpu.make_async_remote_copy(
                        src_ref=pay.at[pl.ds(pl.multiple_of(p * 16, 16), 16)], dst_ref=inbox.at[slot, g],
                        send_sem=rs_send.at[n], recv_sem=rs_recv.at[n, slot], device_id=(t, y), device_id_type=MESH,
                    ).start()

            return c

        lax.fori_loop(1, GRP, body, 0)

    def add_plane(pay, inbox, ybox, count, n):
        for slot in range(2):
            p = g + slot * GRP

            @pl.when(p < count)
            def _():
                got = inbox.at[slot, pl.ds(0, GRP - 1)]
                pltpu.make_async_copy(got, got, rs_recv.at[n, slot]).wait()
                inbox[slot, g] = pay[pl.ds(pl.multiple_of(p * 16, 16), 16), :]
                ybox[slot, y] = jnp.sum(inbox[slot].astype(F32), axis=0)
                blk = ybox.at[slot, y]
                for d in range(1, NAR):
                    link(blk, blk, y_send.at[n, slot, d - 1], y_recv.at[n, slot, d - 1], (y + d) % NAR).start()

    def add_group(ybox, res, count, n):
        for slot in range(2):
            p = g + slot * GRP

            @pl.when(p < count)
            def _():
                blk = ybox.at[slot, y]
                for d in range(1, NAR):
                    link(blk, blk, y_send.at[n, slot, d - 1], y_recv.at[n, slot, d - 1], (y + d) % NAR).wait()
                rows16 = pl.ds(pl.multiple_of(p * 16, 16), 16)
                res[rows16, :] = (ybox[slot, 0] + ybox[slot, 1]) + (ybox[slot, 2] + ybox[slot, 3])

                def tell(i, c):
                    pltpu.make_async_remote_copy(
                        src_ref=res.at[rows16], dst_ref=res.at[rows16], send_sem=ag_send.at[n], recv_sem=ag_recv.at[n],
                        device_id=plane(i), device_id_type=MESH,
                    ).start()
                    return c

                lax.fori_loop(1, GRP, tell, 0)

    def take(res, count, n):
        two_here = g + GRP < count
        for own, here in ((2, two_here), (1, jnp.logical_not(two_here))):
            @pl.when(here)
            def _(own=own):
                got = res.at[pl.ds(0, (count - own) * 16)]
                pltpu.make_async_copy(got, got, ag_recv.at[n]).wait()

    def sums_sent(pay, count, n):
        two_here = g + GRP < count
        for own, here in ((2, two_here), (1, jnp.logical_not(two_here))):
            @pl.when(here)
            def _(own=own):
                gone = pay.at[pl.ds(0, (count - own) * 16)]
                pltpu.make_async_copy(gone, gone, rs_send.at[n]).wait()
                gone = table.at[pl.ds(0, own * (GRP - 1) * 16)]
                pltpu.make_async_copy(gone, gone, ag_send.at[n]).wait()

    to_owner(pay2, inbox2, P2, 1)

    def add_grads(q, fresh=False):
        da = dot(dbuf[q], w2t[...], TN)
        r = rbuf[q].astype(F32)
        ds = (da[:, :HID] + r).astype(BF)
        dn = ((da[:, HID:] - r) * wide(invc[q])).astype(BF)
        both = jnp.concatenate([dn, ds], axis=0)

        def rows512(i, c):
            part = dot(bsel[q, pl.ds(pl.multiple_of(i * 512, 512), 512), :], both)
            for h in range(2):
                rows = pl.ds(pl.multiple_of(h * FRONT + i * 512, 512), 512)
                now = part[:, h * 128:(h + 1) * 128]
                dh1[rows, :] = now if fresh else dh1[rows, :] + now
            return c

        lax.fori_loop(0, FRONT // 512, rows512, 0)

    for c in range(2):
        a1t[c * 128:(c + 1) * 128, :] = a1[c * FRONT:(c + 1) * FRONT, :].T
    db2 = jnp.sum(dlog.astype(F32), axis=1, keepdims=True)
    db2 = jnp.broadcast_to(db2, (CLS_PAD, 128)).T[0:1, :]
    swap_forward(rbuf, r_send, r_recv, SEED // 2)
    add_grads(y, True)
    swap_forward(dbuf, d_send, d_recv, 96)
    add_grads(left)
    add_grads(right)
    add_plane(pay2, inbox2, ybox2, P2, 1)
    swap_end(rbuf, r_send, r_recv, SEED // 2)
    swap_end(dbuf, d_send, d_recv, 96)
    add_group(ybox2, res2, P2, 1)
    add_grads(opp)

    def to_z(i, db):
        z = z1[pl.ds(pl.multiple_of(i * 128, 128), 128), :]
        sig = 1.0 / (1.0 + jnp.exp(-z))
        dh = jnp.concatenate(
            [dh1[pl.ds(pl.multiple_of(h * FRONT + i * 128, 128), 128), :] for h in range(2)], axis=1
        )
        dz = dh * sig * (1.0 + z * (1.0 - sig))
        low = dz.astype(BF)
        for h in range(2):
            a1[pl.ds(pl.multiple_of((2 + h) * FRONT + i * 128, 128), 128), :] = low[:, h * 128:(h + 1) * 128]
        return db + jnp.sum(low.astype(F32), axis=0, keepdims=True)

    db1 = lax.fori_loop(0, FRONT // 128, to_z, jnp.zeros((1, HID), F32))
    dz = jnp.concatenate([a1[2 * FRONT:3 * FRONT, :], a1[3 * FRONT:4 * FRONT, :]], axis=1)
    g1 = dot(a1t[...], dz).astype(BF)
    pay1[0:256, :] = g1[:, :128]
    pay1[256:512, :] = g1[:, 128:]
    misc[...] = jnp.zeros((16, 128), F32)

    def two(rows, v):
        hi = v.astype(BF).astype(F32)
        misc[rows:rows + 1, 0:v.shape[1]] = hi
        misc[rows + 4:rows + 5, 0:v.shape[1]] = v - hi

    two(0, db1[:, :128])
    two(1, db1[:, 128:])
    two(2, db2[:, :128])
    two(3, db2[:, 128:])
    hi = loss.astype(BF).astype(F32)
    misc[8:9, 0:1] = hi
    misc[9:10, 0:1] = loss - hi
    pay1[512:528, :] = misc[...].astype(BF)
    to_owner(pay1, inbox1, P1, 0)

    take(res2, P2, 1)
    mom2 = jnp.concatenate(
        [MU * gm2t[q] + res2[q * CLS_PAD:(q + 1) * CLS_PAD, :] for q in range(NAR)], axis=1
    )
    for q in range(NAR):
        x2s[q] = mom2[:, q * 128:(q + 1) * 128]
    o_all[ROW_M2:ROW_M2 + CLS_PAD, :] = x2s[y]
    x2 = mom2 * (1.0 / (jnp.sqrt(jnp.sum(mom2 * mom2, keepdims=True)) + 1e-07))
    x2 = ns_step(x2)
    add_plane(pay1, inbox1, ybox1, P1, 0)
    x2 = ns_step(x2)
    add_group(ybox1, o_all, P1, 0)
    for _ in range(NS_ITERS - 2):
        x2 = ns_step(x2)
    for q in range(NAR):
        x2s[q] = x2[:, q * 128:(q + 1) * 128]
    o_all[ROW_X2:ROW_X2 + CLS_PAD, :] = x2s[y]
    take(o_all, P1, 0)

    for b in range(8):
        blk = gbuf.at[y, b * 256:(b + 1) * 256, :]
        link(blk, blk, h_send.at[0, b], h_recv.at[0, b], right).wait_send()
        link(blk, blk, h_send.at[1, b], h_recv.at[1, b], left).wait_send()
        blk = gbuf.at[opp, b * 256:(b + 1) * 256, :]
        link(blk, blk, h_send.at[2, b], h_recv.at[2, b], right).wait_send()
    swap_sent(rbuf, r_send, r_recv, SEED // 2)
    swap_sent(dbuf, d_send, d_recv, 96)

    sums_sent(pay2, P2, 1)
    sums_sent(pay1, P1, 0)


def main(reqt, feat, idx1t, msk1t, idx2t, msk2t, labels, live, w1, w2own, m1, m2own, bias):
    vm = pl.BlockSpec(memory_space=pltpu.VMEM)
    dma = pltpu.SemaphoreType.DMA
    sds = jax.ShapeDtypeStruct
    V = pltpu.VMEM
    return pl.pallas_call(
        main_kernel,
        out_shape=sds((ROWS, 128), F32),
        in_specs=[vm, pl.BlockSpec(memory_space=pl.ANY)] + [vm] * 11,
        out_specs=vm,
        scratch_shapes=[
            V((SRC + 8, D_IN), F32),
            V((OWN, D_IN), BF),
            V((SRC, D_IN), BF),
            V((CAP, D_IN), F32),
            V((DEV, 128), jnp.int32),
            V((DEV, 128), jnp.int32),
            V((16, FRONT), jnp.int32),
            V((1, FRONT), F32),
            V((256, D_IN), F32),
            V((256, D_IN), F32),
            V((FRONT, HID), F32),
            V((2 * D_IN, FRONT), BF),
            V((NAR, FRONT, HID), BF),
            V((NAR, 2 * SEED, FRONT), BF),
            V((NAR, FRONT, 2 * SEED), BF),
            V((NAR, 4, 1 + F2, 16, 128), jnp.int16),
            V((SEED, 16), jnp.int32),
            V((NAR, SEED, 128), F32),
            V((SEED, 128), F32),
            V((NAR, SEED, HID), BF),
            V((NAR, CLS_PAD, SEED), BF),
            V((NAR, 64, HID), BF),
            V((NAR, CLS_PAD, 128), BF),
            V((NAR, 64, HID), F32),
            V((NAR, CLS_PAD, 128), F32),
            V((NAR, 16, SEED), jnp.int32),
            V((CLS_PAD, 2 * HID), BF),
            V((HID, 128), F32),
            V((P1 * 16, 128), BF),
            V((P2 * 16, 128), BF),
            V((16, 128), F32),
            V((2, GRP, 16, 128), BF),
            V((2, GRP, 16, 128), BF),
            V((2, NAR, 16, 128), F32),
            V((2, NAR, 16, 128), F32),
            V((P2 * 16, 128), F32),
            V((NAR, CLS_PAD, 128), F32),
            pltpu.SMEM((DEV, 1, 128), jnp.int32),
            pltpu.SMEM((16, FRONT), jnp.int32),
            pltpu.SMEM((1, FRONT), F32),
            dma, dma((2,)), dma((GRP,)), dma, dma((GRP,)), dma, dma, dma((5, 3)), dma((5, 3)),
            dma((3, 8)), dma((3, 8)), dma((4,)), dma((4,)), dma((4,)), dma((4,)),
            dma((2,)), dma((2, 2)), dma((2, 2, 3)), dma((2, 2, 3)), dma((2,)), dma((2,)),
        ],
        compiler_params=pltpu.CompilerParams(
            has_side_effects=True, vmem_limit_bytes=62 * 2**20
        ),
    )(reqt, feat, idx1t, msk1t, idx2t, msk2t, labels, live, w1, w2own, m1, m2own, bias)


def update_kernel(
    res, w1own, w2own, bias, biasm, biasv,
    o_loss, o_first, o_second, o_mom1, o_mom2, o_flow, o_slow, o_bias, o_bm, o_bv,
    x1s,
):
    y = lax.axis_index("nar")
    mom1 = jnp.concatenate(
        [res[i * 256:i * 256 + 256, :] + res[ROW_G1 + i * 256:ROW_G1 + i * 256 + 256, :] for i in range(2)], axis=1
    )
    x1s[...] = mom1
    block64 = pl.ds(pl.multiple_of(y * 64, 64), 64)
    o_mom1[...] = x1s[block64, :]
    x1 = mom1 * (1.0 / (jnp.sqrt(jnp.sum(mom1 * mom1, keepdims=True)) + 1e-07))
    for _ in range(NS_ITERS):
        x1 = ns_step(x1)
    x1s[...] = x1
    first_new = w1own[...] * (1.0 - WDECAY) - x1s[block64, :]
    o_first[...] = first_new
    o_flow[...] = first_new.astype(BF)
    second = w2own[...] * (1.0 - WDECAY) - (2 * HID / CLS) ** 0.5 * res[ROW_X2:ROW_X2 + CLS, :]
    o_second[...] = second
    o_slow[...] = second.astype(BF)
    o_mom2[...] = res[ROW_M2:ROW_M2 + CLS, :]

    gb = res[512:516, :] + res[516:520, :]
    gb = jnp.concatenate([gb[0:1, :], gb[1:2, :], gb[2:3, :], gb[3:4, 0:44]], axis=1)
    m_new = BETA_ONE * biasm[...] + (1.0 - BETA_ONE) * gb
    v_new = BETA_TWO * biasv[...] + (1.0 - BETA_TWO) * gb * gb
    m_hat = m_new / (1.0 - BETA_ONE**STEP)
    v_hat = v_new / (1.0 - BETA_TWO**STEP)
    o_bias[...] = bias[...] * (1.0 - LR_BIAS * WDECAY) - LR_BIAS * m_hat / (jnp.sqrt(v_hat) + EPSILON)
    o_bm[...] = m_new
    o_bv[...] = v_new
    o_loss[...] = res[520:521, 0:1] + res[521:522, 0:1]


def update(*args):
    vm = pl.BlockSpec(memory_space=pltpu.VMEM)
    sds = jax.ShapeDtypeStruct
    return pl.pallas_call(
        update_kernel,
        out_shape=[
            sds((1, 1), F32), sds((64, HID), F32), sds((CLS, 128), F32), sds((64, HID), F32), sds((CLS, 128), F32),
            sds((64, HID), BF), sds((CLS, 128), BF), sds((1, 428), F32), sds((1, 428), F32), sds((1, 428), F32),
        ],
        in_specs=[vm] * 6,
        out_specs=[vm] * 10,
        scratch_shapes=[pltpu.VMEM((2 * D_IN, HID), F32)],
        compiler_params=pltpu.CompilerParams(vmem_limit_bytes=32 * 2**20),
    )(*args)


def per_device(
    features, requests, index_one, mask_one, index_two, mask_two, labels, seed_live,
    w_first, w_second, mom_first, mom_second, biases, bias_m, bias_v,
):
    w2own, bias = w_second.T, biases[None, :]
    res = main(
        requests.T, features, index_one.T, mask_one.T, index_two.T, mask_two.T, labels[None, :], seed_live[None, :],
        w_first, w2own, mom_first, mom_second.T, bias,
    )
    loss, first_new, second_new, mom_one, mom_two, first_low, second_low, bias_new, m_new, v_new = update(
        res, w_first, w2own, bias, bias_m[None, :], bias_v[None, :]
    )
    return (
        loss.reshape(()), first_new, second_new.T, mom_one, mom_two.T, first_low, second_low.T,
        bias_new.reshape(-1), m_new.reshape(-1), v_new.reshape(-1),
    )


def solution(mesh):
    both = ("grp", "nar")
    placed = (
        P(both, None), P(both, None), P(both, None), P(both, None), P(both, None), P(both, None),
        P(both), P(both), P("nar", None), P("nar", None), P("nar", None), P("nar", None), P(), P(), P(),
    )
    nar = P("nar", None)
    return jax.shard_map(
        per_device, mesh=mesh, in_specs=placed,
        out_specs=(P(), nar, nar, nar, nar, nar, nar, P(), P(), P()), check_vma=False,
    )
```

```python
import functools

import jax
import jax.numpy as jnp
from jax import lax
from jax.experimental import pallas as pl
from jax.experimental.pallas import tpu as pltpu
from jax.sharding import PartitionSpec as P

HID = 256
CLS = 172
CLS_PAD = 176
D_IN = 128
F1 = 15
F2 = 10
NS_ITERS = 5
STEP = 10
LAM = 0.5
MU = 0.95
WDECAY = 0.01
LR_BIAS = 0.05
BETA_ONE = 0.9
BETA_TWO = 0.999
EPSILON = 1e-08
NS_A = 3.4445
NS_B = -4.775
NS_C = 2.0315
HIGH = lax.Precision.HIGHEST
MESH = pl.DeviceIdType.MESH
BF = jnp.bfloat16
F32 = jnp.float32

DEV = 128
NAR = 4
OWN = 8192
CAP = 64
SRC = 8192
FRONT = 2048
SEED = 512


def all_to(t):
    return (t // NAR, t % NAR)


PIECE = 32
P1 = 17
Q2 = 192
P2 = 24
GRP = 32
ROW_M2 = P1 * PIECE
ROW_X2 = ROW_M2 + CLS_PAD
ROWS = ROW_X2 + CLS_PAD
SEEDS_ALL = SEED * DEV


def dot(a, b, dims=((1,), (0,))):
    return lax.dot_general(a, b, (dims, ((), ())), preferred_element_type=F32)


NN = ((1,), (0,))
NT = ((1,), (1,))
TN = ((0,), (0,))


def split(a):
    hi = a.astype(BF)
    return hi, (a - hi.astype(F32)).astype(BF)


def dot3(a, b, dims):
    (ah, al), (bh, bl) = a, b
    return dot(ah, bh, dims) + (dot(ah, bl, dims) + dot(al, bh, dims))


def ns_step(x):
    xs = split(x)
    gram = dot3(xs, xs, NT)
    gs = split(gram)
    mix = NS_B * gram + NS_C * dot3(gs, gs, NN)
    return NS_A * x + dot3(split(mix), xs, NN)


def spread(row):
    return jnp.broadcast_to(row, (128, 128)).T


def main_kernel(
    reqt, feat, idx1t, msk1t, idx2t, msk2t, labels, live, w1, w2own, m1, m2own, bias,
    o_all,
    table, featb, pulled, stage, reqv, reqin, mid, idxv, invv, near, own, z1, a1t, gbuf, fsel, bsel, wants, idc, invc, livec, rbuf, dbuf,
    gw1, gw2t, m2pad, gidx2, w2t, b2c, pay1, pay2, misc, inbox1, inbox2, ybox1, ybox2, res2, x2s,
    reqs, idx, inv,
    feat_sem, loc_sem, ask_sem, req_send, mid_recv, req_recv, row_send, row_recv, nar_send, nar_recv,
    h_send, h_recv, r_send, r_recv, d_send, d_recv, rs_send, rs_recv, y_send, y_recv, ag_send, ag_recv,
):
    a1, dh1 = pulled, table
    g = lax.axis_index("grp")
    y = lax.axis_index("nar")
    me = g * NAR + y
    left, right, opp = (y + 3) % NAR, (y + 1) % NAR, (y + 2) % NAR

    load = pltpu.make_async_copy(feat, featb, feat_sem)
    load.start()

    barrier = pltpu.get_barrier_semaphore()

    ys = [(y + d) % NAR for d in range(NAR)]

    def greet(i, c):
        t = (g + i) % GRP
        for d in range(NAR):
            pl.semaphore_signal(barrier, inc=1, device_id=(t, ys[d]), device_id_type=MESH)
        return c

    for d in range(1, NAR):
        pl.semaphore_signal(barrier, inc=1, device_id=(g, ys[d]), device_id_type=MESH)
    lax.fori_loop(1, GRP, greet, 0)

    def link(src, dst, ssem, rsem, to):
        return pltpu.make_async_remote_copy(
            src_ref=src, dst_ref=dst, send_sem=ssem, recv_sem=rsem, device_id=(g, to), device_id_type=MESH
        )

    reqv[...] = jnp.concatenate([reqt[...], jnp.zeros((DEV - CAP, DEV), jnp.int32)], axis=0).T
    ask_rows = reqv.reshape(GRP, NAR, 1, 128)
    got_rows = reqin.reshape(DEV, 1, 128)

    gw1[y] = w1[...].astype(BF)
    pad = CLS_PAD - CLS
    gw2t[y] = jnp.concatenate([w2own[...], jnp.zeros((pad, 128), F32)], axis=0).astype(BF)
    m2pad[...] = jnp.concatenate([m2own[...], jnp.zeros((Q2 - CLS, 128), F32)], axis=0)
    gidx2[y] = jnp.concatenate(
        [idx2t[0:1, :], jnp.where(msk2t[...] > 0, idx2t[1:, :], -1), jnp.zeros((5, SEED), jnp.int32)], axis=0
    )
    shared = (gidx2, gw1, gw2t)

    pl.semaphore_wait(barrier, DEV - 1)

    def ask_group(d):
        return pltpu.make_async_remote_copy(
            src_ref=ask_rows.at[:, ys[d]], dst_ref=mid.at[y], send_sem=req_send.at[d], recv_sem=mid_recv.at[d],
            device_id=(g, ys[d]), device_id_type=MESH,
        )

    for d in range(1, NAR):
        ask_group(d).start()
    keep = pltpu.make_async_copy(ask_rows.at[:, y], mid.at[y], loc_sem.at[2])
    keep.start()
    for n, a in enumerate(shared):
        for d in range(1, NAR):
            link(a.at[y], a.at[y], nar_send.at[n, d - 1], nar_recv.at[n, d - 1], (y + d) % NAR).start()

    msk = msk1t[...]
    idxv[0:1, :] = idx1t[0:1, :]
    idxv[1:16, :] = jnp.where(msk > 0, idx1t[1:16, :], SRC)
    invv[...] = 1.0 / jnp.maximum(jnp.sum(msk.astype(F32), axis=0, keepdims=True), 1.0)
    to_smem = [pltpu.make_async_copy(idxv, idx, loc_sem.at[0]), pltpu.make_async_copy(invv, inv, loc_sem.at[1])]
    for c in to_smem:
        c.start()

    keep.wait()
    for d in range(1, NAR):
        ask_group(d).wait()
    own_rows = pl.ds(pl.multiple_of(g * NAR, NAR), NAR)

    def ask(i, c):
        n = (i * 13) % GRP
        t = (g + n) % GRP
        pltpu.make_async_remote_copy(
            src_ref=mid.at[:, t], dst_ref=got_rows.at[own_rows], send_sem=req_send.at[0], recv_sem=req_recv.at[n],
            device_id=(t, y), device_id_type=MESH,
        ).start()
        return c

    lax.fori_loop(1, GRP, ask, 0)
    keep = pltpu.make_async_copy(mid.at[:, g], got_rows.at[own_rows], loc_sem.at[2])
    keep.start()

    load.wait()

    def widen_features(i, c):
        rows = pl.ds(pl.multiple_of(i * 256, 256), 256)
        table[rows, :] = featb[rows, :].astype(F32)
        return c

    lax.fori_loop(0, OWN // 256, widen_features, 0)

    view = table.reshape(SRC + 8, 1, D_IN)
    my_rows = pl.ds(pl.multiple_of(me * CAP, CAP), CAP)

    def pick(t, u, slot):
        for r in range(CAP):
            stage[r:r + 1, :] = view[reqs[t * NAR + u, 0, r]]
        featb[slot, :] = stage[...].astype(BF)

    def serve_one(t, u, slot):
        pick(t, u, slot)
        pltpu.make_async_remote_copy(
            src_ref=featb.at[slot], dst_ref=pulled.at[my_rows],
            send_sem=row_send, recv_sem=row_recv, device_id=(t, u), device_id_type=MESH,
        ).start()

    def asked(n):
        rows = got_rows.at[pl.ds(0, NAR)]
        pltpu.make_async_copy(rows, rows, req_recv.at[n]).wait()

    def to_scalars(t, n):
        rows = pl.ds(pl.multiple_of(t * NAR, NAR), NAR)
        return pltpu.make_async_copy(got_rows.at[rows], reqs.at[rows], ask_sem.at[n])

    def whose(i):
        n = (i * 13) % GRP
        return n, (g + GRP - n) % GRP

    def fetch(i):
        n, t = whose(i)
        asked(n)
        to_scalars(t, n).start()

    def serve(i, c):
        n, t = whose(i)

        @pl.when(i < GRP - 1)
        def _():
            fetch(i + 1)

        to_scalars(t, n).wait()
        for d in range(NAR):
            serve_one(t, ys[d], pl.ds(pl.multiple_of((i * NAR + d) * CAP, CAP), CAP))
        return c

    fetch(1)
    lax.fori_loop(1, GRP, serve, 0)
    keep.wait()
    to_scalars(g, 0).start()
    to_scalars(g, 0).wait()
    for d in range(1, NAR):
        serve_one(g, ys[d], pl.ds(d * CAP, CAP))
    pick(g, y, pl.ds(0, CAP))
    pulled[my_rows, :] = featb[0:CAP, :]

    for n, a in enumerate(shared):
        for d in range(1, NAR):
            link(a.at[y], a.at[y], nar_send.at[n, d - 1], nar_recv.at[n, d - 1], (y + d) % NAR).wait()
    for q in range(NAR):
        w2t[:, q * 128:(q + 1) * 128] = gw2t[q]
    last = jnp.concatenate([bias[0:1, 384:428], jnp.zeros((1, 84), F32)], axis=1)
    b2c[...] = jnp.concatenate([spread(bias[0:1, 256:384]), spread(last)], axis=0)

    def column(row):
        return jnp.concatenate([spread(row[:, c * 128:(c + 1) * 128]) for c in range(SEED // 128)], axis=0)

    for q in range(NAR):
        n = jnp.sum((gidx2[q, 1:1 + F2, :] >= 0).astype(F32), axis=0, keepdims=True)
        invc[q] = column(1.0 / jnp.maximum(n, 1.0))
    livec[...] = column(2.0 * LAM / HID / SEEDS_ALL * live[...].astype(F32))

    lane16 = lax.broadcasted_iota(jnp.int32, (16, 128), 1).astype(jnp.int16)
    iota16 = lax.broadcasted_iota(jnp.int32, (16, 128), 0).astype(jnp.int16)
    one, zero = jnp.ones((16, 128), BF), jnp.zeros((16, 128), BF)

    def marks(here, want):
        acc = jnp.where(here == want[1], one, zero)
        for k in range(2, 1 + F2):
            acc = acc + jnp.where(here == want[k], one, zero)
        return acc, jnp.where(here == want[0], one, zero)

    idc[...] = gidx2[y].T

    def forward_marks(i, carry):
        at = pl.multiple_of(i * 16, 16)
        blk = idc[pl.ds(at, 16), :]
        want = [jnp.broadcast_to(blk[:, k:k + 1], (16, 128)).astype(jnp.int16) for k in range(1 + F2)]
        for q in range(NAR):
            for c in range(FRONT // 128):
                here = lane16 + jnp.full((16, 128), q * FRONT + c * 128, jnp.int32).astype(jnp.int16)
                a, b = marks(here, want)
                fsel[q, pl.ds(at, 16), c * 128:(c + 1) * 128] = a
                fsel[q, pl.ds(SEED + at, 16), c * 128:(c + 1) * 128] = b
        return carry

    lax.fori_loop(0, SEED // 16, forward_marks, 0)

    for q in range(NAR):
        ids = gidx2[q] - y * FRONT
        for c in range(SEED // 128):
            for k in range(1 + F2):
                row = ids[k:k + 1, c * 128:(c + 1) * 128]
                wants[q, c, k] = jnp.broadcast_to(row, (16, 128)).astype(jnp.int16)

    def backward_marks(i):
        here = iota16 + jnp.full((16, 128), i * 16, jnp.int32).astype(jnp.int16)
        out = pl.ds(pl.multiple_of(i * 16, 16), 16)
        for q in range(NAR):
            for c in range(SEED // 128):
                a, b = marks(here, [wants[q, c, k] for k in range(1 + F2)])
                bsel[q, out, c * 128:(c + 1) * 128] = a
                bsel[q, out, SEED + c * 128:SEED + (c + 1) * 128] = b

    come = pulled.at[pl.ds(0, (DEV - 1) * CAP)]
    pltpu.make_async_copy(come, come, row_recv).wait()
    gone = featb.at[pl.ds(CAP, (DEV - 1) * CAP)]
    pltpu.make_async_copy(gone, gone, row_send).wait()
    sent = mid.at[:, pl.ds(0, GRP - 1)]
    pltpu.make_async_copy(sent, sent, req_send.at[0]).wait()

    def widen(i, c):
        rows = pl.ds(pl.multiple_of(i * 256, 256), 256)
        table[rows, :] = pulled[rows, :].astype(F32)
        return c

    lax.fori_loop(0, SRC // 256, widen, 0)
    table[SRC:SRC + 8, :] = jnp.zeros((8, D_IN), F32)
    for c in to_smem:
        c.wait()

    def cols(b):
        return pl.ds(pl.multiple_of(b * 256, 256), 256)

    def forward(b):
        @pl.when(b % 2 == 0)
        def _():
            blk = gbuf.at[left, cols(b), :]
            link(blk, blk, h_send.at[0, b], h_recv.at[0, b], right).wait_recv()
            link(blk, blk, h_send.at[2, b], h_recv.at[2, b], right).start()

        @pl.when(b % 2 == 1)
        def _():
            blk = gbuf.at[right, cols(b), :]
            link(blk, blk, h_send.at[1, b], h_recv.at[1, b], left).wait_recv()
            link(blk, blk, h_send.at[2, b], h_recv.at[2, b], left).start()

    def block(b, c):
        def some(i, c2):
            backward_marks(b * 16 + i)
            base = pl.multiple_of(b * 256 + i * 16, 16)
            for j in range(16):
                m = base + j
                here = pl.ds(pl.multiple_of(i * 16, 16) + j, 1)
                own[here, :] = view[idx[0, m]]
                rows = [view[idx[1 + k, m]] for k in range(F1)]
                while len(rows) > 1:
                    rows = [p + q for p, q in zip(rows[::2], rows[1::2])] + ([rows[-1]] if len(rows) % 2 else [])
                near[here, :] = rows[0] * inv[0, m]
            return c2

        lax.fori_loop(0, 16, some, 0)
        rows = cols(b)
        act = jnp.concatenate([own[...].astype(BF), near[...].astype(BF)], axis=1)
        a1[rows, :] = act[:, :128]
        a1[pl.ds(pl.multiple_of(FRONT + b * 256, 256), 256), :] = act[:, 128:]
        z = dot(act, gw1[...].reshape(2 * D_IN, HID)) + bias[0:1, 0:HID]
        z1[rows, :] = z
        gbuf[y, rows, :] = (z / (1.0 + jnp.exp(-z))).astype(BF)
        blk = gbuf.at[y, rows, :]
        link(blk, blk, h_send.at[0, b], h_recv.at[0, b], right).start()
        link(blk, blk, h_send.at[1, b], h_recv.at[1, b], left).start()

        @pl.when(b > 0)
        def _():
            forward(b - 1)

        return c

    lax.fori_loop(0, 8, block, 0)
    forward(7)

    def from_source(q):
        return dot(fsel[q], gbuf[q])

    total = from_source(y)
    for b in range(1, 8, 2):
        blk = gbuf.at[left, b * 256:(b + 1) * 256, :]
        link(blk, blk, h_send.at[0, b], h_recv.at[0, b], right).wait_recv()
    total = total + from_source(left)
    for b in range(0, 8, 2):
        blk = gbuf.at[right, b * 256:(b + 1) * 256, :]
        link(blk, blk, h_send.at[1, b], h_recv.at[1, b], left).wait_recv()
    total = total + from_source(right)
    for b in range(8):
        blk = gbuf.at[opp, b * 256:(b + 1) * 256, :]
        link(blk, blk, h_send.at[2, b], h_recv.at[2, b], right).wait_recv()
    total = total + from_source(opp)

    def wide(a):
        return jnp.concatenate([a, a], axis=1)

    near2 = (total[:SEED, :] * wide(invc[y])).astype(BF)
    self2 = total[SEED:, :].astype(BF)
    alive = live[...].astype(F32)
    diff = self2.astype(F32) - near2.astype(F32)
    pull_apart = wide(livec[...]) * diff

    def swap_start(buf, ssem, rsem):
        blk = buf.at[y]
        link(blk, blk, ssem.at[0], rsem.at[0], right).start()
        link(blk, blk, ssem.at[1], rsem.at[1], left).start()

    def swap_forward(buf, ssem, rsem, cut):
        blk = buf.at[left]
        link(blk, blk, ssem.at[0], rsem.at[0], right).wait_recv()
        half = buf.at[left, 0:cut, :]
        link(half, half, ssem.at[2], rsem.at[2], right).start()
        blk = buf.at[right]
        link(blk, blk, ssem.at[1], rsem.at[1], left).wait_recv()
        half = buf.at[right, cut:, :]
        link(half, half, ssem.at[3], rsem.at[3], left).start()

    def swap_end(buf, ssem, rsem, cut):
        half = buf.at[opp, 0:cut, :]
        link(half, half, ssem.at[2], rsem.at[2], right).wait_recv()
        half = buf.at[opp, cut:, :]
        link(half, half, ssem.at[3], rsem.at[3], left).wait_recv()

    def swap_sent(buf, ssem, rsem, cut):
        blk = buf.at[y]
        link(blk, blk, ssem.at[0], rsem.at[0], right).wait_send()
        link(blk, blk, ssem.at[1], rsem.at[1], left).wait_send()
        half = buf.at[left, 0:cut, :]
        link(half, half, ssem.at[2], rsem.at[2], right).wait_send()
        half = buf.at[right, cut:, :]
        link(half, half, ssem.at[3], rsem.at[3], left).wait_send()

    rbuf[y] = pull_apart.astype(BF)
    swap_start(rbuf, r_send, r_recv)

    act2 = jnp.concatenate([self2, near2], axis=1)
    cls = lax.broadcasted_iota(jnp.int32, (CLS_PAD, SEED), 0)
    b2 = b2c[0:CLS_PAD, :]
    logits = dot(w2t[...], act2, NT) + jnp.concatenate([b2] * 4, axis=1)
    logits = jnp.where(cls < CLS, logits, -1e30)
    top = jnp.max(logits, axis=0, keepdims=True)
    e = jnp.exp(logits - top)
    tot = jnp.sum(e, axis=0, keepdims=True)
    hot = cls == labels[...]
    picked = jnp.sum(jnp.where(hot, logits, 0.0), axis=0, keepdims=True)
    dlog = (alive * (e * (1.0 / tot) - jnp.where(hot, 1.0, 0.0)) * (1.0 / SEEDS_ALL)).astype(BF)
    dbuf[y] = dlog
    swap_start(dbuf, d_send, d_recv)

    loss = jnp.sum(alive * (top + jnp.log(tot) - picked), axis=1, keepdims=True)
    loss = loss + SEEDS_ALL / 2 * jnp.sum(pull_apart * diff, keepdims=True)
    g2t = dot(dlog, act2).astype(BF)
    for q in range(NAR):
        pay2[q * Q2:q * Q2 + CLS_PAD, :] = g2t[:, q * 128:(q + 1) * 128]
        pay2[q * Q2 + CLS_PAD:(q + 1) * Q2, :] = jnp.zeros((Q2 - CLS_PAD, 128), BF)

    def to_owner(pay, inbox, first, count, n):
        def body(i, c):
            t = (g + i) % GRP
            p = t - first

            @pl.when((p >= 0) & (p < count))
            def _():
                pltpu.make_async_remote_copy(
                    src_ref=pay.at[pl.ds(pl.multiple_of(p * PIECE, PIECE), PIECE)], dst_ref=inbox.at[g],
                    send_sem=rs_send.at[n], recv_sem=rs_recv.at[n], device_id=(t, y), device_id_type=MESH,
                ).start()

            return c

        lax.fori_loop(1, GRP, body, 0)

    def mine(first, count):
        p = g - first
        return (p >= 0) & (p < count), pl.ds(pl.multiple_of(p * PIECE, PIECE), PIECE)

    def add_first_momentum(p):
        rows = pl.ds(pl.multiple_of(p % 2 * PIECE, PIECE), PIECE)
        for h in range(2):
            @pl.when((y == p % 8 // 2) & (p // 8 == h))
            def _(h=h):
                ybox1[y] = ybox1[y] + MU * m1[rows, h * 128:(h + 1) * 128]

    def add_second_momentum(p):
        @pl.when(y == p // (Q2 // PIECE))
        def _():
            rows = pl.ds(pl.multiple_of(p % (Q2 // PIECE) * PIECE, PIECE), PIECE)
            ybox2[y] = ybox2[y] + MU * m2pad[rows, :]

    def add_plane(pay, inbox, ybox, first, count, n, add_momentum):
        here, rows = mine(first, count)

        @pl.when(here)
        def _():
            got = inbox.at[pl.ds(0, GRP - 1)]
            pltpu.make_async_copy(got, got, rs_recv.at[n]).wait()
            inbox[g] = pay[rows, :]
            ybox[y] = jnp.sum(inbox[...].astype(F32), axis=0)
            add_momentum(g - first)
            for d in range(1, NAR):
                link(ybox.at[y], ybox.at[y], y_send.at[n, d - 1], y_recv.at[n, d - 1], ys[d]).start()

    def add_group(ybox, res, first, count, n):
        here, rows = mine(first, count)

        @pl.when(here)
        def _():
            for d in range(1, NAR):
                link(ybox.at[y], ybox.at[y], y_send.at[n, d - 1], y_recv.at[n, d - 1], ys[d]).wait()
            res[rows, :] = (ybox[0] + ybox[1]) + (ybox[2] + ybox[3])

            def tell(i, c):
                pltpu.make_async_remote_copy(
                    src_ref=res.at[rows], dst_ref=res.at[rows], send_sem=ag_send.at[n], recv_sem=ag_recv.at[n],
                    device_id=((g + i) % GRP, y), device_id_type=MESH,
                ).start()
                return c

            lax.fori_loop(1, GRP, tell, 0)

    def take(res, first, count, n):
        here, rows = mine(first, count)
        for less, when in ((1, here), (0, jnp.logical_not(here))):
            @pl.when(when)
            def _(less=less):
                got = res.at[pl.ds(0, (count - less) * PIECE)]
                pltpu.make_async_copy(got, got, ag_recv.at[n]).wait()

    def sums_sent(pay, first, count, n):
        here, rows = mine(first, count)
        for less, when in ((1, here), (0, jnp.logical_not(here))):
            @pl.when(when)
            def _(less=less):
                gone = pay.at[pl.ds(0, (count - less) * PIECE)]
                pltpu.make_async_copy(gone, gone, rs_send.at[n]).wait()

        @pl.when(here)
        def _():
            gone = table.at[pl.ds(0, (GRP - 1) * PIECE)]
            pltpu.make_async_copy(gone, gone, ag_send.at[n]).wait()

    to_owner(pay2, inbox2, GRP - P2, P2, 1)

    def add_grads(q, fresh=False):
        da = dot(dbuf[q], w2t[...], TN)
        r = rbuf[q].astype(F32)
        ds = (da[:, :HID] + r).astype(BF)
        dn = ((da[:, HID:] - r) * wide(invc[q])).astype(BF)
        both = jnp.concatenate([dn, ds], axis=0)

        def rows512(i, c):
            part = dot(bsel[q, pl.ds(pl.multiple_of(i * 512, 512), 512), :], both)
            for h in range(2):
                rows = pl.ds(pl.multiple_of(h * FRONT + i * 512, 512), 512)
                now = part[:, h * 128:(h + 1) * 128]
                dh1[rows, :] = now if fresh else dh1[rows, :] + now
            return c

        lax.fori_loop(0, FRONT // 512, rows512, 0)

    for c in range(2):
        a1t[c * 128:(c + 1) * 128, :] = a1[c * FRONT:(c + 1) * FRONT, :].T
    db2 = jnp.sum(dlog.astype(F32), axis=1, keepdims=True)
    db2 = jnp.broadcast_to(db2, (CLS_PAD, 128)).T[0:1, :]
    swap_forward(rbuf, r_send, r_recv, SEED // 2)
    add_grads(y, True)
    swap_forward(dbuf, d_send, d_recv, 96)
    add_grads(left)
    add_grads(right)
    add_plane(pay2, inbox2, ybox2, GRP - P2, P2, 1, add_second_momentum)
    swap_end(rbuf, r_send, r_recv, SEED // 2)
    swap_end(dbuf, d_send, d_recv, 96)
    add_group(ybox2, res2, GRP - P2, P2, 1)
    add_grads(opp)

    def to_z(i, db):
        z = z1[pl.ds(pl.multiple_of(i * 128, 128), 128), :]
        sig = 1.0 / (1.0 + jnp.exp(-z))
        dh = jnp.concatenate(
            [dh1[pl.ds(pl.multiple_of(h * FRONT + i * 128, 128), 128), :] for h in range(2)], axis=1
        )
        dz = dh * sig * (1.0 + z * (1.0 - sig))
        low = dz.astype(BF)
        for h in range(2):
            a1[pl.ds(pl.multiple_of((2 + h) * FRONT + i * 128, 128), 128), :] = low[:, h * 128:(h + 1) * 128]
        return db + jnp.sum(low.astype(F32), axis=0, keepdims=True)

    db1 = lax.fori_loop(0, FRONT // 128, to_z, jnp.zeros((1, HID), F32))
    dz = jnp.concatenate([a1[2 * FRONT:3 * FRONT, :], a1[3 * FRONT:4 * FRONT, :]], axis=1)
    g1 = dot(a1t[...], dz).astype(BF)
    pay1[0:256, :] = g1[:, :128]
    pay1[256:512, :] = g1[:, 128:]
    misc[...] = jnp.zeros((PIECE, 128), F32)

    def two(rows, v):
        hi = v.astype(BF).astype(F32)
        misc[rows:rows + 1, 0:v.shape[1]] = hi
        misc[rows + 4:rows + 5, 0:v.shape[1]] = v - hi

    two(0, db1[:, :128])
    two(1, db1[:, 128:])
    two(2, db2[:, :128])
    two(3, db2[:, 128:])
    hi = loss.astype(BF).astype(F32)
    misc[8:9, 0:1] = hi
    misc[9:10, 0:1] = loss - hi
    pay1[512:544, :] = misc[...].astype(BF)
    to_owner(pay1, inbox1, 0, P1, 0)

    take(res2, GRP - P2, P2, 1)
    mom2 = jnp.concatenate([res2[q * Q2:q * Q2 + CLS_PAD, :] for q in range(NAR)], axis=1)
    for q in range(NAR):
        x2s[q] = mom2[:, q * 128:(q + 1) * 128]
    o_all[ROW_M2:ROW_M2 + CLS_PAD, :] = x2s[y]
    x2 = mom2 * (1.0 / (jnp.sqrt(jnp.sum(mom2 * mom2, keepdims=True)) + 1e-07))
    x2 = ns_step(x2)
    add_plane(pay1, inbox1, ybox1, 0, P1, 0, add_first_momentum)
    x2 = ns_step(x2)
    add_group(ybox1, o_all, 0, P1, 0)
    for _ in range(NS_ITERS - 2):
        x2 = ns_step(x2)
    for q in range(NAR):
        x2s[q] = x2[:, q * 128:(q + 1) * 128]
    o_all[ROW_X2:ROW_X2 + CLS_PAD, :] = x2s[y]
    take(o_all, 0, P1, 0)

    for b in range(8):
        blk = gbuf.at[y, b * 256:(b + 1) * 256, :]
        link(blk, blk, h_send.at[0, b], h_recv.at[0, b], right).wait_send()
        link(blk, blk, h_send.at[1, b], h_recv.at[1, b], left).wait_send()
        blk = gbuf.at[opp, b * 256:(b + 1) * 256, :]
        link(blk, blk, h_send.at[2, b], h_recv.at[2, b], right).wait_send()
    swap_sent(rbuf, r_send, r_recv, SEED // 2)
    swap_sent(dbuf, d_send, d_recv, 96)

    sums_sent(pay2, GRP - P2, P2, 1)
    sums_sent(pay1, 0, P1, 0)


def main(reqt, feat, idx1t, msk1t, idx2t, msk2t, labels, live, w1, w2own, m1, m2own, bias):
    vm = pl.BlockSpec(memory_space=pltpu.VMEM)
    dma = pltpu.SemaphoreType.DMA
    sds = jax.ShapeDtypeStruct
    V = pltpu.VMEM
    return pl.pallas_call(
        main_kernel,
        out_shape=sds((ROWS, 128), F32),
        in_specs=[vm, pl.BlockSpec(memory_space=pl.ANY)] + [vm] * 11,
        out_specs=vm,
        scratch_shapes=[
            V((SRC + 8, D_IN), F32),
            V((OWN, D_IN), BF),
            V((SRC, D_IN), BF),
            V((CAP, D_IN), F32),
            V((DEV, 128), jnp.int32),
            V((DEV, 128), jnp.int32),
            V((NAR, GRP, 1, 128), jnp.int32),
            V((16, FRONT), jnp.int32),
            V((1, FRONT), F32),
            V((256, D_IN), F32),
            V((256, D_IN), F32),
            V((FRONT, HID), F32),
            V((2 * D_IN, FRONT), BF),
            V((NAR, FRONT, HID), BF),
            V((NAR, 2 * SEED, FRONT), BF),
            V((NAR, FRONT, 2 * SEED), BF),
            V((NAR, 4, 1 + F2, 16, 128), jnp.int16),
            V((SEED, 16), jnp.int32),
            V((NAR, SEED, 128), F32),
            V((SEED, 128), F32),
            V((NAR, SEED, HID), BF),
            V((NAR, CLS_PAD, SEED), BF),
            V((NAR, 64, HID), BF),
            V((NAR, CLS_PAD, 128), BF),
            V((Q2, 128), F32),
            V((NAR, 16, SEED), jnp.int32),
            V((CLS_PAD, 2 * HID), BF),
            V((HID, 128), F32),
            V((P1 * PIECE, 128), BF),
            V((P2 * PIECE, 128), BF),
            V((PIECE, 128), F32),
            V((GRP, PIECE, 128), BF),
            V((GRP, PIECE, 128), BF),
            V((NAR, PIECE, 128), F32),
            V((NAR, PIECE, 128), F32),
            V((P2 * PIECE, 128), F32),
            V((NAR, CLS_PAD, 128), F32),
            pltpu.SMEM((DEV, 1, 128), jnp.int32),
            pltpu.SMEM((16, FRONT), jnp.int32),
            pltpu.SMEM((1, FRONT), F32),
            dma, dma((3,)), dma((GRP,)), dma((NAR,)), dma((NAR,)), dma((GRP,)), dma, dma, dma((3, 3)), dma((3, 3)),
            dma((3, 8)), dma((3, 8)), dma((4,)), dma((4,)), dma((4,)), dma((4,)),
            dma((2,)), dma((2,)), dma((2, 3)), dma((2, 3)), dma((2,)), dma((2,)),
        ],
        compiler_params=pltpu.CompilerParams(
            collective_id=0, has_side_effects=True, vmem_limit_bytes=62 * 2**20
        ),
    )(reqt, feat, idx1t, msk1t, idx2t, msk2t, labels, live, w1, w2own, m1, m2own, bias)


def update_kernel(
    res, w1own, w2own, bias, biasm, biasv,
    o_loss, o_first, o_second, o_mom1, o_mom2, o_flow, o_slow, o_bias, o_bm, o_bv,
    x1s,
):
    y = lax.axis_index("nar")
    mom1 = jnp.concatenate([res[0:256, :], res[256:512, :]], axis=1)
    x1s[...] = mom1
    block64 = pl.ds(pl.multiple_of(y * 64, 64), 64)
    o_mom1[...] = x1s[block64, :]
    x1 = mom1 * (1.0 / (jnp.sqrt(jnp.sum(mom1 * mom1, keepdims=True)) + 1e-07))
    for _ in range(NS_ITERS):
        x1 = ns_step(x1)
    x1s[...] = x1
    first_new = w1own[...] * (1.0 - WDECAY) - x1s[block64, :]
    o_first[...] = first_new
    o_flow[...] = first_new.astype(BF)
    second = w2own[...] * (1.0 - WDECAY) - (2 * HID / CLS) ** 0.5 * res[ROW_X2:ROW_X2 + CLS, :]
    o_second[...] = second
    o_slow[...] = second.astype(BF)
    o_mom2[...] = res[ROW_M2:ROW_M2 + CLS, :]

    gb = res[512:516, :] + res[516:520, :]
    gb = jnp.concatenate([gb[0:1, :], gb[1:2, :], gb[2:3, :], gb[3:4, 0:44]], axis=1)
    m_new = BETA_ONE * biasm[...] + (1.0 - BETA_ONE) * gb
    v_new = BETA_TWO * biasv[...] + (1.0 - BETA_TWO) * gb * gb
    m_hat = m_new / (1.0 - BETA_ONE**STEP)
    v_hat = v_new / (1.0 - BETA_TWO**STEP)
    o_bias[...] = bias[...] * (1.0 - LR_BIAS * WDECAY) - LR_BIAS * m_hat / (jnp.sqrt(v_hat) + EPSILON)
    o_bm[...] = m_new
    o_bv[...] = v_new
    o_loss[...] = res[520:521, 0:1] + res[521:522, 0:1]


def update(*args):
    vm = pl.BlockSpec(memory_space=pltpu.VMEM)
    sds = jax.ShapeDtypeStruct
    return pl.pallas_call(
        update_kernel,
        out_shape=[
            sds((1, 1), F32), sds((64, HID), F32), sds((CLS, 128), F32), sds((64, HID), F32), sds((CLS, 128), F32),
            sds((64, HID), BF), sds((CLS, 128), BF), sds((1, 428), F32), sds((1, 428), F32), sds((1, 428), F32),
        ],
        in_specs=[vm] * 6,
        out_specs=[vm] * 10,
        scratch_shapes=[pltpu.VMEM((2 * D_IN, HID), F32)],
        compiler_params=pltpu.CompilerParams(vmem_limit_bytes=32 * 2**20),
    )(*args)


def per_device(
    features, requests, index_one, mask_one, index_two, mask_two, labels, seed_live,
    w_first, w_second, mom_first, mom_second, biases, bias_m, bias_v,
):
    w2own, bias = w_second.T, biases[None, :]
    res = main(
        requests.T, features, index_one.T, mask_one.T, index_two.T, mask_two.T, labels[None, :], seed_live[None, :],
        w_first, w2own, mom_first, mom_second.T, bias,
    )
    loss, first_new, second_new, mom_one, mom_two, first_low, second_low, bias_new, m_new, v_new = update(
        res, w_first, w2own, bias, bias_m[None, :], bias_v[None, :]
    )
    return (
        loss.reshape(()), first_new, second_new.T, mom_one, mom_two.T, first_low, second_low.T,
        bias_new.reshape(-1), m_new.reshape(-1), v_new.reshape(-1),
    )


def solution(mesh):
    both = ("grp", "nar")
    placed = (
        P(both, None), P(both, None), P(both, None), P(both, None), P(both, None), P(both, None),
        P(both), P(both), P("nar", None), P("nar", None), P("nar", None), P("nar", None), P(), P(), P(),
    )
    nar = P("nar", None)
    return jax.shard_map(
        per_device, mesh=mesh, in_specs=placed,
        out_specs=(P(), nar, nar, nar, nar, nar, nar, P(), P(), P()), check_vma=False,
    )
```

```python
import functools

import jax
import jax.numpy as jnp
from jax import lax
from jax.experimental import pallas as pl
from jax.experimental.pallas import tpu as pltpu
from jax.sharding import PartitionSpec as P

HID = 256
CLS = 172
CLS_PAD = 176
D_IN = 128
F1 = 15
F2 = 10
NS_ITERS = 5
STEP = 10
LAM = 0.5
MU = 0.95
WDECAY = 0.01
LR_BIAS = 0.05
BETA_ONE = 0.9
BETA_TWO = 0.999
EPSILON = 1e-08
NS_A = 3.4445
NS_B = -4.775
NS_C = 2.0315
HIGH = lax.Precision.HIGHEST
MESH = pl.DeviceIdType.MESH
BF = jnp.bfloat16
F32 = jnp.float32

DEV = 128
NAR = 4
OWN = 8192
CAP = 64
SRC = 8192
FRONT = 2048
SEED = 512


def all_to(t):
    return (t // NAR, t % NAR)


PIECE = 32
P1 = 17
Q2 = 192
P2 = 24
GRP = 32
ROW_M2 = P1 * PIECE
ROW_X2 = ROW_M2 + CLS_PAD
ROWS = ROW_X2 + CLS_PAD
SEEDS_ALL = SEED * DEV


def dot(a, b, dims=((1,), (0,))):
    return lax.dot_general(a, b, (dims, ((), ())), preferred_element_type=F32)


NN = ((1,), (0,))
NT = ((1,), (1,))
TN = ((0,), (0,))


def split(a):
    hi = a.astype(BF)
    return hi, (a - hi.astype(F32)).astype(BF)


def dot3(a, b, dims):
    (ah, al), (bh, bl) = a, b
    return dot(ah, bh, dims) + (dot(ah, bl, dims) + dot(al, bh, dims))


def ns_step(x):
    xs = split(x)
    gram = dot3(xs, xs, NT)
    gs = split(gram)
    mix = NS_B * gram + NS_C * dot3(gs, gs, NN)
    return NS_A * x + dot3(split(mix), xs, NN)


def spread(row):
    return jnp.broadcast_to(row, (128, 128)).T


def main_kernel(
    reqt, feat, idx1t, msk1t, idx2t, msk2t, labels, live, w1, w2own, m1, m2own, bias,
    o_all,
    table, featb, pulled, stage, reqv, reqin, mid, idxv, invv, near, own, z1, a1t, gbuf, fsel, bsel, wants, idc, invc, livec, rbuf, dbuf,
    gw1, gw2t, m2pad, gidx2, w2t, b2c, pay1, pay2, misc, inbox1, inbox2, ybox1, ybox2, res2, x2s,
    reqs, idx, inv,
    feat_sem, loc_sem, ask_sem, req_send, mid_recv, req_recv, row_send, row_recv, nar_send, nar_recv,
    h_send, h_recv, r_send, r_recv, d_send, d_recv, rs_send, rs_recv, y_send, y_recv, ag_send, ag_recv,
):
    dzs, dh1 = pulled, table
    g = lax.axis_index("grp")
    y = lax.axis_index("nar")
    me = g * NAR + y
    left, right, opp = (y + 3) % NAR, (y + 1) % NAR, (y + 2) % NAR

    load = pltpu.make_async_copy(feat, featb, feat_sem)
    load.start()

    barrier = pltpu.get_barrier_semaphore()

    ys = [(y + d) % NAR for d in range(NAR)]

    def greet(i, c):
        pl.semaphore_signal(barrier, inc=1, device_id=((g + i) % GRP, y), device_id_type=MESH)
        return c

    for d in range(1, NAR):
        pl.semaphore_signal(barrier, inc=1, device_id=(g, ys[d]), device_id_type=MESH)
    lax.fori_loop(1, GRP, greet, 0)

    def link(src, dst, ssem, rsem, to):
        return pltpu.make_async_remote_copy(
            src_ref=src, dst_ref=dst, send_sem=ssem, recv_sem=rsem, device_id=(g, to), device_id_type=MESH
        )

    reqv[...] = jnp.concatenate([reqt[...], jnp.zeros((DEV - CAP, DEV), jnp.int32)], axis=0).T
    ask_rows = reqv.reshape(GRP, NAR, 1, 128)
    got_rows = reqin.reshape(DEV, 1, 128)

    gw1[y] = w1[...].astype(BF)
    pad = CLS_PAD - CLS
    gw2t[y] = jnp.concatenate([w2own[...], jnp.zeros((pad, 128), F32)], axis=0).astype(BF)
    m2pad[...] = jnp.concatenate([m2own[...], jnp.zeros((Q2 - CLS, 128), F32)], axis=0)
    gidx2[y] = jnp.concatenate(
        [idx2t[0:1, :], jnp.where(msk2t[...] > 0, idx2t[1:, :], -1), jnp.zeros((5, SEED), jnp.int32)], axis=0
    )
    shared = (gidx2, gw1, gw2t)

    pl.semaphore_wait(barrier, GRP + NAR - 2)

    def ask_group(d):
        return pltpu.make_async_remote_copy(
            src_ref=ask_rows.at[:, ys[d]], dst_ref=mid.at[y], send_sem=req_send.at[d], recv_sem=mid_recv.at[d],
            device_id=(g, ys[d]), device_id_type=MESH,
        )

    for d in range(1, NAR):
        ask_group(d).start()
    keep = pltpu.make_async_copy(ask_rows.at[:, y], mid.at[y], loc_sem.at[2])
    keep.start()
    for n, a in enumerate(shared):
        for d in range(1, NAR):
            link(a.at[y], a.at[y], nar_send.at[n, d - 1], nar_recv.at[n, d - 1], (y + d) % NAR).start()

    msk = msk1t[...]
    idxv[0:1, :] = idx1t[0:1, :]
    idxv[1:16, :] = jnp.where(msk > 0, idx1t[1:16, :], SRC)
    invv[...] = 1.0 / jnp.maximum(jnp.sum(msk.astype(F32), axis=0, keepdims=True), 1.0)
    to_smem = [pltpu.make_async_copy(idxv, idx, loc_sem.at[0]), pltpu.make_async_copy(invv, inv, loc_sem.at[1])]
    for c in to_smem:
        c.start()

    keep.wait()
    for d in range(1, NAR):
        ask_group(d).wait()
    own_rows = pl.ds(pl.multiple_of(g * NAR, NAR), NAR)

    def ask(i, c):
        n = (i * 13) % GRP
        t = (g + n) % GRP
        pltpu.make_async_remote_copy(
            src_ref=mid.at[:, t], dst_ref=got_rows.at[own_rows], send_sem=req_send.at[0], recv_sem=req_recv.at[n],
            device_id=(t, y), device_id_type=MESH,
        ).start()
        return c

    lax.fori_loop(1, GRP, ask, 0)
    keep = pltpu.make_async_copy(mid.at[:, g], got_rows.at[own_rows], loc_sem.at[2])
    keep.start()

    load.wait()

    def widen_features(i, c):
        rows = pl.ds(pl.multiple_of(i * 256, 256), 256)
        table[rows, :] = featb[rows, :].astype(F32)
        return c

    lax.fori_loop(0, OWN // 256, widen_features, 0)

    lane16 = lax.broadcasted_iota(jnp.int32, (16, 128), 1).astype(jnp.int16)
    iota16 = lax.broadcasted_iota(jnp.int32, (16, 128), 0).astype(jnp.int16)
    one, zero = jnp.ones((16, 128), BF), jnp.zeros((16, 128), BF)

    def marks(here, want):
        acc = jnp.where(here == want[1], one, zero)
        for k in range(2, 1 + F2):
            acc = acc + jnp.where(here == want[k], one, zero)
        return acc, jnp.where(here == want[0], one, zero)

    idc[...] = gidx2[y].T

    def seeds16(i):
        at = pl.multiple_of(i * 16, 16)
        blk = idc[pl.ds(at, 16), :]
        return at, [jnp.broadcast_to(blk[:, k:k + 1], (16, 128)).astype(jnp.int16) for k in range(1 + F2)]

    def forward_marks(at, want, q):
        for c in range(FRONT // 128):
            here = lane16 + jnp.full((16, 128), q * FRONT + c * 128, jnp.int32).astype(jnp.int16)
            a, b = marks(here, want)
            fsel[q, pl.ds(at, 16), c * 128:(c + 1) * 128] = a
            fsel[q, pl.ds(SEED + at, 16), c * 128:(c + 1) * 128] = b

    view = table.reshape(SRC + 8, 1, D_IN)
    my_rows = pl.ds(pl.multiple_of(me * CAP, CAP), CAP)

    def pick(t, u, slot):
        for r in range(CAP):
            stage[r:r + 1, :] = view[reqs[t * NAR + u, 0, r]]
        featb[slot, :] = stage[...].astype(BF)

    def serve_one(t, u, slot):
        pick(t, u, slot)
        pltpu.make_async_remote_copy(
            src_ref=featb.at[slot], dst_ref=pulled.at[my_rows],
            send_sem=row_send, recv_sem=row_recv, device_id=(t, u), device_id_type=MESH,
        ).start()

    def asked(n):
        rows = got_rows.at[pl.ds(0, NAR)]
        pltpu.make_async_copy(rows, rows, req_recv.at[n]).wait()

    def to_scalars(t, n):
        rows = pl.ds(pl.multiple_of(t * NAR, NAR), NAR)
        return pltpu.make_async_copy(got_rows.at[rows], reqs.at[rows], ask_sem.at[n])

    def whose(i):
        n = (i * 13) % GRP
        return n, (g + GRP - n) % GRP

    def fetch(i):
        n, t = whose(i)
        asked(n)
        to_scalars(t, n).start()

    def serve(i, c):
        n, t = whose(i)

        @pl.when(i < GRP - 1)
        def _():
            fetch(i + 1)

        to_scalars(t, n).wait()
        at, want = seeds16(i)
        for d in range(NAR):
            forward_marks(at, want, d)
            serve_one(t, ys[d], pl.ds(pl.multiple_of((i * NAR + d) * CAP, CAP), CAP))
        return c

    fetch(1)
    lax.fori_loop(1, GRP, serve, 0)
    keep.wait()
    to_scalars(g, 0).start()
    to_scalars(g, 0).wait()
    at, want = seeds16(0)
    for d in range(NAR):
        forward_marks(at, want, d)
    for d in range(1, NAR):
        serve_one(g, ys[d], pl.ds(d * CAP, CAP))
    pick(g, y, pl.ds(0, CAP))
    pulled[my_rows, :] = featb[0:CAP, :]

    for n, a in enumerate(shared):
        for d in range(1, NAR):
            link(a.at[y], a.at[y], nar_send.at[n, d - 1], nar_recv.at[n, d - 1], (y + d) % NAR).wait()
    for q in range(NAR):
        w2t[:, q * 128:(q + 1) * 128] = gw2t[q]
    last = jnp.concatenate([bias[0:1, 384:428], jnp.zeros((1, 84), F32)], axis=1)
    b2c[...] = jnp.concatenate([spread(bias[0:1, 256:384]), spread(last)], axis=0)

    def column(row):
        return jnp.concatenate([spread(row[:, c * 128:(c + 1) * 128]) for c in range(SEED // 128)], axis=0)

    for q in range(NAR):
        n = jnp.sum((gidx2[q, 1:1 + F2, :] >= 0).astype(F32), axis=0, keepdims=True)
        invc[q] = column(1.0 / jnp.maximum(n, 1.0))
    livec[...] = column(2.0 * LAM / HID / SEEDS_ALL * live[...].astype(F32))

    for q in range(NAR):
        ids = gidx2[q] - y * FRONT
        for c in range(SEED // 128):
            for k in range(1 + F2):
                row = ids[k:k + 1, c * 128:(c + 1) * 128]
                wants[q, c, k] = jnp.broadcast_to(row, (16, 128)).astype(jnp.int16)

    def backward_marks(i):
        here = iota16 + jnp.full((16, 128), i * 16, jnp.int32).astype(jnp.int16)
        out = pl.ds(pl.multiple_of(i * 16, 16), 16)
        for q in range(NAR):
            for c in range(SEED // 128):
                a, b = marks(here, [wants[q, c, k] for k in range(1 + F2)])
                bsel[q, out, c * 128:(c + 1) * 128] = a
                bsel[q, out, SEED + c * 128:SEED + (c + 1) * 128] = b

    come = pulled.at[pl.ds(0, (DEV - 1) * CAP)]
    pltpu.make_async_copy(come, come, row_recv).wait()
    gone = featb.at[pl.ds(CAP, (DEV - 1) * CAP)]
    pltpu.make_async_copy(gone, gone, row_send).wait()
    sent = mid.at[:, pl.ds(0, GRP - 1)]
    pltpu.make_async_copy(sent, sent, req_send.at[0]).wait()

    def widen(i, c):
        rows = pl.ds(pl.multiple_of(i * 256, 256), 256)
        table[rows, :] = pulled[rows, :].astype(F32)
        return c

    lax.fori_loop(0, SRC // 256, widen, 0)
    table[SRC:SRC + 8, :] = jnp.zeros((8, D_IN), F32)
    for c in to_smem:
        c.wait()

    def cols(b):
        return pl.ds(pl.multiple_of(b * 256, 256), 256)

    def forward(b):
        @pl.when(b % 2 == 0)
        def _():
            blk = gbuf.at[left, cols(b), :]
            link(blk, blk, h_send.at[0, b], h_recv.at[0, b], right).wait_recv()
            link(blk, blk, h_send.at[2, b], h_recv.at[2, b], right).start()

        @pl.when(b % 2 == 1)
        def _():
            blk = gbuf.at[right, cols(b), :]
            link(blk, blk, h_send.at[1, b], h_recv.at[1, b], left).wait_recv()
            link(blk, blk, h_send.at[2, b], h_recv.at[2, b], left).start()

    def block(b, c):
        def some(i, c2):
            backward_marks(b * 16 + i)
            base = pl.multiple_of(b * 256 + i * 16, 16)
            for j in range(16):
                m = base + j
                here = pl.ds(pl.multiple_of(i * 16, 16) + j, 1)
                own[here, :] = view[idx[0, m]]
                rows = [view[idx[1 + k, m]] for k in range(F1)]
                while len(rows) > 1:
                    rows = [p + q for p, q in zip(rows[::2], rows[1::2])] + ([rows[-1]] if len(rows) % 2 else [])
                near[here, :] = rows[0] * inv[0, m]
            return c2

        lax.fori_loop(0, 16, some, 0)
        rows = cols(b)
        act = jnp.concatenate([own[...].astype(BF), near[...].astype(BF)], axis=1)
        a1t[:, rows] = act.T
        z = dot(act, gw1[...].reshape(2 * D_IN, HID)) + bias[0:1, 0:HID]
        z1[rows, :] = z
        gbuf[y, rows, :] = (z / (1.0 + jnp.exp(-z))).astype(BF)
        blk = gbuf.at[y, rows, :]
        link(blk, blk, h_send.at[0, b], h_recv.at[0, b], right).start()
        link(blk, blk, h_send.at[1, b], h_recv.at[1, b], left).start()

        @pl.when(b > 0)
        def _():
            forward(b - 1)

        return c

    lax.fori_loop(0, 8, block, 0)
    forward(7)

    def from_source(q):
        return dot(fsel[q], gbuf[q])

    total = from_source(y)
    for b in range(1, 8, 2):
        blk = gbuf.at[left, b * 256:(b + 1) * 256, :]
        link(blk, blk, h_send.at[0, b], h_recv.at[0, b], right).wait_recv()
    total = total + from_source(left)
    for b in range(0, 8, 2):
        blk = gbuf.at[right, b * 256:(b + 1) * 256, :]
        link(blk, blk, h_send.at[1, b], h_recv.at[1, b], left).wait_recv()
    total = total + from_source(right)
    for b in range(8):
        blk = gbuf.at[opp, b * 256:(b + 1) * 256, :]
        link(blk, blk, h_send.at[2, b], h_recv.at[2, b], right).wait_recv()
    total = total + from_source(opp)

    def wide(a):
        return jnp.concatenate([a, a], axis=1)

    near2 = (total[:SEED, :] * wide(invc[y])).astype(BF)
    self2 = total[SEED:, :].astype(BF)
    alive = live[...].astype(F32)
    diff = self2.astype(F32) - near2.astype(F32)
    pull_apart = wide(livec[...]) * diff

    def swap_start(buf, ssem, rsem):
        blk = buf.at[y]
        link(blk, blk, ssem.at[0], rsem.at[0], right).start()
        link(blk, blk, ssem.at[1], rsem.at[1], left).start()

    def swap_forward(buf, ssem, rsem, cut):
        blk = buf.at[left]
        link(blk, blk, ssem.at[0], rsem.at[0], right).wait_recv()
        half = buf.at[left, 0:cut, :]
        link(half, half, ssem.at[2], rsem.at[2], right).start()
        blk = buf.at[right]
        link(blk, blk, ssem.at[1], rsem.at[1], left).wait_recv()
        half = buf.at[right, cut:, :]
        link(half, half, ssem.at[3], rsem.at[3], left).start()

    def swap_end(buf, ssem, rsem, cut):
        half = buf.at[opp, 0:cut, :]
        link(half, half, ssem.at[2], rsem.at[2], right).wait_recv()
        half = buf.at[opp, cut:, :]
        link(half, half, ssem.at[3], rsem.at[3], left).wait_recv()

    def swap_sent(buf, ssem, rsem, cut):
        blk = buf.at[y]
        link(blk, blk, ssem.at[0], rsem.at[0], right).wait_send()
        link(blk, blk, ssem.at[1], rsem.at[1], left).wait_send()
        half = buf.at[left, 0:cut, :]
        link(half, half, ssem.at[2], rsem.at[2], right).wait_send()
        half = buf.at[right, cut:, :]
        link(half, half, ssem.at[3], rsem.at[3], left).wait_send()

    rbuf[y] = pull_apart.astype(BF)
    swap_start(rbuf, r_send, r_recv)

    act2 = jnp.concatenate([self2, near2], axis=1)
    cls = lax.broadcasted_iota(jnp.int32, (CLS_PAD, SEED), 0)
    b2 = b2c[0:CLS_PAD, :]
    logits = dot(w2t[...], act2, NT) + jnp.concatenate([b2] * 4, axis=1)
    logits = jnp.where(cls < CLS, logits, -1e30)
    top = jnp.max(logits, axis=0, keepdims=True)
    e = jnp.exp(logits - top)
    tot = jnp.sum(e, axis=0, keepdims=True)
    hot = cls == labels[...]
    picked = jnp.sum(jnp.where(hot, logits, 0.0), axis=0, keepdims=True)
    dlog = (alive * (e * (1.0 / tot) - jnp.where(hot, 1.0, 0.0)) * (1.0 / SEEDS_ALL)).astype(BF)
    dbuf[y] = dlog
    swap_start(dbuf, d_send, d_recv)

    loss = jnp.sum(alive * (top + jnp.log(tot) - picked), axis=1, keepdims=True)
    loss = loss + SEEDS_ALL / 2 * jnp.sum(pull_apart * diff, keepdims=True)
    g2t = dot(dlog, act2).astype(BF)
    for q in range(NAR):
        pay2[q * Q2:q * Q2 + CLS_PAD, :] = g2t[:, q * 128:(q + 1) * 128]
        pay2[q * Q2 + CLS_PAD:(q + 1) * Q2, :] = jnp.zeros((Q2 - CLS_PAD, 128), BF)

    def to_owner(pay, inbox, first, count, n):
        def body(i, c):
            t = (g + i) % GRP
            p = t - first

            @pl.when((p >= 0) & (p < count))
            def _():
                pltpu.make_async_remote_copy(
                    src_ref=pay.at[pl.ds(pl.multiple_of(p * PIECE, PIECE), PIECE)], dst_ref=inbox.at[g],
                    send_sem=rs_send.at[n], recv_sem=rs_recv.at[n], device_id=(t, y), device_id_type=MESH,
                ).start()

            return c

        lax.fori_loop(1, GRP, body, 0)

    def mine(first, count):
        p = g - first
        return (p >= 0) & (p < count), pl.ds(pl.multiple_of(p * PIECE, PIECE), PIECE)

    def add_first_momentum(p):
        rows = pl.ds(pl.multiple_of(p % 2 * PIECE, PIECE), PIECE)
        for h in range(2):
            @pl.when((y == p % 8 // 2) & (p // 8 == h))
            def _(h=h):
                ybox1[y] = ybox1[y] + MU * m1[rows, h * 128:(h + 1) * 128]

    def add_second_momentum(p):
        @pl.when(y == p // (Q2 // PIECE))
        def _():
            rows = pl.ds(pl.multiple_of(p % (Q2 // PIECE) * PIECE, PIECE), PIECE)
            ybox2[y] = ybox2[y] + MU * m2pad[rows, :]

    def add_plane(pay, inbox, ybox, first, count, n, add_momentum):
        here, rows = mine(first, count)

        @pl.when(here)
        def _():
            got = inbox.at[pl.ds(0, GRP - 1)]
            pltpu.make_async_copy(got, got, rs_recv.at[n]).wait()
            inbox[g] = pay[rows, :]
            ybox[y] = jnp.sum(inbox[...].astype(F32), axis=0)
            add_momentum(g - first)
            for d in range(1, NAR):
                link(ybox.at[y], ybox.at[y], y_send.at[n, d - 1], y_recv.at[n, d - 1], ys[d]).start()

    def add_group(ybox, res, first, count, n):
        here, rows = mine(first, count)

        @pl.when(here)
        def _():
            for d in range(1, NAR):
                link(ybox.at[y], ybox.at[y], y_send.at[n, d - 1], y_recv.at[n, d - 1], ys[d]).wait()
            res[rows, :] = (ybox[0] + ybox[1]) + (ybox[2] + ybox[3])

            def tell(i, c):
                pltpu.make_async_remote_copy(
                    src_ref=res.at[rows], dst_ref=res.at[rows], send_sem=ag_send.at[n], recv_sem=ag_recv.at[n],
                    device_id=((g + i) % GRP, y), device_id_type=MESH,
                ).start()
                return c

            lax.fori_loop(1, GRP, tell, 0)

    def take(res, first, count, n):
        here, rows = mine(first, count)
        for less, when in ((1, here), (0, jnp.logical_not(here))):
            @pl.when(when)
            def _(less=less):
                got = res.at[pl.ds(0, (count - less) * PIECE)]
                pltpu.make_async_copy(got, got, ag_recv.at[n]).wait()

    def sums_sent(pay, first, count, n):
        here, rows = mine(first, count)
        for less, when in ((1, here), (0, jnp.logical_not(here))):
            @pl.when(when)
            def _(less=less):
                gone = pay.at[pl.ds(0, (count - less) * PIECE)]
                pltpu.make_async_copy(gone, gone, rs_send.at[n]).wait()

        @pl.when(here)
        def _():
            gone = table.at[pl.ds(0, (GRP - 1) * PIECE)]
            pltpu.make_async_copy(gone, gone, ag_send.at[n]).wait()

    to_owner(pay2, inbox2, GRP - P2, P2, 1)

    def add_grads(q, fresh=False):
        da = dot(dbuf[q], w2t[...], TN)
        r = rbuf[q].astype(F32)
        ds = (da[:, :HID] + r).astype(BF)
        dn = ((da[:, HID:] - r) * wide(invc[q])).astype(BF)
        both = jnp.concatenate([dn, ds], axis=0)

        def rows512(i, c):
            part = dot(bsel[q, pl.ds(pl.multiple_of(i * 512, 512), 512), :], both)
            for h in range(2):
                rows = pl.ds(pl.multiple_of(h * FRONT + i * 512, 512), 512)
                now = part[:, h * 128:(h + 1) * 128]
                dh1[rows, :] = now if fresh else dh1[rows, :] + now
            return c

        lax.fori_loop(0, FRONT // 512, rows512, 0)

    db2 = jnp.sum(dlog.astype(F32), axis=1, keepdims=True)
    db2 = jnp.broadcast_to(db2, (CLS_PAD, 128)).T[0:1, :]
    swap_forward(rbuf, r_send, r_recv, SEED // 2)
    add_grads(y, True)
    swap_forward(dbuf, d_send, d_recv, 96)
    add_grads(left)
    add_grads(right)
    add_plane(pay2, inbox2, ybox2, GRP - P2, P2, 1, add_second_momentum)
    swap_end(rbuf, r_send, r_recv, SEED // 2)
    swap_end(dbuf, d_send, d_recv, 96)
    add_group(ybox2, res2, GRP - P2, P2, 1)
    add_grads(opp)

    def to_z(i, db):
        z = z1[pl.ds(pl.multiple_of(i * 128, 128), 128), :]
        sig = 1.0 / (1.0 + jnp.exp(-z))
        dh = jnp.concatenate(
            [dh1[pl.ds(pl.multiple_of(h * FRONT + i * 128, 128), 128), :] for h in range(2)], axis=1
        )
        dz = dh * sig * (1.0 + z * (1.0 - sig))
        low = dz.astype(BF)
        for h in range(2):
            dzs[pl.ds(pl.multiple_of(h * FRONT + i * 128, 128), 128), :] = low[:, h * 128:(h + 1) * 128]
        return db + jnp.sum(low.astype(F32), axis=0, keepdims=True)

    db1 = lax.fori_loop(0, FRONT // 128, to_z, jnp.zeros((1, HID), F32))
    dz = jnp.concatenate([dzs[0:FRONT, :], dzs[FRONT:2 * FRONT, :]], axis=1)
    g1 = dot(a1t[...], dz).astype(BF)
    pay1[0:256, :] = g1[:, :128]
    pay1[256:512, :] = g1[:, 128:]
    misc[...] = jnp.zeros((PIECE, 128), F32)

    def two(rows, v):
        hi = v.astype(BF).astype(F32)
        misc[rows:rows + 1, 0:v.shape[1]] = hi
        misc[rows + 4:rows + 5, 0:v.shape[1]] = v - hi

    two(0, db1[:, :128])
    two(1, db1[:, 128:])
    two(2, db2[:, :128])
    two(3, db2[:, 128:])
    hi = loss.astype(BF).astype(F32)
    misc[8:9, 0:1] = hi
    misc[9:10, 0:1] = loss - hi
    pay1[512:544, :] = misc[...].astype(BF)
    to_owner(pay1, inbox1, 0, P1, 0)

    take(res2, GRP - P2, P2, 1)
    mom2 = jnp.concatenate([res2[q * Q2:q * Q2 + CLS_PAD, :] for q in range(NAR)], axis=1)
    for q in range(NAR):
        x2s[q] = mom2[:, q * 128:(q + 1) * 128]
    o_all[ROW_M2:ROW_M2 + CLS_PAD, :] = x2s[y]
    x2 = mom2 * (1.0 / (jnp.sqrt(jnp.sum(mom2 * mom2, keepdims=True)) + 1e-07))
    x2 = ns_step(x2)
    add_plane(pay1, inbox1, ybox1, 0, P1, 0, add_first_momentum)
    x2 = ns_step(x2)
    add_group(ybox1, o_all, 0, P1, 0)
    for _ in range(NS_ITERS - 2):
        x2 = ns_step(x2)
    for q in range(NAR):
        x2s[q] = x2[:, q * 128:(q + 1) * 128]
    o_all[ROW_X2:ROW_X2 + CLS_PAD, :] = x2s[y]
    take(o_all, 0, P1, 0)

    for b in range(8):
        blk = gbuf.at[y, b * 256:(b + 1) * 256, :]
        link(blk, blk, h_send.at[0, b], h_recv.at[0, b], right).wait_send()
        link(blk, blk, h_send.at[1, b], h_recv.at[1, b], left).wait_send()
        blk = gbuf.at[opp, b * 256:(b + 1) * 256, :]
        link(blk, blk, h_send.at[2, b], h_recv.at[2, b], right).wait_send()
    swap_sent(rbuf, r_send, r_recv, SEED // 2)
    swap_sent(dbuf, d_send, d_recv, 96)

    sums_sent(pay2, GRP - P2, P2, 1)
    sums_sent(pay1, 0, P1, 0)


def main(reqt, feat, idx1t, msk1t, idx2t, msk2t, labels, live, w1, w2own, m1, m2own, bias):
    vm = pl.BlockSpec(memory_space=pltpu.VMEM)
    dma = pltpu.SemaphoreType.DMA
    sds = jax.ShapeDtypeStruct
    V = pltpu.VMEM
    return pl.pallas_call(
        main_kernel,
        out_shape=sds((ROWS, 128), F32),
        in_specs=[vm, pl.BlockSpec(memory_space=pl.ANY)] + [vm] * 11,
        out_specs=vm,
        scratch_shapes=[
            V((SRC + 8, D_IN), F32),
            V((OWN, D_IN), BF),
            V((SRC, D_IN), BF),
            V((CAP, D_IN), F32),
            V((DEV, 128), jnp.int32),
            V((DEV, 128), jnp.int32),
            V((NAR, GRP, 1, 128), jnp.int32),
            V((16, FRONT), jnp.int32),
            V((1, FRONT), F32),
            V((256, D_IN), F32),
            V((256, D_IN), F32),
            V((FRONT, HID), F32),
            V((2 * D_IN, FRONT), BF),
            V((NAR, FRONT, HID), BF),
            V((NAR, 2 * SEED, FRONT), BF),
            V((NAR, FRONT, 2 * SEED), BF),
            V((NAR, 4, 1 + F2, 16, 128), jnp.int16),
            V((SEED, 16), jnp.int32),
            V((NAR, SEED, 128), F32),
            V((SEED, 128), F32),
            V((NAR, SEED, HID), BF),
            V((NAR, CLS_PAD, SEED), BF),
            V((NAR, 64, HID), BF),
            V((NAR, CLS_PAD, 128), BF),
            V((Q2, 128), F32),
            V((NAR, 16, SEED), jnp.int32),
            V((CLS_PAD, 2 * HID), BF),
            V((HID, 128), F32),
            V((P1 * PIECE, 128), BF),
            V((P2 * PIECE, 128), BF),
            V((PIECE, 128), F32),
            V((GRP, PIECE, 128), BF),
            V((GRP, PIECE, 128), BF),
            V((NAR, PIECE, 128), F32),
            V((NAR, PIECE, 128), F32),
            V((P2 * PIECE, 128), F32),
            V((NAR, CLS_PAD, 128), F32),
            pltpu.SMEM((DEV, 1, 128), jnp.int32),
            pltpu.SMEM((16, FRONT), jnp.int32),
            pltpu.SMEM((1, FRONT), F32),
            dma, dma((3,)), dma((GRP,)), dma((NAR,)), dma((NAR,)), dma((GRP,)), dma, dma, dma((3, 3)), dma((3, 3)),
            dma((3, 8)), dma((3, 8)), dma((4,)), dma((4,)), dma((4,)), dma((4,)),
            dma((2,)), dma((2,)), dma((2, 3)), dma((2, 3)), dma((2,)), dma((2,)),
        ],
        compiler_params=pltpu.CompilerParams(
            collective_id=0, has_side_effects=True, vmem_limit_bytes=62 * 2**20
        ),
    )(reqt, feat, idx1t, msk1t, idx2t, msk2t, labels, live, w1, w2own, m1, m2own, bias)


def update_kernel(
    res, w1own, w2own, bias, biasm, biasv,
    o_loss, o_first, o_second, o_mom1, o_mom2, o_flow, o_slow, o_bias, o_bm, o_bv,
    x1s,
):
    y = lax.axis_index("nar")
    mom1 = jnp.concatenate([res[0:256, :], res[256:512, :]], axis=1)
    x1s[...] = mom1
    block64 = pl.ds(pl.multiple_of(y * 64, 64), 64)
    o_mom1[...] = x1s[block64, :]
    x1 = mom1 * (1.0 / (jnp.sqrt(jnp.sum(mom1 * mom1, keepdims=True)) + 1e-07))
    for _ in range(NS_ITERS):
        x1 = ns_step(x1)
    x1s[...] = x1
    first_new = w1own[...] * (1.0 - WDECAY) - x1s[block64, :]
    o_first[...] = first_new
    o_flow[...] = first_new.astype(BF)
    second = w2own[...] * (1.0 - WDECAY) - (2 * HID / CLS) ** 0.5 * res[ROW_X2:ROW_X2 + CLS, :]
    o_second[...] = second
    o_slow[...] = second.astype(BF)
    o_mom2[...] = res[ROW_M2:ROW_M2 + CLS, :]

    gb = res[512:516, :] + res[516:520, :]
    gb = jnp.concatenate([gb[0:1, :], gb[1:2, :], gb[2:3, :], gb[3:4, 0:44]], axis=1)
    m_new = BETA_ONE * biasm[...] + (1.0 - BETA_ONE) * gb
    v_new = BETA_TWO * biasv[...] + (1.0 - BETA_TWO) * gb * gb
    m_hat = m_new / (1.0 - BETA_ONE**STEP)
    v_hat = v_new / (1.0 - BETA_TWO**STEP)
    o_bias[...] = bias[...] * (1.0 - LR_BIAS * WDECAY) - LR_BIAS * m_hat / (jnp.sqrt(v_hat) + EPSILON)
    o_bm[...] = m_new
    o_bv[...] = v_new
    o_loss[...] = res[520:521, 0:1] + res[521:522, 0:1]


def update(*args):
    vm = pl.BlockSpec(memory_space=pltpu.VMEM)
    sds = jax.ShapeDtypeStruct
    return pl.pallas_call(
        update_kernel,
        out_shape=[
            sds((1, 1), F32), sds((64, HID), F32), sds((CLS, 128), F32), sds((64, HID), F32), sds((CLS, 128), F32),
            sds((64, HID), BF), sds((CLS, 128), BF), sds((1, 428), F32), sds((1, 428), F32), sds((1, 428), F32),
        ],
        in_specs=[vm] * 6,
        out_specs=[vm] * 10,
        scratch_shapes=[pltpu.VMEM((2 * D_IN, HID), F32)],
        compiler_params=pltpu.CompilerParams(vmem_limit_bytes=32 * 2**20),
    )(*args)


def per_device(
    features, requests, index_one, mask_one, index_two, mask_two, labels, seed_live,
    w_first, w_second, mom_first, mom_second, biases, bias_m, bias_v,
):
    w2own, bias = w_second.T, biases[None, :]
    res = main(
        requests.T, features, index_one.T, mask_one.T, index_two.T, mask_two.T, labels[None, :], seed_live[None, :],
        w_first, w2own, mom_first, mom_second.T, bias,
    )
    loss, first_new, second_new, mom_one, mom_two, first_low, second_low, bias_new, m_new, v_new = update(
        res, w_first, w2own, bias, bias_m[None, :], bias_v[None, :]
    )
    return (
        loss.reshape(()), first_new, second_new.T, mom_one, mom_two.T, first_low, second_low.T,
        bias_new.reshape(-1), m_new.reshape(-1), v_new.reshape(-1),
    )


def solution(mesh):
    both = ("grp", "nar")
    placed = (
        P(both, None), P(both, None), P(both, None), P(both, None), P(both, None), P(both, None),
        P(both), P(both), P("nar", None), P("nar", None), P("nar", None), P("nar", None), P(), P(), P(),
    )
    nar = P("nar", None)
    return jax.shard_map(
        per_device, mesh=mesh, in_specs=placed,
        out_specs=(P(), nar, nar, nar, nar, nar, nar, P(), P(), P()), check_vma=False,
    )
```

```python
import functools

import jax
import jax.numpy as jnp
from jax import lax
from jax.experimental import pallas as pl
from jax.experimental.pallas import tpu as pltpu
from jax.sharding import PartitionSpec as P

HID = 256
CLS = 172
CLS_PAD = 176
D_IN = 128
F1 = 15
F2 = 10
NS_ITERS = 5
STEP = 10
LAM = 0.5
MU = 0.95
WDECAY = 0.01
LR_BIAS = 0.05
BETA_ONE = 0.9
BETA_TWO = 0.999
EPSILON = 1e-08
NS_A = 3.4445
NS_B = -4.775
NS_C = 2.0315
HIGH = lax.Precision.HIGHEST
MESH = pl.DeviceIdType.MESH
BF = jnp.bfloat16
F32 = jnp.float32

DEV = 128
NAR = 4
OWN = 8192
CAP = 64
SRC = 8192
FRONT = 2048
SEED = 512


def all_to(t):
    return (t // NAR, t % NAR)


PIECE = 32
P1 = 17
Q2 = 192
P2 = 24
GRP = 32
ROW_M2 = P1 * PIECE
ROW_X2 = ROW_M2 + CLS_PAD
ROWS = ROW_X2 + CLS_PAD
SEEDS_ALL = SEED * DEV


def dot(a, b, dims=((1,), (0,))):
    return lax.dot_general(a, b, (dims, ((), ())), preferred_element_type=F32)


NN = ((1,), (0,))
NT = ((1,), (1,))
TN = ((0,), (0,))


def split(a):
    hi = a.astype(BF)
    return hi, (a - hi.astype(F32)).astype(BF)


def dot3(a, b, dims):
    (ah, al), (bh, bl) = a, b
    return dot(ah, bh, dims) + (dot(ah, bl, dims) + dot(al, bh, dims))


def ns_step(x):
    xs = split(x)
    gram = dot3(xs, xs, NT)
    gs = split(gram)
    mix = NS_B * gram + NS_C * dot3(gs, gs, NN)
    return NS_A * x + dot3(split(mix), xs, NN)


def spread(row):
    return jnp.broadcast_to(row, (128, 128)).T


def main_kernel(
    reqt, feat, idx1t, msk1t, idx2t, msk2t, labels, live, w1, w2own, m1, m2own, bias,
    o_all,
    table, featb, pulled, stage, reqv, reqin, mid, idxv, invv, near, own, z1, gbuf, fsel, bsel, wants, idc, ssel, idm, invc, livec, rbuf, dbuf,
    gw1, gw2t, m2pad, gidx2, w2t, b2c, pay1, pay2, misc, inbox1, inbox2, ybox1, ybox2, res2, x2s,
    reqs, idx, inv,
    feat_sem, loc_sem, ask_sem, req_send, mid_recv, req_recv, row_send, row_recv, nar_send, nar_recv,
    h_send, h_recv, r_send, r_recv, d_send, d_recv, rs_send, rs_recv, y_send, y_recv, ag_send, ag_recv,
):
    a1t, dh1, tot, gsum = featb, table, table.at[2 * FRONT:3 * FRONT], table.at[3 * FRONT:3 * FRONT + 512]
    g = lax.axis_index("grp")
    y = lax.axis_index("nar")
    me = g * NAR + y
    left, right, opp = (y + 3) % NAR, (y + 1) % NAR, (y + 2) % NAR

    load = pltpu.make_async_copy(feat, featb, feat_sem)
    load.start()

    barrier = pltpu.get_barrier_semaphore()

    ys = [(y + d) % NAR for d in range(NAR)]

    def greet(i, c):
        pl.semaphore_signal(barrier, inc=1, device_id=((g + i) % GRP, y), device_id_type=MESH)
        return c

    for d in range(1, NAR):
        pl.semaphore_signal(barrier, inc=1, device_id=(g, ys[d]), device_id_type=MESH)
    lax.fori_loop(1, GRP, greet, 0)

    def link(src, dst, ssem, rsem, to):
        return pltpu.make_async_remote_copy(
            src_ref=src, dst_ref=dst, send_sem=ssem, recv_sem=rsem, device_id=(g, to), device_id_type=MESH
        )

    reqv[...] = jnp.concatenate([reqt[...], jnp.zeros((DEV - CAP, DEV), jnp.int32)], axis=0).T
    ask_rows = reqv.reshape(GRP, NAR, 1, 128)
    got_rows = reqin.reshape(DEV, 1, 128)

    gw1[y] = w1[...].astype(BF)
    pad = CLS_PAD - CLS
    gw2t[y] = jnp.concatenate([w2own[...], jnp.zeros((pad, 128), F32)], axis=0).astype(BF)
    m2pad[...] = jnp.concatenate([m2own[...], jnp.zeros((Q2 - CLS, 128), F32)], axis=0)
    gidx2[y] = jnp.concatenate(
        [idx2t[0:1, :], jnp.where(msk2t[...] > 0, idx2t[1:, :], -1), jnp.zeros((5, SEED), jnp.int32)], axis=0
    )
    shared = (gidx2, gw1, gw2t)

    pl.semaphore_wait(barrier, GRP + NAR - 2)

    def ask_group(d):
        return pltpu.make_async_remote_copy(
            src_ref=ask_rows.at[:, ys[d]], dst_ref=mid.at[y], send_sem=req_send.at[d], recv_sem=mid_recv.at[d],
            device_id=(g, ys[d]), device_id_type=MESH,
        )

    for d in range(1, NAR):
        ask_group(d).start()
    keep = pltpu.make_async_copy(ask_rows.at[:, y], mid.at[y], loc_sem.at[2])
    keep.start()
    for n, a in enumerate(shared):
        for d in range(1, NAR):
            link(a.at[y], a.at[y], nar_send.at[n, d - 1], nar_recv.at[n, d - 1], (y + d) % NAR).start()

    msk = msk1t[...]
    idxv[0:1, :] = idx1t[0:1, :]
    idxv[1:16, :] = jnp.where(msk > 0, idx1t[1:16, :], SRC)
    invv[...] = 1.0 / jnp.maximum(jnp.sum(msk.astype(F32), axis=0, keepdims=True), 1.0)
    to_smem = [pltpu.make_async_copy(idxv, idx, loc_sem.at[0]), pltpu.make_async_copy(invv, inv, loc_sem.at[1])]
    for c in to_smem:
        c.start()

    keep.wait()
    for d in range(1, NAR):
        ask_group(d).wait()
    own_rows = pl.ds(pl.multiple_of(g * NAR, NAR), NAR)

    def ask(i, c):
        n = (i * 13) % GRP
        t = (g + n) % GRP
        pltpu.make_async_remote_copy(
            src_ref=mid.at[:, t], dst_ref=got_rows.at[own_rows], send_sem=req_send.at[0], recv_sem=req_recv.at[n],
            device_id=(t, y), device_id_type=MESH,
        ).start()
        return c

    lax.fori_loop(1, GRP, ask, 0)
    keep = pltpu.make_async_copy(mid.at[:, g], got_rows.at[own_rows], loc_sem.at[2])
    keep.start()

    load.wait()

    def widen_features(i, c):
        rows = pl.ds(pl.multiple_of(i * 256, 256), 256)
        table[rows, :] = featb[rows, :].astype(F32)
        return c

    lax.fori_loop(0, OWN // 256, widen_features, 0)

    lane16 = lax.broadcasted_iota(jnp.int32, (16, 128), 1).astype(jnp.int16)
    iota16 = lax.broadcasted_iota(jnp.int32, (16, 128), 0).astype(jnp.int16)
    one, zero = jnp.ones((16, 128), BF), jnp.zeros((16, 128), BF)

    def marks(here, want):
        acc = jnp.where(here == want[1], one, zero)
        for k in range(2, 1 + F2):
            acc = acc + jnp.where(here == want[k], one, zero)
        return acc, jnp.where(here == want[0], one, zero)

    idc[...] = gidx2[y].T

    def seeds16(i):
        at = pl.multiple_of(i * 16, 16)
        blk = idc[pl.ds(at, 16), :]
        return at, [jnp.broadcast_to(blk[:, k:k + 1], (16, 128)).astype(jnp.int16) for k in range(1 + F2)]

    def forward_marks(at, want, q):
        for c in range(FRONT // 128):
            here = lane16 + jnp.full((16, 128), q * FRONT + c * 128, jnp.int32).astype(jnp.int16)
            a, b = marks(here, want)
            fsel[q, pl.ds(at, 16), c * 128:(c + 1) * 128] = a
            fsel[q, pl.ds(SEED + at, 16), c * 128:(c + 1) * 128] = b

    view = table.reshape(SRC + 8, 1, D_IN)
    my_rows = pl.ds(pl.multiple_of(me * CAP, CAP), CAP)

    def pick(t, u, slot):
        for r in range(CAP):
            stage[r:r + 1, :] = view[reqs[t * NAR + u, 0, r]]
        featb[slot, :] = stage[...].astype(BF)

    def serve_one(t, u, slot):
        pick(t, u, slot)
        pltpu.make_async_remote_copy(
            src_ref=featb.at[slot], dst_ref=pulled.at[my_rows],
            send_sem=row_send, recv_sem=row_recv, device_id=(t, u), device_id_type=MESH,
        ).start()

    def asked(n):
        rows = got_rows.at[pl.ds(0, NAR)]
        pltpu.make_async_copy(rows, rows, req_recv.at[n]).wait()

    def to_scalars(t, n):
        rows = pl.ds(pl.multiple_of(t * NAR, NAR), NAR)
        return pltpu.make_async_copy(got_rows.at[rows], reqs.at[rows], ask_sem.at[n])

    def whose(i):
        n = (i * 13) % GRP
        return n, (g + GRP - n) % GRP

    def fetch(i):
        n, t = whose(i)
        asked(n)
        to_scalars(t, n).start()

    def serve(i, c):
        n, t = whose(i)

        @pl.when(i < GRP - 1)
        def _():
            fetch(i + 1)

        to_scalars(t, n).wait()
        at, want = seeds16(i)
        for d in range(NAR):
            forward_marks(at, want, d)
            serve_one(t, ys[d], pl.ds(pl.multiple_of((i * NAR + d) * CAP, CAP), CAP))
        return c

    fetch(1)
    lax.fori_loop(1, GRP, serve, 0)
    keep.wait()
    to_scalars(g, 0).start()
    to_scalars(g, 0).wait()
    at, want = seeds16(0)
    for d in range(NAR):
        forward_marks(at, want, d)
    for d in range(1, NAR):
        serve_one(g, ys[d], pl.ds(d * CAP, CAP))
    pick(g, y, pl.ds(0, CAP))
    pulled[my_rows, :] = featb[0:CAP, :]

    for n, a in enumerate(shared):
        for d in range(1, NAR):
            link(a.at[y], a.at[y], nar_send.at[n, d - 1], nar_recv.at[n, d - 1], (y + d) % NAR).wait()
    for q in range(NAR):
        w2t[:, q * 128:(q + 1) * 128] = gw2t[q]
    last = jnp.concatenate([bias[0:1, 384:428], jnp.zeros((1, 84), F32)], axis=1)
    b2c[...] = jnp.concatenate([spread(bias[0:1, 256:384]), spread(last)], axis=0)

    def column(row):
        return jnp.concatenate([spread(row[:, c * 128:(c + 1) * 128]) for c in range(SEED // 128)], axis=0)

    for q in range(NAR):
        n = jnp.sum((gidx2[q, 1:1 + F2, :] >= 0).astype(F32), axis=0, keepdims=True)
        invc[q] = column(1.0 / jnp.maximum(n, 1.0))
    livec[...] = column(2.0 * LAM / HID / SEEDS_ALL * live[...].astype(F32))

    for q in range(NAR):
        ids = gidx2[q] - y * FRONT
        for c in range(SEED // 128):
            for k in range(1 + F2):
                row = ids[k:k + 1, c * 128:(c + 1) * 128]
                wants[q, c, k] = jnp.broadcast_to(row, (16, 128)).astype(jnp.int16)

    def backward_marks(i):
        here = iota16 + jnp.full((16, 128), i * 16, jnp.int32).astype(jnp.int16)
        out = pl.ds(pl.multiple_of(i * 16, 16), 16)
        for q in range(NAR):
            for c in range(SEED // 128):
                a, b = marks(here, [wants[q, c, k] for k in range(1 + F2)])
                bsel[q, out, c * 128:(c + 1) * 128] = a
                bsel[q, out, SEED + c * 128:SEED + (c + 1) * 128] = b

    def sum_marks(i):
        at = pl.multiple_of(i // 2 * 16, 16)
        half = i % 2
        blk = idm[pl.ds(at, 16), :]
        want = [jnp.broadcast_to(blk[:, 1 + k:2 + k], (16, 128)).astype(jnp.int16) for k in range(F1)]
        base = lane16 + jnp.full((16, 128), half * (SRC // 2), jnp.int32).astype(jnp.int16)
        for c in range(SRC // 256):
            here = base + jnp.full((16, 128), c * 128, jnp.int32).astype(jnp.int16)
            acc = jnp.where(here == want[0], one, zero)
            for k in range(1, F1):
                acc = acc + jnp.where(here == want[k], one, zero)
            col = pl.ds(pl.multiple_of(half * (SRC // 2) + c * 128, 128), 128)
            ssel[pl.ds(at, 16), col] = acc

    def sum_ids(b):
        idm[...] = idxv[:, cols(b)].T

    def cols(b):
        return pl.ds(pl.multiple_of(b * 256, 256), 256)

    def one_mark(i, c):
        sum_marks(i)
        return c

    sum_ids(0)
    lax.fori_loop(0, 32, one_mark, 0)

    come = pulled.at[pl.ds(0, (DEV - 1) * CAP)]
    pltpu.make_async_copy(come, come, row_recv).wait()
    gone = featb.at[pl.ds(CAP, (DEV - 1) * CAP)]
    pltpu.make_async_copy(gone, gone, row_send).wait()
    sent = mid.at[:, pl.ds(0, GRP - 1)]
    pltpu.make_async_copy(sent, sent, req_send.at[0]).wait()

    def widen(i, c):
        rows = pl.ds(pl.multiple_of(i * 256, 256), 256)
        table[rows, :] = pulled[rows, :].astype(F32)
        return c

    lax.fori_loop(0, SRC // 256, widen, 0)
    table[SRC:SRC + 8, :] = jnp.zeros((8, D_IN), F32)
    for c in to_smem:
        c.wait()

    def forward(b):
        @pl.when(b % 2 == 0)
        def _():
            blk = gbuf.at[left, cols(b), :]
            link(blk, blk, h_send.at[0, b], h_recv.at[0, b], right).wait_recv()
            link(blk, blk, h_send.at[2, b], h_recv.at[2, b], right).start()

        @pl.when(b % 2 == 1)
        def _():
            blk = gbuf.at[right, cols(b), :]
            link(blk, blk, h_send.at[1, b], h_recv.at[1, b], left).wait_recv()
            link(blk, blk, h_send.at[2, b], h_recv.at[2, b], left).start()

    def own_row(b, i, j):
        m = b * 256 + i * 16 + j
        here = pl.ds(pl.multiple_of(i * 16, 16) + j, 1)
        own[here, :] = view[idx[0, m]]
        return m, here

    def load_sums(b, mark):
        def some(i, c):
            backward_marks(b * 16 + i)
            mark(i)
            for j in range(16):
                m, here = own_row(b, i, j)
                rows = [view[idx[1 + k, m]] for k in range(F1)]
                while len(rows) > 1:
                    rows = [p + q for p, q in zip(rows[::2], rows[1::2])] + ([rows[-1]] if len(rows) % 2 else [])
                near[here, :] = rows[0] * inv[0, m]
            return c

        lax.fori_loop(0, 16, some, 0)
        finish(b)

    def multiply_sums(b):
        def some(i, c):
            backward_marks(b * 16 + i)
            for j in range(16):
                own_row(b, i, j)
            return c

        lax.fori_loop(0, 16, some, 0)
        scale = jnp.concatenate(
            [spread(invv[0:1, pl.ds(pl.multiple_of(b * 256 + c * 128, 128), 128)]) for c in range(2)], axis=0
        )
        near[...] = dot(ssel[...], pulled[...]) * scale
        finish(b)

    def finish(b):
        rows = cols(b)
        act = jnp.concatenate([own[...].astype(BF), near[...].astype(BF)], axis=1)
        a1 = act.T
        for h in range(2):
            a1t[pl.ds(pl.multiple_of((2 * b + h) * 256, 256), 256), :] = a1[:, h * 128:(h + 1) * 128]
        z = dot(act, gw1[...].reshape(2 * D_IN, HID)) + bias[0:1, 0:HID]
        z1[rows, :] = z
        gbuf[y, rows, :] = (z / (1.0 + jnp.exp(-z))).astype(BF)
        blk = gbuf.at[y, rows, :]
        link(blk, blk, h_send.at[0, b], h_recv.at[0, b], right).start()
        link(blk, blk, h_send.at[1, b], h_recv.at[1, b], left).start()

        @pl.when(b > 0)
        def _():
            forward(b - 1)

    multiply_sums(0)

    def three(p, c):
        sum_ids(3 * p + 3)

        def loaded(h, c2):
            load_sums(3 * p + 1 + h, lambda i: sum_marks(h * 16 + i))
            return c2

        lax.fori_loop(0, 2, loaded, 0)
        multiply_sums(3 * p + 3)
        return c

    lax.fori_loop(0, 2, three, 0)
    load_sums(7, lambda i: None)
    forward(7)

    def from_source(q, fresh=False):
        def rows512(i, c):
            part = dot(fsel[q, pl.ds(pl.multiple_of(i * SEED, SEED), SEED), :], gbuf[q])
            for h in range(2):
                rows = pl.ds(pl.multiple_of(h * 2 * SEED + i * SEED, SEED), SEED)
                now = part[:, h * 128:(h + 1) * 128]
                tot[rows, :] = now if fresh else tot[rows, :] + now
            return c

        lax.fori_loop(0, 2, rows512, 0)

    from_source(y, True)
    for b in range(1, 8, 2):
        blk = gbuf.at[left, b * 256:(b + 1) * 256, :]
        link(blk, blk, h_send.at[0, b], h_recv.at[0, b], right).wait_recv()
    from_source(left)
    for b in range(0, 8, 2):
        blk = gbuf.at[right, b * 256:(b + 1) * 256, :]
        link(blk, blk, h_send.at[1, b], h_recv.at[1, b], left).wait_recv()
    from_source(right)
    for b in range(8):
        blk = gbuf.at[opp, b * 256:(b + 1) * 256, :]
        link(blk, blk, h_send.at[2, b], h_recv.at[2, b], right).wait_recv()
    from_source(opp)

    def wide(a):
        return jnp.concatenate([a, a], axis=1)

    def seeds(first):
        return jnp.concatenate([tot[h * 2 * SEED + first:h * 2 * SEED + first + SEED, :] for h in range(2)], axis=1)

    near2 = (seeds(0) * wide(invc[y])).astype(BF)
    self2 = seeds(SEED).astype(BF)
    alive = live[...].astype(F32)
    diff = self2.astype(F32) - near2.astype(F32)
    pull_apart = wide(livec[...]) * diff

    def swap_start(buf, ssem, rsem):
        blk = buf.at[y]
        link(blk, blk, ssem.at[0], rsem.at[0], right).start()
        link(blk, blk, ssem.at[1], rsem.at[1], left).start()

    def swap_forward(buf, ssem, rsem, cut):
        blk = buf.at[left]
        link(blk, blk, ssem.at[0], rsem.at[0], right).wait_recv()
        half = buf.at[left, 0:cut, :]
        link(half, half, ssem.at[2], rsem.at[2], right).start()
        blk = buf.at[right]
        link(blk, blk, ssem.at[1], rsem.at[1], left).wait_recv()
        half = buf.at[right, cut:, :]
        link(half, half, ssem.at[3], rsem.at[3], left).start()

    def swap_end(buf, ssem, rsem, cut):
        half = buf.at[opp, 0:cut, :]
        link(half, half, ssem.at[2], rsem.at[2], right).wait_recv()
        half = buf.at[opp, cut:, :]
        link(half, half, ssem.at[3], rsem.at[3], left).wait_recv()

    def swap_sent(buf, ssem, rsem, cut):
        blk = buf.at[y]
        link(blk, blk, ssem.at[0], rsem.at[0], right).wait_send()
        link(blk, blk, ssem.at[1], rsem.at[1], left).wait_send()
        half = buf.at[left, 0:cut, :]
        link(half, half, ssem.at[2], rsem.at[2], right).wait_send()
        half = buf.at[right, cut:, :]
        link(half, half, ssem.at[3], rsem.at[3], left).wait_send()

    rbuf[y] = pull_apart.astype(BF)
    swap_start(rbuf, r_send, r_recv)

    act2 = jnp.concatenate([self2, near2], axis=1)
    cls = lax.broadcasted_iota(jnp.int32, (CLS_PAD, SEED), 0)
    b2 = b2c[0:CLS_PAD, :]
    logits = dot(w2t[...], act2, NT) + jnp.concatenate([b2] * 4, axis=1)
    logits = jnp.where(cls < CLS, logits, -1e30)
    top = jnp.max(logits, axis=0, keepdims=True)
    e = jnp.exp(logits - top)
    tot = jnp.sum(e, axis=0, keepdims=True)
    hot = cls == labels[...]
    picked = jnp.sum(jnp.where(hot, logits, 0.0), axis=0, keepdims=True)
    dlog = (alive * (e * (1.0 / tot) - jnp.where(hot, 1.0, 0.0)) * (1.0 / SEEDS_ALL)).astype(BF)
    dbuf[y] = dlog
    swap_start(dbuf, d_send, d_recv)

    loss = jnp.sum(alive * (top + jnp.log(tot) - picked), axis=1, keepdims=True)
    loss = loss + SEEDS_ALL / 2 * jnp.sum(pull_apart * diff, keepdims=True)
    g2t = dot(dlog, act2).astype(BF)
    for q in range(NAR):
        pay2[q * Q2:q * Q2 + CLS_PAD, :] = g2t[:, q * 128:(q + 1) * 128]
        pay2[q * Q2 + CLS_PAD:(q + 1) * Q2, :] = jnp.zeros((Q2 - CLS_PAD, 128), BF)

    def to_owner(pay, inbox, first, count, n):
        def body(i, c):
            t = (g + i) % GRP
            p = t - first

            @pl.when((p >= 0) & (p < count))
            def _():
                pltpu.make_async_remote_copy(
                    src_ref=pay.at[pl.ds(pl.multiple_of(p * PIECE, PIECE), PIECE)], dst_ref=inbox.at[g],
                    send_sem=rs_send.at[n], recv_sem=rs_recv.at[n], device_id=(t, y), device_id_type=MESH,
                ).start()

            return c

        lax.fori_loop(1, GRP, body, 0)

    def mine(first, count):
        p = g - first
        return (p >= 0) & (p < count), pl.ds(pl.multiple_of(p * PIECE, PIECE), PIECE)

    def add_first_momentum(p):
        rows = pl.ds(pl.multiple_of(p % 2 * PIECE, PIECE), PIECE)
        for h in range(2):
            @pl.when((y == p % 8 // 2) & (p // 8 == h))
            def _(h=h):
                ybox1[y] = ybox1[y] + MU * m1[rows, h * 128:(h + 1) * 128]

    def add_second_momentum(p):
        @pl.when(y == p // (Q2 // PIECE))
        def _():
            rows = pl.ds(pl.multiple_of(p % (Q2 // PIECE) * PIECE, PIECE), PIECE)
            ybox2[y] = ybox2[y] + MU * m2pad[rows, :]

    def add_plane(pay, inbox, ybox, first, count, n, add_momentum):
        here, rows = mine(first, count)

        @pl.when(here)
        def _():
            got = inbox.at[pl.ds(0, GRP - 1)]
            pltpu.make_async_copy(got, got, rs_recv.at[n]).wait()
            inbox[g] = pay[rows, :]
            ybox[y] = jnp.sum(inbox[...].astype(F32), axis=0)
            add_momentum(g - first)
            for d in range(1, NAR):
                link(ybox.at[y], ybox.at[y], y_send.at[n, d - 1], y_recv.at[n, d - 1], ys[d]).start()

    def add_group(ybox, res, first, count, n):
        here, rows = mine(first, count)

        @pl.when(here)
        def _():
            for d in range(1, NAR):
                link(ybox.at[y], ybox.at[y], y_send.at[n, d - 1], y_recv.at[n, d - 1], ys[d]).wait()
            res[rows, :] = (ybox[0] + ybox[1]) + (ybox[2] + ybox[3])

            def tell(i, c):
                pltpu.make_async_remote_copy(
                    src_ref=res.at[rows], dst_ref=res.at[rows], send_sem=ag_send.at[n], recv_sem=ag_recv.at[n],
                    device_id=((g + i) % GRP, y), device_id_type=MESH,
                ).start()
                return c

            lax.fori_loop(1, GRP, tell, 0)

    def take(res, first, count, n):
        here, rows = mine(first, count)
        for less, when in ((1, here), (0, jnp.logical_not(here))):
            @pl.when(when)
            def _(less=less):
                got = res.at[pl.ds(0, (count - less) * PIECE)]
                pltpu.make_async_copy(got, got, ag_recv.at[n]).wait()

    def sums_sent(pay, first, count, n):
        here, rows = mine(first, count)
        for less, when in ((1, here), (0, jnp.logical_not(here))):
            @pl.when(when)
            def _(less=less):
                gone = pay.at[pl.ds(0, (count - less) * PIECE)]
                pltpu.make_async_copy(gone, gone, rs_send.at[n]).wait()

        @pl.when(here)
        def _():
            gone = table.at[pl.ds(0, (GRP - 1) * PIECE)]
            pltpu.make_async_copy(gone, gone, ag_send.at[n]).wait()

    to_owner(pay2, inbox2, GRP - P2, P2, 1)

    def add_grads(q, fresh=False):
        da = dot(dbuf[q], w2t[...], TN)
        r = rbuf[q].astype(F32)
        ds = (da[:, :HID] + r).astype(BF)
        dn = ((da[:, HID:] - r) * wide(invc[q])).astype(BF)
        both = jnp.concatenate([dn, ds], axis=0)

        def rows512(i, c):
            part = dot(bsel[q, pl.ds(pl.multiple_of(i * 512, 512), 512), :], both)
            for h in range(2):
                rows = pl.ds(pl.multiple_of(h * FRONT + i * 512, 512), 512)
                now = part[:, h * 128:(h + 1) * 128]
                dh1[rows, :] = now if fresh else dh1[rows, :] + now
            return c

        lax.fori_loop(0, FRONT // 512, rows512, 0)

    db2 = jnp.sum(dlog.astype(F32), axis=1, keepdims=True)
    db2 = jnp.broadcast_to(db2, (CLS_PAD, 128)).T[0:1, :]
    swap_forward(rbuf, r_send, r_recv, SEED // 2)
    add_grads(y, True)
    swap_forward(dbuf, d_send, d_recv, 96)
    add_grads(left)
    add_grads(right)
    add_plane(pay2, inbox2, ybox2, GRP - P2, P2, 1, add_second_momentum)
    swap_end(rbuf, r_send, r_recv, SEED // 2)
    swap_end(dbuf, d_send, d_recv, 96)
    add_group(ybox2, res2, GRP - P2, P2, 1)
    add_grads(opp)

    def to_z(b, db):
        rows = pl.ds(pl.multiple_of(b * 256, 256), 256)
        z = z1[rows, :]
        sig = 1.0 / (1.0 + jnp.exp(-z))
        dh = jnp.concatenate(
            [dh1[pl.ds(pl.multiple_of(h * FRONT + b * 256, 256), 256), :] for h in range(2)], axis=1
        )
        dz = (dh * sig * (1.0 + z * (1.0 - sig))).astype(BF)
        a1 = jnp.concatenate(
            [a1t[pl.ds(pl.multiple_of((2 * b + h) * 256, 256), 256), :] for h in range(2)], axis=1
        )
        part = dot(a1, dz)
        for h in range(2):
            now = slice(h * 256, (h + 1) * 256)
            gsum[now, :] = gsum[now, :] + part[:, h * 128:(h + 1) * 128]
        return db + jnp.sum(dz.astype(F32), axis=0, keepdims=True)

    gsum[...] = jnp.zeros((512, 128), F32)
    db1 = lax.fori_loop(0, FRONT // 256, to_z, jnp.zeros((1, HID), F32))
    pay1[0:512, :] = gsum[...].astype(BF)
    misc[...] = jnp.zeros((PIECE, 128), F32)

    def two(rows, v):
        hi = v.astype(BF).astype(F32)
        misc[rows:rows + 1, 0:v.shape[1]] = hi
        misc[rows + 4:rows + 5, 0:v.shape[1]] = v - hi

    two(0, db1[:, :128])
    two(1, db1[:, 128:])
    two(2, db2[:, :128])
    two(3, db2[:, 128:])
    hi = loss.astype(BF).astype(F32)
    misc[8:9, 0:1] = hi
    misc[9:10, 0:1] = loss - hi
    pay1[512:544, :] = misc[...].astype(BF)
    to_owner(pay1, inbox1, 0, P1, 0)

    take(res2, GRP - P2, P2, 1)
    mom2 = jnp.concatenate([res2[q * Q2:q * Q2 + CLS_PAD, :] for q in range(NAR)], axis=1)
    for q in range(NAR):
        x2s[q] = mom2[:, q * 128:(q + 1) * 128]
    o_all[ROW_M2:ROW_M2 + CLS_PAD, :] = x2s[y]
    x2 = mom2 * (1.0 / (jnp.sqrt(jnp.sum(mom2 * mom2, keepdims=True)) + 1e-07))
    x2 = ns_step(x2)
    add_plane(pay1, inbox1, ybox1, 0, P1, 0, add_first_momentum)
    x2 = ns_step(x2)
    add_group(ybox1, o_all, 0, P1, 0)
    for _ in range(NS_ITERS - 2):
        x2 = ns_step(x2)
    for q in range(NAR):
        x2s[q] = x2[:, q * 128:(q + 1) * 128]
    o_all[ROW_X2:ROW_X2 + CLS_PAD, :] = x2s[y]
    take(o_all, 0, P1, 0)

    for b in range(8):
        blk = gbuf.at[y, b * 256:(b + 1) * 256, :]
        link(blk, blk, h_send.at[0, b], h_recv.at[0, b], right).wait_send()
        link(blk, blk, h_send.at[1, b], h_recv.at[1, b], left).wait_send()
        blk = gbuf.at[opp, b * 256:(b + 1) * 256, :]
        link(blk, blk, h_send.at[2, b], h_recv.at[2, b], right).wait_send()
    swap_sent(rbuf, r_send, r_recv, SEED // 2)
    swap_sent(dbuf, d_send, d_recv, 96)

    sums_sent(pay2, GRP - P2, P2, 1)
    sums_sent(pay1, 0, P1, 0)


def main(reqt, feat, idx1t, msk1t, idx2t, msk2t, labels, live, w1, w2own, m1, m2own, bias):
    vm = pl.BlockSpec(memory_space=pltpu.VMEM)
    dma = pltpu.SemaphoreType.DMA
    sds = jax.ShapeDtypeStruct
    V = pltpu.VMEM
    return pl.pallas_call(
        main_kernel,
        out_shape=sds((ROWS, 128), F32),
        in_specs=[vm, pl.BlockSpec(memory_space=pl.ANY)] + [vm] * 11,
        out_specs=vm,
        scratch_shapes=[
            V((SRC + 8, D_IN), F32),
            V((OWN, D_IN), BF),
            V((SRC, D_IN), BF),
            V((CAP, D_IN), F32),
            V((DEV, 128), jnp.int32),
            V((DEV, 128), jnp.int32),
            V((NAR, GRP, 1, 128), jnp.int32),
            V((16, FRONT), jnp.int32),
            V((1, FRONT), F32),
            V((256, D_IN), F32),
            V((256, D_IN), F32),
            V((FRONT, HID), F32),
            V((NAR, FRONT, HID), BF),
            V((NAR, 2 * SEED, FRONT), BF),
            V((NAR, FRONT, 2 * SEED), BF),
            V((NAR, 4, 1 + F2, 16, 128), jnp.int16),
            V((SEED, 16), jnp.int32),
            V((256, SRC), BF),
            V((256, 16), jnp.int32),
            V((NAR, SEED, 128), F32),
            V((SEED, 128), F32),
            V((NAR, SEED, HID), BF),
            V((NAR, CLS_PAD, SEED), BF),
            V((NAR, 64, HID), BF),
            V((NAR, CLS_PAD, 128), BF),
            V((Q2, 128), F32),
            V((NAR, 16, SEED), jnp.int32),
            V((CLS_PAD, 2 * HID), BF),
            V((HID, 128), F32),
            V((P1 * PIECE, 128), BF),
            V((P2 * PIECE, 128), BF),
            V((PIECE, 128), F32),
            V((GRP, PIECE, 128), BF),
            V((GRP, PIECE, 128), BF),
            V((NAR, PIECE, 128), F32),
            V((NAR, PIECE, 128), F32),
            V((P2 * PIECE, 128), F32),
            V((NAR, CLS_PAD, 128), F32),
            pltpu.SMEM((DEV, 1, 128), jnp.int32),
            pltpu.SMEM((16, FRONT), jnp.int32),
            pltpu.SMEM((1, FRONT), F32),
            dma, dma((3,)), dma((GRP,)), dma((NAR,)), dma((NAR,)), dma((GRP,)), dma, dma, dma((3, 3)), dma((3, 3)),
            dma((3, 8)), dma((3, 8)), dma((4,)), dma((4,)), dma((4,)), dma((4,)),
            dma((2,)), dma((2,)), dma((2, 3)), dma((2, 3)), dma((2,)), dma((2,)),
        ],
        compiler_params=pltpu.CompilerParams(
            collective_id=0, has_side_effects=True, vmem_limit_bytes=62 * 2**20
        ),
    )(reqt, feat, idx1t, msk1t, idx2t, msk2t, labels, live, w1, w2own, m1, m2own, bias)


def update_kernel(
    res, w1own, w2own, bias, biasm, biasv,
    o_loss, o_first, o_second, o_mom1, o_mom2, o_flow, o_slow, o_bias, o_bm, o_bv,
    x1s,
):
    y = lax.axis_index("nar")
    mom1 = jnp.concatenate([res[0:256, :], res[256:512, :]], axis=1)
    x1s[...] = mom1
    block64 = pl.ds(pl.multiple_of(y * 64, 64), 64)
    o_mom1[...] = x1s[block64, :]
    x1 = mom1 * (1.0 / (jnp.sqrt(jnp.sum(mom1 * mom1, keepdims=True)) + 1e-07))
    for _ in range(NS_ITERS):
        x1 = ns_step(x1)
    x1s[...] = x1
    first_new = w1own[...] * (1.0 - WDECAY) - x1s[block64, :]
    o_first[...] = first_new
    o_flow[...] = first_new.astype(BF)
    second = w2own[...] * (1.0 - WDECAY) - (2 * HID / CLS) ** 0.5 * res[ROW_X2:ROW_X2 + CLS, :]
    o_second[...] = second
    o_slow[...] = second.astype(BF)
    o_mom2[...] = res[ROW_M2:ROW_M2 + CLS, :]

    gb = res[512:516, :] + res[516:520, :]
    gb = jnp.concatenate([gb[0:1, :], gb[1:2, :], gb[2:3, :], gb[3:4, 0:44]], axis=1)
    m_new = BETA_ONE * biasm[...] + (1.0 - BETA_ONE) * gb
    v_new = BETA_TWO * biasv[...] + (1.0 - BETA_TWO) * gb * gb
    m_hat = m_new / (1.0 - BETA_ONE**STEP)
    v_hat = v_new / (1.0 - BETA_TWO**STEP)
    o_bias[...] = bias[...] * (1.0 - LR_BIAS * WDECAY) - LR_BIAS * m_hat / (jnp.sqrt(v_hat) + EPSILON)
    o_bm[...] = m_new
    o_bv[...] = v_new
    o_loss[...] = res[520:521, 0:1] + res[521:522, 0:1]


def update(*args):
    vm = pl.BlockSpec(memory_space=pltpu.VMEM)
    sds = jax.ShapeDtypeStruct
    return pl.pallas_call(
        update_kernel,
        out_shape=[
            sds((1, 1), F32), sds((64, HID), F32), sds((CLS, 128), F32), sds((64, HID), F32), sds((CLS, 128), F32),
            sds((64, HID), BF), sds((CLS, 128), BF), sds((1, 428), F32), sds((1, 428), F32), sds((1, 428), F32),
        ],
        in_specs=[vm] * 6,
        out_specs=[vm] * 10,
        scratch_shapes=[pltpu.VMEM((2 * D_IN, HID), F32)],
        compiler_params=pltpu.CompilerParams(vmem_limit_bytes=32 * 2**20),
    )(*args)


def per_device(
    features, requests, index_one, mask_one, index_two, mask_two, labels, seed_live,
    w_first, w_second, mom_first, mom_second, biases, bias_m, bias_v,
):
    w2own, bias = w_second.T, biases[None, :]
    res = main(
        requests.T, features, index_one.T, mask_one.T, index_two.T, mask_two.T, labels[None, :], seed_live[None, :],
        w_first, w2own, mom_first, mom_second.T, bias,
    )
    loss, first_new, second_new, mom_one, mom_two, first_low, second_low, bias_new, m_new, v_new = update(
        res, w_first, w2own, bias, bias_m[None, :], bias_v[None, :]
    )
    return (
        loss.reshape(()), first_new, second_new.T, mom_one, mom_two.T, first_low, second_low.T,
        bias_new.reshape(-1), m_new.reshape(-1), v_new.reshape(-1),
    )


def solution(mesh):
    both = ("grp", "nar")
    placed = (
        P(both, None), P(both, None), P(both, None), P(both, None), P(both, None), P(both, None),
        P(both), P(both), P("nar", None), P("nar", None), P("nar", None), P("nar", None), P(), P(), P(),
    )
    nar = P("nar", None)
    return jax.shard_map(
        per_device, mesh=mesh, in_specs=placed,
        out_specs=(P(), nar, nar, nar, nar, nar, nar, P(), P(), P()), check_vma=False,
    )
```

```python
import functools

import jax
import jax.numpy as jnp
from jax import lax
from jax.experimental import pallas as pl
from jax.experimental.pallas import tpu as pltpu
from jax.sharding import PartitionSpec as P

HID = 256
CLS = 172
CLS_PAD = 176
D_IN = 128
F1 = 15
F2 = 10
NS_ITERS = 5
STEP = 10
LAM = 0.5
MU = 0.95
WDECAY = 0.01
LR_BIAS = 0.05
BETA_ONE = 0.9
BETA_TWO = 0.999
EPSILON = 1e-08
NS_A = 3.4445
NS_B = -4.775
NS_C = 2.0315
HIGH = lax.Precision.HIGHEST
MESH = pl.DeviceIdType.MESH
BF = jnp.bfloat16
F32 = jnp.float32

DEV = 128
NAR = 4
OWN = 8192
CAP = 64
SRC = 8192
FRONT = 2048
SEED = 512


def all_to(t):
    return (t // NAR, t % NAR)


PIECE = 32
P1 = 17
Q2 = 192
P2 = 24
GRP = 32
ROW_M2 = P1 * PIECE
ROW_X2 = ROW_M2 + CLS_PAD
ROWS = ROW_X2 + CLS_PAD
SEEDS_ALL = SEED * DEV


def dot(a, b, dims=((1,), (0,))):
    return lax.dot_general(a, b, (dims, ((), ())), preferred_element_type=F32)


NN = ((1,), (0,))
NT = ((1,), (1,))
TN = ((0,), (0,))


def split(a):
    hi = a.astype(BF)
    return hi, (a - hi.astype(F32)).astype(BF)


def dot3(a, b, dims):
    (ah, al), (bh, bl) = a, b
    return dot(ah, bh, dims) + (dot(ah, bl, dims) + dot(al, bh, dims))


def ns_step(x):
    xs = split(x)
    gram = dot3(xs, xs, NT)
    gs = split(gram)
    mix = NS_B * gram + NS_C * dot3(gs, gs, NN)
    return NS_A * x + dot3(split(mix), xs, NN)


def spread(row):
    return jnp.broadcast_to(row, (128, 128)).T


def main_kernel(
    reqt, feat, idx1t, msk1t, idx2t, msk2t, labels, live, w1, w2own, m1, m2own, bias,
    o_all,
    table, featb, pulled, stage, reqv, reqin, mid, idxv, invv, near, own, z1, gbuf, fsel, bsel, wants, idc, ssel, idm, invc, livec, rbuf, dbuf,
    gw1, gw2t, m2pad, gidx2, w2t, b2c, pay1, pay2, misc, inbox1, inbox2, ybox1, ybox2, res2, x2s,
    reqs, idx, inv,
    feat_sem, loc_sem, ask_sem, req_send, mid_recv, req_recv, row_send, row_recv, nar_send, nar_recv,
    h_send, h_recv, r_send, r_recv, d_send, d_recv, rs_send, rs_recv, y_send, y_recv, ag_send, ag_recv,
):
    a1t, dh1, tot, gsum = featb, table, table.at[2 * FRONT:3 * FRONT], table.at[3 * FRONT:3 * FRONT + 512]
    g = lax.axis_index("grp")
    y = lax.axis_index("nar")
    me = g * NAR + y
    left, right, opp = (y + 3) % NAR, (y + 1) % NAR, (y + 2) % NAR

    load = pltpu.make_async_copy(feat, featb, feat_sem)
    load.start()

    barrier = pltpu.get_barrier_semaphore()

    ys = [(y + d) % NAR for d in range(NAR)]

    def greet(i, c):
        pl.semaphore_signal(barrier, inc=1, device_id=((g + i) % GRP, y), device_id_type=MESH)
        return c

    for d in range(1, NAR):
        pl.semaphore_signal(barrier, inc=1, device_id=(g, ys[d]), device_id_type=MESH)
    lax.fori_loop(1, GRP, greet, 0)

    def link(src, dst, ssem, rsem, to):
        return pltpu.make_async_remote_copy(
            src_ref=src, dst_ref=dst, send_sem=ssem, recv_sem=rsem, device_id=(g, to), device_id_type=MESH
        )

    reqv[...] = jnp.concatenate([reqt[...], jnp.zeros((DEV - CAP, DEV), jnp.int32)], axis=0).T
    ask_rows = reqv.reshape(GRP, NAR, 1, 128)
    got_rows = reqin.reshape(DEV, 1, 128)

    gw1[y] = w1[...].astype(BF)
    pad = CLS_PAD - CLS
    gw2t[y] = jnp.concatenate([w2own[...], jnp.zeros((pad, 128), F32)], axis=0).astype(BF)
    m2pad[...] = jnp.concatenate([m2own[...], jnp.zeros((Q2 - CLS, 128), F32)], axis=0)
    gidx2[y] = jnp.concatenate(
        [idx2t[0:1, :], jnp.where(msk2t[...] > 0, idx2t[1:, :], -1), jnp.zeros((5, SEED), jnp.int32)], axis=0
    )
    shared = (gidx2, gw1, gw2t)

    pl.semaphore_wait(barrier, GRP + NAR - 2)

    def ask_group(d):
        return pltpu.make_async_remote_copy(
            src_ref=ask_rows.at[:, ys[d]], dst_ref=mid.at[y], send_sem=req_send.at[d], recv_sem=mid_recv.at[d],
            device_id=(g, ys[d]), device_id_type=MESH,
        )

    for d in range(1, NAR):
        ask_group(d).start()
    keep = pltpu.make_async_copy(ask_rows.at[:, y], mid.at[y], loc_sem.at[2])
    keep.start()
    for n, a in enumerate(shared):
        for d in range(1, NAR):
            link(a.at[y], a.at[y], nar_send.at[n, d - 1], nar_recv.at[n, d - 1], (y + d) % NAR).start()

    msk = msk1t[...]
    idxv[0:1, :] = idx1t[0:1, :]
    idxv[1:16, :] = jnp.where(msk > 0, idx1t[1:16, :], SRC)
    invv[...] = 1.0 / jnp.maximum(jnp.sum(msk.astype(F32), axis=0, keepdims=True), 1.0)
    to_smem = [pltpu.make_async_copy(idxv, idx, loc_sem.at[0]), pltpu.make_async_copy(invv, inv, loc_sem.at[1])]
    for c in to_smem:
        c.start()

    keep.wait()
    for d in range(1, NAR):
        ask_group(d).wait()
    own_rows = pl.ds(pl.multiple_of(g * NAR, NAR), NAR)

    def ask(i, c):
        n = (i * 13) % GRP
        t = (g + n) % GRP
        pltpu.make_async_remote_copy(
            src_ref=mid.at[:, t], dst_ref=got_rows.at[own_rows], send_sem=req_send.at[0], recv_sem=req_recv.at[n],
            device_id=(t, y), device_id_type=MESH,
        ).start()
        return c

    lax.fori_loop(1, GRP, ask, 0)
    keep = pltpu.make_async_copy(mid.at[:, g], got_rows.at[own_rows], loc_sem.at[2])
    keep.start()

    load.wait()

    def widen_features(i, c):
        rows = pl.ds(pl.multiple_of(i * 256, 256), 256)
        table[rows, :] = featb[rows, :].astype(F32)
        return c

    lax.fori_loop(0, OWN // 256, widen_features, 0)

    lane16 = lax.broadcasted_iota(jnp.int32, (16, 128), 1).astype(jnp.int16)
    iota16 = lax.broadcasted_iota(jnp.int32, (16, 128), 0).astype(jnp.int16)
    one, zero = jnp.ones((16, 128), BF), jnp.zeros((16, 128), BF)

    def marks(here, want):
        acc = jnp.where(here == want[1], one, zero)
        for k in range(2, 1 + F2):
            acc = acc + jnp.where(here == want[k], one, zero)
        return acc, jnp.where(here == want[0], one, zero)

    idc[...] = gidx2[y].T

    def seeds16(i):
        at = pl.multiple_of(i * 16, 16)
        blk = idc[pl.ds(at, 16), :]
        return at, [jnp.broadcast_to(blk[:, k:k + 1], (16, 128)).astype(jnp.int16) for k in range(1 + F2)]

    def forward_marks(at, want, q):
        for c in range(FRONT // 128):
            here = lane16 + jnp.full((16, 128), q * FRONT + c * 128, jnp.int32).astype(jnp.int16)
            a, b = marks(here, want)
            fsel[q, pl.ds(at, 16), c * 128:(c + 1) * 128] = a
            fsel[q, pl.ds(SEED + at, 16), c * 128:(c + 1) * 128] = b

    view = table.reshape(SRC + 8, 1, D_IN)
    my_rows = pl.ds(pl.multiple_of(me * CAP, CAP), CAP)

    def pick(t, u, slot):
        for r in range(CAP):
            stage[r:r + 1, :] = view[reqs[t * NAR + u, 0, r]]
        featb[slot, :] = stage[...].astype(BF)

    def serve_one(t, u, slot):
        pick(t, u, slot)
        pltpu.make_async_remote_copy(
            src_ref=featb.at[slot], dst_ref=pulled.at[my_rows],
            send_sem=row_send, recv_sem=row_recv, device_id=(t, u), device_id_type=MESH,
        ).start()

    def asked(n):
        rows = got_rows.at[pl.ds(0, NAR)]
        pltpu.make_async_copy(rows, rows, req_recv.at[n]).wait()

    def to_scalars(t, n):
        rows = pl.ds(pl.multiple_of(t * NAR, NAR), NAR)
        return pltpu.make_async_copy(got_rows.at[rows], reqs.at[rows], ask_sem.at[n])

    def whose(i):
        n = (i * 13) % GRP
        return n, (g + GRP - n) % GRP

    def fetch(i):
        n, t = whose(i)
        asked(n)
        to_scalars(t, n).start()

    def serve(i, c):
        n, t = whose(i)

        @pl.when(i < GRP - 1)
        def _():
            fetch(i + 1)

        to_scalars(t, n).wait()
        at, want = seeds16(i)
        for d in range(NAR):
            forward_marks(at, want, d)
            serve_one(t, ys[d], pl.ds(pl.multiple_of((i * NAR + d) * CAP, CAP), CAP))
        return c

    fetch(1)
    lax.fori_loop(1, GRP, serve, 0)
    keep.wait()
    to_scalars(g, 0).start()
    to_scalars(g, 0).wait()
    at, want = seeds16(0)
    for d in range(NAR):
        forward_marks(at, want, d)
    for d in range(1, NAR):
        serve_one(g, ys[d], pl.ds(d * CAP, CAP))
    pick(g, y, pl.ds(0, CAP))
    pulled[my_rows, :] = featb[0:CAP, :]

    for n, a in enumerate(shared):
        for d in range(1, NAR):
            link(a.at[y], a.at[y], nar_send.at[n, d - 1], nar_recv.at[n, d - 1], (y + d) % NAR).wait()
    for q in range(NAR):
        w2t[:, q * 128:(q + 1) * 128] = gw2t[q]
    last = jnp.concatenate([bias[0:1, 384:428], jnp.zeros((1, 84), F32)], axis=1)
    b2c[...] = jnp.concatenate([spread(bias[0:1, 256:384]), spread(last)], axis=0)

    def column(row):
        return jnp.concatenate([spread(row[:, c * 128:(c + 1) * 128]) for c in range(SEED // 128)], axis=0)

    for q in range(NAR):
        n = jnp.sum((gidx2[q, 1:1 + F2, :] >= 0).astype(F32), axis=0, keepdims=True)
        invc[q] = column(1.0 / jnp.maximum(n, 1.0))
    livec[...] = column(2.0 * LAM / HID / SEEDS_ALL * live[...].astype(F32))

    for q in range(NAR):
        ids = gidx2[q] - y * FRONT
        for c in range(SEED // 128):
            for k in range(1 + F2):
                row = ids[k:k + 1, c * 128:(c + 1) * 128]
                wants[q, c, k] = jnp.broadcast_to(row, (16, 128)).astype(jnp.int16)

    def backward_marks(i):
        here = iota16 + jnp.full((16, 128), i * 16, jnp.int32).astype(jnp.int16)
        out = pl.ds(pl.multiple_of(i * 16, 16), 16)
        for q in range(NAR):
            for c in range(SEED // 128):
                a, b = marks(here, [wants[q, c, k] for k in range(1 + F2)])
                bsel[q, out, c * 128:(c + 1) * 128] = a
                bsel[q, out, SEED + c * 128:SEED + (c + 1) * 128] = b

    def sum_marks(i):
        at = pl.multiple_of(i // 2 * 16, 16)
        half = i % 2
        blk = idm[pl.ds(at, 16), :]
        want = [jnp.broadcast_to(blk[:, 1 + k:2 + k], (16, 128)).astype(jnp.int16) for k in range(F1)]
        base = lane16 + jnp.full((16, 128), half * (SRC // 2), jnp.int32).astype(jnp.int16)
        for c in range(SRC // 256):
            here = base + jnp.full((16, 128), c * 128, jnp.int32).astype(jnp.int16)
            acc = jnp.where(here == want[0], one, zero)
            for k in range(1, F1):
                acc = acc + jnp.where(here == want[k], one, zero)
            col = pl.ds(pl.multiple_of(half * (SRC // 2) + c * 128, 128), 128)
            ssel[pl.ds(at, 16), col] = acc

    def sum_ids(b):
        idm[...] = idxv[:, cols(b)].T

    def cols(b):
        return pl.ds(pl.multiple_of(b * 256, 256), 256)

    def one_mark(i, c):
        sum_marks(i)
        return c

    sum_ids(0)
    lax.fori_loop(0, 32, one_mark, 0)

    come = pulled.at[pl.ds(0, (DEV - 1) * CAP)]
    pltpu.make_async_copy(come, come, row_recv).wait()
    gone = featb.at[pl.ds(CAP, (DEV - 1) * CAP)]
    pltpu.make_async_copy(gone, gone, row_send).wait()
    sent = mid.at[:, pl.ds(0, GRP - 1)]
    pltpu.make_async_copy(sent, sent, req_send.at[0]).wait()

    def widen(i, c):
        rows = pl.ds(pl.multiple_of(i * 256, 256), 256)
        table[rows, :] = pulled[rows, :].astype(F32)
        return c

    lax.fori_loop(0, SRC // 256, widen, 0)
    table[SRC:SRC + 8, :] = jnp.zeros((8, D_IN), F32)
    for c in to_smem:
        c.wait()

    def forward(b):
        @pl.when(b % 2 == 0)
        def _():
            blk = gbuf.at[left, cols(b), :]
            link(blk, blk, h_send.at[0, b], h_recv.at[0, b], right).wait_recv()
            link(blk, blk, h_send.at[2, b], h_recv.at[2, b], right).start()

        @pl.when(b % 2 == 1)
        def _():
            blk = gbuf.at[right, cols(b), :]
            link(blk, blk, h_send.at[1, b], h_recv.at[1, b], left).wait_recv()
            link(blk, blk, h_send.at[2, b], h_recv.at[2, b], left).start()

    def own_row(b, i, j):
        m = b * 256 + i * 16 + j
        here = pl.ds(pl.multiple_of(i * 16, 16) + j, 1)
        own[here, :] = view[idx[0, m]]
        return m, here

    def load_sums(b, mark):
        def some(i, c):
            backward_marks(b * 16 + i)
            mark(i)
            for j in range(16):
                m, here = own_row(b, i, j)
                rows = [view[idx[1 + k, m]] for k in range(F1)]
                while len(rows) > 1:
                    rows = [p + q for p, q in zip(rows[::2], rows[1::2])] + ([rows[-1]] if len(rows) % 2 else [])
                near[here, :] = rows[0] * inv[0, m]
            return c

        lax.fori_loop(0, 16, some, 0)
        finish(b)

    def multiply_sums(b):
        def some(i, c):
            backward_marks(b * 16 + i)
            for j in range(16):
                own_row(b, i, j)
            return c

        lax.fori_loop(0, 16, some, 0)
        scale = jnp.concatenate(
            [spread(invv[0:1, pl.ds(pl.multiple_of(b * 256 + c * 128, 128), 128)]) for c in range(2)], axis=0
        )
        near[...] = dot(ssel[...], pulled[...]) * scale
        finish(b)

    def finish(b):
        rows = cols(b)
        act = jnp.concatenate([own[...].astype(BF), near[...].astype(BF)], axis=1)
        a1 = act.T
        for h in range(2):
            a1t[pl.ds(pl.multiple_of((2 * b + h) * 256, 256), 256), :] = a1[:, h * 128:(h + 1) * 128]
        z = dot(act, gw1[...].reshape(2 * D_IN, HID)) + bias[0:1, 0:HID]
        z1[rows, :] = z
        gbuf[y, rows, :] = (z / (1.0 + jnp.exp(-z))).astype(BF)
        blk = gbuf.at[y, rows, :]
        link(blk, blk, h_send.at[0, b], h_recv.at[0, b], right).start()
        link(blk, blk, h_send.at[1, b], h_recv.at[1, b], left).start()

        @pl.when(b > 0)
        def _():
            forward(b - 1)

    def loaded(b, c):
        load_sums(b, lambda i: None)
        return c

    multiply_sums(0)
    lax.fori_loop(1, 8, loaded, 0)
    forward(7)

    def from_source(q, fresh=False):
        def rows512(i, c):
            part = dot(fsel[q, pl.ds(pl.multiple_of(i * SEED, SEED), SEED), :], gbuf[q])
            for h in range(2):
                rows = pl.ds(pl.multiple_of(h * 2 * SEED + i * SEED, SEED), SEED)
                now = part[:, h * 128:(h + 1) * 128]
                tot[rows, :] = now if fresh else tot[rows, :] + now
            return c

        lax.fori_loop(0, 2, rows512, 0)

    from_source(y, True)
    for b in range(1, 8, 2):
        blk = gbuf.at[left, b * 256:(b + 1) * 256, :]
        link(blk, blk, h_send.at[0, b], h_recv.at[0, b], right).wait_recv()
    from_source(left)
    for b in range(0, 8, 2):
        blk = gbuf.at[right, b * 256:(b + 1) * 256, :]
        link(blk, blk, h_send.at[1, b], h_recv.at[1, b], left).wait_recv()
    from_source(right)
    for b in range(8):
        blk = gbuf.at[opp, b * 256:(b + 1) * 256, :]
        link(blk, blk, h_send.at[2, b], h_recv.at[2, b], right).wait_recv()
    from_source(opp)

    def wide(a):
        return jnp.concatenate([a, a], axis=1)

    def seeds(first):
        return jnp.concatenate([tot[h * 2 * SEED + first:h * 2 * SEED + first + SEED, :] for h in range(2)], axis=1)

    near2 = (seeds(0) * wide(invc[y])).astype(BF)
    self2 = seeds(SEED).astype(BF)
    alive = live[...].astype(F32)
    diff = self2.astype(F32) - near2.astype(F32)
    pull_apart = wide(livec[...]) * diff

    def swap_start(buf, ssem, rsem):
        blk = buf.at[y]
        link(blk, blk, ssem.at[0], rsem.at[0], right).start()
        link(blk, blk, ssem.at[1], rsem.at[1], left).start()

    def swap_forward(buf, ssem, rsem, cut):
        blk = buf.at[left]
        link(blk, blk, ssem.at[0], rsem.at[0], right).wait_recv()
        half = buf.at[left, 0:cut, :]
        link(half, half, ssem.at[2], rsem.at[2], right).start()
        blk = buf.at[right]
        link(blk, blk, ssem.at[1], rsem.at[1], left).wait_recv()
        half = buf.at[right, cut:, :]
        link(half, half, ssem.at[3], rsem.at[3], left).start()

    def swap_end(buf, ssem, rsem, cut):
        half = buf.at[opp, 0:cut, :]
        link(half, half, ssem.at[2], rsem.at[2], right).wait_recv()
        half = buf.at[opp, cut:, :]
        link(half, half, ssem.at[3], rsem.at[3], left).wait_recv()

    def swap_sent(buf, ssem, rsem, cut):
        blk = buf.at[y]
        link(blk, blk, ssem.at[0], rsem.at[0], right).wait_send()
        link(blk, blk, ssem.at[1], rsem.at[1], left).wait_send()
        half = buf.at[left, 0:cut, :]
        link(half, half, ssem.at[2], rsem.at[2], right).wait_send()
        half = buf.at[right, cut:, :]
        link(half, half, ssem.at[3], rsem.at[3], left).wait_send()

    rbuf[y] = pull_apart.astype(BF)
    swap_start(rbuf, r_send, r_recv)

    act2 = jnp.concatenate([self2, near2], axis=1)
    cls = lax.broadcasted_iota(jnp.int32, (CLS_PAD, SEED), 0)
    b2 = b2c[0:CLS_PAD, :]
    logits = dot(w2t[...], act2, NT) + jnp.concatenate([b2] * 4, axis=1)
    logits = jnp.where(cls < CLS, logits, -1e30)
    top = jnp.max(logits, axis=0, keepdims=True)
    e = jnp.exp(logits - top)
    tot = jnp.sum(e, axis=0, keepdims=True)
    hot = cls == labels[...]
    picked = jnp.sum(jnp.where(hot, logits, 0.0), axis=0, keepdims=True)
    dlog = (alive * (e * (1.0 / tot) - jnp.where(hot, 1.0, 0.0)) * (1.0 / SEEDS_ALL)).astype(BF)
    dbuf[y] = dlog
    swap_start(dbuf, d_send, d_recv)

    loss = jnp.sum(alive * (top + jnp.log(tot) - picked), axis=1, keepdims=True)
    loss = loss + SEEDS_ALL / 2 * jnp.sum(pull_apart * diff, keepdims=True)
    g2t = dot(dlog, act2).astype(BF)
    for q in range(NAR):
        pay2[q * Q2:q * Q2 + CLS_PAD, :] = g2t[:, q * 128:(q + 1) * 128]
        pay2[q * Q2 + CLS_PAD:(q + 1) * Q2, :] = jnp.zeros((Q2 - CLS_PAD, 128), BF)

    def to_owner(pay, inbox, first, count, n):
        def body(i, c):
            t = (g + i) % GRP
            p = t - first

            @pl.when((p >= 0) & (p < count))
            def _():
                pltpu.make_async_remote_copy(
                    src_ref=pay.at[pl.ds(pl.multiple_of(p * PIECE, PIECE), PIECE)], dst_ref=inbox.at[g],
                    send_sem=rs_send.at[n], recv_sem=rs_recv.at[n], device_id=(t, y), device_id_type=MESH,
                ).start()

            return c

        lax.fori_loop(1, GRP, body, 0)

    def mine(first, count):
        p = g - first
        return (p >= 0) & (p < count), pl.ds(pl.multiple_of(p * PIECE, PIECE), PIECE)

    def add_first_momentum(p):
        rows = pl.ds(pl.multiple_of(p % 2 * PIECE, PIECE), PIECE)
        for h in range(2):
            @pl.when((y == p % 8 // 2) & (p // 8 == h))
            def _(h=h):
                ybox1[y] = ybox1[y] + MU * m1[rows, h * 128:(h + 1) * 128]

    def add_second_momentum(p):
        @pl.when(y == p // (Q2 // PIECE))
        def _():
            rows = pl.ds(pl.multiple_of(p % (Q2 // PIECE) * PIECE, PIECE), PIECE)
            ybox2[y] = ybox2[y] + MU * m2pad[rows, :]

    def add_plane(pay, inbox, ybox, first, count, n, add_momentum):
        here, rows = mine(first, count)

        @pl.when(here)
        def _():
            got = inbox.at[pl.ds(0, GRP - 1)]
            pltpu.make_async_copy(got, got, rs_recv.at[n]).wait()
            inbox[g] = pay[rows, :]
            ybox[y] = jnp.sum(inbox[...].astype(F32), axis=0)
            add_momentum(g - first)
            for d in range(1, NAR):
                link(ybox.at[y], ybox.at[y], y_send.at[n, d - 1], y_recv.at[n, d - 1], ys[d]).start()

    def add_group(ybox, res, first, count, n):
        here, rows = mine(first, count)

        @pl.when(here)
        def _():
            for d in range(1, NAR):
                link(ybox.at[y], ybox.at[y], y_send.at[n, d - 1], y_recv.at[n, d - 1], ys[d]).wait()
            res[rows, :] = (ybox[0] + ybox[1]) + (ybox[2] + ybox[3])

            def tell(i, c):
                pltpu.make_async_remote_copy(
                    src_ref=res.at[rows], dst_ref=res.at[rows], send_sem=ag_send.at[n], recv_sem=ag_recv.at[n],
                    device_id=((g + i) % GRP, y), device_id_type=MESH,
                ).start()
                return c

            lax.fori_loop(1, GRP, tell, 0)

    def take(res, first, count, n):
        here, rows = mine(first, count)
        for less, when in ((1, here), (0, jnp.logical_not(here))):
            @pl.when(when)
            def _(less=less):
                got = res.at[pl.ds(0, (count - less) * PIECE)]
                pltpu.make_async_copy(got, got, ag_recv.at[n]).wait()

    def sums_sent(pay, first, count, n):
        here, rows = mine(first, count)
        for less, when in ((1, here), (0, jnp.logical_not(here))):
            @pl.when(when)
            def _(less=less):
                gone = pay.at[pl.ds(0, (count - less) * PIECE)]
                pltpu.make_async_copy(gone, gone, rs_send.at[n]).wait()

        @pl.when(here)
        def _():
            gone = table.at[pl.ds(0, (GRP - 1) * PIECE)]
            pltpu.make_async_copy(gone, gone, ag_send.at[n]).wait()

    to_owner(pay2, inbox2, GRP - P2, P2, 1)

    def add_grads(q, fresh=False):
        da = dot(dbuf[q], w2t[...], TN)
        r = rbuf[q].astype(F32)
        ds = (da[:, :HID] + r).astype(BF)
        dn = ((da[:, HID:] - r) * wide(invc[q])).astype(BF)
        both = jnp.concatenate([dn, ds], axis=0)

        def rows512(i, c):
            part = dot(bsel[q, pl.ds(pl.multiple_of(i * 512, 512), 512), :], both)
            for h in range(2):
                rows = pl.ds(pl.multiple_of(h * FRONT + i * 512, 512), 512)
                now = part[:, h * 128:(h + 1) * 128]
                dh1[rows, :] = now if fresh else dh1[rows, :] + now
            return c

        lax.fori_loop(0, FRONT // 512, rows512, 0)

    db2 = jnp.sum(dlog.astype(F32), axis=1, keepdims=True)
    db2 = jnp.broadcast_to(db2, (CLS_PAD, 128)).T[0:1, :]
    swap_forward(rbuf, r_send, r_recv, SEED // 2)
    add_grads(y, True)
    swap_forward(dbuf, d_send, d_recv, 96)
    add_grads(left)
    add_grads(right)
    add_plane(pay2, inbox2, ybox2, GRP - P2, P2, 1, add_second_momentum)
    swap_end(rbuf, r_send, r_recv, SEED // 2)
    swap_end(dbuf, d_send, d_recv, 96)
    add_group(ybox2, res2, GRP - P2, P2, 1)
    add_grads(opp)

    def to_z(b, db):
        rows = pl.ds(pl.multiple_of(b * 256, 256), 256)
        z = z1[rows, :]
        sig = 1.0 / (1.0 + jnp.exp(-z))
        dh = jnp.concatenate(
            [dh1[pl.ds(pl.multiple_of(h * FRONT + b * 256, 256), 256), :] for h in range(2)], axis=1
        )
        dz = (dh * sig * (1.0 + z * (1.0 - sig))).astype(BF)
        a1 = jnp.concatenate(
            [a1t[pl.ds(pl.multiple_of((2 * b + h) * 256, 256), 256), :] for h in range(2)], axis=1
        )
        part = dot(a1, dz)
        for h in range(2):
            now = slice(h * 256, (h + 1) * 256)
            gsum[now, :] = gsum[now, :] + part[:, h * 128:(h + 1) * 128]
        return db + jnp.sum(dz.astype(F32), axis=0, keepdims=True)

    gsum[...] = jnp.zeros((512, 128), F32)
    db1 = lax.fori_loop(0, FRONT // 256, to_z, jnp.zeros((1, HID), F32))
    pay1[0:512, :] = gsum[...].astype(BF)
    misc[...] = jnp.zeros((PIECE, 128), F32)

    def two(rows, v):
        hi = v.astype(BF).astype(F32)
        misc[rows:rows + 1, 0:v.shape[1]] = hi
        misc[rows + 4:rows + 5, 0:v.shape[1]] = v - hi

    two(0, db1[:, :128])
    two(1, db1[:, 128:])
    two(2, db2[:, :128])
    two(3, db2[:, 128:])
    hi = loss.astype(BF).astype(F32)
    misc[8:9, 0:1] = hi
    misc[9:10, 0:1] = loss - hi
    pay1[512:544, :] = misc[...].astype(BF)
    to_owner(pay1, inbox1, 0, P1, 0)

    take(res2, GRP - P2, P2, 1)
    mom2 = jnp.concatenate([res2[q * Q2:q * Q2 + CLS_PAD, :] for q in range(NAR)], axis=1)
    for q in range(NAR):
        x2s[q] = mom2[:, q * 128:(q + 1) * 128]
    o_all[ROW_M2:ROW_M2 + CLS_PAD, :] = x2s[y]
    x2 = mom2 * (1.0 / (jnp.sqrt(jnp.sum(mom2 * mom2, keepdims=True)) + 1e-07))
    x2 = ns_step(x2)
    add_plane(pay1, inbox1, ybox1, 0, P1, 0, add_first_momentum)
    x2 = ns_step(x2)
    add_group(ybox1, o_all, 0, P1, 0)
    for _ in range(NS_ITERS - 2):
        x2 = ns_step(x2)
    for q in range(NAR):
        x2s[q] = x2[:, q * 128:(q + 1) * 128]
    o_all[ROW_X2:ROW_X2 + CLS_PAD, :] = x2s[y]
    take(o_all, 0, P1, 0)

    for b in range(8):
        blk = gbuf.at[y, b * 256:(b + 1) * 256, :]
        link(blk, blk, h_send.at[0, b], h_recv.at[0, b], right).wait_send()
        link(blk, blk, h_send.at[1, b], h_recv.at[1, b], left).wait_send()
        blk = gbuf.at[opp, b * 256:(b + 1) * 256, :]
        link(blk, blk, h_send.at[2, b], h_recv.at[2, b], right).wait_send()
    swap_sent(rbuf, r_send, r_recv, SEED // 2)
    swap_sent(dbuf, d_send, d_recv, 96)

    sums_sent(pay2, GRP - P2, P2, 1)
    sums_sent(pay1, 0, P1, 0)


def main(reqt, feat, idx1t, msk1t, idx2t, msk2t, labels, live, w1, w2own, m1, m2own, bias):
    vm = pl.BlockSpec(memory_space=pltpu.VMEM)
    dma = pltpu.SemaphoreType.DMA
    sds = jax.ShapeDtypeStruct
    V = pltpu.VMEM
    return pl.pallas_call(
        main_kernel,
        out_shape=sds((ROWS, 128), F32),
        in_specs=[vm, pl.BlockSpec(memory_space=pl.ANY)] + [vm] * 11,
        out_specs=vm,
        scratch_shapes=[
            V((SRC + 8, D_IN), F32),
            V((OWN, D_IN), BF),
            V((SRC, D_IN), BF),
            V((CAP, D_IN), F32),
            V((DEV, 128), jnp.int32),
            V((DEV, 128), jnp.int32),
            V((NAR, GRP, 1, 128), jnp.int32),
            V((16, FRONT), jnp.int32),
            V((1, FRONT), F32),
            V((256, D_IN), F32),
            V((256, D_IN), F32),
            V((FRONT, HID), F32),
            V((NAR, FRONT, HID), BF),
            V((NAR, 2 * SEED, FRONT), BF),
            V((NAR, FRONT, 2 * SEED), BF),
            V((NAR, 4, 1 + F2, 16, 128), jnp.int16),
            V((SEED, 16), jnp.int32),
            V((256, SRC), BF),
            V((256, 16), jnp.int32),
            V((NAR, SEED, 128), F32),
            V((SEED, 128), F32),
            V((NAR, SEED, HID), BF),
            V((NAR, CLS_PAD, SEED), BF),
            V((NAR, 64, HID), BF),
            V((NAR, CLS_PAD, 128), BF),
            V((Q2, 128), F32),
            V((NAR, 16, SEED), jnp.int32),
            V((CLS_PAD, 2 * HID), BF),
            V((HID, 128), F32),
            V((P1 * PIECE, 128), BF),
            V((P2 * PIECE, 128), BF),
            V((PIECE, 128), F32),
            V((GRP, PIECE, 128), BF),
            V((GRP, PIECE, 128), BF),
            V((NAR, PIECE, 128), F32),
            V((NAR, PIECE, 128), F32),
            V((P2 * PIECE, 128), F32),
            V((NAR, CLS_PAD, 128), F32),
            pltpu.SMEM((DEV, 1, 128), jnp.int32),
            pltpu.SMEM((16, FRONT), jnp.int32),
            pltpu.SMEM((1, FRONT), F32),
            dma, dma((3,)), dma((GRP,)), dma((NAR,)), dma((NAR,)), dma((GRP,)), dma, dma, dma((3, 3)), dma((3, 3)),
            dma((3, 8)), dma((3, 8)), dma((4,)), dma((4,)), dma((4,)), dma((4,)),
            dma((2,)), dma((2,)), dma((2, 3)), dma((2, 3)), dma((2,)), dma((2,)),
        ],
        compiler_params=pltpu.CompilerParams(
            collective_id=0, has_side_effects=True, vmem_limit_bytes=62 * 2**20
        ),
    )(reqt, feat, idx1t, msk1t, idx2t, msk2t, labels, live, w1, w2own, m1, m2own, bias)


def update_kernel(
    res, w1own, w2own, bias, biasm, biasv,
    o_loss, o_first, o_second, o_mom1, o_mom2, o_flow, o_slow, o_bias, o_bm, o_bv,
    x1s,
):
    y = lax.axis_index("nar")
    mom1 = jnp.concatenate([res[0:256, :], res[256:512, :]], axis=1)
    x1s[...] = mom1
    block64 = pl.ds(pl.multiple_of(y * 64, 64), 64)
    o_mom1[...] = x1s[block64, :]
    x1 = mom1 * (1.0 / (jnp.sqrt(jnp.sum(mom1 * mom1, keepdims=True)) + 1e-07))
    for _ in range(NS_ITERS):
        x1 = ns_step(x1)
    x1s[...] = x1
    first_new = w1own[...] * (1.0 - WDECAY) - x1s[block64, :]
    o_first[...] = first_new
    o_flow[...] = first_new.astype(BF)
    second = w2own[...] * (1.0 - WDECAY) - (2 * HID / CLS) ** 0.5 * res[ROW_X2:ROW_X2 + CLS, :]
    o_second[...] = second
    o_slow[...] = second.astype(BF)
    o_mom2[...] = res[ROW_M2:ROW_M2 + CLS, :]

    gb = res[512:516, :] + res[516:520, :]
    gb = jnp.concatenate([gb[0:1, :], gb[1:2, :], gb[2:3, :], gb[3:4, 0:44]], axis=1)
    m_new = BETA_ONE * biasm[...] + (1.0 - BETA_ONE) * gb
    v_new = BETA_TWO * biasv[...] + (1.0 - BETA_TWO) * gb * gb
    m_hat = m_new / (1.0 - BETA_ONE**STEP)
    v_hat = v_new / (1.0 - BETA_TWO**STEP)
    o_bias[...] = bias[...] * (1.0 - LR_BIAS * WDECAY) - LR_BIAS * m_hat / (jnp.sqrt(v_hat) + EPSILON)
    o_bm[...] = m_new
    o_bv[...] = v_new
    o_loss[...] = res[520:521, 0:1] + res[521:522, 0:1]


def update(*args):
    vm = pl.BlockSpec(memory_space=pltpu.VMEM)
    sds = jax.ShapeDtypeStruct
    return pl.pallas_call(
        update_kernel,
        out_shape=[
            sds((1, 1), F32), sds((64, HID), F32), sds((CLS, 128), F32), sds((64, HID), F32), sds((CLS, 128), F32),
            sds((64, HID), BF), sds((CLS, 128), BF), sds((1, 428), F32), sds((1, 428), F32), sds((1, 428), F32),
        ],
        in_specs=[vm] * 6,
        out_specs=[vm] * 10,
        scratch_shapes=[pltpu.VMEM((2 * D_IN, HID), F32)],
        compiler_params=pltpu.CompilerParams(vmem_limit_bytes=32 * 2**20),
    )(*args)


def per_device(
    features, requests, index_one, mask_one, index_two, mask_two, labels, seed_live,
    w_first, w_second, mom_first, mom_second, biases, bias_m, bias_v,
):
    w2own, bias = w_second.T, biases[None, :]
    res = main(
        requests.T, features, index_one.T, mask_one.T, index_two.T, mask_two.T, labels[None, :], seed_live[None, :],
        w_first, w2own, mom_first, mom_second.T, bias,
    )
    loss, first_new, second_new, mom_one, mom_two, first_low, second_low, bias_new, m_new, v_new = update(
        res, w_first, w2own, bias, bias_m[None, :], bias_v[None, :]
    )
    return (
        loss.reshape(()), first_new, second_new.T, mom_one, mom_two.T, first_low, second_low.T,
        bias_new.reshape(-1), m_new.reshape(-1), v_new.reshape(-1),
    )


def solution(mesh):
    both = ("grp", "nar")
    placed = (
        P(both, None), P(both, None), P(both, None), P(both, None), P(both, None), P(both, None),
        P(both), P(both), P("nar", None), P("nar", None), P("nar", None), P("nar", None), P(), P(), P(),
    )
    nar = P("nar", None)
    return jax.shard_map(
        per_device, mesh=mesh, in_specs=placed,
        out_specs=(P(), nar, nar, nar, nar, nar, nar, P(), P(), P()), check_vma=False,
    )
```

```python
import functools

import jax
import jax.numpy as jnp
from jax import lax
from jax.experimental import pallas as pl
from jax.experimental.pallas import tpu as pltpu
from jax.sharding import PartitionSpec as P

HID = 256
CLS = 172
CLS_PAD = 176
D_IN = 128
F1 = 15
F2 = 10
NS_ITERS = 5
STEP = 10
LAM = 0.5
MU = 0.95
WDECAY = 0.01
LR_BIAS = 0.05
BETA_ONE = 0.9
BETA_TWO = 0.999
EPSILON = 1e-08
NS_A = 3.4445
NS_B = -4.775
NS_C = 2.0315
HIGH = lax.Precision.HIGHEST
MESH = pl.DeviceIdType.MESH
BF = jnp.bfloat16
F32 = jnp.float32

DEV = 128
NAR = 4
OWN = 8192
CAP = 64
SRC = 8192
FRONT = 2048
SEED = 512


def all_to(t):
    return (t // NAR, t % NAR)


PIECE = 32
P1 = 17
Q2 = 192
P2 = 24
GRP = 32
ROW_M2 = P1 * PIECE
ROW_X2 = ROW_M2 + CLS_PAD
ROWS = ROW_X2 + CLS_PAD
SEEDS_ALL = SEED * DEV


def dot(a, b, dims=((1,), (0,))):
    return lax.dot_general(a, b, (dims, ((), ())), preferred_element_type=F32)


NN = ((1,), (0,))
NT = ((1,), (1,))
TN = ((0,), (0,))


def split(a):
    hi = a.astype(BF)
    return hi, (a - hi.astype(F32)).astype(BF)


def dot3(a, b, dims):
    (ah, al), (bh, bl) = a, b
    return dot(ah, bh, dims) + (dot(ah, bl, dims) + dot(al, bh, dims))


def ns_step(x):
    xs = split(x)
    gram = dot3(xs, xs, NT)
    gs = split(gram)
    mix = NS_B * gram + NS_C * dot3(gs, gs, NN)
    return NS_A * x + dot3(split(mix), xs, NN)


def spread(row):
    return jnp.broadcast_to(row, (128, 128)).T


def main_kernel(
    reqt, feat, idx1t, msk1t, idx2t, msk2t, labels, live, w1, w2own, m1, m2own, bias,
    o_all,
    table, featb, pulled, stage, reqv, reqin, mid, idxv, invv, near, own, z1, gbuf, fsel, bsel, unit_of, lows, selfs, idc, ssel, idm, invc, livec, rbuf, dbuf,
    gw1, gw2t, m2pad, gidx2, w2t, b2c, pay1, pay2, misc, inbox1, inbox2, ybox1, ybox2, res2, x2s,
    reqs, idx, inv,
    feat_sem, loc_sem, ask_sem, req_send, mid_recv, req_recv, row_send, row_recv, nar_send, nar_recv,
    h_send, h_recv, r_send, r_recv, d_send, d_recv, rs_send, rs_recv, y_send, y_recv, ag_send, ag_recv,
):
    a1t, dh1, tot, gsum = featb, table, table.at[2 * FRONT:3 * FRONT], table.at[3 * FRONT:3 * FRONT + 512]
    g = lax.axis_index("grp")
    y = lax.axis_index("nar")
    me = g * NAR + y
    left, right, opp = (y + 3) % NAR, (y + 1) % NAR, (y + 2) % NAR

    load = pltpu.make_async_copy(feat, featb, feat_sem)
    load.start()

    barrier = pltpu.get_barrier_semaphore()

    ys = [(y + d) % NAR for d in range(NAR)]

    def greet(i, c):
        pl.semaphore_signal(barrier, inc=1, device_id=((g + i) % GRP, y), device_id_type=MESH)
        return c

    for d in range(1, NAR):
        pl.semaphore_signal(barrier, inc=1, device_id=(g, ys[d]), device_id_type=MESH)
    lax.fori_loop(1, GRP, greet, 0)

    def link(src, dst, ssem, rsem, to):
        return pltpu.make_async_remote_copy(
            src_ref=src, dst_ref=dst, send_sem=ssem, recv_sem=rsem, device_id=(g, to), device_id_type=MESH
        )

    reqv[...] = jnp.concatenate([reqt[...], jnp.zeros((DEV - CAP, DEV), jnp.int32)], axis=0).T
    ask_rows = reqv.reshape(GRP, NAR, 1, 128)
    got_rows = reqin.reshape(DEV, 1, 128)

    gw1[y] = w1[...].astype(BF)
    pad = CLS_PAD - CLS
    gw2t[y] = jnp.concatenate([w2own[...], jnp.zeros((pad, 128), F32)], axis=0).astype(BF)
    m2pad[...] = jnp.concatenate([m2own[...], jnp.zeros((Q2 - CLS, 128), F32)], axis=0)
    gidx2[y] = jnp.concatenate(
        [idx2t[0:1, :], jnp.where(msk2t[...] > 0, idx2t[1:, :], -1), jnp.zeros((5, SEED), jnp.int32)], axis=0
    )
    shared = (gidx2, gw1, gw2t)

    pl.semaphore_wait(barrier, GRP + NAR - 2)

    def ask_group(d):
        return pltpu.make_async_remote_copy(
            src_ref=ask_rows.at[:, ys[d]], dst_ref=mid.at[y], send_sem=req_send.at[d], recv_sem=mid_recv.at[d],
            device_id=(g, ys[d]), device_id_type=MESH,
        )

    for d in range(1, NAR):
        ask_group(d).start()
    keep = pltpu.make_async_copy(ask_rows.at[:, y], mid.at[y], loc_sem.at[2])
    keep.start()
    for n, a in enumerate(shared):
        for d in range(1, NAR):
            link(a.at[y], a.at[y], nar_send.at[n, d - 1], nar_recv.at[n, d - 1], (y + d) % NAR).start()

    msk = msk1t[...]
    idxv[0:1, :] = idx1t[0:1, :]
    idxv[1:16, :] = jnp.where(msk > 0, idx1t[1:16, :], SRC)
    invv[...] = 1.0 / jnp.maximum(jnp.sum(msk.astype(F32), axis=0, keepdims=True), 1.0)
    to_smem = [pltpu.make_async_copy(idxv, idx, loc_sem.at[0]), pltpu.make_async_copy(invv, inv, loc_sem.at[1])]
    for c in to_smem:
        c.start()

    keep.wait()
    for d in range(1, NAR):
        ask_group(d).wait()
    own_rows = pl.ds(pl.multiple_of(g * NAR, NAR), NAR)

    def ask(i, c):
        n = (i * 13) % GRP
        t = (g + n) % GRP
        pltpu.make_async_remote_copy(
            src_ref=mid.at[:, t], dst_ref=got_rows.at[own_rows], send_sem=req_send.at[0], recv_sem=req_recv.at[n],
            device_id=(t, y), device_id_type=MESH,
        ).start()
        return c

    lax.fori_loop(1, GRP, ask, 0)
    keep = pltpu.make_async_copy(mid.at[:, g], got_rows.at[own_rows], loc_sem.at[2])
    keep.start()

    load.wait()

    def widen_features(i, c):
        rows = pl.ds(pl.multiple_of(i * 256, 256), 256)
        table[rows, :] = featb[rows, :].astype(F32)
        return c

    lax.fori_loop(0, OWN // 256, widen_features, 0)

    lane32 = lax.broadcasted_iota(jnp.int32, (16, 128), 1)
    sub32 = lax.broadcasted_iota(jnp.int32, (32, 128), 0)
    lane16 = lane32.astype(jnp.int16)
    iota16 = lax.broadcasted_iota(jnp.int32, (16, 128), 0).astype(jnp.int16)
    one, zero = jnp.ones((16, 128), BF), jnp.zeros((16, 128), BF)

    def unit(digit):
        v = jnp.ones_like(digit)
        for j in range(1, 8):
            v = jnp.where(digit == j, 1 << 4 * j, v)
        return v

    def count(acc, j):
        return ((acc >> (4 * j)) & 15).astype(F32).astype(BF)

    def keys_units(ids):
        return (ids & 127) + (ids >> 10) * 128, unit((ids >> 7) & 7)

    def word(pos, keys, units):
        acc = jnp.zeros((16, 128), jnp.int32)
        for k, u in zip(keys, units):
            acc = acc + jnp.where(pos == k, u, 0)
        return acc

    def spread_columns(blk, ks):
        return [jnp.broadcast_to(blk[:, k:k + 1], (16, 128)) for k in ks]

    ids = gidx2[y]
    keys, units = keys_units(ids)
    idc[...] = jnp.concatenate([ids[0:1, :], keys[1:, :], units], axis=0).T

    def seeds16(i):
        at = pl.multiple_of(i * 16, 16)
        blk = idc[pl.ds(at, 16), :]
        self_row = jnp.broadcast_to(blk[:, 0:1], (16, 128)).astype(jnp.int16)
        return at, (spread_columns(blk, range(1, 1 + F2)), spread_columns(blk, range(17, 17 + F2)), self_row)

    def forward_marks(at, want, q):
        keys, units, self_row = want
        for w in range(2):
            acc = word(lane32 + 128 * (2 * q + w), keys, units)
            for j in range(8):
                c = w * 8 + j
                fsel[q, pl.ds(at, 16), c * 128:(c + 1) * 128] = count(acc, j)
                here = lane16 + jnp.full((16, 128), q * FRONT + c * 128, jnp.int32).astype(jnp.int16)
                fsel[q, pl.ds(SEED + at, 16), c * 128:(c + 1) * 128] = jnp.where(here == self_row, one, zero)

    view = table.reshape(SRC + 8, 1, D_IN)
    my_rows = pl.ds(pl.multiple_of(me * CAP, CAP), CAP)

    def pick(t, u, slot):
        for r in range(CAP):
            stage[r:r + 1, :] = view[reqs[t * NAR + u, 0, r]]
        featb[slot, :] = stage[...].astype(BF)

    def serve_one(t, u, slot):
        pick(t, u, slot)
        pltpu.make_async_remote_copy(
            src_ref=featb.at[slot], dst_ref=pulled.at[my_rows],
            send_sem=row_send, recv_sem=row_recv, device_id=(t, u), device_id_type=MESH,
        ).start()

    def asked(n):
        rows = got_rows.at[pl.ds(0, NAR)]
        pltpu.make_async_copy(rows, rows, req_recv.at[n]).wait()

    def to_scalars(t, n):
        rows = pl.ds(pl.multiple_of(t * NAR, NAR), NAR)
        return pltpu.make_async_copy(got_rows.at[rows], reqs.at[rows], ask_sem.at[n])

    def whose(i):
        n = (i * 13) % GRP
        return n, (g + GRP - n) % GRP

    def fetch(i):
        n, t = whose(i)
        asked(n)
        to_scalars(t, n).start()

    def serve(i, c):
        n, t = whose(i)

        @pl.when(i < GRP - 1)
        def _():
            fetch(i + 1)

        to_scalars(t, n).wait()
        at, want = seeds16(i)
        for d in range(NAR):
            forward_marks(at, want, d)
            serve_one(t, ys[d], pl.ds(pl.multiple_of((i * NAR + d) * CAP, CAP), CAP))
        return c

    fetch(1)
    lax.fori_loop(1, GRP, serve, 0)
    keep.wait()
    to_scalars(g, 0).start()
    to_scalars(g, 0).wait()
    at, want = seeds16(0)
    for d in range(NAR):
        forward_marks(at, want, d)
    for d in range(1, NAR):
        serve_one(g, ys[d], pl.ds(d * CAP, CAP))
    pick(g, y, pl.ds(0, CAP))
    pulled[my_rows, :] = featb[0:CAP, :]

    for n, a in enumerate(shared):
        for d in range(1, NAR):
            link(a.at[y], a.at[y], nar_send.at[n, d - 1], nar_recv.at[n, d - 1], (y + d) % NAR).wait()
    for q in range(NAR):
        w2t[:, q * 128:(q + 1) * 128] = gw2t[q]
    last = jnp.concatenate([bias[0:1, 384:428], jnp.zeros((1, 84), F32)], axis=1)
    b2c[...] = jnp.concatenate([spread(bias[0:1, 256:384]), spread(last)], axis=0)

    def column(row):
        return jnp.concatenate([spread(row[:, c * 128:(c + 1) * 128]) for c in range(SEED // 128)], axis=0)

    for q in range(NAR):
        n = jnp.sum((gidx2[q, 1:1 + F2, :] >= 0).astype(F32), axis=0, keepdims=True)
        invc[q] = column(1.0 / jnp.maximum(n, 1.0))
    livec[...] = column(2.0 * LAM / HID / SEEDS_ALL * live[...].astype(F32))

    def backward_marks(q, carry):
        r = gidx2[q] - y * FRONT
        lows[...] = r & 31
        inside = (r >= 0) & (r < FRONT)
        units = unit((r >> 5) & 7)
        for w in range(8):
            unit_of[w] = jnp.where(inside & ((r >> 8) == w), units, 0)
        selfs[...] = jnp.broadcast_to(r[0:1, :], (16, SEED))

        def column(c, carry2):
            lanes = pl.ds(pl.multiple_of(c * 128, 128), 128)
            accs = [jnp.zeros((32, 128), jnp.int32) for _ in range(8)]
            for k in range(1, 1 + F2):
                hit = sub32 == jnp.broadcast_to(lows[k:k + 1, lanes], (32, 128))
                for w in range(8):
                    u = jnp.broadcast_to(unit_of[w, k:k + 1, lanes], (32, 128))
                    accs[w] = accs[w] + jnp.where(hit, u, 0)
            for w in range(8):
                for j in range(8):
                    first = (w * 8 + j) * 32
                    bsel[q, first:first + 32, lanes] = count(accs[w], j)
            self_row = selfs[:, lanes].astype(jnp.int16)
            lanes = pl.ds(pl.multiple_of(SEED + c * 128, 128), 128)
            for t in range(FRONT // 16):
                here = iota16 + jnp.full((16, 128), t * 16, jnp.int32).astype(jnp.int16)
                bsel[q, t * 16:(t + 1) * 16, lanes] = jnp.where(here == self_row, one, zero)
            return carry2

        lax.fori_loop(0, SEED // 128, column, 0)
        return carry

    def sum_marks(i):
        at = pl.multiple_of(i // 2 * 16, 16)
        half = i % 2
        blk = idm[pl.ds(at, 16), :]
        keys, units = spread_columns(blk, range(1, 1 + F1)), spread_columns(blk, range(17, 17 + F1))
        for w in range(4):
            acc = word(lane32 + (half * 4 + w) * 128, keys, units)
            for j in range(8):
                col = pl.ds(pl.multiple_of(half * (SRC // 2) + (w * 8 + j) * 128, 128), 128)
                ssel[pl.ds(at, 16), col] = count(acc, j)

    def sum_ids(b):
        idm[...] = jnp.concatenate(keys_units(idxv[:, cols(b)]), axis=0).T

    def cols(b):
        return pl.ds(pl.multiple_of(b * 256, 256), 256)

    def one_mark(i, c):
        sum_marks(i)
        return c

    sum_ids(0)
    lax.fori_loop(0, 32, one_mark, 0)
    lax.fori_loop(0, NAR, backward_marks, 0)

    come = pulled.at[pl.ds(0, (DEV - 1) * CAP)]
    pltpu.make_async_copy(come, come, row_recv).wait()
    gone = featb.at[pl.ds(CAP, (DEV - 1) * CAP)]
    pltpu.make_async_copy(gone, gone, row_send).wait()
    sent = mid.at[:, pl.ds(0, GRP - 1)]
    pltpu.make_async_copy(sent, sent, req_send.at[0]).wait()

    def widen(i, c):
        rows = pl.ds(pl.multiple_of(i * 256, 256), 256)
        table[rows, :] = pulled[rows, :].astype(F32)
        return c

    lax.fori_loop(0, SRC // 256, widen, 0)
    table[SRC:SRC + 8, :] = jnp.zeros((8, D_IN), F32)
    for c in to_smem:
        c.wait()

    def forward(b):
        @pl.when(b % 2 == 0)
        def _():
            blk = gbuf.at[left, cols(b), :]
            link(blk, blk, h_send.at[0, b], h_recv.at[0, b], right).wait_recv()
            link(blk, blk, h_send.at[2, b], h_recv.at[2, b], right).start()

        @pl.when(b % 2 == 1)
        def _():
            blk = gbuf.at[right, cols(b), :]
            link(blk, blk, h_send.at[1, b], h_recv.at[1, b], left).wait_recv()
            link(blk, blk, h_send.at[2, b], h_recv.at[2, b], left).start()

    def own_row(b, i, j):
        m = b * 256 + i * 16 + j
        here = pl.ds(pl.multiple_of(i * 16, 16) + j, 1)
        own[here, :] = view[idx[0, m]]
        return m, here

    def load_sums(b, mark):
        def some(i, c):
            mark(i)
            for j in range(16):
                m, here = own_row(b, i, j)
                rows = [view[idx[1 + k, m]] for k in range(F1)]
                while len(rows) > 1:
                    rows = [p + q for p, q in zip(rows[::2], rows[1::2])] + ([rows[-1]] if len(rows) % 2 else [])
                near[here, :] = rows[0] * inv[0, m]
            return c

        lax.fori_loop(0, 16, some, 0)
        finish(b)

    def multiply_sums(b):
        def some(i, c):
            for j in range(16):
                own_row(b, i, j)
            return c

        lax.fori_loop(0, 16, some, 0)
        scale = jnp.concatenate(
            [spread(invv[0:1, pl.ds(pl.multiple_of(b * 256 + c * 128, 128), 128)]) for c in range(2)], axis=0
        )
        near[...] = dot(ssel[...], pulled[...]) * scale
        finish(b)

    def finish(b):
        rows = cols(b)
        act = jnp.concatenate([own[...].astype(BF), near[...].astype(BF)], axis=1)
        a1 = act.T
        for h in range(2):
            a1t[pl.ds(pl.multiple_of((2 * b + h) * 256, 256), 256), :] = a1[:, h * 128:(h + 1) * 128]
        z = dot(act, gw1[...].reshape(2 * D_IN, HID)) + bias[0:1, 0:HID]
        z1[rows, :] = z
        gbuf[y, rows, :] = (z / (1.0 + jnp.exp(-z))).astype(BF)
        blk = gbuf.at[y, rows, :]
        link(blk, blk, h_send.at[0, b], h_recv.at[0, b], right).start()
        link(blk, blk, h_send.at[1, b], h_recv.at[1, b], left).start()

        @pl.when(b > 0)
        def _():
            forward(b - 1)

    def loaded(b, c):
        load_sums(b, lambda i: None)
        return c

    multiply_sums(0)
    lax.fori_loop(1, 8, loaded, 0)
    forward(7)

    def from_source(q, fresh=False):
        def rows512(i, c):
            part = dot(fsel[q, pl.ds(pl.multiple_of(i * SEED, SEED), SEED), :], gbuf[q])
            for h in range(2):
                rows = pl.ds(pl.multiple_of(h * 2 * SEED + i * SEED, SEED), SEED)
                now = part[:, h * 128:(h + 1) * 128]
                tot[rows, :] = now if fresh else tot[rows, :] + now
            return c

        lax.fori_loop(0, 2, rows512, 0)

    from_source(y, True)
    for b in range(1, 8, 2):
        blk = gbuf.at[left, b * 256:(b + 1) * 256, :]
        link(blk, blk, h_send.at[0, b], h_recv.at[0, b], right).wait_recv()
    from_source(left)
    for b in range(0, 8, 2):
        blk = gbuf.at[right, b * 256:(b + 1) * 256, :]
        link(blk, blk, h_send.at[1, b], h_recv.at[1, b], left).wait_recv()
    from_source(right)
    for b in range(8):
        blk = gbuf.at[opp, b * 256:(b + 1) * 256, :]
        link(blk, blk, h_send.at[2, b], h_recv.at[2, b], right).wait_recv()
    from_source(opp)

    def wide(a):
        return jnp.concatenate([a, a], axis=1)

    def seeds(first):
        return jnp.concatenate([tot[h * 2 * SEED + first:h * 2 * SEED + first + SEED, :] for h in range(2)], axis=1)

    near2 = (seeds(0) * wide(invc[y])).astype(BF)
    self2 = seeds(SEED).astype(BF)
    alive = live[...].astype(F32)
    diff = self2.astype(F32) - near2.astype(F32)
    pull_apart = wide(livec[...]) * diff

    def swap_start(buf, ssem, rsem):
        blk = buf.at[y]
        link(blk, blk, ssem.at[0], rsem.at[0], right).start()
        link(blk, blk, ssem.at[1], rsem.at[1], left).start()

    def swap_forward(buf, ssem, rsem, cut):
        blk = buf.at[left]
        link(blk, blk, ssem.at[0], rsem.at[0], right).wait_recv()
        half = buf.at[left, 0:cut, :]
        link(half, half, ssem.at[2], rsem.at[2], right).start()
        blk = buf.at[right]
        link(blk, blk, ssem.at[1], rsem.at[1], left).wait_recv()
        half = buf.at[right, cut:, :]
        link(half, half, ssem.at[3], rsem.at[3], left).start()

    def swap_end(buf, ssem, rsem, cut):
        half = buf.at[opp, 0:cut, :]
        link(half, half, ssem.at[2], rsem.at[2], right).wait_recv()
        half = buf.at[opp, cut:, :]
        link(half, half, ssem.at[3], rsem.at[3], left).wait_recv()

    def swap_sent(buf, ssem, rsem, cut):
        blk = buf.at[y]
        link(blk, blk, ssem.at[0], rsem.at[0], right).wait_send()
        link(blk, blk, ssem.at[1], rsem.at[1], left).wait_send()
        half = buf.at[left, 0:cut, :]
        link(half, half, ssem.at[2], rsem.at[2], right).wait_send()
        half = buf.at[right, cut:, :]
        link(half, half, ssem.at[3], rsem.at[3], left).wait_send()

    rbuf[y] = pull_apart.astype(BF)
    swap_start(rbuf, r_send, r_recv)

    act2 = jnp.concatenate([self2, near2], axis=1)
    cls = lax.broadcasted_iota(jnp.int32, (CLS_PAD, SEED), 0)
    b2 = b2c[0:CLS_PAD, :]
    logits = dot(w2t[...], act2, NT) + jnp.concatenate([b2] * 4, axis=1)
    logits = jnp.where(cls < CLS, logits, -1e30)
    top = jnp.max(logits, axis=0, keepdims=True)
    e = jnp.exp(logits - top)
    tot = jnp.sum(e, axis=0, keepdims=True)
    hot = cls == labels[...]
    picked = jnp.sum(jnp.where(hot, logits, 0.0), axis=0, keepdims=True)
    dlog = (alive * (e * (1.0 / tot) - jnp.where(hot, 1.0, 0.0)) * (1.0 / SEEDS_ALL)).astype(BF)
    dbuf[y] = dlog
    swap_start(dbuf, d_send, d_recv)

    loss = jnp.sum(alive * (top + jnp.log(tot) - picked), axis=1, keepdims=True)
    loss = loss + SEEDS_ALL / 2 * jnp.sum(pull_apart * diff, keepdims=True)
    g2t = dot(dlog, act2).astype(BF)
    for q in range(NAR):
        pay2[q * Q2:q * Q2 + CLS_PAD, :] = g2t[:, q * 128:(q + 1) * 128]
        pay2[q * Q2 + CLS_PAD:(q + 1) * Q2, :] = jnp.zeros((Q2 - CLS_PAD, 128), BF)

    def to_owner(pay, inbox, first, count, n):
        def body(i, c):
            t = (g + i) % GRP
            p = t - first

            @pl.when((p >= 0) & (p < count))
            def _():
                pltpu.make_async_remote_copy(
                    src_ref=pay.at[pl.ds(pl.multiple_of(p * PIECE, PIECE), PIECE)], dst_ref=inbox.at[g],
                    send_sem=rs_send.at[n], recv_sem=rs_recv.at[n], device_id=(t, y), device_id_type=MESH,
                ).start()

            return c

        lax.fori_loop(1, GRP, body, 0)

    def mine(first, count):
        p = g - first
        return (p >= 0) & (p < count), pl.ds(pl.multiple_of(p * PIECE, PIECE), PIECE)

    def add_first_momentum(p):
        rows = pl.ds(pl.multiple_of(p % 2 * PIECE, PIECE), PIECE)
        for h in range(2):
            @pl.when((y == p % 8 // 2) & (p // 8 == h))
            def _(h=h):
                ybox1[y] = ybox1[y] + MU * m1[rows, h * 128:(h + 1) * 128]

    def add_second_momentum(p):
        @pl.when(y == p // (Q2 // PIECE))
        def _():
            rows = pl.ds(pl.multiple_of(p % (Q2 // PIECE) * PIECE, PIECE), PIECE)
            ybox2[y] = ybox2[y] + MU * m2pad[rows, :]

    def add_plane(pay, inbox, ybox, first, count, n, add_momentum):
        here, rows = mine(first, count)

        @pl.when(here)
        def _():
            got = inbox.at[pl.ds(0, GRP - 1)]
            pltpu.make_async_copy(got, got, rs_recv.at[n]).wait()
            inbox[g] = pay[rows, :]
            ybox[y] = jnp.sum(inbox[...].astype(F32), axis=0)
            add_momentum(g - first)
            for d in range(1, NAR):
                link(ybox.at[y], ybox.at[y], y_send.at[n, d - 1], y_recv.at[n, d - 1], ys[d]).start()

    def add_group(ybox, res, first, count, n):
        here, rows = mine(first, count)

        @pl.when(here)
        def _():
            for d in range(1, NAR):
                link(ybox.at[y], ybox.at[y], y_send.at[n, d - 1], y_recv.at[n, d - 1], ys[d]).wait()
            res[rows, :] = (ybox[0] + ybox[1]) + (ybox[2] + ybox[3])

            def tell(i, c):
                pltpu.make_async_remote_copy(
                    src_ref=res.at[rows], dst_ref=res.at[rows], send_sem=ag_send.at[n], recv_sem=ag_recv.at[n],
                    device_id=((g + i) % GRP, y), device_id_type=MESH,
                ).start()
                return c

            lax.fori_loop(1, GRP, tell, 0)

    def take(res, first, count, n):
        here, rows = mine(first, count)
        for less, when in ((1, here), (0, jnp.logical_not(here))):
            @pl.when(when)
            def _(less=less):
                got = res.at[pl.ds(0, (count - less) * PIECE)]
                pltpu.make_async_copy(got, got, ag_recv.at[n]).wait()

    def sums_sent(pay, first, count, n):
        here, rows = mine(first, count)
        for less, when in ((1, here), (0, jnp.logical_not(here))):
            @pl.when(when)
            def _(less=less):
                gone = pay.at[pl.ds(0, (count - less) * PIECE)]
                pltpu.make_async_copy(gone, gone, rs_send.at[n]).wait()

        @pl.when(here)
        def _():
            gone = table.at[pl.ds(0, (GRP - 1) * PIECE)]
            pltpu.make_async_copy(gone, gone, ag_send.at[n]).wait()

    to_owner(pay2, inbox2, GRP - P2, P2, 1)

    def add_grads(q, fresh=False):
        da = dot(dbuf[q], w2t[...], TN)
        r = rbuf[q].astype(F32)
        ds = (da[:, :HID] + r).astype(BF)
        dn = ((da[:, HID:] - r) * wide(invc[q])).astype(BF)
        both = jnp.concatenate([dn, ds], axis=0)

        def rows512(i, c):
            part = dot(bsel[q, pl.ds(pl.multiple_of(i * 512, 512), 512), :], both)
            for h in range(2):
                rows = pl.ds(pl.multiple_of(h * FRONT + i * 512, 512), 512)
                now = part[:, h * 128:(h + 1) * 128]
                dh1[rows, :] = now if fresh else dh1[rows, :] + now
            return c

        lax.fori_loop(0, FRONT // 512, rows512, 0)

    db2 = jnp.sum(dlog.astype(F32), axis=1, keepdims=True)
    db2 = jnp.broadcast_to(db2, (CLS_PAD, 128)).T[0:1, :]
    swap_forward(rbuf, r_send, r_recv, SEED // 2)
    add_grads(y, True)
    swap_forward(dbuf, d_send, d_recv, 96)
    add_grads(left)
    add_grads(right)
    add_plane(pay2, inbox2, ybox2, GRP - P2, P2, 1, add_second_momentum)
    swap_end(rbuf, r_send, r_recv, SEED // 2)
    swap_end(dbuf, d_send, d_recv, 96)
    add_group(ybox2, res2, GRP - P2, P2, 1)
    add_grads(opp)

    def to_z(b, db):
        rows = pl.ds(pl.multiple_of(b * 256, 256), 256)
        z = z1[rows, :]
        sig = 1.0 / (1.0 + jnp.exp(-z))
        dh = jnp.concatenate(
            [dh1[pl.ds(pl.multiple_of(h * FRONT + b * 256, 256), 256), :] for h in range(2)], axis=1
        )
        dz = (dh * sig * (1.0 + z * (1.0 - sig))).astype(BF)
        a1 = jnp.concatenate(
            [a1t[pl.ds(pl.multiple_of((2 * b + h) * 256, 256), 256), :] for h in range(2)], axis=1
        )
        part = dot(a1, dz)
        for h in range(2):
            now = slice(h * 256, (h + 1) * 256)
            gsum[now, :] = gsum[now, :] + part[:, h * 128:(h + 1) * 128]
        return db + jnp.sum(dz.astype(F32), axis=0, keepdims=True)

    gsum[...] = jnp.zeros((512, 128), F32)
    db1 = lax.fori_loop(0, FRONT // 256, to_z, jnp.zeros((1, HID), F32))
    pay1[0:512, :] = gsum[...].astype(BF)
    misc[...] = jnp.zeros((PIECE, 128), F32)

    def two(rows, v):
        hi = v.astype(BF).astype(F32)
        misc[rows:rows + 1, 0:v.shape[1]] = hi
        misc[rows + 4:rows + 5, 0:v.shape[1]] = v - hi

    two(0, db1[:, :128])
    two(1, db1[:, 128:])
    two(2, db2[:, :128])
    two(3, db2[:, 128:])
    hi = loss.astype(BF).astype(F32)
    misc[8:9, 0:1] = hi
    misc[9:10, 0:1] = loss - hi
    pay1[512:544, :] = misc[...].astype(BF)
    to_owner(pay1, inbox1, 0, P1, 0)

    take(res2, GRP - P2, P2, 1)
    mom2 = jnp.concatenate([res2[q * Q2:q * Q2 + CLS_PAD, :] for q in range(NAR)], axis=1)
    for q in range(NAR):
        x2s[q] = mom2[:, q * 128:(q + 1) * 128]
    o_all[ROW_M2:ROW_M2 + CLS_PAD, :] = x2s[y]
    x2 = mom2 * (1.0 / (jnp.sqrt(jnp.sum(mom2 * mom2, keepdims=True)) + 1e-07))
    x2 = ns_step(x2)
    add_plane(pay1, inbox1, ybox1, 0, P1, 0, add_first_momentum)
    x2 = ns_step(x2)
    add_group(ybox1, o_all, 0, P1, 0)
    for _ in range(NS_ITERS - 2):
        x2 = ns_step(x2)
    for q in range(NAR):
        x2s[q] = x2[:, q * 128:(q + 1) * 128]
    o_all[ROW_X2:ROW_X2 + CLS_PAD, :] = x2s[y]
    take(o_all, 0, P1, 0)

    for b in range(8):
        blk = gbuf.at[y, b * 256:(b + 1) * 256, :]
        link(blk, blk, h_send.at[0, b], h_recv.at[0, b], right).wait_send()
        link(blk, blk, h_send.at[1, b], h_recv.at[1, b], left).wait_send()
        blk = gbuf.at[opp, b * 256:(b + 1) * 256, :]
        link(blk, blk, h_send.at[2, b], h_recv.at[2, b], right).wait_send()
    swap_sent(rbuf, r_send, r_recv, SEED // 2)
    swap_sent(dbuf, d_send, d_recv, 96)

    sums_sent(pay2, GRP - P2, P2, 1)
    sums_sent(pay1, 0, P1, 0)


def main(reqt, feat, idx1t, msk1t, idx2t, msk2t, labels, live, w1, w2own, m1, m2own, bias):
    vm = pl.BlockSpec(memory_space=pltpu.VMEM)
    dma = pltpu.SemaphoreType.DMA
    sds = jax.ShapeDtypeStruct
    V = pltpu.VMEM
    return pl.pallas_call(
        main_kernel,
        out_shape=sds((ROWS, 128), F32),
        in_specs=[vm, pl.BlockSpec(memory_space=pl.ANY)] + [vm] * 11,
        out_specs=vm,
        scratch_shapes=[
            V((SRC + 8, D_IN), F32),
            V((OWN, D_IN), BF),
            V((SRC, D_IN), BF),
            V((CAP, D_IN), F32),
            V((DEV, 128), jnp.int32),
            V((DEV, 128), jnp.int32),
            V((NAR, GRP, 1, 128), jnp.int32),
            V((16, FRONT), jnp.int32),
            V((1, FRONT), F32),
            V((256, D_IN), F32),
            V((256, D_IN), F32),
            V((FRONT, HID), F32),
            V((NAR, FRONT, HID), BF),
            V((NAR, 2 * SEED, FRONT), BF),
            V((NAR, FRONT, 2 * SEED), BF),
            V((8, 16, SEED), jnp.int32),
            V((16, SEED), jnp.int32),
            V((16, SEED), jnp.int32),
            V((SEED, 32), jnp.int32),
            V((256, SRC), BF),
            V((256, 32), jnp.int32),
            V((NAR, SEED, 128), F32),
            V((SEED, 128), F32),
            V((NAR, SEED, HID), BF),
            V((NAR, CLS_PAD, SEED), BF),
            V((NAR, 64, HID), BF),
            V((NAR, CLS_PAD, 128), BF),
            V((Q2, 128), F32),
            V((NAR, 16, SEED), jnp.int32),
            V((CLS_PAD, 2 * HID), BF),
            V((HID, 128), F32),
            V((P1 * PIECE, 128), BF),
            V((P2 * PIECE, 128), BF),
            V((PIECE, 128), F32),
            V((GRP, PIECE, 128), BF),
            V((GRP, PIECE, 128), BF),
            V((NAR, PIECE, 128), F32),
            V((NAR, PIECE, 128), F32),
            V((P2 * PIECE, 128), F32),
            V((NAR, CLS_PAD, 128), F32),
            pltpu.SMEM((DEV, 1, 128), jnp.int32),
            pltpu.SMEM((16, FRONT), jnp.int32),
            pltpu.SMEM((1, FRONT), F32),
            dma, dma((3,)), dma((GRP,)), dma((NAR,)), dma((NAR,)), dma((GRP,)), dma, dma, dma((3, 3)), dma((3, 3)),
            dma((3, 8)), dma((3, 8)), dma((4,)), dma((4,)), dma((4,)), dma((4,)),
            dma((2,)), dma((2,)), dma((2, 3)), dma((2, 3)), dma((2,)), dma((2,)),
        ],
        compiler_params=pltpu.CompilerParams(
            collective_id=0, has_side_effects=True, vmem_limit_bytes=62 * 2**20
        ),
    )(reqt, feat, idx1t, msk1t, idx2t, msk2t, labels, live, w1, w2own, m1, m2own, bias)


def update_kernel(
    res, w1own, w2own, bias, biasm, biasv,
    o_loss, o_first, o_second, o_mom1, o_mom2, o_flow, o_slow, o_bias, o_bm, o_bv,
    x1s,
):
    y = lax.axis_index("nar")
    mom1 = jnp.concatenate([res[0:256, :], res[256:512, :]], axis=1)
    x1s[...] = mom1
    block64 = pl.ds(pl.multiple_of(y * 64, 64), 64)
    o_mom1[...] = x1s[block64, :]
    x1 = mom1 * (1.0 / (jnp.sqrt(jnp.sum(mom1 * mom1, keepdims=True)) + 1e-07))
    for _ in range(NS_ITERS):
        x1 = ns_step(x1)
    x1s[...] = x1
    first_new = w1own[...] * (1.0 - WDECAY) - x1s[block64, :]
    o_first[...] = first_new
    o_flow[...] = first_new.astype(BF)
    second = w2own[...] * (1.0 - WDECAY) - (2 * HID / CLS) ** 0.5 * res[ROW_X2:ROW_X2 + CLS, :]
    o_second[...] = second
    o_slow[...] = second.astype(BF)
    o_mom2[...] = res[ROW_M2:ROW_M2 + CLS, :]

    gb = res[512:516, :] + res[516:520, :]
    gb = jnp.concatenate([gb[0:1, :], gb[1:2, :], gb[2:3, :], gb[3:4, 0:44]], axis=1)
    m_new = BETA_ONE * biasm[...] + (1.0 - BETA_ONE) * gb
    v_new = BETA_TWO * biasv[...] + (1.0 - BETA_TWO) * gb * gb
    m_hat = m_new / (1.0 - BETA_ONE**STEP)
    v_hat = v_new / (1.0 - BETA_TWO**STEP)
    o_bias[...] = bias[...] * (1.0 - LR_BIAS * WDECAY) - LR_BIAS * m_hat / (jnp.sqrt(v_hat) + EPSILON)
    o_bm[...] = m_new
    o_bv[...] = v_new
    o_loss[...] = res[520:521, 0:1] + res[521:522, 0:1]


def update(*args):
    vm = pl.BlockSpec(memory_space=pltpu.VMEM)
    sds = jax.ShapeDtypeStruct
    return pl.pallas_call(
        update_kernel,
        out_shape=[
            sds((1, 1), F32), sds((64, HID), F32), sds((CLS, 128), F32), sds((64, HID), F32), sds((CLS, 128), F32),
            sds((64, HID), BF), sds((CLS, 128), BF), sds((1, 428), F32), sds((1, 428), F32), sds((1, 428), F32),
        ],
        in_specs=[vm] * 6,
        out_specs=[vm] * 10,
        scratch_shapes=[pltpu.VMEM((2 * D_IN, HID), F32)],
        compiler_params=pltpu.CompilerParams(vmem_limit_bytes=32 * 2**20),
    )(*args)


def per_device(
    features, requests, index_one, mask_one, index_two, mask_two, labels, seed_live,
    w_first, w_second, mom_first, mom_second, biases, bias_m, bias_v,
):
    w2own, bias = w_second.T, biases[None, :]
    res = main(
        requests.T, features, index_one.T, mask_one.T, index_two.T, mask_two.T, labels[None, :], seed_live[None, :],
        w_first, w2own, mom_first, mom_second.T, bias,
    )
    loss, first_new, second_new, mom_one, mom_two, first_low, second_low, bias_new, m_new, v_new = update(
        res, w_first, w2own, bias, bias_m[None, :], bias_v[None, :]
    )
    return (
        loss.reshape(()), first_new, second_new.T, mom_one, mom_two.T, first_low, second_low.T,
        bias_new.reshape(-1), m_new.reshape(-1), v_new.reshape(-1),
    )


def solution(mesh):
    both = ("grp", "nar")
    placed = (
        P(both, None), P(both, None), P(both, None), P(both, None), P(both, None), P(both, None),
        P(both), P(both), P("nar", None), P("nar", None), P("nar", None), P("nar", None), P(), P(), P(),
    )
    nar = P("nar", None)
    return jax.shard_map(
        per_device, mesh=mesh, in_specs=placed,
        out_specs=(P(), nar, nar, nar, nar, nar, nar, P(), P(), P()), check_vma=False,
    )
```

```python
import functools

import jax
import jax.numpy as jnp
from jax import lax
from jax.experimental import pallas as pl
from jax.experimental.pallas import tpu as pltpu
from jax.sharding import PartitionSpec as P

HID = 256
CLS = 172
CLS_PAD = 176
D_IN = 128
F1 = 15
F2 = 10
NS_ITERS = 5
STEP = 10
LAM = 0.5
MU = 0.95
WDECAY = 0.01
LR_BIAS = 0.05
BETA_ONE = 0.9
BETA_TWO = 0.999
EPSILON = 1e-08
NS_A = 3.4445
NS_B = -4.775
NS_C = 2.0315
HIGH = lax.Precision.HIGHEST
MESH = pl.DeviceIdType.MESH
BF = jnp.bfloat16
F32 = jnp.float32

DEV = 128
NAR = 4
OWN = 8192
CAP = 64
SRC = 8192
FRONT = 2048
SEED = 512


def all_to(t):
    return (t // NAR, t % NAR)


PIECE = 32
P1 = 17
Q2 = 192
P2 = 24
GRP = 32
ROW_M2 = P1 * PIECE
ROW_X2 = ROW_M2 + CLS_PAD
ROWS = ROW_X2 + CLS_PAD
SEEDS_ALL = SEED * DEV


def dot(a, b, dims=((1,), (0,))):
    return lax.dot_general(a, b, (dims, ((), ())), preferred_element_type=F32)


NN = ((1,), (0,))
NT = ((1,), (1,))
TN = ((0,), (0,))


def split(a):
    hi = a.astype(BF)
    return hi, (a - hi.astype(F32)).astype(BF)


def dot3(a, b, dims):
    (ah, al), (bh, bl) = a, b
    return dot(ah, bh, dims) + (dot(ah, bl, dims) + dot(al, bh, dims))


def ns_step(x):
    xs = split(x)
    gram = dot3(xs, xs, NT)
    gs = split(gram)
    mix = NS_B * gram + NS_C * dot3(gs, gs, NN)
    return NS_A * x + dot3(split(mix), xs, NN)


def spread(row):
    return jnp.broadcast_to(row, (128, 128)).T


def main_kernel(
    reqt, feat, idx1t, msk1t, idx2t, msk2t, labels, live, w1, w2own, m1, m2own, bias,
    o_all,
    table, featb, pulled, stage, reqv, reqin, mid, idxv, invv, near, own, z1, gbuf, fsel, bsel, unit_of, lows, selfs, idc, ssel, idm, invc, livec, rbuf, dbuf,
    gw1, gw2t, m2pad, gidx2, w2t, b2c, pay1, pay2, misc, inbox1, inbox2, ybox1, ybox2, res2, x2s,
    reqs, idx, inv,
    feat_sem, loc_sem, ask_sem, req_send, mid_recv, req_recv, row_send, row_recv, nar_send, nar_recv,
    h_send, h_recv, r_send, r_recv, d_send, d_recv, rs_send, rs_recv, y_send, y_recv, ag_send, ag_recv,
):
    a1t, dh1, tot, gsum = featb, table, table.at[2 * FRONT:3 * FRONT], table.at[3 * FRONT:3 * FRONT + 512]
    g = lax.axis_index("grp")
    y = lax.axis_index("nar")
    me = g * NAR + y
    left, right, opp = (y + 3) % NAR, (y + 1) % NAR, (y + 2) % NAR

    load = pltpu.make_async_copy(feat, featb, feat_sem)
    load.start()

    barrier = pltpu.get_barrier_semaphore()

    ys = [(y + d) % NAR for d in range(NAR)]

    def greet(i, c):
        pl.semaphore_signal(barrier, inc=1, device_id=((g + i) % GRP, y), device_id_type=MESH)
        return c

    for d in range(1, NAR):
        pl.semaphore_signal(barrier, inc=1, device_id=(g, ys[d]), device_id_type=MESH)
    lax.fori_loop(1, GRP, greet, 0)

    def link(src, dst, ssem, rsem, to):
        return pltpu.make_async_remote_copy(
            src_ref=src, dst_ref=dst, send_sem=ssem, recv_sem=rsem, device_id=(g, to), device_id_type=MESH
        )

    reqv[...] = jnp.concatenate([reqt[...], jnp.zeros((DEV - CAP, DEV), jnp.int32)], axis=0).T
    ask_rows = reqv.reshape(GRP, NAR, 1, 128)
    got_rows = reqin.reshape(DEV, 1, 128)

    gw1[y] = w1[...].astype(BF)
    pad = CLS_PAD - CLS
    gw2t[y] = jnp.concatenate([w2own[...], jnp.zeros((pad, 128), F32)], axis=0).astype(BF)
    m2pad[...] = jnp.concatenate([m2own[...], jnp.zeros((Q2 - CLS, 128), F32)], axis=0)
    gidx2[y] = jnp.concatenate(
        [idx2t[0:1, :], jnp.where(msk2t[...] > 0, idx2t[1:, :], -1), jnp.zeros((5, SEED), jnp.int32)], axis=0
    )
    shared = (gidx2, gw1, gw2t)

    pl.semaphore_wait(barrier, GRP + NAR - 2)

    def ask_group(d):
        return pltpu.make_async_remote_copy(
            src_ref=ask_rows.at[:, ys[d]], dst_ref=mid.at[y], send_sem=req_send.at[d], recv_sem=mid_recv.at[d],
            device_id=(g, ys[d]), device_id_type=MESH,
        )

    for d in range(1, NAR):
        ask_group(d).start()
    keep = pltpu.make_async_copy(ask_rows.at[:, y], mid.at[y], loc_sem.at[2])
    keep.start()
    for n, a in enumerate(shared):
        for d in range(1, NAR):
            link(a.at[y], a.at[y], nar_send.at[n, d - 1], nar_recv.at[n, d - 1], (y + d) % NAR).start()

    msk = msk1t[...]
    idxv[0:1, :] = idx1t[0:1, :]
    idxv[1:16, :] = jnp.where(msk > 0, idx1t[1:16, :], SRC)
    invv[...] = 1.0 / jnp.maximum(jnp.sum(msk.astype(F32), axis=0, keepdims=True), 1.0)
    to_smem = [pltpu.make_async_copy(idxv, idx, loc_sem.at[0]), pltpu.make_async_copy(invv, inv, loc_sem.at[1])]
    for c in to_smem:
        c.start()

    keep.wait()
    for d in range(1, NAR):
        ask_group(d).wait()
    own_rows = pl.ds(pl.multiple_of(g * NAR, NAR), NAR)

    def ask(i, c):
        n = (i * 13) % GRP
        t = (g + n) % GRP
        pltpu.make_async_remote_copy(
            src_ref=mid.at[:, t], dst_ref=got_rows.at[own_rows], send_sem=req_send.at[0], recv_sem=req_recv.at[n],
            device_id=(t, y), device_id_type=MESH,
        ).start()
        return c

    lax.fori_loop(1, GRP, ask, 0)
    keep = pltpu.make_async_copy(mid.at[:, g], got_rows.at[own_rows], loc_sem.at[2])
    keep.start()

    load.wait()

    def widen_features(i, c):
        rows = pl.ds(pl.multiple_of(i * 256, 256), 256)
        table[rows, :] = featb[rows, :].astype(F32)
        return c

    lax.fori_loop(0, OWN // 256, widen_features, 0)

    lane32 = lax.broadcasted_iota(jnp.int32, (16, 128), 1)
    sub32 = lax.broadcasted_iota(jnp.int32, (32, 128), 0)
    lane16 = lane32.astype(jnp.int16)
    iota16 = lax.broadcasted_iota(jnp.int32, (16, 128), 0).astype(jnp.int16)
    one, zero = jnp.ones((16, 128), BF), jnp.zeros((16, 128), BF)

    def unit(digit):
        v = jnp.ones_like(digit)
        for j in range(1, 8):
            v = jnp.where(digit == j, 1 << 4 * j, v)
        return v

    def count(acc, j):
        return ((acc >> (4 * j)) & 15).astype(F32).astype(BF)

    def keys_units(ids):
        return (ids & 127) + (ids >> 10) * 128, unit((ids >> 7) & 7)

    def word(pos, keys, units):
        acc = jnp.zeros((16, 128), jnp.int32)
        for k, u in zip(keys, units):
            acc = acc + jnp.where(pos == k, u, 0)
        return acc

    def spread_columns(blk, ks):
        return [jnp.broadcast_to(blk[:, k:k + 1], (16, 128)) for k in ks]

    ids = gidx2[y]
    keys, units = keys_units(ids)
    idc[...] = jnp.concatenate([ids[0:1, :], keys[1:, :], units], axis=0).T

    def seeds16(i):
        at = pl.multiple_of(i * 16, 16)
        blk = idc[pl.ds(at, 16), :]
        self_row = jnp.broadcast_to(blk[:, 0:1], (16, 128)).astype(jnp.int16)
        return at, (spread_columns(blk, range(1, 1 + F2)), spread_columns(blk, range(17, 17 + F2)), self_row)

    def forward_marks(at, want, q):
        keys, units, self_row = want
        for w in range(2):
            acc = word(lane32 + 128 * (2 * q + w), keys, units)
            for j in range(8):
                c = w * 8 + j
                fsel[q, pl.ds(at, 16), c * 128:(c + 1) * 128] = count(acc, j)
                here = lane16 + jnp.full((16, 128), q * FRONT + c * 128, jnp.int32).astype(jnp.int16)
                fsel[q, pl.ds(SEED + at, 16), c * 128:(c + 1) * 128] = jnp.where(here == self_row, one, zero)

    view = table.reshape(SRC + 8, 1, D_IN)
    my_rows = pl.ds(pl.multiple_of(me * CAP, CAP), CAP)

    def pick(t, u, slot):
        for r in range(CAP):
            stage[r:r + 1, :] = view[reqs[t * NAR + u, 0, r]]
        featb[slot, :] = stage[...].astype(BF)

    def serve_one(t, u, slot):
        pick(t, u, slot)
        pltpu.make_async_remote_copy(
            src_ref=featb.at[slot], dst_ref=pulled.at[my_rows],
            send_sem=row_send, recv_sem=row_recv, device_id=(t, u), device_id_type=MESH,
        ).start()

    def asked(n):
        rows = got_rows.at[pl.ds(0, NAR)]
        pltpu.make_async_copy(rows, rows, req_recv.at[n]).wait()

    def to_scalars(t, n):
        rows = pl.ds(pl.multiple_of(t * NAR, NAR), NAR)
        return pltpu.make_async_copy(got_rows.at[rows], reqs.at[rows], ask_sem.at[n])

    def whose(i):
        n = (i * 13) % GRP
        return n, (g + GRP - n) % GRP

    def fetch(i):
        n, t = whose(i)
        asked(n)
        to_scalars(t, n).start()

    def serve(i, c):
        n, t = whose(i)

        @pl.when(i < GRP - 1)
        def _():
            fetch(i + 1)

        to_scalars(t, n).wait()
        at, want = seeds16(i)
        for d in range(NAR):
            forward_marks(at, want, d)
            serve_one(t, ys[d], pl.ds(pl.multiple_of((i * NAR + d) * CAP, CAP), CAP))
        return c

    fetch(1)
    lax.fori_loop(1, GRP, serve, 0)
    keep.wait()
    to_scalars(g, 0).start()
    to_scalars(g, 0).wait()
    at, want = seeds16(0)
    for d in range(NAR):
        forward_marks(at, want, d)
    for d in range(1, NAR):
        serve_one(g, ys[d], pl.ds(d * CAP, CAP))
    pick(g, y, pl.ds(0, CAP))
    pulled[my_rows, :] = featb[0:CAP, :]

    for n, a in enumerate(shared):
        for d in range(1, NAR):
            link(a.at[y], a.at[y], nar_send.at[n, d - 1], nar_recv.at[n, d - 1], (y + d) % NAR).wait()
    for q in range(NAR):
        w2t[:, q * 128:(q + 1) * 128] = gw2t[q]
    last = jnp.concatenate([bias[0:1, 384:428], jnp.zeros((1, 84), F32)], axis=1)
    b2c[...] = jnp.concatenate([spread(bias[0:1, 256:384]), spread(last)], axis=0)

    def column(row):
        return jnp.concatenate([spread(row[:, c * 128:(c + 1) * 128]) for c in range(SEED // 128)], axis=0)

    for q in range(NAR):
        n = jnp.sum((gidx2[q, 1:1 + F2, :] >= 0).astype(F32), axis=0, keepdims=True)
        invc[q] = column(1.0 / jnp.maximum(n, 1.0))
    livec[...] = column(2.0 * LAM / HID / SEEDS_ALL * live[...].astype(F32))

    def backward_marks(b):
        q = b // 2
        r = gidx2[q] - y * FRONT
        lows[...] = r & 31
        inside = (r >= 0) & (r < FRONT)
        units = unit((r >> 5) & 7)
        for w in range(8):
            unit_of[w] = jnp.where(inside & ((r >> 8) == w), units, 0)
        selfs[...] = jnp.broadcast_to(r[0:1, :], (16, SEED))

        def column(c, carry2):
            lanes = pl.ds(pl.multiple_of(c * 128, 128), 128)
            accs = [jnp.zeros((32, 128), jnp.int32) for _ in range(8)]
            for k in range(1, 1 + F2):
                hit = sub32 == jnp.broadcast_to(lows[k:k + 1, lanes], (32, 128))
                for w in range(8):
                    u = jnp.broadcast_to(unit_of[w, k:k + 1, lanes], (32, 128))
                    accs[w] = accs[w] + jnp.where(hit, u, 0)
            for w in range(8):
                for j in range(8):
                    first = (w * 8 + j) * 32
                    bsel[q, first:first + 32, lanes] = count(accs[w], j)
            self_row = selfs[:, lanes].astype(jnp.int16)
            lanes = pl.ds(pl.multiple_of(SEED + c * 128, 128), 128)
            for t in range(FRONT // 16):
                here = iota16 + jnp.full((16, 128), t * 16, jnp.int32).astype(jnp.int16)
                bsel[q, t * 16:(t + 1) * 16, lanes] = jnp.where(here == self_row, one, zero)
            return carry2

        lax.fori_loop(b % 2 * 2, b % 2 * 2 + 2, column, 0)

    def sum_marks(i):
        at = pl.multiple_of(i // 2 * 16, 16)
        half = i % 2
        blk = idm[pl.ds(at, 16), :]
        keys, units = spread_columns(blk, range(1, 1 + F1)), spread_columns(blk, range(17, 17 + F1))
        for w in range(4):
            acc = word(lane32 + (half * 4 + w) * 128, keys, units)
            for j in range(8):
                col = pl.ds(pl.multiple_of(half * (SRC // 2) + (w * 8 + j) * 128, 128), 128)
                ssel[pl.ds(at, 16), col] = count(acc, j)

    def sum_ids(b):
        idm[...] = jnp.concatenate(keys_units(idxv[:, cols(b)]), axis=0).T

    def cols(b):
        return pl.ds(pl.multiple_of(b * 256, 256), 256)

    def one_mark(i, c):
        sum_marks(i)
        return c

    sum_ids(0)
    lax.fori_loop(0, 32, one_mark, 0)

    come = pulled.at[pl.ds(0, (DEV - 1) * CAP)]
    pltpu.make_async_copy(come, come, row_recv).wait()
    gone = featb.at[pl.ds(CAP, (DEV - 1) * CAP)]
    pltpu.make_async_copy(gone, gone, row_send).wait()
    sent = mid.at[:, pl.ds(0, GRP - 1)]
    pltpu.make_async_copy(sent, sent, req_send.at[0]).wait()

    def widen(i, c):
        rows = pl.ds(pl.multiple_of(i * 256, 256), 256)
        table[rows, :] = pulled[rows, :].astype(F32)
        return c

    lax.fori_loop(0, SRC // 256, widen, 0)
    table[SRC:SRC + 8, :] = jnp.zeros((8, D_IN), F32)
    for c in to_smem:
        c.wait()

    def forward(b):
        @pl.when(b % 2 == 0)
        def _():
            blk = gbuf.at[left, cols(b), :]
            link(blk, blk, h_send.at[0, b], h_recv.at[0, b], right).wait_recv()
            link(blk, blk, h_send.at[2, b], h_recv.at[2, b], right).start()

        @pl.when(b % 2 == 1)
        def _():
            blk = gbuf.at[right, cols(b), :]
            link(blk, blk, h_send.at[1, b], h_recv.at[1, b], left).wait_recv()
            link(blk, blk, h_send.at[2, b], h_recv.at[2, b], left).start()

    def own_row(b, i, j):
        m = b * 256 + i * 16 + j
        here = pl.ds(pl.multiple_of(i * 16, 16) + j, 1)
        own[here, :] = view[idx[0, m]]
        return m, here

    def load_sums(b, mark):
        backward_marks(b)

        def some(i, c):
            mark(i)
            for j in range(16):
                m, here = own_row(b, i, j)
                rows = [view[idx[1 + k, m]] for k in range(F1)]
                while len(rows) > 1:
                    rows = [p + q for p, q in zip(rows[::2], rows[1::2])] + ([rows[-1]] if len(rows) % 2 else [])
                near[here, :] = rows[0] * inv[0, m]
            return c

        lax.fori_loop(0, 16, some, 0)
        finish(b)

    def multiply_sums(b):
        backward_marks(b)

        def some(i, c):
            for j in range(16):
                own_row(b, i, j)
            return c

        lax.fori_loop(0, 16, some, 0)
        scale = jnp.concatenate(
            [spread(invv[0:1, pl.ds(pl.multiple_of(b * 256 + c * 128, 128), 128)]) for c in range(2)], axis=0
        )
        near[...] = dot(ssel[...], pulled[...]) * scale
        finish(b)

    def finish(b):
        rows = cols(b)
        act = jnp.concatenate([own[...].astype(BF), near[...].astype(BF)], axis=1)
        a1 = act.T
        for h in range(2):
            a1t[pl.ds(pl.multiple_of((2 * b + h) * 256, 256), 256), :] = a1[:, h * 128:(h + 1) * 128]
        z = dot(act, gw1[...].reshape(2 * D_IN, HID)) + bias[0:1, 0:HID]
        z1[rows, :] = z
        gbuf[y, rows, :] = (z / (1.0 + jnp.exp(-z))).astype(BF)
        blk = gbuf.at[y, rows, :]
        link(blk, blk, h_send.at[0, b], h_recv.at[0, b], right).start()
        link(blk, blk, h_send.at[1, b], h_recv.at[1, b], left).start()

        @pl.when(b > 0)
        def _():
            forward(b - 1)

    def loaded(b, c):
        load_sums(b, lambda i: None)
        return c

    multiply_sums(0)
    lax.fori_loop(1, 8, loaded, 0)
    forward(7)

    def from_source(q, fresh=False):
        def rows512(i, c):
            part = dot(fsel[q, pl.ds(pl.multiple_of(i * SEED, SEED), SEED), :], gbuf[q])
            for h in range(2):
                rows = pl.ds(pl.multiple_of(h * 2 * SEED + i * SEED, SEED), SEED)
                now = part[:, h * 128:(h + 1) * 128]
                tot[rows, :] = now if fresh else tot[rows, :] + now
            return c

        lax.fori_loop(0, 2, rows512, 0)

    from_source(y, True)
    for b in range(1, 8, 2):
        blk = gbuf.at[left, b * 256:(b + 1) * 256, :]
        link(blk, blk, h_send.at[0, b], h_recv.at[0, b], right).wait_recv()
    from_source(left)
    for b in range(0, 8, 2):
        blk = gbuf.at[right, b * 256:(b + 1) * 256, :]
        link(blk, blk, h_send.at[1, b], h_recv.at[1, b], left).wait_recv()
    from_source(right)
    for b in range(8):
        blk = gbuf.at[opp, b * 256:(b + 1) * 256, :]
        link(blk, blk, h_send.at[2, b], h_recv.at[2, b], right).wait_recv()
    from_source(opp)

    def wide(a):
        return jnp.concatenate([a, a], axis=1)

    def seeds(first):
        return jnp.concatenate([tot[h * 2 * SEED + first:h * 2 * SEED + first + SEED, :] for h in range(2)], axis=1)

    near2 = (seeds(0) * wide(invc[y])).astype(BF)
    self2 = seeds(SEED).astype(BF)
    alive = live[...].astype(F32)
    diff = self2.astype(F32) - near2.astype(F32)
    pull_apart = wide(livec[...]) * diff

    def swap_start(buf, ssem, rsem):
        blk = buf.at[y]
        link(blk, blk, ssem.at[0], rsem.at[0], right).start()
        link(blk, blk, ssem.at[1], rsem.at[1], left).start()

    def swap_forward(buf, ssem, rsem, cut):
        blk = buf.at[left]
        link(blk, blk, ssem.at[0], rsem.at[0], right).wait_recv()
        half = buf.at[left, 0:cut, :]
        link(half, half, ssem.at[2], rsem.at[2], right).start()
        blk = buf.at[right]
        link(blk, blk, ssem.at[1], rsem.at[1], left).wait_recv()
        half = buf.at[right, cut:, :]
        link(half, half, ssem.at[3], rsem.at[3], left).start()

    def swap_end(buf, ssem, rsem, cut):
        half = buf.at[opp, 0:cut, :]
        link(half, half, ssem.at[2], rsem.at[2], right).wait_recv()
        half = buf.at[opp, cut:, :]
        link(half, half, ssem.at[3], rsem.at[3], left).wait_recv()

    def swap_sent(buf, ssem, rsem, cut):
        blk = buf.at[y]
        link(blk, blk, ssem.at[0], rsem.at[0], right).wait_send()
        link(blk, blk, ssem.at[1], rsem.at[1], left).wait_send()
        half = buf.at[left, 0:cut, :]
        link(half, half, ssem.at[2], rsem.at[2], right).wait_send()
        half = buf.at[right, cut:, :]
        link(half, half, ssem.at[3], rsem.at[3], left).wait_send()

    rbuf[y] = pull_apart.astype(BF)
    swap_start(rbuf, r_send, r_recv)

    act2 = jnp.concatenate([self2, near2], axis=1)
    cls = lax.broadcasted_iota(jnp.int32, (CLS_PAD, SEED), 0)
    b2 = b2c[0:CLS_PAD, :]
    logits = dot(w2t[...], act2, NT) + jnp.concatenate([b2] * 4, axis=1)
    logits = jnp.where(cls < CLS, logits, -1e30)
    top = jnp.max(logits, axis=0, keepdims=True)
    e = jnp.exp(logits - top)
    tot = jnp.sum(e, axis=0, keepdims=True)
    hot = cls == labels[...]
    picked = jnp.sum(jnp.where(hot, logits, 0.0), axis=0, keepdims=True)
    dlog = (alive * (e * (1.0 / tot) - jnp.where(hot, 1.0, 0.0)) * (1.0 / SEEDS_ALL)).astype(BF)
    dbuf[y] = dlog
    swap_start(dbuf, d_send, d_recv)

    loss = jnp.sum(alive * (top + jnp.log(tot) - picked), axis=1, keepdims=True)
    loss = loss + SEEDS_ALL / 2 * jnp.sum(pull_apart * diff, keepdims=True)
    g2t = dot(dlog, act2).astype(BF)
    for q in range(NAR):
        pay2[q * Q2:q * Q2 + CLS_PAD, :] = g2t[:, q * 128:(q + 1) * 128]
        pay2[q * Q2 + CLS_PAD:(q + 1) * Q2, :] = jnp.zeros((Q2 - CLS_PAD, 128), BF)

    def to_owner(pay, inbox, first, count, n):
        def body(i, c):
            t = (g + i) % GRP
            p = t - first

            @pl.when((p >= 0) & (p < count))
            def _():
                pltpu.make_async_remote_copy(
                    src_ref=pay.at[pl.ds(pl.multiple_of(p * PIECE, PIECE), PIECE)], dst_ref=inbox.at[g],
                    send_sem=rs_send.at[n], recv_sem=rs_recv.at[n], device_id=(t, y), device_id_type=MESH,
                ).start()

            return c

        lax.fori_loop(1, GRP, body, 0)

    def mine(first, count):
        p = g - first
        return (p >= 0) & (p < count), pl.ds(pl.multiple_of(p * PIECE, PIECE), PIECE)

    def add_first_momentum(p):
        rows = pl.ds(pl.multiple_of(p % 2 * PIECE, PIECE), PIECE)
        for h in range(2):
            @pl.when((y == p % 8 // 2) & (p // 8 == h))
            def _(h=h):
                ybox1[y] = ybox1[y] + MU * m1[rows, h * 128:(h + 1) * 128]

    def add_second_momentum(p):
        @pl.when(y == p // (Q2 // PIECE))
        def _():
            rows = pl.ds(pl.multiple_of(p % (Q2 // PIECE) * PIECE, PIECE), PIECE)
            ybox2[y] = ybox2[y] + MU * m2pad[rows, :]

    def add_plane(pay, inbox, ybox, first, count, n, add_momentum):
        here, rows = mine(first, count)

        @pl.when(here)
        def _():
            got = inbox.at[pl.ds(0, GRP - 1)]
            pltpu.make_async_copy(got, got, rs_recv.at[n]).wait()
            inbox[g] = pay[rows, :]
            ybox[y] = jnp.sum(inbox[...].astype(F32), axis=0)
            add_momentum(g - first)
            for d in range(1, NAR):
                link(ybox.at[y], ybox.at[y], y_send.at[n, d - 1], y_recv.at[n, d - 1], ys[d]).start()

    def add_group(ybox, res, first, count, n):
        here, rows = mine(first, count)

        @pl.when(here)
        def _():
            for d in range(1, NAR):
                link(ybox.at[y], ybox.at[y], y_send.at[n, d - 1], y_recv.at[n, d - 1], ys[d]).wait()
            res[rows, :] = (ybox[0] + ybox[1]) + (ybox[2] + ybox[3])

            def tell(i, c):
                pltpu.make_async_remote_copy(
                    src_ref=res.at[rows], dst_ref=res.at[rows], send_sem=ag_send.at[n], recv_sem=ag_recv.at[n],
                    device_id=((g + i) % GRP, y), device_id_type=MESH,
                ).start()
                return c

            lax.fori_loop(1, GRP, tell, 0)

    def take(res, first, count, n):
        here, rows = mine(first, count)
        for less, when in ((1, here), (0, jnp.logical_not(here))):
            @pl.when(when)
            def _(less=less):
                got = res.at[pl.ds(0, (count - less) * PIECE)]
                pltpu.make_async_copy(got, got, ag_recv.at[n]).wait()

    def sums_sent(pay, first, count, n):
        here, rows = mine(first, count)
        for less, when in ((1, here), (0, jnp.logical_not(here))):
            @pl.when(when)
            def _(less=less):
                gone = pay.at[pl.ds(0, (count - less) * PIECE)]
                pltpu.make_async_copy(gone, gone, rs_send.at[n]).wait()

        @pl.when(here)
        def _():
            gone = table.at[pl.ds(0, (GRP - 1) * PIECE)]
            pltpu.make_async_copy(gone, gone, ag_send.at[n]).wait()

    to_owner(pay2, inbox2, GRP - P2, P2, 1)

    def add_grads(q, fresh=False):
        da = dot(dbuf[q], w2t[...], TN)
        r = rbuf[q].astype(F32)
        ds = (da[:, :HID] + r).astype(BF)
        dn = ((da[:, HID:] - r) * wide(invc[q])).astype(BF)
        both = jnp.concatenate([dn, ds], axis=0)

        def rows512(i, c):
            part = dot(bsel[q, pl.ds(pl.multiple_of(i * 512, 512), 512), :], both)
            for h in range(2):
                rows = pl.ds(pl.multiple_of(h * FRONT + i * 512, 512), 512)
                now = part[:, h * 128:(h + 1) * 128]
                dh1[rows, :] = now if fresh else dh1[rows, :] + now
            return c

        lax.fori_loop(0, FRONT // 512, rows512, 0)

    db2 = jnp.sum(dlog.astype(F32), axis=1, keepdims=True)
    db2 = jnp.broadcast_to(db2, (CLS_PAD, 128)).T[0:1, :]
    swap_forward(rbuf, r_send, r_recv, SEED // 2)
    add_grads(y, True)
    swap_forward(dbuf, d_send, d_recv, 96)
    add_grads(left)
    add_grads(right)
    add_plane(pay2, inbox2, ybox2, GRP - P2, P2, 1, add_second_momentum)
    swap_end(rbuf, r_send, r_recv, SEED // 2)
    swap_end(dbuf, d_send, d_recv, 96)
    add_group(ybox2, res2, GRP - P2, P2, 1)
    add_grads(opp)

    def to_z(b, db):
        rows = pl.ds(pl.multiple_of(b * 256, 256), 256)
        z = z1[rows, :]
        sig = 1.0 / (1.0 + jnp.exp(-z))
        dh = jnp.concatenate(
            [dh1[pl.ds(pl.multiple_of(h * FRONT + b * 256, 256), 256), :] for h in range(2)], axis=1
        )
        dz = (dh * sig * (1.0 + z * (1.0 - sig))).astype(BF)
        a1 = jnp.concatenate(
            [a1t[pl.ds(pl.multiple_of((2 * b + h) * 256, 256), 256), :] for h in range(2)], axis=1
        )
        part = dot(a1, dz)
        for h in range(2):
            now = slice(h * 256, (h + 1) * 256)
            gsum[now, :] = gsum[now, :] + part[:, h * 128:(h + 1) * 128]
        return db + jnp.sum(dz.astype(F32), axis=0, keepdims=True)

    gsum[...] = jnp.zeros((512, 128), F32)
    db1 = lax.fori_loop(0, FRONT // 256, to_z, jnp.zeros((1, HID), F32))
    pay1[0:512, :] = gsum[...].astype(BF)
    misc[...] = jnp.zeros((PIECE, 128), F32)

    def two(rows, v):
        hi = v.astype(BF).astype(F32)
        misc[rows:rows + 1, 0:v.shape[1]] = hi
        misc[rows + 4:rows + 5, 0:v.shape[1]] = v - hi

    two(0, db1[:, :128])
    two(1, db1[:, 128:])
    two(2, db2[:, :128])
    two(3, db2[:, 128:])
    hi = loss.astype(BF).astype(F32)
    misc[8:9, 0:1] = hi
    misc[9:10, 0:1] = loss - hi
    pay1[512:544, :] = misc[...].astype(BF)
    to_owner(pay1, inbox1, 0, P1, 0)

    take(res2, GRP - P2, P2, 1)
    mom2 = jnp.concatenate([res2[q * Q2:q * Q2 + CLS_PAD, :] for q in range(NAR)], axis=1)
    for q in range(NAR):
        x2s[q] = mom2[:, q * 128:(q + 1) * 128]
    o_all[ROW_M2:ROW_M2 + CLS_PAD, :] = x2s[y]
    x2 = mom2 * (1.0 / (jnp.sqrt(jnp.sum(mom2 * mom2, keepdims=True)) + 1e-07))
    x2 = ns_step(x2)
    add_plane(pay1, inbox1, ybox1, 0, P1, 0, add_first_momentum)
    x2 = ns_step(x2)
    add_group(ybox1, o_all, 0, P1, 0)
    for _ in range(NS_ITERS - 2):
        x2 = ns_step(x2)
    for q in range(NAR):
        x2s[q] = x2[:, q * 128:(q + 1) * 128]
    o_all[ROW_X2:ROW_X2 + CLS_PAD, :] = x2s[y]
    take(o_all, 0, P1, 0)

    for b in range(8):
        blk = gbuf.at[y, b * 256:(b + 1) * 256, :]
        link(blk, blk, h_send.at[0, b], h_recv.at[0, b], right).wait_send()
        link(blk, blk, h_send.at[1, b], h_recv.at[1, b], left).wait_send()
        blk = gbuf.at[opp, b * 256:(b + 1) * 256, :]
        link(blk, blk, h_send.at[2, b], h_recv.at[2, b], right).wait_send()
    swap_sent(rbuf, r_send, r_recv, SEED // 2)
    swap_sent(dbuf, d_send, d_recv, 96)

    sums_sent(pay2, GRP - P2, P2, 1)
    sums_sent(pay1, 0, P1, 0)


def main(reqt, feat, idx1t, msk1t, idx2t, msk2t, labels, live, w1, w2own, m1, m2own, bias):
    vm = pl.BlockSpec(memory_space=pltpu.VMEM)
    dma = pltpu.SemaphoreType.DMA
    sds = jax.ShapeDtypeStruct
    V = pltpu.VMEM
    return pl.pallas_call(
        main_kernel,
        out_shape=sds((ROWS, 128), F32),
        in_specs=[vm, pl.BlockSpec(memory_space=pl.ANY)] + [vm] * 11,
        out_specs=vm,
        scratch_shapes=[
            V((SRC + 8, D_IN), F32),
            V((OWN, D_IN), BF),
            V((SRC, D_IN), BF),
            V((CAP, D_IN), F32),
            V((DEV, 128), jnp.int32),
            V((DEV, 128), jnp.int32),
            V((NAR, GRP, 1, 128), jnp.int32),
            V((16, FRONT), jnp.int32),
            V((1, FRONT), F32),
            V((256, D_IN), F32),
            V((256, D_IN), F32),
            V((FRONT, HID), F32),
            V((NAR, FRONT, HID), BF),
            V((NAR, 2 * SEED, FRONT), BF),
            V((NAR, FRONT, 2 * SEED), BF),
            V((8, 16, SEED), jnp.int32),
            V((16, SEED), jnp.int32),
            V((16, SEED), jnp.int32),
            V((SEED, 32), jnp.int32),
            V((256, SRC), BF),
            V((256, 32), jnp.int32),
            V((NAR, SEED, 128), F32),
            V((SEED, 128), F32),
            V((NAR, SEED, HID), BF),
            V((NAR, CLS_PAD, SEED), BF),
            V((NAR, 64, HID), BF),
            V((NAR, CLS_PAD, 128), BF),
            V((Q2, 128), F32),
            V((NAR, 16, SEED), jnp.int32),
            V((CLS_PAD, 2 * HID), BF),
            V((HID, 128), F32),
            V((P1 * PIECE, 128), BF),
            V((P2 * PIECE, 128), BF),
            V((PIECE, 128), F32),
            V((GRP, PIECE, 128), BF),
            V((GRP, PIECE, 128), BF),
            V((NAR, PIECE, 128), F32),
            V((NAR, PIECE, 128), F32),
            V((P2 * PIECE, 128), F32),
            V((NAR, CLS_PAD, 128), F32),
            pltpu.SMEM((DEV, 1, 128), jnp.int32),
            pltpu.SMEM((16, FRONT), jnp.int32),
            pltpu.SMEM((1, FRONT), F32),
            dma, dma((3,)), dma((GRP,)), dma((NAR,)), dma((NAR,)), dma((GRP,)), dma, dma, dma((3, 3)), dma((3, 3)),
            dma((3, 8)), dma((3, 8)), dma((4,)), dma((4,)), dma((4,)), dma((4,)),
            dma((2,)), dma((2,)), dma((2, 3)), dma((2, 3)), dma((2,)), dma((2,)),
        ],
        compiler_params=pltpu.CompilerParams(
            collective_id=0, has_side_effects=True, vmem_limit_bytes=62 * 2**20
        ),
    )(reqt, feat, idx1t, msk1t, idx2t, msk2t, labels, live, w1, w2own, m1, m2own, bias)


def update_kernel(
    res, w1own, w2own, bias, biasm, biasv,
    o_loss, o_first, o_second, o_mom1, o_mom2, o_flow, o_slow, o_bias, o_bm, o_bv,
    x1s,
):
    y = lax.axis_index("nar")
    mom1 = jnp.concatenate([res[0:256, :], res[256:512, :]], axis=1)
    x1s[...] = mom1
    block64 = pl.ds(pl.multiple_of(y * 64, 64), 64)
    o_mom1[...] = x1s[block64, :]
    x1 = mom1 * (1.0 / (jnp.sqrt(jnp.sum(mom1 * mom1, keepdims=True)) + 1e-07))
    for _ in range(NS_ITERS):
        x1 = ns_step(x1)
    x1s[...] = x1
    first_new = w1own[...] * (1.0 - WDECAY) - x1s[block64, :]
    o_first[...] = first_new
    o_flow[...] = first_new.astype(BF)
    second = w2own[...] * (1.0 - WDECAY) - (2 * HID / CLS) ** 0.5 * res[ROW_X2:ROW_X2 + CLS, :]
    o_second[...] = second
    o_slow[...] = second.astype(BF)
    o_mom2[...] = res[ROW_M2:ROW_M2 + CLS, :]

    gb = res[512:516, :] + res[516:520, :]
    gb = jnp.concatenate([gb[0:1, :], gb[1:2, :], gb[2:3, :], gb[3:4, 0:44]], axis=1)
    m_new = BETA_ONE * biasm[...] + (1.0 - BETA_ONE) * gb
    v_new = BETA_TWO * biasv[...] + (1.0 - BETA_TWO) * gb * gb
    m_hat = m_new / (1.0 - BETA_ONE**STEP)
    v_hat = v_new / (1.0 - BETA_TWO**STEP)
    o_bias[...] = bias[...] * (1.0 - LR_BIAS * WDECAY) - LR_BIAS * m_hat / (jnp.sqrt(v_hat) + EPSILON)
    o_bm[...] = m_new
    o_bv[...] = v_new
    o_loss[...] = res[520:521, 0:1] + res[521:522, 0:1]


def update(*args):
    vm = pl.BlockSpec(memory_space=pltpu.VMEM)
    sds = jax.ShapeDtypeStruct
    return pl.pallas_call(
        update_kernel,
        out_shape=[
            sds((1, 1), F32), sds((64, HID), F32), sds((CLS, 128), F32), sds((64, HID), F32), sds((CLS, 128), F32),
            sds((64, HID), BF), sds((CLS, 128), BF), sds((1, 428), F32), sds((1, 428), F32), sds((1, 428), F32),
        ],
        in_specs=[vm] * 6,
        out_specs=[vm] * 10,
        scratch_shapes=[pltpu.VMEM((2 * D_IN, HID), F32)],
        compiler_params=pltpu.CompilerParams(vmem_limit_bytes=32 * 2**20),
    )(*args)


def per_device(
    features, requests, index_one, mask_one, index_two, mask_two, labels, seed_live,
    w_first, w_second, mom_first, mom_second, biases, bias_m, bias_v,
):
    w2own, bias = w_second.T, biases[None, :]
    res = main(
        requests.T, features, index_one.T, mask_one.T, index_two.T, mask_two.T, labels[None, :], seed_live[None, :],
        w_first, w2own, mom_first, mom_second.T, bias,
    )
    loss, first_new, second_new, mom_one, mom_two, first_low, second_low, bias_new, m_new, v_new = update(
        res, w_first, w2own, bias, bias_m[None, :], bias_v[None, :]
    )
    return (
        loss.reshape(()), first_new, second_new.T, mom_one, mom_two.T, first_low, second_low.T,
        bias_new.reshape(-1), m_new.reshape(-1), v_new.reshape(-1),
    )


def solution(mesh):
    both = ("grp", "nar")
    placed = (
        P(both, None), P(both, None), P(both, None), P(both, None), P(both, None), P(both, None),
        P(both), P(both), P("nar", None), P("nar", None), P("nar", None), P("nar", None), P(), P(), P(),
    )
    nar = P("nar", None)
    return jax.shard_map(
        per_device, mesh=mesh, in_specs=placed,
        out_specs=(P(), nar, nar, nar, nar, nar, nar, P(), P(), P()), check_vma=False,
    )
```

```python
import functools

import jax
import jax.numpy as jnp
from jax import lax
from jax.experimental import pallas as pl
from jax.experimental.pallas import tpu as pltpu
from jax.sharding import PartitionSpec as P

HID = 256
CLS = 172
CLS_PAD = 176
D_IN = 128
F1 = 15
F2 = 10
NS_ITERS = 5
STEP = 10
LAM = 0.5
MU = 0.95
WDECAY = 0.01
LR_BIAS = 0.05
BETA_ONE = 0.9
BETA_TWO = 0.999
EPSILON = 1e-08
NS_A = 3.4445
NS_B = -4.775
NS_C = 2.0315
HIGH = lax.Precision.HIGHEST
MESH = pl.DeviceIdType.MESH
BF = jnp.bfloat16
F32 = jnp.float32

DEV = 128
NAR = 4
OWN = 8192
CAP = 64
SRC = 8192
FRONT = 2048
SEED = 512


def all_to(t):
    return (t // NAR, t % NAR)


PIECE = 32
P1 = 17
Q2 = 192
P2 = 24
GRP = 32
ROW_M2 = P1 * PIECE
ROW_X2 = ROW_M2 + CLS_PAD
ROWS = ROW_X2 + NAR * CLS_PAD
SEEDS_ALL = SEED * DEV


def dot(a, b, dims=((1,), (0,))):
    return lax.dot_general(a, b, (dims, ((), ())), preferred_element_type=F32)


NN = ((1,), (0,))
NT = ((1,), (1,))
TN = ((0,), (0,))


def split(a):
    hi = a.astype(BF)
    return hi, (a - hi.astype(F32)).astype(BF)


def dot3(a, b, dims):
    (ah, al), (bh, bl) = a, b
    return dot(
        jnp.concatenate([ah, ah, al], axis=dims[0][0]), jnp.concatenate([bh, bl, bh], axis=dims[1][0]), dims
    )


def ns_step(x):
    xs = split(x)
    gram = dot3(xs, xs, NT)
    gs = split(gram)
    mix = NS_B * gram + NS_C * dot3(gs, gs, NN)
    return NS_A * x + dot3(split(mix), xs, NN)


def spread(row):
    return jnp.broadcast_to(row, (128, 128)).T


def main_kernel(
    reqt, feat, idx1t, msk1t, idx2t, msk2t, labels, live, w1, w2own, m1, m2own, bias,
    o_all,
    table, featb, pulled, stage, reqv, reqin, mid, idxv, idxp, invv, near, own, slope, gbuf, fsel, bsel, unit_of, lows, selfs, idc, ssel, idm, invc, livec, rbuf, dbuf,
    gw1, gw2t, m2pad, gidx2, w2t, b2c, pay1, pay2, misc, inbox1, inbox2, ybox1, ybox2, res2, x2s,
    reqs, idx,
    feat_sem, loc_sem, ask_sem, req_send, mid_recv, req_recv, row_send, row_recv, nar_send, nar_recv,
    h_send, h_recv, r_send, r_recv, d_send, d_recv, rs_send, rs_recv, y_send, y_recv, ag_send, ag_recv,
):
    a1t, dh1, tot, gsum = featb, table, table.at[2 * FRONT:3 * FRONT], table.at[3 * FRONT:3 * FRONT + 512]
    g = lax.axis_index("grp")
    y = lax.axis_index("nar")
    me = g * NAR + y
    left, right, opp = (y + 3) % NAR, (y + 1) % NAR, (y + 2) % NAR

    load = pltpu.make_async_copy(feat, featb, feat_sem)
    load.start()

    barrier = pltpu.get_barrier_semaphore()

    ys = [(y + d) % NAR for d in range(NAR)]

    def greet(i, c):
        pl.semaphore_signal(barrier, inc=1, device_id=((g + i) % GRP, y), device_id_type=MESH)
        return c

    for d in range(1, NAR):
        pl.semaphore_signal(barrier, inc=1, device_id=(g, ys[d]), device_id_type=MESH)
    lax.fori_loop(1, GRP, greet, 0)

    def link(src, dst, ssem, rsem, to):
        return pltpu.make_async_remote_copy(
            src_ref=src, dst_ref=dst, send_sem=ssem, recv_sem=rsem, device_id=(g, to), device_id_type=MESH
        )

    reqv[...] = jnp.concatenate([reqt[...], jnp.zeros((DEV - CAP, DEV), jnp.int32)], axis=0).T
    ask_rows = reqv.reshape(GRP, NAR, 1, 128)
    got_rows = reqin.reshape(DEV, 1, 128)

    gw1[y] = w1[...].astype(BF)
    pad = CLS_PAD - CLS
    gw2t[y] = jnp.concatenate([w2own[...], jnp.zeros((pad, 128), F32)], axis=0).astype(BF)
    m2pad[...] = jnp.concatenate([m2own[...], jnp.zeros((Q2 - CLS, 128), F32)], axis=0)
    gidx2[y] = jnp.concatenate(
        [idx2t[0:1, :], jnp.where(msk2t[...] > 0, idx2t[1:, :], -1), jnp.zeros((5, SEED), jnp.int32)], axis=0
    )
    shared = (gidx2, gw1, gw2t)

    pl.semaphore_wait(barrier, GRP + NAR - 2)

    def ask_group(d):
        return pltpu.make_async_remote_copy(
            src_ref=ask_rows.at[:, ys[d]], dst_ref=mid.at[y], send_sem=req_send.at[d], recv_sem=mid_recv.at[d],
            device_id=(g, ys[d]), device_id_type=MESH,
        )

    for d in range(1, NAR):
        ask_group(d).start()
    keep = pltpu.make_async_copy(ask_rows.at[:, y], mid.at[y], loc_sem.at[2])
    keep.start()
    for n, a in enumerate(shared):
        for d in range(1, NAR):
            link(a.at[y], a.at[y], nar_send.at[n, d - 1], nar_recv.at[n, d - 1], (y + d) % NAR).start()

    msk = msk1t[...]
    idxv[0:1, :] = idx1t[0:1, :]
    idxv[1:16, :] = jnp.where(msk > 0, idx1t[1:16, :], SRC)
    invv[...] = 1.0 / jnp.maximum(jnp.sum(msk.astype(F32), axis=0, keepdims=True), 1.0)
    for half in range(2):
        parts = []
        for r in range(8):
            parts.append(jnp.concatenate(
                [idxv[:, (half * 4 + b) * 256 + r * 32:(half * 4 + b) * 256 + r * 32 + 32] for b in range(4)], axis=1
            ))
        idxp[half * 128:(half + 1) * 128, :] = jnp.concatenate(parts, axis=0).T
    to_smem = [pltpu.make_async_copy(idxp, idx, loc_sem.at[0])]
    for c in to_smem:
        c.start()

    keep.wait()
    for d in range(1, NAR):
        ask_group(d).wait()
    own_rows = pl.ds(pl.multiple_of(g * NAR, NAR), NAR)

    def ask(i, c):
        n = (i * 13) % GRP
        t = (g + n) % GRP
        pltpu.make_async_remote_copy(
            src_ref=mid.at[:, t], dst_ref=got_rows.at[own_rows], send_sem=req_send.at[0], recv_sem=req_recv.at[n],
            device_id=(t, y), device_id_type=MESH,
        ).start()
        return c

    lax.fori_loop(1, GRP, ask, 0)
    keep = pltpu.make_async_copy(mid.at[:, g], got_rows.at[own_rows], loc_sem.at[2])
    keep.start()

    load.wait()

    def widen_features(i, c):
        rows = pl.ds(pl.multiple_of(i * 256, 256), 256)
        table[rows, :] = featb[rows, :].astype(F32)
        return c

    lax.fori_loop(0, OWN // 256, widen_features, 0)

    lane32 = lax.broadcasted_iota(jnp.int32, (16, 128), 1)
    sub32 = lax.broadcasted_iota(jnp.int32, (32, 128), 0)
    lane16 = lane32.astype(jnp.int16)
    iota16 = lax.broadcasted_iota(jnp.int32, (16, 128), 0).astype(jnp.int16)
    one, zero = jnp.ones((16, 128), BF), jnp.zeros((16, 128), BF)

    def unit(digit):
        v = jnp.ones_like(digit)
        for j in range(1, 8):
            v = jnp.where(digit == j, 1 << 4 * j, v)
        return v

    def count(acc, j):
        return ((acc >> (4 * j)) & 15).astype(F32).astype(BF)

    def keys_units(ids):
        return (ids & 127) + (ids >> 10) * 128, unit((ids >> 7) & 7)

    def word(pos, keys, units):
        acc = jnp.zeros((16, 128), jnp.int32)
        for k, u in zip(keys, units):
            acc = acc + jnp.where(pos == k, u, 0)
        return acc

    def spread_columns(blk, ks):
        return [jnp.broadcast_to(blk[:, k:k + 1], (16, 128)) for k in ks]

    ids = gidx2[y]
    keys, units = keys_units(ids)
    idc[...] = jnp.concatenate([ids[0:1, :], keys[1:, :], units], axis=0).T

    def seeds16(i):
        at = pl.multiple_of(i * 16, 16)
        blk = idc[pl.ds(at, 16), :]
        self_row = jnp.broadcast_to(blk[:, 0:1], (16, 128)).astype(jnp.int16)
        return at, (spread_columns(blk, range(1, 1 + F2)), spread_columns(blk, range(17, 17 + F2)), self_row)

    def forward_marks(at, want, q):
        keys, units, self_row = want
        for w in range(2):
            acc = word(lane32 + 128 * (2 * q + w), keys, units)
            for j in range(8):
                c = w * 8 + j
                fsel[q, pl.ds(at, 16), c * 128:(c + 1) * 128] = count(acc, j)
                here = lane16 + jnp.full((16, 128), q * FRONT + c * 128, jnp.int32).astype(jnp.int16)
                fsel[q, pl.ds(SEED + at, 16), c * 128:(c + 1) * 128] = jnp.where(here == self_row, one, zero)

    view = table.reshape(SRC + 8, 1, D_IN)
    my_rows = pl.ds(pl.multiple_of(me * CAP, CAP), CAP)

    def pick(t, u, slot):
        for r in range(CAP):
            stage[r:r + 1, :] = view[reqs[t * NAR + u, 0, r]]
        featb[slot, :] = stage[...].astype(BF)

    def serve_one(t, u, slot):
        pick(t, u, slot)
        pltpu.make_async_remote_copy(
            src_ref=featb.at[slot], dst_ref=pulled.at[my_rows],
            send_sem=row_send, recv_sem=row_recv, device_id=(t, u), device_id_type=MESH,
        ).start()

    def asked(n):
        rows = got_rows.at[pl.ds(0, NAR)]
        pltpu.make_async_copy(rows, rows, req_recv.at[n]).wait()

    def to_scalars(t, n):
        rows = pl.ds(pl.multiple_of(t * NAR, NAR), NAR)
        return pltpu.make_async_copy(got_rows.at[rows], reqs.at[rows], ask_sem.at[n])

    def whose(i):
        n = (i * 13) % GRP
        return n, (g + GRP - n) % GRP

    def fetch(i):
        n, t = whose(i)
        asked(n)
        to_scalars(t, n).start()

    def serve(i, c):
        n, t = whose(i)

        @pl.when(i < GRP - 1)
        def _():
            fetch(i + 1)

        to_scalars(t, n).wait()
        at, want = seeds16(i)
        for d in range(NAR):
            forward_marks(at, want, d)
            serve_one(t, ys[d], pl.ds(pl.multiple_of((i * NAR + d) * CAP, CAP), CAP))
        return c

    fetch(1)
    lax.fori_loop(1, GRP, serve, 0)
    keep.wait()
    to_scalars(g, 0).start()
    to_scalars(g, 0).wait()
    at, want = seeds16(0)
    for d in range(NAR):
        forward_marks(at, want, d)
    for d in range(1, NAR):
        serve_one(g, ys[d], pl.ds(d * CAP, CAP))
    pick(g, y, pl.ds(0, CAP))
    pulled[my_rows, :] = featb[0:CAP, :]

    for n, a in enumerate(shared):
        for d in range(1, NAR):
            link(a.at[y], a.at[y], nar_send.at[n, d - 1], nar_recv.at[n, d - 1], (y + d) % NAR).wait()
    for q in range(NAR):
        w2t[:, q * 128:(q + 1) * 128] = gw2t[q]
    last = jnp.concatenate([bias[0:1, 384:428], jnp.zeros((1, 84), F32)], axis=1)
    b2c[...] = jnp.concatenate([spread(bias[0:1, 256:384]), spread(last)], axis=0)

    def column(row):
        return jnp.concatenate([spread(row[:, c * 128:(c + 1) * 128]) for c in range(SEED // 128)], axis=0)

    for q in range(NAR):
        n = jnp.sum((gidx2[q, 1:1 + F2, :] >= 0).astype(F32), axis=0, keepdims=True)
        invc[q] = column(1.0 / jnp.maximum(n, 1.0))
    livec[...] = column(2.0 * LAM / HID / SEEDS_ALL * live[...].astype(F32))

    def backward_marks(q, carry):
        r = gidx2[q] - y * FRONT
        lows[...] = r & 31
        inside = (r >= 0) & (r < FRONT)
        units = unit((r >> 5) & 7)
        for w in range(8):
            unit_of[w] = jnp.where(inside & ((r >> 8) == w), units, 0)
        selfs[...] = jnp.broadcast_to(r[0:1, :], (16, SEED))

        def column(c, carry2):
            lanes = pl.ds(pl.multiple_of(c * 128, 128), 128)
            accs = [jnp.zeros((32, 128), jnp.int32) for _ in range(8)]
            for k in range(1, 1 + F2):
                hit = sub32 == jnp.broadcast_to(lows[k:k + 1, lanes], (32, 128))
                for w in range(8):
                    u = jnp.broadcast_to(unit_of[w, k:k + 1, lanes], (32, 128))
                    accs[w] = accs[w] + jnp.where(hit, u, 0)
            for w in range(8):
                for j in range(8):
                    first = (w * 8 + j) * 32
                    bsel[q, first:first + 32, lanes] = count(accs[w], j)
            self_row = selfs[:, lanes].astype(jnp.int16)
            lanes = pl.ds(pl.multiple_of(SEED + c * 128, 128), 128)
            for t in range(FRONT // 16):
                here = iota16 + jnp.full((16, 128), t * 16, jnp.int32).astype(jnp.int16)
                bsel[q, t * 16:(t + 1) * 16, lanes] = jnp.where(here == self_row, one, zero)
            return carry2

        lax.fori_loop(0, SEED // 128, column, 0)
        return carry

    def sum_marks(i):
        at = pl.multiple_of(i // 2 * 16, 16)
        half = i % 2
        blk = idm[pl.ds(at, 16), :]
        keys, units = spread_columns(blk, range(1, 1 + F1)), spread_columns(blk, range(17, 17 + F1))
        for w in range(4):
            acc = word(lane32 + (half * 4 + w) * 128, keys, units)
            for j in range(8):
                col = pl.ds(pl.multiple_of(half * (SRC // 2) + (w * 8 + j) * 128, 128), 128)
                ssel[pl.ds(at, 16), col] = count(acc, j)

    def sum_ids(b):
        idm[...] = jnp.concatenate(keys_units(idxv[:, cols(b)]), axis=0).T

    def cols(b):
        return pl.ds(pl.multiple_of(b * 256, 256), 256)

    def one_mark(i, c):
        sum_marks(i)
        return c

    sum_ids(0)
    lax.fori_loop(0, 32, one_mark, 0)
    lax.fori_loop(0, NAR, backward_marks, 0)

    come = pulled.at[pl.ds(0, (DEV - 1) * CAP)]
    pltpu.make_async_copy(come, come, row_recv).wait()
    gone = featb.at[pl.ds(CAP, (DEV - 1) * CAP)]
    pltpu.make_async_copy(gone, gone, row_send).wait()
    sent = mid.at[:, pl.ds(0, GRP - 1)]
    pltpu.make_async_copy(sent, sent, req_send.at[0]).wait()

    def widen(i, c):
        rows = pl.ds(pl.multiple_of(i * 256, 256), 256)
        table[rows, :] = pulled[rows, :].astype(F32)
        return c

    lax.fori_loop(0, SRC // 256, widen, 0)
    table[SRC:SRC + 8, :] = jnp.zeros((8, D_IN), F32)
    for c in to_smem:
        c.wait()

    def forward(b):
        @pl.when(b % 2 == 0)
        def _():
            blk = gbuf.at[left, cols(b), :]
            link(blk, blk, h_send.at[0, b], h_recv.at[0, b], right).wait_recv()
            link(blk, blk, h_send.at[2, b], h_recv.at[2, b], right).start()

        @pl.when(b % 2 == 1)
        def _():
            blk = gbuf.at[right, cols(b), :]
            link(blk, blk, h_send.at[1, b], h_recv.at[1, b], left).wait_recv()
            link(blk, blk, h_send.at[2, b], h_recv.at[2, b], left).start()

    def load_sums(b):
        def some(i, c):
            for e in range(2):
                line = b * 32 + 2 * i + e
                for r in range(8):
                    here = pl.ds(r * 32 + 2 * i + e, 1)
                    own[here, :] = view[idx[line, r * 16]]
                    rows = [view[idx[line, r * 16 + 1 + k]] for k in range(F1)]
                    while len(rows) > 1:
                        rows = [p + q for p, q in zip(rows[::2], rows[1::2])] + ([rows[-1]] if len(rows) % 2 else [])
                    near[here, :] = rows[0]
            return c

        lax.fori_loop(0, 16, some, 0)
        finish(b)

    def multiply_sums(b):
        def some(i, c):
            for e in range(2):
                for r in range(8):
                    own[pl.ds(r * 32 + 2 * i + e, 1), :] = view[idx[b * 32 + 2 * i + e, r * 16]]
            return c

        lax.fori_loop(0, 16, some, 0)
        near[...] = dot(ssel[...], pulled[...])
        finish(b)

    def finish(b):
        rows = cols(b)
        scale = jnp.concatenate(
            [spread(invv[0:1, pl.ds(pl.multiple_of(b * 256 + c * 128, 128), 128)]) for c in range(2)], axis=0
        )
        act = jnp.concatenate([own[...].astype(BF), (near[...] * scale).astype(BF)], axis=1)
        a1 = act.T
        for h in range(2):
            a1t[pl.ds(pl.multiple_of((2 * b + h) * 256, 256), 256), :] = a1[:, h * 128:(h + 1) * 128]
        z = dot(act, gw1[...].reshape(2 * D_IN, HID)) + bias[0:1, 0:HID]
        sig = 1.0 / (1.0 + jnp.exp(-z))
        h1 = z * sig
        slope[rows, :] = sig + h1 * (1.0 - sig)
        gbuf[y, rows, :] = h1.astype(BF)
        blk = gbuf.at[y, rows, :]
        link(blk, blk, h_send.at[0, b], h_recv.at[0, b], right).start()
        link(blk, blk, h_send.at[1, b], h_recv.at[1, b], left).start()

        @pl.when(b > 0)
        def _():
            forward(b - 1)

    def loaded(b, c):
        load_sums(b)
        return c

    multiply_sums(0)
    lax.fori_loop(1, 8, loaded, 0)
    forward(7)

    def from_source(q, fresh=False):
        def rows512(i, c):
            part = dot(fsel[q, pl.ds(pl.multiple_of(i * SEED, SEED), SEED), :], gbuf[q])
            for h in range(2):
                rows = pl.ds(pl.multiple_of(h * 2 * SEED + i * SEED, SEED), SEED)
                now = part[:, h * 128:(h + 1) * 128]
                tot[rows, :] = now if fresh else tot[rows, :] + now
            return c

        lax.fori_loop(0, 2, rows512, 0)

    from_source(y, True)
    for b in range(1, 8, 2):
        blk = gbuf.at[left, b * 256:(b + 1) * 256, :]
        link(blk, blk, h_send.at[0, b], h_recv.at[0, b], right).wait_recv()
    from_source(left)
    for b in range(0, 8, 2):
        blk = gbuf.at[right, b * 256:(b + 1) * 256, :]
        link(blk, blk, h_send.at[1, b], h_recv.at[1, b], left).wait_recv()
    from_source(right)
    for b in range(8):
        blk = gbuf.at[opp, b * 256:(b + 1) * 256, :]
        link(blk, blk, h_send.at[2, b], h_recv.at[2, b], right).wait_recv()
    from_source(opp)

    def wide(a):
        return jnp.concatenate([a, a], axis=1)

    def seeds(first):
        return jnp.concatenate([tot[h * 2 * SEED + first:h * 2 * SEED + first + SEED, :] for h in range(2)], axis=1)

    near2 = (seeds(0) * wide(invc[y])).astype(BF)
    self2 = seeds(SEED).astype(BF)
    alive = live[...].astype(F32)
    diff = self2.astype(F32) - near2.astype(F32)
    pull_apart = wide(livec[...]) * diff

    def swap_start(buf, ssem, rsem):
        blk = buf.at[y]
        link(blk, blk, ssem.at[0], rsem.at[0], right).start()
        link(blk, blk, ssem.at[1], rsem.at[1], left).start()

    def swap_forward(buf, ssem, rsem, cut):
        blk = buf.at[left]
        link(blk, blk, ssem.at[0], rsem.at[0], right).wait_recv()
        half = buf.at[left, 0:cut, :]
        link(half, half, ssem.at[2], rsem.at[2], right).start()
        blk = buf.at[right]
        link(blk, blk, ssem.at[1], rsem.at[1], left).wait_recv()
        half = buf.at[right, cut:, :]
        link(half, half, ssem.at[3], rsem.at[3], left).start()

    def swap_end(buf, ssem, rsem, cut):
        half = buf.at[opp, 0:cut, :]
        link(half, half, ssem.at[2], rsem.at[2], right).wait_recv()
        half = buf.at[opp, cut:, :]
        link(half, half, ssem.at[3], rsem.at[3], left).wait_recv()

    def swap_sent(buf, ssem, rsem, cut):
        blk = buf.at[y]
        link(blk, blk, ssem.at[0], rsem.at[0], right).wait_send()
        link(blk, blk, ssem.at[1], rsem.at[1], left).wait_send()
        half = buf.at[left, 0:cut, :]
        link(half, half, ssem.at[2], rsem.at[2], right).wait_send()
        half = buf.at[right, cut:, :]
        link(half, half, ssem.at[3], rsem.at[3], left).wait_send()

    rbuf[y] = pull_apart.astype(BF)
    swap_start(rbuf, r_send, r_recv)

    act2 = jnp.concatenate([self2, near2], axis=1)
    cls = lax.broadcasted_iota(jnp.int32, (CLS_PAD, SEED), 0)
    b2 = b2c[0:CLS_PAD, :]
    logits = dot(w2t[...], act2, NT) + jnp.concatenate([b2] * 4, axis=1)
    logits = jnp.where(cls < CLS, logits, -1e30)
    top = jnp.max(logits, axis=0, keepdims=True)
    e = jnp.exp(logits - top)
    tot = jnp.sum(e, axis=0, keepdims=True)
    hot = cls == labels[...]
    picked = jnp.sum(jnp.where(hot, logits, 0.0), axis=0, keepdims=True)
    dlog = (alive * (e * (1.0 / tot) - jnp.where(hot, 1.0, 0.0)) * (1.0 / SEEDS_ALL)).astype(BF)
    dbuf[y] = dlog
    swap_start(dbuf, d_send, d_recv)

    loss = jnp.sum(alive * (top + jnp.log(tot) - picked), axis=1, keepdims=True)
    loss = loss + SEEDS_ALL / 2 * jnp.sum(pull_apart * diff, keepdims=True)
    g2t = dot(dlog, act2).astype(BF)
    for q in range(NAR):
        pay2[q * Q2:q * Q2 + CLS_PAD, :] = g2t[:, q * 128:(q + 1) * 128]
        pay2[q * Q2 + CLS_PAD:(q + 1) * Q2, :] = jnp.zeros((Q2 - CLS_PAD, 128), BF)

    def to_owner(pay, inbox, first, count, n):
        def body(i, c):
            t = (g + i) % GRP
            p = t - first

            @pl.when((p >= 0) & (p < count))
            def _():
                pltpu.make_async_remote_copy(
                    src_ref=pay.at[pl.ds(pl.multiple_of(p * PIECE, PIECE), PIECE)], dst_ref=inbox.at[g],
                    send_sem=rs_send.at[n], recv_sem=rs_recv.at[n], device_id=(t, y), device_id_type=MESH,
                ).start()

            return c

        lax.fori_loop(1, GRP, body, 0)

    def mine(first, count):
        p = g - first
        return (p >= 0) & (p < count), pl.ds(pl.multiple_of(p * PIECE, PIECE), PIECE)

    def add_first_momentum(p):
        rows = pl.ds(pl.multiple_of(p % 2 * PIECE, PIECE), PIECE)
        for h in range(2):
            @pl.when((y == p % 8 // 2) & (p // 8 == h))
            def _(h=h):
                ybox1[y] = ybox1[y] + MU * m1[rows, h * 128:(h + 1) * 128]

    def add_second_momentum(p):
        @pl.when(y == p // (Q2 // PIECE))
        def _():
            rows = pl.ds(pl.multiple_of(p % (Q2 // PIECE) * PIECE, PIECE), PIECE)
            ybox2[y] = ybox2[y] + MU * m2pad[rows, :]

    def add_plane(pay, inbox, ybox, first, count, n, add_momentum):
        here, rows = mine(first, count)

        @pl.when(here)
        def _():
            got = inbox.at[pl.ds(0, GRP - 1)]
            pltpu.make_async_copy(got, got, rs_recv.at[n]).wait()
            inbox[g] = pay[rows, :]
            ybox[y] = jnp.sum(inbox[...].astype(F32), axis=0)
            add_momentum(g - first)
            for d in range(1, NAR):
                link(ybox.at[y], ybox.at[y], y_send.at[n, d - 1], y_recv.at[n, d - 1], ys[d]).start()

    def add_group(ybox, res, first, count, n):
        here, rows = mine(first, count)

        @pl.when(here)
        def _():
            for d in range(1, NAR):
                link(ybox.at[y], ybox.at[y], y_send.at[n, d - 1], y_recv.at[n, d - 1], ys[d]).wait()
            res[rows, :] = (ybox[0] + ybox[1]) + (ybox[2] + ybox[3])

            def tell(i, c):
                pltpu.make_async_remote_copy(
                    src_ref=res.at[rows], dst_ref=res.at[rows], send_sem=ag_send.at[n], recv_sem=ag_recv.at[n],
                    device_id=((g + i) % GRP, y), device_id_type=MESH,
                ).start()
                return c

            lax.fori_loop(1, GRP, tell, 0)

    def take(res, first, count, n):
        here, rows = mine(first, count)
        for less, when in ((1, here), (0, jnp.logical_not(here))):
            @pl.when(when)
            def _(less=less):
                got = res.at[pl.ds(0, (count - less) * PIECE)]
                pltpu.make_async_copy(got, got, ag_recv.at[n]).wait()

    def sums_sent(pay, first, count, n):
        here, rows = mine(first, count)
        for less, when in ((1, here), (0, jnp.logical_not(here))):
            @pl.when(when)
            def _(less=less):
                gone = pay.at[pl.ds(0, (count - less) * PIECE)]
                pltpu.make_async_copy(gone, gone, rs_send.at[n]).wait()

        @pl.when(here)
        def _():
            gone = table.at[pl.ds(0, (GRP - 1) * PIECE)]
            pltpu.make_async_copy(gone, gone, ag_send.at[n]).wait()

    to_owner(pay2, inbox2, GRP - P2, P2, 1)

    def add_grads(q, fresh=False):
        da = dot(dbuf[q], w2t[...], TN)
        r = rbuf[q].astype(F32)
        ds = (da[:, :HID] + r).astype(BF)
        dn = ((da[:, HID:] - r) * wide(invc[q])).astype(BF)
        both = jnp.concatenate([dn, ds], axis=0)

        def rows512(i, c):
            part = dot(bsel[q, pl.ds(pl.multiple_of(i * 512, 512), 512), :], both)
            for h in range(2):
                rows = pl.ds(pl.multiple_of(h * FRONT + i * 512, 512), 512)
                now = part[:, h * 128:(h + 1) * 128]
                dh1[rows, :] = now if fresh else dh1[rows, :] + now
            return c

        lax.fori_loop(0, FRONT // 512, rows512, 0)

    db2 = jnp.sum(dlog.astype(F32), axis=1, keepdims=True)
    db2 = jnp.broadcast_to(db2, (CLS_PAD, 128)).T[0:1, :]
    swap_forward(rbuf, r_send, r_recv, SEED // 2)
    add_grads(y, True)
    swap_forward(dbuf, d_send, d_recv, 96)
    add_grads(left)
    add_grads(right)
    add_plane(pay2, inbox2, ybox2, GRP - P2, P2, 1, add_second_momentum)
    swap_end(rbuf, r_send, r_recv, SEED // 2)
    swap_end(dbuf, d_send, d_recv, 96)
    add_group(ybox2, res2, GRP - P2, P2, 1)
    add_grads(opp)

    def to_z(b, db):
        rows = pl.ds(pl.multiple_of(b * 256, 256), 256)
        dh = jnp.concatenate(
            [dh1[pl.ds(pl.multiple_of(h * FRONT + b * 256, 256), 256), :] for h in range(2)], axis=1
        )
        dz = (dh * slope[rows, :]).astype(BF)
        a1 = jnp.concatenate(
            [a1t[pl.ds(pl.multiple_of((2 * b + h) * 256, 256), 256), :] for h in range(2)], axis=1
        )
        part = dot(a1, dz)
        for h in range(2):
            now = slice(h * 256, (h + 1) * 256)
            gsum[now, :] = gsum[now, :] + part[:, h * 128:(h + 1) * 128]
        return db + jnp.sum(dz.astype(F32), axis=0, keepdims=True)

    gsum[...] = jnp.zeros((512, 128), F32)
    db1 = lax.fori_loop(0, FRONT // 256, to_z, jnp.zeros((1, HID), F32))
    pay1[0:512, :] = gsum[...].astype(BF)
    misc[...] = jnp.zeros((PIECE, 128), F32)

    def two(rows, v):
        hi = v.astype(BF).astype(F32)
        misc[rows:rows + 1, 0:v.shape[1]] = hi
        misc[rows + 4:rows + 5, 0:v.shape[1]] = v - hi

    two(0, db1[:, :128])
    two(1, db1[:, 128:])
    two(2, db2[:, :128])
    two(3, db2[:, 128:])
    hi = loss.astype(BF).astype(F32)
    misc[8:9, 0:1] = hi
    misc[9:10, 0:1] = loss - hi
    pay1[512:544, :] = misc[...].astype(BF)
    to_owner(pay1, inbox1, 0, P1, 0)

    take(res2, GRP - P2, P2, 1)
    mom2 = jnp.concatenate([res2[q * Q2:q * Q2 + CLS_PAD, :] for q in range(NAR)], axis=1)
    for q in range(NAR):
        x2s[q] = mom2[:, q * 128:(q + 1) * 128]
    o_all[ROW_M2:ROW_M2 + CLS_PAD, :] = x2s[y]
    x2 = mom2 * (1.0 / (jnp.sqrt(jnp.sum(mom2 * mom2, keepdims=True)) + 1e-07))
    x2 = ns_step(x2)
    add_plane(pay1, inbox1, ybox1, 0, P1, 0, add_first_momentum)
    x2 = ns_step(x2)
    add_group(ybox1, o_all, 0, P1, 0)
    x2 = ns_step(x2)
    for q in range(NAR):
        o_all[ROW_X2 + q * CLS_PAD:ROW_X2 + (q + 1) * CLS_PAD, :] = x2[:, q * 128:(q + 1) * 128]
    take(o_all, 0, P1, 0)

    for b in range(8):
        blk = gbuf.at[y, b * 256:(b + 1) * 256, :]
        link(blk, blk, h_send.at[0, b], h_recv.at[0, b], right).wait_send()
        link(blk, blk, h_send.at[1, b], h_recv.at[1, b], left).wait_send()
        blk = gbuf.at[opp, b * 256:(b + 1) * 256, :]
        link(blk, blk, h_send.at[2, b], h_recv.at[2, b], right).wait_send()
    swap_sent(rbuf, r_send, r_recv, SEED // 2)
    swap_sent(dbuf, d_send, d_recv, 96)

    sums_sent(pay2, GRP - P2, P2, 1)
    sums_sent(pay1, 0, P1, 0)


def main(reqt, feat, idx1t, msk1t, idx2t, msk2t, labels, live, w1, w2own, m1, m2own, bias):
    vm = pl.BlockSpec(memory_space=pltpu.VMEM)
    dma = pltpu.SemaphoreType.DMA
    sds = jax.ShapeDtypeStruct
    V = pltpu.VMEM
    return pl.pallas_call(
        main_kernel,
        out_shape=sds((ROWS, 128), F32),
        in_specs=[vm, pl.BlockSpec(memory_space=pl.ANY)] + [vm] * 11,
        out_specs=vm,
        scratch_shapes=[
            V((SRC + 8, D_IN), F32),
            V((OWN, D_IN), BF),
            V((SRC, D_IN), BF),
            V((CAP, D_IN), F32),
            V((DEV, 128), jnp.int32),
            V((DEV, 128), jnp.int32),
            V((NAR, GRP, 1, 128), jnp.int32),
            V((16, FRONT), jnp.int32),
            V((256, 128), jnp.int32),
            V((1, FRONT), F32),
            V((256, D_IN), F32),
            V((256, D_IN), F32),
            V((FRONT, HID), F32),
            V((NAR, FRONT, HID), BF),
            V((NAR, 2 * SEED, FRONT), BF),
            V((NAR, FRONT, 2 * SEED), BF),
            V((8, 16, SEED), jnp.int32),
            V((16, SEED), jnp.int32),
            V((16, SEED), jnp.int32),
            V((SEED, 32), jnp.int32),
            V((256, SRC), BF),
            V((256, 32), jnp.int32),
            V((NAR, SEED, 128), F32),
            V((SEED, 128), F32),
            V((NAR, SEED, HID), BF),
            V((NAR, CLS_PAD, SEED), BF),
            V((NAR, 64, HID), BF),
            V((NAR, CLS_PAD, 128), BF),
            V((Q2, 128), F32),
            V((NAR, 16, SEED), jnp.int32),
            V((CLS_PAD, 2 * HID), BF),
            V((HID, 128), F32),
            V((P1 * PIECE, 128), BF),
            V((P2 * PIECE, 128), BF),
            V((PIECE, 128), F32),
            V((GRP, PIECE, 128), BF),
            V((GRP, PIECE, 128), BF),
            V((NAR, PIECE, 128), F32),
            V((NAR, PIECE, 128), F32),
            V((P2 * PIECE, 128), F32),
            V((NAR, CLS_PAD, 128), F32),
            pltpu.SMEM((DEV, 1, 128), jnp.int32),
            pltpu.SMEM((256, 128), jnp.int32),
            dma, dma((3,)), dma((GRP,)), dma((NAR,)), dma((NAR,)), dma((GRP,)), dma, dma, dma((3, 3)), dma((3, 3)),
            dma((3, 8)), dma((3, 8)), dma((4,)), dma((4,)), dma((4,)), dma((4,)),
            dma((2,)), dma((2,)), dma((2, 3)), dma((2, 3)), dma((2,)), dma((2,)),
        ],
        compiler_params=pltpu.CompilerParams(
            collective_id=0, has_side_effects=True, vmem_limit_bytes=62 * 2**20
        ),
    )(reqt, feat, idx1t, msk1t, idx2t, msk2t, labels, live, w1, w2own, m1, m2own, bias)


def update_kernel(
    res, w1own, w2own, bias, biasm, biasv,
    o_loss, o_first, o_second, o_mom1, o_mom2, o_flow, o_slow, o_bias, o_bm, o_bv,
    x1s, x2s,
):
    y = lax.axis_index("nar")
    mom1 = jnp.concatenate([res[0:256, :], res[256:512, :]], axis=1)
    x1s[...] = mom1
    block64 = pl.ds(pl.multiple_of(y * 64, 64), 64)
    o_mom1[...] = x1s[block64, :]
    x1 = mom1 * (1.0 / (jnp.sqrt(jnp.sum(mom1 * mom1, keepdims=True)) + 1e-07))
    x2 = jnp.concatenate([res[ROW_X2 + q * CLS_PAD:ROW_X2 + (q + 1) * CLS_PAD, :] for q in range(NAR)], axis=1)
    for i in range(NS_ITERS):
        x1 = ns_step(x1)
        if i < 2:
            x2 = ns_step(x2)
    x1s[...] = x1
    for q in range(NAR):
        x2s[q] = x2[:, q * 128:(q + 1) * 128]
    first_new = w1own[...] * (1.0 - WDECAY) - x1s[block64, :]
    o_first[...] = first_new
    o_flow[...] = first_new.astype(BF)
    second = w2own[...] * (1.0 - WDECAY) - (2 * HID / CLS) ** 0.5 * x2s[y][0:CLS, :]
    o_second[...] = second
    o_slow[...] = second.astype(BF)
    o_mom2[...] = res[ROW_M2:ROW_M2 + CLS, :]

    gb = res[512:516, :] + res[516:520, :]
    gb = jnp.concatenate([gb[0:1, :], gb[1:2, :], gb[2:3, :], gb[3:4, 0:44]], axis=1)
    m_new = BETA_ONE * biasm[...] + (1.0 - BETA_ONE) * gb
    v_new = BETA_TWO * biasv[...] + (1.0 - BETA_TWO) * gb * gb
    m_hat = m_new / (1.0 - BETA_ONE**STEP)
    v_hat = v_new / (1.0 - BETA_TWO**STEP)
    o_bias[...] = bias[...] * (1.0 - LR_BIAS * WDECAY) - LR_BIAS * m_hat / (jnp.sqrt(v_hat) + EPSILON)
    o_bm[...] = m_new
    o_bv[...] = v_new
    o_loss[...] = res[520:521, 0:1] + res[521:522, 0:1]


def update(*args):
    vm = pl.BlockSpec(memory_space=pltpu.VMEM)
    sds = jax.ShapeDtypeStruct
    return pl.pallas_call(
        update_kernel,
        out_shape=[
            sds((1, 1), F32), sds((64, HID), F32), sds((CLS, 128), F32), sds((64, HID), F32), sds((CLS, 128), F32),
            sds((64, HID), BF), sds((CLS, 128), BF), sds((1, 428), F32), sds((1, 428), F32), sds((1, 428), F32),
        ],
        in_specs=[vm] * 6,
        out_specs=[vm] * 10,
        scratch_shapes=[pltpu.VMEM((2 * D_IN, HID), F32), pltpu.VMEM((NAR, CLS_PAD, 128), F32)],
        compiler_params=pltpu.CompilerParams(vmem_limit_bytes=32 * 2**20),
    )(*args)


def per_device(
    features, requests, index_one, mask_one, index_two, mask_two, labels, seed_live,
    w_first, w_second, mom_first, mom_second, biases, bias_m, bias_v,
):
    w2own, bias = w_second.T, biases[None, :]
    res = main(
        requests.T, features, index_one.T, mask_one.T, index_two.T, mask_two.T, labels[None, :], seed_live[None, :],
        w_first, w2own, mom_first, mom_second.T, bias,
    )
    loss, first_new, second_new, mom_one, mom_two, first_low, second_low, bias_new, m_new, v_new = update(
        res, w_first, w2own, bias, bias_m[None, :], bias_v[None, :]
    )
    return (
        loss.reshape(()), first_new, second_new.T, mom_one, mom_two.T, first_low, second_low.T,
        bias_new.reshape(-1), m_new.reshape(-1), v_new.reshape(-1),
    )


def solution(mesh):
    both = ("grp", "nar")
    placed = (
        P(both, None), P(both, None), P(both, None), P(both, None), P(both, None), P(both, None),
        P(both), P(both), P("nar", None), P("nar", None), P("nar", None), P("nar", None), P(), P(), P(),
    )
    nar = P("nar", None)
    return jax.shard_map(
        per_device, mesh=mesh, in_specs=placed,
        out_specs=(P(), nar, nar, nar, nar, nar, nar, P(), P(), P()), check_vma=False,
    )
```

```python
import functools

import jax
import jax.numpy as jnp
from jax import lax
from jax.experimental import pallas as pl
from jax.experimental.pallas import tpu as pltpu
from jax.sharding import PartitionSpec as P

HID = 256
CLS = 172
CLS_PAD = 176
D_IN = 128
F1 = 15
F2 = 10
NS_ITERS = 5
STEP = 10
LAM = 0.5
MU = 0.95
WDECAY = 0.01
LR_BIAS = 0.05
BETA_ONE = 0.9
BETA_TWO = 0.999
EPSILON = 1e-08
NS_A = 3.4445
NS_B = -4.775
NS_C = 2.0315
HIGH = lax.Precision.HIGHEST
MESH = pl.DeviceIdType.MESH
BF = jnp.bfloat16
F32 = jnp.float32

DEV = 128
NAR = 4
OWN = 8192
CAP = 64
SRC = 8192
FRONT = 2048
SEED = 512


def all_to(t):
    return (t // NAR, t % NAR)


PIECE = 32
P1 = 17
Q2 = 192
P2 = 24
GRP = 32
ROW_M2 = P1 * PIECE
ROW_X2 = ROW_M2 + CLS_PAD
ROWS = ROW_X2 + NAR * CLS_PAD
SEEDS_ALL = SEED * DEV


def dot(a, b, dims=((1,), (0,))):
    return lax.dot_general(a, b, (dims, ((), ())), preferred_element_type=F32)


NN = ((1,), (0,))
NT = ((1,), (1,))
TN = ((0,), (0,))


def split(a):
    hi = a.astype(BF)
    return hi, (a - hi.astype(F32)).astype(BF)


def dot3(a, b, dims):
    (ah, al), (bh, bl) = a, b
    return dot(
        jnp.concatenate([ah, ah, al], axis=dims[0][0]), jnp.concatenate([bh, bl, bh], axis=dims[1][0]), dims
    )


def ns_step(x):
    xs = split(x)
    gram = dot3(xs, xs, NT)
    gs = split(gram)
    mix = NS_B * gram + NS_C * dot3(gs, gs, NN)
    return NS_A * x + dot3(split(mix), xs, NN)


def spread(row):
    return jnp.broadcast_to(row, (128, 128)).T


def main_kernel(
    reqt, feat, idx1t, msk1t, idx2t, msk2t, labels, live, w1, w2own, m1, m2own, bias,
    o_all,
    table, featb, pulled, stage, reqv, reqin, mid, idxv, idxp, invv, near, own, slope, gbuf, fsel, bsel, unit_of, lows, selfs, idc, ssel, idm, invc, livec, rbuf, dbuf,
    gw1, gw2t, m2pad, gidx2, w2t, b2c, pay1, pay2, misc, inbox1, inbox2, ybox1, ybox2, res2, x2s,
    reqs, idx,
    feat_sem, loc_sem, ask_sem, req_send, mid_recv, req_recv, row_send, row_recv, nar_send, nar_recv,
    h_send, h_recv, r_send, r_recv, d_send, d_recv, rs_send, rs_recv, y_send, y_recv, ag_send, ag_recv,
):
    a1t, dh1, tot, gsum = featb, table, table.at[2 * FRONT:3 * FRONT], table.at[3 * FRONT:3 * FRONT + 512]
    g = lax.axis_index("grp")
    y = lax.axis_index("nar")
    me = g * NAR + y
    left, right, opp = (y + 3) % NAR, (y + 1) % NAR, (y + 2) % NAR

    load = pltpu.make_async_copy(feat, featb, feat_sem)
    load.start()

    barrier = pltpu.get_barrier_semaphore()

    ys = [(y + d) % NAR for d in range(NAR)]

    def greet(i, c):
        pl.semaphore_signal(barrier, inc=1, device_id=((g + i) % GRP, y), device_id_type=MESH)
        return c

    for d in range(1, NAR):
        pl.semaphore_signal(barrier, inc=1, device_id=(g, ys[d]), device_id_type=MESH)
    lax.fori_loop(1, GRP, greet, 0)

    def link(src, dst, ssem, rsem, to):
        return pltpu.make_async_remote_copy(
            src_ref=src, dst_ref=dst, send_sem=ssem, recv_sem=rsem, device_id=(g, to), device_id_type=MESH
        )

    reqv[...] = jnp.concatenate([reqt[...], jnp.zeros((DEV - CAP, DEV), jnp.int32)], axis=0).T
    ask_rows = reqv.reshape(GRP, NAR, 1, 128)
    got_rows = reqin.reshape(DEV, 1, 128)

    gw1[y] = w1[...].astype(BF)
    pad = CLS_PAD - CLS
    gw2t[y] = jnp.concatenate([w2own[...], jnp.zeros((pad, 128), F32)], axis=0).astype(BF)
    m2pad[...] = jnp.concatenate([m2own[...], jnp.zeros((Q2 - CLS, 128), F32)], axis=0)
    gidx2[y] = jnp.concatenate(
        [idx2t[0:1, :], jnp.where(msk2t[...] > 0, idx2t[1:, :], -1), jnp.zeros((5, SEED), jnp.int32)], axis=0
    )
    shared = (gidx2, gw1, gw2t)

    pl.semaphore_wait(barrier, GRP + NAR - 2)

    def ask_group(d):
        return pltpu.make_async_remote_copy(
            src_ref=ask_rows.at[:, ys[d]], dst_ref=mid.at[y], send_sem=req_send.at[d], recv_sem=mid_recv.at[d],
            device_id=(g, ys[d]), device_id_type=MESH,
        )

    for d in range(1, NAR):
        ask_group(d).start()
    keep = pltpu.make_async_copy(ask_rows.at[:, y], mid.at[y], loc_sem.at[2])
    keep.start()
    for n, a in enumerate(shared):
        for d in range(1, NAR):
            link(a.at[y], a.at[y], nar_send.at[n, d - 1], nar_recv.at[n, d - 1], (y + d) % NAR).start()

    msk = msk1t[...]
    idxv[0:1, :] = idx1t[0:1, :]
    idxv[1:16, :] = jnp.where(msk > 0, idx1t[1:16, :], SRC)
    invv[...] = 1.0 / jnp.maximum(jnp.sum(msk.astype(F32), axis=0, keepdims=True), 1.0)
    for half in range(2):
        parts = []
        for r in range(8):
            parts.append(jnp.concatenate(
                [idxv[:, (half * 4 + b) * 256 + r * 32:(half * 4 + b) * 256 + r * 32 + 32] for b in range(4)], axis=1
            ))
        idxp[half * 128:(half + 1) * 128, :] = jnp.concatenate(parts, axis=0).T
    to_smem = [pltpu.make_async_copy(idxp, idx, loc_sem.at[0])]
    for c in to_smem:
        c.start()

    keep.wait()
    for d in range(1, NAR):
        ask_group(d).wait()
    own_rows = pl.ds(pl.multiple_of(g * NAR, NAR), NAR)

    def ask(i, c):
        n = (i * 13) % GRP
        t = (g + n) % GRP
        pltpu.make_async_remote_copy(
            src_ref=mid.at[:, t], dst_ref=got_rows.at[own_rows], send_sem=req_send.at[0], recv_sem=req_recv.at[n],
            device_id=(t, y), device_id_type=MESH,
        ).start()
        return c

    lax.fori_loop(1, GRP, ask, 0)
    keep = pltpu.make_async_copy(mid.at[:, g], got_rows.at[own_rows], loc_sem.at[2])
    keep.start()

    load.wait()

    def widen_features(i, c):
        rows = pl.ds(pl.multiple_of(i * 256, 256), 256)
        table[rows, :] = featb[rows, :].astype(F32)
        return c

    lax.fori_loop(0, OWN // 256, widen_features, 0)

    lane32 = lax.broadcasted_iota(jnp.int32, (16, 128), 1)
    sub32 = lax.broadcasted_iota(jnp.int32, (32, 128), 0)
    lane16 = lane32.astype(jnp.int16)
    iota16 = lax.broadcasted_iota(jnp.int32, (16, 128), 0).astype(jnp.int16)
    one, zero = jnp.ones((16, 128), BF), jnp.zeros((16, 128), BF)

    def unit(digit):
        v = jnp.ones_like(digit)
        for j in range(1, 8):
            v = jnp.where(digit == j, 1 << 4 * j, v)
        return v

    def count(acc, j):
        return ((acc >> (4 * j)) & 15).astype(F32).astype(BF)

    def keys_units(ids):
        return (ids & 127) + (ids >> 10) * 128, unit((ids >> 7) & 7)

    def word(pos, keys, units):
        acc = jnp.zeros((16, 128), jnp.int32)
        for k, u in zip(keys, units):
            acc = acc + jnp.where(pos == k, u, 0)
        return acc

    def spread_columns(blk, ks):
        return [jnp.broadcast_to(blk[:, k:k + 1], (16, 128)) for k in ks]

    ids = gidx2[y]
    keys, units = keys_units(ids)
    idc[...] = jnp.concatenate([ids[0:1, :], keys[1:, :], units], axis=0).T

    def seeds16(i):
        at = pl.multiple_of(i * 16, 16)
        blk = idc[pl.ds(at, 16), :]
        self_row = jnp.broadcast_to(blk[:, 0:1], (16, 128)).astype(jnp.int16)
        return at, (spread_columns(blk, range(1, 1 + F2)), spread_columns(blk, range(17, 17 + F2)), self_row)

    def forward_marks(at, want, q):
        keys, units, self_row = want
        for w in range(2):
            acc = word(lane32 + 128 * (2 * q + w), keys, units)
            for j in range(8):
                c = w * 8 + j
                fsel[q, pl.ds(at, 16), c * 128:(c + 1) * 128] = count(acc, j)
                here = lane16 + jnp.full((16, 128), q * FRONT + c * 128, jnp.int32).astype(jnp.int16)
                fsel[q, pl.ds(SEED + at, 16), c * 128:(c + 1) * 128] = jnp.where(here == self_row, one, zero)

    view = table.reshape(SRC + 8, 1, D_IN)
    my_rows = pl.ds(pl.multiple_of(me * CAP, CAP), CAP)

    def pick(t, u, slot):
        for half in range(0, CAP, 32):
            rows = [view[reqs[t * NAR + u, 0, half + r]] for r in range(32)]
            for r in range(32):
                stage[half + r:half + r + 1, :] = rows[r]
        featb[slot, :] = stage[...].astype(BF)

    def serve_one(t, u, slot):
        pick(t, u, slot)
        pltpu.make_async_remote_copy(
            src_ref=featb.at[slot], dst_ref=pulled.at[my_rows],
            send_sem=row_send, recv_sem=row_recv, device_id=(t, u), device_id_type=MESH,
        ).start()

    def asked(n):
        rows = got_rows.at[pl.ds(0, NAR)]
        pltpu.make_async_copy(rows, rows, req_recv.at[n]).wait()

    def to_scalars(t, n):
        rows = pl.ds(pl.multiple_of(t * NAR, NAR), NAR)
        return pltpu.make_async_copy(got_rows.at[rows], reqs.at[rows], ask_sem.at[n])

    def whose(i):
        n = (i * 13) % GRP
        return n, (g + GRP - n) % GRP

    def fetch(i):
        n, t = whose(i)
        asked(n)
        to_scalars(t, n).start()

    def serve(i, c):
        n, t = whose(i)

        @pl.when(i < GRP - 1)
        def _():
            fetch(i + 1)

        to_scalars(t, n).wait()
        at, want = seeds16(i)
        for d in range(NAR):
            forward_marks(at, want, d)
            serve_one(t, ys[d], pl.ds(pl.multiple_of((i * NAR + d) * CAP, CAP), CAP))
        return c

    fetch(1)
    lax.fori_loop(1, GRP, serve, 0)
    keep.wait()
    to_scalars(g, 0).start()
    to_scalars(g, 0).wait()
    at, want = seeds16(0)
    for d in range(NAR):
        forward_marks(at, want, d)
    for d in range(1, NAR):
        serve_one(g, ys[d], pl.ds(d * CAP, CAP))
    pick(g, y, pl.ds(0, CAP))
    pulled[my_rows, :] = featb[0:CAP, :]

    for n, a in enumerate(shared):
        for d in range(1, NAR):
            link(a.at[y], a.at[y], nar_send.at[n, d - 1], nar_recv.at[n, d - 1], (y + d) % NAR).wait()
    for q in range(NAR):
        w2t[:, q * 128:(q + 1) * 128] = gw2t[q]
    last = jnp.concatenate([bias[0:1, 384:428], jnp.zeros((1, 84), F32)], axis=1)
    b2c[...] = jnp.concatenate([spread(bias[0:1, 256:384]), spread(last)], axis=0)

    def column(row):
        return jnp.concatenate([spread(row[:, c * 128:(c + 1) * 128]) for c in range(SEED // 128)], axis=0)

    for q in range(NAR):
        n = jnp.sum((gidx2[q, 1:1 + F2, :] >= 0).astype(F32), axis=0, keepdims=True)
        invc[q] = column(1.0 / jnp.maximum(n, 1.0))
    livec[...] = column(2.0 * LAM / HID / SEEDS_ALL * live[...].astype(F32))

    def backward_marks(q, carry):
        r = gidx2[q] - y * FRONT
        lows[...] = r & 31
        inside = (r >= 0) & (r < FRONT)
        units = unit((r >> 5) & 7)
        for w in range(8):
            unit_of[w] = jnp.where(inside & ((r >> 8) == w), units, 0)
        selfs[...] = jnp.broadcast_to(r[0:1, :], (16, SEED))

        def column(c, carry2):
            lanes = pl.ds(pl.multiple_of(c * 128, 128), 128)
            accs = [jnp.zeros((32, 128), jnp.int32) for _ in range(8)]
            for k in range(1, 1 + F2):
                hit = sub32 == jnp.broadcast_to(lows[k:k + 1, lanes], (32, 128))
                for w in range(8):
                    u = jnp.broadcast_to(unit_of[w, k:k + 1, lanes], (32, 128))
                    accs[w] = accs[w] + jnp.where(hit, u, 0)
            for w in range(8):
                for j in range(8):
                    first = (w * 8 + j) * 32
                    bsel[q, first:first + 32, lanes] = count(accs[w], j)
            self_row = selfs[:, lanes].astype(jnp.int16)
            lanes = pl.ds(pl.multiple_of(SEED + c * 128, 128), 128)
            for t in range(FRONT // 16):
                here = iota16 + jnp.full((16, 128), t * 16, jnp.int32).astype(jnp.int16)
                bsel[q, t * 16:(t + 1) * 16, lanes] = jnp.where(here == self_row, one, zero)
            return carry2

        lax.fori_loop(0, SEED // 128, column, 0)
        return carry

    def sum_marks(i):
        at = pl.multiple_of(i // 2 * 16, 16)
        half = i % 2
        blk = idm[pl.ds(at, 16), :]
        keys, units = spread_columns(blk, range(1, 1 + F1)), spread_columns(blk, range(17, 17 + F1))
        for w in range(4):
            acc = word(lane32 + (half * 4 + w) * 128, keys, units)
            for j in range(8):
                col = pl.ds(pl.multiple_of(half * (SRC // 2) + (w * 8 + j) * 128, 128), 128)
                ssel[pl.ds(at, 16), col] = count(acc, j)

    def sum_ids(b):
        idm[...] = jnp.concatenate(keys_units(idxv[:, cols(b)]), axis=0).T

    def cols(b):
        return pl.ds(pl.multiple_of(b * 256, 256), 256)

    def one_mark(i, c):
        sum_marks(i)
        return c

    sum_ids(0)
    lax.fori_loop(0, 32, one_mark, 0)
    lax.fori_loop(0, NAR, backward_marks, 0)

    come = pulled.at[pl.ds(0, (DEV - 1) * CAP)]
    pltpu.make_async_copy(come, come, row_recv).wait()
    gone = featb.at[pl.ds(CAP, (DEV - 1) * CAP)]
    pltpu.make_async_copy(gone, gone, row_send).wait()
    sent = mid.at[:, pl.ds(0, GRP - 1)]
    pltpu.make_async_copy(sent, sent, req_send.at[0]).wait()

    def widen(i, c):
        rows = pl.ds(pl.multiple_of(i * 256, 256), 256)
        table[rows, :] = pulled[rows, :].astype(F32)
        return c

    lax.fori_loop(0, SRC // 256, widen, 0)
    table[SRC:SRC + 8, :] = jnp.zeros((8, D_IN), F32)
    for c in to_smem:
        c.wait()

    def forward(b):
        @pl.when(b % 2 == 0)
        def _():
            blk = gbuf.at[left, cols(b), :]
            link(blk, blk, h_send.at[0, b], h_recv.at[0, b], right).wait_recv()
            link(blk, blk, h_send.at[2, b], h_recv.at[2, b], right).start()

        @pl.when(b % 2 == 1)
        def _():
            blk = gbuf.at[right, cols(b), :]
            link(blk, blk, h_send.at[1, b], h_recv.at[1, b], left).wait_recv()
            link(blk, blk, h_send.at[2, b], h_recv.at[2, b], left).start()

    def load_sums(b):
        def some(i, c):
            found = []
            for e in range(2):
                line = b * 32 + 2 * i + e
                for r in range(8):
                    self_row = view[idx[line, r * 16]]
                    rows = [view[idx[line, r * 16 + 1 + k]] for k in range(F1)]
                    while len(rows) > 1:
                        rows = [p + q for p, q in zip(rows[::2], rows[1::2])] + ([rows[-1]] if len(rows) % 2 else [])
                    found.append((r * 32 + 2 * i + e, self_row, rows[0]))
            for at, self_row, total in found:
                own[pl.ds(at, 1), :] = self_row
                near[pl.ds(at, 1), :] = total
            return c

        lax.fori_loop(0, 16, some, 0)
        finish(b)

    def multiply_sums(b):
        def some(i, c):
            found = []
            for e in range(2):
                for r in range(8):
                    found.append((r * 32 + 2 * i + e, view[idx[b * 32 + 2 * i + e, r * 16]]))
            for at, self_row in found:
                own[pl.ds(at, 1), :] = self_row
            return c

        lax.fori_loop(0, 16, some, 0)
        near[...] = dot(ssel[...], pulled[...])
        finish(b)

    def finish(b):
        rows = cols(b)
        scale = jnp.concatenate(
            [spread(invv[0:1, pl.ds(pl.multiple_of(b * 256 + c * 128, 128), 128)]) for c in range(2)], axis=0
        )
        act = jnp.concatenate([own[...].astype(BF), (near[...] * scale).astype(BF)], axis=1)
        a1 = act.T
        for h in range(2):
            a1t[pl.ds(pl.multiple_of((2 * b + h) * 256, 256), 256), :] = a1[:, h * 128:(h + 1) * 128]
        z = dot(act, gw1[...].reshape(2 * D_IN, HID)) + bias[0:1, 0:HID]
        sig = 1.0 / (1.0 + jnp.exp(-z))
        h1 = z * sig
        slope[rows, :] = sig + h1 * (1.0 - sig)
        gbuf[y, rows, :] = h1.astype(BF)
        blk = gbuf.at[y, rows, :]
        link(blk, blk, h_send.at[0, b], h_recv.at[0, b], right).start()
        link(blk, blk, h_send.at[1, b], h_recv.at[1, b], left).start()

        @pl.when(b > 0)
        def _():
            forward(b - 1)

    def loaded(b, c):
        load_sums(b)
        return c

    multiply_sums(0)
    lax.fori_loop(1, 8, loaded, 0)
    forward(7)

    def from_source(q, fresh=False):
        def rows512(i, c):
            part = dot(fsel[q, pl.ds(pl.multiple_of(i * SEED, SEED), SEED), :], gbuf[q])
            for h in range(2):
                rows = pl.ds(pl.multiple_of(h * 2 * SEED + i * SEED, SEED), SEED)
                now = part[:, h * 128:(h + 1) * 128]
                tot[rows, :] = now if fresh else tot[rows, :] + now
            return c

        lax.fori_loop(0, 2, rows512, 0)

    from_source(y, True)
    for b in range(1, 8, 2):
        blk = gbuf.at[left, b * 256:(b + 1) * 256, :]
        link(blk, blk, h_send.at[0, b], h_recv.at[0, b], right).wait_recv()
    from_source(left)
    for b in range(0, 8, 2):
        blk = gbuf.at[right, b * 256:(b + 1) * 256, :]
        link(blk, blk, h_send.at[1, b], h_recv.at[1, b], left).wait_recv()
    from_source(right)
    for b in range(8):
        blk = gbuf.at[opp, b * 256:(b + 1) * 256, :]
        link(blk, blk, h_send.at[2, b], h_recv.at[2, b], right).wait_recv()
    from_source(opp)

    def wide(a):
        return jnp.concatenate([a, a], axis=1)

    def seeds(first):
        return jnp.concatenate([tot[h * 2 * SEED + first:h * 2 * SEED + first + SEED, :] for h in range(2)], axis=1)

    near2 = (seeds(0) * wide(invc[y])).astype(BF)
    self2 = seeds(SEED).astype(BF)
    alive = live[...].astype(F32)
    diff = self2.astype(F32) - near2.astype(F32)
    pull_apart = wide(livec[...]) * diff

    def swap_start(buf, ssem, rsem):
        blk = buf.at[y]
        link(blk, blk, ssem.at[0], rsem.at[0], right).start()
        link(blk, blk, ssem.at[1], rsem.at[1], left).start()

    def swap_forward(buf, ssem, rsem, cut):
        blk = buf.at[left]
        link(blk, blk, ssem.at[0], rsem.at[0], right).wait_recv()
        half = buf.at[left, 0:cut, :]
        link(half, half, ssem.at[2], rsem.at[2], right).start()
        blk = buf.at[right]
        link(blk, blk, ssem.at[1], rsem.at[1], left).wait_recv()
        half = buf.at[right, cut:, :]
        link(half, half, ssem.at[3], rsem.at[3], left).start()

    def swap_end(buf, ssem, rsem, cut):
        half = buf.at[opp, 0:cut, :]
        link(half, half, ssem.at[2], rsem.at[2], right).wait_recv()
        half = buf.at[opp, cut:, :]
        link(half, half, ssem.at[3], rsem.at[3], left).wait_recv()

    def swap_sent(buf, ssem, rsem, cut):
        blk = buf.at[y]
        link(blk, blk, ssem.at[0], rsem.at[0], right).wait_send()
        link(blk, blk, ssem.at[1], rsem.at[1], left).wait_send()
        half = buf.at[left, 0:cut, :]
        link(half, half, ssem.at[2], rsem.at[2], right).wait_send()
        half = buf.at[right, cut:, :]
        link(half, half, ssem.at[3], rsem.at[3], left).wait_send()

    rbuf[y] = pull_apart.astype(BF)
    swap_start(rbuf, r_send, r_recv)

    act2 = jnp.concatenate([self2, near2], axis=1)
    cls = lax.broadcasted_iota(jnp.int32, (CLS_PAD, SEED), 0)
    b2 = b2c[0:CLS_PAD, :]
    logits = dot(w2t[...], act2, NT) + jnp.concatenate([b2] * 4, axis=1)
    logits = jnp.where(cls < CLS, logits, -1e30)
    top = jnp.max(logits, axis=0, keepdims=True)
    e = jnp.exp(logits - top)
    tot = jnp.sum(e, axis=0, keepdims=True)
    hot = cls == labels[...]
    picked = jnp.sum(jnp.where(hot, logits, 0.0), axis=0, keepdims=True)
    dlog = (alive * (e * (1.0 / tot) - jnp.where(hot, 1.0, 0.0)) * (1.0 / SEEDS_ALL)).astype(BF)
    dbuf[y] = dlog
    swap_start(dbuf, d_send, d_recv)

    loss = jnp.sum(alive * (top + jnp.log(tot) - picked), axis=1, keepdims=True)
    loss = loss + SEEDS_ALL / 2 * jnp.sum(pull_apart * diff, keepdims=True)
    g2t = dot(dlog, act2).astype(BF)
    for q in range(NAR):
        pay2[q * Q2:q * Q2 + CLS_PAD, :] = g2t[:, q * 128:(q + 1) * 128]
        pay2[q * Q2 + CLS_PAD:(q + 1) * Q2, :] = jnp.zeros((Q2 - CLS_PAD, 128), BF)

    def to_owner(pay, inbox, first, count, n):
        def body(i, c):
            t = (g + i) % GRP
            p = t - first

            @pl.when((p >= 0) & (p < count))
            def _():
                pltpu.make_async_remote_copy(
                    src_ref=pay.at[pl.ds(pl.multiple_of(p * PIECE, PIECE), PIECE)], dst_ref=inbox.at[g],
                    send_sem=rs_send.at[n], recv_sem=rs_recv.at[n], device_id=(t, y), device_id_type=MESH,
                ).start()

            return c

        lax.fori_loop(1, GRP, body, 0)

    def mine(first, count):
        p = g - first
        return (p >= 0) & (p < count), pl.ds(pl.multiple_of(p * PIECE, PIECE), PIECE)

    def add_first_momentum(p):
        rows = pl.ds(pl.multiple_of(p % 2 * PIECE, PIECE), PIECE)
        for h in range(2):
            @pl.when((y == p % 8 // 2) & (p // 8 == h))
            def _(h=h):
                ybox1[y] = ybox1[y] + MU * m1[rows, h * 128:(h + 1) * 128]

    def add_second_momentum(p):
        @pl.when(y == p // (Q2 // PIECE))
        def _():
            rows = pl.ds(pl.multiple_of(p % (Q2 // PIECE) * PIECE, PIECE), PIECE)
            ybox2[y] = ybox2[y] + MU * m2pad[rows, :]

    def add_plane(pay, inbox, ybox, first, count, n, add_momentum):
        here, rows = mine(first, count)

        @pl.when(here)
        def _():
            got = inbox.at[pl.ds(0, GRP - 1)]
            pltpu.make_async_copy(got, got, rs_recv.at[n]).wait()
            inbox[g] = pay[rows, :]
            ybox[y] = jnp.sum(inbox[...].astype(F32), axis=0)
            add_momentum(g - first)
            for d in range(1, NAR):
                link(ybox.at[y], ybox.at[y], y_send.at[n, d - 1], y_recv.at[n, d - 1], ys[d]).start()

    def add_group(ybox, res, first, count, n):
        here, rows = mine(first, count)

        @pl.when(here)
        def _():
            for d in range(1, NAR):
                link(ybox.at[y], ybox.at[y], y_send.at[n, d - 1], y_recv.at[n, d - 1], ys[d]).wait()
            res[rows, :] = (ybox[0] + ybox[1]) + (ybox[2] + ybox[3])

            def tell(i, c):
                pltpu.make_async_remote_copy(
                    src_ref=res.at[rows], dst_ref=res.at[rows], send_sem=ag_send.at[n], recv_sem=ag_recv.at[n],
                    device_id=((g + i) % GRP, y), device_id_type=MESH,
                ).start()
                return c

            lax.fori_loop(1, GRP, tell, 0)

    def take(res, first, count, n):
        here, rows = mine(first, count)
        for less, when in ((1, here), (0, jnp.logical_not(here))):
            @pl.when(when)
            def _(less=less):
                got = res.at[pl.ds(0, (count - less) * PIECE)]
                pltpu.make_async_copy(got, got, ag_recv.at[n]).wait()

    def sums_sent(pay, first, count, n):
        here, rows = mine(first, count)
        for less, when in ((1, here), (0, jnp.logical_not(here))):
            @pl.when(when)
            def _(less=less):
                gone = pay.at[pl.ds(0, (count - less) * PIECE)]
                pltpu.make_async_copy(gone, gone, rs_send.at[n]).wait()

        @pl.when(here)
        def _():
            gone = table.at[pl.ds(0, (GRP - 1) * PIECE)]
            pltpu.make_async_copy(gone, gone, ag_send.at[n]).wait()

    to_owner(pay2, inbox2, GRP - P2, P2, 1)

    def add_grads(q, fresh=False):
        da = dot(dbuf[q], w2t[...], TN)
        r = rbuf[q].astype(F32)
        ds = (da[:, :HID] + r).astype(BF)
        dn = ((da[:, HID:] - r) * wide(invc[q])).astype(BF)
        both = jnp.concatenate([dn, ds], axis=0)

        def rows512(i, c):
            part = dot(bsel[q, pl.ds(pl.multiple_of(i * 512, 512), 512), :], both)
            for h in range(2):
                rows = pl.ds(pl.multiple_of(h * FRONT + i * 512, 512), 512)
                now = part[:, h * 128:(h + 1) * 128]
                dh1[rows, :] = now if fresh else dh1[rows, :] + now
            return c

        lax.fori_loop(0, FRONT // 512, rows512, 0)

    db2 = jnp.sum(dlog.astype(F32), axis=1, keepdims=True)
    db2 = jnp.broadcast_to(db2, (CLS_PAD, 128)).T[0:1, :]
    swap_forward(rbuf, r_send, r_recv, SEED // 2)
    add_grads(y, True)
    swap_forward(dbuf, d_send, d_recv, 96)
    add_grads(left)
    add_grads(right)
    add_plane(pay2, inbox2, ybox2, GRP - P2, P2, 1, add_second_momentum)
    swap_end(rbuf, r_send, r_recv, SEED // 2)
    swap_end(dbuf, d_send, d_recv, 96)
    add_group(ybox2, res2, GRP - P2, P2, 1)
    add_grads(opp)

    def to_z(b, db):
        rows = pl.ds(pl.multiple_of(b * 256, 256), 256)
        dh = jnp.concatenate(
            [dh1[pl.ds(pl.multiple_of(h * FRONT + b * 256, 256), 256), :] for h in range(2)], axis=1
        )
        dz = (dh * slope[rows, :]).astype(BF)
        a1 = jnp.concatenate(
            [a1t[pl.ds(pl.multiple_of((2 * b + h) * 256, 256), 256), :] for h in range(2)], axis=1
        )
        part = dot(a1, dz)
        for h in range(2):
            now = slice(h * 256, (h + 1) * 256)
            gsum[now, :] = gsum[now, :] + part[:, h * 128:(h + 1) * 128]
        return db + jnp.sum(dz.astype(F32), axis=0, keepdims=True)

    gsum[...] = jnp.zeros((512, 128), F32)
    db1 = lax.fori_loop(0, FRONT // 256, to_z, jnp.zeros((1, HID), F32))
    pay1[0:512, :] = gsum[...].astype(BF)
    misc[...] = jnp.zeros((PIECE, 128), F32)

    def two(rows, v):
        hi = v.astype(BF).astype(F32)
        misc[rows:rows + 1, 0:v.shape[1]] = hi
        misc[rows + 4:rows + 5, 0:v.shape[1]] = v - hi

    two(0, db1[:, :128])
    two(1, db1[:, 128:])
    two(2, db2[:, :128])
    two(3, db2[:, 128:])
    hi = loss.astype(BF).astype(F32)
    misc[8:9, 0:1] = hi
    misc[9:10, 0:1] = loss - hi
    pay1[512:544, :] = misc[...].astype(BF)
    to_owner(pay1, inbox1, 0, P1, 0)

    take(res2, GRP - P2, P2, 1)
    mom2 = jnp.concatenate([res2[q * Q2:q * Q2 + CLS_PAD, :] for q in range(NAR)], axis=1)
    for q in range(NAR):
        x2s[q] = mom2[:, q * 128:(q + 1) * 128]
    o_all[ROW_M2:ROW_M2 + CLS_PAD, :] = x2s[y]
    x2 = mom2 * (1.0 / (jnp.sqrt(jnp.sum(mom2 * mom2, keepdims=True)) + 1e-07))
    x2 = ns_step(x2)
    add_plane(pay1, inbox1, ybox1, 0, P1, 0, add_first_momentum)
    x2 = ns_step(x2)
    add_group(ybox1, o_all, 0, P1, 0)
    x2 = ns_step(x2)
    for q in range(NAR):
        o_all[ROW_X2 + q * CLS_PAD:ROW_X2 + (q + 1) * CLS_PAD, :] = x2[:, q * 128:(q + 1) * 128]
    take(o_all, 0, P1, 0)

    for b in range(8):
        blk = gbuf.at[y, b * 256:(b + 1) * 256, :]
        link(blk, blk, h_send.at[0, b], h_recv.at[0, b], right).wait_send()
        link(blk, blk, h_send.at[1, b], h_recv.at[1, b], left).wait_send()
        blk = gbuf.at[opp, b * 256:(b + 1) * 256, :]
        link(blk, blk, h_send.at[2, b], h_recv.at[2, b], right).wait_send()
    swap_sent(rbuf, r_send, r_recv, SEED // 2)
    swap_sent(dbuf, d_send, d_recv, 96)

    sums_sent(pay2, GRP - P2, P2, 1)
    sums_sent(pay1, 0, P1, 0)


def main(reqt, feat, idx1t, msk1t, idx2t, msk2t, labels, live, w1, w2own, m1, m2own, bias):
    vm = pl.BlockSpec(memory_space=pltpu.VMEM)
    dma = pltpu.SemaphoreType.DMA
    sds = jax.ShapeDtypeStruct
    V = pltpu.VMEM
    return pl.pallas_call(
        main_kernel,
        out_shape=sds((ROWS, 128), F32),
        in_specs=[vm, pl.BlockSpec(memory_space=pl.ANY)] + [vm] * 11,
        out_specs=vm,
        scratch_shapes=[
            V((SRC + 8, D_IN), F32),
            V((OWN, D_IN), BF),
            V((SRC, D_IN), BF),
            V((CAP, D_IN), F32),
            V((DEV, 128), jnp.int32),
            V((DEV, 128), jnp.int32),
            V((NAR, GRP, 1, 128), jnp.int32),
            V((16, FRONT), jnp.int32),
            V((256, 128), jnp.int32),
            V((1, FRONT), F32),
            V((256, D_IN), F32),
            V((256, D_IN), F32),
            V((FRONT, HID), F32),
            V((NAR, FRONT, HID), BF),
            V((NAR, 2 * SEED, FRONT), BF),
            V((NAR, FRONT, 2 * SEED), BF),
            V((8, 16, SEED), jnp.int32),
            V((16, SEED), jnp.int32),
            V((16, SEED), jnp.int32),
            V((SEED, 32), jnp.int32),
            V((256, SRC), BF),
            V((256, 32), jnp.int32),
            V((NAR, SEED, 128), F32),
            V((SEED, 128), F32),
            V((NAR, SEED, HID), BF),
            V((NAR, CLS_PAD, SEED), BF),
            V((NAR, 64, HID), BF),
            V((NAR, CLS_PAD, 128), BF),
            V((Q2, 128), F32),
            V((NAR, 16, SEED), jnp.int32),
            V((CLS_PAD, 2 * HID), BF),
            V((HID, 128), F32),
            V((P1 * PIECE, 128), BF),
            V((P2 * PIECE, 128), BF),
            V((PIECE, 128), F32),
            V((GRP, PIECE, 128), BF),
            V((GRP, PIECE, 128), BF),
            V((NAR, PIECE, 128), F32),
            V((NAR, PIECE, 128), F32),
            V((P2 * PIECE, 128), F32),
            V((NAR, CLS_PAD, 128), F32),
            pltpu.SMEM((DEV, 1, 128), jnp.int32),
            pltpu.SMEM((256, 128), jnp.int32),
            dma, dma((3,)), dma((GRP,)), dma((NAR,)), dma((NAR,)), dma((GRP,)), dma, dma, dma((3, 3)), dma((3, 3)),
            dma((3, 8)), dma((3, 8)), dma((4,)), dma((4,)), dma((4,)), dma((4,)),
            dma((2,)), dma((2,)), dma((2, 3)), dma((2, 3)), dma((2,)), dma((2,)),
        ],
        compiler_params=pltpu.CompilerParams(
            collective_id=0, has_side_effects=True, vmem_limit_bytes=62 * 2**20
        ),
    )(reqt, feat, idx1t, msk1t, idx2t, msk2t, labels, live, w1, w2own, m1, m2own, bias)


def update_kernel(
    res, w1own, w2own, bias, biasm, biasv,
    o_loss, o_first, o_second, o_mom1, o_mom2, o_flow, o_slow, o_bias, o_bm, o_bv,
    x1s, x2s,
):
    y = lax.axis_index("nar")
    mom1 = jnp.concatenate([res[0:256, :], res[256:512, :]], axis=1)
    x1s[...] = mom1
    block64 = pl.ds(pl.multiple_of(y * 64, 64), 64)
    o_mom1[...] = x1s[block64, :]
    x1 = mom1 * (1.0 / (jnp.sqrt(jnp.sum(mom1 * mom1, keepdims=True)) + 1e-07))
    x2 = jnp.concatenate([res[ROW_X2 + q * CLS_PAD:ROW_X2 + (q + 1) * CLS_PAD, :] for q in range(NAR)], axis=1)
    for i in range(NS_ITERS):
        x1 = ns_step(x1)
        if i < 2:
            x2 = ns_step(x2)
    x1s[...] = x1
    for q in range(NAR):
        x2s[q] = x2[:, q * 128:(q + 1) * 128]
    first_new = w1own[...] * (1.0 - WDECAY) - x1s[block64, :]
    o_first[...] = first_new
    o_flow[...] = first_new.astype(BF)
    second = w2own[...] * (1.0 - WDECAY) - (2 * HID / CLS) ** 0.5 * x2s[y][0:CLS, :]
    o_second[...] = second
    o_slow[...] = second.astype(BF)
    o_mom2[...] = res[ROW_M2:ROW_M2 + CLS, :]

    gb = res[512:516, :] + res[516:520, :]
    gb = jnp.concatenate([gb[0:1, :], gb[1:2, :], gb[2:3, :], gb[3:4, 0:44]], axis=1)
    m_new = BETA_ONE * biasm[...] + (1.0 - BETA_ONE) * gb
    v_new = BETA_TWO * biasv[...] + (1.0 - BETA_TWO) * gb * gb
    m_hat = m_new / (1.0 - BETA_ONE**STEP)
    v_hat = v_new / (1.0 - BETA_TWO**STEP)
    o_bias[...] = bias[...] * (1.0 - LR_BIAS * WDECAY) - LR_BIAS * m_hat / (jnp.sqrt(v_hat) + EPSILON)
    o_bm[...] = m_new
    o_bv[...] = v_new
    o_loss[...] = res[520:521, 0:1] + res[521:522, 0:1]


def update(*args):
    vm = pl.BlockSpec(memory_space=pltpu.VMEM)
    sds = jax.ShapeDtypeStruct
    return pl.pallas_call(
        update_kernel,
        out_shape=[
            sds((1, 1), F32), sds((64, HID), F32), sds((CLS, 128), F32), sds((64, HID), F32), sds((CLS, 128), F32),
            sds((64, HID), BF), sds((CLS, 128), BF), sds((1, 428), F32), sds((1, 428), F32), sds((1, 428), F32),
        ],
        in_specs=[vm] * 6,
        out_specs=[vm] * 10,
        scratch_shapes=[pltpu.VMEM((2 * D_IN, HID), F32), pltpu.VMEM((NAR, CLS_PAD, 128), F32)],
        compiler_params=pltpu.CompilerParams(vmem_limit_bytes=32 * 2**20),
    )(*args)


def per_device(
    features, requests, index_one, mask_one, index_two, mask_two, labels, seed_live,
    w_first, w_second, mom_first, mom_second, biases, bias_m, bias_v,
):
    w2own, bias = w_second.T, biases[None, :]
    res = main(
        requests.T, features, index_one.T, mask_one.T, index_two.T, mask_two.T, labels[None, :], seed_live[None, :],
        w_first, w2own, mom_first, mom_second.T, bias,
    )
    loss, first_new, second_new, mom_one, mom_two, first_low, second_low, bias_new, m_new, v_new = update(
        res, w_first, w2own, bias, bias_m[None, :], bias_v[None, :]
    )
    return (
        loss.reshape(()), first_new, second_new.T, mom_one, mom_two.T, first_low, second_low.T,
        bias_new.reshape(-1), m_new.reshape(-1), v_new.reshape(-1),
    )


def solution(mesh):
    both = ("grp", "nar")
    placed = (
        P(both, None), P(both, None), P(both, None), P(both, None), P(both, None), P(both, None),
        P(both), P(both), P("nar", None), P("nar", None), P("nar", None), P("nar", None), P(), P(), P(),
    )
    nar = P("nar", None)
    return jax.shard_map(
        per_device, mesh=mesh, in_specs=placed,
        out_specs=(P(), nar, nar, nar, nar, nar, nar, P(), P(), P()), check_vma=False,
    )
```

```python
import functools

import jax
import jax.numpy as jnp
from jax import lax
from jax.experimental import pallas as pl
from jax.experimental.pallas import tpu as pltpu
from jax.sharding import PartitionSpec as P

HID = 256
CLS = 172
CLS_PAD = 176
D_IN = 128
F1 = 15
F2 = 10
NS_ITERS = 5
STEP = 10
LAM = 0.5
MU = 0.95
WDECAY = 0.01
LR_BIAS = 0.05
BETA_ONE = 0.9
BETA_TWO = 0.999
EPSILON = 1e-08
NS_A = 3.4445
NS_B = -4.775
NS_C = 2.0315
HIGH = lax.Precision.HIGHEST
MESH = pl.DeviceIdType.MESH
BF = jnp.bfloat16
F32 = jnp.float32

DEV = 128
NAR = 4
OWN = 8192
CAP = 64
SRC = 8192
FRONT = 2048
SEED = 512


def all_to(t):
    return (t // NAR, t % NAR)


PIECE = 32
P1 = 17
Q2 = 192
P2 = 24
GRP = 32
ROW_M2 = P1 * PIECE
ROW_X2 = ROW_M2 + CLS_PAD
ROWS = ROW_X2 + NAR * CLS_PAD
SEEDS_ALL = SEED * DEV


def dot(a, b, dims=((1,), (0,))):
    return lax.dot_general(a, b, (dims, ((), ())), preferred_element_type=F32)


NN = ((1,), (0,))
NT = ((1,), (1,))
TN = ((0,), (0,))


def split(a):
    hi = a.astype(BF)
    return hi, (a - hi.astype(F32)).astype(BF)


def dot3(a, b, dims):
    (ah, al), (bh, bl) = a, b
    return dot(
        jnp.concatenate([ah, ah, al], axis=dims[0][0]), jnp.concatenate([bh, bl, bh], axis=dims[1][0]), dims
    )


def ns_step(x):
    xs = split(x)
    gram = dot3(xs, xs, NT)
    gs = split(gram)
    mix = NS_B * gram + NS_C * dot3(gs, gs, NN)
    return NS_A * x + dot3(split(mix), xs, NN)


def spread(row):
    return jnp.broadcast_to(row, (128, 128)).T


def main_kernel(
    reqt, feat, idx1t, msk1t, idx2t, msk2t, labels, live, w1, w2own, m1, m2own, bias,
    o_all,
    sums, table, featb, pulled, stage, reqv, reqin, mid, idxv, idxp, invv, near, own, slope, gbuf, fsel, bsel, unit_of, lows, selfs, idc, ssel, idm, invc, livec, rbuf, dbuf,
    gw1, gw2t, m2pad, gidx2, w2t, b2c, pay1, pay2, misc, inbox1, inbox2, ybox1, ybox2, res2, x2s,
    reqs, idx,
    feat_sem, loc_sem, ask_sem, req_send, mid_recv, req_recv, row_send, row_recv, nar_send, nar_recv,
    h_send, h_recv, r_send, r_recv, d_send, d_recv, rs_send, rs_recv, y_send, y_recv, ag_send, ag_recv,
):
    a1t, dh1, gsum = featb, table, table.at[3 * FRONT:3 * FRONT + 512]
    g = lax.axis_index("grp")
    y = lax.axis_index("nar")
    me = g * NAR + y
    left, right, opp = (y + 3) % NAR, (y + 1) % NAR, (y + 2) % NAR

    load = pltpu.make_async_copy(feat, featb, feat_sem)
    load.start()

    barrier = pltpu.get_barrier_semaphore()

    ys = [(y + d) % NAR for d in range(NAR)]

    def greet(i, c):
        pl.semaphore_signal(barrier, inc=1, device_id=((g + i) % GRP, y), device_id_type=MESH)
        return c

    for d in range(1, NAR):
        pl.semaphore_signal(barrier, inc=1, device_id=(g, ys[d]), device_id_type=MESH)
    lax.fori_loop(1, GRP, greet, 0)

    def link(src, dst, ssem, rsem, to):
        return pltpu.make_async_remote_copy(
            src_ref=src, dst_ref=dst, send_sem=ssem, recv_sem=rsem, device_id=(g, to), device_id_type=MESH
        )

    reqv[...] = jnp.concatenate([reqt[...], jnp.zeros((DEV - CAP, DEV), jnp.int32)], axis=0).T
    ask_rows = reqv.reshape(GRP, NAR, 1, 128)
    got_rows = reqin.reshape(DEV, 1, 128)

    gw1[y] = w1[...].astype(BF)
    pad = CLS_PAD - CLS
    gw2t[y] = jnp.concatenate([w2own[...], jnp.zeros((pad, 128), F32)], axis=0).astype(BF)
    m2pad[...] = jnp.concatenate([m2own[...], jnp.zeros((Q2 - CLS, 128), F32)], axis=0)
    gidx2[y] = jnp.concatenate(
        [idx2t[0:1, :], jnp.where(msk2t[...] > 0, idx2t[1:, :], -1), jnp.zeros((5, SEED), jnp.int32)], axis=0
    )
    shared = (gidx2, gw1, gw2t)

    pl.semaphore_wait(barrier, GRP + NAR - 2)

    def ask_group(d):
        return pltpu.make_async_remote_copy(
            src_ref=ask_rows.at[:, ys[d]], dst_ref=mid.at[y], send_sem=req_send.at[d], recv_sem=mid_recv.at[d],
            device_id=(g, ys[d]), device_id_type=MESH,
        )

    for d in range(1, NAR):
        ask_group(d).start()
    keep = pltpu.make_async_copy(ask_rows.at[:, y], mid.at[y], loc_sem.at[2])
    keep.start()
    for n, a in enumerate(shared):
        for d in range(1, NAR):
            link(a.at[y], a.at[y], nar_send.at[n, d - 1], nar_recv.at[n, d - 1], (y + d) % NAR).start()

    msk = msk1t[...]
    idxv[0:1, :] = idx1t[0:1, :]
    idxv[1:16, :] = jnp.where(msk > 0, idx1t[1:16, :], SRC)
    invv[...] = 1.0 / jnp.maximum(jnp.sum(msk.astype(F32), axis=0, keepdims=True), 1.0)
    for half in range(2):
        parts = []
        for r in range(8):
            parts.append(jnp.concatenate(
                [idxv[:, (half * 4 + b) * 256 + r * 32:(half * 4 + b) * 256 + r * 32 + 32] for b in range(4)], axis=1
            ))
        idxp[half * 128:(half + 1) * 128, :] = jnp.concatenate(parts, axis=0).T
    to_smem = [pltpu.make_async_copy(idxp, idx, loc_sem.at[0])]
    for c in to_smem:
        c.start()

    keep.wait()
    for d in range(1, NAR):
        ask_group(d).wait()
    own_rows = pl.ds(pl.multiple_of(g * NAR, NAR), NAR)

    def ask(i, c):
        n = (i * 13) % GRP
        t = (g + n) % GRP
        pltpu.make_async_remote_copy(
            src_ref=mid.at[:, t], dst_ref=got_rows.at[own_rows], send_sem=req_send.at[0], recv_sem=req_recv.at[n],
            device_id=(t, y), device_id_type=MESH,
        ).start()
        return c

    lax.fori_loop(1, GRP, ask, 0)
    keep = pltpu.make_async_copy(mid.at[:, g], got_rows.at[own_rows], loc_sem.at[2])
    keep.start()

    load.wait()

    def widen_features(i, c):
        rows = pl.ds(pl.multiple_of(i * 256, 256), 256)
        table[rows, :] = featb[rows, :].astype(F32)
        return c

    lax.fori_loop(0, OWN // 256, widen_features, 0)

    lane32 = lax.broadcasted_iota(jnp.int32, (16, 128), 1)
    sub32 = lax.broadcasted_iota(jnp.int32, (32, 128), 0)
    lane16 = lane32.astype(jnp.int16)
    iota16 = lax.broadcasted_iota(jnp.int32, (16, 128), 0).astype(jnp.int16)
    one, zero = jnp.ones((16, 128), BF), jnp.zeros((16, 128), BF)

    def unit(digit):
        v = jnp.ones_like(digit)
        for j in range(1, 8):
            v = jnp.where(digit == j, 1 << 4 * j, v)
        return v

    def count(acc, j):
        return ((acc >> (4 * j)) & 15).astype(F32).astype(BF)

    def keys_units(ids):
        return (ids & 127) + (ids >> 10) * 128, unit((ids >> 7) & 7)

    def word(pos, keys, units):
        acc = jnp.zeros((16, 128), jnp.int32)
        for k, u in zip(keys, units):
            acc = acc + jnp.where(pos == k, u, 0)
        return acc

    def spread_columns(blk, ks):
        return [jnp.broadcast_to(blk[:, k:k + 1], (16, 128)) for k in ks]

    ids = gidx2[y]
    keys, units = keys_units(ids)
    idc[...] = jnp.concatenate([ids[0:1, :], keys[1:, :], units], axis=0).T

    def seeds16(i):
        at = pl.multiple_of(i * 16, 16)
        blk = idc[pl.ds(at, 16), :]
        self_row = jnp.broadcast_to(blk[:, 0:1], (16, 128)).astype(jnp.int16)
        return at, (spread_columns(blk, range(1, 1 + F2)), spread_columns(blk, range(17, 17 + F2)), self_row)

    def forward_marks(at, want, q):
        keys, units, self_row = want
        for w in range(2):
            acc = word(lane32 + 128 * (2 * q + w), keys, units)
            for j in range(8):
                c = w * 8 + j
                fsel[q, pl.ds(at, 16), c * 128:(c + 1) * 128] = count(acc, j)
                here = lane16 + jnp.full((16, 128), q * FRONT + c * 128, jnp.int32).astype(jnp.int16)
                fsel[q, pl.ds(SEED + at, 16), c * 128:(c + 1) * 128] = jnp.where(here == self_row, one, zero)

    view = table.reshape(SRC + 8, 1, D_IN)
    my_rows = pl.ds(pl.multiple_of(me * CAP, CAP), CAP)

    def pick(t, u, slot):
        for half in range(0, CAP, 32):
            rows = [view[reqs[t * NAR + u, 0, half + r]] for r in range(32)]
            for r in range(32):
                stage[half + r:half + r + 1, :] = rows[r]
        featb[slot, :] = stage[...].astype(BF)

    def serve_one(t, u, slot):
        pick(t, u, slot)
        pltpu.make_async_remote_copy(
            src_ref=featb.at[slot], dst_ref=pulled.at[my_rows],
            send_sem=row_send, recv_sem=row_recv, device_id=(t, u), device_id_type=MESH,
        ).start()

    def asked(n):
        rows = got_rows.at[pl.ds(0, NAR)]
        pltpu.make_async_copy(rows, rows, req_recv.at[n]).wait()

    def to_scalars(t, n):
        rows = pl.ds(pl.multiple_of(t * NAR, NAR), NAR)
        return pltpu.make_async_copy(got_rows.at[rows], reqs.at[rows], ask_sem.at[n])

    def whose(i):
        n = (i * 13) % GRP
        return n, (g + GRP - n) % GRP

    def fetch(i):
        n, t = whose(i)
        asked(n)
        to_scalars(t, n).start()

    def serve(i, c):
        n, t = whose(i)

        @pl.when(i < GRP - 1)
        def _():
            fetch(i + 1)

        to_scalars(t, n).wait()
        at, want = seeds16(i)
        for d in range(NAR):
            forward_marks(at, want, d)
            serve_one(t, ys[d], pl.ds(pl.multiple_of((i * NAR + d) * CAP, CAP), CAP))
        return c

    fetch(1)
    lax.fori_loop(1, GRP, serve, 0)
    keep.wait()
    to_scalars(g, 0).start()
    to_scalars(g, 0).wait()
    at, want = seeds16(0)
    for d in range(NAR):
        forward_marks(at, want, d)
    for d in range(1, NAR):
        serve_one(g, ys[d], pl.ds(d * CAP, CAP))
    pick(g, y, pl.ds(0, CAP))
    pulled[my_rows, :] = featb[0:CAP, :]

    for n, a in enumerate(shared):
        for d in range(1, NAR):
            link(a.at[y], a.at[y], nar_send.at[n, d - 1], nar_recv.at[n, d - 1], (y + d) % NAR).wait()
    for q in range(NAR):
        w2t[:, q * 128:(q + 1) * 128] = gw2t[q]
    last = jnp.concatenate([bias[0:1, 384:428], jnp.zeros((1, 84), F32)], axis=1)
    b2c[...] = jnp.concatenate([spread(bias[0:1, 256:384]), spread(last)], axis=0)

    def column(row):
        return jnp.concatenate([spread(row[:, c * 128:(c + 1) * 128]) for c in range(SEED // 128)], axis=0)

    for q in range(NAR):
        n = jnp.sum((gidx2[q, 1:1 + F2, :] >= 0).astype(F32), axis=0, keepdims=True)
        invc[q] = column(1.0 / jnp.maximum(n, 1.0))
    livec[...] = column(2.0 * LAM / HID / SEEDS_ALL * live[...].astype(F32))

    def backward_marks(q, carry):
        r = gidx2[q] - y * FRONT
        lows[...] = r & 31
        inside = (r >= 0) & (r < FRONT)
        units = unit((r >> 5) & 7)
        for w in range(8):
            unit_of[w] = jnp.where(inside & ((r >> 8) == w), units, 0)
        selfs[...] = jnp.broadcast_to(r[0:1, :], (16, SEED))

        def column(c, carry2):
            lanes = pl.ds(pl.multiple_of(c * 128, 128), 128)
            accs = [jnp.zeros((32, 128), jnp.int32) for _ in range(8)]
            for k in range(1, 1 + F2):
                hit = sub32 == jnp.broadcast_to(lows[k:k + 1, lanes], (32, 128))
                for w in range(8):
                    u = jnp.broadcast_to(unit_of[w, k:k + 1, lanes], (32, 128))
                    accs[w] = accs[w] + jnp.where(hit, u, 0)
            for w in range(8):
                for j in range(8):
                    first = (w * 8 + j) * 32
                    bsel[q, first:first + 32, lanes] = count(accs[w], j)
            self_row = selfs[:, lanes].astype(jnp.int16)
            lanes = pl.ds(pl.multiple_of(SEED + c * 128, 128), 128)
            for t in range(FRONT // 16):
                here = iota16 + jnp.full((16, 128), t * 16, jnp.int32).astype(jnp.int16)
                bsel[q, t * 16:(t + 1) * 16, lanes] = jnp.where(here == self_row, one, zero)
            return carry2

        lax.fori_loop(0, SEED // 128, column, 0)
        return carry

    def sum_marks(i):
        at = pl.multiple_of(i // 2 * 16, 16)
        half = i % 2
        blk = idm[pl.ds(at, 16), :]
        keys, units = spread_columns(blk, range(1, 1 + F1)), spread_columns(blk, range(17, 17 + F1))
        for w in range(4):
            acc = word(lane32 + (half * 4 + w) * 128, keys, units)
            for j in range(8):
                col = pl.ds(pl.multiple_of(half * (SRC // 2) + (w * 8 + j) * 128, 128), 128)
                ssel[pl.ds(at, 16), col] = count(acc, j)

    def sum_ids(b):
        idm[...] = jnp.concatenate(keys_units(idxv[:, cols(b)]), axis=0).T

    def cols(b):
        return pl.ds(pl.multiple_of(b * 256, 256), 256)

    def one_mark(i, c):
        sum_marks(i)
        return c

    sum_ids(0)
    lax.fori_loop(0, 32, one_mark, 0)
    lax.fori_loop(0, NAR, backward_marks, 0)

    come = pulled.at[pl.ds(0, (DEV - 1) * CAP)]
    pltpu.make_async_copy(come, come, row_recv).wait()
    gone = featb.at[pl.ds(CAP, (DEV - 1) * CAP)]
    pltpu.make_async_copy(gone, gone, row_send).wait()
    sent = mid.at[:, pl.ds(0, GRP - 1)]
    pltpu.make_async_copy(sent, sent, req_send.at[0]).wait()

    def widen(i, c):
        rows = pl.ds(pl.multiple_of(i * 256, 256), 256)
        table[rows, :] = pulled[rows, :].astype(F32)
        return c

    lax.fori_loop(0, SRC // 256, widen, 0)
    table[SRC:SRC + 8, :] = jnp.zeros((8, D_IN), F32)
    for c in to_smem:
        c.wait()

    def add_blocks(which):
        marks = [lambda n, q=q, b=b: fsel[q, pl.ds(n, SEED), cols(b)] for q, b in which]
        blocks = jnp.concatenate([gbuf[q, cols(b), :] for q, b in which], axis=0)

        def rows512(i, c):
            n = pl.multiple_of(i * SEED, SEED)
            part = dot(jnp.concatenate([m(n) for m in marks], axis=1), blocks)
            for h in range(2):
                rows = pl.ds(pl.multiple_of(h * 2 * SEED + i * SEED, SEED), SEED)
                sums[rows, :] = sums[rows, :] + part[:, h * 128:(h + 1) * 128]
            return c

        lax.fori_loop(0, 2, rows512, 0)

    def forward(b):
        from_left, from_right = gbuf.at[left, cols(b), :], gbuf.at[right, cols(b), :]
        link(from_left, from_left, h_send.at[0, b], h_recv.at[0, b], right).wait_recv()

        @pl.when(b % 2 == 0)
        def _():
            link(from_left, from_left, h_send.at[2, b], h_recv.at[2, b], right).start()

        link(from_right, from_right, h_send.at[1, b], h_recv.at[1, b], left).wait_recv()

        @pl.when(b % 2 == 1)
        def _():
            link(from_right, from_right, h_send.at[2, b], h_recv.at[2, b], left).start()

        add_blocks([(left, b), (right, b)])

    def add_opposite(b):
        blk = gbuf.at[opp, cols(b), :]
        link(blk, blk, h_send.at[2, b], h_recv.at[2, b], right).wait_recv()
        add_blocks([(opp, b)])

    def load_sums(b):
        def some(i, c):
            found = []
            for e in range(2):
                line = b * 32 + 2 * i + e
                for r in range(8):
                    self_row = view[idx[line, r * 16]]
                    rows = [view[idx[line, r * 16 + 1 + k]] for k in range(F1)]
                    while len(rows) > 1:
                        rows = [p + q for p, q in zip(rows[::2], rows[1::2])] + ([rows[-1]] if len(rows) % 2 else [])
                    found.append((r * 32 + 2 * i + e, self_row, rows[0]))
            for at, self_row, total in found:
                own[pl.ds(at, 1), :] = self_row
                near[pl.ds(at, 1), :] = total
            return c

        lax.fori_loop(0, 16, some, 0)
        finish(b)

    def multiply_sums(b):
        def some(i, c):
            found = []
            for e in range(2):
                for r in range(8):
                    found.append((r * 32 + 2 * i + e, view[idx[b * 32 + 2 * i + e, r * 16]]))
            for at, self_row in found:
                own[pl.ds(at, 1), :] = self_row
            return c

        lax.fori_loop(0, 16, some, 0)
        near[...] = dot(ssel[...], pulled[...])
        finish(b)

    def finish(b):
        rows = cols(b)
        scale = jnp.concatenate(
            [spread(invv[0:1, pl.ds(pl.multiple_of(b * 256 + c * 128, 128), 128)]) for c in range(2)], axis=0
        )
        act = jnp.concatenate([own[...].astype(BF), (near[...] * scale).astype(BF)], axis=1)
        a1 = act.T
        for h in range(2):
            a1t[pl.ds(pl.multiple_of((2 * b + h) * 256, 256), 256), :] = a1[:, h * 128:(h + 1) * 128]
        z = dot(act, gw1[...].reshape(2 * D_IN, HID)) + bias[0:1, 0:HID]
        sig = 1.0 / (1.0 + jnp.exp(-z))
        h1 = z * sig
        slope[rows, :] = sig + h1 * (1.0 - sig)
        gbuf[y, rows, :] = h1.astype(BF)
        blk = gbuf.at[y, rows, :]
        link(blk, blk, h_send.at[0, b], h_recv.at[0, b], right).start()
        link(blk, blk, h_send.at[1, b], h_recv.at[1, b], left).start()

        add_blocks([(y, b)])

        @pl.when(b > 0)
        def _():
            forward(b - 1)

        @pl.when(b > 2)
        def _():
            add_opposite(b - 3)

    def loaded(b, c):
        load_sums(b)
        return c

    sums[...] = jnp.zeros((4 * SEED, 128), F32)
    multiply_sums(0)
    lax.fori_loop(1, 8, loaded, 0)
    forward(7)

    for b in range(5, 8):
        add_opposite(b)

    def wide(a):
        return jnp.concatenate([a, a], axis=1)

    def seeds(first):
        return jnp.concatenate([sums[h * 2 * SEED + first:h * 2 * SEED + first + SEED, :] for h in range(2)], axis=1)

    near2 = (seeds(0) * wide(invc[y])).astype(BF)
    self2 = seeds(SEED).astype(BF)
    alive = live[...].astype(F32)
    diff = self2.astype(F32) - near2.astype(F32)
    pull_apart = wide(livec[...]) * diff

    def swap_start(buf, ssem, rsem):
        blk = buf.at[y]
        link(blk, blk, ssem.at[0], rsem.at[0], right).start()
        link(blk, blk, ssem.at[1], rsem.at[1], left).start()

    def swap_forward(buf, ssem, rsem, cut):
        blk = buf.at[left]
        link(blk, blk, ssem.at[0], rsem.at[0], right).wait_recv()
        half = buf.at[left, 0:cut, :]
        link(half, half, ssem.at[2], rsem.at[2], right).start()
        blk = buf.at[right]
        link(blk, blk, ssem.at[1], rsem.at[1], left).wait_recv()
        half = buf.at[right, cut:, :]
        link(half, half, ssem.at[3], rsem.at[3], left).start()

    def swap_end(buf, ssem, rsem, cut):
        half = buf.at[opp, 0:cut, :]
        link(half, half, ssem.at[2], rsem.at[2], right).wait_recv()
        half = buf.at[opp, cut:, :]
        link(half, half, ssem.at[3], rsem.at[3], left).wait_recv()

    def swap_sent(buf, ssem, rsem, cut):
        blk = buf.at[y]
        link(blk, blk, ssem.at[0], rsem.at[0], right).wait_send()
        link(blk, blk, ssem.at[1], rsem.at[1], left).wait_send()
        half = buf.at[left, 0:cut, :]
        link(half, half, ssem.at[2], rsem.at[2], right).wait_send()
        half = buf.at[right, cut:, :]
        link(half, half, ssem.at[3], rsem.at[3], left).wait_send()

    rbuf[y] = pull_apart.astype(BF)
    swap_start(rbuf, r_send, r_recv)

    act2 = jnp.concatenate([self2, near2], axis=1)
    cls = lax.broadcasted_iota(jnp.int32, (CLS_PAD, SEED), 0)
    b2 = b2c[0:CLS_PAD, :]
    logits = dot(w2t[...], act2, NT) + jnp.concatenate([b2] * 4, axis=1)
    logits = jnp.where(cls < CLS, logits, -1e30)
    top = jnp.max(logits, axis=0, keepdims=True)
    e = jnp.exp(logits - top)
    tot = jnp.sum(e, axis=0, keepdims=True)
    hot = cls == labels[...]
    picked = jnp.sum(jnp.where(hot, logits, 0.0), axis=0, keepdims=True)
    dlog = (alive * (e * (1.0 / tot) - jnp.where(hot, 1.0, 0.0)) * (1.0 / SEEDS_ALL)).astype(BF)
    dbuf[y] = dlog
    swap_start(dbuf, d_send, d_recv)

    loss = jnp.sum(alive * (top + jnp.log(tot) - picked), axis=1, keepdims=True)
    loss = loss + SEEDS_ALL / 2 * jnp.sum(pull_apart * diff, keepdims=True)
    g2t = dot(dlog, act2).astype(BF)
    for q in range(NAR):
        pay2[q * Q2:q * Q2 + CLS_PAD, :] = g2t[:, q * 128:(q + 1) * 128]
        pay2[q * Q2 + CLS_PAD:(q + 1) * Q2, :] = jnp.zeros((Q2 - CLS_PAD, 128), BF)

    def to_owner(pay, inbox, first, count, n):
        def body(i, c):
            t = (g + i) % GRP
            p = t - first

            @pl.when((p >= 0) & (p < count))
            def _():
                pltpu.make_async_remote_copy(
                    src_ref=pay.at[pl.ds(pl.multiple_of(p * PIECE, PIECE), PIECE)], dst_ref=inbox.at[g],
                    send_sem=rs_send.at[n], recv_sem=rs_recv.at[n], device_id=(t, y), device_id_type=MESH,
                ).start()

            return c

        lax.fori_loop(1, GRP, body, 0)

    def mine(first, count):
        p = g - first
        return (p >= 0) & (p < count), pl.ds(pl.multiple_of(p * PIECE, PIECE), PIECE)

    def add_first_momentum(p):
        rows = pl.ds(pl.multiple_of(p % 2 * PIECE, PIECE), PIECE)
        for h in range(2):
            @pl.when((y == p % 8 // 2) & (p // 8 == h))
            def _(h=h):
                ybox1[y] = ybox1[y] + MU * m1[rows, h * 128:(h + 1) * 128]

    def add_second_momentum(p):
        @pl.when(y == p // (Q2 // PIECE))
        def _():
            rows = pl.ds(pl.multiple_of(p % (Q2 // PIECE) * PIECE, PIECE), PIECE)
            ybox2[y] = ybox2[y] + MU * m2pad[rows, :]

    def add_plane(pay, inbox, ybox, first, count, n, add_momentum):
        here, rows = mine(first, count)

        @pl.when(here)
        def _():
            got = inbox.at[pl.ds(0, GRP - 1)]
            pltpu.make_async_copy(got, got, rs_recv.at[n]).wait()
            inbox[g] = pay[rows, :]
            ybox[y] = jnp.sum(inbox[...].astype(F32), axis=0)
            add_momentum(g - first)
            for d in range(1, NAR):
                link(ybox.at[y], ybox.at[y], y_send.at[n, d - 1], y_recv.at[n, d - 1], ys[d]).start()

    def add_group(ybox, res, first, count, n):
        here, rows = mine(first, count)

        @pl.when(here)
        def _():
            for d in range(1, NAR):
                link(ybox.at[y], ybox.at[y], y_send.at[n, d - 1], y_recv.at[n, d - 1], ys[d]).wait()
            res[rows, :] = (ybox[0] + ybox[1]) + (ybox[2] + ybox[3])

            def tell(i, c):
                pltpu.make_async_remote_copy(
                    src_ref=res.at[rows], dst_ref=res.at[rows], send_sem=ag_send.at[n], recv_sem=ag_recv.at[n],
                    device_id=((g + i) % GRP, y), device_id_type=MESH,
                ).start()
                return c

            lax.fori_loop(1, GRP, tell, 0)

    def take(res, first, count, n):
        here, rows = mine(first, count)
        for less, when in ((1, here), (0, jnp.logical_not(here))):
            @pl.when(when)
            def _(less=less):
                got = res.at[pl.ds(0, (count - less) * PIECE)]
                pltpu.make_async_copy(got, got, ag_recv.at[n]).wait()

    def sums_sent(pay, first, count, n):
        here, rows = mine(first, count)
        for less, when in ((1, here), (0, jnp.logical_not(here))):
            @pl.when(when)
            def _(less=less):
                gone = pay.at[pl.ds(0, (count - less) * PIECE)]
                pltpu.make_async_copy(gone, gone, rs_send.at[n]).wait()

        @pl.when(here)
        def _():
            gone = table.at[pl.ds(0, (GRP - 1) * PIECE)]
            pltpu.make_async_copy(gone, gone, ag_send.at[n]).wait()

    to_owner(pay2, inbox2, GRP - P2, P2, 1)

    def add_grads(q, fresh=False):
        da = dot(dbuf[q], w2t[...], TN)
        r = rbuf[q].astype(F32)
        ds = (da[:, :HID] + r).astype(BF)
        dn = ((da[:, HID:] - r) * wide(invc[q])).astype(BF)
        both = jnp.concatenate([dn, ds], axis=0)

        def rows512(i, c):
            part = dot(bsel[q, pl.ds(pl.multiple_of(i * 512, 512), 512), :], both)
            for h in range(2):
                rows = pl.ds(pl.multiple_of(h * FRONT + i * 512, 512), 512)
                now = part[:, h * 128:(h + 1) * 128]
                dh1[rows, :] = now if fresh else dh1[rows, :] + now
            return c

        lax.fori_loop(0, FRONT // 512, rows512, 0)

    db2 = jnp.sum(dlog.astype(F32), axis=1, keepdims=True)
    db2 = jnp.broadcast_to(db2, (CLS_PAD, 128)).T[0:1, :]
    swap_forward(rbuf, r_send, r_recv, SEED // 2)
    add_grads(y, True)
    swap_forward(dbuf, d_send, d_recv, 96)
    add_grads(left)
    add_grads(right)
    add_plane(pay2, inbox2, ybox2, GRP - P2, P2, 1, add_second_momentum)
    swap_end(rbuf, r_send, r_recv, SEED // 2)
    swap_end(dbuf, d_send, d_recv, 96)
    add_group(ybox2, res2, GRP - P2, P2, 1)
    add_grads(opp)

    def to_z(b, db):
        rows = pl.ds(pl.multiple_of(b * 256, 256), 256)
        dh = jnp.concatenate(
            [dh1[pl.ds(pl.multiple_of(h * FRONT + b * 256, 256), 256), :] for h in range(2)], axis=1
        )
        dz = (dh * slope[rows, :]).astype(BF)
        a1 = jnp.concatenate(
            [a1t[pl.ds(pl.multiple_of((2 * b + h) * 256, 256), 256), :] for h in range(2)], axis=1
        )
        part = dot(a1, dz)
        for h in range(2):
            now = slice(h * 256, (h + 1) * 256)
            gsum[now, :] = gsum[now, :] + part[:, h * 128:(h + 1) * 128]
        return db + jnp.sum(dz.astype(F32), axis=0, keepdims=True)

    gsum[...] = jnp.zeros((512, 128), F32)
    db1 = lax.fori_loop(0, FRONT // 256, to_z, jnp.zeros((1, HID), F32))
    pay1[0:512, :] = gsum[...].astype(BF)
    misc[...] = jnp.zeros((PIECE, 128), F32)

    def two(rows, v):
        hi = v.astype(BF).astype(F32)
        misc[rows:rows + 1, 0:v.shape[1]] = hi
        misc[rows + 4:rows + 5, 0:v.shape[1]] = v - hi

    two(0, db1[:, :128])
    two(1, db1[:, 128:])
    two(2, db2[:, :128])
    two(3, db2[:, 128:])
    hi = loss.astype(BF).astype(F32)
    misc[8:9, 0:1] = hi
    misc[9:10, 0:1] = loss - hi
    pay1[512:544, :] = misc[...].astype(BF)
    to_owner(pay1, inbox1, 0, P1, 0)

    take(res2, GRP - P2, P2, 1)
    mom2 = jnp.concatenate([res2[q * Q2:q * Q2 + CLS_PAD, :] for q in range(NAR)], axis=1)
    for q in range(NAR):
        x2s[q] = mom2[:, q * 128:(q + 1) * 128]
    o_all[ROW_M2:ROW_M2 + CLS_PAD, :] = x2s[y]
    x2 = mom2 * (1.0 / (jnp.sqrt(jnp.sum(mom2 * mom2, keepdims=True)) + 1e-07))
    x2 = ns_step(x2)
    add_plane(pay1, inbox1, ybox1, 0, P1, 0, add_first_momentum)
    x2 = ns_step(x2)
    add_group(ybox1, o_all, 0, P1, 0)
    x2 = ns_step(x2)
    for q in range(NAR):
        o_all[ROW_X2 + q * CLS_PAD:ROW_X2 + (q + 1) * CLS_PAD, :] = x2[:, q * 128:(q + 1) * 128]
    take(o_all, 0, P1, 0)

    for b in range(8):
        blk = gbuf.at[y, b * 256:(b + 1) * 256, :]
        link(blk, blk, h_send.at[0, b], h_recv.at[0, b], right).wait_send()
        link(blk, blk, h_send.at[1, b], h_recv.at[1, b], left).wait_send()
        blk = gbuf.at[opp, b * 256:(b + 1) * 256, :]
        link(blk, blk, h_send.at[2, b], h_recv.at[2, b], right).wait_send()
    swap_sent(rbuf, r_send, r_recv, SEED // 2)
    swap_sent(dbuf, d_send, d_recv, 96)

    sums_sent(pay2, GRP - P2, P2, 1)
    sums_sent(pay1, 0, P1, 0)


def main(reqt, feat, idx1t, msk1t, idx2t, msk2t, labels, live, w1, w2own, m1, m2own, bias):
    vm = pl.BlockSpec(memory_space=pltpu.VMEM)
    dma = pltpu.SemaphoreType.DMA
    sds = jax.ShapeDtypeStruct
    V = pltpu.VMEM
    return pl.pallas_call(
        main_kernel,
        out_shape=sds((ROWS, 128), F32),
        in_specs=[vm, pl.BlockSpec(memory_space=pl.ANY)] + [vm] * 11,
        out_specs=vm,
        scratch_shapes=[
            V((4 * SEED, 128), F32),
            V((SRC + 8, D_IN), F32),
            V((OWN, D_IN), BF),
            V((SRC, D_IN), BF),
            V((CAP, D_IN), F32),
            V((DEV, 128), jnp.int32),
            V((DEV, 128), jnp.int32),
            V((NAR, GRP, 1, 128), jnp.int32),
            V((16, FRONT), jnp.int32),
            V((256, 128), jnp.int32),
            V((1, FRONT), F32),
            V((256, D_IN), F32),
            V((256, D_IN), F32),
            V((FRONT, HID), F32),
            V((NAR, FRONT, HID), BF),
            V((NAR, 2 * SEED, FRONT), BF),
            V((NAR, FRONT, 2 * SEED), BF),
            V((8, 16, SEED), jnp.int32),
            V((16, SEED), jnp.int32),
            V((16, SEED), jnp.int32),
            V((SEED, 32), jnp.int32),
            V((256, SRC), BF),
            V((256, 32), jnp.int32),
            V((NAR, SEED, 128), F32),
            V((SEED, 128), F32),
            V((NAR, SEED, HID), BF),
            V((NAR, CLS_PAD, SEED), BF),
            V((NAR, 64, HID), BF),
            V((NAR, CLS_PAD, 128), BF),
            V((Q2, 128), F32),
            V((NAR, 16, SEED), jnp.int32),
            V((CLS_PAD, 2 * HID), BF),
            V((HID, 128), F32),
            V((P1 * PIECE, 128), BF),
            V((P2 * PIECE, 128), BF),
            V((PIECE, 128), F32),
            V((GRP, PIECE, 128), BF),
            V((GRP, PIECE, 128), BF),
            V((NAR, PIECE, 128), F32),
            V((NAR, PIECE, 128), F32),
            V((P2 * PIECE, 128), F32),
            V((NAR, CLS_PAD, 128), F32),
            pltpu.SMEM((DEV, 1, 128), jnp.int32),
            pltpu.SMEM((256, 128), jnp.int32),
            dma, dma((3,)), dma((GRP,)), dma((NAR,)), dma((NAR,)), dma((GRP,)), dma, dma, dma((3, 3)), dma((3, 3)),
            dma((3, 8)), dma((3, 8)), dma((4,)), dma((4,)), dma((4,)), dma((4,)),
            dma((2,)), dma((2,)), dma((2, 3)), dma((2, 3)), dma((2,)), dma((2,)),
        ],
        compiler_params=pltpu.CompilerParams(
            collective_id=0, has_side_effects=True, vmem_limit_bytes=62 * 2**20
        ),
    )(reqt, feat, idx1t, msk1t, idx2t, msk2t, labels, live, w1, w2own, m1, m2own, bias)


def update_kernel(
    res, w1own, w2own, bias, biasm, biasv,
    o_loss, o_first, o_second, o_mom1, o_mom2, o_flow, o_slow, o_bias, o_bm, o_bv,
    x1s, x2s,
):
    y = lax.axis_index("nar")
    mom1 = jnp.concatenate([res[0:256, :], res[256:512, :]], axis=1)
    x1s[...] = mom1
    block64 = pl.ds(pl.multiple_of(y * 64, 64), 64)
    o_mom1[...] = x1s[block64, :]
    x1 = mom1 * (1.0 / (jnp.sqrt(jnp.sum(mom1 * mom1, keepdims=True)) + 1e-07))
    x2 = jnp.concatenate([res[ROW_X2 + q * CLS_PAD:ROW_X2 + (q + 1) * CLS_PAD, :] for q in range(NAR)], axis=1)
    for i in range(NS_ITERS):
        x1 = ns_step(x1)
        if i < 2:
            x2 = ns_step(x2)
    x1s[...] = x1
    for q in range(NAR):
        x2s[q] = x2[:, q * 128:(q + 1) * 128]
    first_new = w1own[...] * (1.0 - WDECAY) - x1s[block64, :]
    o_first[...] = first_new
    o_flow[...] = first_new.astype(BF)
    second = w2own[...] * (1.0 - WDECAY) - (2 * HID / CLS) ** 0.5 * x2s[y][0:CLS, :]
    o_second[...] = second
    o_slow[...] = second.astype(BF)
    o_mom2[...] = res[ROW_M2:ROW_M2 + CLS, :]

    gb = res[512:516, :] + res[516:520, :]
    gb = jnp.concatenate([gb[0:1, :], gb[1:2, :], gb[2:3, :], gb[3:4, 0:44]], axis=1)
    m_new = BETA_ONE * biasm[...] + (1.0 - BETA_ONE) * gb
    v_new = BETA_TWO * biasv[...] + (1.0 - BETA_TWO) * gb * gb
    m_hat = m_new / (1.0 - BETA_ONE**STEP)
    v_hat = v_new / (1.0 - BETA_TWO**STEP)
    o_bias[...] = bias[...] * (1.0 - LR_BIAS * WDECAY) - LR_BIAS * m_hat / (jnp.sqrt(v_hat) + EPSILON)
    o_bm[...] = m_new
    o_bv[...] = v_new
    o_loss[...] = res[520:521, 0:1] + res[521:522, 0:1]


def update(*args):
    vm = pl.BlockSpec(memory_space=pltpu.VMEM)
    sds = jax.ShapeDtypeStruct
    return pl.pallas_call(
        update_kernel,
        out_shape=[
            sds((1, 1), F32), sds((64, HID), F32), sds((CLS, 128), F32), sds((64, HID), F32), sds((CLS, 128), F32),
            sds((64, HID), BF), sds((CLS, 128), BF), sds((1, 428), F32), sds((1, 428), F32), sds((1, 428), F32),
        ],
        in_specs=[vm] * 6,
        out_specs=[vm] * 10,
        scratch_shapes=[pltpu.VMEM((2 * D_IN, HID), F32), pltpu.VMEM((NAR, CLS_PAD, 128), F32)],
        compiler_params=pltpu.CompilerParams(vmem_limit_bytes=32 * 2**20),
    )(*args)


def per_device(
    features, requests, index_one, mask_one, index_two, mask_two, labels, seed_live,
    w_first, w_second, mom_first, mom_second, biases, bias_m, bias_v,
):
    w2own, bias = w_second.T, biases[None, :]
    res = main(
        requests.T, features, index_one.T, mask_one.T, index_two.T, mask_two.T, labels[None, :], seed_live[None, :],
        w_first, w2own, mom_first, mom_second.T, bias,
    )
    loss, first_new, second_new, mom_one, mom_two, first_low, second_low, bias_new, m_new, v_new = update(
        res, w_first, w2own, bias, bias_m[None, :], bias_v[None, :]
    )
    return (
        loss.reshape(()), first_new, second_new.T, mom_one, mom_two.T, first_low, second_low.T,
        bias_new.reshape(-1), m_new.reshape(-1), v_new.reshape(-1),
    )


def solution(mesh):
    both = ("grp", "nar")
    placed = (
        P(both, None), P(both, None), P(both, None), P(both, None), P(both, None), P(both, None),
        P(both), P(both), P("nar", None), P("nar", None), P("nar", None), P("nar", None), P(), P(), P(),
    )
    nar = P("nar", None)
    return jax.shard_map(
        per_device, mesh=mesh, in_specs=placed,
        out_specs=(P(), nar, nar, nar, nar, nar, nar, P(), P(), P()), check_vma=False,
    )
```

```python
import functools

import jax
import jax.numpy as jnp
from jax import lax
from jax.experimental import pallas as pl
from jax.experimental.pallas import tpu as pltpu
from jax.sharding import PartitionSpec as P

HID = 256
CLS = 172
CLS_PAD = 176
D_IN = 128
F1 = 15
F2 = 10
NS_ITERS = 5
STEP = 10
LAM = 0.5
MU = 0.95
WDECAY = 0.01
LR_BIAS = 0.05
BETA_ONE = 0.9
BETA_TWO = 0.999
EPSILON = 1e-08
NS_A = 3.4445
NS_B = -4.775
NS_C = 2.0315
HIGH = lax.Precision.HIGHEST
MESH = pl.DeviceIdType.MESH
BF = jnp.bfloat16
F32 = jnp.float32

DEV = 128
NAR = 4
OWN = 8192
CAP = 64
SRC = 8192
FRONT = 2048
SEED = 512


def all_to(t):
    return (t // NAR, t % NAR)


PIECE = 32
P1 = 17
Q2 = 192
P2 = 24
GRP = 32
ROW_M2 = P1 * PIECE
ROW_X2 = ROW_M2 + CLS_PAD
ROWS = ROW_X2 + NAR * CLS_PAD
SEEDS_ALL = SEED * DEV


def dot(a, b, dims=((1,), (0,))):
    return lax.dot_general(a, b, (dims, ((), ())), preferred_element_type=F32)


NN = ((1,), (0,))
NT = ((1,), (1,))
TN = ((0,), (0,))


def split(a):
    hi = a.astype(BF)
    return hi, (a - hi.astype(F32)).astype(BF)


def dot3(a, b, dims):
    (ah, al), (bh, bl) = a, b
    return dot(
        jnp.concatenate([ah, ah, al], axis=dims[0][0]), jnp.concatenate([bh, bl, bh], axis=dims[1][0]), dims
    )


def ns_step(x):
    xs = split(x)
    gram = dot3(xs, xs, NT)
    gs = split(gram)
    mix = NS_B * gram + NS_C * dot3(gs, gs, NN)
    return NS_A * x + dot3(split(mix), xs, NN)


def spread(row):
    return jnp.broadcast_to(row, (128, 128)).T


def main_kernel(
    reqt, feat, idx1t, msk1t, idx2t, msk2t, labels, live, w1, w2own, m1, m2own, bias,
    o_all,
    table, featb, pulled, stage, reqv, reqin, mid, idxv, idxp, invv, near, own, slope, gbuf, fsel, bsel, unit_of, lows, idc, ssel, idm, invc, livec, rbuf, dbuf,
    gw1, gw2t, m2pad, gidx2, w2t, b2c, pay1, pay2, misc, inbox1, inbox2, ybox1, ybox2, res2, x2s,
    reqs, idx,
    feat_sem, loc_sem, ask_sem, req_send, mid_recv, req_recv, row_send, row_recv, nar_send, nar_recv,
    h_send, h_recv, r_send, r_recv, d_send, d_recv, rs_send, rs_recv, y_send, y_recv, ag_send, ag_recv,
):
    a1t, dh1, tot, gsum = featb, table, table.at[2 * FRONT:3 * FRONT], table.at[3 * FRONT:3 * FRONT + 512]
    g = lax.axis_index("grp")
    y = lax.axis_index("nar")
    me = g * NAR + y
    left, right, opp = (y + 3) % NAR, (y + 1) % NAR, (y + 2) % NAR

    load = pltpu.make_async_copy(feat, featb, feat_sem)
    load.start()

    barrier = pltpu.get_barrier_semaphore()

    ys = [(y + d) % NAR for d in range(NAR)]

    def greet(i, c):
        pl.semaphore_signal(barrier, inc=1, device_id=((g + i) % GRP, y), device_id_type=MESH)
        return c

    for d in range(1, NAR):
        pl.semaphore_signal(barrier, inc=1, device_id=(g, ys[d]), device_id_type=MESH)
    lax.fori_loop(1, GRP, greet, 0)

    def link(src, dst, ssem, rsem, to):
        return pltpu.make_async_remote_copy(
            src_ref=src, dst_ref=dst, send_sem=ssem, recv_sem=rsem, device_id=(g, to), device_id_type=MESH
        )

    reqv[...] = jnp.concatenate([reqt[...], jnp.zeros((DEV - CAP, DEV), jnp.int32)], axis=0).T
    ask_rows = reqv.reshape(GRP, NAR, 1, 128)
    got_rows = reqin.reshape(DEV, 1, 128)

    gw1[y] = w1[...].astype(BF)
    pad = CLS_PAD - CLS
    gw2t[y] = jnp.concatenate([w2own[...], jnp.zeros((pad, 128), F32)], axis=0).astype(BF)
    m2pad[...] = jnp.concatenate([m2own[...], jnp.zeros((Q2 - CLS, 128), F32)], axis=0)
    gidx2[y] = jnp.concatenate(
        [idx2t[0:1, :], jnp.where(msk2t[...] > 0, idx2t[1:, :], -1), jnp.zeros((5, SEED), jnp.int32)], axis=0
    )
    shared = (gidx2, gw1, gw2t)

    pl.semaphore_wait(barrier, GRP + NAR - 2)

    def ask_group(d):
        return pltpu.make_async_remote_copy(
            src_ref=ask_rows.at[:, ys[d]], dst_ref=mid.at[y], send_sem=req_send.at[d], recv_sem=mid_recv.at[d],
            device_id=(g, ys[d]), device_id_type=MESH,
        )

    for d in range(1, NAR):
        ask_group(d).start()
    keep = pltpu.make_async_copy(ask_rows.at[:, y], mid.at[y], loc_sem.at[2])
    keep.start()
    for n, a in enumerate(shared):
        for d in range(1, NAR):
            link(a.at[y], a.at[y], nar_send.at[n, d - 1], nar_recv.at[n, d - 1], (y + d) % NAR).start()

    msk = msk1t[...]
    idxv[0:1, :] = idx1t[0:1, :]
    idxv[1:16, :] = jnp.where(msk > 0, idx1t[1:16, :], SRC)
    invv[...] = 1.0 / jnp.maximum(jnp.sum(msk.astype(F32), axis=0, keepdims=True), 1.0)
    for half in range(2):
        parts = []
        for r in range(8):
            parts.append(jnp.concatenate(
                [idxv[:, (half * 4 + b) * 256 + r * 32:(half * 4 + b) * 256 + r * 32 + 32] for b in range(4)], axis=1
            ))
        idxp[half * 128:(half + 1) * 128, :] = jnp.concatenate(parts, axis=0).T
    to_smem = [pltpu.make_async_copy(idxp, idx, loc_sem.at[0])]
    for c in to_smem:
        c.start()

    keep.wait()
    for d in range(1, NAR):
        ask_group(d).wait()
    own_rows = pl.ds(pl.multiple_of(g * NAR, NAR), NAR)

    def ask(i, c):
        n = (i * 13) % GRP
        t = (g + n) % GRP
        pltpu.make_async_remote_copy(
            src_ref=mid.at[:, t], dst_ref=got_rows.at[own_rows], send_sem=req_send.at[0], recv_sem=req_recv.at[n],
            device_id=(t, y), device_id_type=MESH,
        ).start()
        return c

    lax.fori_loop(1, GRP, ask, 0)
    keep = pltpu.make_async_copy(mid.at[:, g], got_rows.at[own_rows], loc_sem.at[2])
    keep.start()

    load.wait()

    def widen_features(i, c):
        rows = pl.ds(pl.multiple_of(i * 256, 256), 256)
        table[rows, :] = featb[rows, :].astype(F32)
        return c

    lax.fori_loop(0, OWN // 256, widen_features, 0)

    lane32 = lax.broadcasted_iota(jnp.int32, (16, 128), 1)
    sub32 = lax.broadcasted_iota(jnp.int32, (32, 128), 0)
    lane16 = lane32.astype(jnp.int16)
    iota16 = lax.broadcasted_iota(jnp.int32, (16, 128), 0).astype(jnp.int16)
    one, zero = jnp.ones((16, 128), BF), jnp.zeros((16, 128), BF)

    def unit(digit):
        v = jnp.ones_like(digit)
        for j in range(1, 8):
            v = jnp.where(digit == j, 1 << 4 * j, v)
        return v

    def count(acc, j):
        return ((acc >> (4 * j)) & 15).astype(F32).astype(BF)

    def keys_units(ids):
        return (ids & 127) + (ids >> 10) * 128, unit((ids >> 7) & 7)

    def word(pos, keys, units):
        acc = jnp.zeros((16, 128), jnp.int32)
        for k, u in zip(keys, units):
            acc = acc + jnp.where(pos == k, u, 0)
        return acc

    def spread_columns(blk, ks):
        return [jnp.broadcast_to(blk[:, k:k + 1], (16, 128)) for k in ks]

    ids = gidx2[y]
    keys, units = keys_units(ids)
    idc[...] = jnp.concatenate([ids[0:1, :], keys[1:, :], units], axis=0).T

    def seeds16(i):
        at = pl.multiple_of(i * 16, 16)
        blk = idc[pl.ds(at, 16), :]
        self_row = jnp.broadcast_to(blk[:, 0:1], (16, 128)).astype(jnp.int16)
        return at, (spread_columns(blk, range(1, 1 + F2)), spread_columns(blk, range(17, 17 + F2)), self_row)

    def forward_marks(at, want, q):
        keys, units, self_row = want
        for w in range(2):
            acc = word(lane32 + 128 * (2 * q + w), keys, units)
            for j in range(8):
                c = w * 8 + j
                fsel[q, pl.ds(at, 16), c * 128:(c + 1) * 128] = count(acc, j)
                here = lane16 + jnp.full((16, 128), q * FRONT + c * 128, jnp.int32).astype(jnp.int16)
                fsel[q, pl.ds(SEED + at, 16), c * 128:(c + 1) * 128] = jnp.where(here == self_row, one, zero)

    view = table.reshape(SRC + 8, 1, D_IN)
    my_rows = pl.ds(pl.multiple_of(me * CAP, CAP), CAP)

    def pick(t, u, slot):
        for half in range(0, CAP, 32):
            rows = [view[reqs[t * NAR + u, 0, half + r]] for r in range(32)]
            for r in range(32):
                stage[half + r:half + r + 1, :] = rows[r]
        featb[slot, :] = stage[...].astype(BF)

    def serve_one(t, u, slot):
        pick(t, u, slot)
        pltpu.make_async_remote_copy(
            src_ref=featb.at[slot], dst_ref=pulled.at[my_rows],
            send_sem=row_send, recv_sem=row_recv, device_id=(t, u), device_id_type=MESH,
        ).start()

    def asked(n):
        rows = got_rows.at[pl.ds(0, NAR)]
        pltpu.make_async_copy(rows, rows, req_recv.at[n]).wait()

    def to_scalars(t, n):
        rows = pl.ds(pl.multiple_of(t * NAR, NAR), NAR)
        return pltpu.make_async_copy(got_rows.at[rows], reqs.at[rows], ask_sem.at[n])

    def whose(i):
        n = (i * 13) % GRP
        return n, (g + GRP - n) % GRP

    def fetch(i):
        n, t = whose(i)
        asked(n)
        to_scalars(t, n).start()

    def serve(i, c):
        n, t = whose(i)

        @pl.when(i < GRP - 1)
        def _():
            fetch(i + 1)

        to_scalars(t, n).wait()
        at, want = seeds16(i)
        for d in range(NAR):
            forward_marks(at, want, d)
            serve_one(t, ys[d], pl.ds(pl.multiple_of((i * NAR + d) * CAP, CAP), CAP))
        return c

    fetch(1)
    lax.fori_loop(1, GRP, serve, 0)
    keep.wait()
    to_scalars(g, 0).start()
    to_scalars(g, 0).wait()
    at, want = seeds16(0)
    for d in range(NAR):
        forward_marks(at, want, d)
    for d in range(1, NAR):
        serve_one(g, ys[d], pl.ds(d * CAP, CAP))
    pick(g, y, pl.ds(0, CAP))
    pulled[my_rows, :] = featb[0:CAP, :]

    for n, a in enumerate(shared):
        for d in range(1, NAR):
            link(a.at[y], a.at[y], nar_send.at[n, d - 1], nar_recv.at[n, d - 1], (y + d) % NAR).wait()
    for q in range(NAR):
        w2t[:, q * 128:(q + 1) * 128] = gw2t[q]
    last = jnp.concatenate([bias[0:1, 384:428], jnp.zeros((1, 84), F32)], axis=1)
    b2c[...] = jnp.concatenate([spread(bias[0:1, 256:384]), spread(last)], axis=0)

    def column(row):
        return jnp.concatenate([spread(row[:, c * 128:(c + 1) * 128]) for c in range(SEED // 128)], axis=0)

    for q in range(NAR):
        n = jnp.sum((gidx2[q, 1:1 + F2, :] >= 0).astype(F32), axis=0, keepdims=True)
        invc[q] = column(1.0 / jnp.maximum(n, 1.0))
    livec[...] = column(2.0 * LAM / HID / SEEDS_ALL * live[...].astype(F32))

    for q in range(NAR):
        r = gidx2[q] - y * FRONT
        units = unit((r >> 5) & 7)
        inside = (r >= 0) & (r < FRONT)
        for w in range(8):
            unit_of[q, w] = jnp.where(inside & ((r >> 8) == w), units, 0)
        lows[q] = jnp.concatenate([r[0:1, :], r[1:, :] & 31], axis=0)

    def backward_marks(n):
        q, c, w = n // 32, n // 8 % 4, n % 8
        lanes = pl.ds(pl.multiple_of(c * 128, 128), 128)
        acc = jnp.zeros((32, 128), jnp.int32)
        for k in range(1, 1 + F2):
            hit = sub32 == jnp.broadcast_to(lows[q, k:k + 1, lanes], (32, 128))
            acc = acc + jnp.where(hit, jnp.broadcast_to(unit_of[q, w, k:k + 1, lanes], (32, 128)), 0)
        self_row = jnp.broadcast_to(lows[q, 0:1, lanes], (16, 128)).astype(jnp.int16)
        for j in range(8):
            bsel[q, pl.ds(pl.multiple_of(w * 256 + j * 32, 32), 32), lanes] = count(acc, j)
        lanes = pl.ds(pl.multiple_of(SEED + c * 128, 128), 128)
        for t in range(16):
            here = iota16 + jnp.full((16, 128), w * 256 + t * 16, jnp.int32).astype(jnp.int16)
            rows = pl.ds(pl.multiple_of(w * 256 + t * 16, 16), 16)
            bsel[q, rows, lanes] = jnp.where(here == self_row, one, zero)

    def sum_marks(i):
        at = pl.multiple_of(i // 2 * 16, 16)
        half = i % 2
        blk = idm[pl.ds(at, 16), :]
        keys, units = spread_columns(blk, range(1, 1 + F1)), spread_columns(blk, range(17, 17 + F1))
        for w in range(4):
            acc = word(lane32 + (half * 4 + w) * 128, keys, units)
            for j in range(8):
                col = pl.ds(pl.multiple_of(half * (SRC // 2) + (w * 8 + j) * 128, 128), 128)
                ssel[pl.ds(at, 16), col] = count(acc, j)

    def sum_ids(b):
        idm[...] = jnp.concatenate(keys_units(idxv[:, cols(b)]), axis=0).T

    def cols(b):
        return pl.ds(pl.multiple_of(b * 256, 256), 256)

    def one_mark(i, c):
        sum_marks(i)
        return c

    sum_ids(0)
    lax.fori_loop(0, 32, one_mark, 0)

    come = pulled.at[pl.ds(0, (DEV - 1) * CAP)]
    pltpu.make_async_copy(come, come, row_recv).wait()
    gone = featb.at[pl.ds(CAP, (DEV - 1) * CAP)]
    pltpu.make_async_copy(gone, gone, row_send).wait()
    sent = mid.at[:, pl.ds(0, GRP - 1)]
    pltpu.make_async_copy(sent, sent, req_send.at[0]).wait()

    def widen(i, c):
        rows = pl.ds(pl.multiple_of(i * 256, 256), 256)
        table[rows, :] = pulled[rows, :].astype(F32)
        return c

    lax.fori_loop(0, SRC // 256, widen, 0)
    table[SRC:SRC + 8, :] = jnp.zeros((8, D_IN), F32)
    for c in to_smem:
        c.wait()

    def forward(b):
        @pl.when(b % 2 == 0)
        def _():
            blk = gbuf.at[left, cols(b), :]
            link(blk, blk, h_send.at[0, b], h_recv.at[0, b], right).wait_recv()
            link(blk, blk, h_send.at[2, b], h_recv.at[2, b], right).start()

        @pl.when(b % 2 == 1)
        def _():
            blk = gbuf.at[right, cols(b), :]
            link(blk, blk, h_send.at[1, b], h_recv.at[1, b], left).wait_recv()
            link(blk, blk, h_send.at[2, b], h_recv.at[2, b], left).start()

    def load_sums(b, mark):
        def some(i, c):
            backward_marks(b * 16 + i)
            mark(i)
            found = []
            for e in range(2):
                line = b * 32 + 2 * i + e
                for r in range(8):
                    self_row = view[idx[line, r * 16]]
                    rows = [view[idx[line, r * 16 + 1 + k]] for k in range(F1)]
                    while len(rows) > 1:
                        rows = [p + q for p, q in zip(rows[::2], rows[1::2])] + ([rows[-1]] if len(rows) % 2 else [])
                    found.append((r * 32 + 2 * i + e, self_row, rows[0]))
            for at, self_row, total in found:
                own[pl.ds(at, 1), :] = self_row
                near[pl.ds(at, 1), :] = total
            return c

        lax.fori_loop(0, 16, some, 0)
        finish(b)

    def multiply_sums(b):
        def some(i, c):
            backward_marks(b * 16 + i)
            found = []
            for e in range(2):
                for r in range(8):
                    found.append((r * 32 + 2 * i + e, view[idx[b * 32 + 2 * i + e, r * 16]]))
            for at, self_row in found:
                own[pl.ds(at, 1), :] = self_row
            return c

        lax.fori_loop(0, 16, some, 0)
        near[...] = dot(ssel[...], pulled[...])
        finish(b)

    def finish(b):
        rows = cols(b)
        scale = jnp.concatenate(
            [spread(invv[0:1, pl.ds(pl.multiple_of(b * 256 + c * 128, 128), 128)]) for c in range(2)], axis=0
        )
        act = jnp.concatenate([own[...].astype(BF), (near[...] * scale).astype(BF)], axis=1)
        a1 = act.T
        for h in range(2):
            a1t[pl.ds(pl.multiple_of((2 * b + h) * 256, 256), 256), :] = a1[:, h * 128:(h + 1) * 128]
        z = dot(act, gw1[...].reshape(2 * D_IN, HID)) + bias[0:1, 0:HID]
        sig = 1.0 / (1.0 + jnp.exp(-z))
        h1 = z * sig
        slope[rows, :] = sig + h1 * (1.0 - sig)
        gbuf[y, rows, :] = h1.astype(BF)
        blk = gbuf.at[y, rows, :]
        link(blk, blk, h_send.at[0, b], h_recv.at[0, b], right).start()
        link(blk, blk, h_send.at[1, b], h_recv.at[1, b], left).start()

        @pl.when(b > 0)
        def _():
            forward(b - 1)

    multiply_sums(0)

    def three(p, c):
        sum_ids(3 * p + 3)

        def loaded(h, c2):
            load_sums(3 * p + 1 + h, lambda i: sum_marks(h * 16 + i))
            return c2

        lax.fori_loop(0, 2, loaded, 0)
        multiply_sums(3 * p + 3)
        return c

    lax.fori_loop(0, 2, three, 0)
    load_sums(7, lambda i: None)
    forward(7)

    def from_source(q, fresh=False):
        def rows512(i, c):
            part = dot(fsel[q, pl.ds(pl.multiple_of(i * SEED, SEED), SEED), :], gbuf[q])
            for h in range(2):
                rows = pl.ds(pl.multiple_of(h * 2 * SEED + i * SEED, SEED), SEED)
                now = part[:, h * 128:(h + 1) * 128]
                tot[rows, :] = now if fresh else tot[rows, :] + now
            return c

        lax.fori_loop(0, 2, rows512, 0)

    from_source(y, True)
    for b in range(1, 8, 2):
        blk = gbuf.at[left, b * 256:(b + 1) * 256, :]
        link(blk, blk, h_send.at[0, b], h_recv.at[0, b], right).wait_recv()
    from_source(left)
    for b in range(0, 8, 2):
        blk = gbuf.at[right, b * 256:(b + 1) * 256, :]
        link(blk, blk, h_send.at[1, b], h_recv.at[1, b], left).wait_recv()
    from_source(right)
    for b in range(8):
        blk = gbuf.at[opp, b * 256:(b + 1) * 256, :]
        link(blk, blk, h_send.at[2, b], h_recv.at[2, b], right).wait_recv()
    from_source(opp)

    def wide(a):
        return jnp.concatenate([a, a], axis=1)

    def seeds(first):
        return jnp.concatenate([tot[h * 2 * SEED + first:h * 2 * SEED + first + SEED, :] for h in range(2)], axis=1)

    near2 = (seeds(0) * wide(invc[y])).astype(BF)
    self2 = seeds(SEED).astype(BF)
    alive = live[...].astype(F32)
    diff = self2.astype(F32) - near2.astype(F32)
    pull_apart = wide(livec[...]) * diff

    def swap_start(buf, ssem, rsem):
        blk = buf.at[y]
        link(blk, blk, ssem.at[0], rsem.at[0], right).start()
        link(blk, blk, ssem.at[1], rsem.at[1], left).start()

    def swap_forward(buf, ssem, rsem, cut):
        blk = buf.at[left]
        link(blk, blk, ssem.at[0], rsem.at[0], right).wait_recv()
        half = buf.at[left, 0:cut, :]
        link(half, half, ssem.at[2], rsem.at[2], right).start()
        blk = buf.at[right]
        link(blk, blk, ssem.at[1], rsem.at[1], left).wait_recv()
        half = buf.at[right, cut:, :]
        link(half, half, ssem.at[3], rsem.at[3], left).start()

    def swap_end(buf, ssem, rsem, cut):
        half = buf.at[opp, 0:cut, :]
        link(half, half, ssem.at[2], rsem.at[2], right).wait_recv()
        half = buf.at[opp, cut:, :]
        link(half, half, ssem.at[3], rsem.at[3], left).wait_recv()

    def swap_sent(buf, ssem, rsem, cut):
        blk = buf.at[y]
        link(blk, blk, ssem.at[0], rsem.at[0], right).wait_send()
        link(blk, blk, ssem.at[1], rsem.at[1], left).wait_send()
        half = buf.at[left, 0:cut, :]
        link(half, half, ssem.at[2], rsem.at[2], right).wait_send()
        half = buf.at[right, cut:, :]
        link(half, half, ssem.at[3], rsem.at[3], left).wait_send()

    rbuf[y] = pull_apart.astype(BF)
    swap_start(rbuf, r_send, r_recv)

    act2 = jnp.concatenate([self2, near2], axis=1)
    cls = lax.broadcasted_iota(jnp.int32, (CLS_PAD, SEED), 0)
    b2 = b2c[0:CLS_PAD, :]
    logits = dot(w2t[...], act2, NT) + jnp.concatenate([b2] * 4, axis=1)
    logits = jnp.where(cls < CLS, logits, -1e30)
    top = jnp.max(logits, axis=0, keepdims=True)
    e = jnp.exp(logits - top)
    tot = jnp.sum(e, axis=0, keepdims=True)
    hot = cls == labels[...]
    picked = jnp.sum(jnp.where(hot, logits, 0.0), axis=0, keepdims=True)
    dlog = (alive * (e * (1.0 / tot) - jnp.where(hot, 1.0, 0.0)) * (1.0 / SEEDS_ALL)).astype(BF)
    dbuf[y] = dlog
    swap_start(dbuf, d_send, d_recv)

    loss = jnp.sum(alive * (top + jnp.log(tot) - picked), axis=1, keepdims=True)
    loss = loss + SEEDS_ALL / 2 * jnp.sum(pull_apart * diff, keepdims=True)
    g2t = dot(dlog, act2).astype(BF)
    for q in range(NAR):
        pay2[q * Q2:q * Q2 + CLS_PAD, :] = g2t[:, q * 128:(q + 1) * 128]
        pay2[q * Q2 + CLS_PAD:(q + 1) * Q2, :] = jnp.zeros((Q2 - CLS_PAD, 128), BF)

    def to_owner(pay, inbox, first, count, n):
        def body(i, c):
            t = (g + i) % GRP
            p = t - first

            @pl.when((p >= 0) & (p < count))
            def _():
                pltpu.make_async_remote_copy(
                    src_ref=pay.at[pl.ds(pl.multiple_of(p * PIECE, PIECE), PIECE)], dst_ref=inbox.at[g],
                    send_sem=rs_send.at[n], recv_sem=rs_recv.at[n], device_id=(t, y), device_id_type=MESH,
                ).start()

            return c

        lax.fori_loop(1, GRP, body, 0)

    def mine(first, count):
        p = g - first
        return (p >= 0) & (p < count), pl.ds(pl.multiple_of(p * PIECE, PIECE), PIECE)

    def add_first_momentum(p):
        rows = pl.ds(pl.multiple_of(p % 2 * PIECE, PIECE), PIECE)
        for h in range(2):
            @pl.when((y == p % 8 // 2) & (p // 8 == h))
            def _(h=h):
                ybox1[y] = ybox1[y] + MU * m1[rows, h * 128:(h + 1) * 128]

    def add_second_momentum(p):
        @pl.when(y == p // (Q2 // PIECE))
        def _():
            rows = pl.ds(pl.multiple_of(p % (Q2 // PIECE) * PIECE, PIECE), PIECE)
            ybox2[y] = ybox2[y] + MU * m2pad[rows, :]

    def add_plane(pay, inbox, ybox, first, count, n, add_momentum):
        here, rows = mine(first, count)

        @pl.when(here)
        def _():
            got = inbox.at[pl.ds(0, GRP - 1)]
            pltpu.make_async_copy(got, got, rs_recv.at[n]).wait()
            inbox[g] = pay[rows, :]
            ybox[y] = jnp.sum(inbox[...].astype(F32), axis=0)
            add_momentum(g - first)
            for d in range(1, NAR):
                link(ybox.at[y], ybox.at[y], y_send.at[n, d - 1], y_recv.at[n, d - 1], ys[d]).start()

    def add_group(ybox, res, first, count, n):
        here, rows = mine(first, count)

        @pl.when(here)
        def _():
            for d in range(1, NAR):
                link(ybox.at[y], ybox.at[y], y_send.at[n, d - 1], y_recv.at[n, d - 1], ys[d]).wait()
            res[rows, :] = (ybox[0] + ybox[1]) + (ybox[2] + ybox[3])

            def tell(i, c):
                pltpu.make_async_remote_copy(
                    src_ref=res.at[rows], dst_ref=res.at[rows], send_sem=ag_send.at[n], recv_sem=ag_recv.at[n],
                    device_id=((g + i) % GRP, y), device_id_type=MESH,
                ).start()
                return c

            lax.fori_loop(1, GRP, tell, 0)

    def take(res, first, count, n):
        here, rows = mine(first, count)
        for less, when in ((1, here), (0, jnp.logical_not(here))):
            @pl.when(when)
            def _(less=less):
                got = res.at[pl.ds(0, (count - less) * PIECE)]
                pltpu.make_async_copy(got, got, ag_recv.at[n]).wait()

    def sums_sent(pay, first, count, n):
        here, rows = mine(first, count)
        for less, when in ((1, here), (0, jnp.logical_not(here))):
            @pl.when(when)
            def _(less=less):
                gone = pay.at[pl.ds(0, (count - less) * PIECE)]
                pltpu.make_async_copy(gone, gone, rs_send.at[n]).wait()

        @pl.when(here)
        def _():
            gone = table.at[pl.ds(0, (GRP - 1) * PIECE)]
            pltpu.make_async_copy(gone, gone, ag_send.at[n]).wait()

    to_owner(pay2, inbox2, GRP - P2, P2, 1)

    def add_grads(q, fresh=False):
        da = dot(dbuf[q], w2t[...], TN)
        r = rbuf[q].astype(F32)
        ds = (da[:, :HID] + r).astype(BF)
        dn = ((da[:, HID:] - r) * wide(invc[q])).astype(BF)
        both = jnp.concatenate([dn, ds], axis=0)

        def rows512(i, c):
            part = dot(bsel[q, pl.ds(pl.multiple_of(i * 512, 512), 512), :], both)
            for h in range(2):
                rows = pl.ds(pl.multiple_of(h * FRONT + i * 512, 512), 512)
                now = part[:, h * 128:(h + 1) * 128]
                dh1[rows, :] = now if fresh else dh1[rows, :] + now
            return c

        lax.fori_loop(0, FRONT // 512, rows512, 0)

    db2 = jnp.sum(dlog.astype(F32), axis=1, keepdims=True)
    db2 = jnp.broadcast_to(db2, (CLS_PAD, 128)).T[0:1, :]
    swap_forward(rbuf, r_send, r_recv, SEED // 2)
    add_grads(y, True)
    swap_forward(dbuf, d_send, d_recv, 96)
    add_grads(left)
    add_grads(right)
    add_plane(pay2, inbox2, ybox2, GRP - P2, P2, 1, add_second_momentum)
    swap_end(rbuf, r_send, r_recv, SEED // 2)
    swap_end(dbuf, d_send, d_recv, 96)
    add_group(ybox2, res2, GRP - P2, P2, 1)
    add_grads(opp)

    def to_z(b, db):
        rows = pl.ds(pl.multiple_of(b * 256, 256), 256)
        dh = jnp.concatenate(
            [dh1[pl.ds(pl.multiple_of(h * FRONT + b * 256, 256), 256), :] for h in range(2)], axis=1
        )
        dz = (dh * slope[rows, :]).astype(BF)
        a1 = jnp.concatenate(
            [a1t[pl.ds(pl.multiple_of((2 * b + h) * 256, 256), 256), :] for h in range(2)], axis=1
        )
        part = dot(a1, dz)
        for h in range(2):
            now = slice(h * 256, (h + 1) * 256)
            gsum[now, :] = gsum[now, :] + part[:, h * 128:(h + 1) * 128]
        return db + jnp.sum(dz.astype(F32), axis=0, keepdims=True)

    gsum[...] = jnp.zeros((512, 128), F32)
    db1 = lax.fori_loop(0, FRONT // 256, to_z, jnp.zeros((1, HID), F32))
    pay1[0:512, :] = gsum[...].astype(BF)
    misc[...] = jnp.zeros((PIECE, 128), F32)

    def two(rows, v):
        hi = v.astype(BF).astype(F32)
        misc[rows:rows + 1, 0:v.shape[1]] = hi
        misc[rows + 4:rows + 5, 0:v.shape[1]] = v - hi

    two(0, db1[:, :128])
    two(1, db1[:, 128:])
    two(2, db2[:, :128])
    two(3, db2[:, 128:])
    hi = loss.astype(BF).astype(F32)
    misc[8:9, 0:1] = hi
    misc[9:10, 0:1] = loss - hi
    pay1[512:544, :] = misc[...].astype(BF)
    to_owner(pay1, inbox1, 0, P1, 0)

    take(res2, GRP - P2, P2, 1)
    mom2 = jnp.concatenate([res2[q * Q2:q * Q2 + CLS_PAD, :] for q in range(NAR)], axis=1)
    for q in range(NAR):
        x2s[q] = mom2[:, q * 128:(q + 1) * 128]
    o_all[ROW_M2:ROW_M2 + CLS_PAD, :] = x2s[y]
    x2 = mom2 * (1.0 / (jnp.sqrt(jnp.sum(mom2 * mom2, keepdims=True)) + 1e-07))
    x2 = ns_step(x2)
    add_plane(pay1, inbox1, ybox1, 0, P1, 0, add_first_momentum)
    x2 = ns_step(x2)
    add_group(ybox1, o_all, 0, P1, 0)
    x2 = ns_step(x2)
    for q in range(NAR):
        o_all[ROW_X2 + q * CLS_PAD:ROW_X2 + (q + 1) * CLS_PAD, :] = x2[:, q * 128:(q + 1) * 128]
    take(o_all, 0, P1, 0)

    for b in range(8):
        blk = gbuf.at[y, b * 256:(b + 1) * 256, :]
        link(blk, blk, h_send.at[0, b], h_recv.at[0, b], right).wait_send()
        link(blk, blk, h_send.at[1, b], h_recv.at[1, b], left).wait_send()
        blk = gbuf.at[opp, b * 256:(b + 1) * 256, :]
        link(blk, blk, h_send.at[2, b], h_recv.at[2, b], right).wait_send()
    swap_sent(rbuf, r_send, r_recv, SEED // 2)
    swap_sent(dbuf, d_send, d_recv, 96)

    sums_sent(pay2, GRP - P2, P2, 1)
    sums_sent(pay1, 0, P1, 0)


def main(reqt, feat, idx1t, msk1t, idx2t, msk2t, labels, live, w1, w2own, m1, m2own, bias):
    vm = pl.BlockSpec(memory_space=pltpu.VMEM)
    dma = pltpu.SemaphoreType.DMA
    sds = jax.ShapeDtypeStruct
    V = pltpu.VMEM
    return pl.pallas_call(
        main_kernel,
        out_shape=sds((ROWS, 128), F32),
        in_specs=[vm, pl.BlockSpec(memory_space=pl.ANY)] + [vm] * 11,
        out_specs=vm,
        scratch_shapes=[
            V((SRC + 8, D_IN), F32),
            V((OWN, D_IN), BF),
            V((SRC, D_IN), BF),
            V((CAP, D_IN), F32),
            V((DEV, 128), jnp.int32),
            V((DEV, 128), jnp.int32),
            V((NAR, GRP, 1, 128), jnp.int32),
            V((16, FRONT), jnp.int32),
            V((256, 128), jnp.int32),
            V((1, FRONT), F32),
            V((256, D_IN), F32),
            V((256, D_IN), F32),
            V((FRONT, HID), F32),
            V((NAR, FRONT, HID), BF),
            V((NAR, 2 * SEED, FRONT), BF),
            V((NAR, FRONT, 2 * SEED), BF),
            V((NAR, 8, 16, SEED), jnp.int32),
            V((NAR, 16, SEED), jnp.int32),
            V((SEED, 32), jnp.int32),
            V((256, SRC), BF),
            V((256, 32), jnp.int32),
            V((NAR, SEED, 128), F32),
            V((SEED, 128), F32),
            V((NAR, SEED, HID), BF),
            V((NAR, CLS_PAD, SEED), BF),
            V((NAR, 64, HID), BF),
            V((NAR, CLS_PAD, 128), BF),
            V((Q2, 128), F32),
            V((NAR, 16, SEED), jnp.int32),
            V((CLS_PAD, 2 * HID), BF),
            V((HID, 128), F32),
            V((P1 * PIECE, 128), BF),
            V((P2 * PIECE, 128), BF),
            V((PIECE, 128), F32),
            V((GRP, PIECE, 128), BF),
            V((GRP, PIECE, 128), BF),
            V((NAR, PIECE, 128), F32),
            V((NAR, PIECE, 128), F32),
            V((P2 * PIECE, 128), F32),
            V((NAR, CLS_PAD, 128), F32),
            pltpu.SMEM((DEV, 1, 128), jnp.int32),
            pltpu.SMEM((256, 128), jnp.int32),
            dma, dma((3,)), dma((GRP,)), dma((NAR,)), dma((NAR,)), dma((GRP,)), dma, dma, dma((3, 3)), dma((3, 3)),
            dma((3, 8)), dma((3, 8)), dma((4,)), dma((4,)), dma((4,)), dma((4,)),
            dma((2,)), dma((2,)), dma((2, 3)), dma((2, 3)), dma((2,)), dma((2,)),
        ],
        compiler_params=pltpu.CompilerParams(
            collective_id=0, has_side_effects=True, vmem_limit_bytes=62 * 2**20
        ),
    )(reqt, feat, idx1t, msk1t, idx2t, msk2t, labels, live, w1, w2own, m1, m2own, bias)


def update_kernel(
    res, w1own, w2own, bias, biasm, biasv,
    o_loss, o_first, o_second, o_mom1, o_mom2, o_flow, o_slow, o_bias, o_bm, o_bv,
    x1s, x2s,
):
    y = lax.axis_index("nar")
    mom1 = jnp.concatenate([res[0:256, :], res[256:512, :]], axis=1)
    x1s[...] = mom1
    block64 = pl.ds(pl.multiple_of(y * 64, 64), 64)
    o_mom1[...] = x1s[block64, :]
    x1 = mom1 * (1.0 / (jnp.sqrt(jnp.sum(mom1 * mom1, keepdims=True)) + 1e-07))
    x2 = jnp.concatenate([res[ROW_X2 + q * CLS_PAD:ROW_X2 + (q + 1) * CLS_PAD, :] for q in range(NAR)], axis=1)
    for i in range(NS_ITERS):
        x1 = ns_step(x1)
        if i < 2:
            x2 = ns_step(x2)
    x1s[...] = x1
    for q in range(NAR):
        x2s[q] = x2[:, q * 128:(q + 1) * 128]
    first_new = w1own[...] * (1.0 - WDECAY) - x1s[block64, :]
    o_first[...] = first_new
    o_flow[...] = first_new.astype(BF)
    second = w2own[...] * (1.0 - WDECAY) - (2 * HID / CLS) ** 0.5 * x2s[y][0:CLS, :]
    o_second[...] = second
    o_slow[...] = second.astype(BF)
    o_mom2[...] = res[ROW_M2:ROW_M2 + CLS, :]

    gb = res[512:516, :] + res[516:520, :]
    gb = jnp.concatenate([gb[0:1, :], gb[1:2, :], gb[2:3, :], gb[3:4, 0:44]], axis=1)
    m_new = BETA_ONE * biasm[...] + (1.0 - BETA_ONE) * gb
    v_new = BETA_TWO * biasv[...] + (1.0 - BETA_TWO) * gb * gb
    m_hat = m_new / (1.0 - BETA_ONE**STEP)
    v_hat = v_new / (1.0 - BETA_TWO**STEP)
    o_bias[...] = bias[...] * (1.0 - LR_BIAS * WDECAY) - LR_BIAS * m_hat / (jnp.sqrt(v_hat) + EPSILON)
    o_bm[...] = m_new
    o_bv[...] = v_new
    o_loss[...] = res[520:521, 0:1] + res[521:522, 0:1]


def update(*args):
    vm = pl.BlockSpec(memory_space=pltpu.VMEM)
    sds = jax.ShapeDtypeStruct
    return pl.pallas_call(
        update_kernel,
        out_shape=[
            sds((1, 1), F32), sds((64, HID), F32), sds((CLS, 128), F32), sds((64, HID), F32), sds((CLS, 128), F32),
            sds((64, HID), BF), sds((CLS, 128), BF), sds((1, 428), F32), sds((1, 428), F32), sds((1, 428), F32),
        ],
        in_specs=[vm] * 6,
        out_specs=[vm] * 10,
        scratch_shapes=[pltpu.VMEM((2 * D_IN, HID), F32), pltpu.VMEM((NAR, CLS_PAD, 128), F32)],
        compiler_params=pltpu.CompilerParams(vmem_limit_bytes=32 * 2**20),
    )(*args)


def per_device(
    features, requests, index_one, mask_one, index_two, mask_two, labels, seed_live,
    w_first, w_second, mom_first, mom_second, biases, bias_m, bias_v,
):
    w2own, bias = w_second.T, biases[None, :]
    res = main(
        requests.T, features, index_one.T, mask_one.T, index_two.T, mask_two.T, labels[None, :], seed_live[None, :],
        w_first, w2own, mom_first, mom_second.T, bias,
    )
    loss, first_new, second_new, mom_one, mom_two, first_low, second_low, bias_new, m_new, v_new = update(
        res, w_first, w2own, bias, bias_m[None, :], bias_v[None, :]
    )
    return (
        loss.reshape(()), first_new, second_new.T, mom_one, mom_two.T, first_low, second_low.T,
        bias_new.reshape(-1), m_new.reshape(-1), v_new.reshape(-1),
    )


def solution(mesh):
    both = ("grp", "nar")
    placed = (
        P(both, None), P(both, None), P(both, None), P(both, None), P(both, None), P(both, None),
        P(both), P(both), P("nar", None), P("nar", None), P("nar", None), P("nar", None), P(), P(), P(),
    )
    nar = P("nar", None)
    return jax.shard_map(
        per_device, mesh=mesh, in_specs=placed,
        out_specs=(P(), nar, nar, nar, nar, nar, nar, P(), P(), P()), check_vma=False,
    )
```

```python
import functools

import jax
import jax.numpy as jnp
from jax import lax
from jax.experimental import pallas as pl
from jax.experimental.pallas import tpu as pltpu
from jax.sharding import PartitionSpec as P

HID = 256
CLS = 172
CLS_PAD = 176
D_IN = 128
F1 = 15
F2 = 10
NS_ITERS = 5
STEP = 10
LAM = 0.5
MU = 0.95
WDECAY = 0.01
LR_BIAS = 0.05
BETA_ONE = 0.9
BETA_TWO = 0.999
EPSILON = 1e-08
NS_A = 3.4445
NS_B = -4.775
NS_C = 2.0315
HIGH = lax.Precision.HIGHEST
MESH = pl.DeviceIdType.MESH
BF = jnp.bfloat16
F32 = jnp.float32

DEV = 128
NAR = 4
OWN = 8192
CAP = 64
SRC = 8192
FRONT = 2048
SEED = 512


def all_to(t):
    return (t // NAR, t % NAR)


GRP = 32
PIECE = 48
PIECES = 26
ROW_2 = 512
ROW_MISC = ROW_2 + NAR * CLS_PAD
ROWS = PIECES * PIECE
SEEDS_ALL = SEED * DEV


def dot(a, b, dims=((1,), (0,))):
    return lax.dot_general(a, b, (dims, ((), ())), preferred_element_type=F32)


NN = ((1,), (0,))
NT = ((1,), (1,))
TN = ((0,), (0,))


def split(a):
    hi = a.astype(BF)
    return hi, (a - hi.astype(F32)).astype(BF)


def dot3(a, b, dims):
    (ah, al), (bh, bl) = a, b
    return dot(
        jnp.concatenate([ah, ah, al], axis=dims[0][0]), jnp.concatenate([bh, bl, bh], axis=dims[1][0]), dims
    )


def ns_step(x):
    xs = split(x)
    gram = dot3(xs, xs, NT)
    gs = split(gram)
    mix = NS_B * gram + NS_C * dot3(gs, gs, NN)
    return NS_A * x + dot3(split(mix), xs, NN)


def spread(row):
    return jnp.broadcast_to(row, (128, 128)).T


def main_kernel(
    reqt, feat, idx1t, msk1t, idx2t, msk2t, labels, live, w1, w2own, m1, m2own, bias,
    o_all,
    table, featb, pulled, stage, reqv, reqin, mid, idxv, idxp, invv, near, own, slope, gbuf, fsel, bsel, unit_of, lows, selfs, idc, ssel, idm, invc, livec, rbuf, dbuf,
    gw1, gw2t, momenta, gidx2, w2t, b2c, pay, misc, inbox, ybox,
    reqs, idx,
    feat_sem, loc_sem, ask_sem, req_send, mid_recv, req_recv, row_send, row_recv, nar_send, nar_recv,
    h_send, h_recv, r_send, r_recv, d_send, d_recv, rs_send, rs_recv, y_send, y_recv, ag_send, ag_recv,
):
    a1t, dh1, tot, gsum = featb, table, table.at[2 * FRONT:3 * FRONT], table.at[3 * FRONT:3 * FRONT + 512]
    g = lax.axis_index("grp")
    y = lax.axis_index("nar")
    me = g * NAR + y
    left, right, opp = (y + 3) % NAR, (y + 1) % NAR, (y + 2) % NAR

    load = pltpu.make_async_copy(feat, featb, feat_sem)
    load.start()

    barrier = pltpu.get_barrier_semaphore()

    ys = [(y + d) % NAR for d in range(NAR)]

    def greet(i, c):
        pl.semaphore_signal(barrier, inc=1, device_id=((g + i) % GRP, y), device_id_type=MESH)
        return c

    for d in range(1, NAR):
        pl.semaphore_signal(barrier, inc=1, device_id=(g, ys[d]), device_id_type=MESH)
    lax.fori_loop(1, GRP, greet, 0)

    def link(src, dst, ssem, rsem, to):
        return pltpu.make_async_remote_copy(
            src_ref=src, dst_ref=dst, send_sem=ssem, recv_sem=rsem, device_id=(g, to), device_id_type=MESH
        )

    reqv[...] = jnp.concatenate([reqt[...], jnp.zeros((DEV - CAP, DEV), jnp.int32)], axis=0).T
    ask_rows = reqv.reshape(GRP, NAR, 1, 128)
    got_rows = reqin.reshape(DEV, 1, 128)

    gw1[y] = w1[...].astype(BF)
    pad = CLS_PAD - CLS
    gw2t[y] = jnp.concatenate([w2own[...], jnp.zeros((pad, 128), F32)], axis=0).astype(BF)
    momenta[...] = jnp.zeros((ROWS, 128), F32)
    for h in range(2):
        momenta[pl.ds(pl.multiple_of(h * 256 + y * 64, 64), 64), :] = MU * m1[:, h * 128:(h + 1) * 128]
    momenta[pl.ds(pl.multiple_of(ROW_2 + y * CLS_PAD, 16), CLS_PAD), :] = jnp.concatenate(
        [MU * m2own[...], jnp.zeros((pad, 128), F32)], axis=0
    )
    gidx2[y] = jnp.concatenate(
        [idx2t[0:1, :], jnp.where(msk2t[...] > 0, idx2t[1:, :], -1), jnp.zeros((5, SEED), jnp.int32)], axis=0
    )
    shared = (gidx2, gw1, gw2t)

    pl.semaphore_wait(barrier, GRP + NAR - 2)

    def ask_group(d):
        return pltpu.make_async_remote_copy(
            src_ref=ask_rows.at[:, ys[d]], dst_ref=mid.at[y], send_sem=req_send.at[d], recv_sem=mid_recv.at[d],
            device_id=(g, ys[d]), device_id_type=MESH,
        )

    for d in range(1, NAR):
        ask_group(d).start()
    keep = pltpu.make_async_copy(ask_rows.at[:, y], mid.at[y], loc_sem.at[2])
    keep.start()
    for n, a in enumerate(shared):
        for d in range(1, NAR):
            link(a.at[y], a.at[y], nar_send.at[n, d - 1], nar_recv.at[n, d - 1], (y + d) % NAR).start()

    msk = msk1t[...]
    idxv[0:1, :] = idx1t[0:1, :]
    idxv[1:16, :] = jnp.where(msk > 0, idx1t[1:16, :], SRC)
    invv[...] = 1.0 / jnp.maximum(jnp.sum(msk.astype(F32), axis=0, keepdims=True), 1.0)
    for half in range(2):
        parts = []
        for r in range(8):
            parts.append(jnp.concatenate(
                [idxv[:, (half * 4 + b) * 256 + r * 32:(half * 4 + b) * 256 + r * 32 + 32] for b in range(4)], axis=1
            ))
        idxp[half * 128:(half + 1) * 128, :] = jnp.concatenate(parts, axis=0).T
    to_smem = [pltpu.make_async_copy(idxp, idx, loc_sem.at[0])]
    for c in to_smem:
        c.start()

    keep.wait()
    for d in range(1, NAR):
        ask_group(d).wait()
    own_rows = pl.ds(pl.multiple_of(g * NAR, NAR), NAR)

    def ask(i, c):
        n = (i * 13) % GRP
        t = (g + n) % GRP
        pltpu.make_async_remote_copy(
            src_ref=mid.at[:, t], dst_ref=got_rows.at[own_rows], send_sem=req_send.at[0], recv_sem=req_recv.at[n],
            device_id=(t, y), device_id_type=MESH,
        ).start()
        return c

    lax.fori_loop(1, GRP, ask, 0)
    keep = pltpu.make_async_copy(mid.at[:, g], got_rows.at[own_rows], loc_sem.at[2])
    keep.start()

    load.wait()

    def widen_features(i, c):
        rows = pl.ds(pl.multiple_of(i * 256, 256), 256)
        table[rows, :] = featb[rows, :].astype(F32)
        return c

    lax.fori_loop(0, OWN // 256, widen_features, 0)

    lane32 = lax.broadcasted_iota(jnp.int32, (16, 128), 1)
    sub32 = lax.broadcasted_iota(jnp.int32, (32, 128), 0)
    lane16 = lane32.astype(jnp.int16)
    iota16 = lax.broadcasted_iota(jnp.int32, (16, 128), 0).astype(jnp.int16)
    one, zero = jnp.ones((16, 128), BF), jnp.zeros((16, 128), BF)

    def unit(digit):
        v = jnp.ones_like(digit)
        for j in range(1, 8):
            v = jnp.where(digit == j, 1 << 4 * j, v)
        return v

    def count(acc, j):
        return ((acc >> (4 * j)) & 15).astype(F32).astype(BF)

    def keys_units(ids):
        return (ids & 127) + (ids >> 10) * 128, unit((ids >> 7) & 7)

    def word(pos, keys, units):
        acc = jnp.zeros((16, 128), jnp.int32)
        for k, u in zip(keys, units):
            acc = acc + jnp.where(pos == k, u, 0)
        return acc

    def spread_columns(blk, ks):
        return [jnp.broadcast_to(blk[:, k:k + 1], (16, 128)) for k in ks]

    ids = gidx2[y]
    keys, units = keys_units(ids)
    idc[...] = jnp.concatenate([ids[0:1, :], keys[1:, :], units], axis=0).T

    def seeds16(i):
        at = pl.multiple_of(i * 16, 16)
        blk = idc[pl.ds(at, 16), :]
        self_row = jnp.broadcast_to(blk[:, 0:1], (16, 128)).astype(jnp.int16)
        return at, (spread_columns(blk, range(1, 1 + F2)), spread_columns(blk, range(17, 17 + F2)), self_row)

    def forward_marks(at, want, q):
        keys, units, self_row = want
        for w in range(2):
            acc = word(lane32 + 128 * (2 * q + w), keys, units)
            for j in range(8):
                c = w * 8 + j
                fsel[q, pl.ds(at, 16), c * 128:(c + 1) * 128] = count(acc, j)
                here = lane16 + jnp.full((16, 128), q * FRONT + c * 128, jnp.int32).astype(jnp.int16)
                fsel[q, pl.ds(SEED + at, 16), c * 128:(c + 1) * 128] = jnp.where(here == self_row, one, zero)

    view = table.reshape(SRC + 8, 1, D_IN)
    my_rows = pl.ds(pl.multiple_of(me * CAP, CAP), CAP)

    def pick(t, u, slot):
        for half in range(0, CAP, 32):
            rows = [view[reqs[t * NAR + u, 0, half + r]] for r in range(32)]
            for r in range(32):
                stage[half + r:half + r + 1, :] = rows[r]
        featb[slot, :] = stage[...].astype(BF)

    def serve_one(t, u, slot):
        pick(t, u, slot)
        pltpu.make_async_remote_copy(
            src_ref=featb.at[slot], dst_ref=pulled.at[my_rows],
            send_sem=row_send, recv_sem=row_recv, device_id=(t, u), device_id_type=MESH,
        ).start()

    def asked(n):
        rows = got_rows.at[pl.ds(0, NAR)]
        pltpu.make_async_copy(rows, rows, req_recv.at[n]).wait()

    def to_scalars(t, n):
        rows = pl.ds(pl.multiple_of(t * NAR, NAR), NAR)
        return pltpu.make_async_copy(got_rows.at[rows], reqs.at[rows], ask_sem.at[n])

    def whose(i):
        n = (i * 13) % GRP
        return n, (g + GRP - n) % GRP

    def fetch(i):
        n, t = whose(i)
        asked(n)
        to_scalars(t, n).start()

    def serve(i, c):
        n, t = whose(i)

        @pl.when(i < GRP - 1)
        def _():
            fetch(i + 1)

        to_scalars(t, n).wait()
        at, want = seeds16(i)
        for d in range(NAR):
            forward_marks(at, want, d)
            serve_one(t, ys[d], pl.ds(pl.multiple_of((i * NAR + d) * CAP, CAP), CAP))
        return c

    fetch(1)
    lax.fori_loop(1, GRP, serve, 0)
    keep.wait()
    to_scalars(g, 0).start()
    to_scalars(g, 0).wait()
    at, want = seeds16(0)
    for d in range(NAR):
        forward_marks(at, want, d)
    for d in range(1, NAR):
        serve_one(g, ys[d], pl.ds(d * CAP, CAP))
    pick(g, y, pl.ds(0, CAP))
    pulled[my_rows, :] = featb[0:CAP, :]

    for n, a in enumerate(shared):
        for d in range(1, NAR):
            link(a.at[y], a.at[y], nar_send.at[n, d - 1], nar_recv.at[n, d - 1], (y + d) % NAR).wait()
    for q in range(NAR):
        w2t[:, q * 128:(q + 1) * 128] = gw2t[q]
    last = jnp.concatenate([bias[0:1, 384:428], jnp.zeros((1, 84), F32)], axis=1)
    b2c[...] = jnp.concatenate([spread(bias[0:1, 256:384]), spread(last)], axis=0)

    def column(row):
        return jnp.concatenate([spread(row[:, c * 128:(c + 1) * 128]) for c in range(SEED // 128)], axis=0)

    for q in range(NAR):
        n = jnp.sum((gidx2[q, 1:1 + F2, :] >= 0).astype(F32), axis=0, keepdims=True)
        invc[q] = column(1.0 / jnp.maximum(n, 1.0))
    livec[...] = column(2.0 * LAM / HID / SEEDS_ALL * live[...].astype(F32))

    def backward_marks(q, carry):
        r = gidx2[q] - y * FRONT
        lows[...] = r & 31
        inside = (r >= 0) & (r < FRONT)
        units = unit((r >> 5) & 7)
        for w in range(8):
            unit_of[w] = jnp.where(inside & ((r >> 8) == w), units, 0)
        selfs[...] = jnp.broadcast_to(r[0:1, :], (16, SEED))

        def column(c, carry2):
            lanes = pl.ds(pl.multiple_of(c * 128, 128), 128)
            accs = [jnp.zeros((32, 128), jnp.int32) for _ in range(8)]
            for k in range(1, 1 + F2):
                hit = sub32 == jnp.broadcast_to(lows[k:k + 1, lanes], (32, 128))
                for w in range(8):
                    u = jnp.broadcast_to(unit_of[w, k:k + 1, lanes], (32, 128))
                    accs[w] = accs[w] + jnp.where(hit, u, 0)
            for w in range(8):
                for j in range(8):
                    first = (w * 8 + j) * 32
                    bsel[q, first:first + 32, lanes] = count(accs[w], j)
            self_row = selfs[:, lanes].astype(jnp.int16)
            lanes = pl.ds(pl.multiple_of(SEED + c * 128, 128), 128)
            for t in range(FRONT // 16):
                here = iota16 + jnp.full((16, 128), t * 16, jnp.int32).astype(jnp.int16)
                bsel[q, t * 16:(t + 1) * 16, lanes] = jnp.where(here == self_row, one, zero)
            return carry2

        lax.fori_loop(0, SEED // 128, column, 0)
        return carry

    def sum_marks(i):
        at = pl.multiple_of(i // 2 * 16, 16)
        half = i % 2
        blk = idm[pl.ds(at, 16), :]
        keys, units = spread_columns(blk, range(1, 1 + F1)), spread_columns(blk, range(17, 17 + F1))
        for w in range(4):
            acc = word(lane32 + (half * 4 + w) * 128, keys, units)
            for j in range(8):
                col = pl.ds(pl.multiple_of(half * (SRC // 2) + (w * 8 + j) * 128, 128), 128)
                ssel[pl.ds(at, 16), col] = count(acc, j)

    def sum_ids(b):
        idm[...] = jnp.concatenate(keys_units(idxv[:, cols(b)]), axis=0).T

    def cols(b):
        return pl.ds(pl.multiple_of(b * 256, 256), 256)

    def one_mark(i, c):
        sum_marks(i)
        return c

    sum_ids(0)
    lax.fori_loop(0, 32, one_mark, 0)
    lax.fori_loop(0, NAR, backward_marks, 0)

    come = pulled.at[pl.ds(0, (DEV - 1) * CAP)]
    pltpu.make_async_copy(come, come, row_recv).wait()
    gone = featb.at[pl.ds(CAP, (DEV - 1) * CAP)]
    pltpu.make_async_copy(gone, gone, row_send).wait()
    sent = mid.at[:, pl.ds(0, GRP - 1)]
    pltpu.make_async_copy(sent, sent, req_send.at[0]).wait()

    def widen(i, c):
        rows = pl.ds(pl.multiple_of(i * 256, 256), 256)
        table[rows, :] = pulled[rows, :].astype(F32)
        return c

    lax.fori_loop(0, SRC // 256, widen, 0)
    table[SRC:SRC + 8, :] = jnp.zeros((8, D_IN), F32)
    for c in to_smem:
        c.wait()

    def forward(b):
        @pl.when(b % 2 == 0)
        def _():
            blk = gbuf.at[left, cols(b), :]
            link(blk, blk, h_send.at[0, b], h_recv.at[0, b], right).wait_recv()
            link(blk, blk, h_send.at[2, b], h_recv.at[2, b], right).start()

        @pl.when(b % 2 == 1)
        def _():
            blk = gbuf.at[right, cols(b), :]
            link(blk, blk, h_send.at[1, b], h_recv.at[1, b], left).wait_recv()
            link(blk, blk, h_send.at[2, b], h_recv.at[2, b], left).start()

    def load_sums(b):
        def some(i, c):
            found = []
            for e in range(2):
                line = b * 32 + 2 * i + e
                for r in range(8):
                    self_row = view[idx[line, r * 16]]
                    rows = [view[idx[line, r * 16 + 1 + k]] for k in range(F1)]
                    while len(rows) > 1:
                        rows = [p + q for p, q in zip(rows[::2], rows[1::2])] + ([rows[-1]] if len(rows) % 2 else [])
                    found.append((r * 32 + 2 * i + e, self_row, rows[0]))
            for at, self_row, total in found:
                own[pl.ds(at, 1), :] = self_row
                near[pl.ds(at, 1), :] = total
            return c

        lax.fori_loop(0, 16, some, 0)
        finish(b)

    def multiply_sums(b):
        def some(i, c):
            found = []
            for e in range(2):
                for r in range(8):
                    found.append((r * 32 + 2 * i + e, view[idx[b * 32 + 2 * i + e, r * 16]]))
            for at, self_row in found:
                own[pl.ds(at, 1), :] = self_row
            return c

        lax.fori_loop(0, 16, some, 0)
        near[...] = dot(ssel[...], pulled[...])
        finish(b)

    def finish(b):
        rows = cols(b)
        scale = jnp.concatenate(
            [spread(invv[0:1, pl.ds(pl.multiple_of(b * 256 + c * 128, 128), 128)]) for c in range(2)], axis=0
        )
        act = jnp.concatenate([own[...].astype(BF), (near[...] * scale).astype(BF)], axis=1)
        a1 = act.T
        for h in range(2):
            a1t[pl.ds(pl.multiple_of((2 * b + h) * 256, 256), 256), :] = a1[:, h * 128:(h + 1) * 128]
        z = dot(act, gw1[...].reshape(2 * D_IN, HID)) + bias[0:1, 0:HID]
        sig = 1.0 / (1.0 + jnp.exp(-z))
        h1 = z * sig
        slope[rows, :] = sig + h1 * (1.0 - sig)
        gbuf[y, rows, :] = h1.astype(BF)
        blk = gbuf.at[y, rows, :]
        link(blk, blk, h_send.at[0, b], h_recv.at[0, b], right).start()
        link(blk, blk, h_send.at[1, b], h_recv.at[1, b], left).start()

        @pl.when(b > 0)
        def _():
            forward(b - 1)

    def loaded(b, c):
        load_sums(b)
        return c

    multiply_sums(0)
    lax.fori_loop(1, 8, loaded, 0)
    forward(7)

    def from_source(q, fresh=False):
        def rows512(i, c):
            part = dot(fsel[q, pl.ds(pl.multiple_of(i * SEED, SEED), SEED), :], gbuf[q])
            for h in range(2):
                rows = pl.ds(pl.multiple_of(h * 2 * SEED + i * SEED, SEED), SEED)
                now = part[:, h * 128:(h + 1) * 128]
                tot[rows, :] = now if fresh else tot[rows, :] + now
            return c

        lax.fori_loop(0, 2, rows512, 0)

    from_source(y, True)
    for b in range(1, 8, 2):
        blk = gbuf.at[left, b * 256:(b + 1) * 256, :]
        link(blk, blk, h_send.at[0, b], h_recv.at[0, b], right).wait_recv()
    from_source(left)
    for b in range(0, 8, 2):
        blk = gbuf.at[right, b * 256:(b + 1) * 256, :]
        link(blk, blk, h_send.at[1, b], h_recv.at[1, b], left).wait_recv()
    from_source(right)
    for b in range(8):
        blk = gbuf.at[opp, b * 256:(b + 1) * 256, :]
        link(blk, blk, h_send.at[2, b], h_recv.at[2, b], right).wait_recv()
    from_source(opp)

    def wide(a):
        return jnp.concatenate([a, a], axis=1)

    def seeds(first):
        return jnp.concatenate([tot[h * 2 * SEED + first:h * 2 * SEED + first + SEED, :] for h in range(2)], axis=1)

    near2 = (seeds(0) * wide(invc[y])).astype(BF)
    self2 = seeds(SEED).astype(BF)
    alive = live[...].astype(F32)
    diff = self2.astype(F32) - near2.astype(F32)
    pull_apart = wide(livec[...]) * diff

    def swap_start(buf, ssem, rsem):
        blk = buf.at[y]
        link(blk, blk, ssem.at[0], rsem.at[0], right).start()
        link(blk, blk, ssem.at[1], rsem.at[1], left).start()

    def swap_forward(buf, ssem, rsem, cut):
        blk = buf.at[left]
        link(blk, blk, ssem.at[0], rsem.at[0], right).wait_recv()
        half = buf.at[left, 0:cut, :]
        link(half, half, ssem.at[2], rsem.at[2], right).start()
        blk = buf.at[right]
        link(blk, blk, ssem.at[1], rsem.at[1], left).wait_recv()
        half = buf.at[right, cut:, :]
        link(half, half, ssem.at[3], rsem.at[3], left).start()

    def swap_end(buf, ssem, rsem, cut):
        half = buf.at[opp, 0:cut, :]
        link(half, half, ssem.at[2], rsem.at[2], right).wait_recv()
        half = buf.at[opp, cut:, :]
        link(half, half, ssem.at[3], rsem.at[3], left).wait_recv()

    def swap_sent(buf, ssem, rsem, cut):
        blk = buf.at[y]
        link(blk, blk, ssem.at[0], rsem.at[0], right).wait_send()
        link(blk, blk, ssem.at[1], rsem.at[1], left).wait_send()
        half = buf.at[left, 0:cut, :]
        link(half, half, ssem.at[2], rsem.at[2], right).wait_send()
        half = buf.at[right, cut:, :]
        link(half, half, ssem.at[3], rsem.at[3], left).wait_send()

    rbuf[y] = pull_apart.astype(BF)
    swap_start(rbuf, r_send, r_recv)

    act2 = jnp.concatenate([self2, near2], axis=1)
    cls = lax.broadcasted_iota(jnp.int32, (CLS_PAD, SEED), 0)
    b2 = b2c[0:CLS_PAD, :]
    logits = dot(w2t[...], act2, NT) + jnp.concatenate([b2] * 4, axis=1)
    logits = jnp.where(cls < CLS, logits, -1e30)
    top = jnp.max(logits, axis=0, keepdims=True)
    e = jnp.exp(logits - top)
    tot = jnp.sum(e, axis=0, keepdims=True)
    hot = cls == labels[...]
    picked = jnp.sum(jnp.where(hot, logits, 0.0), axis=0, keepdims=True)
    dlog = (alive * (e * (1.0 / tot) - jnp.where(hot, 1.0, 0.0)) * (1.0 / SEEDS_ALL)).astype(BF)
    dbuf[y] = dlog
    swap_start(dbuf, d_send, d_recv)

    loss = jnp.sum(alive * (top + jnp.log(tot) - picked), axis=1, keepdims=True)
    loss = loss + SEEDS_ALL / 2 * jnp.sum(pull_apart * diff, keepdims=True)
    g2t = dot(dlog, act2).astype(BF)
    for q in range(NAR):
        pay[ROW_2 + q * CLS_PAD:ROW_2 + (q + 1) * CLS_PAD, :] = g2t[:, q * 128:(q + 1) * 128]

    def add_grads(q, fresh=False):
        da = dot(dbuf[q], w2t[...], TN)
        r = rbuf[q].astype(F32)
        ds = (da[:, :HID] + r).astype(BF)
        dn = ((da[:, HID:] - r) * wide(invc[q])).astype(BF)
        both = jnp.concatenate([dn, ds], axis=0)

        def rows512(i, c):
            part = dot(bsel[q, pl.ds(pl.multiple_of(i * 512, 512), 512), :], both)
            for h in range(2):
                rows = pl.ds(pl.multiple_of(h * FRONT + i * 512, 512), 512)
                now = part[:, h * 128:(h + 1) * 128]
                dh1[rows, :] = now if fresh else dh1[rows, :] + now
            return c

        lax.fori_loop(0, FRONT // 512, rows512, 0)

    db2 = jnp.sum(dlog.astype(F32), axis=1, keepdims=True)
    db2 = jnp.broadcast_to(db2, (CLS_PAD, 128)).T[0:1, :]
    swap_forward(rbuf, r_send, r_recv, SEED // 2)
    add_grads(y, True)
    swap_forward(dbuf, d_send, d_recv, 96)
    add_grads(left)
    add_grads(right)
    swap_end(rbuf, r_send, r_recv, SEED // 2)
    swap_end(dbuf, d_send, d_recv, 96)
    add_grads(opp)

    def to_z(b, db):
        rows = pl.ds(pl.multiple_of(b * 256, 256), 256)
        dh = jnp.concatenate(
            [dh1[pl.ds(pl.multiple_of(h * FRONT + b * 256, 256), 256), :] for h in range(2)], axis=1
        )
        dz = (dh * slope[rows, :]).astype(BF)
        a1 = jnp.concatenate(
            [a1t[pl.ds(pl.multiple_of((2 * b + h) * 256, 256), 256), :] for h in range(2)], axis=1
        )
        part = dot(a1, dz)
        for h in range(2):
            now = slice(h * 256, (h + 1) * 256)
            gsum[now, :] = gsum[now, :] + part[:, h * 128:(h + 1) * 128]
        return db + jnp.sum(dz.astype(F32), axis=0, keepdims=True)

    gsum[...] = jnp.zeros((512, 128), F32)
    db1 = lax.fori_loop(0, FRONT // 256, to_z, jnp.zeros((1, HID), F32))
    pay[0:512, :] = gsum[...].astype(BF)
    misc[...] = jnp.zeros((32, 128), F32)

    def two(rows, v):
        hi = v.astype(BF).astype(F32)
        misc[rows:rows + 1, 0:v.shape[1]] = hi
        misc[rows + 4:rows + 5, 0:v.shape[1]] = v - hi

    two(0, db1[:, :128])
    two(1, db1[:, 128:])
    two(2, db2[:, :128])
    two(3, db2[:, 128:])
    hi = loss.astype(BF).astype(F32)
    misc[8:9, 0:1] = hi
    misc[9:10, 0:1] = loss - hi
    pay[ROW_MISC:ROWS, :] = misc[...].astype(BF)

    def to_owner(i, c):
        t = (g + i) % GRP

        @pl.when(t < PIECES)
        def _():
            pltpu.make_async_remote_copy(
                src_ref=pay.at[pl.ds(pl.multiple_of(t * PIECE, 16), PIECE)], dst_ref=inbox.at[g],
                send_sem=rs_send, recv_sem=rs_recv, device_id=(t, y), device_id_type=MESH,
            ).start()

        return c

    lax.fori_loop(1, GRP, to_owner, 0)
    mine = pl.ds(pl.multiple_of(g * PIECE, 16), PIECE)

    @pl.when(g < PIECES)
    def _():
        got = inbox.at[pl.ds(0, GRP - 1)]
        pltpu.make_async_copy(got, got, rs_recv).wait()
        inbox[g] = pay[mine, :]
        ybox[y] = jnp.sum(inbox[...].astype(F32), axis=0) + momenta[mine, :]
        for d in range(1, NAR):
            link(ybox.at[y], ybox.at[y], y_send.at[d - 1], y_recv.at[d - 1], ys[d]).start()
        for d in range(1, NAR):
            link(ybox.at[y], ybox.at[y], y_send.at[d - 1], y_recv.at[d - 1], ys[d]).wait()
        o_all[mine, :] = (ybox[0] + ybox[1]) + (ybox[2] + ybox[3])

        def tell(i, c):
            pltpu.make_async_remote_copy(
                src_ref=o_all.at[mine], dst_ref=o_all.at[mine], send_sem=ag_send, recv_sem=ag_recv,
                device_id=((g + i) % GRP, y), device_id_type=MESH,
            ).start()
            return c

        lax.fori_loop(1, GRP, tell, 0)
        got = o_all.at[pl.ds(0, (PIECES - 1) * PIECE)]
        pltpu.make_async_copy(got, got, ag_recv).wait()
        gone = pay.at[pl.ds(0, (PIECES - 1) * PIECE)]
        pltpu.make_async_copy(gone, gone, rs_send).wait()
        gone = table.at[pl.ds(0, (GRP - 1) * PIECE)]
        pltpu.make_async_copy(gone, gone, ag_send).wait()

    @pl.when(g >= PIECES)
    def _():
        pltpu.make_async_copy(o_all, o_all, ag_recv).wait()
        pltpu.make_async_copy(pay, pay, rs_send).wait()

    for b in range(8):
        blk = gbuf.at[y, b * 256:(b + 1) * 256, :]
        link(blk, blk, h_send.at[0, b], h_recv.at[0, b], right).wait_send()
        link(blk, blk, h_send.at[1, b], h_recv.at[1, b], left).wait_send()
        blk = gbuf.at[opp, b * 256:(b + 1) * 256, :]
        link(blk, blk, h_send.at[2, b], h_recv.at[2, b], right).wait_send()
    swap_sent(rbuf, r_send, r_recv, SEED // 2)
    swap_sent(dbuf, d_send, d_recv, 96)


def main(reqt, feat, idx1t, msk1t, idx2t, msk2t, labels, live, w1, w2own, m1, m2own, bias):
    vm = pl.BlockSpec(memory_space=pltpu.VMEM)
    dma = pltpu.SemaphoreType.DMA
    sds = jax.ShapeDtypeStruct
    V = pltpu.VMEM
    return pl.pallas_call(
        main_kernel,
        out_shape=sds((ROWS, 128), F32),
        in_specs=[vm, pl.BlockSpec(memory_space=pl.ANY)] + [vm] * 11,
        out_specs=vm,
        scratch_shapes=[
            V((SRC + 8, D_IN), F32),
            V((OWN, D_IN), BF),
            V((SRC, D_IN), BF),
            V((CAP, D_IN), F32),
            V((DEV, 128), jnp.int32),
            V((DEV, 128), jnp.int32),
            V((NAR, GRP, 1, 128), jnp.int32),
            V((16, FRONT), jnp.int32),
            V((256, 128), jnp.int32),
            V((1, FRONT), F32),
            V((256, D_IN), F32),
            V((256, D_IN), F32),
            V((FRONT, HID), F32),
            V((NAR, FRONT, HID), BF),
            V((NAR, 2 * SEED, FRONT), BF),
            V((NAR, FRONT, 2 * SEED), BF),
            V((8, 16, SEED), jnp.int32),
            V((16, SEED), jnp.int32),
            V((16, SEED), jnp.int32),
            V((SEED, 32), jnp.int32),
            V((256, SRC), BF),
            V((256, 32), jnp.int32),
            V((NAR, SEED, 128), F32),
            V((SEED, 128), F32),
            V((NAR, SEED, HID), BF),
            V((NAR, CLS_PAD, SEED), BF),
            V((NAR, 64, HID), BF),
            V((NAR, CLS_PAD, 128), BF),
            V((ROWS, 128), F32),
            V((NAR, 16, SEED), jnp.int32),
            V((CLS_PAD, 2 * HID), BF),
            V((HID, 128), F32),
            V((ROWS, 128), BF),
            V((32, 128), F32),
            V((GRP, PIECE, 128), BF),
            V((NAR, PIECE, 128), F32),
            pltpu.SMEM((DEV, 1, 128), jnp.int32),
            pltpu.SMEM((256, 128), jnp.int32),
            dma, dma((3,)), dma((GRP,)), dma((NAR,)), dma((NAR,)), dma((GRP,)), dma, dma, dma((3, 3)), dma((3, 3)),
            dma((3, 8)), dma((3, 8)), dma((4,)), dma((4,)), dma((4,)), dma((4,)),
            dma, dma, dma((3,)), dma((3,)), dma, dma,
        ],
        compiler_params=pltpu.CompilerParams(
            collective_id=0, has_side_effects=True, vmem_limit_bytes=62 * 2**20
        ),
    )(reqt, feat, idx1t, msk1t, idx2t, msk2t, labels, live, w1, w2own, m1, m2own, bias)


def update_kernel(
    res, w1own, w2own, bias, biasm, biasv,
    o_loss, o_first, o_second, o_mom1, o_mom2, o_flow, o_slow, o_bias, o_bm, o_bv,
    x1s, x2s,
):
    y = lax.axis_index("nar")
    mom1 = jnp.concatenate([res[0:256, :], res[256:512, :]], axis=1)
    x1s[...] = mom1
    block64 = pl.ds(pl.multiple_of(y * 64, 64), 64)
    o_mom1[...] = x1s[block64, :]
    x1 = mom1 * (1.0 / (jnp.sqrt(jnp.sum(mom1 * mom1, keepdims=True)) + 1e-07))
    mom2 = jnp.concatenate([res[ROW_2 + q * CLS_PAD:ROW_2 + (q + 1) * CLS_PAD, :] for q in range(NAR)], axis=1)
    x2 = mom2 * (1.0 / (jnp.sqrt(jnp.sum(mom2 * mom2, keepdims=True)) + 1e-07))
    for i in range(NS_ITERS):
        x1 = ns_step(x1)
        x2 = ns_step(x2)
    x1s[...] = x1
    for q in range(NAR):
        x2s[q] = x2[:, q * 128:(q + 1) * 128]
    first_new = w1own[...] * (1.0 - WDECAY) - x1s[block64, :]
    o_first[...] = first_new
    o_flow[...] = first_new.astype(BF)
    second = w2own[...] * (1.0 - WDECAY) - (2 * HID / CLS) ** 0.5 * x2s[y][0:CLS, :]
    o_second[...] = second
    o_slow[...] = second.astype(BF)
    o_mom2[...] = res[pl.ds(pl.multiple_of(ROW_2 + y * CLS_PAD, 16), CLS_PAD), :][0:CLS, :]

    gb = res[ROW_MISC + 0:ROW_MISC + 4, :] + res[ROW_MISC + 4:ROW_MISC + 8, :]
    gb = jnp.concatenate([gb[0:1, :], gb[1:2, :], gb[2:3, :], gb[3:4, 0:44]], axis=1)
    m_new = BETA_ONE * biasm[...] + (1.0 - BETA_ONE) * gb
    v_new = BETA_TWO * biasv[...] + (1.0 - BETA_TWO) * gb * gb
    m_hat = m_new / (1.0 - BETA_ONE**STEP)
    v_hat = v_new / (1.0 - BETA_TWO**STEP)
    o_bias[...] = bias[...] * (1.0 - LR_BIAS * WDECAY) - LR_BIAS * m_hat / (jnp.sqrt(v_hat) + EPSILON)
    o_bm[...] = m_new
    o_bv[...] = v_new
    o_loss[...] = res[ROW_MISC + 8:ROW_MISC + 9, 0:1] + res[ROW_MISC + 9:ROW_MISC + 10, 0:1]


def update(*args):
    vm = pl.BlockSpec(memory_space=pltpu.VMEM)
    sds = jax.ShapeDtypeStruct
    return pl.pallas_call(
        update_kernel,
        out_shape=[
            sds((1, 1), F32), sds((64, HID), F32), sds((CLS, 128), F32), sds((64, HID), F32), sds((CLS, 128), F32),
            sds((64, HID), BF), sds((CLS, 128), BF), sds((1, 428), F32), sds((1, 428), F32), sds((1, 428), F32),
        ],
        in_specs=[vm] * 6,
        out_specs=[vm] * 10,
        scratch_shapes=[pltpu.VMEM((2 * D_IN, HID), F32), pltpu.VMEM((NAR, CLS_PAD, 128), F32)],
        compiler_params=pltpu.CompilerParams(vmem_limit_bytes=32 * 2**20),
    )(*args)


def per_device(
    features, requests, index_one, mask_one, index_two, mask_two, labels, seed_live,
    w_first, w_second, mom_first, mom_second, biases, bias_m, bias_v,
):
    w2own, bias = w_second.T, biases[None, :]
    res = main(
        requests.T, features, index_one.T, mask_one.T, index_two.T, mask_two.T, labels[None, :], seed_live[None, :],
        w_first, w2own, mom_first, mom_second.T, bias,
    )
    loss, first_new, second_new, mom_one, mom_two, first_low, second_low, bias_new, m_new, v_new = update(
        res, w_first, w2own, bias, bias_m[None, :], bias_v[None, :]
    )
    return (
        loss.reshape(()), first_new, second_new.T, mom_one, mom_two.T, first_low, second_low.T,
        bias_new.reshape(-1), m_new.reshape(-1), v_new.reshape(-1),
    )


def solution(mesh):
    both = ("grp", "nar")
    placed = (
        P(both, None), P(both, None), P(both, None), P(both, None), P(both, None), P(both, None),
        P(both), P(both), P("nar", None), P("nar", None), P("nar", None), P("nar", None), P(), P(), P(),
    )
    nar = P("nar", None)
    return jax.shard_map(
        per_device, mesh=mesh, in_specs=placed,
        out_specs=(P(), nar, nar, nar, nar, nar, nar, P(), P(), P()), check_vma=False,
    )
```

```python
import functools

import jax
import jax.numpy as jnp
from jax import lax
from jax.experimental import pallas as pl
from jax.experimental.pallas import tpu as pltpu
from jax.sharding import PartitionSpec as P

HID = 256
CLS = 172
CLS_PAD = 176
D_IN = 128
F1 = 15
F2 = 10
NS_ITERS = 5
STEP = 10
LAM = 0.5
MU = 0.95
WDECAY = 0.01
LR_BIAS = 0.05
BETA_ONE = 0.9
BETA_TWO = 0.999
EPSILON = 1e-08
NS_A = 3.4445
NS_B = -4.775
NS_C = 2.0315
HIGH = lax.Precision.HIGHEST
MESH = pl.DeviceIdType.MESH
BF = jnp.bfloat16
F32 = jnp.float32

DEV = 128
NAR = 4
OWN = 8192
CAP = 64
SRC = 8192
FRONT = 2048
SEED = 512


def all_to(t):
    return (t // NAR, t % NAR)


GRP = 32
PIECE = 48
PIECES = 26
ROW_2 = 512
ROW_MISC = ROW_2 + NAR * CLS_PAD
ROWS = PIECES * PIECE
SEEDS_ALL = SEED * DEV


def dot(a, b, dims=((1,), (0,))):
    return lax.dot_general(a, b, (dims, ((), ())), preferred_element_type=F32)


NN = ((1,), (0,))
NT = ((1,), (1,))
TN = ((0,), (0,))


def split(a):
    hi = a.astype(BF)
    return hi, (a - hi.astype(F32)).astype(BF)


def dot3(a, b, dims):
    (ah, al), (bh, bl) = a, b
    return dot(
        jnp.concatenate([ah, ah, al], axis=dims[0][0]), jnp.concatenate([bh, bl, bh], axis=dims[1][0]), dims
    )


def ns_step(x):
    xs = split(x)
    gram = dot3(xs, xs, NT)
    gs = split(gram)
    mix = NS_B * gram + NS_C * dot3(gs, gs, NN)
    return NS_A * x + dot3(split(mix), xs, NN)


def spread(row):
    return jnp.broadcast_to(row, (128, 128)).T


def main_kernel(
    reqt, feat, idx1t, msk1t, idx2t, msk2t, labels, live, w1, w2own, m1, m2own, bias,
    o_all,
    table, featb, pulled, stage, reqv, reqin, mid, idxv, idxp, invv, near, own, slope, gbuf, fsel, bsel, wants, idc, ssel, idm, invc, livec, rbuf, dbuf,
    gw1, gw2t, momenta, gidx2, w2t, b2c, pay, misc, inbox, ybox,
    reqs, idx,
    feat_sem, loc_sem, ask_sem, req_send, mid_recv, req_recv, row_send, row_recv, nar_send, nar_recv,
    h_send, h_recv, r_send, r_recv, d_send, d_recv, rs_send, rs_recv, y_send, y_recv, ag_send, ag_recv,
):
    a1t, dh1, tot, gsum = featb, table, table.at[2 * FRONT:3 * FRONT], table.at[3 * FRONT:3 * FRONT + 512]
    g = lax.axis_index("grp")
    y = lax.axis_index("nar")
    me = g * NAR + y
    left, right, opp = (y + 3) % NAR, (y + 1) % NAR, (y + 2) % NAR

    load = pltpu.make_async_copy(feat, featb, feat_sem)
    load.start()

    barrier = pltpu.get_barrier_semaphore()

    ys = [(y + d) % NAR for d in range(NAR)]

    def greet(i, c):
        pl.semaphore_signal(barrier, inc=1, device_id=((g + i) % GRP, y), device_id_type=MESH)
        return c

    for d in range(1, NAR):
        pl.semaphore_signal(barrier, inc=1, device_id=(g, ys[d]), device_id_type=MESH)
    lax.fori_loop(1, GRP, greet, 0)

    def link(src, dst, ssem, rsem, to):
        return pltpu.make_async_remote_copy(
            src_ref=src, dst_ref=dst, send_sem=ssem, recv_sem=rsem, device_id=(g, to), device_id_type=MESH
        )

    reqv[...] = jnp.concatenate([reqt[...], jnp.zeros((DEV - CAP, DEV), jnp.int32)], axis=0).T
    ask_rows = reqv.reshape(GRP, NAR, 1, 128)
    got_rows = reqin.reshape(DEV, 1, 128)

    gw1[y] = w1[...].astype(BF)
    pad = CLS_PAD - CLS
    gw2t[y] = jnp.concatenate([w2own[...], jnp.zeros((pad, 128), F32)], axis=0).astype(BF)
    momenta[...] = jnp.zeros((ROWS, 128), F32)
    for h in range(2):
        momenta[pl.ds(pl.multiple_of(h * 256 + y * 64, 64), 64), :] = MU * m1[:, h * 128:(h + 1) * 128]
    momenta[pl.ds(pl.multiple_of(ROW_2 + y * CLS_PAD, 16), CLS_PAD), :] = jnp.concatenate(
        [MU * m2own[...], jnp.zeros((pad, 128), F32)], axis=0
    )
    gidx2[y] = jnp.concatenate(
        [idx2t[0:1, :], jnp.where(msk2t[...] > 0, idx2t[1:, :], -1), jnp.zeros((5, SEED), jnp.int32)], axis=0
    )
    shared = (gidx2, gw1, gw2t)

    pl.semaphore_wait(barrier, GRP + NAR - 2)

    def ask_group(d):
        return pltpu.make_async_remote_copy(
            src_ref=ask_rows.at[:, ys[d]], dst_ref=mid.at[y], send_sem=req_send.at[d], recv_sem=mid_recv.at[d],
            device_id=(g, ys[d]), device_id_type=MESH,
        )

    for d in range(1, NAR):
        ask_group(d).start()
    keep = pltpu.make_async_copy(ask_rows.at[:, y], mid.at[y], loc_sem.at[2])
    keep.start()
    for n, a in enumerate(shared):
        for d in range(1, NAR):
            link(a.at[y], a.at[y], nar_send.at[n, d - 1], nar_recv.at[n, d - 1], (y + d) % NAR).start()

    msk = msk1t[...]
    idxv[0:1, :] = idx1t[0:1, :]
    idxv[1:16, :] = jnp.where(msk > 0, idx1t[1:16, :], SRC)
    invv[...] = 1.0 / jnp.maximum(jnp.sum(msk.astype(F32), axis=0, keepdims=True), 1.0)
    for half in range(2):
        parts = []
        for r in range(8):
            parts.append(jnp.concatenate(
                [idxv[:, (half * 4 + b) * 256 + r * 32:(half * 4 + b) * 256 + r * 32 + 32] for b in range(4)], axis=1
            ))
        idxp[half * 128:(half + 1) * 128, :] = jnp.concatenate(parts, axis=0).T
    to_smem = [pltpu.make_async_copy(idxp, idx, loc_sem.at[0])]
    for c in to_smem:
        c.start()

    keep.wait()
    for d in range(1, NAR):
        ask_group(d).wait()
    own_rows = pl.ds(pl.multiple_of(g * NAR, NAR), NAR)

    def ask(i, c):
        n = (i * 13) % GRP
        t = (g + n) % GRP
        pltpu.make_async_remote_copy(
            src_ref=mid.at[:, t], dst_ref=got_rows.at[own_rows], send_sem=req_send.at[0], recv_sem=req_recv.at[n],
            device_id=(t, y), device_id_type=MESH,
        ).start()
        return c

    lax.fori_loop(1, GRP, ask, 0)
    keep = pltpu.make_async_copy(mid.at[:, g], got_rows.at[own_rows], loc_sem.at[2])
    keep.start()

    load.wait()

    def widen_features(i, c):
        rows = pl.ds(pl.multiple_of(i * 256, 256), 256)
        table[rows, :] = featb[rows, :].astype(F32)
        return c

    lax.fori_loop(0, OWN // 256, widen_features, 0)

    lane32 = lax.broadcasted_iota(jnp.int32, (16, 128), 1)
    lane16 = lane32.astype(jnp.int16)
    iota16 = lax.broadcasted_iota(jnp.int32, (16, 128), 0).astype(jnp.int16)
    one, zero = jnp.ones((16, 128), BF), jnp.zeros((16, 128), BF)

    def unit(digit):
        v = jnp.ones_like(digit)
        for j in range(1, 8):
            v = jnp.where(digit == j, 1 << 4 * j, v)
        return v

    def count(acc, j):
        return ((acc >> (4 * j)) & 15).astype(F32).astype(BF)

    def keys_units(ids):
        return (ids & 127) + (ids >> 10) * 128, unit((ids >> 7) & 7)

    def word(pos, keys, units):
        acc = jnp.zeros((16, 128), jnp.int32)
        for k, u in zip(keys, units):
            acc = acc + jnp.where(pos == k, u, 0)
        return acc

    def spread_columns(blk, ks):
        return [jnp.broadcast_to(blk[:, k:k + 1], (16, 128)) for k in ks]

    ids = gidx2[y]
    keys, units = keys_units(ids)
    idc[...] = jnp.concatenate([ids[0:1, :], keys[1:, :], units], axis=0).T

    def seeds16(i):
        at = pl.multiple_of(i * 16, 16)
        blk = idc[pl.ds(at, 16), :]
        self_row = jnp.broadcast_to(blk[:, 0:1], (16, 128)).astype(jnp.int16)
        return at, (spread_columns(blk, range(1, 1 + F2)), spread_columns(blk, range(17, 17 + F2)), self_row)

    def forward_marks(at, want, q):
        keys, units, self_row = want
        for w in range(2):
            acc = word(lane32 + 128 * (2 * q + w), keys, units)
            for j in range(8):
                c = w * 8 + j
                fsel[q, pl.ds(at, 16), c * 128:(c + 1) * 128] = count(acc, j)
                here = lane16 + jnp.full((16, 128), q * FRONT + c * 128, jnp.int32).astype(jnp.int16)
                fsel[q, pl.ds(SEED + at, 16), c * 128:(c + 1) * 128] = jnp.where(here == self_row, one, zero)

    view = table.reshape(SRC + 8, 1, D_IN)
    my_rows = pl.ds(pl.multiple_of(me * CAP, CAP), CAP)

    def pick(t, u, slot):
        for half in range(0, CAP, 32):
            rows = [view[reqs[t * NAR + u, 0, half + r]] for r in range(32)]
            for r in range(32):
                stage[half + r:half + r + 1, :] = rows[r]
        featb[slot, :] = stage[...].astype(BF)

    def serve_one(t, u, slot):
        pick(t, u, slot)
        pltpu.make_async_remote_copy(
            src_ref=featb.at[slot], dst_ref=pulled.at[my_rows],
            send_sem=row_send, recv_sem=row_recv, device_id=(t, u), device_id_type=MESH,
        ).start()

    def asked(n):
        rows = got_rows.at[pl.ds(0, NAR)]
        pltpu.make_async_copy(rows, rows, req_recv.at[n]).wait()

    def to_scalars(t, n):
        rows = pl.ds(pl.multiple_of(t * NAR, NAR), NAR)
        return pltpu.make_async_copy(got_rows.at[rows], reqs.at[rows], ask_sem.at[n])

    def whose(i):
        n = (i * 13) % GRP
        return n, (g + GRP - n) % GRP

    def fetch(i):
        n, t = whose(i)
        asked(n)
        to_scalars(t, n).start()

    def serve(i, c):
        n, t = whose(i)

        @pl.when(i < GRP - 1)
        def _():
            fetch(i + 1)

        to_scalars(t, n).wait()
        at, want = seeds16(i)
        for d in range(NAR):
            forward_marks(at, want, d)
            serve_one(t, ys[d], pl.ds(pl.multiple_of((i * NAR + d) * CAP, CAP), CAP))
        return c

    fetch(1)
    lax.fori_loop(1, GRP, serve, 0)
    keep.wait()
    to_scalars(g, 0).start()
    to_scalars(g, 0).wait()
    at, want = seeds16(0)
    for d in range(NAR):
        forward_marks(at, want, d)
    for d in range(1, NAR):
        serve_one(g, ys[d], pl.ds(d * CAP, CAP))
    pick(g, y, pl.ds(0, CAP))
    pulled[my_rows, :] = featb[0:CAP, :]

    for n, a in enumerate(shared):
        for d in range(1, NAR):
            link(a.at[y], a.at[y], nar_send.at[n, d - 1], nar_recv.at[n, d - 1], (y + d) % NAR).wait()
    for q in range(NAR):
        w2t[:, q * 128:(q + 1) * 128] = gw2t[q]
    last = jnp.concatenate([bias[0:1, 384:428], jnp.zeros((1, 84), F32)], axis=1)
    b2c[...] = jnp.concatenate([spread(bias[0:1, 256:384]), spread(last)], axis=0)

    def column(row):
        return jnp.concatenate([spread(row[:, c * 128:(c + 1) * 128]) for c in range(SEED // 128)], axis=0)

    for q in range(NAR):
        n = jnp.sum((gidx2[q, 1:1 + F2, :] >= 0).astype(F32), axis=0, keepdims=True)
        invc[q] = column(1.0 / jnp.maximum(n, 1.0))
    livec[...] = column(2.0 * LAM / HID / SEEDS_ALL * live[...].astype(F32))

    for q in range(NAR):
        ids = gidx2[q] - y * FRONT
        for c in range(SEED // 128):
            for k in range(1 + F2):
                row = ids[k:k + 1, c * 128:(c + 1) * 128]
                wants[q, c, k] = jnp.broadcast_to(row, (16, 128)).astype(jnp.int16)

    def backward_marks(i):
        here = iota16 + jnp.full((16, 128), i * 16, jnp.int32).astype(jnp.int16)
        out = pl.ds(pl.multiple_of(i * 16, 16), 16)
        for q in range(NAR):
            for c in range(SEED // 128):
                acc = jnp.where(here == wants[q, c, 1], one, zero)
                for k in range(2, 1 + F2):
                    acc = acc + jnp.where(here == wants[q, c, k], one, zero)
                bsel[q, out, c * 128:(c + 1) * 128] = acc
                bsel[q, out, SEED + c * 128:SEED + (c + 1) * 128] = jnp.where(here == wants[q, c, 0], one, zero)

    def some_marks(i, c):
        backward_marks(i)
        return c

    def sum_marks(i):
        at = pl.multiple_of(i // 2 * 16, 16)
        half = i % 2
        blk = idm[pl.ds(at, 16), :]
        keys, units = spread_columns(blk, range(1, 1 + F1)), spread_columns(blk, range(17, 17 + F1))
        for w in range(4):
            acc = word(lane32 + (half * 4 + w) * 128, keys, units)
            for j in range(8):
                col = pl.ds(pl.multiple_of(half * (SRC // 2) + (w * 8 + j) * 128, 128), 128)
                ssel[pl.ds(at, 16), col] = count(acc, j)

    def sum_ids(b):
        idm[...] = jnp.concatenate(keys_units(idxv[:, cols(b)]), axis=0).T

    def cols(b):
        return pl.ds(pl.multiple_of(b * 256, 256), 256)

    def one_mark(i, c):
        sum_marks(i)
        return c

    sum_ids(0)
    lax.fori_loop(0, 32, one_mark, 0)
    lax.fori_loop(0, 16, some_marks, 0)

    come = pulled.at[pl.ds(0, (DEV - 1) * CAP)]
    pltpu.make_async_copy(come, come, row_recv).wait()
    gone = featb.at[pl.ds(CAP, (DEV - 1) * CAP)]
    pltpu.make_async_copy(gone, gone, row_send).wait()
    sent = mid.at[:, pl.ds(0, GRP - 1)]
    pltpu.make_async_copy(sent, sent, req_send.at[0]).wait()

    def widen(i, c):
        rows = pl.ds(pl.multiple_of(i * 256, 256), 256)
        table[rows, :] = pulled[rows, :].astype(F32)
        return c

    lax.fori_loop(0, SRC // 256, widen, 0)
    table[SRC:SRC + 8, :] = jnp.zeros((8, D_IN), F32)
    for c in to_smem:
        c.wait()

    def forward(b):
        @pl.when(b % 2 == 0)
        def _():
            blk = gbuf.at[left, cols(b), :]
            link(blk, blk, h_send.at[0, b], h_recv.at[0, b], right).wait_recv()
            link(blk, blk, h_send.at[2, b], h_recv.at[2, b], right).start()

        @pl.when(b % 2 == 1)
        def _():
            blk = gbuf.at[right, cols(b), :]
            link(blk, blk, h_send.at[1, b], h_recv.at[1, b], left).wait_recv()
            link(blk, blk, h_send.at[2, b], h_recv.at[2, b], left).start()

    def load_sums(b):
        def some(i, c):
            backward_marks(b * 16 + i)
            found = []
            for e in range(2):
                line = b * 32 + 2 * i + e
                for r in range(8):
                    self_row = view[idx[line, r * 16]]
                    rows = [view[idx[line, r * 16 + 1 + k]] for k in range(F1)]
                    while len(rows) > 1:
                        rows = [p + q for p, q in zip(rows[::2], rows[1::2])] + ([rows[-1]] if len(rows) % 2 else [])
                    found.append((r * 32 + 2 * i + e, self_row, rows[0]))
            for at, self_row, total in found:
                own[pl.ds(at, 1), :] = self_row
                near[pl.ds(at, 1), :] = total
            return c

        lax.fori_loop(0, 16, some, 0)
        finish(b)

    def multiply_sums(b):
        def some(i, c):
            found = []
            for e in range(2):
                for r in range(8):
                    found.append((r * 32 + 2 * i + e, view[idx[b * 32 + 2 * i + e, r * 16]]))
            for at, self_row in found:
                own[pl.ds(at, 1), :] = self_row
            return c

        lax.fori_loop(0, 16, some, 0)
        near[...] = dot(ssel[...], pulled[...])
        finish(b)

    def finish(b):
        rows = cols(b)
        scale = jnp.concatenate(
            [spread(invv[0:1, pl.ds(pl.multiple_of(b * 256 + c * 128, 128), 128)]) for c in range(2)], axis=0
        )
        act = jnp.concatenate([own[...].astype(BF), (near[...] * scale).astype(BF)], axis=1)
        a1 = act.T
        for h in range(2):
            a1t[pl.ds(pl.multiple_of((2 * b + h) * 256, 256), 256), :] = a1[:, h * 128:(h + 1) * 128]
        z = dot(act, gw1[...].reshape(2 * D_IN, HID)) + bias[0:1, 0:HID]
        sig = 1.0 / (1.0 + jnp.exp(-z))
        h1 = z * sig
        slope[rows, :] = sig + h1 * (1.0 - sig)
        gbuf[y, rows, :] = h1.astype(BF)
        blk = gbuf.at[y, rows, :]
        link(blk, blk, h_send.at[0, b], h_recv.at[0, b], right).start()
        link(blk, blk, h_send.at[1, b], h_recv.at[1, b], left).start()

        @pl.when(b > 0)
        def _():
            forward(b - 1)

    def loaded(b, c):
        load_sums(b)
        return c

    multiply_sums(0)
    lax.fori_loop(1, 8, loaded, 0)
    forward(7)

    def from_source(q, fresh=False):
        def rows512(i, c):
            part = dot(fsel[q, pl.ds(pl.multiple_of(i * SEED, SEED), SEED), :], gbuf[q])
            for h in range(2):
                rows = pl.ds(pl.multiple_of(h * 2 * SEED + i * SEED, SEED), SEED)
                now = part[:, h * 128:(h + 1) * 128]
                tot[rows, :] = now if fresh else tot[rows, :] + now
            return c

        lax.fori_loop(0, 2, rows512, 0)

    from_source(y, True)
    for b in range(1, 8, 2):
        blk = gbuf.at[left, b * 256:(b + 1) * 256, :]
        link(blk, blk, h_send.at[0, b], h_recv.at[0, b], right).wait_recv()
    from_source(left)
    for b in range(0, 8, 2):
        blk = gbuf.at[right, b * 256:(b + 1) * 256, :]
        link(blk, blk, h_send.at[1, b], h_recv.at[1, b], left).wait_recv()
    from_source(right)
    for b in range(8):
        blk = gbuf.at[opp, b * 256:(b + 1) * 256, :]
        link(blk, blk, h_send.at[2, b], h_recv.at[2, b], right).wait_recv()
    from_source(opp)

    def wide(a):
        return jnp.concatenate([a, a], axis=1)

    def seeds(first):
        return jnp.concatenate([tot[h * 2 * SEED + first:h * 2 * SEED + first + SEED, :] for h in range(2)], axis=1)

    near2 = (seeds(0) * wide(invc[y])).astype(BF)
    self2 = seeds(SEED).astype(BF)
    alive = live[...].astype(F32)
    diff = self2.astype(F32) - near2.astype(F32)
    pull_apart = wide(livec[...]) * diff

    def swap_start(buf, ssem, rsem):
        blk = buf.at[y]
        link(blk, blk, ssem.at[0], rsem.at[0], right).start()
        link(blk, blk, ssem.at[1], rsem.at[1], left).start()

    def swap_forward(buf, ssem, rsem, cut):
        blk = buf.at[left]
        link(blk, blk, ssem.at[0], rsem.at[0], right).wait_recv()
        half = buf.at[left, 0:cut, :]
        link(half, half, ssem.at[2], rsem.at[2], right).start()
        blk = buf.at[right]
        link(blk, blk, ssem.at[1], rsem.at[1], left).wait_recv()
        half = buf.at[right, cut:, :]
        link(half, half, ssem.at[3], rsem.at[3], left).start()

    def swap_end(buf, ssem, rsem, cut):
        half = buf.at[opp, 0:cut, :]
        link(half, half, ssem.at[2], rsem.at[2], right).wait_recv()
        half = buf.at[opp, cut:, :]
        link(half, half, ssem.at[3], rsem.at[3], left).wait_recv()

    def swap_sent(buf, ssem, rsem, cut):
        blk = buf.at[y]
        link(blk, blk, ssem.at[0], rsem.at[0], right).wait_send()
        link(blk, blk, ssem.at[1], rsem.at[1], left).wait_send()
        half = buf.at[left, 0:cut, :]
        link(half, half, ssem.at[2], rsem.at[2], right).wait_send()
        half = buf.at[right, cut:, :]
        link(half, half, ssem.at[3], rsem.at[3], left).wait_send()

    rbuf[y] = pull_apart.astype(BF)
    swap_start(rbuf, r_send, r_recv)

    act2 = jnp.concatenate([self2, near2], axis=1)
    cls = lax.broadcasted_iota(jnp.int32, (CLS_PAD, SEED), 0)
    b2 = b2c[0:CLS_PAD, :]
    logits = dot(w2t[...], act2, NT) + jnp.concatenate([b2] * 4, axis=1)
    logits = jnp.where(cls < CLS, logits, -1e30)
    top = jnp.max(logits, axis=0, keepdims=True)
    e = jnp.exp(logits - top)
    tot = jnp.sum(e, axis=0, keepdims=True)
    hot = cls == labels[...]
    picked = jnp.sum(jnp.where(hot, logits, 0.0), axis=0, keepdims=True)
    dlog = (alive * (e * (1.0 / tot) - jnp.where(hot, 1.0, 0.0)) * (1.0 / SEEDS_ALL)).astype(BF)
    dbuf[y] = dlog
    swap_start(dbuf, d_send, d_recv)

    loss = jnp.sum(alive * (top + jnp.log(tot) - picked), axis=1, keepdims=True)
    loss = loss + SEEDS_ALL / 2 * jnp.sum(pull_apart * diff, keepdims=True)
    g2t = dot(dlog, act2).astype(BF)
    for q in range(NAR):
        pay[ROW_2 + q * CLS_PAD:ROW_2 + (q + 1) * CLS_PAD, :] = g2t[:, q * 128:(q + 1) * 128]

    def add_grads(q, fresh=False):
        da = dot(dbuf[q], w2t[...], TN)
        r = rbuf[q].astype(F32)
        ds = (da[:, :HID] + r).astype(BF)
        dn = ((da[:, HID:] - r) * wide(invc[q])).astype(BF)
        both = jnp.concatenate([dn, ds], axis=0)

        def rows512(i, c):
            part = dot(bsel[q, pl.ds(pl.multiple_of(i * 512, 512), 512), :], both)
            for h in range(2):
                rows = pl.ds(pl.multiple_of(h * FRONT + i * 512, 512), 512)
                now = part[:, h * 128:(h + 1) * 128]
                dh1[rows, :] = now if fresh else dh1[rows, :] + now
            return c

        lax.fori_loop(0, FRONT // 512, rows512, 0)

    db2 = jnp.sum(dlog.astype(F32), axis=1, keepdims=True)
    db2 = jnp.broadcast_to(db2, (CLS_PAD, 128)).T[0:1, :]
    swap_forward(rbuf, r_send, r_recv, SEED // 2)
    add_grads(y, True)
    swap_forward(dbuf, d_send, d_recv, 96)
    add_grads(left)
    add_grads(right)
    swap_end(rbuf, r_send, r_recv, SEED // 2)
    swap_end(dbuf, d_send, d_recv, 96)
    add_grads(opp)

    def to_z(b, db):
        rows = pl.ds(pl.multiple_of(b * 256, 256), 256)
        dh = jnp.concatenate(
            [dh1[pl.ds(pl.multiple_of(h * FRONT + b * 256, 256), 256), :] for h in range(2)], axis=1
        )
        dz = (dh * slope[rows, :]).astype(BF)
        a1 = jnp.concatenate(
            [a1t[pl.ds(pl.multiple_of((2 * b + h) * 256, 256), 256), :] for h in range(2)], axis=1
        )
        part = dot(a1, dz)
        for h in range(2):
            now = slice(h * 256, (h + 1) * 256)
            gsum[now, :] = gsum[now, :] + part[:, h * 128:(h + 1) * 128]
        return db + jnp.sum(dz.astype(F32), axis=0, keepdims=True)

    gsum[...] = jnp.zeros((512, 128), F32)
    db1 = lax.fori_loop(0, FRONT // 256, to_z, jnp.zeros((1, HID), F32))
    pay[0:512, :] = gsum[...].astype(BF)
    misc[...] = jnp.zeros((32, 128), F32)

    def two(rows, v):
        hi = v.astype(BF).astype(F32)
        misc[rows:rows + 1, 0:v.shape[1]] = hi
        misc[rows + 4:rows + 5, 0:v.shape[1]] = v - hi

    two(0, db1[:, :128])
    two(1, db1[:, 128:])
    two(2, db2[:, :128])
    two(3, db2[:, 128:])
    hi = loss.astype(BF).astype(F32)
    misc[8:9, 0:1] = hi
    misc[9:10, 0:1] = loss - hi
    pay[ROW_MISC:ROWS, :] = misc[...].astype(BF)

    def to_owner(i, c):
        t = (g + i) % GRP

        @pl.when(t < PIECES)
        def _():
            pltpu.make_async_remote_copy(
                src_ref=pay.at[pl.ds(pl.multiple_of(t * PIECE, 16), PIECE)], dst_ref=inbox.at[g],
                send_sem=rs_send, recv_sem=rs_recv, device_id=(t, y), device_id_type=MESH,
            ).start()

        return c

    lax.fori_loop(1, GRP, to_owner, 0)
    mine = pl.ds(pl.multiple_of(g * PIECE, 16), PIECE)

    @pl.when(g < PIECES)
    def _():
        got = inbox.at[pl.ds(0, GRP - 1)]
        pltpu.make_async_copy(got, got, rs_recv).wait()
        inbox[g] = pay[mine, :]
        ybox[y] = jnp.sum(inbox[...].astype(F32), axis=0) + momenta[mine, :]
        for d in range(1, NAR):
            link(ybox.at[y], ybox.at[y], y_send.at[d - 1], y_recv.at[d - 1], ys[d]).start()
        for d in range(1, NAR):
            link(ybox.at[y], ybox.at[y], y_send.at[d - 1], y_recv.at[d - 1], ys[d]).wait()
        o_all[mine, :] = (ybox[0] + ybox[1]) + (ybox[2] + ybox[3])

        def tell(i, c):
            pltpu.make_async_remote_copy(
                src_ref=o_all.at[mine], dst_ref=o_all.at[mine], send_sem=ag_send, recv_sem=ag_recv,
                device_id=((g + i) % GRP, y), device_id_type=MESH,
            ).start()
            return c

        lax.fori_loop(1, GRP, tell, 0)
        got = o_all.at[pl.ds(0, (PIECES - 1) * PIECE)]
        pltpu.make_async_copy(got, got, ag_recv).wait()
        gone = pay.at[pl.ds(0, (PIECES - 1) * PIECE)]
        pltpu.make_async_copy(gone, gone, rs_send).wait()
        gone = table.at[pl.ds(0, (GRP - 1) * PIECE)]
        pltpu.make_async_copy(gone, gone, ag_send).wait()

    @pl.when(g >= PIECES)
    def _():
        pltpu.make_async_copy(o_all, o_all, ag_recv).wait()
        pltpu.make_async_copy(pay, pay, rs_send).wait()

    for b in range(8):
        blk = gbuf.at[y, b * 256:(b + 1) * 256, :]
        link(blk, blk, h_send.at[0, b], h_recv.at[0, b], right).wait_send()
        link(blk, blk, h_send.at[1, b], h_recv.at[1, b], left).wait_send()
        blk = gbuf.at[opp, b * 256:(b + 1) * 256, :]
        link(blk, blk, h_send.at[2, b], h_recv.at[2, b], right).wait_send()
    swap_sent(rbuf, r_send, r_recv, SEED // 2)
    swap_sent(dbuf, d_send, d_recv, 96)


def main(reqt, feat, idx1t, msk1t, idx2t, msk2t, labels, live, w1, w2own, m1, m2own, bias):
    vm = pl.BlockSpec(memory_space=pltpu.VMEM)
    dma = pltpu.SemaphoreType.DMA
    sds = jax.ShapeDtypeStruct
    V = pltpu.VMEM
    return pl.pallas_call(
        main_kernel,
        out_shape=sds((ROWS, 128), F32),
        in_specs=[vm, pl.BlockSpec(memory_space=pl.ANY)] + [vm] * 11,
        out_specs=vm,
        scratch_shapes=[
            V((SRC + 8, D_IN), F32),
            V((OWN, D_IN), BF),
            V((SRC, D_IN), BF),
            V((CAP, D_IN), F32),
            V((DEV, 128), jnp.int32),
            V((DEV, 128), jnp.int32),
            V((NAR, GRP, 1, 128), jnp.int32),
            V((16, FRONT), jnp.int32),
            V((256, 128), jnp.int32),
            V((1, FRONT), F32),
            V((256, D_IN), F32),
            V((256, D_IN), F32),
            V((FRONT, HID), F32),
            V((NAR, FRONT, HID), BF),
            V((NAR, 2 * SEED, FRONT), BF),
            V((NAR, FRONT, 2 * SEED), BF),
            V((NAR, 4, 1 + F2, 16, 128), jnp.int16),
            V((SEED, 32), jnp.int32),
            V((256, SRC), BF),
            V((256, 32), jnp.int32),
            V((NAR, SEED, 128), F32),
            V((SEED, 128), F32),
            V((NAR, SEED, HID), BF),
            V((NAR, CLS_PAD, SEED), BF),
            V((NAR, 64, HID), BF),
            V((NAR, CLS_PAD, 128), BF),
            V((ROWS, 128), F32),
            V((NAR, 16, SEED), jnp.int32),
            V((CLS_PAD, 2 * HID), BF),
            V((HID, 128), F32),
            V((ROWS, 128), BF),
            V((32, 128), F32),
            V((GRP, PIECE, 128), BF),
            V((NAR, PIECE, 128), F32),
            pltpu.SMEM((DEV, 1, 128), jnp.int32),
            pltpu.SMEM((256, 128), jnp.int32),
            dma, dma((3,)), dma((GRP,)), dma((NAR,)), dma((NAR,)), dma((GRP,)), dma, dma, dma((3, 3)), dma((3, 3)),
            dma((3, 8)), dma((3, 8)), dma((4,)), dma((4,)), dma((4,)), dma((4,)),
            dma, dma, dma((3,)), dma((3,)), dma, dma,
        ],
        compiler_params=pltpu.CompilerParams(
            collective_id=0, has_side_effects=True, vmem_limit_bytes=62 * 2**20
        ),
    )(reqt, feat, idx1t, msk1t, idx2t, msk2t, labels, live, w1, w2own, m1, m2own, bias)


def update_kernel(
    res, w1own, w2own, bias, biasm, biasv,
    o_loss, o_first, o_second, o_mom1, o_mom2, o_flow, o_slow, o_bias, o_bm, o_bv,
    x1s, x2s,
):
    y = lax.axis_index("nar")
    mom1 = jnp.concatenate([res[0:256, :], res[256:512, :]], axis=1)
    x1s[...] = mom1
    block64 = pl.ds(pl.multiple_of(y * 64, 64), 64)
    o_mom1[...] = x1s[block64, :]
    x1 = mom1 * (1.0 / (jnp.sqrt(jnp.sum(mom1 * mom1, keepdims=True)) + 1e-07))
    mom2 = jnp.concatenate([res[ROW_2 + q * CLS_PAD:ROW_2 + (q + 1) * CLS_PAD, :] for q in range(NAR)], axis=1)
    x2 = mom2 * (1.0 / (jnp.sqrt(jnp.sum(mom2 * mom2, keepdims=True)) + 1e-07))
    for i in range(NS_ITERS):
        x1 = ns_step(x1)
        x2 = ns_step(x2)
    x1s[...] = x1
    for q in range(NAR):
        x2s[q] = x2[:, q * 128:(q + 1) * 128]
    first_new = w1own[...] * (1.0 - WDECAY) - x1s[block64, :]
    o_first[...] = first_new
    o_flow[...] = first_new.astype(BF)
    second = w2own[...] * (1.0 - WDECAY) - (2 * HID / CLS) ** 0.5 * x2s[y][0:CLS, :]
    o_second[...] = second
    o_slow[...] = second.astype(BF)
    o_mom2[...] = res[pl.ds(pl.multiple_of(ROW_2 + y * CLS_PAD, 16), CLS_PAD), :][0:CLS, :]

    gb = res[ROW_MISC + 0:ROW_MISC + 4, :] + res[ROW_MISC + 4:ROW_MISC + 8, :]
    gb = jnp.concatenate([gb[0:1, :], gb[1:2, :], gb[2:3, :], gb[3:4, 0:44]], axis=1)
    m_new = BETA_ONE * biasm[...] + (1.0 - BETA_ONE) * gb
    v_new = BETA_TWO * biasv[...] + (1.0 - BETA_TWO) * gb * gb
    m_hat = m_new / (1.0 - BETA_ONE**STEP)
    v_hat = v_new / (1.0 - BETA_TWO**STEP)
    o_bias[...] = bias[...] * (1.0 - LR_BIAS * WDECAY) - LR_BIAS * m_hat / (jnp.sqrt(v_hat) + EPSILON)
    o_bm[...] = m_new
    o_bv[...] = v_new
    o_loss[...] = res[ROW_MISC + 8:ROW_MISC + 9, 0:1] + res[ROW_MISC + 9:ROW_MISC + 10, 0:1]


def update(*args):
    vm = pl.BlockSpec(memory_space=pltpu.VMEM)
    sds = jax.ShapeDtypeStruct
    return pl.pallas_call(
        update_kernel,
        out_shape=[
            sds((1, 1), F32), sds((64, HID), F32), sds((CLS, 128), F32), sds((64, HID), F32), sds((CLS, 128), F32),
            sds((64, HID), BF), sds((CLS, 128), BF), sds((1, 428), F32), sds((1, 428), F32), sds((1, 428), F32),
        ],
        in_specs=[vm] * 6,
        out_specs=[vm] * 10,
        scratch_shapes=[pltpu.VMEM((2 * D_IN, HID), F32), pltpu.VMEM((NAR, CLS_PAD, 128), F32)],
        compiler_params=pltpu.CompilerParams(vmem_limit_bytes=32 * 2**20),
    )(*args)


def per_device(
    features, requests, index_one, mask_one, index_two, mask_two, labels, seed_live,
    w_first, w_second, mom_first, mom_second, biases, bias_m, bias_v,
):
    w2own, bias = w_second.T, biases[None, :]
    res = main(
        requests.T, features, index_one.T, mask_one.T, index_two.T, mask_two.T, labels[None, :], seed_live[None, :],
        w_first, w2own, mom_first, mom_second.T, bias,
    )
    loss, first_new, second_new, mom_one, mom_two, first_low, second_low, bias_new, m_new, v_new = update(
        res, w_first, w2own, bias, bias_m[None, :], bias_v[None, :]
    )
    return (
        loss.reshape(()), first_new, second_new.T, mom_one, mom_two.T, first_low, second_low.T,
        bias_new.reshape(-1), m_new.reshape(-1), v_new.reshape(-1),
    )


def solution(mesh):
    both = ("grp", "nar")
    placed = (
        P(both, None), P(both, None), P(both, None), P(both, None), P(both, None), P(both, None),
        P(both), P(both), P("nar", None), P("nar", None), P("nar", None), P("nar", None), P(), P(), P(),
    )
    nar = P("nar", None)
    return jax.shard_map(
        per_device, mesh=mesh, in_specs=placed,
        out_specs=(P(), nar, nar, nar, nar, nar, nar, P(), P(), P()), check_vma=False,
    )
```

```python
import functools

import jax
import jax.numpy as jnp
from jax import lax
from jax.experimental import pallas as pl
from jax.experimental.pallas import tpu as pltpu
from jax.sharding import PartitionSpec as P

HID = 256
CLS = 172
CLS_PAD = 176
D_IN = 128
F1 = 15
F2 = 10
NS_ITERS = 5
STEP = 10
LAM = 0.5
MU = 0.95
WDECAY = 0.01
LR_BIAS = 0.05
BETA_ONE = 0.9
BETA_TWO = 0.999
EPSILON = 1e-08
NS_A = 3.4445
NS_B = -4.775
NS_C = 2.0315
HIGH = lax.Precision.HIGHEST
MESH = pl.DeviceIdType.MESH
BF = jnp.bfloat16
F32 = jnp.float32

DEV = 128
NAR = 4
OWN = 8192
CAP = 64
SRC = 8192
FRONT = 2048
SEED = 512


def all_to(t):
    return (t // NAR, t % NAR)


GRP = 32
PIECE = 48
PIECES = 26
ROW_2 = 512
ROW_MISC = ROW_2 + NAR * CLS_PAD
ROWS = PIECES * PIECE
SEEDS_ALL = SEED * DEV


def dot(a, b, dims=((1,), (0,))):
    return lax.dot_general(a, b, (dims, ((), ())), preferred_element_type=F32)


NN = ((1,), (0,))
NT = ((1,), (1,))
TN = ((0,), (0,))


def split(a):
    hi = a.astype(BF)
    return hi, (a - hi.astype(F32)).astype(BF)


def dot3(a, b, dims):
    (ah, al), (bh, bl) = a, b
    return dot(
        jnp.concatenate([ah, ah, al], axis=dims[0][0]), jnp.concatenate([bh, bl, bh], axis=dims[1][0]), dims
    )


def ns_step(x):
    xs = split(x)
    gram = dot3(xs, xs, NT)
    gs = split(gram)
    mix = NS_B * gram + NS_C * dot3(gs, gs, NN)
    return NS_A * x + dot3(split(mix), xs, NN)


def spread(row):
    return jnp.broadcast_to(row, (128, 128)).T


def main_kernel(
    reqt, feat, idx1t, msk1t, idx2t, msk2t, labels, live, w1, w2own, m1, m2own, bias,
    o_all,
    table, featb, pulled, stage, reqv, reqin, mid, idxv, idxp, invv, near, own, slope, gbuf, fsel, bsel, wants, idc, ssel, idm, invc, livec, rbuf, dbuf,
    gw1, gw2t, momenta, gidx2, w2t, b2c, pay, misc, inbox, ybox,
    reqs, idx,
    feat_sem, loc_sem, ask_sem, req_send, mid_recv, req_recv, row_send, row_recv, nar_send, nar_recv,
    h_send, h_recv, r_send, r_recv, d_send, d_recv, rs_send, rs_recv, y_send, y_recv, ag_send, ag_recv, pair_send, pair_recv,
):
    a1t, dh1, tot, gsum = featb, table, table.at[2 * FRONT:3 * FRONT], table.at[3 * FRONT:3 * FRONT + 512]
    g = lax.axis_index("grp")
    y = lax.axis_index("nar")
    me = g * NAR + y
    left, right, opp = (y + 3) % NAR, (y + 1) % NAR, (y + 2) % NAR

    load = pltpu.make_async_copy(feat, featb, feat_sem)
    load.start()

    barrier = pltpu.get_barrier_semaphore()

    ys = [(y + d) % NAR for d in range(NAR)]

    def greet(i, c):
        pl.semaphore_signal(barrier, inc=1, device_id=((g + i) % GRP, y), device_id_type=MESH)
        return c

    for d in range(1, NAR):
        pl.semaphore_signal(barrier, inc=1, device_id=(g, ys[d]), device_id_type=MESH)
    lax.fori_loop(1, GRP, greet, 0)

    def link(src, dst, ssem, rsem, to):
        return pltpu.make_async_remote_copy(
            src_ref=src, dst_ref=dst, send_sem=ssem, recv_sem=rsem, device_id=(g, to), device_id_type=MESH
        )

    reqv[...] = jnp.concatenate([reqt[...], jnp.zeros((DEV - CAP, DEV), jnp.int32)], axis=0).T
    ask_rows = reqv.reshape(GRP, NAR, 1, 128)
    got_rows = reqin.reshape(DEV, 1, 128)

    gw1[y] = w1[...].astype(BF)
    pad = CLS_PAD - CLS
    gw2t[y] = jnp.concatenate([w2own[...], jnp.zeros((pad, 128), F32)], axis=0).astype(BF)
    momenta[...] = jnp.zeros((ROWS, 128), F32)
    for h in range(2):
        momenta[pl.ds(pl.multiple_of(h * 256 + y * 64, 64), 64), :] = MU * m1[:, h * 128:(h + 1) * 128]
    momenta[pl.ds(pl.multiple_of(ROW_2 + y * CLS_PAD, 16), CLS_PAD), :] = jnp.concatenate(
        [MU * m2own[...], jnp.zeros((pad, 128), F32)], axis=0
    )
    gidx2[y] = jnp.concatenate(
        [idx2t[0:1, :], jnp.where(msk2t[...] > 0, idx2t[1:, :], -1), jnp.zeros((5, SEED), jnp.int32)], axis=0
    )
    shared = (gidx2, gw1, gw2t)

    pl.semaphore_wait(barrier, GRP + NAR - 2)

    def ask_group(d):
        return pltpu.make_async_remote_copy(
            src_ref=ask_rows.at[:, ys[d]], dst_ref=mid.at[y], send_sem=req_send.at[d], recv_sem=mid_recv.at[d],
            device_id=(g, ys[d]), device_id_type=MESH,
        )

    for d in range(1, NAR):
        ask_group(d).start()
    keep = pltpu.make_async_copy(ask_rows.at[:, y], mid.at[y], loc_sem.at[2])
    keep.start()
    for n, a in enumerate(shared):
        for d in range(1, NAR):
            link(a.at[y], a.at[y], nar_send.at[n, d - 1], nar_recv.at[n, d - 1], (y + d) % NAR).start()

    msk = msk1t[...]
    idxv[0:1, :] = idx1t[0:1, :]
    idxv[1:16, :] = jnp.where(msk > 0, idx1t[1:16, :], SRC)
    invv[...] = 1.0 / jnp.maximum(jnp.sum(msk.astype(F32), axis=0, keepdims=True), 1.0)
    for half in range(2):
        parts = []
        for r in range(8):
            parts.append(jnp.concatenate(
                [idxv[:, (half * 4 + b) * 256 + r * 32:(half * 4 + b) * 256 + r * 32 + 32] for b in range(4)], axis=1
            ))
        idxp[half * 128:(half + 1) * 128, :] = jnp.concatenate(parts, axis=0).T
    to_smem = [pltpu.make_async_copy(idxp, idx, loc_sem.at[0])]
    for c in to_smem:
        c.start()

    keep.wait()
    for d in range(1, NAR):
        ask_group(d).wait()
    own_rows = pl.ds(pl.multiple_of(g * NAR, NAR), NAR)

    def ask(i, c):
        n = (i * 13) % GRP
        t = (g + n) % GRP
        pltpu.make_async_remote_copy(
            src_ref=mid.at[:, t], dst_ref=got_rows.at[own_rows], send_sem=req_send.at[0], recv_sem=req_recv.at[n],
            device_id=(t, y), device_id_type=MESH,
        ).start()
        return c

    lax.fori_loop(1, GRP, ask, 0)
    keep = pltpu.make_async_copy(mid.at[:, g], got_rows.at[own_rows], loc_sem.at[2])
    keep.start()

    load.wait()

    def widen_features(i, c):
        rows = pl.ds(pl.multiple_of(i * 256, 256), 256)
        table[rows, :] = featb[rows, :].astype(F32)
        return c

    lax.fori_loop(0, OWN // 256, widen_features, 0)

    lane32 = lax.broadcasted_iota(jnp.int32, (16, 128), 1)
    lane16 = lane32.astype(jnp.int16)
    iota16 = lax.broadcasted_iota(jnp.int32, (16, 128), 0).astype(jnp.int16)
    one, zero = jnp.ones((16, 128), BF), jnp.zeros((16, 128), BF)

    def unit(digit):
        v = jnp.ones_like(digit)
        for j in range(1, 8):
            v = jnp.where(digit == j, 1 << 4 * j, v)
        return v

    def count(acc, j):
        return ((acc >> (4 * j)) & 15).astype(F32).astype(BF)

    def keys_units(ids):
        return (ids & 127) + (ids >> 10) * 128, unit((ids >> 7) & 7)

    def word(pos, keys, units):
        acc = jnp.zeros((16, 128), jnp.int32)
        for k, u in zip(keys, units):
            acc = acc + jnp.where(pos == k, u, 0)
        return acc

    def spread_columns(blk, ks):
        return [jnp.broadcast_to(blk[:, k:k + 1], (16, 128)) for k in ks]

    ids = gidx2[y]
    keys, units = keys_units(ids)
    idc[...] = jnp.concatenate([ids[0:1, :], keys[1:, :], units], axis=0).T

    def seeds16(i):
        at = pl.multiple_of(i * 16, 16)
        blk = idc[pl.ds(at, 16), :]
        self_row = jnp.broadcast_to(blk[:, 0:1], (16, 128)).astype(jnp.int16)
        return at, (spread_columns(blk, range(1, 1 + F2)), spread_columns(blk, range(17, 17 + F2)), self_row)

    def forward_marks(at, want, q):
        keys, units, self_row = want
        for w in range(2):
            acc = word(lane32 + 128 * (2 * q + w), keys, units)
            for j in range(8):
                c = w * 8 + j
                fsel[q, pl.ds(at, 16), c * 128:(c + 1) * 128] = count(acc, j)
                here = lane16 + jnp.full((16, 128), q * FRONT + c * 128, jnp.int32).astype(jnp.int16)
                fsel[q, pl.ds(SEED + at, 16), c * 128:(c + 1) * 128] = jnp.where(here == self_row, one, zero)

    view = table.reshape(SRC + 8, 1, D_IN)
    my_rows = pl.ds(pl.multiple_of(me * CAP, CAP), CAP)

    def pick(t, u, slot):
        for half in range(0, CAP, 32):
            rows = [view[reqs[t * NAR + u, 0, half + r]] for r in range(32)]
            for r in range(32):
                stage[half + r:half + r + 1, :] = rows[r]
        featb[slot, :] = stage[...].astype(BF)

    def serve_one(t, u, slot):
        pick(t, u, slot)
        pltpu.make_async_remote_copy(
            src_ref=featb.at[slot], dst_ref=pulled.at[my_rows],
            send_sem=row_send, recv_sem=row_recv, device_id=(t, u), device_id_type=MESH,
        ).start()

    def asked(n):
        rows = got_rows.at[pl.ds(0, NAR)]
        pltpu.make_async_copy(rows, rows, req_recv.at[n]).wait()

    def to_scalars(t, n):
        rows = pl.ds(pl.multiple_of(t * NAR, NAR), NAR)
        return pltpu.make_async_copy(got_rows.at[rows], reqs.at[rows], ask_sem.at[n])

    def whose(i):
        n = (i * 13) % GRP
        return n, (g + GRP - n) % GRP

    def fetch(i):
        n, t = whose(i)
        asked(n)
        to_scalars(t, n).start()

    def serve(i, c):
        n, t = whose(i)

        @pl.when(i < GRP - 1)
        def _():
            fetch(i + 1)

        to_scalars(t, n).wait()
        at, want = seeds16(i)
        for d in range(NAR):
            forward_marks(at, want, d)
            serve_one(t, ys[d], pl.ds(pl.multiple_of((i * NAR + d) * CAP, CAP), CAP))
        return c

    fetch(1)
    lax.fori_loop(1, GRP, serve, 0)
    keep.wait()
    to_scalars(g, 0).start()
    to_scalars(g, 0).wait()
    at, want = seeds16(0)
    for d in range(NAR):
        forward_marks(at, want, d)
    for d in range(1, NAR):
        serve_one(g, ys[d], pl.ds(d * CAP, CAP))
    pick(g, y, pl.ds(0, CAP))
    pulled[my_rows, :] = featb[0:CAP, :]

    for n, a in enumerate(shared):
        for d in range(1, NAR):
            link(a.at[y], a.at[y], nar_send.at[n, d - 1], nar_recv.at[n, d - 1], (y + d) % NAR).wait()
    for q in range(NAR):
        w2t[:, q * 128:(q + 1) * 128] = gw2t[q]
    last = jnp.concatenate([bias[0:1, 384:428], jnp.zeros((1, 84), F32)], axis=1)
    b2c[...] = jnp.concatenate([spread(bias[0:1, 256:384]), spread(last)], axis=0)

    def column(row):
        return jnp.concatenate([spread(row[:, c * 128:(c + 1) * 128]) for c in range(SEED // 128)], axis=0)

    for q in range(NAR):
        n = jnp.sum((gidx2[q, 1:1 + F2, :] >= 0).astype(F32), axis=0, keepdims=True)
        invc[q] = column(1.0 / jnp.maximum(n, 1.0))
    livec[...] = column(2.0 * LAM / HID / SEEDS_ALL * live[...].astype(F32))

    for q in range(NAR):
        ids = gidx2[q] - y * FRONT
        for c in range(SEED // 128):
            for k in range(1 + F2):
                row = ids[k:k + 1, c * 128:(c + 1) * 128]
                wants[q, c, k] = jnp.broadcast_to(row, (16, 128)).astype(jnp.int16)

    def backward_marks(i):
        here = iota16 + jnp.full((16, 128), i * 16, jnp.int32).astype(jnp.int16)
        out = pl.ds(pl.multiple_of(i * 16, 16), 16)
        for q in range(NAR):
            for c in range(SEED // 128):
                acc = jnp.where(here == wants[q, c, 1], one, zero)
                for k in range(2, 1 + F2):
                    acc = acc + jnp.where(here == wants[q, c, k], one, zero)
                bsel[q, out, c * 128:(c + 1) * 128] = acc
                bsel[q, out, SEED + c * 128:SEED + (c + 1) * 128] = jnp.where(here == wants[q, c, 0], one, zero)

    def some_marks(i, c):
        backward_marks(i)
        return c

    def sum_marks(i):
        at = pl.multiple_of(i // 2 * 16, 16)
        half = i % 2
        blk = idm[pl.ds(at, 16), :]
        keys, units = spread_columns(blk, range(1, 1 + F1)), spread_columns(blk, range(17, 17 + F1))
        for w in range(4):
            acc = word(lane32 + (half * 4 + w) * 128, keys, units)
            for j in range(8):
                col = pl.ds(pl.multiple_of(half * (SRC // 2) + (w * 8 + j) * 128, 128), 128)
                ssel[pl.ds(at, 16), col] = count(acc, j)

    def sum_ids(b):
        idm[...] = jnp.concatenate(keys_units(idxv[:, cols(b)]), axis=0).T

    def cols(b):
        return pl.ds(pl.multiple_of(b * 256, 256), 256)

    def one_mark(i, c):
        sum_marks(i)
        return c

    sum_ids(0)
    lax.fori_loop(0, 32, one_mark, 0)
    lax.fori_loop(0, 16, some_marks, 0)

    come = pulled.at[pl.ds(0, (DEV - 1) * CAP)]
    pltpu.make_async_copy(come, come, row_recv).wait()
    gone = featb.at[pl.ds(CAP, (DEV - 1) * CAP)]
    pltpu.make_async_copy(gone, gone, row_send).wait()
    sent = mid.at[:, pl.ds(0, GRP - 1)]
    pltpu.make_async_copy(sent, sent, req_send.at[0]).wait()

    def widen(i, c):
        rows = pl.ds(pl.multiple_of(i * 256, 256), 256)
        table[rows, :] = pulled[rows, :].astype(F32)
        return c

    lax.fori_loop(0, SRC // 256, widen, 0)
    table[SRC:SRC + 8, :] = jnp.zeros((8, D_IN), F32)
    for c in to_smem:
        c.wait()

    def forward(b):
        @pl.when(b % 2 == 0)
        def _():
            blk = gbuf.at[left, cols(b), :]
            link(blk, blk, h_send.at[0, b], h_recv.at[0, b], right).wait_recv()
            link(blk, blk, h_send.at[2, b], h_recv.at[2, b], right).start()

        @pl.when(b % 2 == 1)
        def _():
            blk = gbuf.at[right, cols(b), :]
            link(blk, blk, h_send.at[1, b], h_recv.at[1, b], left).wait_recv()
            link(blk, blk, h_send.at[2, b], h_recv.at[2, b], left).start()

    def load_sums(b):
        def some(i, c):
            backward_marks(b * 16 + i)
            found = []
            for e in range(2):
                line = b * 32 + 2 * i + e
                for r in range(8):
                    self_row = view[idx[line, r * 16]]
                    rows = [view[idx[line, r * 16 + 1 + k]] for k in range(F1)]
                    while len(rows) > 1:
                        rows = [p + q for p, q in zip(rows[::2], rows[1::2])] + ([rows[-1]] if len(rows) % 2 else [])
                    found.append((r * 32 + 2 * i + e, self_row, rows[0]))
            for at, self_row, total in found:
                own[pl.ds(at, 1), :] = self_row
                near[pl.ds(at, 1), :] = total
            return c

        lax.fori_loop(0, 16, some, 0)
        finish(b)

    def multiply_sums(b):
        def some(i, c):
            found = []
            for e in range(2):
                for r in range(8):
                    found.append((r * 32 + 2 * i + e, view[idx[b * 32 + 2 * i + e, r * 16]]))
            for at, self_row in found:
                own[pl.ds(at, 1), :] = self_row
            return c

        lax.fori_loop(0, 16, some, 0)
        near[...] = dot(ssel[...], pulled[...])
        finish(b)

    def finish(b):
        rows = cols(b)
        scale = jnp.concatenate(
            [spread(invv[0:1, pl.ds(pl.multiple_of(b * 256 + c * 128, 128), 128)]) for c in range(2)], axis=0
        )
        act = jnp.concatenate([own[...].astype(BF), (near[...] * scale).astype(BF)], axis=1)
        a1 = act.T
        for h in range(2):
            a1t[pl.ds(pl.multiple_of((2 * b + h) * 256, 256), 256), :] = a1[:, h * 128:(h + 1) * 128]
        z = dot(act, gw1[...].reshape(2 * D_IN, HID)) + bias[0:1, 0:HID]
        sig = 1.0 / (1.0 + jnp.exp(-z))
        h1 = z * sig
        slope[rows, :] = sig + h1 * (1.0 - sig)
        gbuf[y, rows, :] = h1.astype(BF)
        blk = gbuf.at[y, rows, :]
        link(blk, blk, h_send.at[0, b], h_recv.at[0, b], right).start()
        link(blk, blk, h_send.at[1, b], h_recv.at[1, b], left).start()

        @pl.when(b > 0)
        def _():
            forward(b - 1)

    def loaded(b, c):
        load_sums(b)
        return c

    multiply_sums(0)
    lax.fori_loop(1, 8, loaded, 0)
    forward(7)

    def from_source(q, fresh=False):
        def rows512(i, c):
            part = dot(fsel[q, pl.ds(pl.multiple_of(i * SEED, SEED), SEED), :], gbuf[q])
            for h in range(2):
                rows = pl.ds(pl.multiple_of(h * 2 * SEED + i * SEED, SEED), SEED)
                now = part[:, h * 128:(h + 1) * 128]
                tot[rows, :] = now if fresh else tot[rows, :] + now
            return c

        lax.fori_loop(0, 2, rows512, 0)

    from_source(y, True)
    for b in range(1, 8, 2):
        blk = gbuf.at[left, b * 256:(b + 1) * 256, :]
        link(blk, blk, h_send.at[0, b], h_recv.at[0, b], right).wait_recv()
    from_source(left)
    for b in range(0, 8, 2):
        blk = gbuf.at[right, b * 256:(b + 1) * 256, :]
        link(blk, blk, h_send.at[1, b], h_recv.at[1, b], left).wait_recv()
    from_source(right)
    for b in range(8):
        blk = gbuf.at[opp, b * 256:(b + 1) * 256, :]
        link(blk, blk, h_send.at[2, b], h_recv.at[2, b], right).wait_recv()
    from_source(opp)

    def wide(a):
        return jnp.concatenate([a, a], axis=1)

    def seeds(first):
        return jnp.concatenate([tot[h * 2 * SEED + first:h * 2 * SEED + first + SEED, :] for h in range(2)], axis=1)

    near2 = (seeds(0) * wide(invc[y])).astype(BF)
    self2 = seeds(SEED).astype(BF)
    alive = live[...].astype(F32)
    diff = self2.astype(F32) - near2.astype(F32)
    pull_apart = wide(livec[...]) * diff

    def swap_start(buf, ssem, rsem):
        blk = buf.at[y]
        link(blk, blk, ssem.at[0], rsem.at[0], right).start()
        link(blk, blk, ssem.at[1], rsem.at[1], left).start()

    def swap_forward(buf, ssem, rsem, cut):
        blk = buf.at[left]
        link(blk, blk, ssem.at[0], rsem.at[0], right).wait_recv()
        half = buf.at[left, 0:cut, :]
        link(half, half, ssem.at[2], rsem.at[2], right).start()
        blk = buf.at[right]
        link(blk, blk, ssem.at[1], rsem.at[1], left).wait_recv()
        half = buf.at[right, cut:, :]
        link(half, half, ssem.at[3], rsem.at[3], left).start()

    def swap_end(buf, ssem, rsem, cut):
        half = buf.at[opp, 0:cut, :]
        link(half, half, ssem.at[2], rsem.at[2], right).wait_recv()
        half = buf.at[opp, cut:, :]
        link(half, half, ssem.at[3], rsem.at[3], left).wait_recv()

    def swap_sent(buf, ssem, rsem, cut):
        blk = buf.at[y]
        link(blk, blk, ssem.at[0], rsem.at[0], right).wait_send()
        link(blk, blk, ssem.at[1], rsem.at[1], left).wait_send()
        half = buf.at[left, 0:cut, :]
        link(half, half, ssem.at[2], rsem.at[2], right).wait_send()
        half = buf.at[right, cut:, :]
        link(half, half, ssem.at[3], rsem.at[3], left).wait_send()

    rbuf[y] = pull_apart.astype(BF)
    swap_start(rbuf, r_send, r_recv)

    act2 = jnp.concatenate([self2, near2], axis=1)
    cls = lax.broadcasted_iota(jnp.int32, (CLS_PAD, SEED), 0)
    b2 = b2c[0:CLS_PAD, :]
    logits = dot(w2t[...], act2, NT) + jnp.concatenate([b2] * 4, axis=1)
    logits = jnp.where(cls < CLS, logits, -1e30)
    top = jnp.max(logits, axis=0, keepdims=True)
    e = jnp.exp(logits - top)
    tot = jnp.sum(e, axis=0, keepdims=True)
    hot = cls == labels[...]
    picked = jnp.sum(jnp.where(hot, logits, 0.0), axis=0, keepdims=True)
    dlog = (alive * (e * (1.0 / tot) - jnp.where(hot, 1.0, 0.0)) * (1.0 / SEEDS_ALL)).astype(BF)
    dbuf[y] = dlog
    swap_start(dbuf, d_send, d_recv)

    loss = jnp.sum(alive * (top + jnp.log(tot) - picked), axis=1, keepdims=True)
    loss = loss + SEEDS_ALL / 2 * jnp.sum(pull_apart * diff, keepdims=True)
    g2t = dot(dlog, act2).astype(BF)
    for q in range(NAR):
        pay[ROW_2 + q * CLS_PAD:ROW_2 + (q + 1) * CLS_PAD, :] = g2t[:, q * 128:(q + 1) * 128]

    def add_grads(q, fresh=False):
        da = dot(dbuf[q], w2t[...], TN)
        r = rbuf[q].astype(F32)
        ds = (da[:, :HID] + r).astype(BF)
        dn = ((da[:, HID:] - r) * wide(invc[q])).astype(BF)
        both = jnp.concatenate([dn, ds], axis=0)

        def rows512(i, c):
            part = dot(bsel[q, pl.ds(pl.multiple_of(i * 512, 512), 512), :], both)
            for h in range(2):
                rows = pl.ds(pl.multiple_of(h * FRONT + i * 512, 512), 512)
                now = part[:, h * 128:(h + 1) * 128]
                dh1[rows, :] = now if fresh else dh1[rows, :] + now
            return c

        lax.fori_loop(0, FRONT // 512, rows512, 0)

    db2 = jnp.sum(dlog.astype(F32), axis=1, keepdims=True)
    db2 = jnp.broadcast_to(db2, (CLS_PAD, 128)).T[0:1, :]
    swap_forward(rbuf, r_send, r_recv, SEED // 2)
    add_grads(y, True)
    swap_forward(dbuf, d_send, d_recv, 96)
    add_grads(left)
    add_grads(right)
    swap_end(rbuf, r_send, r_recv, SEED // 2)
    swap_end(dbuf, d_send, d_recv, 96)
    add_grads(opp)

    def to_z(b, db):
        rows = pl.ds(pl.multiple_of(b * 256, 256), 256)
        dh = jnp.concatenate(
            [dh1[pl.ds(pl.multiple_of(h * FRONT + b * 256, 256), 256), :] for h in range(2)], axis=1
        )
        dz = (dh * slope[rows, :]).astype(BF)
        a1 = jnp.concatenate(
            [a1t[pl.ds(pl.multiple_of((2 * b + h) * 256, 256), 256), :] for h in range(2)], axis=1
        )
        part = dot(a1, dz)
        for h in range(2):
            now = slice(h * 256, (h + 1) * 256)
            gsum[now, :] = gsum[now, :] + part[:, h * 128:(h + 1) * 128]
        return db + jnp.sum(dz.astype(F32), axis=0, keepdims=True)

    gsum[...] = jnp.zeros((512, 128), F32)
    db1 = lax.fori_loop(0, FRONT // 256, to_z, jnp.zeros((1, HID), F32))
    pay[0:512, :] = gsum[...].astype(BF)
    misc[...] = jnp.zeros((32, 128), F32)

    def two(rows, v):
        hi = v.astype(BF).astype(F32)
        misc[rows:rows + 1, 0:v.shape[1]] = hi
        misc[rows + 4:rows + 5, 0:v.shape[1]] = v - hi

    two(0, db1[:, :128])
    two(1, db1[:, 128:])
    two(2, db2[:, :128])
    two(3, db2[:, 128:])
    hi = loss.astype(BF).astype(F32)
    misc[8:9, 0:1] = hi
    misc[9:10, 0:1] = loss - hi
    pay[ROW_MISC:ROWS, :] = misc[...].astype(BF)

    def to_owner(i, c):
        t = (g + i) % GRP

        @pl.when(t < PIECES)
        def _():
            pltpu.make_async_remote_copy(
                src_ref=pay.at[pl.ds(pl.multiple_of(t * PIECE, 16), PIECE)], dst_ref=inbox.at[g],
                send_sem=rs_send, recv_sem=rs_recv, device_id=(t, y), device_id_type=MESH,
            ).start()

        return c

    lax.fori_loop(1, GRP, to_owner, 0)
    mine = pl.ds(pl.multiple_of(g * PIECE, 16), PIECE)

    @pl.when(g < PIECES)
    def _():
        got = inbox.at[pl.ds(0, GRP - 1)]
        pltpu.make_async_copy(got, got, rs_recv).wait()
        inbox[g] = pay[mine, :]
        ybox[y] = jnp.sum(inbox[...].astype(F32), axis=0) + momenta[mine, :]
        for d in range(1, NAR):
            link(ybox.at[y], ybox.at[y], y_send.at[d - 1], y_recv.at[d - 1], ys[d]).start()
        for d in range(1, NAR):
            link(ybox.at[y], ybox.at[y], y_send.at[d - 1], y_recv.at[d - 1], ys[d]).wait()
        o_all[mine, :] = (ybox[0] + ybox[1]) + (ybox[2] + ybox[3])

        def tell(i, c):
            pltpu.make_async_remote_copy(
                src_ref=o_all.at[mine], dst_ref=o_all.at[mine], send_sem=ag_send, recv_sem=ag_recv,
                device_id=((g + 2 * i) % GRP, y), device_id_type=MESH,
            ).start()
            return c

        lax.fori_loop(1, GRP // 2, tell, 0)
        got = o_all.at[pl.ds(0, (PIECES // 2 - 1) * PIECE)]
        pltpu.make_async_copy(got, got, ag_recv).wait()

    @pl.when(g >= PIECES)
    def _():
        got = o_all.at[pl.ds(0, PIECES // 2 * PIECE)]
        pltpu.make_async_copy(got, got, ag_recv).wait()

    pairs = o_all.reshape(PIECES // 2, 2, PIECE, 128)
    half = pltpu.make_async_remote_copy(
        src_ref=pairs.at[:, g % 2], dst_ref=pairs.at[:, g % 2], send_sem=pair_send, recv_sem=pair_recv,
        device_id=(g + 1 - 2 * (g % 2), y), device_id_type=MESH,
    )
    half.start()

    @pl.when(g < PIECES)
    def _():
        gone = pay.at[pl.ds(0, (PIECES - 1) * PIECE)]
        pltpu.make_async_copy(gone, gone, rs_send).wait()
        gone = table.at[pl.ds(0, (GRP // 2 - 1) * PIECE)]
        pltpu.make_async_copy(gone, gone, ag_send).wait()

    @pl.when(g >= PIECES)
    def _():
        pltpu.make_async_copy(pay, pay, rs_send).wait()

    for b in range(8):
        blk = gbuf.at[y, b * 256:(b + 1) * 256, :]
        link(blk, blk, h_send.at[0, b], h_recv.at[0, b], right).wait_send()
        link(blk, blk, h_send.at[1, b], h_recv.at[1, b], left).wait_send()
        blk = gbuf.at[opp, b * 256:(b + 1) * 256, :]
        link(blk, blk, h_send.at[2, b], h_recv.at[2, b], right).wait_send()
    swap_sent(rbuf, r_send, r_recv, SEED // 2)
    swap_sent(dbuf, d_send, d_recv, 96)
    half.wait()


def main(reqt, feat, idx1t, msk1t, idx2t, msk2t, labels, live, w1, w2own, m1, m2own, bias):
    vm = pl.BlockSpec(memory_space=pltpu.VMEM)
    dma = pltpu.SemaphoreType.DMA
    sds = jax.ShapeDtypeStruct
    V = pltpu.VMEM
    return pl.pallas_call(
        main_kernel,
        out_shape=sds((ROWS, 128), F32),
        in_specs=[vm, pl.BlockSpec(memory_space=pl.ANY)] + [vm] * 11,
        out_specs=vm,
        scratch_shapes=[
            V((SRC + 8, D_IN), F32),
            V((OWN, D_IN), BF),
            V((SRC, D_IN), BF),
            V((CAP, D_IN), F32),
            V((DEV, 128), jnp.int32),
            V((DEV, 128), jnp.int32),
            V((NAR, GRP, 1, 128), jnp.int32),
            V((16, FRONT), jnp.int32),
            V((256, 128), jnp.int32),
            V((1, FRONT), F32),
            V((256, D_IN), F32),
            V((256, D_IN), F32),
            V((FRONT, HID), F32),
            V((NAR, FRONT, HID), BF),
            V((NAR, 2 * SEED, FRONT), BF),
            V((NAR, FRONT, 2 * SEED), BF),
            V((NAR, 4, 1 + F2, 16, 128), jnp.int16),
            V((SEED, 32), jnp.int32),
            V((256, SRC), BF),
            V((256, 32), jnp.int32),
            V((NAR, SEED, 128), F32),
            V((SEED, 128), F32),
            V((NAR, SEED, HID), BF),
            V((NAR, CLS_PAD, SEED), BF),
            V((NAR, 64, HID), BF),
            V((NAR, CLS_PAD, 128), BF),
            V((ROWS, 128), F32),
            V((NAR, 16, SEED), jnp.int32),
            V((CLS_PAD, 2 * HID), BF),
            V((HID, 128), F32),
            V((ROWS, 128), BF),
            V((32, 128), F32),
            V((GRP, PIECE, 128), BF),
            V((NAR, PIECE, 128), F32),
            pltpu.SMEM((DEV, 1, 128), jnp.int32),
            pltpu.SMEM((256, 128), jnp.int32),
            dma, dma((3,)), dma((GRP,)), dma((NAR,)), dma((NAR,)), dma((GRP,)), dma, dma, dma((3, 3)), dma((3, 3)),
            dma((3, 8)), dma((3, 8)), dma((4,)), dma((4,)), dma((4,)), dma((4,)),
            dma, dma, dma((3,)), dma((3,)), dma, dma, dma, dma,
        ],
        compiler_params=pltpu.CompilerParams(
            collective_id=0, has_side_effects=True, vmem_limit_bytes=62 * 2**20
        ),
    )(reqt, feat, idx1t, msk1t, idx2t, msk2t, labels, live, w1, w2own, m1, m2own, bias)


def update_kernel(
    res, w1own, w2own, bias, biasm, biasv,
    o_loss, o_first, o_second, o_mom1, o_mom2, o_flow, o_slow, o_bias, o_bm, o_bv,
    x1s, x2s,
):
    y = lax.axis_index("nar")
    mom1 = jnp.concatenate([res[0:256, :], res[256:512, :]], axis=1)
    x1s[...] = mom1
    block64 = pl.ds(pl.multiple_of(y * 64, 64), 64)
    o_mom1[...] = x1s[block64, :]
    x1 = mom1 * (1.0 / (jnp.sqrt(jnp.sum(mom1 * mom1, keepdims=True)) + 1e-07))
    mom2 = jnp.concatenate([res[ROW_2 + q * CLS_PAD:ROW_2 + (q + 1) * CLS_PAD, :] for q in range(NAR)], axis=1)
    x2 = mom2 * (1.0 / (jnp.sqrt(jnp.sum(mom2 * mom2, keepdims=True)) + 1e-07))
    for i in range(NS_ITERS):
        x1 = ns_step(x1)
        x2 = ns_step(x2)
    x1s[...] = x1
    for q in range(NAR):
        x2s[q] = x2[:, q * 128:(q + 1) * 128]
    first_new = w1own[...] * (1.0 - WDECAY) - x1s[block64, :]
    o_first[...] = first_new
    o_flow[...] = first_new.astype(BF)
    second = w2own[...] * (1.0 - WDECAY) - (2 * HID / CLS) ** 0.5 * x2s[y][0:CLS, :]
    o_second[...] = second
    o_slow[...] = second.astype(BF)
    o_mom2[...] = res[pl.ds(pl.multiple_of(ROW_2 + y * CLS_PAD, 16), CLS_PAD), :][0:CLS, :]

    gb = res[ROW_MISC + 0:ROW_MISC + 4, :] + res[ROW_MISC + 4:ROW_MISC + 8, :]
    gb = jnp.concatenate([gb[0:1, :], gb[1:2, :], gb[2:3, :], gb[3:4, 0:44]], axis=1)
    m_new = BETA_ONE * biasm[...] + (1.0 - BETA_ONE) * gb
    v_new = BETA_TWO * biasv[...] + (1.0 - BETA_TWO) * gb * gb
    m_hat = m_new / (1.0 - BETA_ONE**STEP)
    v_hat = v_new / (1.0 - BETA_TWO**STEP)
    o_bias[...] = bias[...] * (1.0 - LR_BIAS * WDECAY) - LR_BIAS * m_hat / (jnp.sqrt(v_hat) + EPSILON)
    o_bm[...] = m_new
    o_bv[...] = v_new
    o_loss[...] = res[ROW_MISC + 8:ROW_MISC + 9, 0:1] + res[ROW_MISC + 9:ROW_MISC + 10, 0:1]


def update(*args):
    vm = pl.BlockSpec(memory_space=pltpu.VMEM)
    sds = jax.ShapeDtypeStruct
    return pl.pallas_call(
        update_kernel,
        out_shape=[
            sds((1, 1), F32), sds((64, HID), F32), sds((CLS, 128), F32), sds((64, HID), F32), sds((CLS, 128), F32),
            sds((64, HID), BF), sds((CLS, 128), BF), sds((1, 428), F32), sds((1, 428), F32), sds((1, 428), F32),
        ],
        in_specs=[vm] * 6,
        out_specs=[vm] * 10,
        scratch_shapes=[pltpu.VMEM((2 * D_IN, HID), F32), pltpu.VMEM((NAR, CLS_PAD, 128), F32)],
        compiler_params=pltpu.CompilerParams(vmem_limit_bytes=32 * 2**20),
    )(*args)


def per_device(
    features, requests, index_one, mask_one, index_two, mask_two, labels, seed_live,
    w_first, w_second, mom_first, mom_second, biases, bias_m, bias_v,
):
    w2own, bias = w_second.T, biases[None, :]
    res = main(
        requests.T, features, index_one.T, mask_one.T, index_two.T, mask_two.T, labels[None, :], seed_live[None, :],
        w_first, w2own, mom_first, mom_second.T, bias,
    )
    loss, first_new, second_new, mom_one, mom_two, first_low, second_low, bias_new, m_new, v_new = update(
        res, w_first, w2own, bias, bias_m[None, :], bias_v[None, :]
    )
    return (
        loss.reshape(()), first_new, second_new.T, mom_one, mom_two.T, first_low, second_low.T,
        bias_new.reshape(-1), m_new.reshape(-1), v_new.reshape(-1),
    )


def solution(mesh):
    both = ("grp", "nar")
    placed = (
        P(both, None), P(both, None), P(both, None), P(both, None), P(both, None), P(both, None),
        P(both), P(both), P("nar", None), P("nar", None), P("nar", None), P("nar", None), P(), P(), P(),
    )
    nar = P("nar", None)
    return jax.shard_map(
        per_device, mesh=mesh, in_specs=placed,
        out_specs=(P(), nar, nar, nar, nar, nar, nar, P(), P(), P()), check_vma=False,
    )
```

```python
import functools

import jax
import jax.numpy as jnp
from jax import lax
from jax.experimental import pallas as pl
from jax.experimental.pallas import tpu as pltpu
from jax.sharding import PartitionSpec as P

HID = 256
CLS = 172
CLS_PAD = 176
D_IN = 128
F1 = 15
F2 = 10
NS_ITERS = 5
STEP = 10
LAM = 0.5
MU = 0.95
WDECAY = 0.01
LR_BIAS = 0.05
BETA_ONE = 0.9
BETA_TWO = 0.999
EPSILON = 1e-08
NS_A = 3.4445
NS_B = -4.775
NS_C = 2.0315
HIGH = lax.Precision.HIGHEST
MESH = pl.DeviceIdType.MESH
BF = jnp.bfloat16
F32 = jnp.float32

DEV = 128
NAR = 4
OWN = 8192
CAP = 64
SRC = 8192
FRONT = 2048
SEED = 512


def all_to(t):
    return (t // NAR, t % NAR)


GRP = 32
PIECE = 48
PIECES = 26
ROW_2 = 512
ROW_MISC = ROW_2 + NAR * CLS_PAD
ROWS = PIECES * PIECE
SEEDS_ALL = SEED * DEV


def dot(a, b, dims=((1,), (0,))):
    return lax.dot_general(a, b, (dims, ((), ())), preferred_element_type=F32)


NN = ((1,), (0,))
NT = ((1,), (1,))
TN = ((0,), (0,))


def split(a):
    hi = a.astype(BF)
    return hi, (a - hi.astype(F32)).astype(BF)


def dot3(a, b, dims):
    (ah, al), (bh, bl) = a, b
    return dot(
        jnp.concatenate([ah, ah, al], axis=dims[0][0]), jnp.concatenate([bh, bl, bh], axis=dims[1][0]), dims
    )


def ns_step(x):
    xs = split(x)
    gram = dot3(xs, xs, NT)
    gs = split(gram)
    mix = NS_B * gram + NS_C * dot3(gs, gs, NN)
    return NS_A * x + dot3(split(mix), xs, NN)


def spread(row):
    return jnp.broadcast_to(row, (128, 128)).T


def main_kernel(
    reqt, feat, idx1t, msk1t, idx2t, msk2t, labels, live, w1, w2own, m1, m2own, bias,
    o_all,
    table, featb, pulled, stage, reqv, reqin, mid, idxv, idxp, invv, near, own, slope, gbuf, fsel, bsel, wants, idc, ssel, idm, invc, livec, rbuf, dbuf,
    gw1, gw2t, momenta, gidx2, w2t, b2c, pay, misc, inbox, ybox,
    reqs, idx,
    feat_sem, loc_sem, ask_sem, req_send, mid_recv, req_recv, row_send, row_recv, nar_send, nar_recv,
    h_send, h_recv, r_send, r_recv, d_send, d_recv, rs_send, rs_recv, y_send, y_recv, ag_send, ag_recv, pair_send, pair_recv,
):
    a1t, dh1, tot, gsum = featb, table, table.at[2 * FRONT:3 * FRONT], table.at[3 * FRONT:3 * FRONT + 512]
    g = lax.axis_index("grp")
    y = lax.axis_index("nar")
    me = g * NAR + y
    left, right, opp = (y + 3) % NAR, (y + 1) % NAR, (y + 2) % NAR

    load = pltpu.make_async_copy(feat, featb, feat_sem)
    load.start()

    barrier = pltpu.get_barrier_semaphore()

    ys = [(y + d) % NAR for d in range(NAR)]

    def greet(i, c):
        pl.semaphore_signal(barrier, inc=1, device_id=((g + i) % GRP, y), device_id_type=MESH)
        return c

    for d in range(1, NAR):
        pl.semaphore_signal(barrier, inc=1, device_id=(g, ys[d]), device_id_type=MESH)
    lax.fori_loop(1, GRP, greet, 0)

    def link(src, dst, ssem, rsem, to):
        return pltpu.make_async_remote_copy(
            src_ref=src, dst_ref=dst, send_sem=ssem, recv_sem=rsem, device_id=(g, to), device_id_type=MESH
        )

    reqv[...] = jnp.concatenate([reqt[...], jnp.zeros((DEV - CAP, DEV), jnp.int32)], axis=0).T
    ask_rows = reqv.reshape(GRP, NAR, 1, 128)
    got_rows = reqin.reshape(DEV, 1, 128)

    gw1[y] = w1[...].astype(BF)
    pad = CLS_PAD - CLS
    gw2t[y] = jnp.concatenate([w2own[...], jnp.zeros((pad, 128), F32)], axis=0).astype(BF)
    momenta[...] = jnp.zeros((ROWS, 128), F32)
    for h in range(2):
        momenta[pl.ds(pl.multiple_of(h * 256 + y * 64, 64), 64), :] = MU * m1[:, h * 128:(h + 1) * 128]
    momenta[pl.ds(pl.multiple_of(ROW_2 + y * CLS_PAD, 16), CLS_PAD), :] = jnp.concatenate(
        [MU * m2own[...], jnp.zeros((pad, 128), F32)], axis=0
    )
    gidx2[y] = jnp.concatenate(
        [idx2t[0:1, :], jnp.where(msk2t[...] > 0, idx2t[1:, :], -1), jnp.zeros((5, SEED), jnp.int32)], axis=0
    )
    shared = (gidx2, gw1, gw2t)

    pl.semaphore_wait(barrier, GRP + NAR - 2)

    def ask_group(d):
        return pltpu.make_async_remote_copy(
            src_ref=ask_rows.at[:, ys[d]], dst_ref=mid.at[y], send_sem=req_send.at[d], recv_sem=mid_recv.at[d],
            device_id=(g, ys[d]), device_id_type=MESH,
        )

    for d in range(1, NAR):
        ask_group(d).start()
    keep = pltpu.make_async_copy(ask_rows.at[:, y], mid.at[y], loc_sem.at[2])
    keep.start()
    for n, a in enumerate(shared):
        for d in range(1, NAR):
            link(a.at[y], a.at[y], nar_send.at[n, d - 1], nar_recv.at[n, d - 1], (y + d) % NAR).start()

    msk = msk1t[...]
    idxv[0:1, :] = idx1t[0:1, :]
    idxv[1:16, :] = jnp.where(msk > 0, idx1t[1:16, :], SRC)
    invv[...] = 1.0 / jnp.maximum(jnp.sum(msk.astype(F32), axis=0, keepdims=True), 1.0)
    for half in range(2):
        parts = []
        for r in range(8):
            parts.append(jnp.concatenate(
                [idxv[:, (half * 4 + b) * 256 + r * 32:(half * 4 + b) * 256 + r * 32 + 32] for b in range(4)], axis=1
            ))
        idxp[half * 128:(half + 1) * 128, :] = jnp.concatenate(parts, axis=0).T
    to_smem = [pltpu.make_async_copy(idxp, idx, loc_sem.at[0])]
    for c in to_smem:
        c.start()

    keep.wait()
    for d in range(1, NAR):
        ask_group(d).wait()
    own_rows = pl.ds(pl.multiple_of(g * NAR, NAR), NAR)

    def ask(i, c):
        n = (i * 13) % GRP
        t = (g + n) % GRP
        pltpu.make_async_remote_copy(
            src_ref=mid.at[:, t], dst_ref=got_rows.at[own_rows], send_sem=req_send.at[0], recv_sem=req_recv.at[n],
            device_id=(t, y), device_id_type=MESH,
        ).start()
        return c

    lax.fori_loop(1, GRP, ask, 0)
    keep = pltpu.make_async_copy(mid.at[:, g], got_rows.at[own_rows], loc_sem.at[2])
    keep.start()

    load.wait()

    def widen_features(i, c):
        rows = pl.ds(pl.multiple_of(i * 256, 256), 256)
        table[rows, :] = featb[rows, :].astype(F32)
        return c

    lax.fori_loop(0, OWN // 256, widen_features, 0)

    lane32 = lax.broadcasted_iota(jnp.int32, (16, 128), 1)
    lane16 = lane32.astype(jnp.int16)
    iota16 = lax.broadcasted_iota(jnp.int32, (16, 128), 0).astype(jnp.int16)
    one, zero = jnp.ones((16, 128), BF), jnp.zeros((16, 128), BF)

    def unit(digit):
        v = jnp.ones_like(digit)
        for j in range(1, 8):
            v = jnp.where(digit == j, 1 << 4 * j, v)
        return v

    def count(acc, j):
        return ((acc >> (4 * j)) & 15).astype(F32).astype(BF)

    def keys_units(ids):
        return (ids & 127) + (ids >> 10) * 128, unit((ids >> 7) & 7)

    def word(pos, keys, units):
        acc = jnp.zeros((16, 128), jnp.int32)
        for k, u in zip(keys, units):
            acc = acc + jnp.where(pos == k, u, 0)
        return acc

    def spread_columns(blk, ks):
        return [jnp.broadcast_to(blk[:, k:k + 1], (16, 128)) for k in ks]

    ids = gidx2[y]
    keys, units = keys_units(ids)
    idc[...] = jnp.concatenate([ids[0:1, :], keys[1:, :], units], axis=0).T

    def seeds16(i):
        at = pl.multiple_of(i * 16, 16)
        blk = idc[pl.ds(at, 16), :]
        self_row = jnp.broadcast_to(blk[:, 0:1], (16, 128)).astype(jnp.int16)
        return at, (spread_columns(blk, range(1, 1 + F2)), spread_columns(blk, range(17, 17 + F2)), self_row)

    def forward_marks(at, want, q):
        keys, units, self_row = want
        for w in range(2):
            acc = word(lane32 + 128 * (2 * q + w), keys, units)
            for j in range(8):
                c = w * 8 + j
                fsel[q, pl.ds(at, 16), c * 128:(c + 1) * 128] = count(acc, j)
                here = lane16 + jnp.full((16, 128), q * FRONT + c * 128, jnp.int32).astype(jnp.int16)
                fsel[q, pl.ds(SEED + at, 16), c * 128:(c + 1) * 128] = jnp.where(here == self_row, one, zero)

    view = table.reshape(SRC + 8, 1, D_IN)
    my_rows = pl.ds(pl.multiple_of(me * CAP, CAP), CAP)

    def pick(t, u, slot):
        for half in range(0, CAP, 32):
            rows = [view[reqs[t * NAR + u, 0, half + r]] for r in range(32)]
            for r in range(32):
                stage[half + r:half + r + 1, :] = rows[r]
        featb[slot, :] = stage[...].astype(BF)

    def serve_one(t, u, slot):
        pick(t, u, slot)
        pltpu.make_async_remote_copy(
            src_ref=featb.at[slot], dst_ref=pulled.at[my_rows],
            send_sem=row_send, recv_sem=row_recv, device_id=(t, u), device_id_type=MESH,
        ).start()

    def asked(n):
        rows = got_rows.at[pl.ds(0, NAR)]
        pltpu.make_async_copy(rows, rows, req_recv.at[n]).wait()

    def to_scalars(t, n):
        rows = pl.ds(pl.multiple_of(t * NAR, NAR), NAR)
        return pltpu.make_async_copy(got_rows.at[rows], reqs.at[rows], ask_sem.at[n])

    def whose(i):
        n = (i * 13) % GRP
        return n, (g + GRP - n) % GRP

    def fetch(i):
        n, t = whose(i)
        asked(n)
        to_scalars(t, n).start()

    def serve(i, c):
        n, t = whose(i)

        @pl.when(i < GRP - 1)
        def _():
            fetch(i + 1)

        to_scalars(t, n).wait()
        at, want = seeds16(i)
        for d in range(NAR):
            forward_marks(at, want, d)
            serve_one(t, ys[d], pl.ds(pl.multiple_of((i * NAR + d) * CAP, CAP), CAP))
        return c

    fetch(1)
    lax.fori_loop(1, GRP, serve, 0)
    keep.wait()
    to_scalars(g, 0).start()
    to_scalars(g, 0).wait()
    at, want = seeds16(0)
    for d in range(NAR):
        forward_marks(at, want, d)
    for d in range(1, NAR):
        serve_one(g, ys[d], pl.ds(d * CAP, CAP))
    pick(g, y, pl.ds(0, CAP))
    pulled[my_rows, :] = featb[0:CAP, :]

    for n, a in enumerate(shared):
        for d in range(1, NAR):
            link(a.at[y], a.at[y], nar_send.at[n, d - 1], nar_recv.at[n, d - 1], (y + d) % NAR).wait()
    for q in range(NAR):
        w2t[:, q * 128:(q + 1) * 128] = gw2t[q]
    last = jnp.concatenate([bias[0:1, 384:428], jnp.zeros((1, 84), F32)], axis=1)
    b2c[...] = jnp.concatenate([spread(bias[0:1, 256:384]), spread(last)], axis=0)

    def column(row):
        return jnp.concatenate([spread(row[:, c * 128:(c + 1) * 128]) for c in range(SEED // 128)], axis=0)

    for q in range(NAR):
        n = jnp.sum((gidx2[q, 1:1 + F2, :] >= 0).astype(F32), axis=0, keepdims=True)
        invc[q] = column(1.0 / jnp.maximum(n, 1.0))
    livec[...] = column(2.0 * LAM / HID / SEEDS_ALL * live[...].astype(F32))

    for q in range(NAR):
        ids = gidx2[q] - y * FRONT
        for c in range(SEED // 128):
            for k in range(1 + F2):
                row = ids[k:k + 1, c * 128:(c + 1) * 128]
                wants[q, c, k] = jnp.broadcast_to(row, (16, 128)).astype(jnp.int16)

    def backward_marks(i):
        here = iota16 + jnp.full((16, 128), i * 16, jnp.int32).astype(jnp.int16)
        out = pl.ds(pl.multiple_of(i * 16, 16), 16)
        for q in range(NAR):
            for c in range(SEED // 128):
                acc = jnp.where(here == wants[q, c, 1], one, zero)
                for k in range(2, 1 + F2):
                    acc = acc + jnp.where(here == wants[q, c, k], one, zero)
                bsel[q, out, c * 128:(c + 1) * 128] = acc
                bsel[q, out, SEED + c * 128:SEED + (c + 1) * 128] = jnp.where(here == wants[q, c, 0], one, zero)

    def some_marks(i, c):
        backward_marks(i)
        return c

    def sum_marks(i):
        at = pl.multiple_of(i // 2 * 16, 16)
        half = i % 2
        blk = idm[pl.ds(at, 16), :]
        keys, units = spread_columns(blk, range(1, 1 + F1)), spread_columns(blk, range(17, 17 + F1))
        for w in range(4):
            acc = word(lane32 + (half * 4 + w) * 128, keys, units)
            for j in range(8):
                col = pl.ds(pl.multiple_of(half * (SRC // 2) + (w * 8 + j) * 128, 128), 128)
                ssel[pl.ds(at, 16), col] = count(acc, j)

    def sum_ids(b):
        idm[...] = jnp.concatenate(keys_units(idxv[:, cols(b)]), axis=0).T

    def cols(b):
        return pl.ds(pl.multiple_of(b * 256, 256), 256)

    def one_mark(i, c):
        sum_marks(i)
        return c

    sum_ids(0)
    lax.fori_loop(0, 32, one_mark, 0)
    lax.fori_loop(0, 16, some_marks, 0)

    come = pulled.at[pl.ds(0, (DEV - 1) * CAP)]
    pltpu.make_async_copy(come, come, row_recv).wait()
    gone = featb.at[pl.ds(CAP, (DEV - 1) * CAP)]
    pltpu.make_async_copy(gone, gone, row_send).wait()
    sent = mid.at[:, pl.ds(0, GRP - 1)]
    pltpu.make_async_copy(sent, sent, req_send.at[0]).wait()

    def widen(i, c):
        rows = pl.ds(pl.multiple_of(i * 256, 256), 256)
        table[rows, :] = pulled[rows, :].astype(F32)
        return c

    lax.fori_loop(0, SRC // 256, widen, 0)
    table[SRC:SRC + 8, :] = jnp.zeros((8, D_IN), F32)
    for c in to_smem:
        c.wait()

    def forward(b):
        @pl.when(b % 2 == 0)
        def _():
            blk = gbuf.at[left, cols(b), :]
            link(blk, blk, h_send.at[0, b], h_recv.at[0, b], right).wait_recv()
            link(blk, blk, h_send.at[2, b], h_recv.at[2, b], right).start()

        @pl.when(b % 2 == 1)
        def _():
            blk = gbuf.at[right, cols(b), :]
            link(blk, blk, h_send.at[1, b], h_recv.at[1, b], left).wait_recv()
            link(blk, blk, h_send.at[2, b], h_recv.at[2, b], left).start()

    def load_sums(b):
        def some(i, c):
            backward_marks(b * 16 + i)
            found = []
            for e in range(2):
                line = b * 32 + 2 * i + e
                for r in range(8):
                    self_row = view[idx[line, r * 16]]
                    rows = [view[idx[line, r * 16 + 1 + k]] for k in range(F1)]
                    while len(rows) > 1:
                        rows = [p + q for p, q in zip(rows[::2], rows[1::2])] + ([rows[-1]] if len(rows) % 2 else [])
                    found.append((r * 32 + 2 * i + e, self_row, rows[0]))
            for at, self_row, total in found:
                own[pl.ds(at, 1), :] = self_row
                near[pl.ds(at, 1), :] = total
            return c

        lax.fori_loop(0, 16, some, 0)
        finish(b)

    def multiply_sums(b):
        def some(i, c):
            found = []
            for e in range(2):
                for r in range(8):
                    found.append((r * 32 + 2 * i + e, view[idx[b * 32 + 2 * i + e, r * 16]]))
            for at, self_row in found:
                own[pl.ds(at, 1), :] = self_row
            return c

        lax.fori_loop(0, 16, some, 0)
        near[...] = dot(ssel[...], pulled[...])
        finish(b)

    def finish(b):
        rows = cols(b)
        scale = jnp.concatenate(
            [spread(invv[0:1, pl.ds(pl.multiple_of(b * 256 + c * 128, 128), 128)]) for c in range(2)], axis=0
        )
        act = jnp.concatenate([own[...].astype(BF), (near[...] * scale).astype(BF)], axis=1)
        a1 = act.T
        for h in range(2):
            a1t[pl.ds(pl.multiple_of((2 * b + h) * 256, 256), 256), :] = a1[:, h * 128:(h + 1) * 128]
        z = dot(act, gw1[...].reshape(2 * D_IN, HID)) + bias[0:1, 0:HID]
        sig = 1.0 / (1.0 + jnp.exp(-z))
        h1 = z * sig
        slope[rows, :] = sig + h1 * (1.0 - sig)
        gbuf[y, rows, :] = h1.astype(BF)
        blk = gbuf.at[y, rows, :]
        link(blk, blk, h_send.at[0, b], h_recv.at[0, b], right).start()
        link(blk, blk, h_send.at[1, b], h_recv.at[1, b], left).start()

        @pl.when(b > 0)
        def _():
            forward(b - 1)

    def loaded(b, c):
        load_sums(b)
        return c

    multiply_sums(0)
    lax.fori_loop(1, 8, loaded, 0)
    forward(7)

    def from_source(q, fresh=False):
        def rows512(i, c):
            part = dot(fsel[q, pl.ds(pl.multiple_of(i * SEED, SEED), SEED), :], gbuf[q])
            for h in range(2):
                rows = pl.ds(pl.multiple_of(h * 2 * SEED + i * SEED, SEED), SEED)
                now = part[:, h * 128:(h + 1) * 128]
                tot[rows, :] = now if fresh else tot[rows, :] + now
            return c

        lax.fori_loop(0, 2, rows512, 0)

    from_source(y, True)
    for b in range(1, 8, 2):
        blk = gbuf.at[left, b * 256:(b + 1) * 256, :]
        link(blk, blk, h_send.at[0, b], h_recv.at[0, b], right).wait_recv()
    from_source(left)
    for b in range(0, 8, 2):
        blk = gbuf.at[right, b * 256:(b + 1) * 256, :]
        link(blk, blk, h_send.at[1, b], h_recv.at[1, b], left).wait_recv()
    from_source(right)
    for b in range(8):
        blk = gbuf.at[opp, b * 256:(b + 1) * 256, :]
        link(blk, blk, h_send.at[2, b], h_recv.at[2, b], right).wait_recv()
    from_source(opp)

    def wide(a):
        return jnp.concatenate([a, a], axis=1)

    def seeds(first):
        return jnp.concatenate([tot[h * 2 * SEED + first:h * 2 * SEED + first + SEED, :] for h in range(2)], axis=1)

    near2 = (seeds(0) * wide(invc[y])).astype(BF)
    self2 = seeds(SEED).astype(BF)
    alive = live[...].astype(F32)
    diff = self2.astype(F32) - near2.astype(F32)
    pull_apart = wide(livec[...]) * diff

    def swap_start(buf, ssem, rsem):
        blk = buf.at[y]
        link(blk, blk, ssem.at[0], rsem.at[0], right).start()
        link(blk, blk, ssem.at[1], rsem.at[1], left).start()

    def swap_forward(buf, ssem, rsem, cut):
        blk = buf.at[left]
        link(blk, blk, ssem.at[0], rsem.at[0], right).wait_recv()
        half = buf.at[left, 0:cut, :]
        link(half, half, ssem.at[2], rsem.at[2], right).start()
        blk = buf.at[right]
        link(blk, blk, ssem.at[1], rsem.at[1], left).wait_recv()
        half = buf.at[right, cut:, :]
        link(half, half, ssem.at[3], rsem.at[3], left).start()

    def swap_end(buf, ssem, rsem, cut):
        half = buf.at[opp, 0:cut, :]
        link(half, half, ssem.at[2], rsem.at[2], right).wait_recv()
        half = buf.at[opp, cut:, :]
        link(half, half, ssem.at[3], rsem.at[3], left).wait_recv()

    def swap_sent(buf, ssem, rsem, cut):
        blk = buf.at[y]
        link(blk, blk, ssem.at[0], rsem.at[0], right).wait_send()
        link(blk, blk, ssem.at[1], rsem.at[1], left).wait_send()
        half = buf.at[left, 0:cut, :]
        link(half, half, ssem.at[2], rsem.at[2], right).wait_send()
        half = buf.at[right, cut:, :]
        link(half, half, ssem.at[3], rsem.at[3], left).wait_send()

    rbuf[y] = pull_apart.astype(BF)
    swap_start(rbuf, r_send, r_recv)

    act2 = jnp.concatenate([self2, near2], axis=1)
    cls = lax.broadcasted_iota(jnp.int32, (CLS_PAD, SEED), 0)
    b2 = b2c[0:CLS_PAD, :]
    logits = dot(w2t[...], act2, NT) + jnp.concatenate([b2] * 4, axis=1)
    logits = jnp.where(cls < CLS, logits, -1e30)
    top = jnp.max(logits, axis=0, keepdims=True)
    e = jnp.exp(logits - top)
    tot = jnp.sum(e, axis=0, keepdims=True)
    hot = cls == labels[...]
    picked = jnp.sum(jnp.where(hot, logits, 0.0), axis=0, keepdims=True)
    dlog = (alive * (e * (1.0 / tot) - jnp.where(hot, 1.0, 0.0)) * (1.0 / SEEDS_ALL)).astype(BF)
    dbuf[y] = dlog
    swap_start(dbuf, d_send, d_recv)

    loss = jnp.sum(alive * (top + jnp.log(tot) - picked), axis=1, keepdims=True)
    loss = loss + SEEDS_ALL / 2 * jnp.sum(pull_apart * diff, keepdims=True)
    g2t = dot(dlog, act2).astype(BF)
    for q in range(NAR):
        pay[ROW_2 + q * CLS_PAD:ROW_2 + (q + 1) * CLS_PAD, :] = g2t[:, q * 128:(q + 1) * 128]

    def to_owners(first, last):
        def one_owner(t, c):
            @pl.when(t != g)
            def _():
                pltpu.make_async_remote_copy(
                    src_ref=pay.at[pl.ds(pl.multiple_of(t * PIECE, 16), PIECE)], dst_ref=inbox.at[g],
                    send_sem=rs_send, recv_sem=rs_recv, device_id=(t, y), device_id_type=MESH,
                ).start()

            return c

        def turned(i, c):
            return one_owner(first + (i + g) % (last - first), c)

        lax.fori_loop(0, last - first, turned, 0)

    early, late = -(-ROW_2 // PIECE), ROW_MISC // PIECE
    to_owners(early, late)

    def add_grads(q, fresh=False):
        da = dot(dbuf[q], w2t[...], TN)
        r = rbuf[q].astype(F32)
        ds = (da[:, :HID] + r).astype(BF)
        dn = ((da[:, HID:] - r) * wide(invc[q])).astype(BF)
        both = jnp.concatenate([dn, ds], axis=0)

        def rows512(i, c):
            part = dot(bsel[q, pl.ds(pl.multiple_of(i * 512, 512), 512), :], both)
            for h in range(2):
                rows = pl.ds(pl.multiple_of(h * FRONT + i * 512, 512), 512)
                now = part[:, h * 128:(h + 1) * 128]
                dh1[rows, :] = now if fresh else dh1[rows, :] + now
            return c

        lax.fori_loop(0, FRONT // 512, rows512, 0)

    db2 = jnp.sum(dlog.astype(F32), axis=1, keepdims=True)
    db2 = jnp.broadcast_to(db2, (CLS_PAD, 128)).T[0:1, :]
    swap_forward(rbuf, r_send, r_recv, SEED // 2)
    add_grads(y, True)
    swap_forward(dbuf, d_send, d_recv, 96)
    add_grads(left)
    add_grads(right)
    swap_end(rbuf, r_send, r_recv, SEED // 2)
    swap_end(dbuf, d_send, d_recv, 96)
    add_grads(opp)

    def to_z(b, db):
        rows = pl.ds(pl.multiple_of(b * 256, 256), 256)
        dh = jnp.concatenate(
            [dh1[pl.ds(pl.multiple_of(h * FRONT + b * 256, 256), 256), :] for h in range(2)], axis=1
        )
        dz = (dh * slope[rows, :]).astype(BF)
        a1 = jnp.concatenate(
            [a1t[pl.ds(pl.multiple_of((2 * b + h) * 256, 256), 256), :] for h in range(2)], axis=1
        )
        part = dot(a1, dz)
        for h in range(2):
            now = slice(h * 256, (h + 1) * 256)
            gsum[now, :] = gsum[now, :] + part[:, h * 128:(h + 1) * 128]
        return db + jnp.sum(dz.astype(F32), axis=0, keepdims=True)

    gsum[...] = jnp.zeros((512, 128), F32)
    db1 = lax.fori_loop(0, FRONT // 256, to_z, jnp.zeros((1, HID), F32))
    pay[0:512, :] = gsum[...].astype(BF)
    misc[...] = jnp.zeros((32, 128), F32)

    def two(rows, v):
        hi = v.astype(BF).astype(F32)
        misc[rows:rows + 1, 0:v.shape[1]] = hi
        misc[rows + 4:rows + 5, 0:v.shape[1]] = v - hi

    two(0, db1[:, :128])
    two(1, db1[:, 128:])
    two(2, db2[:, :128])
    two(3, db2[:, 128:])
    hi = loss.astype(BF).astype(F32)
    misc[8:9, 0:1] = hi
    misc[9:10, 0:1] = loss - hi
    pay[ROW_MISC:ROWS, :] = misc[...].astype(BF)

    to_owners(0, early)
    to_owners(late, PIECES)
    mine = pl.ds(pl.multiple_of(g * PIECE, 16), PIECE)

    @pl.when(g < PIECES)
    def _():
        got = inbox.at[pl.ds(0, GRP - 1)]
        pltpu.make_async_copy(got, got, rs_recv).wait()
        inbox[g] = pay[mine, :]
        ybox[y] = jnp.sum(inbox[...].astype(F32), axis=0) + momenta[mine, :]
        for d in range(1, NAR):
            link(ybox.at[y], ybox.at[y], y_send.at[d - 1], y_recv.at[d - 1], ys[d]).start()
        for d in range(1, NAR):
            link(ybox.at[y], ybox.at[y], y_send.at[d - 1], y_recv.at[d - 1], ys[d]).wait()
        o_all[mine, :] = (ybox[0] + ybox[1]) + (ybox[2] + ybox[3])

        def tell(i, c):
            pltpu.make_async_remote_copy(
                src_ref=o_all.at[mine], dst_ref=o_all.at[mine], send_sem=ag_send, recv_sem=ag_recv,
                device_id=((g + 2 * i) % GRP, y), device_id_type=MESH,
            ).start()
            return c

        lax.fori_loop(1, GRP // 2, tell, 0)
        got = o_all.at[pl.ds(0, (PIECES // 2 - 1) * PIECE)]
        pltpu.make_async_copy(got, got, ag_recv).wait()

    @pl.when(g >= PIECES)
    def _():
        got = o_all.at[pl.ds(0, PIECES // 2 * PIECE)]
        pltpu.make_async_copy(got, got, ag_recv).wait()

    pairs = o_all.reshape(PIECES // 2, 2, PIECE, 128)
    half = pltpu.make_async_remote_copy(
        src_ref=pairs.at[:, g % 2], dst_ref=pairs.at[:, g % 2], send_sem=pair_send, recv_sem=pair_recv,
        device_id=(g + 1 - 2 * (g % 2), y), device_id_type=MESH,
    )
    half.start()

    @pl.when(g < PIECES)
    def _():
        gone = pay.at[pl.ds(0, (PIECES - 1) * PIECE)]
        pltpu.make_async_copy(gone, gone, rs_send).wait()
        gone = table.at[pl.ds(0, (GRP // 2 - 1) * PIECE)]
        pltpu.make_async_copy(gone, gone, ag_send).wait()

    @pl.when(g >= PIECES)
    def _():
        pltpu.make_async_copy(pay, pay, rs_send).wait()

    for b in range(8):
        blk = gbuf.at[y, b * 256:(b + 1) * 256, :]
        link(blk, blk, h_send.at[0, b], h_recv.at[0, b], right).wait_send()
        link(blk, blk, h_send.at[1, b], h_recv.at[1, b], left).wait_send()
        blk = gbuf.at[opp, b * 256:(b + 1) * 256, :]
        link(blk, blk, h_send.at[2, b], h_recv.at[2, b], right).wait_send()
    swap_sent(rbuf, r_send, r_recv, SEED // 2)
    swap_sent(dbuf, d_send, d_recv, 96)
    half.wait()


def main(reqt, feat, idx1t, msk1t, idx2t, msk2t, labels, live, w1, w2own, m1, m2own, bias):
    vm = pl.BlockSpec(memory_space=pltpu.VMEM)
    dma = pltpu.SemaphoreType.DMA
    sds = jax.ShapeDtypeStruct
    V = pltpu.VMEM
    return pl.pallas_call(
        main_kernel,
        out_shape=sds((ROWS, 128), F32),
        in_specs=[vm, pl.BlockSpec(memory_space=pl.ANY)] + [vm] * 11,
        out_specs=vm,
        scratch_shapes=[
            V((SRC + 8, D_IN), F32),
            V((OWN, D_IN), BF),
            V((SRC, D_IN), BF),
            V((CAP, D_IN), F32),
            V((DEV, 128), jnp.int32),
            V((DEV, 128), jnp.int32),
            V((NAR, GRP, 1, 128), jnp.int32),
            V((16, FRONT), jnp.int32),
            V((256, 128), jnp.int32),
            V((1, FRONT), F32),
            V((256, D_IN), F32),
            V((256, D_IN), F32),
            V((FRONT, HID), F32),
            V((NAR, FRONT, HID), BF),
            V((NAR, 2 * SEED, FRONT), BF),
            V((NAR, FRONT, 2 * SEED), BF),
            V((NAR, 4, 1 + F2, 16, 128), jnp.int16),
            V((SEED, 32), jnp.int32),
            V((256, SRC), BF),
            V((256, 32), jnp.int32),
            V((NAR, SEED, 128), F32),
            V((SEED, 128), F32),
            V((NAR, SEED, HID), BF),
            V((NAR, CLS_PAD, SEED), BF),
            V((NAR, 64, HID), BF),
            V((NAR, CLS_PAD, 128), BF),
            V((ROWS, 128), F32),
            V((NAR, 16, SEED), jnp.int32),
            V((CLS_PAD, 2 * HID), BF),
            V((HID, 128), F32),
            V((ROWS, 128), BF),
            V((32, 128), F32),
            V((GRP, PIECE, 128), BF),
            V((NAR, PIECE, 128), F32),
            pltpu.SMEM((DEV, 1, 128), jnp.int32),
            pltpu.SMEM((256, 128), jnp.int32),
            dma, dma((3,)), dma((GRP,)), dma((NAR,)), dma((NAR,)), dma((GRP,)), dma, dma, dma((3, 3)), dma((3, 3)),
            dma((3, 8)), dma((3, 8)), dma((4,)), dma((4,)), dma((4,)), dma((4,)),
            dma, dma, dma((3,)), dma((3,)), dma, dma, dma, dma,
        ],
        compiler_params=pltpu.CompilerParams(
            collective_id=0, has_side_effects=True, vmem_limit_bytes=62 * 2**20
        ),
    )(reqt, feat, idx1t, msk1t, idx2t, msk2t, labels, live, w1, w2own, m1, m2own, bias)


def update_kernel(
    res, w1own, w2own, bias, biasm, biasv,
    o_loss, o_first, o_second, o_mom1, o_mom2, o_flow, o_slow, o_bias, o_bm, o_bv,
    x1s, x2s,
):
    y = lax.axis_index("nar")
    mom1 = jnp.concatenate([res[0:256, :], res[256:512, :]], axis=1)
    x1s[...] = mom1
    block64 = pl.ds(pl.multiple_of(y * 64, 64), 64)
    o_mom1[...] = x1s[block64, :]
    x1 = mom1 * (1.0 / (jnp.sqrt(jnp.sum(mom1 * mom1, keepdims=True)) + 1e-07))
    mom2 = jnp.concatenate([res[ROW_2 + q * CLS_PAD:ROW_2 + (q + 1) * CLS_PAD, :] for q in range(NAR)], axis=1)
    x2 = mom2 * (1.0 / (jnp.sqrt(jnp.sum(mom2 * mom2, keepdims=True)) + 1e-07))
    for i in range(NS_ITERS):
        x1 = ns_step(x1)
        x2 = ns_step(x2)
    x1s[...] = x1
    for q in range(NAR):
        x2s[q] = x2[:, q * 128:(q + 1) * 128]
    first_new = w1own[...] * (1.0 - WDECAY) - x1s[block64, :]
    o_first[...] = first_new
    o_flow[...] = first_new.astype(BF)
    second = w2own[...] * (1.0 - WDECAY) - (2 * HID / CLS) ** 0.5 * x2s[y][0:CLS, :]
    o_second[...] = second
    o_slow[...] = second.astype(BF)
    o_mom2[...] = res[pl.ds(pl.multiple_of(ROW_2 + y * CLS_PAD, 16), CLS_PAD), :][0:CLS, :]

    gb = res[ROW_MISC + 0:ROW_MISC + 4, :] + res[ROW_MISC + 4:ROW_MISC + 8, :]
    gb = jnp.concatenate([gb[0:1, :], gb[1:2, :], gb[2:3, :], gb[3:4, 0:44]], axis=1)
    m_new = BETA_ONE * biasm[...] + (1.0 - BETA_ONE) * gb
    v_new = BETA_TWO * biasv[...] + (1.0 - BETA_TWO) * gb * gb
    m_hat = m_new / (1.0 - BETA_ONE**STEP)
    v_hat = v_new / (1.0 - BETA_TWO**STEP)
    o_bias[...] = bias[...] * (1.0 - LR_BIAS * WDECAY) - LR_BIAS * m_hat / (jnp.sqrt(v_hat) + EPSILON)
    o_bm[...] = m_new
    o_bv[...] = v_new
    o_loss[...] = res[ROW_MISC + 8:ROW_MISC + 9, 0:1] + res[ROW_MISC + 9:ROW_MISC + 10, 0:1]


def update(*args):
    vm = pl.BlockSpec(memory_space=pltpu.VMEM)
    sds = jax.ShapeDtypeStruct
    return pl.pallas_call(
        update_kernel,
        out_shape=[
            sds((1, 1), F32), sds((64, HID), F32), sds((CLS, 128), F32), sds((64, HID), F32), sds((CLS, 128), F32),
            sds((64, HID), BF), sds((CLS, 128), BF), sds((1, 428), F32), sds((1, 428), F32), sds((1, 428), F32),
        ],
        in_specs=[vm] * 6,
        out_specs=[vm] * 10,
        scratch_shapes=[pltpu.VMEM((2 * D_IN, HID), F32), pltpu.VMEM((NAR, CLS_PAD, 128), F32)],
        compiler_params=pltpu.CompilerParams(vmem_limit_bytes=32 * 2**20),
    )(*args)


def per_device(
    features, requests, index_one, mask_one, index_two, mask_two, labels, seed_live,
    w_first, w_second, mom_first, mom_second, biases, bias_m, bias_v,
):
    w2own, bias = w_second.T, biases[None, :]
    res = main(
        requests.T, features, index_one.T, mask_one.T, index_two.T, mask_two.T, labels[None, :], seed_live[None, :],
        w_first, w2own, mom_first, mom_second.T, bias,
    )
    loss, first_new, second_new, mom_one, mom_two, first_low, second_low, bias_new, m_new, v_new = update(
        res, w_first, w2own, bias, bias_m[None, :], bias_v[None, :]
    )
    return (
        loss.reshape(()), first_new, second_new.T, mom_one, mom_two.T, first_low, second_low.T,
        bias_new.reshape(-1), m_new.reshape(-1), v_new.reshape(-1),
    )


def solution(mesh):
    both = ("grp", "nar")
    placed = (
        P(both, None), P(both, None), P(both, None), P(both, None), P(both, None), P(both, None),
        P(both), P(both), P("nar", None), P("nar", None), P("nar", None), P("nar", None), P(), P(), P(),
    )
    nar = P("nar", None)
    return jax.shard_map(
        per_device, mesh=mesh, in_specs=placed,
        out_specs=(P(), nar, nar, nar, nar, nar, nar, P(), P(), P()), check_vma=False,
    )
```

```python
import functools

import jax
import jax.numpy as jnp
from jax import lax
from jax.experimental import pallas as pl
from jax.experimental.pallas import tpu as pltpu
from jax.sharding import PartitionSpec as P

HID = 256
CLS = 172
CLS_PAD = 176
D_IN = 128
F1 = 15
F2 = 10
NS_ITERS = 5
STEP = 10
LAM = 0.5
MU = 0.95
WDECAY = 0.01
LR_BIAS = 0.05
BETA_ONE = 0.9
BETA_TWO = 0.999
EPSILON = 1e-08
NS_A = 3.4445
NS_B = -4.775
NS_C = 2.0315
HIGH = lax.Precision.HIGHEST
MESH = pl.DeviceIdType.MESH
BF = jnp.bfloat16
F32 = jnp.float32

DEV = 128
NAR = 4
OWN = 8192
CAP = 64
SRC = 8192
FRONT = 2048
SEED = 512


def all_to(t):
    return (t // NAR, t % NAR)


GRP = 32
PIECE = 48
PIECES = 26
ROW_2 = 512
ROW_MISC = ROW_2 + NAR * CLS_PAD
ROWS = PIECES * PIECE
SEEDS_ALL = SEED * DEV


def dot(a, b, dims=((1,), (0,))):
    return lax.dot_general(a, b, (dims, ((), ())), preferred_element_type=F32)


NN = ((1,), (0,))
NT = ((1,), (1,))
TN = ((0,), (0,))


def split(a):
    hi = a.astype(BF)
    return hi, (a - hi.astype(F32)).astype(BF)


def dot3(a, b, dims):
    (ah, al), (bh, bl) = a, b
    return dot(
        jnp.concatenate([ah, ah, al], axis=dims[0][0]), jnp.concatenate([bh, bl, bh], axis=dims[1][0]), dims
    )


def ns_step(x):
    xs = split(x)
    gram = dot3(xs, xs, NT)
    gs = split(gram)
    mix = NS_B * gram + NS_C * dot3(gs, gs, NN)
    return NS_A * x + dot3(split(mix), xs, NN)


def spread(row):
    return jnp.broadcast_to(row, (128, 128)).T


def main_kernel(
    reqt, feat, idx1t, msk1t, idx2t, msk2t, labels, live, w1, w2own, m1, m2own, bias,
    o_all,
    table, featb, pulled, stage, reqv, reqin, mid, idxv, idxp, invv, scale, near, own, slope, gbuf, fsel, bsel, wants, idc, ssel, idm, invc, livec, rbuf, dbuf,
    gw1, gw2t, momenta, gidx2, w2t, b2c, pay, misc, inbox, ybox,
    reqs, idx,
    feat_sem, loc_sem, ask_sem, req_send, mid_recv, req_recv, row_send, row_recv, nar_send, nar_recv,
    h_send, h_recv, r_send, r_recv, d_send, d_recv, rs_send, rs_recv, y_send, y_recv, ag_send, ag_recv, pair_send, pair_recv,
):
    a1t, dh1, tot, gsum = featb, table, table.at[2 * FRONT:3 * FRONT], table.at[3 * FRONT:3 * FRONT + 512]
    g = lax.axis_index("grp")
    y = lax.axis_index("nar")
    me = g * NAR + y
    left, right, opp = (y + 3) % NAR, (y + 1) % NAR, (y + 2) % NAR

    load = pltpu.make_async_copy(feat, featb, feat_sem)
    load.start()

    barrier = pltpu.get_barrier_semaphore()

    ys = [(y + d) % NAR for d in range(NAR)]

    def greet(i, c):
        pl.semaphore_signal(barrier, inc=1, device_id=((g + i) % GRP, y), device_id_type=MESH)
        return c

    for d in range(1, NAR):
        pl.semaphore_signal(barrier, inc=1, device_id=(g, ys[d]), device_id_type=MESH)
    lax.fori_loop(1, GRP, greet, 0)

    def link(src, dst, ssem, rsem, to):
        return pltpu.make_async_remote_copy(
            src_ref=src, dst_ref=dst, send_sem=ssem, recv_sem=rsem, device_id=(g, to), device_id_type=MESH
        )

    reqv[...] = jnp.concatenate([reqt[...], jnp.zeros((DEV - CAP, DEV), jnp.int32)], axis=0).T
    ask_rows = reqv.reshape(GRP, NAR, 1, 128)
    got_rows = reqin.reshape(DEV, 1, 128)

    gw1[y] = w1[...].astype(BF)
    pad = CLS_PAD - CLS
    gw2t[y] = jnp.concatenate([w2own[...], jnp.zeros((pad, 128), F32)], axis=0).astype(BF)
    momenta[...] = jnp.zeros((ROWS, 128), F32)
    for h in range(2):
        momenta[pl.ds(pl.multiple_of(h * 256 + y * 64, 64), 64), :] = MU * m1[:, h * 128:(h + 1) * 128]
    momenta[pl.ds(pl.multiple_of(ROW_2 + y * CLS_PAD, 16), CLS_PAD), :] = jnp.concatenate(
        [MU * m2own[...], jnp.zeros((pad, 128), F32)], axis=0
    )
    gidx2[y] = jnp.concatenate(
        [idx2t[0:1, :], jnp.where(msk2t[...] > 0, idx2t[1:, :], -1), jnp.zeros((5, SEED), jnp.int32)], axis=0
    )
    shared = (gidx2, gw1, gw2t)

    pl.semaphore_wait(barrier, GRP + NAR - 2)

    def ask_group(d):
        return pltpu.make_async_remote_copy(
            src_ref=ask_rows.at[:, ys[d]], dst_ref=mid.at[y], send_sem=req_send.at[d], recv_sem=mid_recv.at[d],
            device_id=(g, ys[d]), device_id_type=MESH,
        )

    for d in range(1, NAR):
        ask_group(d).start()
    keep = pltpu.make_async_copy(ask_rows.at[:, y], mid.at[y], loc_sem.at[2])
    keep.start()
    for n, a in enumerate(shared):
        for d in range(1, NAR):
            link(a.at[y], a.at[y], nar_send.at[n, d - 1], nar_recv.at[n, d - 1], (y + d) % NAR).start()

    msk = msk1t[...]
    idxv[0:1, :] = idx1t[0:1, :]
    idxv[1:16, :] = jnp.where(msk > 0, idx1t[1:16, :], SRC)
    invv[...] = 1.0 / jnp.maximum(jnp.sum(msk.astype(F32), axis=0, keepdims=True), 1.0)
    for half in range(2):
        parts = []
        for r in range(8):
            parts.append(jnp.concatenate(
                [idxv[:, (half * 4 + b) * 256 + r * 32:(half * 4 + b) * 256 + r * 32 + 32] for b in range(4)], axis=1
            ))
        idxp[half * 128:(half + 1) * 128, :] = jnp.concatenate(parts, axis=0).T
    to_smem = [pltpu.make_async_copy(idxp, idx, loc_sem.at[0])]
    for c in to_smem:
        c.start()

    keep.wait()
    for d in range(1, NAR):
        ask_group(d).wait()
    own_rows = pl.ds(pl.multiple_of(g * NAR, NAR), NAR)

    def ask(i, c):
        n = (i * 13) % GRP
        t = (g + n) % GRP
        pltpu.make_async_remote_copy(
            src_ref=mid.at[:, t], dst_ref=got_rows.at[own_rows], send_sem=req_send.at[0], recv_sem=req_recv.at[n],
            device_id=(t, y), device_id_type=MESH,
        ).start()
        return c

    lax.fori_loop(1, GRP, ask, 0)
    keep = pltpu.make_async_copy(mid.at[:, g], got_rows.at[own_rows], loc_sem.at[2])
    keep.start()

    load.wait()

    def widen_features(i, c):
        rows = pl.ds(pl.multiple_of(i * 256, 256), 256)
        table[rows, :] = featb[rows, :].astype(F32)
        return c

    lax.fori_loop(0, OWN // 256, widen_features, 0)

    lane32 = lax.broadcasted_iota(jnp.int32, (16, 128), 1)
    lane16 = lane32.astype(jnp.int16)
    iota16 = lax.broadcasted_iota(jnp.int32, (16, 128), 0).astype(jnp.int16)
    one, zero = jnp.ones((16, 128), BF), jnp.zeros((16, 128), BF)

    def unit(digit):
        v = jnp.ones_like(digit)
        for j in range(1, 8):
            v = jnp.where(digit == j, 1 << 4 * j, v)
        return v

    def count(acc, j):
        return ((acc >> (4 * j)) & 15).astype(F32).astype(BF)

    def keys_units(ids):
        return (ids & 127) + (ids >> 10) * 128, unit((ids >> 7) & 7)

    def word(pos, keys, units):
        acc = jnp.zeros((16, 128), jnp.int32)
        for k, u in zip(keys, units):
            acc = acc + jnp.where(pos == k, u, 0)
        return acc

    def spread_columns(blk, ks):
        return [jnp.broadcast_to(blk[:, k:k + 1], (16, 128)) for k in ks]

    ids = gidx2[y]
    keys, units = keys_units(ids)
    idc[...] = jnp.concatenate([ids[0:1, :], keys[1:, :], units], axis=0).T

    def seeds16(i):
        at = pl.multiple_of(i * 16, 16)
        blk = idc[pl.ds(at, 16), :]
        self_row = jnp.broadcast_to(blk[:, 0:1], (16, 128)).astype(jnp.int16)
        return at, (spread_columns(blk, range(1, 1 + F2)), spread_columns(blk, range(17, 17 + F2)), self_row)

    def forward_marks(at, want, q):
        keys, units, self_row = want
        for w in range(2):
            acc = word(lane32 + 128 * (2 * q + w), keys, units)
            for j in range(8):
                c = w * 8 + j
                fsel[q, pl.ds(at, 16), c * 128:(c + 1) * 128] = count(acc, j)
                here = lane16 + jnp.full((16, 128), q * FRONT + c * 128, jnp.int32).astype(jnp.int16)
                fsel[q, pl.ds(SEED + at, 16), c * 128:(c + 1) * 128] = jnp.where(here == self_row, one, zero)

    view = table.reshape(SRC + 8, 1, D_IN)
    my_rows = pl.ds(pl.multiple_of(me * CAP, CAP), CAP)

    def pick(t, u, slot):
        for half in range(0, CAP, 32):
            rows = [view[reqs[t * NAR + u, 0, half + r]] for r in range(32)]
            for r in range(32):
                stage[half + r:half + r + 1, :] = rows[r]
        featb[slot, :] = stage[...].astype(BF)

    def serve_one(t, u, slot):
        pick(t, u, slot)
        pltpu.make_async_remote_copy(
            src_ref=featb.at[slot], dst_ref=pulled.at[my_rows],
            send_sem=row_send, recv_sem=row_recv, device_id=(t, u), device_id_type=MESH,
        ).start()

    def asked(n):
        rows = got_rows.at[pl.ds(0, NAR)]
        pltpu.make_async_copy(rows, rows, req_recv.at[n]).wait()

    def to_scalars(t, n):
        rows = pl.ds(pl.multiple_of(t * NAR, NAR), NAR)
        return pltpu.make_async_copy(got_rows.at[rows], reqs.at[rows], ask_sem.at[n])

    def whose(i):
        n = (i * 13) % GRP
        return n, (g + GRP - n) % GRP

    def fetch(i):
        n, t = whose(i)
        asked(n)
        to_scalars(t, n).start()

    def serve(i, c):
        n, t = whose(i)

        @pl.when(i < GRP - 1)
        def _():
            fetch(i + 1)

        to_scalars(t, n).wait()
        at, want = seeds16(i)
        for d in range(NAR):
            forward_marks(at, want, d)
            serve_one(t, ys[d], pl.ds(pl.multiple_of((i * NAR + d) * CAP, CAP), CAP))
        return c

    fetch(1)
    lax.fori_loop(1, GRP, serve, 0)
    keep.wait()
    to_scalars(g, 0).start()
    to_scalars(g, 0).wait()
    at, want = seeds16(0)
    for d in range(NAR):
        forward_marks(at, want, d)
    for d in range(1, NAR):
        serve_one(g, ys[d], pl.ds(d * CAP, CAP))
    pick(g, y, pl.ds(0, CAP))
    pulled[my_rows, :] = featb[0:CAP, :]

    for n, a in enumerate(shared):
        for d in range(1, NAR):
            link(a.at[y], a.at[y], nar_send.at[n, d - 1], nar_recv.at[n, d - 1], (y + d) % NAR).wait()
    for q in range(NAR):
        w2t[:, q * 128:(q + 1) * 128] = gw2t[q]
    last = jnp.concatenate([bias[0:1, 384:428], jnp.zeros((1, 84), F32)], axis=1)
    b2c[...] = jnp.concatenate([spread(bias[0:1, 256:384]), spread(last)], axis=0)

    def column(row):
        return jnp.concatenate([spread(row[:, c * 128:(c + 1) * 128]) for c in range(SEED // 128)], axis=0)

    for q in range(NAR):
        n = jnp.sum((gidx2[q, 1:1 + F2, :] >= 0).astype(F32), axis=0, keepdims=True)
        invc[q] = column(1.0 / jnp.maximum(n, 1.0))
    livec[...] = column(2.0 * LAM / HID / SEEDS_ALL * live[...].astype(F32))

    for q in range(NAR):
        ids = gidx2[q] - y * FRONT
        for c in range(SEED // 128):
            for k in range(1 + F2):
                row = ids[k:k + 1, c * 128:(c + 1) * 128]
                wants[q, c, k] = jnp.broadcast_to(row, (16, 128)).astype(jnp.int16)

    def backward_marks(i):
        here = iota16 + jnp.full((16, 128), i * 16, jnp.int32).astype(jnp.int16)
        out = pl.ds(pl.multiple_of(i * 16, 16), 16)
        for q in range(NAR):
            for c in range(SEED // 128):
                acc = jnp.where(here == wants[q, c, 1], one, zero)
                for k in range(2, 1 + F2):
                    acc = acc + jnp.where(here == wants[q, c, k], one, zero)
                bsel[q, out, c * 128:(c + 1) * 128] = acc
                bsel[q, out, SEED + c * 128:SEED + (c + 1) * 128] = jnp.where(here == wants[q, c, 0], one, zero)

    def some_marks(i, c):
        backward_marks(i)
        return c

    def sum_marks(i):
        at = pl.multiple_of(i // 2 * 16, 16)
        half = i % 2
        blk = idm[pl.ds(at, 16), :]
        keys, units = spread_columns(blk, range(1, 1 + F1)), spread_columns(blk, range(17, 17 + F1))
        for w in range(4):
            acc = word(lane32 + (half * 4 + w) * 128, keys, units)
            for j in range(8):
                col = pl.ds(pl.multiple_of(half * (SRC // 2) + (w * 8 + j) * 128, 128), 128)
                ssel[pl.ds(at, 16), col] = count(acc, j)

    def sum_ids(b):
        idm[...] = jnp.concatenate(keys_units(idxv[:, cols(b)]), axis=0).T

    def cols(b):
        return pl.ds(pl.multiple_of(b * 256, 256), 256)

    def one_mark(i, c):
        sum_marks(i)
        return c

    sum_ids(0)
    lax.fori_loop(0, 32, one_mark, 0)
    lax.fori_loop(0, 16, some_marks, 0)

    def scales(i, c):
        at = pl.multiple_of(i * 128, 128)
        scale[pl.ds(at, 128), :] = spread(invv[0:1, pl.ds(at, 128)])
        return c

    lax.fori_loop(0, FRONT // 128, scales, 0)

    come = pulled.at[pl.ds(0, (DEV - 1) * CAP)]
    pltpu.make_async_copy(come, come, row_recv).wait()
    gone = featb.at[pl.ds(CAP, (DEV - 1) * CAP)]
    pltpu.make_async_copy(gone, gone, row_send).wait()
    sent = mid.at[:, pl.ds(0, GRP - 1)]
    pltpu.make_async_copy(sent, sent, req_send.at[0]).wait()

    def widen(i, c):
        rows = pl.ds(pl.multiple_of(i * 256, 256), 256)
        table[rows, :] = pulled[rows, :].astype(F32)
        return c

    lax.fori_loop(0, SRC // 256, widen, 0)
    table[SRC:SRC + 8, :] = jnp.zeros((8, D_IN), F32)
    for c in to_smem:
        c.wait()

    def forward(b):
        @pl.when(b % 2 == 0)
        def _():
            blk = gbuf.at[left, cols(b), :]
            link(blk, blk, h_send.at[0, b], h_recv.at[0, b], right).wait_recv()
            link(blk, blk, h_send.at[2, b], h_recv.at[2, b], right).start()

        @pl.when(b % 2 == 1)
        def _():
            blk = gbuf.at[right, cols(b), :]
            link(blk, blk, h_send.at[1, b], h_recv.at[1, b], left).wait_recv()
            link(blk, blk, h_send.at[2, b], h_recv.at[2, b], left).start()

    def load_sums(b):
        def some(i, c):
            backward_marks(b * 16 + i)
            found = []
            for e in range(2):
                line = b * 32 + 2 * i + e
                for r in range(8):
                    self_row = view[idx[line, r * 16]]
                    rows = [view[idx[line, r * 16 + 1 + k]] for k in range(F1)]
                    while len(rows) > 1:
                        rows = [p + q for p, q in zip(rows[::2], rows[1::2])] + ([rows[-1]] if len(rows) % 2 else [])
                    found.append((r * 32 + 2 * i + e, self_row, rows[0]))
            for at, self_row, total in found:
                own[pl.ds(at, 1), :] = self_row
                near[pl.ds(at, 1), :] = total
            return c

        lax.fori_loop(0, 16, some, 0)
        finish(b)

    def multiply_sums(b):
        def some(i, c):
            found = []
            for e in range(2):
                for r in range(8):
                    found.append((r * 32 + 2 * i + e, view[idx[b * 32 + 2 * i + e, r * 16]]))
            for at, self_row in found:
                own[pl.ds(at, 1), :] = self_row
            return c

        lax.fori_loop(0, 16, some, 0)
        near[...] = dot(ssel[...], pulled[...])
        finish(b)

    def finish(b):
        rows = cols(b)
        act = jnp.concatenate([own[...].astype(BF), (near[...] * scale[rows, :]).astype(BF)], axis=1)
        a1 = act.T
        for h in range(2):
            a1t[pl.ds(pl.multiple_of((2 * b + h) * 256, 256), 256), :] = a1[:, h * 128:(h + 1) * 128]
        z = dot(act, gw1[...].reshape(2 * D_IN, HID)) + bias[0:1, 0:HID]
        sig = 1.0 / (1.0 + jnp.exp(-z))
        h1 = z * sig
        slope[rows, :] = sig + h1 * (1.0 - sig)
        gbuf[y, rows, :] = h1.astype(BF)
        blk = gbuf.at[y, rows, :]
        link(blk, blk, h_send.at[0, b], h_recv.at[0, b], right).start()
        link(blk, blk, h_send.at[1, b], h_recv.at[1, b], left).start()

        @pl.when(b > 0)
        def _():
            forward(b - 1)

    def loaded(b, c):
        load_sums(b)
        return c

    multiply_sums(0)
    lax.fori_loop(1, 8, loaded, 0)
    forward(7)

    def from_sources(qs, fresh=False):
        def rows512(i, c):
            n = pl.multiple_of(i * SEED, SEED)
            part = sum(dot(fsel[q, pl.ds(n, SEED), :], gbuf[q]) for q in qs)
            for h in range(2):
                rows = pl.ds(pl.multiple_of(h * 2 * SEED + i * SEED, SEED), SEED)
                now = part[:, h * 128:(h + 1) * 128]
                tot[rows, :] = now if fresh else tot[rows, :] + now
            return c

        lax.fori_loop(0, 2, rows512, 0)

    from_sources([y], True)
    for b in range(1, 8, 2):
        blk = gbuf.at[left, b * 256:(b + 1) * 256, :]
        link(blk, blk, h_send.at[0, b], h_recv.at[0, b], right).wait_recv()
    for b in range(0, 8, 2):
        blk = gbuf.at[right, b * 256:(b + 1) * 256, :]
        link(blk, blk, h_send.at[1, b], h_recv.at[1, b], left).wait_recv()
    from_sources([left, right])
    for b in range(8):
        blk = gbuf.at[opp, b * 256:(b + 1) * 256, :]
        link(blk, blk, h_send.at[2, b], h_recv.at[2, b], right).wait_recv()
    from_sources([opp])

    def wide(a):
        return jnp.concatenate([a, a], axis=1)

    def seeds(first):
        return jnp.concatenate([tot[h * 2 * SEED + first:h * 2 * SEED + first + SEED, :] for h in range(2)], axis=1)

    near2 = (seeds(0) * wide(invc[y])).astype(BF)
    self2 = seeds(SEED).astype(BF)
    alive = live[...].astype(F32)
    diff = self2.astype(F32) - near2.astype(F32)
    pull_apart = wide(livec[...]) * diff

    def swap_start(buf, ssem, rsem):
        blk = buf.at[y]
        link(blk, blk, ssem.at[0], rsem.at[0], right).start()
        link(blk, blk, ssem.at[1], rsem.at[1], left).start()

    def swap_forward(buf, ssem, rsem, cut):
        blk = buf.at[left]
        link(blk, blk, ssem.at[0], rsem.at[0], right).wait_recv()
        half = buf.at[left, 0:cut, :]
        link(half, half, ssem.at[2], rsem.at[2], right).start()
        blk = buf.at[right]
        link(blk, blk, ssem.at[1], rsem.at[1], left).wait_recv()
        half = buf.at[right, cut:, :]
        link(half, half, ssem.at[3], rsem.at[3], left).start()

    def swap_end(buf, ssem, rsem, cut):
        half = buf.at[opp, 0:cut, :]
        link(half, half, ssem.at[2], rsem.at[2], right).wait_recv()
        half = buf.at[opp, cut:, :]
        link(half, half, ssem.at[3], rsem.at[3], left).wait_recv()

    def swap_sent(buf, ssem, rsem, cut):
        blk = buf.at[y]
        link(blk, blk, ssem.at[0], rsem.at[0], right).wait_send()
        link(blk, blk, ssem.at[1], rsem.at[1], left).wait_send()
        half = buf.at[left, 0:cut, :]
        link(half, half, ssem.at[2], rsem.at[2], right).wait_send()
        half = buf.at[right, cut:, :]
        link(half, half, ssem.at[3], rsem.at[3], left).wait_send()

    rbuf[y] = pull_apart.astype(BF)
    swap_start(rbuf, r_send, r_recv)

    act2 = jnp.concatenate([self2, near2], axis=1)
    cls = lax.broadcasted_iota(jnp.int32, (CLS_PAD, SEED), 0)
    b2 = b2c[0:CLS_PAD, :]
    logits = dot(w2t[...], act2, NT) + jnp.concatenate([b2] * 4, axis=1)
    logits = jnp.where(cls < CLS, logits, -1e30)
    top = jnp.max(logits, axis=0, keepdims=True)
    e = jnp.exp(logits - top)
    tot = jnp.sum(e, axis=0, keepdims=True)
    hot = cls == labels[...]
    picked = jnp.sum(jnp.where(hot, logits, 0.0), axis=0, keepdims=True)
    dlog = (alive * (e * (1.0 / tot) - jnp.where(hot, 1.0, 0.0)) * (1.0 / SEEDS_ALL)).astype(BF)
    dbuf[y] = dlog
    swap_start(dbuf, d_send, d_recv)

    loss = jnp.sum(alive * (top + jnp.log(tot) - picked), axis=1, keepdims=True)
    loss = loss + SEEDS_ALL / 2 * jnp.sum(pull_apart * diff, keepdims=True)
    g2t = dot(dlog, act2).astype(BF)
    for q in range(NAR):
        pay[ROW_2 + q * CLS_PAD:ROW_2 + (q + 1) * CLS_PAD, :] = g2t[:, q * 128:(q + 1) * 128]

    def to_owners(first, last):
        def one_owner(t, c):
            @pl.when(t != g)
            def _():
                pltpu.make_async_remote_copy(
                    src_ref=pay.at[pl.ds(pl.multiple_of(t * PIECE, 16), PIECE)], dst_ref=inbox.at[g],
                    send_sem=rs_send, recv_sem=rs_recv, device_id=(t, y), device_id_type=MESH,
                ).start()

            return c

        def turned(i, c):
            return one_owner(first + (i + g) % (last - first), c)

        lax.fori_loop(0, last - first, turned, 0)

    early, late = -(-ROW_2 // PIECE), ROW_MISC // PIECE
    to_owners(early, late)

    def add_grads(qs, fresh=False):
        both = []
        for q in qs:
            da = dot(dbuf[q], w2t[...], TN)
            r = rbuf[q].astype(F32)
            near_part = ((da[:, HID:] - r) * wide(invc[q])).astype(BF)
            both.append(jnp.concatenate([near_part, (da[:, :HID] + r).astype(BF)], axis=0))

        def rows512(i, c):
            n = pl.multiple_of(i * 512, 512)
            part = sum(dot(bsel[q, pl.ds(n, 512), :], d) for q, d in zip(qs, both))
            for h in range(2):
                rows = pl.ds(pl.multiple_of(h * FRONT + i * 512, 512), 512)
                now = part[:, h * 128:(h + 1) * 128]
                dh1[rows, :] = now if fresh else dh1[rows, :] + now
            return c

        lax.fori_loop(0, FRONT // 512, rows512, 0)

    db2 = jnp.sum(dlog.astype(F32), axis=1, keepdims=True)
    db2 = jnp.broadcast_to(db2, (CLS_PAD, 128)).T[0:1, :]
    swap_forward(rbuf, r_send, r_recv, SEED // 2)
    add_grads([y], True)
    swap_forward(dbuf, d_send, d_recv, 96)
    add_grads([left, right])
    swap_end(rbuf, r_send, r_recv, SEED // 2)
    swap_end(dbuf, d_send, d_recv, 96)
    add_grads([opp])

    def to_z(b, db):
        rows = pl.ds(pl.multiple_of(b * 256, 256), 256)
        dh = jnp.concatenate(
            [dh1[pl.ds(pl.multiple_of(h * FRONT + b * 256, 256), 256), :] for h in range(2)], axis=1
        )
        dz = (dh * slope[rows, :]).astype(BF)
        a1 = jnp.concatenate(
            [a1t[pl.ds(pl.multiple_of((2 * b + h) * 256, 256), 256), :] for h in range(2)], axis=1
        )
        part = dot(a1, dz)
        for h in range(2):
            now = slice(h * 256, (h + 1) * 256)
            gsum[now, :] = gsum[now, :] + part[:, h * 128:(h + 1) * 128]
        return db + jnp.sum(dz.astype(F32), axis=0, keepdims=True)

    gsum[...] = jnp.zeros((512, 128), F32)
    db1 = lax.fori_loop(0, FRONT // 256, to_z, jnp.zeros((1, HID), F32))
    pay[0:512, :] = gsum[...].astype(BF)
    misc[...] = jnp.zeros((32, 128), F32)

    def two(rows, v):
        hi = v.astype(BF).astype(F32)
        misc[rows:rows + 1, 0:v.shape[1]] = hi
        misc[rows + 4:rows + 5, 0:v.shape[1]] = v - hi

    two(0, db1[:, :128])
    two(1, db1[:, 128:])
    two(2, db2[:, :128])
    two(3, db2[:, 128:])
    hi = loss.astype(BF).astype(F32)
    misc[8:9, 0:1] = hi
    misc[9:10, 0:1] = loss - hi
    pay[ROW_MISC:ROWS, :] = misc[...].astype(BF)

    to_owners(0, early)
    to_owners(late, PIECES)
    mine = pl.ds(pl.multiple_of(g * PIECE, 16), PIECE)

    @pl.when(g < PIECES)
    def _():
        got = inbox.at[pl.ds(0, GRP - 1)]
        pltpu.make_async_copy(got, got, rs_recv).wait()
        inbox[g] = pay[mine, :]
        ybox[y] = jnp.sum(inbox[...].astype(F32), axis=0) + momenta[mine, :]
        for d in range(1, NAR):
            link(ybox.at[y], ybox.at[y], y_send.at[d - 1], y_recv.at[d - 1], ys[d]).start()
        for d in range(1, NAR):
            link(ybox.at[y], ybox.at[y], y_send.at[d - 1], y_recv.at[d - 1], ys[d]).wait()
        o_all[mine, :] = (ybox[0] + ybox[1]) + (ybox[2] + ybox[3])

        def tell(i, c):
            pltpu.make_async_remote_copy(
                src_ref=o_all.at[mine], dst_ref=o_all.at[mine], send_sem=ag_send, recv_sem=ag_recv,
                device_id=((g + 2 * i) % GRP, y), device_id_type=MESH,
            ).start()
            return c

        lax.fori_loop(1, GRP // 2, tell, 0)
        got = o_all.at[pl.ds(0, (PIECES // 2 - 1) * PIECE)]
        pltpu.make_async_copy(got, got, ag_recv).wait()

    @pl.when(g >= PIECES)
    def _():
        got = o_all.at[pl.ds(0, PIECES // 2 * PIECE)]
        pltpu.make_async_copy(got, got, ag_recv).wait()

    pairs = o_all.reshape(PIECES // 2, 2, PIECE, 128)
    half = pltpu.make_async_remote_copy(
        src_ref=pairs.at[:, g % 2], dst_ref=pairs.at[:, g % 2], send_sem=pair_send, recv_sem=pair_recv,
        device_id=(g + 1 - 2 * (g % 2), y), device_id_type=MESH,
    )
    half.start()

    @pl.when(g < PIECES)
    def _():
        gone = pay.at[pl.ds(0, (PIECES - 1) * PIECE)]
        pltpu.make_async_copy(gone, gone, rs_send).wait()
        gone = table.at[pl.ds(0, (GRP // 2 - 1) * PIECE)]
        pltpu.make_async_copy(gone, gone, ag_send).wait()

    @pl.when(g >= PIECES)
    def _():
        pltpu.make_async_copy(pay, pay, rs_send).wait()

    for b in range(8):
        blk = gbuf.at[y, b * 256:(b + 1) * 256, :]
        link(blk, blk, h_send.at[0, b], h_recv.at[0, b], right).wait_send()
        link(blk, blk, h_send.at[1, b], h_recv.at[1, b], left).wait_send()
        blk = gbuf.at[opp, b * 256:(b + 1) * 256, :]
        link(blk, blk, h_send.at[2, b], h_recv.at[2, b], right).wait_send()
    swap_sent(rbuf, r_send, r_recv, SEED // 2)
    swap_sent(dbuf, d_send, d_recv, 96)
    half.wait()


def main(reqt, feat, idx1t, msk1t, idx2t, msk2t, labels, live, w1, w2own, m1, m2own, bias):
    vm = pl.BlockSpec(memory_space=pltpu.VMEM)
    dma = pltpu.SemaphoreType.DMA
    sds = jax.ShapeDtypeStruct
    V = pltpu.VMEM
    return pl.pallas_call(
        main_kernel,
        out_shape=sds((ROWS, 128), F32),
        in_specs=[vm, pl.BlockSpec(memory_space=pl.ANY)] + [vm] * 11,
        out_specs=vm,
        scratch_shapes=[
            V((SRC + 8, D_IN), F32),
            V((OWN, D_IN), BF),
            V((SRC, D_IN), BF),
            V((CAP, D_IN), F32),
            V((DEV, 128), jnp.int32),
            V((DEV, 128), jnp.int32),
            V((NAR, GRP, 1, 128), jnp.int32),
            V((16, FRONT), jnp.int32),
            V((256, 128), jnp.int32),
            V((1, FRONT), F32),
            V((FRONT, 128), F32),
            V((256, D_IN), F32),
            V((256, D_IN), F32),
            V((FRONT, HID), F32),
            V((NAR, FRONT, HID), BF),
            V((NAR, 2 * SEED, FRONT), BF),
            V((NAR, FRONT, 2 * SEED), BF),
            V((NAR, 4, 1 + F2, 16, 128), jnp.int16),
            V((SEED, 32), jnp.int32),
            V((256, SRC), BF),
            V((256, 32), jnp.int32),
            V((NAR, SEED, 128), F32),
            V((SEED, 128), F32),
            V((NAR, SEED, HID), BF),
            V((NAR, CLS_PAD, SEED), BF),
            V((NAR, 64, HID), BF),
            V((NAR, CLS_PAD, 128), BF),
            V((ROWS, 128), F32),
            V((NAR, 16, SEED), jnp.int32),
            V((CLS_PAD, 2 * HID), BF),
            V((HID, 128), F32),
            V((ROWS, 128), BF),
            V((32, 128), F32),
            V((GRP, PIECE, 128), BF),
            V((NAR, PIECE, 128), F32),
            pltpu.SMEM((DEV, 1, 128), jnp.int32),
            pltpu.SMEM((256, 128), jnp.int32),
            dma, dma((3,)), dma((GRP,)), dma((NAR,)), dma((NAR,)), dma((GRP,)), dma, dma, dma((3, 3)), dma((3, 3)),
            dma((3, 8)), dma((3, 8)), dma((4,)), dma((4,)), dma((4,)), dma((4,)),
            dma, dma, dma((3,)), dma((3,)), dma, dma, dma, dma,
        ],
        compiler_params=pltpu.CompilerParams(
            collective_id=0, has_side_effects=True, vmem_limit_bytes=62 * 2**20
        ),
    )(reqt, feat, idx1t, msk1t, idx2t, msk2t, labels, live, w1, w2own, m1, m2own, bias)


def update_kernel(
    res, w1own, w2own, bias, biasm, biasv,
    o_loss, o_first, o_second, o_mom1, o_mom2, o_flow, o_slow, o_bias, o_bm, o_bv,
    x1s, x2s,
):
    y = lax.axis_index("nar")
    mom1 = jnp.concatenate([res[0:256, :], res[256:512, :]], axis=1)
    x1s[...] = mom1
    block64 = pl.ds(pl.multiple_of(y * 64, 64), 64)
    o_mom1[...] = x1s[block64, :]
    x1 = mom1 * (1.0 / (jnp.sqrt(jnp.sum(mom1 * mom1, keepdims=True)) + 1e-07))
    mom2 = jnp.concatenate([res[ROW_2 + q * CLS_PAD:ROW_2 + (q + 1) * CLS_PAD, :] for q in range(NAR)], axis=1)
    x2 = mom2 * (1.0 / (jnp.sqrt(jnp.sum(mom2 * mom2, keepdims=True)) + 1e-07))
    for i in range(NS_ITERS):
        x1 = ns_step(x1)
        x2 = ns_step(x2)
    x1s[...] = x1
    for q in range(NAR):
        x2s[q] = x2[:, q * 128:(q + 1) * 128]
    first_new = w1own[...] * (1.0 - WDECAY) - x1s[block64, :]
    o_first[...] = first_new
    o_flow[...] = first_new.astype(BF)
    second = w2own[...] * (1.0 - WDECAY) - (2 * HID / CLS) ** 0.5 * x2s[y][0:CLS, :]
    o_second[...] = second
    o_slow[...] = second.astype(BF)
    o_mom2[...] = res[pl.ds(pl.multiple_of(ROW_2 + y * CLS_PAD, 16), CLS_PAD), :][0:CLS, :]

    gb = res[ROW_MISC + 0:ROW_MISC + 4, :] + res[ROW_MISC + 4:ROW_MISC + 8, :]
    gb = jnp.concatenate([gb[0:1, :], gb[1:2, :], gb[2:3, :], gb[3:4, 0:44]], axis=1)
    m_new = BETA_ONE * biasm[...] + (1.0 - BETA_ONE) * gb
    v_new = BETA_TWO * biasv[...] + (1.0 - BETA_TWO) * gb * gb
    m_hat = m_new / (1.0 - BETA_ONE**STEP)
    v_hat = v_new / (1.0 - BETA_TWO**STEP)
    o_bias[...] = bias[...] * (1.0 - LR_BIAS * WDECAY) - LR_BIAS * m_hat / (jnp.sqrt(v_hat) + EPSILON)
    o_bm[...] = m_new
    o_bv[...] = v_new
    o_loss[...] = res[ROW_MISC + 8:ROW_MISC + 9, 0:1] + res[ROW_MISC + 9:ROW_MISC + 10, 0:1]


def update(*args):
    vm = pl.BlockSpec(memory_space=pltpu.VMEM)
    sds = jax.ShapeDtypeStruct
    return pl.pallas_call(
        update_kernel,
        out_shape=[
            sds((1, 1), F32), sds((64, HID), F32), sds((CLS, 128), F32), sds((64, HID), F32), sds((CLS, 128), F32),
            sds((64, HID), BF), sds((CLS, 128), BF), sds((1, 428), F32), sds((1, 428), F32), sds((1, 428), F32),
        ],
        in_specs=[vm] * 6,
        out_specs=[vm] * 10,
        scratch_shapes=[pltpu.VMEM((2 * D_IN, HID), F32), pltpu.VMEM((NAR, CLS_PAD, 128), F32)],
        compiler_params=pltpu.CompilerParams(vmem_limit_bytes=32 * 2**20),
    )(*args)


def per_device(
    features, requests, index_one, mask_one, index_two, mask_two, labels, seed_live,
    w_first, w_second, mom_first, mom_second, biases, bias_m, bias_v,
):
    w2own, bias = w_second.T, biases[None, :]
    res = main(
        requests.T, features, index_one.T, mask_one.T, index_two.T, mask_two.T, labels[None, :], seed_live[None, :],
        w_first, w2own, mom_first, mom_second.T, bias,
    )
    loss, first_new, second_new, mom_one, mom_two, first_low, second_low, bias_new, m_new, v_new = update(
        res, w_first, w2own, bias, bias_m[None, :], bias_v[None, :]
    )
    return (
        loss.reshape(()), first_new, second_new.T, mom_one, mom_two.T, first_low, second_low.T,
        bias_new.reshape(-1), m_new.reshape(-1), v_new.reshape(-1),
    )


def solution(mesh):
    both = ("grp", "nar")
    placed = (
        P(both, None), P(both, None), P(both, None), P(both, None), P(both, None), P(both, None),
        P(both), P(both), P("nar", None), P("nar", None), P("nar", None), P("nar", None), P(), P(), P(),
    )
    nar = P("nar", None)
    return jax.shard_map(
        per_device, mesh=mesh, in_specs=placed,
        out_specs=(P(), nar, nar, nar, nar, nar, nar, P(), P(), P()), check_vma=False,
    )
```
